32 devices in a mesh: gx: 2 (over y), gz: 4 (over x, core), gy: 4 (over z).
Axes of the slice: x: 2, y: 2, z: 4, core: 2. Of those that a mesh axis runs over, the one named last changes fastest.
Arguments:
- gas_field: float32 [3, 32, 64, 512], P(None, 'gx', 'gy', 'gz'), may hold values from -6 to 6
- velocity: float32 [2048, 3, 128], P(('gx', 'gz', 'gy')), may hold values from -6 to 6
- fraction: float32 [2048, 3, 128], P(('gx', 'gz', 'gy')), may hold values from 0 to 1
- response: float32 [2048, 128], P(('gx', 'gz', 'gy')), may hold values from 0.25 to 2
- cell_index: int32 [2048, 128], P(('gx', 'gz', 'gy')), may hold values from 0 to 127
- brick_index: int32 [2048], P(('gx', 'gz', 'gy')), may hold values from 0 to 255
- crossing: int32 [192, 8], P(('gx', 'gz', 'gy')), may hold values from -1 to 63, as said below
Outputs:
- gas_next: float32 [3, 32, 64, 512], P(None, 'gx', 'gy', 'gz')
- velocity_next: float32 [2048, 3, 128], P(('gx', 'gz', 'gy'))
- arrivals: float32 [192, 8, 7, 128], P(('gx', 'gz', 'gy'))
The draws below stay inside these ranges and needn't reach their ends.
Inputs may be any that keep to these rules, and one draw needn't show every extreme that they name: `crossing`: row 6 d + f lists the blocks of tile d (numbers 0 to 63 within the tile) that leave through face f (+x, -x, +y, -y, +z, -z): listed blocks first, then -1. No block is listed twice in one tile. Some face of some tile lists 8 blocks.
All inputs are finite; a program needn't handle non-finite values.
Results may differ from the reference program's by a relative error of at most 0.0003.
Values sent between devices are 32-bit elements; how exact they have to be, the bound alone decides.
No kernel may reach another device: no remote copies, remote signals or barrier semaphores. Data moves between devices by JAX's collectives and lax.ppermute only.
A program may use at most 128 MiB of HBM per device.

```python
import math
import jax
import jax.numpy as jnp
from jax import lax

BX = 4
BY = 4
BZ = 8
CX = 16
CY = 16
CZ = 128
NB = 64
CAP = 8
NBR = 256
NX = 32
NY = 64
NZ = 512
PB = 2048
N_GX = 2
N_GZ = 4
N_GY = 4


def draw_crossing(key, part):
    key = jax.random.fold_in(key, 11)
    tiles = N_GX * N_GZ * N_GY
    key_order, key_count, key_pick, key_full, key_face = jax.random.split(key, 5)
    orders = jax.vmap(lambda lone_particle: jax.random.permutation(lone_particle, NB))(jax.random.split(key_order, tiles)).astype(jnp.int32)
    picked = jax.random.randint(key_pick, (), 0, tiles)
    turned = (orders - orders[:, :1] + NB - 1) % NB
    device_index = jnp.arange(tiles, dtype=jnp.int32)
    orders = jnp.where((device_index == picked)[:, None], turned, orders)
    tile_y = device_index % N_GY
    at_wall = (tile_y == 0) | (tile_y == N_GY - 1)
    lowest = jnp.where(at_wall, max(1, CAP // 2), max(1, CAP // 4))
    counts = jax.random.randint(key_count, (tiles, 6), lowest[:, None], CAP + 1)
    full_tile = jax.random.randint(key_full, (), 0, tiles)
    complete_face = jax.random.randint(key_face, (), 0, 6)
    faces = jnp.arange(6, dtype=jnp.int32)
    counts = jnp.where((device_index[:, None] == full_tile) & (faces[None, :] == complete_face), CAP, counts)
    slots = jnp.arange(CAP, dtype=jnp.int32)
    chosen = orders[:, :6 * CAP].reshape(tiles, 6, CAP)
    lists = jnp.where(slots[None, None, :] < counts[:, :, None], chosen, -1)
    return lists.reshape(tiles * 6, CAP).astype(jnp.int32)


def touch_ends(values, key, smallest, high):
    longest = values.shape.index(max(values.shape))
    spots = []
    for shift in (0, 1):
        where = [jax.random.randint(jax.random.fold_in(key, axis), (), 0, length) for axis, length in enumerate(values.shape)]
        where[longest] = (where[longest] + shift) % values.shape[longest]
        spots.append(tuple(where))
    return values.at[spots[0]].set(smallest).at[spots[1]].set(high)


def block_levels(key, shape, cuts, low, top_value):
    def one(axis_at, shards_of):
        steps = jax.random.uniform(jax.random.fold_in(jax.random.fold_in(key, 6), axis_at), (shards_of,), jnp.float32, low / len(cuts), top_value / len(cuts))
        return jnp.repeat(jnp.exp(steps), shape[axis_at] // shards_of).reshape((-1,) + (1,) * (len(shape) - axis_at - 1))

    level = one(*cuts[0])
    for cut in cuts[1:]:
        level = level * one(*cut)
    return level


def normal_values(own_key, dims, spread, bound, cuts=(), kind=jnp.bfloat16):
    array = spread * jax.random.normal(own_key, dims, jnp.float32)
    if cuts:
        array = array * block_levels(own_key, dims, cuts, -0.22, 0.18)
    return jnp.clip(array, -bound, bound).astype(kind)


def setup_inputs(seed: int = 0) -> dict:
    splits = jax.random.split(jax.random.key(seed), 8)
    return {
        "gas_field": normal_values(splits[0], (3, NX, NY, NZ), 1.0, 6.0, ((1, 2), (2, 4), (3, 4)), jnp.float32),
        "velocity": normal_values(splits[1], (PB, 3, 128), 1.0, 6.0, ((0, 32),), jnp.float32),
        "fraction": jnp.clip(1.0 * jax.random.uniform(splits[2], (PB, 3, 128), jnp.float32) ** block_levels(splits[2], (PB, 3, 128), ((0, 32),), -0.2, 0.2), 0.0, 1.0),
        "response": jnp.clip(jnp.exp(math.log(2.0) - 2.0794415 * jax.random.uniform(splits[3], (PB, 128), jnp.float32) ** block_levels(splits[3], (PB, 128), ((0, 32),), -0.2, 0.2)), 0.25, 2.0),
        "cell_index": touch_ends(jax.random.randint(splits[4], (PB, 128), 0, BX * BY * BZ), jax.random.fold_in(splits[4], 1), 0, (BX * BY * BZ) - 1).astype(jnp.int32),
        "brick_index": touch_ends(jax.random.randint(splits[5], (PB,), 0, NBR), jax.random.fold_in(splits[5], 1), 0, NBR - 1).astype(jnp.int32),
        "crossing": draw_crossing(jax.random.fold_in(splits[7], 71), 0),
    }


TIME_STEP = 0.25
VISCOSITY = 0.4


def corners(fraction):
    along_x, along_y, along_z = fraction[:, 0], fraction[:, 1], fraction[:, 2]
    result = []
    for step_x in (0, 1):
        for step_y in (0, 1):
            for step_z in (0, 1):
                weight = (along_x if step_x else 1.0 - along_x) * (along_y if step_y else 1.0 - along_y) * (along_z if step_z else 1.0 - along_z)
                result.append((step_x, step_y, step_z, weight))
    return result


def reference(gas_field, velocity, fraction, response, cell_index, brick_index, crossing):
    tiles = N_GX * N_GZ * N_GY
    span_x, span_y, span_z = CX * N_GX, CY * N_GY, CZ * N_GZ
    bricks_y, bricks_z = CY // BY, CZ // BZ
    padded = jnp.pad(gas_field, ((0, 0), (0, 1), (0, 1), (0, 1)))
    padded = padded.at[:, span_x].set(padded[:, 0])
    padded = padded.at[:, :, :, span_z].set(padded[:, :, :, 0])

    def visit(totals, things):
        device_index, moving, offsets, timing, cells, bricks = things
        tile_x = device_index // (N_GZ * N_GY)
        tile_z = (device_index // N_GY) % N_GZ
        tile_y = device_index % N_GY
        brick_x = bricks // (bricks_y * bricks_z)
        brick_y = (bricks // bricks_z) % bricks_y
        brick_z = bricks % bricks_z
        base_x = (tile_x * CX + brick_x * BX)[:, None] + cells // (BY * BZ)
        base_y = (tile_y * CY + brick_y * BY)[:, None] + (cells // BZ) % BY
        base_z = (tile_z * CZ + brick_z * BZ)[:, None] + cells % BZ
        gas_sample = jnp.zeros((3, NB, 128), jnp.float32)
        for step_x, step_y, step_z, weight in corners(offsets):
            gas_sample = gas_sample + weight[None] * padded[:, base_x + step_x, base_y + step_y, base_z + step_z]
        drag_force = (jnp.transpose(gas_sample, (1, 0, 2)) - moving) / timing[:, None, :]
        moved = moving + TIME_STEP * drag_force
        pushed = jnp.transpose(drag_force, (1, 0, 2))
        for step_x, step_y, step_z, weight in corners(offsets):
            totals = totals.at[:, base_x + step_x, base_y + step_y, base_z + step_z].add(weight[None] * pushed)
        return totals, moved

    start = jnp.zeros((3, span_x + 1, span_y + 1, span_z + 1), jnp.float32)
    things = (jnp.arange(tiles, dtype=jnp.int32), velocity.reshape(tiles, NB, 3, 128), fraction.reshape(tiles, NB, 3, 128),
              response.reshape(tiles, NB, 128), cell_index.reshape(tiles, NB, 128), brick_index.reshape(tiles, NB))
    totals, moved = lax.scan(visit, start, things)
    totals = totals.at[:, 0].add(totals[:, span_x])
    totals = totals[:, :span_x]
    totals = totals.at[:, :, :, 0].add(totals[:, :, :, span_z])
    deposit = totals[:, :, :span_y, :span_z]

    walled = jnp.pad(gas_field, ((0, 0), (0, 0), (1, 1), (0, 0)))
    laplace = jnp.roll(gas_field, 1, 1) + jnp.roll(gas_field, -1, 1) + walled[:, :, 2:] + walled[:, :, :-2]
    laplace = laplace + jnp.roll(gas_field, 1, 3) + jnp.roll(gas_field, -1, 3) - 6.0 * gas_field
    loading = 0.5 * CX * CY * CZ / (NB * 128)
    gas_next = gas_field + TIME_STEP * (VISCOSITY * laplace - loading * deposit)

    state = jnp.concatenate([moved, fraction.reshape(tiles, NB, 3, 128) + TIME_STEP * moved, response.reshape(tiles, NB, 1, 128)], axis=2)
    lists = crossing.reshape(tiles, 6, CAP)
    device_index = jnp.arange(tiles, dtype=jnp.int32)
    tile_x = device_index // (N_GZ * N_GY)
    tile_z = (device_index // N_GY) % N_GZ
    tile_y = device_index % N_GY
    offsets = ((1, 0, 0), (-1, 0, 0), (0, 1, 0), (0, -1, 0), (0, 0, 1), (0, 0, -1))
    pieces = []
    for face, (step_x, step_y, step_z) in enumerate(offsets):
        from_x = (tile_x - step_x) % N_GX
        from_z = (tile_z - step_z) % N_GZ
        from_y = tile_y - step_y
        inside = (from_y >= 0) & (from_y < N_GY)
        source = (from_x * N_GZ + from_z) * N_GY + jnp.clip(from_y, 0, N_GY - 1)
        chosen = lists[source, face]
        picked = state[source[:, None], jnp.maximum(chosen, 0)]
        live = inside[:, None] & (chosen >= 0)
        pieces.append(jnp.where(live[:, :, None, None], picked, 0.0))
    arrivals = jnp.stack(pieces, axis=1).reshape(tiles * 6, CAP, 7, 128)
    return gas_next, moved.reshape(tiles * NB, 3, 128), arrivals
```

```python
import functools

import jax
import jax.numpy as jnp
from jax import lax
from jax.experimental import pallas as pl
from jax.experimental.pallas import tpu as pltpu
from jax.sharding import PartitionSpec as P

BX = 4
BY = 4
BZ = 8

TIME_STEP = 0.25
VISCOSITY = 0.4

LANES = 128
PACK = 32
HEAD = 8
ROWS_Y = 24
UNROLL = 4

VMEM = pl.BlockSpec(memory_space=pltpu.VMEM)
SMEM = pl.BlockSpec(memory_space=pltpu.SMEM)


def moved_along(block, axis, distance):
    count = lax.axis_size(axis)
    return lax.ppermute(block, axis, [(i, (i + distance) % count) for i in range(count)])


def call(body, outs, *operands, smem=(), scratch=(), aliases=None, cost=None):
    return pl.pallas_call(
        body,
        out_shape=[jax.ShapeDtypeStruct(shape, jnp.float32) for shape in outs],
        in_specs=[SMEM if i in smem else VMEM for i in range(len(operands))],
        out_specs=[VMEM] * len(outs),
        scratch_shapes=list(scratch),
        input_output_aliases=aliases or {},
        compiler_params=pltpu.CompilerParams(vmem_limit_bytes=40 * 1024 * 1024),
        cost_estimate=cost,
    )(*operands)


def lane_ids(rows):
    return lax.broadcasted_iota(jnp.int32, (rows, LANES), 1)


def turned(value, shift):
    shift = shift % LANES
    return pltpu.roll(value, shift, 1) if shift else value


def pack_face_kernel(gas_ref, face_ref):
    comps, size_x, size_y, _ = gas_ref.shape
    lane = lane_ids(size_y)
    face = jnp.zeros((size_y, LANES), jnp.float32)
    for c in range(comps):
        for x in range(size_x):
            place = PACK * c + x
            face = jnp.where(lane == place, turned(gas_ref[c, x], place), face)
    face_ref[...] = face


def halo_y_kernel(gas_ref, face_ref, from_x_ref, out_ref):
    comps, size_x, size_y, _ = gas_ref.shape
    for c in range(comps):
        out_ref[c * size_x : (c + 1) * size_x] = gas_ref[c, :, 0]
        out_ref[comps * size_x + c : comps * size_x + c + 1] = from_x_ref[c * size_y : c * size_y + 1]
    start = comps * size_y
    own = face_ref[0:8]
    far = turned(from_x_ref[start : start + 8], size_x)
    line = jnp.where(lane_ids(8) % PACK == size_x, far, own)
    out_ref[comps * size_x + comps : comps * size_x + comps + 1] = line[0:1]


def step_kernel(
    loading, brick_ref, crossing_ref, gas_ref, face_ref, from_x_ref, from_y_ref,
    velocity_ref, fraction_ref, response_ref, cell_ref,
    moved_ref, base_ref, to_y_ref, to_x_ref, to_z_ref, out_ref,
    grid_ref, deposit_ref, weight_ref, rows_ref,
):
    comps, size_x, size_y, size_z = gas_ref.shape
    nblocks = velocity_ref.shape[1]
    count_y, count_z = size_y // BY, size_z // BZ
    reach_x, reach_y = BX + 1, 8
    inside = lax.axis_index("gy") != lax.axis_size("gy") - 1
    lane = lane_ids(8)
    sub = lax.broadcasted_iota(jnp.int32, (8, LANES), 0)
    first_lane = lane == 0

    def row_of(sel, c, x):
        return HEAD + ((sel * comps + c) * (size_x + 1) + x) * ROWS_Y

    grid_ref[0:HEAD] = jnp.zeros((HEAD, LANES), jnp.float32)
    edge = comps * size_y
    for c in range(comps):
        for x in range(size_x + 1):
            if x < size_x:
                plane, line = gas_ref[c, x], from_y_ref[c * size_x + x : c * size_x + x + 1]
                far = turned(face_ref[...], -(PACK * c + x))
            else:
                plane = from_x_ref[c * size_y : (c + 1) * size_y]
                line = from_y_ref[comps * size_x + c : comps * size_x + c + 1]
                far = turned(from_x_ref[edge : edge + size_y], -PACK * c)
            corner = from_y_ref[comps * size_x + comps : comps * size_x + comps + 1]
            corner = turned(jnp.broadcast_to(corner, (8, LANES)), -(PACK * c + x))
            line = jnp.broadcast_to(line, (8, LANES))
            kept = (sub == 0) & inside
            zeros = jnp.zeros((8, LANES), jnp.float32)
            at = row_of(0, c, x)
            grid_ref[at : at + size_y] = plane
            grid_ref[at + size_y : at + ROWS_Y] = jnp.where(kept, line, zeros)
            at = row_of(1, c, x)
            grid_ref[at : at + size_y] = jnp.where(lane_ids(size_y) == 0, far, plane)
            grid_ref[at + size_y : at + ROWS_Y] = jnp.where(kept, jnp.where(first_lane, corner, line), zeros)
    deposit_ref[...] = jnp.zeros_like(deposit_ref)

    cells = cell_ref[...]
    cell_x, cell_y, cell_z = cells // (BY * BZ), cells // BZ % BY, cells % BZ
    along_x, along_z = fraction_ref[0], fraction_ref[2]
    for a in range(reach_x):
        weight_ref[a] = jnp.where(cell_x == a, 1.0 - along_x, 0.0) + jnp.where(cell_x == a - 1, along_x, 0.0)
    low, high = 1.0 - along_z, along_z
    low_main = low.astype(jnp.bfloat16).astype(jnp.float32)
    high_main = high.astype(jnp.bfloat16).astype(jnp.float32)
    rows_ref[0] = cell_y.astype(jnp.float32)
    rows_ref[1] = cell_z.astype(jnp.float32)
    rows_ref[2] = low_main
    rows_ref[3] = low - low_main
    rows_ref[4] = high_main
    rows_ref[5] = high - high_main
    rows_ref[6] = 1.0 / response_ref[...]

    packed_z = lax.broadcasted_iota(jnp.int32, (16, LANES), 0).astype(jnp.float32).astype(jnp.bfloat16)
    sub_y = sub.astype(jnp.float32)
    last = count_z - 1

    def one(k):
        brick = brick_ref[k]
        brick_x = brick // (count_y * count_z)
        brick_y = brick // count_z % count_y
        brick_z = brick % count_z
        sel = jnp.where(brick_z == last, 1, 0)
        start = HEAD + (sel * comps * (size_x + 1) + brick_x * BX) * ROWS_Y + brick_y * BY

        def row(i):
            return rows_ref[i, pl.ds(k, 1)]

        def tall(value):
            return jnp.broadcast_to(value, (16, LANES)).astype(jnp.bfloat16)

        place = row(1) + (brick_z * BZ).astype(jnp.float32)
        after = place + 1.0
        after = jnp.where(after == float(size_z), 0.0, after)
        place, after = tall(place), tall(after)
        low_main, low_rest, high_main, high_rest = [tall(row(i)) for i in (2, 3, 4, 5)]
        nothing = jnp.zeros((16, LANES), jnp.bfloat16)
        main, rest = [], []
        for j in range(size_z // 16):
            here = packed_z + jnp.bfloat16(16 * j)
            at_low, at_high = here == place, here == after
            main.append(jnp.where(at_low, low_main, jnp.where(at_high, high_main, nothing)))
            rest.append(jnp.where(at_low, low_rest, jnp.where(at_high, high_rest, nothing)))
        main, rest = jnp.concatenate(main, axis=0), jnp.concatenate(rest, axis=0)
        both = jnp.concatenate([main, rest], axis=1)
        table = jnp.concatenate([both, both], axis=0)
        both_t = jnp.concatenate([main, rest], axis=0)
        table_t = jnp.concatenate([both_t, both_t], axis=1)

        def cut(value):
            top = value.astype(jnp.bfloat16)
            return jnp.concatenate([top, (value - top.astype(jnp.float32)).astype(jnp.bfloat16)], axis=1)

        offsets = [(c * (size_x + 1) + a) * ROWS_Y for c in range(comps) for a in range(reach_x)]
        window = jnp.concatenate([grid_ref[pl.ds(start + o, reach_y)] for o in offsets], axis=0)
        lines = lax.dot_general(cut(window), table, (((1,), (0,)), ((), ())), preferred_element_type=jnp.float32)
        lines = lines[:, :LANES] + lines[:, LANES:]
        lines = lines.reshape(comps, reach_x, reach_y, LANES)
        weight_x = [weight_ref[a, pl.ds(k, 1)] for a in range(reach_x)]
        in_y, along_y = row(0), fraction_ref[1, pl.ds(k, 1)]
        weight_y = jnp.where(sub_y == in_y, 1.0 - along_y, 0.0) + jnp.where(sub_y == in_y + 1.0, along_y, 0.0)
        rate = row(6)
        pushed = []
        for c in range(comps):
            total = lines[c, 0] * weight_x[0]
            for a in range(1, reach_x):
                total = total + lines[c, a] * weight_x[a]
            gas_sample = jnp.sum(total * weight_y, axis=0, keepdims=True)
            moving = velocity_ref[c, pl.ds(k, 1)]
            drag = (gas_sample - moving) * rate
            moved_ref[c, pl.ds(k, 1)] = moving + TIME_STEP * drag
            spread = drag * weight_y
            pushed.extend(spread * weight_x[a] for a in range(reach_x))
        pushed = jnp.concatenate(pushed, axis=0)
        shares = lax.dot_general(cut(pushed), table_t, (((1,), (1,)), ((), ())), preferred_element_type=jnp.float32)
        shares = shares[:, :LANES] + shares[:, LANES:]
        return start, offsets, shares

    @pl.loop(0, nblocks // UNROLL)
    def _(group):
        results = [one(group * UNROLL + u) for u in range(UNROLL)]
        for start, offsets, shares in results:
            for i, o in enumerate(offsets):
                spot = pl.ds(start + o, reach_y)
                deposit_ref[spot] = deposit_ref[spot] + shares[i * reach_y : (i + 1) * reach_y]

    push, diffuse = -TIME_STEP * loading, TIME_STEP * VISCOSITY
    for y in range(0, size_y, 8):
        to_z_ref[y : y + 8] = jnp.zeros((8, LANES), jnp.float32)
    tall_lane = lane_ids(ROWS_Y)
    face_out = jnp.zeros((ROWS_Y, LANES), jnp.float32)
    for c in range(comps):
        for x in range(size_x + 1):
            at, up = row_of(0, c, x), row_of(1, c, x)
            wrapped = deposit_ref[up : up + ROWS_Y]
            total = push * (deposit_ref[at : at + ROWS_Y] + jnp.where(tall_lane == 0, 0.0, wrapped))
            beyond = push * wrapped
            if x < size_x:
                here = grid_ref[at : at + size_y]
                laplace = grid_ref[at + ROWS_Y : at + ROWS_Y + size_y]
                if x:
                    laplace = laplace + grid_ref[at - ROWS_Y : at - ROWS_Y + size_y]
                laplace = laplace + grid_ref[at + 1 : at + 1 + size_y] + grid_ref[at - 1 : at - 1 + size_y]
                behind = turned(here, 1)
                ahead = turned(grid_ref[up : up + size_y], -1)
                laplace = laplace + ahead + jnp.where(lane_ids(size_y) == 0, 0.0, behind) - 6.0 * here
                base_ref[c, x] = here + diffuse * laplace + total[:size_y]
                line = diffuse * here[size_y - 1 :] + total[size_y : size_y + 1]
                beyond = jnp.concatenate([beyond[:size_y] + diffuse * behind, beyond[size_y:]], axis=0)
            else:
                here = grid_ref[at - ROWS_Y : at - ROWS_Y + size_y]
                to_x_ref[c * size_y : (c + 1) * size_y] = diffuse * here + total[:size_y]
                line = total[size_y : size_y + 1]
            to_y_ref[c * ROWS_Y + x : c * ROWS_Y + x + 1] = line
            place = PACK * c + x
            face_out = jnp.where(tall_lane == place, turned(beyond, place), face_out)
    to_z_ref[...] = face_out[:size_y]
    to_y_ref[size_x + 1 : size_x + 2] = face_out[size_y : size_y + 1]

    capacity = crossing_ref.shape[1]
    for face in range(6):
        for slot in range(capacity):
            block = crossing_ref[face, slot]
            live = block >= 0
            spot = pl.ds(jnp.maximum(block, 0), 1)
            state = [moved_ref[c, spot] for c in range(comps)]
            state = state + [fraction_ref[c, spot] + TIME_STEP * state[c] for c in range(comps)]
            state.append(response_ref[spot])
            for i, value in enumerate(state):
                out_ref[face, i, slot : slot + 1] = jnp.where(live, value, 0.0)


def relay_x_kernel(size_x, size_y, comps, from_y_ref, to_x_ref, to_z_ref, x_ref, z_ref):
    inside = lax.axis_index("gy") != 0
    x_ref[...] = to_x_ref[...]
    z_ref[...] = to_z_ref[...]
    for c in range(comps):
        at = c * ROWS_Y + size_x
        spot = slice(c * size_y, c * size_y + 1)
        x_ref[spot] = to_x_ref[spot] + jnp.where(inside, from_y_ref[at : at + 1], 0.0)
    line = jnp.where(inside, from_y_ref[size_x + 1 : size_x + 2], 0.0)
    z_ref[0:1] = to_z_ref[0:1] + line
    edge = comps * size_y
    x_ref[edge : edge + size_y] = z_ref[...]


def relay_z_kernel(size_x, comps, edge, from_x_ref, to_z_ref, z_ref):
    size_y = to_z_ref.shape[0]
    lane = lane_ids(size_y)
    far = turned(from_x_ref[edge : edge + size_y], -size_x)
    z_ref[...] = to_z_ref[...] + jnp.where(lane % PACK == 0, far, 0.0)


def finish_kernel(base_ref, from_y_ref, from_x_ref, from_z_ref, gas_ref):
    comps, size_x, size_y, _ = base_ref.shape
    inside = lax.axis_index("gy") != 0
    lane = lane_ids(size_y)
    row = lax.broadcasted_iota(jnp.int32, (size_y, LANES), 0)
    first = (row == 0) & inside
    face = from_z_ref[...]
    for c in range(comps):
        for x in range(size_x):
            total = base_ref[c, x]
            line = jnp.broadcast_to(from_y_ref[c * ROWS_Y + x : c * ROWS_Y + x + 1], (size_y, LANES))
            total = total + jnp.where(first, line, 0.0)
            if x == 0:
                total = total + from_x_ref[c * size_y : (c + 1) * size_y]
            total = total + jnp.where(lane == 0, turned(face, -(PACK * c + x)), 0.0)
            gas_ref[c, x] = total


def per_device(gas_field, velocity, fraction, response, cell_index, brick_index, crossing):
    comps, size_x, size_y, size_z = gas_field.shape
    nblocks = velocity.shape[0]
    loading = 0.5 * size_x * size_y * size_z / (nblocks * 128)
    velocity = jnp.transpose(velocity, (1, 0, 2))
    fraction = jnp.transpose(fraction, (1, 0, 2))

    (face,) = call(pack_face_kernel, [(size_y, LANES)], gas_field)
    face = moved_along(face, "gz", -1)
    plane = jnp.concatenate([gas_field[:, 0].reshape(comps * size_y, LANES), face], axis=0)
    from_x = moved_along(plane, "gx", -1)
    rows = -(-(comps * size_x + comps + 1) // 8) * 8
    (lines,) = call(halo_y_kernel, [(rows, LANES)], gas_field, face, from_x)
    from_y = moved_along(lines, "gy", -1)

    grid_rows = HEAD + 2 * comps * (size_x + 1) * ROWS_Y
    moved, base, to_y, to_x, to_z, leaving = call(
        functools.partial(step_kernel, loading),
        [
            (comps, nblocks, LANES),
            (comps, size_x, size_y, LANES),
            (comps * ROWS_Y, LANES),
            (comps * size_y, LANES),
            (size_y, LANES),
            (6, 7, crossing.shape[1], LANES),
        ],
        brick_index, crossing, gas_field, face, from_x, from_y, velocity, fraction, response, cell_index,
        smem=(0, 1),
        scratch=(
            pltpu.VMEM((grid_rows, LANES), jnp.float32),
            pltpu.VMEM((grid_rows, LANES), jnp.float32),
            pltpu.VMEM((BX + 1, nblocks, LANES), jnp.float32),
            pltpu.VMEM((7, nblocks, LANES), jnp.float32),
        ),
    )

    def flat(array):
        return array.reshape(-1, LANES)

    def joined(*arrays):
        return jnp.concatenate([flat(array) for array in arrays], axis=0)

    count = flat(leaving[0]).shape[0]
    got_y = moved_along(joined(to_y, leaving[2]), "gy", 1)
    got_my = moved_along(leaving[3], "gy", -1)
    got_mz = moved_along(leaving[5], "gz", -1)
    edge = comps * size_y
    x_part, z_part = call(
        functools.partial(relay_x_kernel, size_x, size_y, comps),
        [(edge + size_y, LANES), (size_y, LANES)],
        got_y, jnp.concatenate([to_x, to_z], axis=0), to_z,
    )
    if lax.axis_size("gx") == 2:
        got_x = moved_along(joined(x_part, leaving[0], leaving[1]), "gx", 1)
        got_mx = got_x[edge + size_y + count :]
    else:
        got_x = moved_along(joined(x_part, leaving[0]), "gx", 1)
        got_mx = moved_along(leaving[1], "gx", -1)
    (z_part,) = call(functools.partial(relay_z_kernel, size_x, comps, edge), [(size_y, LANES)], got_x, z_part)
    got_z = moved_along(joined(z_part, leaving[4]), "gz", 1)
    (gas_next,) = call(finish_kernel, [gas_field.shape], base, got_y[: comps * ROWS_Y], got_x[:edge], got_z[:size_y])

    low = lax.axis_index("gy") == 0
    high = lax.axis_index("gy") == lax.axis_size("gy") - 1
    parts = [
        got_x[edge + size_y : edge + size_y + count],
        got_mx,
        jnp.where(low, 0.0, got_y[comps * ROWS_Y :]),
        jnp.where(high, 0.0, flat(got_my)),
        got_z[size_y:],
        got_mz,
    ]
    arrivals = jnp.stack([part.reshape(7, -1, LANES) for part in parts], axis=0)
    return gas_next, jnp.transpose(moved, (1, 0, 2)), jnp.transpose(arrivals, (0, 2, 1, 3))


def solution(mesh):
    owner = ("gx", "gz", "gy")
    in_specs = (
        P(None, "gx", "gy", "gz"),
        P(owner, None, None),
        P(owner, None, None),
        P(owner, None),
        P(owner, None),
        P(owner),
        P(owner, None),
    )
    out_specs = (
        P(None, "gx", "gy", "gz"),
        P(owner, None, None),
        P(owner, None, None, None),
    )
    return jax.shard_map(
        per_device, mesh=mesh, in_specs=in_specs, out_specs=out_specs, check_vma=False
    )
```

```python
import functools

import jax
import jax.numpy as jnp
from jax import lax
from jax.experimental import pallas as pl
from jax.experimental.pallas import tpu as pltpu
from jax.sharding import PartitionSpec as P

BX = 4
BY = 4
BZ = 8

TIME_STEP = 0.25
VISCOSITY = 0.4

LANES = 128
PACK = 32
HEAD = 8
ROWS_Y = 24
UNROLL = 8

VMEM = pl.BlockSpec(memory_space=pltpu.VMEM)
SMEM = pl.BlockSpec(memory_space=pltpu.SMEM)


def moved_along(block, axis, distance):
    count = lax.axis_size(axis)
    return lax.ppermute(block, axis, [(i, (i + distance) % count) for i in range(count)])


def moved_inside(block, axis, distance):
    count = lax.axis_size(axis)
    route = [(i, i + distance) for i in range(count) if 0 <= i + distance < count]
    return lax.ppermute(block, axis, route)


def call(body, outs, *operands, smem=(), scratch=(), aliases=None, cost=None):
    return pl.pallas_call(
        body,
        out_shape=[jax.ShapeDtypeStruct(shape, jnp.float32) for shape in outs],
        in_specs=[SMEM if i in smem else VMEM for i in range(len(operands))],
        out_specs=[VMEM] * len(outs),
        scratch_shapes=list(scratch),
        input_output_aliases=aliases or {},
        compiler_params=pltpu.CompilerParams(vmem_limit_bytes=40 * 1024 * 1024),
        cost_estimate=cost,
    )(*operands)


def lane_ids(rows):
    return lax.broadcasted_iota(jnp.int32, (rows, LANES), 1)


def turned(value, shift):
    shift = shift % LANES
    return pltpu.roll(value, shift, 1) if shift else value


def pack_face_kernel(gas_ref, face_ref):
    comps, size_x, size_y, _ = gas_ref.shape
    lane = lane_ids(size_y)
    face = jnp.zeros((size_y, LANES), jnp.float32)
    for c in range(comps):
        for x in range(size_x):
            place = PACK * c + x
            face = jnp.where(lane == place, turned(gas_ref[c, x], place), face)
    face_ref[...] = face


def halo_y_kernel(gas_ref, face_ref, from_x_ref, out_ref):
    comps, size_x, size_y, _ = gas_ref.shape
    for c in range(comps):
        out_ref[c * size_x : (c + 1) * size_x] = gas_ref[c, :, 0]
        out_ref[comps * size_x + c : comps * size_x + c + 1] = from_x_ref[c * size_y : c * size_y + 1]
    start = comps * size_y
    own = face_ref[0:8]
    far = turned(from_x_ref[start : start + 8], size_x)
    line = jnp.where(lane_ids(8) % PACK == size_x, far, own)
    out_ref[comps * size_x + comps : comps * size_x + comps + 1] = line[0:1]


def step_kernel(
    loading, brick_ref, crossing_ref, gas_ref, face_ref, from_x_ref, from_y_ref,
    velocity_ref, fraction_ref, response_ref, cell_ref,
    moved_ref, base_ref, to_y_ref, to_x_ref, to_z_ref, out_ref,
    grid_ref, deposit_ref, weight_ref, rows_ref, drag_ref,
):
    comps, size_x, size_y, size_z = gas_ref.shape
    nblocks = velocity_ref.shape[1]
    count_y, count_z = size_y // BY, size_z // BZ
    reach_x, reach_y = BX + 1, 8
    inside = lax.axis_index("gy") != lax.axis_size("gy") - 1
    lane = lane_ids(8)
    sub = lax.broadcasted_iota(jnp.int32, (8, LANES), 0)
    first_lane = lane == 0

    def row_of(sel, c, x):
        return HEAD + ((sel * comps + c) * (size_x + 1) + x) * ROWS_Y

    grid_ref[0:HEAD] = jnp.zeros((HEAD, LANES), jnp.float32)
    edge = comps * size_y
    for c in range(comps):
        for x in range(size_x + 1):
            if x < size_x:
                plane, line = gas_ref[c, x], from_y_ref[c * size_x + x : c * size_x + x + 1]
                far = turned(face_ref[...], -(PACK * c + x))
            else:
                plane = from_x_ref[c * size_y : (c + 1) * size_y]
                line = from_y_ref[comps * size_x + c : comps * size_x + c + 1]
                far = turned(from_x_ref[edge : edge + size_y], -PACK * c)
            corner = from_y_ref[comps * size_x + comps : comps * size_x + comps + 1]
            corner = turned(jnp.broadcast_to(corner, (8, LANES)), -(PACK * c + x))
            line = jnp.broadcast_to(line, (8, LANES))
            kept = (sub == 0) & inside
            zeros = jnp.zeros((8, LANES), jnp.float32)
            at = row_of(0, c, x)
            grid_ref[at : at + size_y] = plane
            grid_ref[at + size_y : at + ROWS_Y] = jnp.where(kept, line, zeros)
            at = row_of(1, c, x)
            grid_ref[at : at + size_y] = jnp.where(lane_ids(size_y) == 0, far, plane)
            grid_ref[at + size_y : at + ROWS_Y] = jnp.where(kept, jnp.where(first_lane, corner, line), zeros)
    deposit_ref[...] = jnp.zeros_like(deposit_ref)

    cells = cell_ref[...]
    cell_x, cell_y, cell_z = cells // (BY * BZ), cells // BZ % BY, cells % BZ
    along_x, along_z = fraction_ref[0], fraction_ref[2]
    for a in range(reach_x):
        weight_ref[a] = jnp.where(cell_x == a, 1.0 - along_x, 0.0) + jnp.where(cell_x == a - 1, along_x, 0.0)
    low, high = 1.0 - along_z, along_z
    low_main = low.astype(jnp.bfloat16).astype(jnp.float32)
    high_main = high.astype(jnp.bfloat16).astype(jnp.float32)
    rows_ref[0] = cell_y.astype(jnp.float32)
    rows_ref[1] = cell_z.astype(jnp.float32)
    rows_ref[2] = low_main
    rows_ref[3] = low - low_main
    rows_ref[4] = high_main
    rows_ref[5] = high - high_main
    rows_ref[6] = 1.0 / response_ref[...]
    rows_ref[7] = low
    rows_ref[8] = high

    packed_z = lax.broadcasted_iota(jnp.int32, (16, LANES), 0).astype(jnp.float32).astype(jnp.bfloat16)
    sub_y = sub.astype(jnp.float32)
    last = count_z - 1
    offsets = [(c * (size_x + 1) + a) * ROWS_Y for c in range(comps) for a in range(reach_x)]

    def row(i, k):
        return rows_ref[i, pl.ds(k, 1)]

    def spot_of(k):
        brick = brick_ref[k]
        brick_x = brick // (count_y * count_z)
        brick_y = brick // count_z % count_y
        brick_z = brick % count_z
        sel = jnp.where(brick_z == last, 1, 0)
        start = HEAD + (sel * comps * (size_x + 1) + brick_x * BX) * ROWS_Y + brick_y * BY
        return start, brick_z * BZ

    def weight_y_of(k):
        in_y, along_y = row(0, k), fraction_ref[1, pl.ds(k, 1)]
        return jnp.where(sub_y == in_y, 1.0 - along_y, 0.0) + jnp.where(sub_y == in_y + 1.0, along_y, 0.0)

    def drag_of(k):
        start, first_z = spot_of(k)
        place = cell_ref[pl.ds(k, 1)] % BZ + first_z
        place = jnp.broadcast_to(place, (reach_y, LANES))
        after = (place + 1) % size_z
        low, high = row(7, k), row(8, k)
        weight_x = [weight_ref[a, pl.ds(k, 1)] for a in range(reach_x)]
        weight_low = [w * low for w in weight_x]
        weight_high = [w * high for w in weight_x]
        weight_y = weight_y_of(k)
        rate = row(6, k)
        for c in range(comps):
            total = None
            for a in range(reach_x):
                window = grid_ref[pl.ds(start + offsets[c * reach_x + a], reach_y)]
                one = jnp.take_along_axis(window, place, axis=1, mode="promise_in_bounds") * weight_low[a]
                two = jnp.take_along_axis(window, after, axis=1, mode="promise_in_bounds") * weight_high[a]
                total = one + two if total is None else total + (one + two)
            gas_sample = jnp.sum(total * weight_y, axis=0, keepdims=True)
            moving = velocity_ref[c, pl.ds(k, 1)]
            drag = (gas_sample - moving) * rate
            moved_ref[c, pl.ds(k, 1)] = moving + TIME_STEP * drag
            drag_ref[c, pl.ds(k, 1)] = drag

    def shares_of(k):
        start, first_z = spot_of(k)

        def tall(value):
            return jnp.broadcast_to(value, (16, LANES)).astype(jnp.bfloat16)

        place = row(1, k) + first_z.astype(jnp.float32)
        after = place + 1.0
        after = jnp.where(after == float(size_z), 0.0, after)
        place, after = tall(place), tall(after)
        low_main, low_rest, high_main, high_rest = [tall(row(i, k)) for i in (2, 3, 4, 5)]
        nothing = jnp.zeros((16, LANES), jnp.bfloat16)
        main, rest = [], []
        for j in range(size_z // 16):
            here = packed_z + jnp.bfloat16(16 * j)
            at_low, at_high = here == place, here == after
            main.append(jnp.where(at_low, low_main, jnp.where(at_high, high_main, nothing)))
            rest.append(jnp.where(at_low, low_rest, jnp.where(at_high, high_rest, nothing)))
        both = jnp.concatenate(main + rest, axis=0)
        table = jnp.concatenate([both, both], axis=1)
        weight_x = [weight_ref[a, pl.ds(k, 1)] for a in range(reach_x)]
        weight_y = weight_y_of(k)
        pushed = []
        for c in range(comps):
            spread = drag_ref[c, pl.ds(k, 1)] * weight_y
            pushed.extend(spread * weight_x[a] for a in range(reach_x))
        pushed = jnp.concatenate(pushed, axis=0)
        top = pushed.astype(jnp.bfloat16)
        pushed = jnp.concatenate([top, (pushed - top.astype(jnp.float32)).astype(jnp.bfloat16)], axis=1)
        shares = lax.dot_general(pushed, table, (((1,), (1,)), ((), ())), preferred_element_type=jnp.float32)
        return start, shares[:, :LANES] + shares[:, LANES:]

    @pl.loop(0, nblocks // UNROLL)
    def _(group):
        for u in range(UNROLL):
            drag_of(group * UNROLL + u)

    @pl.loop(0, nblocks // UNROLL)
    def _(group):
        results = [shares_of(group * UNROLL + u) for u in range(UNROLL)]
        for start, shares in results:
            for i, o in enumerate(offsets):
                spot = pl.ds(start + o, reach_y)
                deposit_ref[spot] = deposit_ref[spot] + shares[i * reach_y : (i + 1) * reach_y]

    push, diffuse = -TIME_STEP * loading, TIME_STEP * VISCOSITY
    for y in range(0, size_y, 8):
        to_z_ref[y : y + 8] = jnp.zeros((8, LANES), jnp.float32)
    tall_lane = lane_ids(ROWS_Y)
    face_out = jnp.zeros((ROWS_Y, LANES), jnp.float32)
    for c in range(comps):
        for x in range(size_x + 1):
            at, up = row_of(0, c, x), row_of(1, c, x)
            wrapped = deposit_ref[up : up + ROWS_Y]
            total = push * (deposit_ref[at : at + ROWS_Y] + jnp.where(tall_lane == 0, 0.0, wrapped))
            beyond = push * wrapped
            if x < size_x:
                here = grid_ref[at : at + size_y]
                laplace = grid_ref[at + ROWS_Y : at + ROWS_Y + size_y]
                if x:
                    laplace = laplace + grid_ref[at - ROWS_Y : at - ROWS_Y + size_y]
                laplace = laplace + grid_ref[at + 1 : at + 1 + size_y] + grid_ref[at - 1 : at - 1 + size_y]
                behind = turned(here, 1)
                ahead = turned(grid_ref[up : up + size_y], -1)
                laplace = laplace + ahead + jnp.where(lane_ids(size_y) == 0, 0.0, behind) - 6.0 * here
                base_ref[c, x] = here + diffuse * laplace + total[:size_y]
                line = diffuse * here[size_y - 1 :] + total[size_y : size_y + 1]
                beyond = jnp.concatenate([beyond[:size_y] + diffuse * behind, beyond[size_y:]], axis=0)
            else:
                here = grid_ref[at - ROWS_Y : at - ROWS_Y + size_y]
                to_x_ref[c * size_y : (c + 1) * size_y] = diffuse * here + total[:size_y]
                line = total[size_y : size_y + 1]
            to_y_ref[c * ROWS_Y + x : c * ROWS_Y + x + 1] = line
            place = PACK * c + x
            face_out = jnp.where(tall_lane == place, turned(beyond, place), face_out)
    to_z_ref[...] = face_out[:size_y]
    to_y_ref[size_x + 1 : size_x + 2] = face_out[size_y : size_y + 1]

    capacity = crossing_ref.shape[1]
    for face in range(6):
        for slot in range(capacity):
            block = crossing_ref[face, slot]
            live = block >= 0
            spot = pl.ds(jnp.maximum(block, 0), 1)
            state = [moved_ref[c, spot] for c in range(comps)]
            state = state + [fraction_ref[c, spot] + TIME_STEP * state[c] for c in range(comps)]
            state.append(response_ref[spot])
            for i, value in enumerate(state):
                out_ref[face, i, slot : slot + 1] = jnp.where(live, value, 0.0)


def relay_x_kernel(size_x, size_y, comps, from_y_ref, to_x_ref, to_z_ref, x_ref, z_ref):
    inside = lax.axis_index("gy") != 0
    x_ref[...] = to_x_ref[...]
    z_ref[...] = to_z_ref[...]
    for c in range(comps):
        at = c * ROWS_Y + size_x
        spot = slice(c * size_y, c * size_y + 1)
        x_ref[spot] = to_x_ref[spot] + jnp.where(inside, from_y_ref[at : at + 1], 0.0)
    line = jnp.where(inside, from_y_ref[size_x + 1 : size_x + 2], 0.0)
    z_ref[0:1] = to_z_ref[0:1] + line
    edge = comps * size_y
    x_ref[edge : edge + size_y] = z_ref[...]


def relay_z_kernel(size_x, comps, edge, from_x_ref, to_z_ref, z_ref):
    size_y = to_z_ref.shape[0]
    lane = lane_ids(size_y)
    far = turned(from_x_ref[edge : edge + size_y], -size_x)
    z_ref[...] = to_z_ref[...] + jnp.where(lane % PACK == 0, far, 0.0)


def finish_kernel(base_ref, from_y_ref, from_x_ref, from_z_ref, gas_ref):
    comps, size_x, size_y, _ = base_ref.shape
    inside = lax.axis_index("gy") != 0
    lane = lane_ids(size_y)
    row = lax.broadcasted_iota(jnp.int32, (size_y, LANES), 0)
    first = (row == 0) & inside
    face = from_z_ref[...]
    for c in range(comps):
        for x in range(size_x):
            total = base_ref[c, x]
            line = jnp.broadcast_to(from_y_ref[c * ROWS_Y + x : c * ROWS_Y + x + 1], (size_y, LANES))
            total = total + jnp.where(first, line, 0.0)
            if x == 0:
                total = total + from_x_ref[c * size_y : (c + 1) * size_y]
            total = total + jnp.where(lane == 0, turned(face, -(PACK * c + x)), 0.0)
            gas_ref[c, x] = total


def per_device(gas_field, velocity, fraction, response, cell_index, brick_index, crossing):
    comps, size_x, size_y, size_z = gas_field.shape
    nblocks = velocity.shape[0]
    loading = 0.5 * size_x * size_y * size_z / (nblocks * 128)
    velocity = jnp.transpose(velocity, (1, 0, 2))
    fraction = jnp.transpose(fraction, (1, 0, 2))

    (face,) = call(pack_face_kernel, [(size_y, LANES)], gas_field)
    face = moved_along(face, "gz", -1)
    plane = jnp.concatenate([gas_field[:, 0].reshape(comps * size_y, LANES), face], axis=0)
    from_x = moved_along(plane, "gx", -1)
    rows = -(-(comps * size_x + comps + 1) // 8) * 8
    (lines,) = call(halo_y_kernel, [(rows, LANES)], gas_field, face, from_x)
    from_y = moved_inside(lines, "gy", -1)

    grid_rows = HEAD + 2 * comps * (size_x + 1) * ROWS_Y
    moved, base, to_y, to_x, to_z, leaving = call(
        functools.partial(step_kernel, loading),
        [
            (comps, nblocks, LANES),
            (comps, size_x, size_y, LANES),
            (comps * ROWS_Y, LANES),
            (comps * size_y, LANES),
            (size_y, LANES),
            (6, 7, crossing.shape[1], LANES),
        ],
        brick_index, crossing, gas_field, face, from_x, from_y, velocity, fraction, response, cell_index,
        smem=(0, 1),
        scratch=(
            pltpu.VMEM((grid_rows, LANES), jnp.float32),
            pltpu.VMEM((grid_rows, LANES), jnp.float32),
            pltpu.VMEM((BX + 1, nblocks, LANES), jnp.float32),
            pltpu.VMEM((9, nblocks, LANES), jnp.float32),
            pltpu.VMEM((comps, nblocks, LANES), jnp.float32),
        ),
    )

    def flat(array):
        return array.reshape(-1, LANES)

    def joined(*arrays):
        return jnp.concatenate([flat(array) for array in arrays], axis=0)

    count = flat(leaving[0]).shape[0]
    got_y = moved_inside(joined(to_y, leaving[2]), "gy", 1)
    got_my = moved_inside(leaving[3], "gy", -1)
    got_mz = moved_along(leaving[5], "gz", -1)
    edge = comps * size_y
    x_part, z_part = call(
        functools.partial(relay_x_kernel, size_x, size_y, comps),
        [(edge + size_y, LANES), (size_y, LANES)],
        got_y, jnp.concatenate([to_x, to_z], axis=0), to_z,
    )
    if lax.axis_size("gx") == 2:
        got_x = moved_along(joined(x_part, leaving[0], leaving[1]), "gx", 1)
        got_mx = got_x[edge + size_y + count :]
    else:
        got_x = moved_along(joined(x_part, leaving[0]), "gx", 1)
        got_mx = moved_along(leaving[1], "gx", -1)
    (z_part,) = call(functools.partial(relay_z_kernel, size_x, comps, edge), [(size_y, LANES)], got_x, z_part)
    got_z = moved_along(joined(z_part, leaving[4]), "gz", 1)
    (gas_next,) = call(finish_kernel, [gas_field.shape], base, got_y[: comps * ROWS_Y], got_x[:edge], got_z[:size_y])

    low = lax.axis_index("gy") == 0
    high = lax.axis_index("gy") == lax.axis_size("gy") - 1
    parts = [
        got_x[edge + size_y : edge + size_y + count],
        got_mx,
        jnp.where(low, 0.0, got_y[comps * ROWS_Y :]),
        jnp.where(high, 0.0, flat(got_my)),
        got_z[size_y:],
        got_mz,
    ]
    arrivals = jnp.stack([part.reshape(7, -1, LANES) for part in parts], axis=0)
    return gas_next, jnp.transpose(moved, (1, 0, 2)), jnp.transpose(arrivals, (0, 2, 1, 3))


def solution(mesh):
    owner = ("gx", "gz", "gy")
    in_specs = (
        P(None, "gx", "gy", "gz"),
        P(owner, None, None),
        P(owner, None, None),
        P(owner, None),
        P(owner, None),
        P(owner),
        P(owner, None),
    )
    out_specs = (
        P(None, "gx", "gy", "gz"),
        P(owner, None, None),
        P(owner, None, None, None),
    )
    return jax.shard_map(
        per_device, mesh=mesh, in_specs=in_specs, out_specs=out_specs, check_vma=False
    )
```

```python
import functools

import jax
import jax.numpy as jnp
from jax import lax
from jax.experimental import pallas as pl
from jax.experimental.pallas import tpu as pltpu
from jax.sharding import PartitionSpec as P

BX = 4
BY = 4
BZ = 8

TIME_STEP = 0.25
VISCOSITY = 0.4

LANES = 128
PACK = 32
HEAD = 8
ROWS_Y = 24
REACH_X = BX + 1
REACH_Y = 8
UNROLL = 8

LOW, HIGH, WEIGHT, ALONG_Y, IN_Y, IN_Z = 0, 5, 10, 15, 16, 17
LOW_MAIN, LOW_REST, HIGH_MAIN, HIGH_REST, RATE, MOVING = 18, 19, 20, 21, 22, 23
TABLE_ROWS = 26

VMEM = pl.BlockSpec(memory_space=pltpu.VMEM)
SMEM = pl.BlockSpec(memory_space=pltpu.SMEM)


def moved_along(block, axis, distance):
    count = lax.axis_size(axis)
    return lax.ppermute(block, axis, [(i, (i + distance) % count) for i in range(count)])


def swapped(blocks, axis, periodic):
    count = lax.axis_size(axis)
    first = [(i, i ^ 1) for i in range(count)]
    second = [(i, (((i + 1) ^ 1) - 1) % count) for i in range(count)]
    if not periodic:
        second[0], second[-1] = (0, 0), (count - 1, count - 1)
    return lax.ppermute(blocks[0], axis, first), lax.ppermute(blocks[1], axis, second)


def moved_diagonally(block, distance):
    nx, nz = lax.axis_size("gx"), lax.axis_size("gz")
    route = [(i * nz + k, (i + distance) % nx * nz + (k + distance) % nz) for i in range(nx) for k in range(nz)]
    return lax.ppermute(block, ("gx", "gz"), route)


def call(body, outs, *operands, smem=(), smem_outs=(), scratch=(), aliases=None, cycles=0):
    return pl.pallas_call(
        body,
        out_shape=[o if isinstance(o, jax.ShapeDtypeStruct) else jax.ShapeDtypeStruct(o, jnp.float32) for o in outs],
        in_specs=[SMEM if i in smem else VMEM for i in range(len(operands))],
        out_specs=[SMEM if i in smem_outs else VMEM for i in range(len(outs))],
        scratch_shapes=list(scratch),
        input_output_aliases=aliases or {},
        compiler_params=pltpu.CompilerParams(vmem_limit_bytes=40 * 1024 * 1024),
        cost_estimate=pl.CostEstimate(flops=cycles * 4096, bytes_accessed=cycles * 1024, transcendentals=0),
    )(*operands)


def lane_ids(rows):
    return lax.broadcasted_iota(jnp.int32, (rows, LANES), 1)


def row_ids(rows):
    return lax.broadcasted_iota(jnp.int32, (rows, LANES), 0)


def turned(value, shift):
    shift = shift % LANES
    return pltpu.roll(value, shift, 1) if shift else value


def row_of(sel, c, x, comps, size_x):
    return HEAD + ((sel * comps + c) * (size_x + 1) + x) * ROWS_Y


def odd(axis):
    return lax.axis_index(axis) % 2


def pack_face_kernel(gas_ref, face_ref):
    comps, size_x, size_y, _ = gas_ref.shape
    lane = lane_ids(size_y)
    face = jnp.zeros((size_y, LANES), jnp.float32)
    for c in range(comps):
        for x in range(size_x):
            place = PACK * c + x
            face = jnp.where(lane == place, turned(gas_ref[c, x], place), face)
    face_ref[...] = face


def prepare_kernel(
    gas_ref, velocity_ref, fraction_ref, response_ref, cell_ref, brick_ref,
    grid_ref, deposit_ref, table_ref, list_ref,
):
    comps, size_x, size_y, size_z = gas_ref.shape
    nblocks = velocity_ref.shape[1]
    count_y, count_z = size_y // BY, size_z // BZ
    spare = table_ref.shape[1] - nblocks

    cells = cell_ref[...]
    cell_x, cell_y, cell_z = cells // (BY * BZ), cells // BZ % BY, cells % BZ
    along_x, along_z = fraction_ref[0], fraction_ref[2]
    low, high = 1.0 - along_z, along_z

    def put(row, value):
        table_ref[row, 0:nblocks] = value
        table_ref[row, nblocks : nblocks + spare] = jnp.zeros((spare, LANES), jnp.float32)

    for a in range(REACH_X):
        weight = jnp.where(cell_x == a, 1.0 - along_x, 0.0) + jnp.where(cell_x == a - 1, along_x, 0.0)
        put(LOW + a, weight * low)
        put(HIGH + a, weight * high)
        put(WEIGHT + a, weight)
    put(ALONG_Y, fraction_ref[1])
    put(IN_Y, cell_y.astype(jnp.float32))
    put(IN_Z, cell_z.astype(jnp.float32))
    low_main = low.astype(jnp.bfloat16).astype(jnp.float32)
    high_main = high.astype(jnp.bfloat16).astype(jnp.float32)
    put(LOW_MAIN, low_main)
    put(LOW_REST, low - low_main)
    put(HIGH_MAIN, high_main)
    put(HIGH_REST, high - high_main)
    put(RATE, 1.0 / response_ref[...])
    for c in range(comps):
        put(MOVING + c, velocity_ref[c])

    room = nblocks + UNROLL

    def visit(k, counts):
        brick = brick_ref[k]
        brick_x = brick // (count_y * count_z)
        brick_y = brick // count_z % count_y
        brick_z = brick % count_z
        sel = jnp.where(brick_z == count_z - 1, 1, 0)
        late = jnp.where(brick_y == count_y - 1, 1, 0)
        at = jnp.where(late == 1, room + counts[1], counts[0])
        list_ref[0, at] = k
        list_ref[1, at] = HEAD + (sel * comps * (size_x + 1) + brick_x * BX) * ROWS_Y + brick_y * BY
        list_ref[2, at] = brick_z * BZ
        return counts[0] + 1 - late, counts[1] + late

    early, late = lax.fori_loop(0, nblocks, visit, (jnp.int32(0), jnp.int32(0)))
    for base, count in ((0, early), (room, late)):
        for u in range(UNROLL):
            list_ref[0, base + count + u] = nblocks
            list_ref[1, base + count + u] = HEAD
            list_ref[2, base + count + u] = 0
    list_ref[0, 2 * room] = early
    list_ref[0, 2 * room + 1] = late

    zeros = jnp.zeros((8, LANES), jnp.float32)
    grid_ref[0:HEAD] = zeros
    for c in range(comps):
        for x in range(size_x + 1):
            for sel in (0, 1):
                at = row_of(sel, c, x, comps, size_x)
                if x < size_x and sel == 0:
                    grid_ref[at : at + size_y] = gas_ref[c, x]
                grid_ref[at + size_y : at + ROWS_Y] = zeros
    deposit_ref[...] = jnp.zeros_like(deposit_ref)


def halo_xz_kernel(gas_ref, grid_in_ref, face_ref, from_x_ref, edge_ref, grid_ref, lines_ref):
    comps, size_x, size_y, _ = gas_ref.shape
    first_lane = lane_ids(size_y) == 0
    for c in range(comps):
        for x in range(size_x + 1):
            if x < size_x:
                plane, far = gas_ref[c, x], turned(face_ref[...], -(PACK * c + x))
                lines_ref[c * size_x + x : c * size_x + x + 1] = gas_ref[c, x, 0:1]
            else:
                plane = from_x_ref[c * size_y : (c + 1) * size_y]
                far = turned(edge_ref[...], -PACK * c)
                at = row_of(0, c, x, comps, size_x)
                grid_ref[at : at + size_y] = plane
                lines_ref[comps * size_x + c : comps * size_x + c + 1] = plane[0:1]
            at = row_of(1, c, x, comps, size_x)
            grid_ref[at : at + size_y] = jnp.where(first_lane, far, plane)
    line = jnp.where(lane_ids(8) % PACK == size_x, turned(edge_ref[0:8], size_x), face_ref[0:8])
    lines_ref[comps * size_x + comps : comps * size_x + comps + 1] = line[0:1]


def halo_y_kernel(comps, size_x, size_y, grid_in_ref, first_ref, second_ref, grid_ref):
    inside = lax.axis_index("gy") != lax.axis_size("gy") - 1
    even = odd("gy") == 0
    kept = (row_ids(8) == 0) & inside
    first_lane = lane_ids(8) == 0
    zeros = jnp.zeros((8, LANES), jnp.float32)

    def line_at(row):
        line = jnp.where(even, first_ref[row : row + 1], second_ref[row : row + 1])
        return jnp.broadcast_to(line, (8, LANES))

    corner = line_at(comps * size_x + comps)
    for c in range(comps):
        for x in range(size_x + 1):
            line = line_at(c * size_x + x if x < size_x else comps * size_x + c)
            at = row_of(0, c, x, comps, size_x) + size_y
            grid_ref[at : at + 8] = jnp.where(kept, line, zeros)
            at = row_of(1, c, x, comps, size_x) + size_y
            far = turned(corner, -(PACK * c + x))
            grid_ref[at : at + 8] = jnp.where(kept, jnp.where(first_lane, far, line), zeros)


def offsets_of(comps, size_x):
    return [(c * (size_x + 1) + a) * ROWS_Y for c in range(comps) for a in range(REACH_X)]


def weight_y_of(table_ref, k):
    along, inside = table_ref[ALONG_Y, pl.ds(k, 1)], table_ref[IN_Y, pl.ds(k, 1)]
    row = row_ids(REACH_Y).astype(jnp.float32)
    return jnp.where(row == inside, 1.0 - along, 0.0) + jnp.where(row == inside + 1.0, along, 0.0)


def drag_kernel(late, size_x, list_ref, grid_ref, table_ref, *refs):
    moved_ref, drag_ref = refs[-2:]
    comps, room = moved_ref.shape[0], (list_ref.shape[1] - 2) // 2
    offsets = offsets_of(comps, size_x)

    def one(k, start, first_z):
        def row(i):
            return table_ref[i, pl.ds(k, 1)]

        place = row(IN_Z).astype(jnp.int32) + first_z
        place = jnp.broadcast_to(place, (REACH_Y, LANES))
        after = (place + 1) % LANES
        low = [row(LOW + a) for a in range(REACH_X)]
        high = [row(HIGH + a) for a in range(REACH_X)]
        weight_y = weight_y_of(table_ref, k)
        rate = row(RATE)
        for c in range(comps):
            total = None
            for a in range(REACH_X):
                window = grid_ref[pl.ds(start + offsets[c * REACH_X + a], REACH_Y)]
                near = jnp.take_along_axis(window, place, axis=1, mode="promise_in_bounds") * low[a]
                far = jnp.take_along_axis(window, after, axis=1, mode="promise_in_bounds") * high[a]
                total = near + far if total is None else total + (near + far)
            gas_sample = jnp.sum(total * weight_y, axis=0, keepdims=True)
            moving = row(MOVING + c)
            drag = (gas_sample - moving) * rate
            moved_ref[c, pl.ds(k, 1)] = moving + TIME_STEP * drag
            drag_ref[c, pl.ds(k, 1)] = drag

    count = list_ref[0, 2 * room + late]

    @pl.loop(0, (count + UNROLL - 1) // UNROLL)
    def _(group):
        for u in range(UNROLL):
            at = late * room + group * UNROLL + u
            one(list_ref[0, at], list_ref[1, at], list_ref[2, at])


def deposit_kernel(late, size_x, list_ref, table_ref, drag_ref, deposit_in_ref, deposit_ref):
    comps, room = drag_ref.shape[0], (list_ref.shape[1] - 2) // 2
    offsets = offsets_of(comps, size_x)
    packed_z = row_ids(16).astype(jnp.float32).astype(jnp.bfloat16)

    def tall(value):
        return jnp.broadcast_to(value, (16, LANES)).astype(jnp.bfloat16)

    def shares_of(k, first_z):
        def row(i):
            return table_ref[i, pl.ds(k, 1)]

        place = row(IN_Z) + first_z.astype(jnp.float32)
        after = place + 1.0
        after = jnp.where(after == float(LANES), 0.0, after)
        place, after = tall(place), tall(after)
        low_main, low_rest, high_main, high_rest = [tall(row(LOW_MAIN + i)) for i in range(4)]
        nothing = jnp.zeros((16, LANES), jnp.bfloat16)
        main, rest = [], []
        for j in range(LANES // 16):
            here = packed_z + jnp.bfloat16(16 * j)
            at_low, at_high = here == place, here == after
            main.append(jnp.where(at_low, low_main, jnp.where(at_high, high_main, nothing)))
            rest.append(jnp.where(at_low, low_rest, jnp.where(at_high, high_rest, nothing)))
        both = jnp.concatenate(main + rest, axis=0)
        table = jnp.concatenate([both, both], axis=1)
        weight_x = [row(WEIGHT + a) for a in range(REACH_X)]
        weight_y = weight_y_of(table_ref, k)
        pushed = []
        for c in range(comps):
            spread = drag_ref[c, pl.ds(k, 1)] * weight_y
            pushed.extend(spread * weight_x[a] for a in range(REACH_X))
        pushed = jnp.concatenate(pushed, axis=0)
        top = pushed.astype(jnp.bfloat16)
        pushed = jnp.concatenate([top, (pushed - top.astype(jnp.float32)).astype(jnp.bfloat16)], axis=1)
        shares = lax.dot_general(pushed, table, (((1,), (1,)), ((), ())), preferred_element_type=jnp.float32)
        return shares[:, :LANES] + shares[:, LANES:]

    count = list_ref[0, 2 * room + late]

    @pl.loop(0, (count + UNROLL - 1) // UNROLL)
    def _(group):
        at = late * room + group * UNROLL
        shares = [shares_of(list_ref[0, at + u], list_ref[2, at + u]) for u in range(UNROLL)]
        for u in range(UNROLL):
            start = list_ref[1, at + u]
            for i, o in enumerate(offsets):
                spot = pl.ds(start + o, REACH_Y)
                deposit_ref[spot] = deposit_ref[spot] + shares[u][i * REACH_Y : (i + 1) * REACH_Y]


def leave_kernel(crossing_ref, moved_ref, fraction_ref, response_ref, out_ref, velocity_ref):
    comps, nblocks = fraction_ref.shape[:2]
    velocity_ref[...] = moved_ref[:, 0:nblocks]
    for face in range(6):
        for slot in range(crossing_ref.shape[1]):
            block = crossing_ref[face, slot]
            live = block >= 0
            spot = pl.ds(jnp.maximum(block, 0), 1)
            state = [moved_ref[c, spot] for c in range(comps)]
            state = state + [fraction_ref[c, spot] + TIME_STEP * state[c] for c in range(comps)]
            state.append(response_ref[spot])
            for i, value in enumerate(state):
                out_ref[face, i, slot : slot + 1] = jnp.where(live, value, 0.0)


def send_kernel(push, diffuse, size_x, size_y, comps, grid_ref, deposit_ref, leaving_ref, y_ref, x_ref, z_ref):
    rows = leaving_ref.shape[1]
    up = odd("gy")
    y_ref[up, 0:rows] = leaving_ref[2]
    y_ref[1 - up, 0:rows] = leaving_ref[3]
    y_ref[1 - up, rows:] = jnp.zeros((y_ref.shape[1] - rows, LANES), jnp.float32)
    lane = lane_ids(ROWS_Y)
    face = jnp.zeros((ROWS_Y, LANES), jnp.float32)
    for c in range(comps):
        for x in range(size_x + 1):
            at, wrap = row_of(0, c, x, comps, size_x), row_of(1, c, x, comps, size_x)
            beyond = push * deposit_ref[wrap : wrap + ROWS_Y]
            line = slice(at + size_y, at + size_y + 1)
            line = push * deposit_ref[line] + jnp.where(lane_ids(1) == 0, 0.0, beyond[size_y : size_y + 1])
            if x < size_x:
                line = line + diffuse * grid_ref[at + size_y - 1 : at + size_y]
                behind = diffuse * turned(grid_ref[at : at + size_y], 1)
                beyond = jnp.concatenate([beyond[:size_y] + behind, beyond[size_y:]], axis=0)
            else:
                here = grid_ref[at - ROWS_Y : at - ROWS_Y + size_y]
                total = push * deposit_ref[at : at + size_y] + jnp.where(lane_ids(size_y) == 0, 0.0, beyond[:size_y])
                x_ref[c * size_y : (c + 1) * size_y] = diffuse * here + total
            y_ref[up, rows + c * ROWS_Y + x : rows + c * ROWS_Y + x + 1] = line
            place = PACK * c + x
            face = jnp.where(lane == place, turned(beyond, place), face)
    z_ref[...] = face[:size_y]
    y_ref[up, rows + size_x + 1 : rows + size_x + 2] = face[size_y : size_y + 1]


def base_kernel(push, diffuse, grid_ref, deposit_ref, base_ref):
    comps, size_x, size_y, _ = base_ref.shape
    first_lane = lane_ids(size_y) == 0
    for c in range(comps):
        for x in range(size_x):
            at, wrap = row_of(0, c, x, comps, size_x), row_of(1, c, x, comps, size_x)
            here = grid_ref[at : at + size_y]
            laplace = grid_ref[at + ROWS_Y : at + ROWS_Y + size_y]
            if x:
                laplace = laplace + grid_ref[at - ROWS_Y : at - ROWS_Y + size_y]
            laplace = laplace + grid_ref[at + 1 : at + 1 + size_y] + grid_ref[at - 1 : at - 1 + size_y]
            ahead = turned(grid_ref[wrap : wrap + size_y], -1)
            laplace = laplace + ahead + jnp.where(first_lane, 0.0, turned(here, 1)) - 6.0 * here
            total = deposit_ref[at : at + size_y] + jnp.where(first_lane, 0.0, deposit_ref[wrap : wrap + size_y])
            base_ref[c, x] = here + diffuse * laplace + push * total


def below(first_ref, second_ref, rows):
    got = jnp.where(odd("gy") == 1, first_ref[rows], second_ref[rows])
    return jnp.where(lax.axis_index("gy") != 0, got, 0.0)


def relay_kernel(size_x, size_y, comps, count, first_ref, second_ref, x_in_ref, z_in_ref, leaving_ref, x_ref, z_ref, edge_ref):
    edge = comps * size_y
    x_ref[0:edge] = x_in_ref[...]
    for c in range(comps):
        at = count + c * ROWS_Y + size_x
        spot = slice(c * size_y, c * size_y + 1)
        x_ref[spot] = x_in_ref[spot] + below(first_ref, second_ref, slice(at, at + 1))
    x_ref[edge : edge + count] = leaving_ref[0]
    if x_ref.shape[0] > edge + count:
        x_ref[edge + count : edge + 2 * count] = leaving_ref[1]
    at = count + size_x + 1
    edge_ref[...] = z_in_ref[...]
    edge_ref[0:1] = z_in_ref[0:1] + below(first_ref, second_ref, slice(at, at + 1))
    up = odd("gz")
    z_ref[up, 0:count] = leaving_ref[4]
    z_ref[up, count : count + size_y] = edge_ref[...]
    z_ref[1 - up, 0:count] = leaving_ref[5]
    z_ref[1 - up, count : count + size_y] = jnp.zeros((size_y, LANES), jnp.float32)


def finish_kernel(count, base_ref, y1_ref, y2_ref, x_ref, z1_ref, z2_ref, edge_ref, gas_ref):
    comps, size_x, size_y, _ = base_ref.shape
    first_row, first_lane = row_ids(size_y) == 0, lane_ids(size_y) == 0
    rows = slice(count, count + size_y)
    face = jnp.where(odd("gz") == 1, z1_ref[rows], z2_ref[rows])
    corner = edge_ref[...]
    for c in range(comps):
        for x in range(size_x):
            at = count + c * ROWS_Y + x
            line = jnp.broadcast_to(below(y1_ref, y2_ref, slice(at, at + 1)), (size_y, LANES))
            total = base_ref[c, x] + jnp.where(first_row, line, 0.0)
            far = turned(face, -(PACK * c + x))
            if x == 0:
                total = total + x_ref[c * size_y : (c + 1) * size_y]
                far = far + turned(corner, -(PACK * c + size_x))
            gas_ref[c, x] = total + jnp.where(first_lane, far, 0.0)


def per_device(gas_field, velocity, fraction, response, cell_index, brick_index, crossing):
    comps, size_x, size_y, size_z = gas_field.shape
    nblocks = velocity.shape[0]
    loading = 0.5 * size_x * size_y * size_z / (nblocks * 128)
    push, diffuse = -TIME_STEP * loading, TIME_STEP * VISCOSITY
    velocity = jnp.transpose(velocity, (1, 0, 2))
    fraction = jnp.transpose(fraction, (1, 0, 2))
    grid_rows = HEAD + 2 * comps * (size_x + 1) * ROWS_Y
    spare = nblocks + 8

    (face,) = call(pack_face_kernel, [(size_y, LANES)], gas_field)
    plane = gas_field[:, 0].reshape(comps * size_y, LANES)
    from_z = moved_along(face, "gz", -1)
    from_x = moved_along(plane, "gx", -1)
    from_xz = moved_diagonally(face, -1)
    grid, deposit, table, blocks = call(
        prepare_kernel,
        [
            (grid_rows, LANES),
            (grid_rows, LANES),
            (TABLE_ROWS, spare, LANES),
            jax.ShapeDtypeStruct((3, 2 * (nblocks + UNROLL) + 2), jnp.int32),
        ],
        gas_field, velocity, fraction, response, cell_index, brick_index,
        smem=(5,), smem_outs=(3,), cycles=3000,
    )
    line_rows = -(-(comps * size_x + comps + 1) // 8) * 8
    grid, lines = call(
        halo_xz_kernel, [(grid_rows, LANES), (line_rows, LANES)], gas_field, grid, from_z, from_x, from_xz,
        aliases={1: 0},
    )
    y1, y2 = swapped((lines, lines), "gy", False)

    rows_shape = (comps, spare, LANES)
    moved, drag = call(
        functools.partial(drag_kernel, 0, size_x), [rows_shape, rows_shape], blocks, grid, table,
        smem=(0,), cycles=6000,
    )
    deposit = call(
        functools.partial(deposit_kernel, 0, size_x), [(grid_rows, LANES)], blocks, table, drag, deposit,
        smem=(0,), aliases={3: 0}, cycles=6000,
    )[0]
    (grid,) = call(
        functools.partial(halo_y_kernel, comps, size_x, size_y), [(grid_rows, LANES)], grid, y1, y2,
        aliases={0: 0},
    )
    moved, drag = call(
        functools.partial(drag_kernel, 1, size_x), [rows_shape, rows_shape], blocks, grid, table, moved, drag,
        smem=(0,), aliases={3: 0, 4: 1}, cycles=2000,
    )
    deposit = call(
        functools.partial(deposit_kernel, 1, size_x), [(grid_rows, LANES)], blocks, table, drag, deposit,
        smem=(0,), aliases={3: 0}, cycles=2000,
    )[0]

    slots = crossing.shape[1]
    leaving, velocity_next = call(
        leave_kernel, [(6, 7, slots, LANES), (comps, nblocks, LANES)], crossing, moved, fraction, response,
        smem=(0,), cycles=1000,
    )
    count = 7 * slots
    leaving = leaving.reshape(6, count, LANES)
    to_y, to_x, to_z = call(
        functools.partial(send_kernel, push, diffuse, size_x, size_y, comps),
        [(2, count + comps * ROWS_Y, LANES), (comps * size_y, LANES), (size_y, LANES)],
        grid, deposit, leaving, cycles=1000,
    )
    y1, y2 = swapped((to_y[0], to_y[1]), "gy", False)
    (base,) = call(
        functools.partial(base_kernel, push, diffuse), [gas_field.shape], grid, deposit, cycles=2000,
    )
    edge = comps * size_y
    both = lax.axis_size("gx") == 2
    to_x, to_z, to_xz = call(
        functools.partial(relay_kernel, size_x, size_y, comps, count),
        [(edge + (2 if both else 1) * count, LANES), (2, count + size_y, LANES), (size_y, LANES)],
        y1, y2, to_x, to_z, leaving,
    )
    got_x = moved_along(to_x, "gx", 1)
    z1, z2 = swapped((to_z[0], to_z[1]), "gz", True)
    got_xz = moved_diagonally(to_xz, 1)
    got_mx = got_x[edge + count :] if both else moved_along(leaving[1], "gx", -1)
    (gas_next,) = call(
        functools.partial(finish_kernel, count), [gas_field.shape], base, y1, y2, got_x, z1, z2, got_xz,
    )

    j, k = lax.axis_index("gy"), lax.axis_index("gz")
    last = lax.axis_size("gy") - 1
    y1, y2, z1, z2 = y1[:count], y2[:count], z1[:count], z2[:count]
    parts = [
        got_x[edge : edge + count],
        got_mx,
        jnp.where(j == 0, 0.0, jnp.where(j % 2 == 1, y1, y2)),
        jnp.where(j == last, 0.0, jnp.where(j % 2 == 1, y2, y1)),
        jnp.where(k % 2 == 1, z1, z2),
        jnp.where(k % 2 == 1, z2, z1),
    ]
    arrivals = jnp.stack([part.reshape(7, slots, LANES) for part in parts], axis=0)
    return gas_next, jnp.transpose(velocity_next, (1, 0, 2)), jnp.transpose(arrivals, (0, 2, 1, 3))


def solution(mesh):
    owner = ("gx", "gz", "gy")
    in_specs = (
        P(None, "gx", "gy", "gz"),
        P(owner, None, None),
        P(owner, None, None),
        P(owner, None),
        P(owner, None),
        P(owner),
        P(owner, None),
    )
    out_specs = (
        P(None, "gx", "gy", "gz"),
        P(owner, None, None),
        P(owner, None, None, None),
    )
    return jax.shard_map(
        per_device, mesh=mesh, in_specs=in_specs, out_specs=out_specs, check_vma=False
    )
```

```python
import functools

import jax
import jax.numpy as jnp
from jax import lax
from jax.experimental import pallas as pl
from jax.experimental.pallas import tpu as pltpu
from jax.sharding import PartitionSpec as P

BX = 4
BY = 4
BZ = 8

TIME_STEP = 0.25
VISCOSITY = 0.4

LANES = 128
PACK = 32
ROWS_Y = 24
REACH_X = BX + 1
REACH_Y = 8
SPREAD = REACH_X * REACH_Y
REACH_Z = 2 * BZ
UNROLL = 8

WEIGHT, ALONG_Y, IN_Y, ALONG_Z, IN_Z, RATE, MOVING, OFFSET = 0, 5, 6, 7, 8, 9, 10, 13
TABLE_ROWS = 16
STATE = 8

VMEM = pl.BlockSpec(memory_space=pltpu.VMEM)
SMEM = pl.BlockSpec(memory_space=pltpu.SMEM)
HBM = pl.BlockSpec(memory_space=pltpu.HBM)


def moved_along(block, axis, distance):
    count = lax.axis_size(axis)
    return lax.ppermute(block, axis, [(i, (i + distance) % count) for i in range(count)])


def swapped(blocks, axis, periodic):
    count = lax.axis_size(axis)
    first = [(i, i ^ 1) for i in range(count)]
    second = [(i, (((i + 1) ^ 1) - 1) % count) for i in range(count)]
    if not periodic:
        second[0], second[-1] = (0, 0), (count - 1, count - 1)
    return lax.ppermute(blocks[0], axis, first), lax.ppermute(blocks[1], axis, second)


def moved_diagonally(block, distance):
    nx, nz = lax.axis_size("gx"), lax.axis_size("gz")
    route = [(i * nz + k, (i + distance) % nx * nz + (k + distance) % nz) for i in range(nx) for k in range(nz)]
    return lax.ppermute(block, ("gx", "gz"), route)


def call(body, outs, *operands, smem=(), hbm=(), smem_outs=(), scratch=(), aliases=None, cycles=0):
    return pl.pallas_call(
        body,
        out_shape=[o if isinstance(o, jax.ShapeDtypeStruct) else jax.ShapeDtypeStruct(o, jnp.float32) for o in outs],
        in_specs=[SMEM if i in smem else HBM if i in hbm else VMEM for i in range(len(operands))],
        out_specs=[SMEM if i in smem_outs else VMEM for i in range(len(outs))],
        scratch_shapes=list(scratch),
        input_output_aliases=aliases or {},
        compiler_params=pltpu.CompilerParams(vmem_limit_bytes=40 * 1024 * 1024),
        cost_estimate=pl.CostEstimate(flops=cycles * 4096, bytes_accessed=cycles * 1024, transcendentals=0),
    )(*operands)


def lane_ids(rows):
    return lax.broadcasted_iota(jnp.int32, (rows, LANES), 1)


def row_ids(rows):
    return lax.broadcasted_iota(jnp.int32, (rows, LANES), 0)


def turned(value, shift):
    shift = shift % LANES
    return pltpu.roll(value, shift, 1) if shift else value


def odd(axis):
    return lax.axis_index(axis) % 2


def begin_kernel(gas_ref, grid_ref, face_ref, plane_ref, sem):
    comps, size_x, size_y, _ = gas_ref.shape
    copy = pltpu.make_async_copy(gas_ref, grid_ref.at[:, 1 : size_x + 1, 0:size_y], sem)
    copy.start()
    zeros = jnp.zeros((ROWS_Y, LANES), jnp.float32)
    for c in range(comps):
        grid_ref[c, 0] = zeros
        grid_ref[c, size_x + 1] = zeros
        for x in range(size_x):
            grid_ref[c, x + 1, size_y:] = zeros[size_y:]
    copy.wait()
    lane = lane_ids(size_y)
    face = jnp.zeros((size_y, LANES), jnp.float32)
    for c in range(comps):
        plane_ref[c * size_y : (c + 1) * size_y] = grid_ref[c, 1, 0:size_y]
        for x in range(size_x):
            place = PACK * c + x
            face = jnp.where(lane == place, turned(grid_ref[c, x + 1, 0:size_y], place), face)
    face_ref[...] = face


def parts_of(value):
    main = value.astype(jnp.bfloat16).astype(jnp.float32)
    return main, value - main


def lay_out(grid_ref, lines_ref, p, q, size_y, size_z):
    comps = grid_ref.shape[0]
    rows_z = size_z + 8
    count_y = size_y // BY
    for c in range(comps):
        planes = [grid_ref[c, p * BX + a + 1, q * BY : q * BY + REACH_Y] for a in range(REACH_X)]
        main, rest = parts_of(jnp.concatenate(planes, axis=0))
        stack = jnp.concatenate([main, rest, main, jnp.zeros((LANES - 3 * SPREAD, LANES), jnp.float32)], axis=0)
        at = ((p * count_y + q) * comps + c) * rows_z
        lines_ref[at : at + size_z] = jnp.transpose(stack)


def lay_out_top(turned_ref, lines_ref, q, comps, count_x, count_y, size_z):
    lane = lane_ids(count_x)
    rows_z = size_z + 8
    for c in range(comps):
        total = jnp.zeros((count_x, LANES), jnp.float32)
        for a in range(REACH_X):
            rows = turned_ref[pl.ds(PACK * c + a, count_x, stride=BX)]
            total = jnp.where(lane // REACH_Y == a, turned(rows, a * REACH_Y - q * BY), total)
        main, rest = parts_of(total)
        line = main + turned(rest, SPREAD) + turned(main, 2 * SPREAD)
        for p in range(count_x):
            at = ((p * count_y + q) * comps + c) * rows_z + size_z
            lines_ref[at : at + 1] = line[p : p + 1]


def prepare_kernel(
    grid_ref, velocity_hbm, fraction_hbm, response_hbm, cell_hbm, brick_ref,
    lines_ref, deposit_ref, table_ref, state_ref, list_ref,
    velocity_ref, fraction_ref, response_ref, cell_ref, sems,
):
    pairs = [(velocity_hbm, velocity_ref), (fraction_hbm, fraction_ref), (response_hbm, response_ref), (cell_hbm, cell_ref)]
    copies = [pltpu.make_async_copy(source, target, sems.at[i]) for i, (source, target) in enumerate(pairs)]
    for copy in copies:
        copy.start()
    comps, size_x, size_y, size_z = grid_ref.shape[0], grid_ref.shape[1] - 2, grid_ref.shape[2] - 8, grid_ref.shape[3]
    nblocks = velocity_ref.shape[1]
    count_x, count_y, count_z = size_x // BX, size_y // BY, size_z // BZ
    rows_z = size_z + 8
    spare = table_ref.shape[1] - nblocks

    room = nblocks + UNROLL

    def visit(k, counts):
        brick = brick_ref[k]
        brick_x = brick // (count_y * count_z)
        brick_y = brick // count_z % count_y
        brick_z = brick % count_z
        sel = jnp.where(brick_z == count_z - 1, 1, 0)
        late = jnp.where(brick_y == count_y - 1, 1, 0)
        at = jnp.where(late == 1, room + counts[1], counts[0])
        list_ref[0, at] = k
        list_ref[1, at] = (sel * comps * (size_x + 1) + brick_x * BX) * ROWS_Y + brick_y * BY
        list_ref[2, at] = (brick_x * count_y + brick_y) * comps * rows_z + brick_z * BZ
        list_ref[3, at] = brick_z * BZ
        return counts[0] + 1 - late, counts[1] + late

    early, late = lax.fori_loop(0, nblocks, visit, (jnp.int32(0), jnp.int32(0)))
    for base, count in ((0, early), (room, late)):
        for u in range(UNROLL):
            list_ref[0, base + count + u] = nblocks
            for i in (1, 2, 3):
                list_ref[i, base + count + u] = 0
    list_ref[0, 2 * room] = early
    list_ref[0, 2 * room + 1] = late

    deposit_ref[...] = jnp.zeros_like(deposit_ref)
    for p in range(count_x):
        for q in range(count_y):
            for c in range(comps):
                at = ((p * count_y + q) * comps + c) * rows_z + size_z
                lines_ref[at : at + 8] = jnp.zeros((8, LANES), jnp.float32)
    for p in range(count_x - 1):
        for q in range(count_y - 1):
            lay_out(grid_ref, lines_ref, p, q, size_y, size_z)

    for copy in copies:
        copy.wait()
    cells = cell_ref[...]
    cell_x, cell_y, cell_z = cells // (BY * BZ), cells // BZ % BY, cells % BZ
    along_x = fraction_ref[0]

    def put(row, value):
        table_ref[row, 0:nblocks] = value
        table_ref[row, nblocks : nblocks + spare] = jnp.zeros((spare, LANES), jnp.float32)

    for a in range(REACH_X):
        put(WEIGHT + a, jnp.where(cell_x == a, 1.0 - along_x, 0.0) + jnp.where(cell_x == a - 1, along_x, 0.0))
    put(ALONG_Y, fraction_ref[1])
    put(IN_Y, cell_y.astype(jnp.float32))
    put(ALONG_Z, fraction_ref[2])
    put(IN_Z, cell_z.astype(jnp.float32))
    put(RATE, 1.0 / response_ref[...])
    for c in range(comps):
        put(MOVING + c, velocity_ref[c])
        put(OFFSET + c, fraction_ref[c])
    state_ref[...] = jnp.zeros_like(state_ref)
    state_ref[pl.ds(2 * comps, nblocks, stride=STATE)] = response_ref[...]


def y_lines_kernel(grid_ref, face_ref, from_x_ref, edge_ref, out_ref):
    comps, size_x = grid_ref.shape[0], grid_ref.shape[1] - 2
    size_y = face_ref.shape[0]
    for c in range(comps):
        out_ref[c * size_x : (c + 1) * size_x] = grid_ref[c, 1 : size_x + 1, 0]
        out_ref[comps * size_x + c : comps * size_x + c + 1] = from_x_ref[c * size_y : c * size_y + 1]
    line = jnp.where(lane_ids(8) % PACK == size_x, turned(edge_ref[0:8], size_x), face_ref[0:8])
    out_ref[comps * size_x + comps : comps * size_x + comps + 1] = line[0:1]


def halo_xz_kernel(grid_in_ref, lines_in_ref, face_ref, from_x_ref, edge_ref, grid_ref, lines_ref, top_ref, turned_ref):
    comps, size_x = grid_ref.shape[0], grid_ref.shape[1] - 2
    size_y, size_z = face_ref.shape[0], grid_ref.shape[3]
    count_x, count_y = size_x // BX, size_y // BY
    for c in range(comps):
        grid_ref[c, size_x + 1, 0:size_y] = from_x_ref[c * size_y : (c + 1) * size_y]
    for q in range(count_y - 1):
        lay_out(grid_ref, lines_ref, count_x - 1, q, size_y, size_z)
    top = jnp.where(lane_ids(size_y) % PACK == size_x, turned(edge_ref[...], size_x), face_ref[...])
    top_ref[0:size_y] = top
    top_ref[size_y:] = jnp.zeros((LANES - size_y, LANES), jnp.float32)
    turned_ref[...] = jnp.transpose(top_ref[...])
    for q in range(count_y - 1):
        lay_out_top(turned_ref, lines_ref, q, comps, count_x, count_y, size_z)


def halo_y_kernel(size_y, grid_in_ref, lines_in_ref, top_in_ref, first_ref, second_ref, grid_ref, lines_ref, turned_ref):
    comps, size_x, size_z = grid_ref.shape[0], grid_ref.shape[1] - 2, grid_ref.shape[3]
    count_x, count_y = size_x // BX, size_y // BY
    inside = lax.axis_index("gy") != lax.axis_size("gy") - 1
    even = odd("gy") == 0
    kept = (row_ids(8) == 0) & inside

    def line_at(row):
        line = jnp.where(even, first_ref[row : row + 1], second_ref[row : row + 1])
        return jnp.where(kept, jnp.broadcast_to(line, (8, LANES)), 0.0)

    for c in range(comps):
        for x in range(size_x + 1):
            grid_ref[c, x + 1, size_y:] = line_at(c * size_x + x if x < size_x else comps * size_x + c)
    for p in range(count_x):
        lay_out(grid_ref, lines_ref, p, count_y - 1, size_y, size_z)
    corner = line_at(comps * size_x + comps)
    rest = jnp.zeros((LANES - size_y - 8, LANES), jnp.float32)
    turned_ref[...] = jnp.transpose(jnp.concatenate([top_in_ref[0:size_y], corner, rest], axis=0))
    lay_out_top(turned_ref, lines_ref, count_y - 1, comps, count_x, count_y, size_z)


def blocks_kernel(late, comps, size_x, rows_z, list_ref, lines_ref, table_ref, state_in_ref, deposit_in_ref, state_ref, deposit_ref):
    room = (list_ref.shape[1] - 2) // 2
    row_y = row_ids(REACH_Y).astype(jnp.float32)
    row_z = row_ids(REACH_Z).astype(jnp.float32)
    lane = lane_ids(REACH_Y)

    def hat(rows, inside, along):
        return jnp.where(rows == inside, 1.0 - along, 0.0) + jnp.where(rows == inside + 1.0, along, 0.0)

    def shares_of(at):
        k = list_ref[0, at]

        def row(i):
            return table_ref[i, pl.ds(k, 1)]

        weight_y = hat(row_y, row(IN_Y), row(ALONG_Y))
        weight_z = hat(row_z, row(IN_Z), row(ALONG_Z))
        weight = jnp.concatenate([row(WEIGHT + a) * weight_y for a in range(REACH_X)], axis=0)
        main, rest = parts_of(weight)
        unused = jnp.zeros((LANES - 3 * SPREAD, LANES), jnp.float32)
        table = jnp.concatenate([main, main, rest, unused], axis=0).astype(jnp.bfloat16)
        first = pl.multiple_of(list_ref[2, at], 8)
        window = jnp.concatenate([lines_ref[pl.ds(first + c * rows_z, REACH_Z)] for c in range(comps)], axis=0)
        seen = lax.dot_general(
            window.astype(jnp.bfloat16), table, (((1,), (0,)), ((), ())), preferred_element_type=jnp.float32
        )
        rate = row(RATE)
        pushed = []
        for c in range(comps):
            gas_sample = jnp.sum(seen[c * REACH_Z : (c + 1) * REACH_Z] * weight_z, axis=0, keepdims=True)
            moving = row(MOVING + c)
            drag = (gas_sample - moving) * rate
            moved = moving + TIME_STEP * drag
            state_ref[pl.ds(STATE * k + c, 1)] = moved
            state_ref[pl.ds(STATE * k + comps + c, 1)] = row(OFFSET + c) + TIME_STEP * moved
            pushed.append(drag * weight_z)
        pushed.append(jnp.zeros((LANES - comps * REACH_Z, LANES), jnp.float32))
        push_main, push_rest = parts_of(jnp.concatenate(pushed, axis=0))
        push = jnp.concatenate([push_main, push_rest, push_main], axis=1).astype(jnp.bfloat16)
        spread = jnp.concatenate([main, main, rest], axis=1).astype(jnp.bfloat16)
        return lax.dot_general(spread, push, (((1,), (1,)), ((), ())), preferred_element_type=jnp.float32)

    count = list_ref[0, 2 * room + late]

    @pl.loop(0, (count + UNROLL - 1) // UNROLL)
    def _(group):
        at = late * room + group * UNROLL
        shares = [shares_of(at + u) for u in range(UNROLL)]
        for u in range(UNROLL):
            start, first_z = list_ref[1, at + u], list_ref[3, at + u]
            within = (lane - first_z + LANES) % LANES < REACH_Z
            for c in range(comps):
                shift = (first_z - c * REACH_Z + LANES) % LANES
                for a in range(REACH_X):
                    spot = pl.ds(start + (c * (size_x + 1) + a) * ROWS_Y, REACH_Y)
                    part = pltpu.roll(shares[u][a * REACH_Y : (a + 1) * REACH_Y], shift, 1)
                    deposit_ref[spot] = deposit_ref[spot] + jnp.where(within, part, 0.0)


def send_kernel(push, diffuse, crossing_ref, state_ref, grid_ref, deposit_ref, leaving_ref, velocity_ref, y_ref, x_ref, z_ref):
    comps, size_x = grid_ref.shape[0], grid_ref.shape[1] - 2
    size_y = z_ref.shape[0]
    nblocks = velocity_ref.shape[1]
    slots = crossing_ref.shape[1]
    rows = STATE * slots
    up = odd("gy")
    for face in range(6):
        for slot in range(slots):
            block = crossing_ref[face, slot]
            spot = pl.ds(pl.multiple_of(jnp.maximum(block, 0) * STATE, STATE), STATE)
            tile = jnp.where(block >= 0, state_ref[spot], 0.0)
            here = slice(slot * STATE, (slot + 1) * STATE)
            if face == 2:
                y_ref[up, here] = tile
            elif face == 3:
                y_ref[1 - up, here] = tile
            else:
                leaving_ref[face, here] = tile
    y_ref[1 - up, rows:] = jnp.zeros((y_ref.shape[1] - rows, LANES), jnp.float32)
    lane = lane_ids(ROWS_Y)
    face = jnp.zeros((ROWS_Y, LANES), jnp.float32)
    for c in range(comps):
        for x in range(size_x + 1):
            beyond = push * deposit_ref[1, c, x]
            if x < size_x:
                behind = diffuse * turned(grid_ref[c, x + 1, 0:size_y], 1)
                beyond = jnp.concatenate([beyond[:size_y] + behind, beyond[size_y:]], axis=0)
            place = PACK * c + x
            face = jnp.where(lane == place, turned(beyond, place), face)
        wrapped = jnp.where(lane_ids(size_x) == 0, 0.0, deposit_ref[1, c, 0:size_x, size_y])
        line = diffuse * grid_ref[c, 1 : size_x + 1, size_y - 1] + push * (deposit_ref[0, c, 0:size_x, size_y] + wrapped)
        y_ref[up, rows + c * ROWS_Y : rows + c * ROWS_Y + size_x] = line
        wrapped = jnp.where(lane_ids(ROWS_Y) == 0, 0.0, deposit_ref[1, c, size_x])
        total = push * (deposit_ref[0, c, size_x] + wrapped)
        x_ref[c * size_y : (c + 1) * size_y] = diffuse * grid_ref[c, size_x, 0:size_y] + total[:size_y]
        at = rows + c * ROWS_Y + size_x
        y_ref[up, at : at + 1] = total[size_y : size_y + 1]
    z_ref[...] = face[:size_y]
    y_ref[up, rows + size_x + 1 : rows + size_x + 2] = face[size_y : size_y + 1]
    for c in range(comps):
        velocity_ref[c] = state_ref[pl.ds(c, nblocks, stride=STATE)]


def base_kernel(push, diffuse, grid_ref, deposit_ref, top_ref, base_ref):
    comps, size_x, size_y, size_z = base_ref.shape
    lane = lane_ids(size_y)
    top = top_ref[0:size_y]
    for c in range(comps):
        for x in range(size_x):
            here = grid_ref[c, x + 1, 0:size_y]
            laplace = grid_ref[c, x + 2, 0:size_y]
            if x:
                laplace = laplace + grid_ref[c, x, 0:size_y]
            before = jnp.where(row_ids(size_y) == 0, 0.0, pltpu.roll(here, 1, 0))
            laplace = laplace + grid_ref[c, x + 1, 1 : size_y + 1] + before
            ahead = jnp.where(lane == size_z - 1, turned(top, size_z - 1 - (PACK * c + x)), turned(here, -1))
            laplace = laplace + ahead + jnp.where(lane == 0, 0.0, turned(here, 1)) - 6.0 * here
            total = deposit_ref[0, c, x, 0:size_y] + jnp.where(lane == 0, 0.0, deposit_ref[1, c, x, 0:size_y])
            base_ref[c, x] = here + diffuse * laplace + push * total


def below(first_ref, second_ref, rows):
    got = jnp.where(odd("gy") == 1, first_ref[rows], second_ref[rows])
    return jnp.where(lax.axis_index("gy") != 0, got, 0.0)


def relay_kernel(size_x, size_y, comps, count, first_ref, second_ref, x_in_ref, z_in_ref, leaving_ref, x_ref, z_ref, edge_ref):
    edge = comps * size_y
    x_ref[0:edge] = x_in_ref[...]
    for c in range(comps):
        at = count + c * ROWS_Y + size_x
        spot = slice(c * size_y, c * size_y + 1)
        x_ref[spot] = x_in_ref[spot] + below(first_ref, second_ref, slice(at, at + 1))
    x_ref[edge : edge + count] = leaving_ref[0]
    if x_ref.shape[0] > edge + count:
        x_ref[edge + count : edge + 2 * count] = leaving_ref[1]
    at = count + size_x + 1
    edge_ref[...] = z_in_ref[...]
    edge_ref[0:1] = z_in_ref[0:1] + below(first_ref, second_ref, slice(at, at + 1))
    up = odd("gz")
    z_ref[up, 0:count] = leaving_ref[4]
    z_ref[up, count : count + size_y] = edge_ref[...]
    z_ref[1 - up, 0:count] = leaving_ref[5]
    z_ref[1 - up, count : count + size_y] = jnp.zeros((size_y, LANES), jnp.float32)


def finish_kernel(
    count, base_ref, y1_ref, y2_ref, x_ref, minus_x_ref, z1_ref, z2_ref, edge_ref, gas_ref, arrivals_ref
):
    comps, size_x, size_y, _ = base_ref.shape
    first_row, first_lane = row_ids(size_y) == 0, lane_ids(size_y) == 0
    rows = slice(count, count + size_y)
    from_first = odd("gz") == 1
    face = jnp.where(from_first, z1_ref[rows], z2_ref[rows])
    corner = edge_ref[...]
    for c in range(comps):
        for x in range(size_x):
            at = count + c * ROWS_Y + x
            line = jnp.broadcast_to(below(y1_ref, y2_ref, slice(at, at + 1)), (size_y, LANES))
            total = base_ref[c, x] + jnp.where(first_row, line, 0.0)
            far = turned(face, -(PACK * c + x))
            if x == 0:
                total = total + x_ref[c * size_y : (c + 1) * size_y]
                far = far + turned(corner, -(PACK * c + size_x))
            gas_ref[c, x] = total + jnp.where(first_lane, far, 0.0)

    slots = arrivals_ref.shape[2]
    lower, upper = lax.axis_index("gy") != 0, lax.axis_index("gy") != lax.axis_size("gy") - 1
    odd_y = odd("gy") == 1
    for i in range(arrivals_ref.shape[1]):

        def rows_of(ref, at=0):
            return ref[pl.ds(at + i, slots, stride=STATE)]

        arrivals_ref[0, i] = rows_of(x_ref, comps * size_y)
        arrivals_ref[1, i] = rows_of(minus_x_ref, minus_x_ref.shape[0] - count)
        y1, y2 = rows_of(y1_ref), rows_of(y2_ref)
        arrivals_ref[2, i] = jnp.where(lower, jnp.where(odd_y, y1, y2), 0.0)
        arrivals_ref[3, i] = jnp.where(upper, jnp.where(odd_y, y2, y1), 0.0)
        z1, z2 = rows_of(z1_ref), rows_of(z2_ref)
        arrivals_ref[4, i] = jnp.where(from_first, z1, z2)
        arrivals_ref[5, i] = jnp.where(from_first, z2, z1)


def per_device(gas_field, velocity, fraction, response, cell_index, brick_index, crossing):
    comps, size_x, size_y, size_z = gas_field.shape
    nblocks = velocity.shape[0]
    loading = 0.5 * size_x * size_y * size_z / (nblocks * 128)
    push, diffuse = -TIME_STEP * loading, TIME_STEP * VISCOSITY
    velocity = jnp.transpose(velocity, (1, 0, 2))
    fraction = jnp.transpose(fraction, (1, 0, 2))
    spare = nblocks + 8
    rows_z = size_z + 8
    grid_shape = (comps, size_x + 2, ROWS_Y, LANES)
    lines_shape = ((size_x // BX) * (size_y // BY) * comps * rows_z, LANES)
    deposit_shape = (2 * comps * (size_x + 1) * ROWS_Y, LANES)

    grid, face, plane = call(
        begin_kernel, [grid_shape, (size_y, LANES), (comps * size_y, LANES)], gas_field,
        hbm=(0,), scratch=(pltpu.SemaphoreType.DMA(()),),
    )
    from_z = moved_along(face, "gz", -1)
    from_x = moved_along(plane, "gx", -1)
    from_xz = moved_diagonally(face, -1)
    lines, deposit, table, state, blocks = call(
        prepare_kernel,
        [
            lines_shape,
            deposit_shape,
            (TABLE_ROWS, spare, LANES),
            (STATE * spare, LANES),
            jax.ShapeDtypeStruct((4, 2 * (nblocks + UNROLL) + 2), jnp.int32),
        ],
        grid, velocity, fraction, response, cell_index, brick_index,
        smem=(5,), hbm=(1, 2, 3, 4), smem_outs=(4,), cycles=3000,
        scratch=(
            pltpu.VMEM(velocity.shape, jnp.float32),
            pltpu.VMEM(velocity.shape, jnp.float32),
            pltpu.VMEM(response.shape, jnp.float32),
            pltpu.VMEM(response.shape, jnp.int32),
            pltpu.SemaphoreType.DMA((4,)),
        ),
    )
    line_rows = -(-(comps * size_x + comps + 1) // 8) * 8
    (y_lines,) = call(y_lines_kernel, [(line_rows, LANES)], grid, from_z, from_x, from_xz)
    y1, y2 = swapped((y_lines, y_lines), "gy", False)
    square = pltpu.VMEM((LANES, LANES), jnp.float32)
    grid, lines, top = call(
        halo_xz_kernel, [grid_shape, lines_shape, (LANES, LANES)], grid, lines, from_z, from_x, from_xz,
        aliases={0: 0, 1: 1}, scratch=(square,), cycles=1000,
    )

    def advance(late, lines, state, deposit):
        return call(
            functools.partial(blocks_kernel, late, comps, size_x, rows_z),
            [(STATE * spare, LANES), deposit_shape], blocks, lines, table, state, deposit,
            smem=(0,), aliases={3: 0, 4: 1}, cycles=6000 - 4000 * late,
        )

    state, deposit = advance(0, lines, state, deposit)
    grid, lines = call(
        functools.partial(halo_y_kernel, size_y), [grid_shape, lines_shape], grid, lines, top, y1, y2,
        aliases={0: 0, 1: 1}, scratch=(square,), cycles=1000,
    )
    state, deposit = advance(1, lines, state, deposit)

    deposit = deposit.reshape(2, comps, size_x + 1, ROWS_Y, LANES)
    count = STATE * crossing.shape[1]
    leaving, velocity_next, to_y, to_x, to_z = call(
        functools.partial(send_kernel, push, diffuse),
        [
            (6, count, LANES),
            (comps, nblocks, LANES),
            (2, count + comps * ROWS_Y, LANES),
            (comps * size_y, LANES),
            (size_y, LANES),
        ],
        crossing, state, grid, deposit, smem=(0,), cycles=1000,
    )
    y1, y2 = swapped((to_y[0], to_y[1]), "gy", False)
    (base,) = call(
        functools.partial(base_kernel, push, diffuse), [gas_field.shape], grid, deposit, top, cycles=1000,
    )
    edge = comps * size_y
    both = lax.axis_size("gx") == 2
    to_x, to_z, to_xz = call(
        functools.partial(relay_kernel, size_x, size_y, comps, count),
        [(edge + (2 if both else 1) * count, LANES), (2, count + size_y, LANES), (size_y, LANES)],
        y1, y2, to_x, to_z, leaving,
    )
    got_x = moved_along(to_x, "gx", 1)
    z1, z2 = swapped((to_z[0], to_z[1]), "gz", True)
    got_xz = moved_diagonally(to_xz, 1)
    got_mx = got_x if both else moved_along(leaving[1], "gx", -1)
    gas_next, arrivals = call(
        functools.partial(finish_kernel, count), [gas_field.shape, (6, 7, crossing.shape[1], LANES)],
        base, y1, y2, got_x, got_mx, z1, z2, got_xz,
    )
    return gas_next, jnp.transpose(velocity_next, (1, 0, 2)), jnp.transpose(arrivals, (0, 2, 1, 3))


def solution(mesh):
    owner = ("gx", "gz", "gy")
    in_specs = (
        P(None, "gx", "gy", "gz"),
        P(owner, None, None),
        P(owner, None, None),
        P(owner, None),
        P(owner, None),
        P(owner),
        P(owner, None),
    )
    out_specs = (
        P(None, "gx", "gy", "gz"),
        P(owner, None, None),
        P(owner, None, None, None),
    )
    return jax.shard_map(
        per_device, mesh=mesh, in_specs=in_specs, out_specs=out_specs, check_vma=False
    )
```

```python
import functools

import jax
import jax.numpy as jnp
from jax import lax
from jax.experimental import pallas as pl
from jax.experimental.pallas import tpu as pltpu
from jax.sharding import PartitionSpec as P

BX = 4
BY = 4
BZ = 8

TIME_STEP = 0.25
VISCOSITY = 0.4

LANES = 128
PACK = 32
ROWS_Y = 24
REACH_X = BX + 1
REACH_Y = 8
SPREAD = REACH_X * REACH_Y
REACH_Z = 2 * BZ
UNROLL = 8

WEIGHT, ALONG_Y, IN_Y, ALONG_Z, IN_Z, RATE, MOVING, OFFSET = 0, 5, 6, 7, 8, 9, 10, 13
TABLE_ROWS = 16
STATE = 8

VMEM = pl.BlockSpec(memory_space=pltpu.VMEM)
SMEM = pl.BlockSpec(memory_space=pltpu.SMEM)
HBM = pl.BlockSpec(memory_space=pltpu.HBM)


def moved_along(block, axis, distance):
    count = lax.axis_size(axis)
    return lax.ppermute(block, axis, [(i, (i + distance) % count) for i in range(count)])


def swapped_z(blocks):
    count = lax.axis_size("gz")
    first = [(i, i ^ 1) for i in range(count)]
    second = [(i, (((i + 1) ^ 1) - 1) % count) for i in range(count)]
    return lax.ppermute(blocks[0], "gz", first), lax.ppermute(blocks[1], "gz", second)


def swapped_y(blocks):
    nz, ny = lax.axis_size("gz"), lax.axis_size("gy")
    first = [(j, j ^ 1) for j in range(ny)]
    second = []
    for k in range(nz):
        second.append((k * ny, (k ^ 1) * ny))
        second.append((k * ny + ny - 1, (k ^ 1) * ny + ny - 1))
        second.extend((k * ny + j, k * ny + ((j + 1) ^ 1) - 1) for j in range(1, ny - 1))
    return lax.ppermute(blocks[0], "gy", first), lax.ppermute(blocks[1], ("gz", "gy"), second)


def moved_diagonally(block, distance):
    nx, nz = lax.axis_size("gx"), lax.axis_size("gz")
    route = [(i * nz + k, (i + distance) % nx * nz + (k + distance) % nz) for i in range(nx) for k in range(nz)]
    return lax.ppermute(block, ("gx", "gz"), route)


def call(body, outs, *operands, smem=(), hbm=(), smem_outs=(), scratch=(), aliases=None, cycles=0, limit=40):
    return pl.pallas_call(
        body,
        out_shape=[o if isinstance(o, jax.ShapeDtypeStruct) else jax.ShapeDtypeStruct(o, jnp.float32) for o in outs],
        in_specs=[SMEM if i in smem else HBM if i in hbm else VMEM for i in range(len(operands))],
        out_specs=[SMEM if i in smem_outs else VMEM for i in range(len(outs))],
        scratch_shapes=list(scratch),
        input_output_aliases=aliases or {},
        compiler_params=pltpu.CompilerParams(vmem_limit_bytes=limit * 1024 * 1024),
        cost_estimate=pl.CostEstimate(flops=cycles * 4096, bytes_accessed=cycles * 1024, transcendentals=0),
    )(*operands)


def lane_ids(rows):
    return lax.broadcasted_iota(jnp.int32, (rows, LANES), 1)


def row_ids(rows):
    return lax.broadcasted_iota(jnp.int32, (rows, LANES), 0)


def turned(value, shift):
    shift = shift % LANES
    return pltpu.roll(value, shift, 1) if shift else value


def odd(axis):
    return lax.axis_index(axis) % 2


def begin_kernel(
    gas_ref, velocity_in, fraction_in, response_in, cell_in, brick_in, crossing_in,
    grid_ref, face_ref, plane_ref, velocity_ref, fraction_ref, response_ref, cell_ref, brick_ref, crossing_ref, sems,
):
    comps, size_x, size_y, _ = gas_ref.shape
    pairs = [
        (gas_ref, grid_ref.at[:, 1 : size_x + 1, 0:size_y]),
        (velocity_in, velocity_ref), (fraction_in, fraction_ref), (response_in, response_ref),
        (cell_in, cell_ref), (brick_in, brick_ref), (crossing_in, crossing_ref),
    ]
    copies = [pltpu.make_async_copy(source, target, sems.at[i]) for i, (source, target) in enumerate(pairs)]
    for copy in copies:
        copy.start()
    zeros = jnp.zeros((ROWS_Y, LANES), jnp.float32)
    for c in range(comps):
        grid_ref[c, 0] = zeros
        grid_ref[c, size_x + 1] = zeros
        for x in range(size_x):
            grid_ref[c, x + 1, size_y:] = zeros[size_y:]
    copies[0].wait()
    lane = lane_ids(size_y)
    face = jnp.zeros((size_y, LANES), jnp.float32)
    for c in range(comps):
        plane_ref[c * size_y : (c + 1) * size_y] = grid_ref[c, 1, 0:size_y]
        for x in range(size_x):
            place = PACK * c + x
            face = jnp.where(lane == place, turned(grid_ref[c, x + 1, 0:size_y], place), face)
    face_ref[...] = face
    for copy in copies[1:]:
        copy.wait()


def parts_of(value):
    main = value.astype(jnp.bfloat16).astype(jnp.float32)
    return main, value - main


def lay_out(grid_ref, lines_ref, p, q, size_y, size_z):
    comps = grid_ref.shape[0]
    rows_z = size_z + 8
    count_y = size_y // BY
    for c in range(comps):
        planes = [grid_ref[c, p * BX + a + 1, q * BY : q * BY + REACH_Y] for a in range(REACH_X)]
        main, rest = parts_of(jnp.concatenate(planes, axis=0))
        stack = jnp.concatenate([main, rest, main, jnp.zeros((LANES - 3 * SPREAD, LANES), jnp.float32)], axis=0)
        at = ((p * count_y + q) * comps + c) * rows_z
        lines_ref[at : at + size_z] = jnp.transpose(stack)


def lay_out_top(turned_ref, lines_ref, q, comps, count_x, count_y, size_z):
    lane = lane_ids(count_x)
    rows_z = size_z + 8
    for c in range(comps):
        total = jnp.zeros((count_x, LANES), jnp.float32)
        for a in range(REACH_X):
            rows = turned_ref[pl.ds(PACK * c + a, count_x, stride=BX)]
            total = jnp.where(lane // REACH_Y == a, turned(rows, a * REACH_Y - q * BY), total)
        main, rest = parts_of(total)
        line = main + turned(rest, SPREAD) + turned(main, 2 * SPREAD)
        for p in range(count_x):
            at = ((p * count_y + q) * comps + c) * rows_z + size_z
            lines_ref[at : at + 1] = line[p : p + 1]


def prepare_kernel(
    grid_ref, velocity_ref, fraction_ref, response_ref, cell_ref, brick_ref,
    lines_ref, deposit_ref, table_ref, state_ref, ready_ref, list_ref,
):
    comps, size_x, size_y, size_z = grid_ref.shape[0], grid_ref.shape[1] - 2, grid_ref.shape[2] - 8, grid_ref.shape[3]
    nblocks = velocity_ref.shape[1]
    count_x, count_y, count_z = size_x // BX, size_y // BY, size_z // BZ
    rows_z = size_z + 8
    spare = table_ref.shape[1] - nblocks

    room = nblocks + UNROLL

    def visit(k, counts):
        late = jnp.where(lax.rem(lax.div(brick_ref[k], count_z), count_y) == count_y - 1, 1, 0)
        list_ref[jnp.where(late == 1, room + counts[1], counts[0])] = k
        return counts[0] + 1 - late, counts[1] + late

    early, late = lax.fori_loop(0, nblocks, visit, (jnp.int32(0), jnp.int32(0)), unroll=8)
    for base, count in ((0, early), (room, late)):
        for u in range(UNROLL):
            list_ref[base + count + u] = nblocks
    list_ref[2 * room] = early
    list_ref[2 * room + 1] = late
    ready_ref[...] = jnp.zeros_like(ready_ref)

    deposit_ref[...] = jnp.zeros_like(deposit_ref)
    for p in range(count_x):
        for q in range(count_y):
            for c in range(comps):
                at = ((p * count_y + q) * comps + c) * rows_z + size_z
                lines_ref[at : at + 8] = jnp.zeros((8, LANES), jnp.float32)
    for p in range(count_x - 1):
        for q in range(count_y - 1):
            lay_out(grid_ref, lines_ref, p, q, size_y, size_z)

    cells = cell_ref[...]
    cell_x, cell_y, cell_z = cells // (BY * BZ), cells // BZ % BY, cells % BZ
    along_x = fraction_ref[0]

    def put(row, value):
        table_ref[row, 0:nblocks] = value
        table_ref[row, nblocks : nblocks + spare] = jnp.zeros((spare, LANES), jnp.float32)

    for a in range(REACH_X):
        put(WEIGHT + a, jnp.where(cell_x == a, 1.0 - along_x, 0.0) + jnp.where(cell_x == a - 1, along_x, 0.0))
    put(ALONG_Y, fraction_ref[1])
    put(IN_Y, cell_y.astype(jnp.float32))
    put(ALONG_Z, fraction_ref[2])
    put(IN_Z, cell_z.astype(jnp.float32))
    put(RATE, 1.0 / response_ref[...])
    for c in range(comps):
        put(MOVING + c, velocity_ref[c])
        put(OFFSET + c, fraction_ref[c])
    state_ref[...] = jnp.zeros_like(state_ref)
    state_ref[pl.ds(2 * comps, nblocks, stride=STATE)] = response_ref[...]


def y_lines_kernel(grid_ref, face_ref, from_x_ref, edge_ref, ready_ref, out_ref):
    comps, size_x = grid_ref.shape[0], grid_ref.shape[1] - 2
    size_y = face_ref.shape[0]
    for c in range(comps):
        out_ref[c * size_x : (c + 1) * size_x] = grid_ref[c, 1 : size_x + 1, 0]
        out_ref[comps * size_x + c : comps * size_x + c + 1] = from_x_ref[c * size_y : c * size_y + 1]
    line = jnp.where(lane_ids(8) % PACK == size_x, turned(edge_ref[0:8], size_x), face_ref[0:8])
    out_ref[comps * size_x + comps : comps * size_x + comps + 1] = line[0:1]


def halo_xz_kernel(grid_in_ref, lines_in_ref, face_ref, from_x_ref, edge_ref, grid_ref, lines_ref, top_ref, turned_ref):
    comps, size_x = grid_ref.shape[0], grid_ref.shape[1] - 2
    size_y, size_z = face_ref.shape[0], grid_ref.shape[3]
    count_x, count_y = size_x // BX, size_y // BY
    for c in range(comps):
        grid_ref[c, size_x + 1, 0:size_y] = from_x_ref[c * size_y : (c + 1) * size_y]
    for q in range(count_y - 1):
        lay_out(grid_ref, lines_ref, count_x - 1, q, size_y, size_z)
    top = jnp.where(lane_ids(size_y) % PACK == size_x, turned(edge_ref[...], size_x), face_ref[...])
    top_ref[0:size_y] = top
    top_ref[size_y:] = jnp.zeros((LANES - size_y, LANES), jnp.float32)
    turned_ref[...] = jnp.transpose(top_ref[...])
    for q in range(count_y - 1):
        lay_out_top(turned_ref, lines_ref, q, comps, count_x, count_y, size_z)


def halo_y_kernel(size_y, grid_in_ref, lines_in_ref, top_in_ref, first_ref, second_ref, grid_ref, lines_ref, turned_ref):
    comps, size_x, size_z = grid_ref.shape[0], grid_ref.shape[1] - 2, grid_ref.shape[3]
    count_x, count_y = size_x // BX, size_y // BY
    inside = lax.axis_index("gy") != lax.axis_size("gy") - 1
    even = odd("gy") == 0
    kept = (row_ids(8) == 0) & inside

    def line_at(row):
        line = jnp.where(even, first_ref[row : row + 1], second_ref[row : row + 1])
        return jnp.where(kept, jnp.broadcast_to(line, (8, LANES)), 0.0)

    for c in range(comps):
        for x in range(size_x + 1):
            grid_ref[c, x + 1, size_y:] = line_at(c * size_x + x if x < size_x else comps * size_x + c)
    for p in range(count_x):
        lay_out(grid_ref, lines_ref, p, count_y - 1, size_y, size_z)
    corner = line_at(comps * size_x + comps)
    rest = jnp.zeros((LANES - size_y - 8, LANES), jnp.float32)
    turned_ref[...] = jnp.transpose(jnp.concatenate([top_in_ref[0:size_y], corner, rest], axis=0))
    lay_out_top(turned_ref, lines_ref, count_y - 1, comps, count_x, count_y, size_z)


def blocks_kernel(
    late, comps, size_x, count_y, count_z, rows_z,
    list_ref, brick_ref, lines_ref, table_ref, state_in_ref, deposit_in_ref, state_ref, deposit_ref,
):
    nblocks = brick_ref.shape[0]
    room = (list_ref.shape[0] - 2) // 2
    row_y = row_ids(REACH_Y).astype(jnp.float32)
    row_z = row_ids(REACH_Z).astype(jnp.float32)
    lane = lane_ids(REACH_Y)

    def hat(rows, inside, along):
        return jnp.where(rows == inside, 1.0 - along, 0.0) + jnp.where(rows == inside + 1.0, along, 0.0)

    def loaded(at):
        k = list_ref[at]
        brick = brick_ref[jnp.minimum(k, nblocks - 1)]
        brick_x = lax.div(brick, count_y * count_z)
        brick_y = lax.rem(lax.div(brick, count_z), count_y)
        brick_z = lax.rem(brick, count_z)
        sel = jnp.where(brick_z == count_z - 1, 1, 0)
        start = (sel * comps * (size_x + 1) + brick_x * BX) * ROWS_Y + brick_y * BY
        first = pl.multiple_of((brick_x * count_y + brick_y) * comps * rows_z + brick_z * BZ, 8)
        window = jnp.concatenate([lines_ref[pl.ds(first + c * rows_z, REACH_Z)] for c in range(comps)], axis=0)
        rows = [table_ref[i, pl.ds(k, 1)] for i in range(OFFSET + comps)]
        return k, start, brick_z * BZ, window, rows

    def moved_of(window, rows):
        weight_y = hat(row_y, rows[IN_Y], rows[ALONG_Y])
        weight_z = hat(row_z, rows[IN_Z], rows[ALONG_Z])
        main, rest = parts_of(jnp.concatenate([rows[WEIGHT + a] * weight_y for a in range(REACH_X)], axis=0))
        unused = jnp.zeros((LANES - 3 * SPREAD, LANES), jnp.float32)
        table = jnp.concatenate([main, main, rest, unused], axis=0).astype(jnp.bfloat16)
        seen = lax.dot_general(
            window.astype(jnp.bfloat16), table, (((1,), (0,)), ((), ())), preferred_element_type=jnp.float32
        )
        state, moved, pushed = [], [], []
        for c in range(comps):
            gas_sample = jnp.sum(seen[c * REACH_Z : (c + 1) * REACH_Z] * weight_z, axis=0, keepdims=True)
            drag = (gas_sample - rows[MOVING + c]) * rows[RATE]
            state.append(rows[MOVING + c] + TIME_STEP * drag)
            moved.append(rows[OFFSET + c] + TIME_STEP * state[c])
            pushed.append(drag * weight_z)
        pushed.append(jnp.zeros((LANES - comps * REACH_Z, LANES), jnp.float32))
        push_main, push_rest = parts_of(jnp.concatenate(pushed, axis=0))
        push = jnp.concatenate([push_main, push_rest, push_main], axis=1).astype(jnp.bfloat16)
        spread = jnp.concatenate([main, main, rest], axis=1).astype(jnp.bfloat16)
        shares = lax.dot_general(spread, push, (((1,), (1,)), ((), ())), preferred_element_type=jnp.float32)
        return state + moved, shares

    count = list_ref[2 * room + late]

    @pl.loop(0, (count + UNROLL - 1) // UNROLL)
    def _(group):
        at = late * room + group * UNROLL
        taken = [loaded(at + u) for u in range(UNROLL)]
        results = [moved_of(window, rows) for _, _, _, window, rows in taken]
        parts = []
        for (_, _, first_z, _, _), (_, shares) in zip(taken, results):
            within = ((lane - first_z) & (LANES - 1)) < REACH_Z
            parts.append([])
            for c in range(comps):
                shift = (first_z - c * REACH_Z + LANES) & (LANES - 1)
                for a in range(REACH_X):
                    part = pltpu.roll(shares[a * REACH_Y : (a + 1) * REACH_Y], shift, 1)
                    parts[-1].append(jnp.where(within, part, 0.0))
        for (k, _, _, _, _), (state, _) in zip(taken, results):
            for i, value in enumerate(state):
                state_ref[pl.ds(STATE * k + i, 1)] = value
        for (_, start, _, _, _), mine in zip(taken, parts):
            spots = [
                pl.ds(start + (c * (size_x + 1) + a) * ROWS_Y, REACH_Y) for c in range(comps) for a in range(REACH_X)
            ]
            sums = [deposit_ref[spot] + part for spot, part in zip(spots, mine)]
            for spot, total in zip(spots, sums):
                deposit_ref[spot] = total


def send_kernel(push, diffuse, crossing_ref, state_ref, grid_ref, deposit_ref, leaving_ref, velocity_ref, y_ref, x_ref, z_ref):
    comps, size_x = grid_ref.shape[0], grid_ref.shape[1] - 2
    size_y = z_ref.shape[0]
    nblocks = velocity_ref.shape[1]
    slots = crossing_ref.shape[1]
    rows = STATE * slots
    first = odd("gy") == 0
    velocity = [state_ref[pl.ds(c, nblocks, stride=STATE)] for c in range(comps)]
    for face in range(6):
        tiles = []
        for slot in range(slots):
            block = crossing_ref[face, slot]
            spot = pl.ds(pl.multiple_of(jnp.maximum(block, 0) * STATE, STATE), STATE)
            tiles.append(jnp.where(block >= 0, state_ref[spot], 0.0))
        leaving_ref[face] = jnp.concatenate(tiles, axis=0)
    y_ref[0, 0:rows] = jnp.where(first, leaving_ref[2], leaving_ref[3])
    y_ref[1, 0:rows] = jnp.where(first, leaving_ref[3], leaving_ref[2])
    for c in range(comps):
        velocity_ref[c] = velocity[c]
    lane = lane_ids(ROWS_Y)
    face = jnp.zeros((ROWS_Y, LANES), jnp.float32)
    for c in range(comps):
        for x in range(size_x + 1):
            beyond = push * deposit_ref[1, c, x]
            if x < size_x:
                behind = diffuse * turned(grid_ref[c, x + 1, 0:size_y], 1)
                beyond = jnp.concatenate([beyond[:size_y] + behind, beyond[size_y:]], axis=0)
            place = PACK * c + x
            face = jnp.where(lane == place, turned(beyond, place), face)
        wrapped = jnp.where(lane_ids(size_x) == 0, 0.0, deposit_ref[1, c, 0:size_x, size_y])
        line = diffuse * grid_ref[c, 1 : size_x + 1, size_y - 1] + push * (deposit_ref[0, c, 0:size_x, size_y] + wrapped)
        y_ref[0, rows + c * ROWS_Y : rows + c * ROWS_Y + size_x] = line
        wrapped = jnp.where(lane_ids(ROWS_Y) == 0, 0.0, deposit_ref[1, c, size_x])
        total = push * (deposit_ref[0, c, size_x] + wrapped)
        x_ref[c * size_y : (c + 1) * size_y] = diffuse * grid_ref[c, size_x, 0:size_y] + total[:size_y]
        at = rows + c * ROWS_Y + size_x
        y_ref[0, at : at + 8] = total[size_y:]
    z_ref[...] = face[:size_y]
    y_ref[0, rows + size_x + 1 : rows + size_x + 2] = face[size_y : size_y + 1]
    y_ref[1, rows:] = y_ref[0, rows:]


def base_kernel(push, diffuse, grid_ref, deposit_ref, top_ref, base_ref):
    comps, size_x, size_y, size_z = base_ref.shape
    lane = lane_ids(size_y)
    top = top_ref[0:size_y]
    for c in range(comps):
        for x in range(size_x):
            here = grid_ref[c, x + 1, 0:size_y]
            laplace = grid_ref[c, x + 2, 0:size_y]
            if x:
                laplace = laplace + grid_ref[c, x, 0:size_y]
            before = jnp.where(row_ids(size_y) == 0, 0.0, pltpu.roll(here, 1, 0))
            laplace = laplace + grid_ref[c, x + 1, 1 : size_y + 1] + before
            ahead = jnp.where(lane == size_z - 1, turned(top, size_z - 1 - (PACK * c + x)), turned(here, -1))
            laplace = laplace + ahead + jnp.where(lane == 0, 0.0, turned(here, 1)) - 6.0 * here
            total = deposit_ref[0, c, x, 0:size_y] + jnp.where(lane == 0, 0.0, deposit_ref[1, c, x, 0:size_y])
            base_ref[c, x] = here + diffuse * laplace + push * total


def below(first_ref, second_ref, rows):
    got = jnp.where(odd("gy") == 1, first_ref[rows], second_ref[rows])
    return jnp.where(lax.axis_index("gy") != 0, got, 0.0)


def relay_kernel(size_x, size_y, comps, count, first_ref, second_ref, x_in_ref, z_in_ref, leaving_ref, x_ref, z_ref, edge_ref):
    edge = comps * size_y
    x_ref[0:edge] = x_in_ref[...]
    for c in range(comps):
        at = count + c * ROWS_Y + size_x
        spot = slice(c * size_y, c * size_y + 1)
        x_ref[spot] = x_in_ref[spot] + below(first_ref, second_ref, slice(at, at + 1))
    x_ref[edge : edge + count] = leaving_ref[0]
    if x_ref.shape[0] > edge + count:
        x_ref[edge + count : edge + 2 * count] = leaving_ref[1]
    at = count + size_x + 1
    edge_ref[...] = z_in_ref[...]
    edge_ref[0:1] = z_in_ref[0:1] + below(first_ref, second_ref, slice(at, at + 1))
    up = odd("gz")
    z_ref[up, 0:count] = leaving_ref[4]
    z_ref[up, count : count + size_y] = edge_ref[...]
    z_ref[1 - up, 0:count] = leaving_ref[5]
    z_ref[1 - up, count : count + size_y] = jnp.zeros((size_y, LANES), jnp.float32)


def finish_kernel(
    count, base_ref, y1_ref, y2_ref, x_ref, minus_x_ref, z1_ref, z2_ref, edge_ref, gas_ref, arrivals_ref
):
    comps, size_x, size_y, _ = base_ref.shape
    first_row, first_lane = row_ids(size_y) == 0, lane_ids(size_y) == 0
    rows = slice(count, count + size_y)
    from_first = odd("gz") == 1
    face = jnp.where(from_first, z1_ref[rows], z2_ref[rows])
    corner = edge_ref[...]
    for c in range(comps):
        for x in range(size_x):
            at = count + c * ROWS_Y + x
            line = jnp.broadcast_to(below(y1_ref, y2_ref, slice(at, at + 1)), (size_y, LANES))
            total = base_ref[c, x] + jnp.where(first_row, line, 0.0)
            far = turned(face, -(PACK * c + x))
            if x == 0:
                total = total + x_ref[c * size_y : (c + 1) * size_y]
                far = far + turned(corner, -(PACK * c + size_x))
            gas_ref[c, x] = total + jnp.where(first_lane, far, 0.0)

    slots = arrivals_ref.shape[2]
    lower, upper = lax.axis_index("gy") != 0, lax.axis_index("gy") != lax.axis_size("gy") - 1
    odd_y = odd("gy") == 1
    for i in range(arrivals_ref.shape[1]):

        def rows_of(ref, at=0):
            return ref[pl.ds(at + i, slots, stride=STATE)]

        arrivals_ref[0, i] = rows_of(x_ref, comps * size_y)
        arrivals_ref[1, i] = rows_of(minus_x_ref, minus_x_ref.shape[0] - count)
        y1, y2 = rows_of(y1_ref), rows_of(y2_ref)
        arrivals_ref[2, i] = jnp.where(lower, jnp.where(odd_y, y1, y2), 0.0)
        arrivals_ref[3, i] = jnp.where(upper, jnp.where(odd_y, y2, y1), 0.0)
        z1, z2 = rows_of(z1_ref), rows_of(z2_ref)
        arrivals_ref[4, i] = jnp.where(from_first, z1, z2)
        arrivals_ref[5, i] = jnp.where(from_first, z2, z1)


def per_device(gas_field, velocity, fraction, response, cell_index, brick_index, crossing):
    comps, size_x, size_y, size_z = gas_field.shape
    nblocks = velocity.shape[0]
    loading = 0.5 * size_x * size_y * size_z / (nblocks * 128)
    push, diffuse = -TIME_STEP * loading, TIME_STEP * VISCOSITY
    velocity = jnp.transpose(velocity, (1, 0, 2))
    fraction = jnp.transpose(fraction, (1, 0, 2))
    spare = nblocks + 8
    rows_z = size_z + 8
    grid_shape = (comps, size_x + 2, ROWS_Y, LANES)
    lines_shape = ((size_x // BX) * (size_y // BY) * comps * rows_z, LANES)
    deposit_shape = (2 * comps * (size_x + 1) * ROWS_Y, LANES)

    inputs = (gas_field, velocity, fraction, response, cell_index, brick_index, crossing)
    inputs = [pltpu.with_memory_space_constraint(array, pltpu.HBM) for array in inputs]
    grid, face, plane, velocity, fraction, response, cell_index, brick_index, crossing = call(
        begin_kernel,
        [grid_shape, (size_y, LANES), (comps * size_y, LANES)]
        + [jax.ShapeDtypeStruct(array.shape, array.dtype) for array in inputs[1:]],
        *inputs, hbm=range(7), scratch=(pltpu.SemaphoreType.DMA((7,)),), limit=40,
    )
    from_z = moved_along(face, "gz", -1)
    from_x = moved_along(plane, "gx", -1)
    from_xz = moved_diagonally(face, -1)
    lines, deposit, table, state, ready, blocks = call(
        prepare_kernel,
        [
            lines_shape,
            deposit_shape,
            (TABLE_ROWS, spare, LANES),
            (STATE * spare, LANES),
            (8, LANES),
            jax.ShapeDtypeStruct((2 * (nblocks + UNROLL) + 2,), jnp.int32),
        ],
        grid, velocity, fraction, response, cell_index, brick_index,
        smem=(5,), smem_outs=(5,), cycles=3000,
    )
    line_rows = -(-(comps * size_x + comps + 1) // 8) * 8
    (y_lines,) = call(y_lines_kernel, [(line_rows, LANES)], grid, from_z, from_x, from_xz, ready)
    y1, y2 = swapped_y((y_lines, y_lines))
    square = pltpu.VMEM((LANES, LANES), jnp.float32)
    grid, lines, top = call(
        halo_xz_kernel, [grid_shape, lines_shape, (LANES, LANES)], grid, lines, from_z, from_x, from_xz,
        aliases={0: 0, 1: 1}, scratch=(square,), cycles=1000,
    )

    def advance(late, lines, state, deposit):
        return call(
            functools.partial(blocks_kernel, late, comps, size_x, size_y // BY, size_z // BZ, rows_z),
            [(STATE * spare, LANES), deposit_shape], blocks, brick_index, lines, table, state, deposit,
            smem=(0, 1), aliases={4: 0, 5: 1}, cycles=6000 - 4000 * late,
        )

    state, deposit = advance(0, lines, state, deposit)
    grid, lines = call(
        functools.partial(halo_y_kernel, size_y), [grid_shape, lines_shape], grid, lines, top, y1, y2,
        aliases={0: 0, 1: 1}, scratch=(square,), cycles=1000,
    )
    state, deposit = advance(1, lines, state, deposit)

    deposit = deposit.reshape(2, comps, size_x + 1, ROWS_Y, LANES)
    count = STATE * crossing.shape[1]
    leaving, velocity_next, to_y, to_x, to_z = call(
        functools.partial(send_kernel, push, diffuse),
        [
            (6, count, LANES),
            (comps, nblocks, LANES),
            (2, count + comps * ROWS_Y, LANES),
            (comps * size_y, LANES),
            (size_y, LANES),
        ],
        crossing, state, grid, deposit, smem=(0,), cycles=1000,
    )
    y1, y2 = swapped_y((to_y[0], to_y[1]))
    (base,) = call(
        functools.partial(base_kernel, push, diffuse), [gas_field.shape], grid, deposit, top, cycles=1000,
    )
    edge = comps * size_y
    both = lax.axis_size("gx") == 2
    to_x, to_z, to_xz = call(
        functools.partial(relay_kernel, size_x, size_y, comps, count),
        [(edge + (2 if both else 1) * count, LANES), (2, count + size_y, LANES), (size_y, LANES)],
        y1, y2, to_x, to_z, leaving,
    )
    got_x = moved_along(to_x, "gx", 1)
    z1, z2 = swapped_z((to_z[0], to_z[1]))
    got_xz = moved_diagonally(to_xz, 1)
    got_mx = got_x if both else moved_along(leaving[1], "gx", -1)
    gas_next, arrivals = call(
        functools.partial(finish_kernel, count), [gas_field.shape, (6, 7, crossing.shape[1], LANES)],
        base, y1, y2, got_x, got_mx, z1, z2, got_xz,
    )
    return gas_next, jnp.transpose(velocity_next, (1, 0, 2)), jnp.transpose(arrivals, (0, 2, 1, 3))


def solution(mesh):
    owner = ("gx", "gz", "gy")
    in_specs = (
        P(None, "gx", "gy", "gz"),
        P(owner, None, None),
        P(owner, None, None),
        P(owner, None),
        P(owner, None),
        P(owner),
        P(owner, None),
    )
    out_specs = (
        P(None, "gx", "gy", "gz"),
        P(owner, None, None),
        P(owner, None, None, None),
    )
    return jax.shard_map(
        per_device, mesh=mesh, in_specs=in_specs, out_specs=out_specs, check_vma=False
    )
```

```python
import functools

import jax
import jax.numpy as jnp
from jax import lax
from jax.experimental import pallas as pl
from jax.experimental.pallas import tpu as pltpu
from jax.sharding import PartitionSpec as P

BX = 4
BY = 4
BZ = 8

TIME_STEP = 0.25
VISCOSITY = 0.4

LANES = 128
PACK = 32
ROWS_Y = 24
REACH_X = BX + 1
REACH_Y = 8
SPREAD = REACH_X * REACH_Y
REACH_Z = 2 * BZ
UNROLL = 8

WEIGHT, ALONG_Y, IN_Y, ALONG_Z, IN_Z, RESPONSE, MOVING, OFFSET = 0, 5, 6, 7, 8, 9, 10, 13
TABLE_ROWS = 16
STATE = 8

VMEM = pl.BlockSpec(memory_space=pltpu.VMEM)
SMEM = pl.BlockSpec(memory_space=pltpu.SMEM)
HBM = pl.BlockSpec(memory_space=pltpu.HBM)


def moved_along(block, axis, distance):
    count = lax.axis_size(axis)
    return lax.ppermute(block, axis, [(i, (i + distance) % count) for i in range(count)])


def swapped_z(blocks):
    count = lax.axis_size("gz")
    first = [(i, i ^ 1) for i in range(count)]
    second = [(i, (((i + 1) ^ 1) - 1) % count) for i in range(count)]
    return lax.ppermute(blocks[0], "gz", first), lax.ppermute(blocks[1], "gz", second)


def swapped_y(blocks):
    nz, ny = lax.axis_size("gz"), lax.axis_size("gy")
    first = [(j, j ^ 1) for j in range(ny)]
    second = []
    for k in range(nz):
        second.append((k * ny, (k ^ 1) * ny))
        second.append((k * ny + ny - 1, (k ^ 1) * ny + ny - 1))
        second.extend((k * ny + j, k * ny + ((j + 1) ^ 1) - 1) for j in range(1, ny - 1))
    return lax.ppermute(blocks[0], "gy", first), lax.ppermute(blocks[1], ("gz", "gy"), second)


def moved_diagonally(block, distance):
    nx, nz = lax.axis_size("gx"), lax.axis_size("gz")
    route = [(i * nz + k, (i + distance) % nx * nz + (k + distance) % nz) for i in range(nx) for k in range(nz)]
    return lax.ppermute(block, ("gx", "gz"), route)


def call(body, outs, *operands, smem=(), hbm=(), smem_outs=(), scratch=(), aliases=None, cycles=0, limit=40):
    return pl.pallas_call(
        body,
        out_shape=[o if isinstance(o, jax.ShapeDtypeStruct) else jax.ShapeDtypeStruct(o, jnp.float32) for o in outs],
        in_specs=[SMEM if i in smem else HBM if i in hbm else VMEM for i in range(len(operands))],
        out_specs=[SMEM if i in smem_outs else VMEM for i in range(len(outs))],
        scratch_shapes=list(scratch),
        input_output_aliases=aliases or {},
        compiler_params=pltpu.CompilerParams(vmem_limit_bytes=limit * 1024 * 1024),
        cost_estimate=pl.CostEstimate(flops=cycles * 4096, bytes_accessed=cycles * 1024, transcendentals=0),
    )(*operands)


def lane_ids(rows):
    return lax.broadcasted_iota(jnp.int32, (rows, LANES), 1)


def row_ids(rows):
    return lax.broadcasted_iota(jnp.int32, (rows, LANES), 0)


def turned(value, shift):
    shift = shift % LANES
    return pltpu.roll(value, shift, 1) if shift else value


def odd(axis):
    return lax.axis_index(axis) % 2


def begin_kernel(
    gas_ref, velocity_in, fraction_in, response_in, cell_in, brick_in, crossing_in,
    grid_ref, face_ref, plane_ref, velocity_ref, fraction_ref, response_ref, cell_ref, brick_ref, crossing_ref, sems,
):
    comps, size_x, size_y, _ = gas_ref.shape
    pairs = [
        (gas_ref, grid_ref.at[:, 1 : size_x + 1, 0:size_y]),
        (velocity_in, velocity_ref), (fraction_in, fraction_ref), (response_in, response_ref),
        (cell_in, cell_ref), (brick_in, brick_ref), (crossing_in, crossing_ref),
    ]
    copies = [pltpu.make_async_copy(source, target, sems.at[i]) for i, (source, target) in enumerate(pairs)]
    for copy in copies:
        copy.start()
    zeros = jnp.zeros((ROWS_Y, LANES), jnp.float32)
    for c in range(comps):
        grid_ref[c, 0] = zeros
        grid_ref[c, size_x + 1] = zeros
        for x in range(size_x):
            grid_ref[c, x + 1, size_y:] = zeros[size_y:]
    copies[0].wait()
    lane = lane_ids(size_y)
    face = jnp.zeros((size_y, LANES), jnp.float32)
    for c in range(comps):
        plane_ref[c * size_y : (c + 1) * size_y] = grid_ref[c, 1, 0:size_y]
        for x in range(size_x):
            place = PACK * c + x
            face = jnp.where(lane == place, turned(grid_ref[c, x + 1, 0:size_y], place), face)
    face_ref[...] = face
    for copy in copies[1:]:
        copy.wait()


def parts_of(value):
    main = value.astype(jnp.bfloat16).astype(jnp.float32)
    return main, value - main


def lay_out(grid_ref, lines_ref, p, q, size_y, size_z):
    comps = grid_ref.shape[0]
    rows_z = size_z + 8
    count_y = size_y // BY
    for c in range(comps):
        planes = [grid_ref[c, p * BX + a + 1, q * BY : q * BY + REACH_Y] for a in range(REACH_X)]
        main, rest = parts_of(jnp.concatenate(planes, axis=0))
        stack = jnp.concatenate([main, rest, main, jnp.zeros((LANES - 3 * SPREAD, LANES), jnp.float32)], axis=0)
        at = ((p * count_y + q) * comps + c) * rows_z
        lines_ref[at : at + size_z] = jnp.transpose(stack)


def lay_out_top(turned_ref, lines_ref, q, comps, count_x, count_y, size_z):
    lane = lane_ids(count_x)
    rows_z = size_z + 8
    for c in range(comps):
        total = jnp.zeros((count_x, LANES), jnp.float32)
        for a in range(REACH_X):
            rows = turned_ref[pl.ds(PACK * c + a, count_x, stride=BX)]
            total = jnp.where(lane // REACH_Y == a, turned(rows, a * REACH_Y - q * BY), total)
        main, rest = parts_of(total)
        line = main + turned(rest, SPREAD) + turned(main, 2 * SPREAD)
        for p in range(count_x):
            at = ((p * count_y + q) * comps + c) * rows_z + size_z
            lines_ref[at : at + 1] = line[p : p + 1]


def prepare_kernel(
    grid_ref, velocity_ref, fraction_ref, response_ref, cell_ref, brick_ref,
    lines_ref, deposit_ref, table_ref, ready_ref, list_ref,
):
    comps, size_x, size_y, size_z = grid_ref.shape[0], grid_ref.shape[1] - 2, grid_ref.shape[2] - 8, grid_ref.shape[3]
    nblocks = velocity_ref.shape[1]
    count_x, count_y, count_z = size_x // BX, size_y // BY, size_z // BZ
    rows_z = size_z + 8

    room = nblocks + UNROLL

    def visit(k, counts):
        late = jnp.where(lax.rem(lax.div(brick_ref[k], count_z), count_y) == count_y - 1, 1, 0)
        list_ref[jnp.where(late == 1, room + counts[1], counts[0])] = k
        return counts[0] + 1 - late, counts[1] + late

    early, late = lax.fori_loop(0, nblocks, visit, (jnp.int32(0), jnp.int32(0)), unroll=8)
    for base, count in ((0, early), (room, late)):
        for u in range(UNROLL):
            list_ref[base + count + u] = nblocks
    list_ref[2 * room] = early
    list_ref[2 * room + 1] = late
    ready_ref[...] = jnp.zeros_like(ready_ref)

    deposit_ref[...] = jnp.zeros_like(deposit_ref)
    for p in range(count_x):
        for q in range(count_y):
            for c in range(comps):
                at = ((p * count_y + q) * comps + c) * rows_z + size_z
                lines_ref[at : at + 8] = jnp.zeros((8, LANES), jnp.float32)
    for p in range(count_x - 1):
        for q in range(count_y - 1):
            lay_out(grid_ref, lines_ref, p, q, size_y, size_z)

    cells = cell_ref[...]
    cell_x, cell_y, cell_z = cells // (BY * BZ), cells // BZ % BY, cells % BZ
    along_x = fraction_ref[0]

    def put(row, value):
        table_ref[pl.ds(row, nblocks, stride=TABLE_ROWS)] = value

    for a in range(REACH_X):
        put(WEIGHT + a, jnp.where(cell_x == a, 1.0 - along_x, 0.0) + jnp.where(cell_x == a - 1, along_x, 0.0))
    put(ALONG_Y, fraction_ref[1])
    put(IN_Y, cell_y.astype(jnp.float32))
    put(ALONG_Z, fraction_ref[2])
    put(IN_Z, cell_z.astype(jnp.float32))
    put(RESPONSE, response_ref[...])
    for c in range(comps):
        put(MOVING + c, velocity_ref[c])
        put(OFFSET + c, fraction_ref[c])
    spare = table_ref.shape[0] - nblocks * TABLE_ROWS
    row = row_ids(spare)
    table_ref[nblocks * TABLE_ROWS :] = jnp.where(row % TABLE_ROWS == RESPONSE, 1.0, 0.0)


def y_lines_kernel(grid_ref, face_ref, from_x_ref, edge_ref, ready_ref, out_ref):
    comps, size_x = grid_ref.shape[0], grid_ref.shape[1] - 2
    size_y = face_ref.shape[0]
    for c in range(comps):
        out_ref[c * size_x : (c + 1) * size_x] = grid_ref[c, 1 : size_x + 1, 0]
        out_ref[comps * size_x + c : comps * size_x + c + 1] = from_x_ref[c * size_y : c * size_y + 1]
    line = jnp.where(lane_ids(8) % PACK == size_x, turned(edge_ref[0:8], size_x), face_ref[0:8])
    out_ref[comps * size_x + comps : comps * size_x + comps + 1] = line[0:1]


def halo_xz_kernel(grid_in_ref, lines_in_ref, face_ref, from_x_ref, edge_ref, grid_ref, lines_ref, top_ref, turned_ref):
    comps, size_x = grid_ref.shape[0], grid_ref.shape[1] - 2
    size_y, size_z = face_ref.shape[0], grid_ref.shape[3]
    count_x, count_y = size_x // BX, size_y // BY
    for c in range(comps):
        grid_ref[c, size_x + 1, 0:size_y] = from_x_ref[c * size_y : (c + 1) * size_y]
    for q in range(count_y - 1):
        lay_out(grid_ref, lines_ref, count_x - 1, q, size_y, size_z)
    top = jnp.where(lane_ids(size_y) % PACK == size_x, turned(edge_ref[...], size_x), face_ref[...])
    top_ref[0:size_y] = top
    top_ref[size_y:] = jnp.zeros((LANES - size_y, LANES), jnp.float32)
    turned_ref[...] = jnp.transpose(top_ref[...])
    for q in range(count_y - 1):
        lay_out_top(turned_ref, lines_ref, q, comps, count_x, count_y, size_z)


def halo_y_kernel(size_y, grid_in_ref, lines_in_ref, top_in_ref, first_ref, second_ref, grid_ref, lines_ref, turned_ref):
    comps, size_x, size_z = grid_ref.shape[0], grid_ref.shape[1] - 2, grid_ref.shape[3]
    count_x, count_y = size_x // BX, size_y // BY
    inside = lax.axis_index("gy") != lax.axis_size("gy") - 1
    even = odd("gy") == 0
    kept = (row_ids(8) == 0) & inside

    def line_at(row):
        line = jnp.where(even, first_ref[row : row + 1], second_ref[row : row + 1])
        return jnp.where(kept, jnp.broadcast_to(line, (8, LANES)), 0.0)

    for c in range(comps):
        for x in range(size_x + 1):
            grid_ref[c, x + 1, size_y:] = line_at(c * size_x + x if x < size_x else comps * size_x + c)
    for p in range(count_x):
        lay_out(grid_ref, lines_ref, p, count_y - 1, size_y, size_z)
    corner = line_at(comps * size_x + comps)
    rest = jnp.zeros((LANES - size_y - 8, LANES), jnp.float32)
    turned_ref[...] = jnp.transpose(jnp.concatenate([top_in_ref[0:size_y], corner, rest], axis=0))
    lay_out_top(turned_ref, lines_ref, count_y - 1, comps, count_x, count_y, size_z)


def blocks_kernel(
    late, comps, count_x, count_y, count_z, rows_z,
    list_ref, brick_ref, lines_ref, table_ref, *refs,
):
    state_ref, deposit_ref = refs[-2:]
    nblocks = brick_ref.shape[0]
    room = (list_ref.shape[0] - 2) // 2
    sub = row_ids(8)
    row_y = row_ids(REACH_Y).astype(jnp.float32)
    row_z = row_ids(REACH_Z).astype(jnp.float32)
    lane = lane_ids(REACH_Y)

    def hat(rows, inside, along):
        return jnp.where(rows == inside, 1.0 - along, 0.0) + jnp.where(rows == inside + 1.0, along, 0.0)

    def loaded(at):
        k = list_ref[at]
        brick = jnp.where(k < nblocks, brick_ref[jnp.minimum(k, nblocks - 1)], 0)
        brick_x = lax.div(brick, count_y * count_z)
        brick_y = lax.rem(lax.div(brick, count_z), count_y)
        brick_z = lax.rem(brick, count_z)
        sel = jnp.where(brick_z == count_z - 1, 1, 0)
        pair = brick_x * count_y + brick_y
        start = pl.multiple_of((sel * count_x * count_y + pair) * comps * SPREAD, 8)
        first = pl.multiple_of(pair * comps * rows_z + brick_z * BZ, 8)
        window = jnp.concatenate([lines_ref[pl.ds(first + c * rows_z, REACH_Z)] for c in range(comps)], axis=0)
        table = table_ref[pl.ds(pl.multiple_of(k * TABLE_ROWS, TABLE_ROWS), TABLE_ROWS)]
        rows = [table[i : i + 1] for i in range(TABLE_ROWS)]
        return k, start, brick_z * BZ, window, rows

    def moved_of(window, rows):
        weight_y = hat(row_y, rows[IN_Y], rows[ALONG_Y])
        weight_z = hat(row_z, rows[IN_Z], rows[ALONG_Z])
        main, rest = parts_of(jnp.concatenate([rows[WEIGHT + a] * weight_y for a in range(REACH_X)], axis=0))
        unused = jnp.zeros((LANES - 3 * SPREAD, LANES), jnp.float32)
        table = jnp.concatenate([main, main, rest, unused], axis=0).astype(jnp.bfloat16)
        seen = lax.dot_general(
            window.astype(jnp.bfloat16), table, (((1,), (0,)), ((), ())), preferred_element_type=jnp.float32
        )
        rate = 1.0 / rows[RESPONSE]
        state, moved, pushed = [], [], []
        for c in range(comps):
            gas_sample = jnp.sum(seen[c * REACH_Z : (c + 1) * REACH_Z] * weight_z, axis=0, keepdims=True)
            drag = (gas_sample - rows[MOVING + c]) * rate
            state.append(rows[MOVING + c] + TIME_STEP * drag)
            moved.append(rows[OFFSET + c] + TIME_STEP * state[c])
            pushed.append(drag * weight_z)
        pushed.append(jnp.zeros((LANES - comps * REACH_Z, LANES), jnp.float32))
        push_main, push_rest = parts_of(jnp.concatenate(pushed, axis=0))
        push = jnp.concatenate([push_main, push_rest, push_main], axis=1).astype(jnp.bfloat16)
        spread = jnp.concatenate([main, main, rest], axis=1).astype(jnp.bfloat16)
        shares = lax.dot_general(spread, push, (((1,), (1,)), ((), ())), preferred_element_type=jnp.float32)
        tile = jnp.broadcast_to(rows[RESPONSE], (STATE, LANES))
        for i, value in enumerate(state + moved):
            tile = jnp.where(sub == i, value, tile)
        return tile, shares

    count = list_ref[2 * room + late]

    @pl.loop(0, (count + UNROLL - 1) // UNROLL)
    def _(group):
        at = late * room + group * UNROLL
        taken = [loaded(at + u) for u in range(UNROLL)]
        results = [moved_of(window, rows) for _, _, _, window, rows in taken]
        parts = []
        for (_, _, first_z, _, _), (_, shares) in zip(taken, results):
            within = ((lane - first_z) & (LANES - 1)) < REACH_Z
            parts.append([])
            for c in range(comps):
                shift = (first_z - c * REACH_Z + LANES) & (LANES - 1)
                for a in range(REACH_X):
                    part = pltpu.roll(shares[a * REACH_Y : (a + 1) * REACH_Y], shift, 1)
                    parts[-1].append(jnp.where(within, part, 0.0))
        for (k, _, _, _, _), (tile, _) in zip(taken, results):
            state_ref[pl.ds(pl.multiple_of(STATE * k, STATE), STATE)] = tile
        for (_, start, _, _, _), mine in zip(taken, parts):
            spots = [pl.ds(start + i * REACH_Y, REACH_Y) for i in range(comps * REACH_X)]
            sums = [deposit_ref[spot] + part for spot, part in zip(spots, mine)]
            for spot, total in zip(spots, sums):
                deposit_ref[spot] = total


def merge_kernel(tiles_ref, plane_ref):
    _, comps, planes, _, _ = plane_ref.shape
    count_x, count_y = (planes - 1) // BX, tiles_ref.shape[0] // (2 * ((planes - 1) // BX) * comps * SPREAD)
    top = row_ids(REACH_Y) >= BY

    for sel in (0, 1):
        for c in range(comps):
            for x in range(planes):
                bricks = [(x // BX, x % BX)] if x < planes - 1 else []
                if x and x % BX == 0:
                    bricks.append((x // BX - 1, BX))

                def tile(q):
                    total = None
                    for p, a in bricks:
                        at = (((sel * count_x + p) * count_y + q) * comps + c) * SPREAD + a * REACH_Y
                        value = tiles_ref[at : at + REACH_Y]
                        total = value if total is None else total + value
                    return total

                carried = None
                for q in range(0, count_y, 2):
                    here = tile(q)
                    if carried is not None:
                        here = here + carried
                    between = pltpu.roll(tile(q + 1), BY, 0)
                    here = here + jnp.where(top, between, 0.0)
                    carried = jnp.where(top, 0.0, between)
                    plane_ref[sel, c, x, q * BY : q * BY + REACH_Y] = here
                plane_ref[sel, c, x, count_y * BY :] = carried


def send_kernel(push, diffuse, crossing_ref, state_ref, grid_ref, deposit_ref, leaving_ref, velocity_ref, y_ref, x_ref, z_ref):
    comps, size_x = grid_ref.shape[0], grid_ref.shape[1] - 2
    size_y = z_ref.shape[0]
    nblocks = velocity_ref.shape[1]
    slots = crossing_ref.shape[1]
    rows = STATE * slots
    first = odd("gy") == 0
    velocity = [state_ref[pl.ds(c, nblocks, stride=STATE)] for c in range(comps)]
    for face in range(6):
        tiles = []
        for slot in range(slots):
            block = crossing_ref[face, slot]
            spot = pl.ds(pl.multiple_of(jnp.maximum(block, 0) * STATE, STATE), STATE)
            live = jnp.full((STATE, LANES), block, jnp.int32) >= 0
            tiles.append(jnp.where(live, state_ref[spot], 0.0))
        leaving_ref[face] = jnp.concatenate(tiles, axis=0)
    y_ref[0, 0:rows] = jnp.where(first, leaving_ref[2], leaving_ref[3])
    y_ref[1, 0:rows] = jnp.where(first, leaving_ref[3], leaving_ref[2])
    for c in range(comps):
        velocity_ref[c] = velocity[c]
    lane = lane_ids(ROWS_Y)
    face = jnp.zeros((ROWS_Y, LANES), jnp.float32)
    for c in range(comps):
        for x in range(size_x + 1):
            beyond = push * deposit_ref[1, c, x]
            if x < size_x:
                behind = diffuse * turned(grid_ref[c, x + 1, 0:size_y], 1)
                beyond = jnp.concatenate([beyond[:size_y] + behind, beyond[size_y:]], axis=0)
            place = PACK * c + x
            face = jnp.where(lane == place, turned(beyond, place), face)
        wrapped = jnp.where(lane_ids(size_x) == 0, 0.0, deposit_ref[1, c, 0:size_x, size_y])
        line = diffuse * grid_ref[c, 1 : size_x + 1, size_y - 1] + push * (deposit_ref[0, c, 0:size_x, size_y] + wrapped)
        y_ref[0, rows + c * ROWS_Y : rows + c * ROWS_Y + size_x] = line
        wrapped = jnp.where(lane_ids(ROWS_Y) == 0, 0.0, deposit_ref[1, c, size_x])
        total = push * (deposit_ref[0, c, size_x] + wrapped)
        x_ref[c * size_y : (c + 1) * size_y] = diffuse * grid_ref[c, size_x, 0:size_y] + total[:size_y]
        at = rows + c * ROWS_Y + size_x
        y_ref[0, at : at + 8] = total[size_y:]
    z_ref[...] = face[:size_y]
    y_ref[0, rows + size_x + 1 : rows + size_x + 2] = face[size_y : size_y + 1]
    y_ref[1, rows:] = y_ref[0, rows:]


def base_kernel(push, diffuse, grid_ref, deposit_ref, top_ref, base_ref):
    comps, size_x, size_y, size_z = base_ref.shape
    lane = lane_ids(size_y)
    top = top_ref[0:size_y]
    for c in range(comps):
        for x in range(size_x):
            here = grid_ref[c, x + 1, 0:size_y]
            laplace = grid_ref[c, x + 2, 0:size_y]
            if x:
                laplace = laplace + grid_ref[c, x, 0:size_y]
            before = jnp.where(row_ids(size_y) == 0, 0.0, pltpu.roll(here, 1, 0))
            laplace = laplace + grid_ref[c, x + 1, 1 : size_y + 1] + before
            ahead = jnp.where(lane == size_z - 1, turned(top, size_z - 1 - (PACK * c + x)), turned(here, -1))
            laplace = laplace + ahead + jnp.where(lane == 0, 0.0, turned(here, 1)) - 6.0 * here
            total = deposit_ref[0, c, x, 0:size_y] + jnp.where(lane == 0, 0.0, deposit_ref[1, c, x, 0:size_y])
            base_ref[c, x] = here + diffuse * laplace + push * total


def below(first_ref, second_ref, rows):
    got = jnp.where(odd("gy") == 1, first_ref[rows], second_ref[rows])
    return jnp.where(lax.axis_index("gy") != 0, got, 0.0)


def relay_kernel(size_x, size_y, comps, count, first_ref, second_ref, x_in_ref, z_in_ref, leaving_ref, x_ref, z_ref, edge_ref):
    edge = comps * size_y
    x_ref[0:edge] = x_in_ref[...]
    for c in range(comps):
        at = count + c * ROWS_Y + size_x
        spot = slice(c * size_y, c * size_y + 1)
        x_ref[spot] = x_in_ref[spot] + below(first_ref, second_ref, slice(at, at + 1))
    x_ref[edge : edge + count] = leaving_ref[0]
    if x_ref.shape[0] > edge + count:
        x_ref[edge + count : edge + 2 * count] = leaving_ref[1]
    at = count + size_x + 1
    edge_ref[...] = z_in_ref[...]
    edge_ref[0:1] = z_in_ref[0:1] + below(first_ref, second_ref, slice(at, at + 1))
    up = odd("gz")
    z_ref[up, 0:count] = leaving_ref[4]
    z_ref[up, count : count + size_y] = edge_ref[...]
    z_ref[1 - up, 0:count] = leaving_ref[5]
    z_ref[1 - up, count : count + size_y] = jnp.zeros((size_y, LANES), jnp.float32)


def finish_kernel(
    count, base_ref, y1_ref, y2_ref, x_ref, minus_x_ref, z1_ref, z2_ref, edge_ref, gas_ref, arrivals_ref
):
    comps, size_x, size_y, _ = base_ref.shape
    first_row, first_lane = row_ids(size_y) == 0, lane_ids(size_y) == 0
    rows = slice(count, count + size_y)
    from_first = odd("gz") == 1
    face = jnp.where(from_first, z1_ref[rows], z2_ref[rows])
    corner = edge_ref[...]
    for c in range(comps):
        for x in range(size_x):
            at = count + c * ROWS_Y + x
            line = jnp.broadcast_to(below(y1_ref, y2_ref, slice(at, at + 1)), (size_y, LANES))
            total = base_ref[c, x] + jnp.where(first_row, line, 0.0)
            far = turned(face, -(PACK * c + x))
            if x == 0:
                total = total + x_ref[c * size_y : (c + 1) * size_y]
                far = far + turned(corner, -(PACK * c + size_x))
            gas_ref[c, x] = total + jnp.where(first_lane, far, 0.0)

    slots = arrivals_ref.shape[2]
    lower, upper = lax.axis_index("gy") != 0, lax.axis_index("gy") != lax.axis_size("gy") - 1
    odd_y = odd("gy") == 1
    for i in range(arrivals_ref.shape[1]):

        def rows_of(ref, at=0):
            return ref[pl.ds(at + i, slots, stride=STATE)]

        arrivals_ref[0, i] = rows_of(x_ref, comps * size_y)
        arrivals_ref[1, i] = rows_of(minus_x_ref, minus_x_ref.shape[0] - count)
        y1, y2 = rows_of(y1_ref), rows_of(y2_ref)
        arrivals_ref[2, i] = jnp.where(lower, jnp.where(odd_y, y1, y2), 0.0)
        arrivals_ref[3, i] = jnp.where(upper, jnp.where(odd_y, y2, y1), 0.0)
        z1, z2 = rows_of(z1_ref), rows_of(z2_ref)
        arrivals_ref[4, i] = jnp.where(from_first, z1, z2)
        arrivals_ref[5, i] = jnp.where(from_first, z2, z1)


def per_device(gas_field, velocity, fraction, response, cell_index, brick_index, crossing):
    comps, size_x, size_y, size_z = gas_field.shape
    nblocks = velocity.shape[0]
    loading = 0.5 * size_x * size_y * size_z / (nblocks * 128)
    push, diffuse = -TIME_STEP * loading, TIME_STEP * VISCOSITY
    velocity = jnp.transpose(velocity, (1, 0, 2))
    fraction = jnp.transpose(fraction, (1, 0, 2))
    spare = nblocks + 8
    rows_z = size_z + 8
    grid_shape = (comps, size_x + 2, ROWS_Y, LANES)
    lines_shape = ((size_x // BX) * (size_y // BY) * comps * rows_z, LANES)
    deposit_shape = (2 * (size_x // BX) * (size_y // BY) * comps * SPREAD, LANES)

    inputs = (gas_field, velocity, fraction, response, cell_index, brick_index, crossing)
    inputs = [pltpu.with_memory_space_constraint(array, pltpu.HBM) for array in inputs]
    grid, face, plane, velocity, fraction, response, cell_index, brick_index, crossing = call(
        begin_kernel,
        [grid_shape, (size_y, LANES), (comps * size_y, LANES)]
        + [jax.ShapeDtypeStruct(array.shape, array.dtype) for array in inputs[1:]],
        *inputs, hbm=range(7), scratch=(pltpu.SemaphoreType.DMA((7,)),), limit=40,
    )
    from_z = moved_along(face, "gz", -1)
    from_x = moved_along(plane, "gx", -1)
    from_xz = moved_diagonally(face, -1)
    lines, deposit, table, ready, blocks = call(
        prepare_kernel,
        [
            lines_shape,
            deposit_shape,
            (TABLE_ROWS * spare, LANES),
            (8, LANES),
            jax.ShapeDtypeStruct((2 * (nblocks + UNROLL) + 2,), jnp.int32),
        ],
        grid, velocity, fraction, response, cell_index, brick_index,
        smem=(5,), smem_outs=(4,), cycles=3000,
    )
    line_rows = -(-(comps * size_x + comps + 1) // 8) * 8
    (y_lines,) = call(y_lines_kernel, [(line_rows, LANES)], grid, from_z, from_x, from_xz, ready)
    y1, y2 = swapped_y((y_lines, y_lines))
    square = pltpu.VMEM((LANES, LANES), jnp.float32)
    grid, lines, top = call(
        halo_xz_kernel, [grid_shape, lines_shape, (LANES, LANES)], grid, lines, from_z, from_x, from_xz,
        aliases={0: 0, 1: 1}, scratch=(square,), cycles=1000,
    )

    def advance(late, lines, deposit, *state):
        return call(
            functools.partial(blocks_kernel, late, comps, size_x // BX, size_y // BY, size_z // BZ, rows_z),
            [(STATE * spare, LANES), deposit_shape], blocks, brick_index, lines, table, deposit, *state,
            smem=(0, 1), aliases={4: 1, 5: 0} if state else {4: 1}, cycles=6000 - 4000 * late,
        )

    state, deposit = advance(0, lines, deposit)
    grid, lines = call(
        functools.partial(halo_y_kernel, size_y), [grid_shape, lines_shape], grid, lines, top, y1, y2,
        aliases={0: 0, 1: 1}, scratch=(square,), cycles=1000,
    )
    state, deposit = advance(1, lines, deposit, state)

    (deposit,) = call(merge_kernel, [(2, comps, size_x + 1, ROWS_Y, LANES)], deposit, cycles=500)
    count = STATE * crossing.shape[1]
    leaving, velocity_next, to_y, to_x, to_z = call(
        functools.partial(send_kernel, push, diffuse),
        [
            (6, count, LANES),
            (comps, nblocks, LANES),
            (2, count + comps * ROWS_Y, LANES),
            (comps * size_y, LANES),
            (size_y, LANES),
        ],
        crossing, state, grid, deposit, smem=(0,), cycles=1000,
    )
    y1, y2 = swapped_y((to_y[0], to_y[1]))
    (base,) = call(
        functools.partial(base_kernel, push, diffuse), [gas_field.shape], grid, deposit, top, cycles=1000,
    )
    edge = comps * size_y
    both = lax.axis_size("gx") == 2
    to_x, to_z, to_xz = call(
        functools.partial(relay_kernel, size_x, size_y, comps, count),
        [(edge + (2 if both else 1) * count, LANES), (2, count + size_y, LANES), (size_y, LANES)],
        y1, y2, to_x, to_z, leaving,
    )
    got_x = moved_along(to_x, "gx", 1)
    z1, z2 = swapped_z((to_z[0], to_z[1]))
    got_xz = moved_diagonally(to_xz, 1)
    got_mx = got_x if both else moved_along(leaving[1], "gx", -1)
    gas_next, arrivals = call(
        functools.partial(finish_kernel, count), [gas_field.shape, (6, 7, crossing.shape[1], LANES)],
        base, y1, y2, got_x, got_mx, z1, z2, got_xz,
    )
    return gas_next, jnp.transpose(velocity_next, (1, 0, 2)), jnp.transpose(arrivals, (0, 2, 1, 3))


def solution(mesh):
    owner = ("gx", "gz", "gy")
    in_specs = (
        P(None, "gx", "gy", "gz"),
        P(owner, None, None),
        P(owner, None, None),
        P(owner, None),
        P(owner, None),
        P(owner),
        P(owner, None),
    )
    out_specs = (
        P(None, "gx", "gy", "gz"),
        P(owner, None, None),
        P(owner, None, None, None),
    )
    return jax.shard_map(
        per_device, mesh=mesh, in_specs=in_specs, out_specs=out_specs, check_vma=False
    )
```

```python
import functools

import jax
import jax.numpy as jnp
from jax import lax
from jax.experimental import pallas as pl
from jax.experimental.pallas import tpu as pltpu
from jax.sharding import PartitionSpec as P

BX = 4
BY = 4
BZ = 8

TIME_STEP = 0.25
VISCOSITY = 0.4

LANES = 128
PACK = 32
ROWS_Y = 24
REACH_X = BX + 1
REACH_Y = 8
SPREAD = REACH_X * REACH_Y
REACH_Z = 2 * BZ
UNROLL = 8

WEIGHT, ALONG_Y, IN_Y, ALONG_Z, IN_Z, RESPONSE, MOVING, OFFSET = 0, 5, 6, 7, 8, 9, 10, 13
TABLE_ROWS = 16
STATE = 8

VMEM = pl.BlockSpec(memory_space=pltpu.VMEM)
SMEM = pl.BlockSpec(memory_space=pltpu.SMEM)
HBM = pl.BlockSpec(memory_space=pltpu.HBM)


def moved_along(block, axis, distance):
    count = lax.axis_size(axis)
    return lax.ppermute(block, axis, [(i, (i + distance) % count) for i in range(count)])


def swapped_z(blocks):
    count = lax.axis_size("gz")
    first = [(i, i ^ 1) for i in range(count)]
    second = [(i, (((i + 1) ^ 1) - 1) % count) for i in range(count)]
    return lax.ppermute(blocks[0], "gz", first), lax.ppermute(blocks[1], "gz", second)


def swapped_y(blocks):
    nz, ny = lax.axis_size("gz"), lax.axis_size("gy")
    first = [(j, j ^ 1) for j in range(ny)]
    second = []
    for k in range(nz):
        second.append((k * ny, (k ^ 1) * ny))
        second.append((k * ny + ny - 1, (k ^ 1) * ny + ny - 1))
        second.extend((k * ny + j, k * ny + ((j + 1) ^ 1) - 1) for j in range(1, ny - 1))
    return lax.ppermute(blocks[0], "gy", first), lax.ppermute(blocks[1], ("gz", "gy"), second)


def moved_diagonally(block, distance):
    nx, nz = lax.axis_size("gx"), lax.axis_size("gz")
    route = [(i * nz + k, (i + distance) % nx * nz + (k + distance) % nz) for i in range(nx) for k in range(nz)]
    return lax.ppermute(block, ("gx", "gz"), route)


def call(body, outs, *operands, smem=(), hbm=(), smem_outs=(), scratch=(), aliases=None, cycles=0, limit=40):
    return pl.pallas_call(
        body,
        out_shape=[o if isinstance(o, jax.ShapeDtypeStruct) else jax.ShapeDtypeStruct(o, jnp.float32) for o in outs],
        in_specs=[SMEM if i in smem else HBM if i in hbm else VMEM for i in range(len(operands))],
        out_specs=[SMEM if i in smem_outs else VMEM for i in range(len(outs))],
        scratch_shapes=list(scratch),
        input_output_aliases=aliases or {},
        compiler_params=pltpu.CompilerParams(vmem_limit_bytes=limit * 1024 * 1024),
        cost_estimate=pl.CostEstimate(flops=cycles * 4096, bytes_accessed=cycles * 1024, transcendentals=0),
    )(*operands)


def lane_ids(rows):
    return lax.broadcasted_iota(jnp.int32, (rows, LANES), 1)


def row_ids(rows):
    return lax.broadcasted_iota(jnp.int32, (rows, LANES), 0)


def turned(value, shift):
    shift = shift % LANES
    return pltpu.roll(value, shift, 1) if shift else value


def odd(axis):
    return lax.axis_index(axis) % 2


def begin_kernel(
    gas_ref, velocity_in, fraction_in, response_in, cell_in, brick_in, crossing_in,
    grid_ref, face_ref, plane_ref, velocity_ref, fraction_ref, response_ref, cell_ref, brick_ref, crossing_ref, sems,
):
    comps, size_x, size_y, _ = gas_ref.shape
    pairs = [
        (gas_ref, grid_ref.at[:, 1 : size_x + 1, 0:size_y]),
        (velocity_in, velocity_ref), (fraction_in, fraction_ref), (response_in, response_ref),
        (cell_in, cell_ref), (brick_in, brick_ref), (crossing_in, crossing_ref),
    ]
    copies = [pltpu.make_async_copy(source, target, sems.at[i]) for i, (source, target) in enumerate(pairs)]
    for copy in copies:
        copy.start()
    zeros = jnp.zeros((ROWS_Y, LANES), jnp.float32)
    for c in range(comps):
        grid_ref[c, 0] = zeros
        grid_ref[c, size_x + 1] = zeros
        for x in range(size_x):
            grid_ref[c, x + 1, size_y:] = zeros[size_y:]
    copies[0].wait()
    lane = lane_ids(size_y)
    face = jnp.zeros((size_y, LANES), jnp.float32)
    for c in range(comps):
        plane_ref[c * size_y : (c + 1) * size_y] = grid_ref[c, 1, 0:size_y]
        for x in range(size_x):
            place = PACK * c + x
            face = jnp.where(lane == place, turned(grid_ref[c, x + 1, 0:size_y], place), face)
    face_ref[...] = face
    for copy in copies[1:]:
        copy.wait()


def parts_of(value):
    main = value.astype(jnp.bfloat16).astype(jnp.float32)
    return main, value - main


def lay_out(grid_ref, lines_ref, p, q, size_y, size_z):
    comps = grid_ref.shape[0]
    rows_z = size_z + 8
    count_y = size_y // BY
    for c in range(comps):
        planes = [grid_ref[c, p * BX + a + 1, q * BY : q * BY + REACH_Y] for a in range(REACH_X)]
        main, rest = parts_of(jnp.concatenate(planes, axis=0))
        stack = jnp.concatenate([main, rest, main, jnp.zeros((LANES - 3 * SPREAD, LANES), jnp.float32)], axis=0)
        at = ((p * count_y + q) * comps + c) * rows_z
        lines_ref[at : at + size_z] = jnp.transpose(stack)


def lay_out_top(turned_ref, lines_ref, q, comps, count_x, count_y, size_z):
    lane = lane_ids(count_x)
    rows_z = size_z + 8
    for c in range(comps):
        total = jnp.zeros((count_x, LANES), jnp.float32)
        for a in range(REACH_X):
            rows = turned_ref[pl.ds(PACK * c + a, count_x, stride=BX)]
            total = jnp.where(lane // REACH_Y == a, turned(rows, a * REACH_Y - q * BY), total)
        main, rest = parts_of(total)
        line = main + turned(rest, SPREAD) + turned(main, 2 * SPREAD)
        for p in range(count_x):
            at = ((p * count_y + q) * comps + c) * rows_z + size_z
            lines_ref[at : at + 1] = line[p : p + 1]


def prepare_kernel(
    grid_ref, velocity_ref, fraction_ref, response_ref, cell_ref, brick_ref,
    lines_ref, deposit_ref, table_ref, ready_ref, list_ref,
):
    comps, size_x, size_y, size_z = grid_ref.shape[0], grid_ref.shape[1] - 2, grid_ref.shape[2] - 8, grid_ref.shape[3]
    nblocks = velocity_ref.shape[1]
    count_x, count_y, count_z = size_x // BX, size_y // BY, size_z // BZ
    rows_z = size_z + 8

    room = nblocks + UNROLL

    def visit(k, counts):
        late = jnp.where(lax.rem(lax.div(brick_ref[k], count_z), count_y) == count_y - 1, 1, 0)
        list_ref[jnp.where(late == 1, room + counts[1], counts[0])] = k
        return counts[0] + 1 - late, counts[1] + late

    early, late = lax.fori_loop(0, nblocks, visit, (jnp.int32(0), jnp.int32(0)), unroll=8)
    for base, count in ((0, early), (room, late)):
        for u in range(UNROLL):
            list_ref[base + count + u] = nblocks
    list_ref[2 * room] = early
    list_ref[2 * room + 1] = late
    ready_ref[...] = jnp.zeros_like(ready_ref)

    deposit_ref[...] = jnp.zeros_like(deposit_ref)
    for p in range(count_x):
        for q in range(count_y):
            for c in range(comps):
                at = ((p * count_y + q) * comps + c) * rows_z + size_z
                lines_ref[at : at + 8] = jnp.zeros((8, LANES), jnp.float32)
    for p in range(count_x - 1):
        for q in range(count_y - 1):
            lay_out(grid_ref, lines_ref, p, q, size_y, size_z)

    cells = cell_ref[...]
    cell_x, cell_y, cell_z = cells // (BY * BZ), cells // BZ % BY, cells % BZ
    along_x = fraction_ref[0]

    def put(row, value):
        table_ref[pl.ds(row, nblocks, stride=TABLE_ROWS)] = value

    for a in range(REACH_X):
        put(WEIGHT + a, jnp.where(cell_x == a, 1.0 - along_x, 0.0) + jnp.where(cell_x == a - 1, along_x, 0.0))
    put(ALONG_Y, fraction_ref[1])
    put(IN_Y, cell_y.astype(jnp.float32))
    put(ALONG_Z, fraction_ref[2])
    put(IN_Z, cell_z.astype(jnp.float32))
    put(RESPONSE, response_ref[...])
    for c in range(comps):
        put(MOVING + c, velocity_ref[c])
        put(OFFSET + c, fraction_ref[c])
    spare = table_ref.shape[0] - nblocks * TABLE_ROWS
    row = row_ids(spare)
    table_ref[nblocks * TABLE_ROWS :] = jnp.where(row % TABLE_ROWS == RESPONSE, 1.0, 0.0)


def y_lines_kernel(grid_ref, face_ref, from_x_ref, edge_ref, ready_ref, out_ref):
    comps, size_x = grid_ref.shape[0], grid_ref.shape[1] - 2
    size_y = face_ref.shape[0]
    for c in range(comps):
        out_ref[c * size_x : (c + 1) * size_x] = grid_ref[c, 1 : size_x + 1, 0]
        out_ref[comps * size_x + c : comps * size_x + c + 1] = from_x_ref[c * size_y : c * size_y + 1]
    line = jnp.where(lane_ids(8) % PACK == size_x, turned(edge_ref[0:8], size_x), face_ref[0:8])
    out_ref[comps * size_x + comps : comps * size_x + comps + 1] = line[0:1]


def halo_xz_kernel(grid_in_ref, lines_in_ref, face_ref, from_x_ref, edge_ref, grid_ref, lines_ref, top_ref, turned_ref):
    comps, size_x = grid_ref.shape[0], grid_ref.shape[1] - 2
    size_y, size_z = face_ref.shape[0], grid_ref.shape[3]
    count_x, count_y = size_x // BX, size_y // BY
    for c in range(comps):
        grid_ref[c, size_x + 1, 0:size_y] = from_x_ref[c * size_y : (c + 1) * size_y]
    for q in range(count_y - 1):
        lay_out(grid_ref, lines_ref, count_x - 1, q, size_y, size_z)
    top = jnp.where(lane_ids(size_y) % PACK == size_x, turned(edge_ref[...], size_x), face_ref[...])
    top_ref[0:size_y] = top
    top_ref[size_y:] = jnp.zeros((LANES - size_y, LANES), jnp.float32)
    turned_ref[...] = jnp.transpose(top_ref[...])
    for q in range(count_y - 1):
        lay_out_top(turned_ref, lines_ref, q, comps, count_x, count_y, size_z)


def halo_y_kernel(size_y, grid_in_ref, lines_in_ref, top_in_ref, first_ref, second_ref, grid_ref, lines_ref, turned_ref):
    comps, size_x, size_z = grid_ref.shape[0], grid_ref.shape[1] - 2, grid_ref.shape[3]
    count_x, count_y = size_x // BX, size_y // BY
    inside = lax.axis_index("gy") != lax.axis_size("gy") - 1
    even = odd("gy") == 0
    kept = (row_ids(8) == 0) & inside

    def line_at(row):
        line = jnp.where(even, first_ref[row : row + 1], second_ref[row : row + 1])
        return jnp.where(kept, jnp.broadcast_to(line, (8, LANES)), 0.0)

    for c in range(comps):
        for x in range(size_x + 1):
            grid_ref[c, x + 1, size_y:] = line_at(c * size_x + x if x < size_x else comps * size_x + c)
    for p in range(count_x):
        lay_out(grid_ref, lines_ref, p, count_y - 1, size_y, size_z)
    corner = line_at(comps * size_x + comps)
    rest = jnp.zeros((LANES - size_y - 8, LANES), jnp.float32)
    turned_ref[...] = jnp.transpose(jnp.concatenate([top_in_ref[0:size_y], corner, rest], axis=0))
    lay_out_top(turned_ref, lines_ref, count_y - 1, comps, count_x, count_y, size_z)


def blocks_kernel(
    late, comps, count_x, count_y, count_z, rows_z,
    list_ref, brick_ref, lines_ref, table_ref, *refs,
):
    state_ref, deposit_ref = refs[-2:]
    nblocks = brick_ref.shape[0]
    room = (list_ref.shape[0] - 2) // 2
    sub = row_ids(8)
    row_y = row_ids(REACH_Y).astype(jnp.float32)
    row_z = row_ids(REACH_Z).astype(jnp.float32)
    lane = lane_ids(REACH_Y)

    def hat(rows, inside, along):
        return jnp.where(rows == inside, 1.0 - along, 0.0) + jnp.where(rows == inside + 1.0, along, 0.0)

    def loaded(at):
        k = list_ref[at]
        brick = jnp.where(k < nblocks, brick_ref[jnp.minimum(k, nblocks - 1)], 0)
        brick_x = lax.div(brick, count_y * count_z)
        brick_y = lax.rem(lax.div(brick, count_z), count_y)
        brick_z = lax.rem(brick, count_z)
        sel = jnp.where(brick_z == count_z - 1, 1, 0)
        pair = brick_x * count_y + brick_y
        start = pl.multiple_of((sel * count_x * count_y + pair) * comps * SPREAD, 8)
        first = pl.multiple_of(pair * comps * rows_z + brick_z * BZ, 8)
        window = jnp.concatenate([lines_ref[pl.ds(first + c * rows_z, REACH_Z)] for c in range(comps)], axis=0)
        table = table_ref[pl.ds(pl.multiple_of(k * TABLE_ROWS, TABLE_ROWS), TABLE_ROWS)]
        rows = [table[i : i + 1] for i in range(TABLE_ROWS)]
        return k, start, brick_z * BZ, window, rows

    def weighted(rows):
        weight_y = hat(row_y, rows[IN_Y], rows[ALONG_Y])
        weight_z = hat(row_z, rows[IN_Z], rows[ALONG_Z])
        weight = jnp.concatenate([rows[WEIGHT + a] * weight_y for a in range(REACH_X)], axis=0)
        return weight_z, *parts_of(weight)

    def stepped(seen, weight_z, rows):
        rate = 1.0 / rows[RESPONSE]
        state, moved, pushed = [], [], []
        for c in range(comps):
            gas_sample = jnp.sum(seen[c * REACH_Z : (c + 1) * REACH_Z] * weight_z, axis=0, keepdims=True)
            drag = (gas_sample - rows[MOVING + c]) * rate
            state.append(rows[MOVING + c] + TIME_STEP * drag)
            moved.append(rows[OFFSET + c] + TIME_STEP * state[c])
            pushed.append(drag * weight_z)
        tile = jnp.broadcast_to(rows[RESPONSE], (STATE, LANES))
        for i, value in enumerate(state + moved):
            tile = jnp.where(sub == i, value, tile)
        gap = jnp.zeros((LANES // 2 - comps * REACH_Z, LANES), jnp.float32)
        main, rest = parts_of(jnp.concatenate(pushed, axis=0))
        return tile, jnp.concatenate([main, gap, rest, gap], axis=0)

    def pair_of(one, two):
        tables, windows, weights = [], [], []
        for _, _, _, window, rows in (one, two):
            weight_z, main, rest = weighted(rows)
            weights.append((weight_z, main, rest))
            unused = jnp.zeros((LANES - 3 * SPREAD, LANES), jnp.float32)
            tables.append(jnp.concatenate([main, main, rest, unused], axis=0).astype(jnp.bfloat16))
            windows.append(window)
        seen = lax.dot_general(
            jnp.concatenate(windows, axis=0).astype(jnp.bfloat16), jnp.concatenate(tables, axis=1),
            (((1,), (0,)), ((), ())), preferred_element_type=jnp.float32,
        )
        height = comps * REACH_Z
        tiles, pushes, spreads = [], [], []
        for i, (_, _, _, _, rows) in enumerate((one, two)):
            mine = seen[i * height : (i + 1) * height, i * LANES : (i + 1) * LANES]
            tile, push = stepped(mine, weights[i][0], rows)
            tiles.append(tile)
            pushes.append(push)
            spreads.extend(weights[i][1:])
        shares = lax.dot_general(
            jnp.concatenate(spreads, axis=0).astype(jnp.bfloat16), jnp.concatenate(pushes, axis=0).astype(jnp.bfloat16),
            (((1,), (1,)), ((), ())), preferred_element_type=jnp.float32,
        )
        results = []
        for i, tile in enumerate(tiles):
            mine = shares[2 * i * SPREAD : 2 * (i + 1) * SPREAD, i * LANES : (i + 1) * LANES]
            mine = mine[:SPREAD] + mine[SPREAD:]
            results.append((tile, mine + pltpu.roll(mine, LANES // 2, 1)))
        return results

    count = list_ref[2 * room + late]

    @pl.loop(0, (count + UNROLL - 1) // UNROLL)
    def _(group):
        at = late * room + group * UNROLL
        taken = [loaded(at + u) for u in range(UNROLL)]
        results = []
        for u in range(0, UNROLL, 2):
            results.extend(pair_of(taken[u], taken[u + 1]))
        parts = []
        for (_, _, first_z, _, _), (_, shares) in zip(taken, results):
            within = ((lane - first_z) & (LANES - 1)) < REACH_Z
            parts.append([])
            for c in range(comps):
                shift = (first_z - c * REACH_Z + LANES) & (LANES - 1)
                for a in range(REACH_X):
                    part = pltpu.roll(shares[a * REACH_Y : (a + 1) * REACH_Y], shift, 1)
                    parts[-1].append(jnp.where(within, part, 0.0))
        for (k, _, _, _, _), (tile, _) in zip(taken, results):
            state_ref[pl.ds(pl.multiple_of(STATE * k, STATE), STATE)] = tile
        for (_, start, _, _, _), mine in zip(taken, parts):
            spots = [pl.ds(start + i * REACH_Y, REACH_Y) for i in range(comps * REACH_X)]
            sums = [deposit_ref[spot] + part for spot, part in zip(spots, mine)]
            for spot, total in zip(spots, sums):
                deposit_ref[spot] = total


def merge_kernel(tiles_ref, plane_ref):
    _, comps, planes, _, _ = plane_ref.shape
    count_x, count_y = (planes - 1) // BX, tiles_ref.shape[0] // (2 * ((planes - 1) // BX) * comps * SPREAD)
    top = row_ids(REACH_Y) >= BY

    for sel in (0, 1):
        for c in range(comps):
            for x in range(planes):
                bricks = [(x // BX, x % BX)] if x < planes - 1 else []
                if x and x % BX == 0:
                    bricks.append((x // BX - 1, BX))

                def tile(q):
                    total = None
                    for p, a in bricks:
                        at = (((sel * count_x + p) * count_y + q) * comps + c) * SPREAD + a * REACH_Y
                        value = tiles_ref[at : at + REACH_Y]
                        total = value if total is None else total + value
                    return total

                carried = None
                for q in range(0, count_y, 2):
                    here = tile(q)
                    if carried is not None:
                        here = here + carried
                    between = pltpu.roll(tile(q + 1), BY, 0)
                    here = here + jnp.where(top, between, 0.0)
                    carried = jnp.where(top, 0.0, between)
                    plane_ref[sel, c, x, q * BY : q * BY + REACH_Y] = here
                plane_ref[sel, c, x, count_y * BY :] = carried


def leave_kernel(crossing_ref, state_ref, leaving_ref, velocity_ref):
    comps, nblocks = velocity_ref.shape[:2]
    slots = crossing_ref.shape[1]
    velocity = [state_ref[pl.ds(c, nblocks, stride=STATE)] for c in range(comps)]
    for face in range(6):
        tiles = []
        for slot in range(slots):
            block = crossing_ref[face, slot]
            spot = pl.ds(pl.multiple_of(jnp.maximum(block, 0) * STATE, STATE), STATE)
            live = jnp.full((STATE, LANES), block, jnp.int32) >= 0
            tiles.append(jnp.where(live, state_ref[spot], 0.0))
        leaving_ref[face] = jnp.concatenate(tiles, axis=0)
    for c in range(comps):
        velocity_ref[c] = velocity[c]


def send_kernel(push, diffuse, leaving_ref, grid_ref, deposit_ref, y_ref, x_ref, z_ref):
    comps, size_x = grid_ref.shape[0], grid_ref.shape[1] - 2
    size_y = z_ref.shape[0]
    rows = leaving_ref.shape[1]
    first = odd("gy") == 0
    y_ref[0, 0:rows] = jnp.where(first, leaving_ref[2], leaving_ref[3])
    y_ref[1, 0:rows] = jnp.where(first, leaving_ref[3], leaving_ref[2])
    lane = lane_ids(ROWS_Y)
    face = jnp.zeros((ROWS_Y, LANES), jnp.float32)
    for c in range(comps):
        for x in range(size_x + 1):
            beyond = push * deposit_ref[1, c, x]
            if x < size_x:
                behind = diffuse * turned(grid_ref[c, x + 1, 0:size_y], 1)
                beyond = jnp.concatenate([beyond[:size_y] + behind, beyond[size_y:]], axis=0)
            place = PACK * c + x
            face = jnp.where(lane == place, turned(beyond, place), face)
        wrapped = jnp.where(lane_ids(size_x) == 0, 0.0, deposit_ref[1, c, 0:size_x, size_y])
        line = diffuse * grid_ref[c, 1 : size_x + 1, size_y - 1] + push * (deposit_ref[0, c, 0:size_x, size_y] + wrapped)
        y_ref[0, rows + c * ROWS_Y : rows + c * ROWS_Y + size_x] = line
        wrapped = jnp.where(lane_ids(ROWS_Y) == 0, 0.0, deposit_ref[1, c, size_x])
        total = push * (deposit_ref[0, c, size_x] + wrapped)
        x_ref[c * size_y : (c + 1) * size_y] = diffuse * grid_ref[c, size_x, 0:size_y] + total[:size_y]
        at = rows + c * ROWS_Y + size_x
        y_ref[0, at : at + 8] = total[size_y:]
    z_ref[...] = face[:size_y]
    y_ref[0, rows + size_x + 1 : rows + size_x + 2] = face[size_y : size_y + 1]
    y_ref[1, rows:] = y_ref[0, rows:]


def base_kernel(push, diffuse, grid_ref, deposit_ref, top_ref, base_ref):
    comps, size_x, size_y, size_z = base_ref.shape
    lane = lane_ids(size_y)
    top = top_ref[0:size_y]
    for c in range(comps):
        for x in range(size_x):
            here = grid_ref[c, x + 1, 0:size_y]
            laplace = grid_ref[c, x + 2, 0:size_y]
            if x:
                laplace = laplace + grid_ref[c, x, 0:size_y]
            before = jnp.where(row_ids(size_y) == 0, 0.0, pltpu.roll(here, 1, 0))
            laplace = laplace + grid_ref[c, x + 1, 1 : size_y + 1] + before
            ahead = jnp.where(lane == size_z - 1, turned(top, size_z - 1 - (PACK * c + x)), turned(here, -1))
            laplace = laplace + ahead + jnp.where(lane == 0, 0.0, turned(here, 1)) - 6.0 * here
            total = deposit_ref[0, c, x, 0:size_y] + jnp.where(lane == 0, 0.0, deposit_ref[1, c, x, 0:size_y])
            base_ref[c, x] = here + diffuse * laplace + push * total


def below(first_ref, second_ref, rows):
    got = jnp.where(odd("gy") == 1, first_ref[rows], second_ref[rows])
    return jnp.where(lax.axis_index("gy") != 0, got, 0.0)


def relay_kernel(size_x, size_y, comps, count, first_ref, second_ref, x_in_ref, z_in_ref, leaving_ref, x_ref, z_ref, edge_ref):
    edge = comps * size_y
    x_ref[0:edge] = x_in_ref[...]
    for c in range(comps):
        at = count + c * ROWS_Y + size_x
        spot = slice(c * size_y, c * size_y + 1)
        x_ref[spot] = x_in_ref[spot] + below(first_ref, second_ref, slice(at, at + 1))
    x_ref[edge : edge + count] = leaving_ref[0]
    if x_ref.shape[0] > edge + count:
        x_ref[edge + count : edge + 2 * count] = leaving_ref[1]
    at = count + size_x + 1
    edge_ref[...] = z_in_ref[...]
    edge_ref[0:1] = z_in_ref[0:1] + below(first_ref, second_ref, slice(at, at + 1))
    up = odd("gz")
    z_ref[up, 0:count] = leaving_ref[4]
    z_ref[up, count : count + size_y] = edge_ref[...]
    z_ref[1 - up, 0:count] = leaving_ref[5]
    z_ref[1 - up, count : count + size_y] = jnp.zeros((size_y, LANES), jnp.float32)


def finish_kernel(
    count, base_ref, y1_ref, y2_ref, x_ref, minus_x_ref, z1_ref, z2_ref, edge_ref, gas_ref, arrivals_ref
):
    comps, size_x, size_y, _ = base_ref.shape
    first_row, first_lane = row_ids(size_y) == 0, lane_ids(size_y) == 0
    rows = slice(count, count + size_y)
    from_first = odd("gz") == 1
    face = jnp.where(from_first, z1_ref[rows], z2_ref[rows])
    corner = edge_ref[...]
    for c in range(comps):
        for x in range(size_x):
            at = count + c * ROWS_Y + x
            line = jnp.broadcast_to(below(y1_ref, y2_ref, slice(at, at + 1)), (size_y, LANES))
            total = base_ref[c, x] + jnp.where(first_row, line, 0.0)
            far = turned(face, -(PACK * c + x))
            if x == 0:
                total = total + x_ref[c * size_y : (c + 1) * size_y]
                far = far + turned(corner, -(PACK * c + size_x))
            gas_ref[c, x] = total + jnp.where(first_lane, far, 0.0)

    slots = arrivals_ref.shape[2]
    lower, upper = lax.axis_index("gy") != 0, lax.axis_index("gy") != lax.axis_size("gy") - 1
    odd_y = odd("gy") == 1
    for i in range(arrivals_ref.shape[1]):

        def rows_of(ref, at=0):
            return ref[pl.ds(at + i, slots, stride=STATE)]

        arrivals_ref[0, i] = rows_of(x_ref, comps * size_y)
        arrivals_ref[1, i] = rows_of(minus_x_ref, minus_x_ref.shape[0] - count)
        y1, y2 = rows_of(y1_ref), rows_of(y2_ref)
        arrivals_ref[2, i] = jnp.where(lower, jnp.where(odd_y, y1, y2), 0.0)
        arrivals_ref[3, i] = jnp.where(upper, jnp.where(odd_y, y2, y1), 0.0)
        z1, z2 = rows_of(z1_ref), rows_of(z2_ref)
        arrivals_ref[4, i] = jnp.where(from_first, z1, z2)
        arrivals_ref[5, i] = jnp.where(from_first, z2, z1)


def per_device(gas_field, velocity, fraction, response, cell_index, brick_index, crossing):
    comps, size_x, size_y, size_z = gas_field.shape
    nblocks = velocity.shape[0]
    loading = 0.5 * size_x * size_y * size_z / (nblocks * 128)
    push, diffuse = -TIME_STEP * loading, TIME_STEP * VISCOSITY
    velocity = jnp.transpose(velocity, (1, 0, 2))
    fraction = jnp.transpose(fraction, (1, 0, 2))
    spare = nblocks + 8
    rows_z = size_z + 8
    grid_shape = (comps, size_x + 2, ROWS_Y, LANES)
    lines_shape = ((size_x // BX) * (size_y // BY) * comps * rows_z, LANES)
    deposit_shape = (2 * (size_x // BX) * (size_y // BY) * comps * SPREAD, LANES)

    inputs = (gas_field, velocity, fraction, response, cell_index, brick_index, crossing)
    inputs = [pltpu.with_memory_space_constraint(array, pltpu.HBM) for array in inputs]
    grid, face, plane, velocity, fraction, response, cell_index, brick_index, crossing = call(
        begin_kernel,
        [grid_shape, (size_y, LANES), (comps * size_y, LANES)]
        + [jax.ShapeDtypeStruct(array.shape, array.dtype) for array in inputs[1:]],
        *inputs, hbm=range(7), scratch=(pltpu.SemaphoreType.DMA((7,)),), limit=40,
    )
    from_z = moved_along(face, "gz", -1)
    from_x = moved_along(plane, "gx", -1)
    from_xz = moved_diagonally(face, -1)
    lines, deposit, table, ready, blocks = call(
        prepare_kernel,
        [
            lines_shape,
            deposit_shape,
            (TABLE_ROWS * spare, LANES),
            (8, LANES),
            jax.ShapeDtypeStruct((2 * (nblocks + UNROLL) + 2,), jnp.int32),
        ],
        grid, velocity, fraction, response, cell_index, brick_index,
        smem=(5,), smem_outs=(4,), cycles=3000,
    )
    line_rows = -(-(comps * size_x + comps + 1) // 8) * 8
    (y_lines,) = call(y_lines_kernel, [(line_rows, LANES)], grid, from_z, from_x, from_xz, ready)
    y1, y2 = swapped_y((y_lines, y_lines))
    square = pltpu.VMEM((LANES, LANES), jnp.float32)
    grid, lines, top = call(
        halo_xz_kernel, [grid_shape, lines_shape, (LANES, LANES)], grid, lines, from_z, from_x, from_xz,
        aliases={0: 0, 1: 1}, scratch=(square,), cycles=1000,
    )

    def advance(late, lines, deposit, *state):
        return call(
            functools.partial(blocks_kernel, late, comps, size_x // BX, size_y // BY, size_z // BZ, rows_z),
            [(STATE * spare, LANES), deposit_shape], blocks, brick_index, lines, table, deposit, *state,
            smem=(0, 1), aliases={4: 1, 5: 0} if state else {4: 1}, cycles=6000 - 4000 * late,
        )

    state, deposit = advance(0, lines, deposit)
    grid, lines = call(
        functools.partial(halo_y_kernel, size_y), [grid_shape, lines_shape], grid, lines, top, y1, y2,
        aliases={0: 0, 1: 1}, scratch=(square,), cycles=1000,
    )
    state, deposit = advance(1, lines, deposit, state)

    (deposit,) = call(merge_kernel, [(2, comps, size_x + 1, ROWS_Y, LANES)], deposit, cycles=500)
    count = STATE * crossing.shape[1]
    leaving, velocity_next = call(
        leave_kernel, [(6, count, LANES), (comps, nblocks, LANES)], crossing, state, smem=(0,), cycles=500,
    )
    to_y, to_x, to_z = call(
        functools.partial(send_kernel, push, diffuse),
        [(2, count + comps * ROWS_Y, LANES), (comps * size_y, LANES), (size_y, LANES)],
        leaving, grid, deposit, cycles=500,
    )
    y1, y2 = swapped_y((to_y[0], to_y[1]))
    (base,) = call(
        functools.partial(base_kernel, push, diffuse), [gas_field.shape], grid, deposit, top, cycles=1000,
    )
    edge = comps * size_y
    both = lax.axis_size("gx") == 2
    to_x, to_z, to_xz = call(
        functools.partial(relay_kernel, size_x, size_y, comps, count),
        [(edge + (2 if both else 1) * count, LANES), (2, count + size_y, LANES), (size_y, LANES)],
        y1, y2, to_x, to_z, leaving,
    )
    got_x = moved_along(to_x, "gx", 1)
    z1, z2 = swapped_z((to_z[0], to_z[1]))
    got_xz = moved_diagonally(to_xz, 1)
    got_mx = got_x if both else moved_along(leaving[1], "gx", -1)
    gas_next, arrivals = call(
        functools.partial(finish_kernel, count), [gas_field.shape, (6, 7, crossing.shape[1], LANES)],
        base, y1, y2, got_x, got_mx, z1, z2, got_xz,
    )
    return gas_next, jnp.transpose(velocity_next, (1, 0, 2)), jnp.transpose(arrivals, (0, 2, 1, 3))


def solution(mesh):
    owner = ("gx", "gz", "gy")
    in_specs = (
        P(None, "gx", "gy", "gz"),
        P(owner, None, None),
        P(owner, None, None),
        P(owner, None),
        P(owner, None),
        P(owner),
        P(owner, None),
    )
    out_specs = (
        P(None, "gx", "gy", "gz"),
        P(owner, None, None),
        P(owner, None, None, None),
    )
    return jax.shard_map(
        per_device, mesh=mesh, in_specs=in_specs, out_specs=out_specs, check_vma=False
    )
```

```python
import functools

import jax
import jax.numpy as jnp
from jax import lax
from jax.experimental import pallas as pl
from jax.experimental.pallas import tpu as pltpu
from jax.sharding import PartitionSpec as P

BX = 4
BY = 4
BZ = 8

TIME_STEP = 0.25
VISCOSITY = 0.4

LANES = 128
PACK = 32
ROWS_Y = 24
REACH_X = BX + 1
REACH_Y = 8
SPREAD = REACH_X * REACH_Y
REACH_Z = 2 * BZ
UNROLL = 4

WEIGHT, ALONG_Y, IN_Y, ALONG_Z, IN_Z, RESPONSE, MOVING, OFFSET = 0, 5, 6, 7, 8, 9, 10, 13
TABLE_ROWS = 16
STATE = 8

VMEM = pl.BlockSpec(memory_space=pltpu.VMEM)
SMEM = pl.BlockSpec(memory_space=pltpu.SMEM)
HBM = pl.BlockSpec(memory_space=pltpu.HBM)


def moved_along(block, axis, distance):
    count = lax.axis_size(axis)
    return lax.ppermute(block, axis, [(i, (i + distance) % count) for i in range(count)])


def swapped_z(blocks):
    count = lax.axis_size("gz")
    first = [(i, i ^ 1) for i in range(count)]
    second = [(i, (((i + 1) ^ 1) - 1) % count) for i in range(count)]
    return lax.ppermute(blocks[0], "gz", first), lax.ppermute(blocks[1], "gz", second)


def swapped_y(blocks):
    nz, ny = lax.axis_size("gz"), lax.axis_size("gy")
    first = [(j, j ^ 1) for j in range(ny)]
    second = []
    for k in range(nz):
        second.append((k * ny, (k ^ 1) * ny))
        second.append((k * ny + ny - 1, (k ^ 1) * ny + ny - 1))
        second.extend((k * ny + j, k * ny + ((j + 1) ^ 1) - 1) for j in range(1, ny - 1))
    return lax.ppermute(blocks[0], "gy", first), lax.ppermute(blocks[1], ("gz", "gy"), second)


def moved_diagonally(block, distance):
    nx, nz = lax.axis_size("gx"), lax.axis_size("gz")
    route = [(i * nz + k, (i + distance) % nx * nz + (k + distance) % nz) for i in range(nx) for k in range(nz)]
    return lax.ppermute(block, ("gx", "gz"), route)


def call(body, outs, *operands, smem=(), hbm=(), smem_outs=(), scratch=(), aliases=None, cycles=0, limit=40):
    return pl.pallas_call(
        body,
        out_shape=[o if isinstance(o, jax.ShapeDtypeStruct) else jax.ShapeDtypeStruct(o, jnp.float32) for o in outs],
        in_specs=[SMEM if i in smem else HBM if i in hbm else VMEM for i in range(len(operands))],
        out_specs=[SMEM if i in smem_outs else VMEM for i in range(len(outs))],
        scratch_shapes=list(scratch),
        input_output_aliases=aliases or {},
        compiler_params=pltpu.CompilerParams(vmem_limit_bytes=limit * 1024 * 1024),
        cost_estimate=pl.CostEstimate(flops=cycles * 4096, bytes_accessed=cycles * 1024, transcendentals=0),
    )(*operands)


def lane_ids(rows):
    return lax.broadcasted_iota(jnp.int32, (rows, LANES), 1)


def row_ids(rows):
    return lax.broadcasted_iota(jnp.int32, (rows, LANES), 0)


def turned(value, shift):
    shift = shift % LANES
    return pltpu.roll(value, shift, 1) if shift else value


def odd(axis):
    return lax.axis_index(axis) % 2


def begin_kernel(
    gas_ref, velocity_in, fraction_in, response_in, cell_in, brick_in, crossing_in,
    grid_ref, face_ref, plane_ref, velocity_ref, fraction_ref, response_ref, cell_ref, brick_ref, crossing_ref, sems,
):
    comps, size_x, size_y, _ = gas_ref.shape
    pairs = [
        (gas_ref, grid_ref.at[:, 1 : size_x + 1, 0:size_y]),
        (velocity_in, velocity_ref), (fraction_in, fraction_ref), (response_in, response_ref),
        (cell_in, cell_ref), (brick_in, brick_ref), (crossing_in, crossing_ref),
    ]
    copies = [pltpu.make_async_copy(source, target, sems.at[i]) for i, (source, target) in enumerate(pairs)]
    for copy in copies:
        copy.start()
    zeros = jnp.zeros((ROWS_Y, LANES), jnp.float32)

    @pl.loop(0, comps)
    def _(c):
        grid_ref[c, 0] = zeros
        grid_ref[c, size_x + 1] = zeros
        for x in range(size_x):
            grid_ref[c, x + 1, size_y:] = zeros[size_y:]

    copies[0].wait()
    lane = lane_ids(size_y)
    face_ref[...] = jnp.zeros_like(face_ref)

    @pl.loop(0, comps)
    def _(c):
        plane_ref[pl.ds(pl.multiple_of(c * size_y, 8), size_y)] = grid_ref[c, 1, 0:size_y]
        face = jnp.zeros((size_y, LANES), jnp.float32)
        for x in range(size_x):
            face = jnp.where(lane == x, turned(grid_ref[c, x + 1, 0:size_y], x), face)
        face_ref[...] = face_ref[...] + pltpu.roll(face, PACK * c, 1)

    for copy in copies[1:]:
        copy.wait()


def parts_of(value):
    main = value.astype(jnp.bfloat16).astype(jnp.float32)
    return main, value - main


def lay_out(grid_ref, lines_ref, first, last, size_y, size_z, columns):
    comps = grid_ref.shape[0]
    rows_z = size_z + 8
    count_y = size_y // BY

    @pl.loop(first, last)
    def _(p):
        @pl.loop(0, comps)
        def _(c):
            for q in columns:
                planes = [grid_ref[c, p * BX + a + 1, q * BY : q * BY + REACH_Y] for a in range(REACH_X)]
                main, rest = parts_of(jnp.concatenate(planes, axis=0))
                unused = jnp.zeros((LANES - 3 * SPREAD, LANES), jnp.float32)
                stack = jnp.concatenate([main, rest, main, unused], axis=0)
                at = pl.multiple_of(((p * count_y + q) * comps + c) * rows_z, 8)
                lines_ref[pl.ds(at, size_z)] = jnp.transpose(stack)


def lay_out_top(turned_ref, lines_ref, q, comps, count_x, count_y, size_z):
    lane = lane_ids(count_x)
    rows_z = size_z + 8
    for c in range(comps):
        total = jnp.zeros((count_x, LANES), jnp.float32)
        for a in range(REACH_X):
            rows = turned_ref[pl.ds(PACK * c + a, count_x, stride=BX)]
            total = jnp.where(lane // REACH_Y == a, turned(rows, a * REACH_Y - q * BY), total)
        main, rest = parts_of(total)
        line = main + turned(rest, SPREAD) + turned(main, 2 * SPREAD)
        for p in range(count_x):
            at = ((p * count_y + q) * comps + c) * rows_z + size_z
            lines_ref[at : at + 1] = line[p : p + 1]


def prepare_kernel(
    grid_ref, velocity_ref, fraction_ref, response_ref, cell_ref, brick_ref,
    lines_ref, deposit_ref, table_ref, ready_ref, list_ref,
):
    comps, size_x, size_y, size_z = grid_ref.shape[0], grid_ref.shape[1] - 2, grid_ref.shape[2] - 8, grid_ref.shape[3]
    nblocks = velocity_ref.shape[1]
    count_x, count_y, count_z = size_x // BX, size_y // BY, size_z // BZ
    rows_z = size_z + 8

    room = nblocks + UNROLL

    def visit(k, counts):
        late = jnp.where(lax.rem(lax.div(brick_ref[k], count_z), count_y) == count_y - 1, 1, 0)
        list_ref[jnp.where(late == 1, room + counts[1], counts[0])] = k
        return counts[0] + 1 - late, counts[1] + late

    early, late = lax.fori_loop(0, nblocks, visit, (jnp.int32(0), jnp.int32(0)), unroll=8)
    for base, count in ((0, early), (room, late)):
        for u in range(UNROLL):
            list_ref[base + count + u] = nblocks
    list_ref[2 * room] = early
    list_ref[2 * room + 1] = late
    ready_ref[...] = jnp.zeros_like(ready_ref)

    @pl.loop(0, deposit_ref.shape[0] // SPREAD)
    def _(i):
        deposit_ref[pl.ds(pl.multiple_of(i * SPREAD, 8), SPREAD)] = jnp.zeros((SPREAD, LANES), jnp.float32)

    @pl.loop(0, lines_ref.shape[0] // rows_z)
    def _(i):
        lines_ref[pl.ds(pl.multiple_of(i * rows_z + size_z, 8), 8)] = jnp.zeros((8, LANES), jnp.float32)

    lay_out(grid_ref, lines_ref, 0, count_x - 1, size_y, size_z, range(count_y - 1))
    cells = cell_ref[...]
    cell_x, cell_y, cell_z = cells // (BY * BZ), cells // BZ % BY, cells % BZ
    along_x = fraction_ref[0]

    def put(row, value):
        table_ref[pl.ds(row, nblocks, stride=TABLE_ROWS)] = value

    for a in range(REACH_X):
        put(WEIGHT + a, jnp.where(cell_x == a, 1.0 - along_x, 0.0) + jnp.where(cell_x == a - 1, along_x, 0.0))
    put(ALONG_Y, fraction_ref[1])
    put(IN_Y, cell_y.astype(jnp.float32))
    put(ALONG_Z, fraction_ref[2])
    put(IN_Z, cell_z.astype(jnp.float32))
    put(RESPONSE, response_ref[...])
    for c in range(comps):
        put(MOVING + c, velocity_ref[c])
        put(OFFSET + c, fraction_ref[c])
    spare = table_ref.shape[0] - nblocks * TABLE_ROWS
    row = row_ids(spare)
    table_ref[nblocks * TABLE_ROWS :] = jnp.where(row % TABLE_ROWS == RESPONSE, 1.0, 0.0)


def y_lines_kernel(grid_ref, face_ref, from_x_ref, edge_ref, ready_ref, out_ref):
    comps, size_x = grid_ref.shape[0], grid_ref.shape[1] - 2
    size_y = face_ref.shape[0]
    for c in range(comps):
        out_ref[c * size_x : (c + 1) * size_x] = grid_ref[c, 1 : size_x + 1, 0]
        out_ref[comps * size_x + c : comps * size_x + c + 1] = from_x_ref[c * size_y : c * size_y + 1]
    line = jnp.where(lane_ids(8) % PACK == size_x, turned(edge_ref[0:8], size_x), face_ref[0:8])
    out_ref[comps * size_x + comps : comps * size_x + comps + 1] = line[0:1]


def halo_xz_kernel(grid_in_ref, lines_in_ref, face_ref, from_x_ref, edge_ref, grid_ref, lines_ref, top_ref, turned_ref):
    comps, size_x = grid_ref.shape[0], grid_ref.shape[1] - 2
    size_y, size_z = face_ref.shape[0], grid_ref.shape[3]
    count_x, count_y = size_x // BX, size_y // BY
    for c in range(comps):
        grid_ref[c, size_x + 1, 0:size_y] = from_x_ref[c * size_y : (c + 1) * size_y]
    lay_out(grid_ref, lines_ref, count_x - 1, count_x, size_y, size_z, range(count_y - 1))
    top = jnp.where(lane_ids(size_y) % PACK == size_x, turned(edge_ref[...], size_x), face_ref[...])
    top_ref[0:size_y] = top
    top_ref[size_y:] = jnp.zeros((LANES - size_y, LANES), jnp.float32)
    turned_ref[...] = jnp.transpose(top_ref[...])
    for q in range(count_y - 1):
        lay_out_top(turned_ref, lines_ref, q, comps, count_x, count_y, size_z)


def halo_y_kernel(size_y, grid_in_ref, lines_in_ref, top_in_ref, first_ref, second_ref, grid_ref, lines_ref, turned_ref):
    comps, size_x, size_z = grid_ref.shape[0], grid_ref.shape[1] - 2, grid_ref.shape[3]
    count_x, count_y = size_x // BX, size_y // BY
    inside = lax.axis_index("gy") != lax.axis_size("gy") - 1
    kept = (row_ids(8) == 0) & inside

    def top_of(line):
        return jnp.where(kept, jnp.broadcast_to(line, (8, LANES)), 0.0)

    def rows_at(rows):
        return jnp.where(jnp.full((1, LANES), odd("gy")) == 0, first_ref[rows], second_ref[rows])

    @pl.loop(0, comps)
    def _(c):
        lines = rows_at(pl.ds(pl.multiple_of(c * size_x, 8), size_x))
        for x in range(size_x):
            grid_ref[c, x + 1, size_y:] = top_of(lines[x : x + 1])

    for c in range(comps):
        row = comps * size_x + c
        grid_ref[c, size_x + 1, size_y:] = top_of(rows_at(slice(row, row + 1)))
    lay_out(grid_ref, lines_ref, 0, count_x, size_y, size_z, [count_y - 1])
    row = comps * size_x + comps
    corner = top_of(rows_at(slice(row, row + 1)))
    rest = jnp.zeros((LANES - size_y - 8, LANES), jnp.float32)
    turned_ref[...] = jnp.transpose(jnp.concatenate([top_in_ref[0:size_y], corner, rest], axis=0))
    lay_out_top(turned_ref, lines_ref, count_y - 1, comps, count_x, count_y, size_z)


def blocks_kernel(
    late, comps, count_x, count_y, count_z, rows_z,
    list_ref, brick_ref, lines_ref, table_ref, *refs,
):
    state_ref, deposit_ref = refs[-2:]
    nblocks = brick_ref.shape[0]
    room = (list_ref.shape[0] - 2) // 2
    sub = row_ids(8)
    row_y = row_ids(REACH_Y).astype(jnp.float32)
    row_z = row_ids(REACH_Z).astype(jnp.float32)
    lane = lane_ids(REACH_Y)

    def hat(rows, inside, along):
        return jnp.where(rows == inside, 1.0 - along, 0.0) + jnp.where(rows == inside + 1.0, along, 0.0)

    def loaded(at):
        k = list_ref[at]
        brick = jnp.where(k < nblocks, brick_ref[jnp.minimum(k, nblocks - 1)], 0)
        brick_x = lax.div(brick, count_y * count_z)
        brick_y = lax.rem(lax.div(brick, count_z), count_y)
        brick_z = lax.rem(brick, count_z)
        sel = jnp.where(brick_z == count_z - 1, 1, 0)
        pair = brick_x * count_y + brick_y
        start = pl.multiple_of((sel * count_x * count_y + pair) * comps * SPREAD, 8)
        first = pl.multiple_of(pair * comps * rows_z + brick_z * BZ, 8)
        window = jnp.concatenate([lines_ref[pl.ds(first + c * rows_z, REACH_Z)] for c in range(comps)], axis=0)
        table = table_ref[pl.ds(pl.multiple_of(k * TABLE_ROWS, TABLE_ROWS), TABLE_ROWS)]
        rows = [table[i : i + 1] for i in range(TABLE_ROWS)]
        return k, start, brick_z * BZ, window, rows

    def weighted(rows):
        weight_y = hat(row_y, rows[IN_Y], rows[ALONG_Y])
        weight_z = hat(row_z, rows[IN_Z], rows[ALONG_Z])
        weight = jnp.concatenate([rows[WEIGHT + a] * weight_y for a in range(REACH_X)], axis=0)
        return weight_z, *parts_of(weight)

    def stepped(seen, weight_z, rows):
        rate = 1.0 / rows[RESPONSE]
        state, moved, pushed = [], [], []
        for c in range(comps):
            gas_sample = jnp.sum(seen[c * REACH_Z : (c + 1) * REACH_Z] * weight_z, axis=0, keepdims=True)
            drag = (gas_sample - rows[MOVING + c]) * rate
            state.append(rows[MOVING + c] + TIME_STEP * drag)
            moved.append(rows[OFFSET + c] + TIME_STEP * state[c])
            pushed.append(drag * weight_z)
        tile = jnp.broadcast_to(rows[RESPONSE], (STATE, LANES))
        for i, value in enumerate(state + moved):
            tile = jnp.where(sub == i, value, tile)
        gap = jnp.zeros((LANES // 2 - comps * REACH_Z, LANES), jnp.float32)
        main, rest = parts_of(jnp.concatenate(pushed, axis=0))
        return tile, jnp.concatenate([main, gap, rest, gap], axis=0)

    def pair_of(one, two):
        tables, windows, weights = [], [], []
        for _, _, _, window, rows in (one, two):
            weight_z, main, rest = weighted(rows)
            weights.append((weight_z, main, rest))
            unused = jnp.zeros((LANES - 3 * SPREAD, LANES), jnp.float32)
            tables.append(jnp.concatenate([main, main, rest, unused], axis=0).astype(jnp.bfloat16))
            windows.append(window)
        seen = lax.dot_general(
            jnp.concatenate(windows, axis=0).astype(jnp.bfloat16), jnp.concatenate(tables, axis=1),
            (((1,), (0,)), ((), ())), preferred_element_type=jnp.float32,
        )
        height = comps * REACH_Z
        tiles, pushes, spreads = [], [], []
        for i, (_, _, _, _, rows) in enumerate((one, two)):
            mine = seen[i * height : (i + 1) * height, i * LANES : (i + 1) * LANES]
            tile, push = stepped(mine, weights[i][0], rows)
            tiles.append(tile)
            pushes.append(push)
            spreads.extend(weights[i][1:])
        shares = lax.dot_general(
            jnp.concatenate(spreads, axis=0).astype(jnp.bfloat16), jnp.concatenate(pushes, axis=0).astype(jnp.bfloat16),
            (((1,), (1,)), ((), ())), preferred_element_type=jnp.float32,
        )
        results = []
        for i, tile in enumerate(tiles):
            mine = shares[2 * i * SPREAD : 2 * (i + 1) * SPREAD, i * LANES : (i + 1) * LANES]
            mine = mine[:SPREAD] + mine[SPREAD:]
            results.append((tile, mine + pltpu.roll(mine, LANES // 2, 1)))
        return results

    count = list_ref[2 * room + late]

    @pl.loop(0, (count + UNROLL - 1) // UNROLL)
    def _(group):
        at = late * room + group * UNROLL
        taken = [loaded(at + u) for u in range(UNROLL)]
        results = []
        for u in range(0, UNROLL, 2):
            results.extend(pair_of(taken[u], taken[u + 1]))
        parts = []
        for (_, _, first_z, _, _), (_, shares) in zip(taken, results):
            within = ((lane - first_z) & (LANES - 1)) < REACH_Z
            parts.append([])
            for c in range(comps):
                shift = (first_z - c * REACH_Z + LANES) & (LANES - 1)
                for a in range(REACH_X):
                    part = pltpu.roll(shares[a * REACH_Y : (a + 1) * REACH_Y], shift, 1)
                    parts[-1].append(jnp.where(within, part, 0.0))
        for (k, _, _, _, _), (tile, _) in zip(taken, results):
            state_ref[pl.ds(pl.multiple_of(STATE * k, STATE), STATE)] = tile
        for (_, start, _, _, _), mine in zip(taken, parts):
            spots = [pl.ds(start + i * REACH_Y, REACH_Y) for i in range(comps * REACH_X)]
            sums = [deposit_ref[spot] + part for spot, part in zip(spots, mine)]
            for spot, total in zip(spots, sums):
                deposit_ref[spot] = total


def merge_kernel(tiles_ref, plane_ref):
    _, comps, planes, _, _ = plane_ref.shape
    count_x, count_y = (planes - 1) // BX, tiles_ref.shape[0] // (2 * ((planes - 1) // BX) * comps * SPREAD)
    top = row_ids(REACH_Y) >= BY

    @pl.loop(0, 2 * comps)
    def _(i):
        sel, c = lax.div(i, comps), lax.rem(i, comps)
        base = (sel * count_x * count_y * comps + c) * SPREAD
        for x in range(planes):
            bricks = [(x // BX, x % BX)] if x < planes - 1 else []
            if x and x % BX == 0:
                bricks.append((x // BX - 1, BX))

            def tile(q):
                total = None
                for p, a in bricks:
                    at = pl.multiple_of(base + (p * count_y + q) * comps * SPREAD + a * REACH_Y, 8)
                    value = tiles_ref[pl.ds(at, REACH_Y)]
                    total = value if total is None else total + value
                return total

            carried = None
            for q in range(0, count_y, 2):
                here = tile(q)
                if carried is not None:
                    here = here + carried
                between = pltpu.roll(tile(q + 1), BY, 0)
                here = here + jnp.where(top, between, 0.0)
                carried = jnp.where(top, 0.0, between)
                plane_ref[sel, c, x, q * BY : q * BY + REACH_Y] = here
            plane_ref[sel, c, x, count_y * BY :] = carried


def leave_kernel(crossing_ref, state_ref, leaving_ref):
    slots = crossing_ref.shape[1]

    @pl.loop(0, 6)
    def _(face):
        tiles = []
        for slot in range(slots):
            block = crossing_ref[face, slot]
            spot = pl.ds(pl.multiple_of(jnp.maximum(block, 0) * STATE, STATE), STATE)
            live = jnp.full((STATE, LANES), block, jnp.int32) >= 0
            tiles.append(jnp.where(live, state_ref[spot], 0.0))
        leaving_ref[face] = jnp.concatenate(tiles, axis=0)


def send_kernel(push, diffuse, leaving_ref, grid_ref, deposit_ref, y_ref, x_ref, z_ref, face_ref):
    comps, size_x = grid_ref.shape[0], grid_ref.shape[1] - 2
    size_y = z_ref.shape[0]
    rows = leaving_ref.shape[1]
    first = jnp.full((rows, LANES), odd("gy")) == 0
    y_ref[0, 0:rows] = jnp.where(first, leaving_ref[2], leaving_ref[3])
    y_ref[1, 0:rows] = jnp.where(first, leaving_ref[3], leaving_ref[2])
    lane = lane_ids(ROWS_Y)
    sub = row_ids(ROWS_Y)
    face_ref[...] = jnp.zeros_like(face_ref)

    @pl.loop(0, comps)
    def _(c):
        face = jnp.zeros((ROWS_Y, LANES), jnp.float32)
        lines = jnp.zeros((ROWS_Y, LANES), jnp.float32)
        for x in range(size_x + 1):
            beyond = push * deposit_ref[1, c, x]
            top = push * deposit_ref[0, c, x, size_y:] + jnp.where(lane[:8] == 0, 0.0, beyond[size_y:])
            if x < size_x:
                here = grid_ref[c, x + 1, 0:size_y]
                beyond = jnp.concatenate([beyond[:size_y] + diffuse * turned(here, 1), beyond[size_y:]], axis=0)
                top = top[0:1] + diffuse * here[size_y - 1 :]
            else:
                here = grid_ref[c, size_x, 0:size_y]
                total = push * deposit_ref[0, c, x, 0:size_y] + jnp.where(lane[:size_y] == 0, 0.0, beyond[:size_y])
                x_ref[pl.ds(pl.multiple_of(c * size_y, 8), size_y)] = diffuse * here + total
                top = top[0:1]
            lines = jnp.where(sub == x, top, lines)
            face = jnp.where(lane == x, turned(beyond, x), face)
        y_ref[0, pl.ds(pl.multiple_of(rows + c * ROWS_Y, 8), ROWS_Y)] = lines
        face_ref[...] = face_ref[...] + pltpu.roll(face, PACK * c, 1)

    z_ref[...] = face_ref[0:size_y]
    y_ref[0, rows + size_x + 1 : rows + size_x + 2] = face_ref[size_y : size_y + 1]
    y_ref[1, rows:] = y_ref[0, rows:]


def base_kernel(push, diffuse, grid_ref, deposit_ref, top_ref, base_ref):
    comps, size_x, size_y, size_z = base_ref.shape
    lane = lane_ids(size_y)

    @pl.loop(0, comps)
    def _(c):
        top = pltpu.roll(top_ref[0:size_y], (LANES - PACK * c) % LANES, 1)
        for x in range(size_x):
            here = grid_ref[c, x + 1, 0:size_y]
            before = jnp.where(row_ids(size_y) == 0, 0.0, pltpu.roll(here, 1, 0))
            laplace = grid_ref[c, x, 0:size_y] + grid_ref[c, x + 2, 0:size_y]
            laplace = laplace + grid_ref[c, x + 1, 1 : size_y + 1] + before
            ahead = jnp.where(lane == size_z - 1, turned(top, size_z - 1 - x), turned(here, -1))
            laplace = laplace + ahead + jnp.where(lane == 0, 0.0, turned(here, 1)) - 6.0 * here
            total = deposit_ref[0, c, x, 0:size_y] + jnp.where(lane == 0, 0.0, deposit_ref[1, c, x, 0:size_y])
            base_ref[c, x] = here + diffuse * laplace + push * total


def below(first_ref, second_ref, rows):
    got = jnp.where(odd("gy") == 1, first_ref[rows], second_ref[rows])
    return jnp.where(lax.axis_index("gy") != 0, got, 0.0)


def relay_kernel(size_x, size_y, comps, count, first_ref, second_ref, x_in_ref, z_in_ref, leaving_ref, x_ref, z_ref, edge_ref):
    edge = comps * size_y
    x_ref[0:edge] = x_in_ref[...]
    for c in range(comps):
        at = count + c * ROWS_Y + size_x
        spot = slice(c * size_y, c * size_y + 1)
        x_ref[spot] = x_in_ref[spot] + below(first_ref, second_ref, slice(at, at + 1))
    x_ref[edge : edge + count] = leaving_ref[0]
    if x_ref.shape[0] > edge + count:
        x_ref[edge + count : edge + 2 * count] = leaving_ref[1]
    at = count + size_x + 1
    edge_ref[...] = z_in_ref[...]
    edge_ref[0:1] = z_in_ref[0:1] + below(first_ref, second_ref, slice(at, at + 1))
    up = odd("gz")
    z_ref[up, 0:count] = leaving_ref[4]
    z_ref[up, count : count + size_y] = edge_ref[...]
    z_ref[1 - up, 0:count] = leaving_ref[5]
    z_ref[1 - up, count : count + size_y] = jnp.zeros((size_y, LANES), jnp.float32)


def finish_kernel(
    count, base_ref, y1_ref, y2_ref, x_ref, minus_x_ref, z1_ref, z2_ref, edge_ref, state_ref,
    gas_ref, arrivals_ref, velocity_ref,
):
    comps, size_x, size_y, _ = base_ref.shape
    first_row, first_lane = row_ids(size_y) == 0, lane_ids(size_y) == 0
    rows = slice(count, count + size_y)
    odd_y, odd_z = jnp.full((1, LANES), odd("gy")) == 1, jnp.full((1, LANES), odd("gz")) == 1
    place = jnp.full((1, LANES), lax.axis_index("gy"))
    lower, upper = place != 0, place != lax.axis_size("gy") - 1
    face = jnp.where(odd_z, z1_ref[rows], z2_ref[rows])

    @pl.loop(0, comps)
    def _(c):
        spot = pl.ds(pl.multiple_of(count + c * ROWS_Y, 8), ROWS_Y)
        lines = jnp.where(lower, jnp.where(odd_y, y1_ref[spot], y2_ref[spot]), 0.0)
        mine = pltpu.roll(face, (LANES - PACK * c) % LANES, 1)
        for x in range(size_x):
            line = jnp.broadcast_to(lines[x : x + 1], (size_y, LANES))
            total = base_ref[c, x] + jnp.where(first_row, line, 0.0)
            far = turned(mine, -x)
            if x == 0:
                total = total + x_ref[pl.ds(pl.multiple_of(c * size_y, 8), size_y)]
                far = far + pltpu.roll(edge_ref[...], (2 * LANES - PACK * c - size_x) % LANES, 1)
            gas_ref[c, x] = total + jnp.where(first_lane, far, 0.0)

    slots = arrivals_ref.shape[2]
    for i in range(arrivals_ref.shape[1]):

        def rows_of(ref, at=0):
            return ref[pl.ds(at + i, slots, stride=STATE)]

        arrivals_ref[0, i] = rows_of(x_ref, comps * size_y)
        arrivals_ref[1, i] = rows_of(minus_x_ref, minus_x_ref.shape[0] - count)
        y1, y2 = rows_of(y1_ref), rows_of(y2_ref)
        arrivals_ref[2, i] = jnp.where(lower, jnp.where(odd_y, y1, y2), 0.0)
        arrivals_ref[3, i] = jnp.where(upper, jnp.where(odd_y, y2, y1), 0.0)
        z1, z2 = rows_of(z1_ref), rows_of(z2_ref)
        arrivals_ref[4, i] = jnp.where(odd_z, z1, z2)
        arrivals_ref[5, i] = jnp.where(odd_z, z2, z1)
    for c in range(comps):
        velocity_ref[c] = state_ref[pl.ds(c, velocity_ref.shape[1], stride=STATE)]


def per_device(gas_field, velocity, fraction, response, cell_index, brick_index, crossing):
    comps, size_x, size_y, size_z = gas_field.shape
    nblocks = velocity.shape[0]
    loading = 0.5 * size_x * size_y * size_z / (nblocks * 128)
    push, diffuse = -TIME_STEP * loading, TIME_STEP * VISCOSITY
    velocity = jnp.transpose(velocity, (1, 0, 2))
    fraction = jnp.transpose(fraction, (1, 0, 2))
    spare = nblocks + 8
    rows_z = size_z + 8
    grid_shape = (comps, size_x + 2, ROWS_Y, LANES)
    lines_shape = ((size_x // BX) * (size_y // BY) * comps * rows_z, LANES)
    deposit_shape = (2 * (size_x // BX) * (size_y // BY) * comps * SPREAD, LANES)

    inputs = (gas_field, velocity, fraction, response, cell_index, brick_index, crossing)
    inputs = [pltpu.with_memory_space_constraint(array, pltpu.HBM) for array in inputs]
    grid, face, plane, velocity, fraction, response, cell_index, brick_index, crossing = call(
        begin_kernel,
        [grid_shape, (size_y, LANES), (comps * size_y, LANES)]
        + [jax.ShapeDtypeStruct(array.shape, array.dtype) for array in inputs[1:]],
        *inputs, hbm=range(7), scratch=(pltpu.SemaphoreType.DMA((7,)),), limit=40,
    )
    from_z = moved_along(face, "gz", -1)
    from_x = moved_along(plane, "gx", -1)
    from_xz = moved_diagonally(face, -1)
    lines, deposit, table, ready, blocks = call(
        prepare_kernel,
        [
            lines_shape,
            deposit_shape,
            (TABLE_ROWS * spare, LANES),
            (8, LANES),
            jax.ShapeDtypeStruct((2 * (nblocks + UNROLL) + 2,), jnp.int32),
        ],
        grid, velocity, fraction, response, cell_index, brick_index,
        smem=(5,), smem_outs=(4,), cycles=3000,
    )
    line_rows = -(-(comps * size_x + comps + 1) // 8) * 8
    (y_lines,) = call(y_lines_kernel, [(line_rows, LANES)], grid, from_z, from_x, from_xz, ready)
    y1, y2 = swapped_y((y_lines, y_lines))
    square = pltpu.VMEM((LANES, LANES), jnp.float32)
    grid, lines, top = call(
        halo_xz_kernel, [grid_shape, lines_shape, (LANES, LANES)], grid, lines, from_z, from_x, from_xz,
        aliases={0: 0, 1: 1}, scratch=(square,), cycles=1000,
    )

    def advance(late, lines, deposit, *state):
        return call(
            functools.partial(blocks_kernel, late, comps, size_x // BX, size_y // BY, size_z // BZ, rows_z),
            [(STATE * spare, LANES), deposit_shape], blocks, brick_index, lines, table, deposit, *state,
            smem=(0, 1), aliases={4: 1, 5: 0} if state else {4: 1}, cycles=6000 - 4000 * late,
        )

    state, deposit = advance(0, lines, deposit)
    grid, lines = call(
        functools.partial(halo_y_kernel, size_y), [grid_shape, lines_shape], grid, lines, top, y1, y2,
        aliases={0: 0, 1: 1}, scratch=(square,), cycles=1000,
    )
    state, deposit = advance(1, lines, deposit, state)

    (deposit,) = call(merge_kernel, [(2, comps, size_x + 1, ROWS_Y, LANES)], deposit, cycles=500)
    count = STATE * crossing.shape[1]
    (leaving,) = call(leave_kernel, [(6, count, LANES)], crossing, state, smem=(0,), cycles=500)
    to_y, to_x, to_z = call(
        functools.partial(send_kernel, push, diffuse),
        [(2, count + comps * ROWS_Y, LANES), (comps * size_y, LANES), (size_y, LANES)],
        leaving, grid, deposit, cycles=500, scratch=(pltpu.VMEM((ROWS_Y, LANES), jnp.float32),),
    )
    y1, y2 = swapped_y((to_y[0], to_y[1]))
    (base,) = call(
        functools.partial(base_kernel, push, diffuse), [gas_field.shape], grid, deposit, top, cycles=1000,
    )
    edge = comps * size_y
    both = lax.axis_size("gx") == 2
    to_x, to_z, to_xz = call(
        functools.partial(relay_kernel, size_x, size_y, comps, count),
        [(edge + (2 if both else 1) * count, LANES), (2, count + size_y, LANES), (size_y, LANES)],
        y1, y2, to_x, to_z, leaving,
    )
    got_x = moved_along(to_x, "gx", 1)
    z1, z2 = swapped_z((to_z[0], to_z[1]))
    got_xz = moved_diagonally(to_xz, 1)
    got_mx = got_x if both else moved_along(leaving[1], "gx", -1)
    gas_next, arrivals, velocity_next = call(
        functools.partial(finish_kernel, count),
        [gas_field.shape, (6, 7, crossing.shape[1], LANES), (comps, nblocks, LANES)],
        base, y1, y2, got_x, got_mx, z1, z2, got_xz, state,
    )
    return gas_next, jnp.transpose(velocity_next, (1, 0, 2)), jnp.transpose(arrivals, (0, 2, 1, 3))


def solution(mesh):
    owner = ("gx", "gz", "gy")
    in_specs = (
        P(None, "gx", "gy", "gz"),
        P(owner, None, None),
        P(owner, None, None),
        P(owner, None),
        P(owner, None),
        P(owner),
        P(owner, None),
    )
    out_specs = (
        P(None, "gx", "gy", "gz"),
        P(owner, None, None),
        P(owner, None, None, None),
    )
    return jax.shard_map(
        per_device, mesh=mesh, in_specs=in_specs, out_specs=out_specs, check_vma=False
    )
```

```python
import functools

import jax
import jax.numpy as jnp
from jax import lax
from jax.experimental import pallas as pl
from jax.experimental.pallas import tpu as pltpu
from jax.sharding import PartitionSpec as P

BX = 4
BY = 4
BZ = 8

TIME_STEP = 0.25
VISCOSITY = 0.4

LANES = 128
PACK = 32
ROWS_Y = 24
REACH_X = BX + 1
REACH_Y = 8
SPREAD = REACH_X * REACH_Y
REACH_Z = 2 * BZ
UNROLL = 8

WEIGHT, ALONG_Y, IN_Y, ALONG_Z, IN_Z, RESPONSE, MOVING, OFFSET = 0, 5, 6, 7, 8, 9, 10, 13
TABLE_ROWS = 16
STATE = 8

VMEM = pl.BlockSpec(memory_space=pltpu.VMEM)
SMEM = pl.BlockSpec(memory_space=pltpu.SMEM)
HBM = pl.BlockSpec(memory_space=pltpu.HBM)


def moved_along(block, axis, distance):
    count = lax.axis_size(axis)
    return lax.ppermute(block, axis, [(i, (i + distance) % count) for i in range(count)])


def swapped_z(blocks):
    count = lax.axis_size("gz")
    first = [(i, i ^ 1) for i in range(count)]
    second = [(i, (((i + 1) ^ 1) - 1) % count) for i in range(count)]
    return lax.ppermute(blocks[0], "gz", first), lax.ppermute(blocks[1], "gz", second)


def swapped_y(blocks):
    nz, ny = lax.axis_size("gz"), lax.axis_size("gy")
    first = [(j, j ^ 1) for j in range(ny)]
    second = []
    for k in range(nz):
        second.append((k * ny, (k ^ 1) * ny))
        second.append((k * ny + ny - 1, (k ^ 1) * ny + ny - 1))
        second.extend((k * ny + j, k * ny + ((j + 1) ^ 1) - 1) for j in range(1, ny - 1))
    return lax.ppermute(blocks[0], "gy", first), lax.ppermute(blocks[1], ("gz", "gy"), second)


def moved_diagonally(block, distance):
    nx, nz = lax.axis_size("gx"), lax.axis_size("gz")
    route = [(i * nz + k, (i + distance) % nx * nz + (k + distance) % nz) for i in range(nx) for k in range(nz)]
    return lax.ppermute(block, ("gx", "gz"), route)


def call(body, outs, *operands, smem=(), hbm=(), smem_outs=(), scratch=(), aliases=None, cycles=0, limit=40):
    return pl.pallas_call(
        body,
        out_shape=[o if isinstance(o, jax.ShapeDtypeStruct) else jax.ShapeDtypeStruct(o, jnp.float32) for o in outs],
        in_specs=[SMEM if i in smem else HBM if i in hbm else VMEM for i in range(len(operands))],
        out_specs=[SMEM if i in smem_outs else VMEM for i in range(len(outs))],
        scratch_shapes=list(scratch),
        input_output_aliases=aliases or {},
        compiler_params=pltpu.CompilerParams(vmem_limit_bytes=limit * 1024 * 1024),
        cost_estimate=pl.CostEstimate(flops=cycles * 4096, bytes_accessed=cycles * 1024, transcendentals=0),
    )(*operands)


def lane_ids(rows):
    return lax.broadcasted_iota(jnp.int32, (rows, LANES), 1)


def row_ids(rows):
    return lax.broadcasted_iota(jnp.int32, (rows, LANES), 0)


def turned(value, shift):
    shift = shift % LANES
    return pltpu.roll(value, shift, 1) if shift else value


def odd(axis):
    return lax.axis_index(axis) % 2


def begin_kernel(
    gas_ref, velocity_in, fraction_in, response_in, cell_in, brick_in, crossing_in,
    grid_ref, face_ref, plane_ref, velocity_ref, fraction_ref, response_ref, cell_ref, brick_ref, crossing_ref, sems,
):
    comps, size_x, size_y, _ = gas_ref.shape
    pairs = [
        (gas_ref, grid_ref.at[:, 1 : size_x + 1, 0:size_y]),
        (velocity_in, velocity_ref), (fraction_in, fraction_ref), (response_in, response_ref),
        (cell_in, cell_ref), (brick_in, brick_ref), (crossing_in, crossing_ref),
    ]
    copies = [pltpu.make_async_copy(source, target, sems.at[i]) for i, (source, target) in enumerate(pairs)]
    for copy in copies:
        copy.start()
    zeros = jnp.zeros((ROWS_Y, LANES), jnp.float32)
    for c in range(comps):
        grid_ref[c, 0] = zeros
        grid_ref[c, size_x + 1] = zeros
        for x in range(size_x):
            grid_ref[c, x + 1, size_y:] = zeros[size_y:]
    copies[0].wait()
    lane = lane_ids(size_y)
    face = jnp.zeros((size_y, LANES), jnp.float32)
    for c in range(comps):
        plane_ref[c * size_y : (c + 1) * size_y] = grid_ref[c, 1, 0:size_y]
        for x in range(size_x):
            place = PACK * c + x
            face = jnp.where(lane == place, turned(grid_ref[c, x + 1, 0:size_y], place), face)
    face_ref[...] = face
    for copy in copies[1:]:
        copy.wait()


def parts_of(value):
    main = value.astype(jnp.bfloat16).astype(jnp.float32)
    return main, value - main


def lay_out(grid_ref, lines_ref, p, q, size_y, size_z):
    comps = grid_ref.shape[0]
    rows_z = size_z + 8
    count_y = size_y // BY
    for c in range(comps):
        planes = [grid_ref[c, p * BX + a + 1, q * BY : q * BY + REACH_Y] for a in range(REACH_X)]
        main, rest = parts_of(jnp.concatenate(planes, axis=0))
        stack = jnp.concatenate([main, rest, main, jnp.zeros((LANES - 3 * SPREAD, LANES), jnp.float32)], axis=0)
        at = ((p * count_y + q) * comps + c) * rows_z
        lines_ref[at : at + size_z] = jnp.transpose(stack)


def lay_out_top(turned_ref, lines_ref, q, comps, count_x, count_y, size_z):
    lane = lane_ids(count_x)
    rows_z = size_z + 8
    for c in range(comps):
        total = jnp.zeros((count_x, LANES), jnp.float32)
        for a in range(REACH_X):
            rows = turned_ref[pl.ds(PACK * c + a, count_x, stride=BX)]
            total = jnp.where(lane // REACH_Y == a, turned(rows, a * REACH_Y - q * BY), total)
        main, rest = parts_of(total)
        line = main + turned(rest, SPREAD) + turned(main, 2 * SPREAD)
        for p in range(count_x):
            at = ((p * count_y + q) * comps + c) * rows_z + size_z
            lines_ref[at : at + 1] = line[p : p + 1]


def prepare_kernel(
    grid_ref, velocity_ref, fraction_ref, response_ref, cell_ref, brick_ref,
    lines_ref, deposit_ref, table_ref, ready_ref, list_ref,
):
    comps, size_x, size_y, size_z = grid_ref.shape[0], grid_ref.shape[1] - 2, grid_ref.shape[2] - 8, grid_ref.shape[3]
    nblocks = velocity_ref.shape[1]
    count_x, count_y, count_z = size_x // BX, size_y // BY, size_z // BZ
    rows_z = size_z + 8

    room = nblocks + UNROLL

    def visit(k, counts):
        late = jnp.where(lax.rem(lax.div(brick_ref[k], count_z), count_y) == count_y - 1, 1, 0)
        list_ref[jnp.where(late == 1, room + counts[1], counts[0])] = k
        return counts[0] + 1 - late, counts[1] + late

    early, late = lax.fori_loop(0, nblocks, visit, (jnp.int32(0), jnp.int32(0)), unroll=8)
    for base, count in ((0, early), (room, late)):
        for u in range(UNROLL):
            list_ref[base + count + u] = nblocks
    list_ref[2 * room] = early
    list_ref[2 * room + 1] = late
    ready_ref[...] = jnp.zeros_like(ready_ref)

    deposit_ref[...] = jnp.zeros_like(deposit_ref)
    for p in range(count_x):
        for q in range(count_y):
            for c in range(comps):
                at = ((p * count_y + q) * comps + c) * rows_z + size_z
                lines_ref[at : at + 8] = jnp.zeros((8, LANES), jnp.float32)
    for p in range(count_x - 1):
        for q in range(count_y - 1):
            lay_out(grid_ref, lines_ref, p, q, size_y, size_z)

    cells = cell_ref[...]
    cell_x, cell_y, cell_z = cells // (BY * BZ), cells // BZ % BY, cells % BZ
    along_x = fraction_ref[0]

    def put(row, value):
        table_ref[pl.ds(row, nblocks, stride=TABLE_ROWS)] = value

    for a in range(REACH_X):
        put(WEIGHT + a, jnp.where(cell_x == a, 1.0 - along_x, 0.0) + jnp.where(cell_x == a - 1, along_x, 0.0))
    put(ALONG_Y, fraction_ref[1])
    put(IN_Y, cell_y.astype(jnp.float32))
    put(ALONG_Z, fraction_ref[2])
    put(IN_Z, cell_z.astype(jnp.float32))
    put(RESPONSE, response_ref[...])
    for c in range(comps):
        put(MOVING + c, velocity_ref[c])
        put(OFFSET + c, fraction_ref[c])
    spare = table_ref.shape[0] - nblocks * TABLE_ROWS
    row = row_ids(spare)
    table_ref[nblocks * TABLE_ROWS :] = jnp.where(row % TABLE_ROWS == RESPONSE, 1.0, 0.0)


def y_lines_kernel(grid_ref, face_ref, from_x_ref, edge_ref, ready_ref, out_ref):
    comps, size_x = grid_ref.shape[0], grid_ref.shape[1] - 2
    size_y = face_ref.shape[0]
    for c in range(comps):
        out_ref[c * size_x : (c + 1) * size_x] = grid_ref[c, 1 : size_x + 1, 0]
        out_ref[comps * size_x + c : comps * size_x + c + 1] = from_x_ref[c * size_y : c * size_y + 1]
    line = jnp.where(lane_ids(8) % PACK == size_x, turned(edge_ref[0:8], size_x), face_ref[0:8])
    out_ref[comps * size_x + comps : comps * size_x + comps + 1] = line[0:1]


def halo_xz_kernel(grid_in_ref, lines_in_ref, face_ref, from_x_ref, edge_ref, grid_ref, lines_ref, top_ref, turned_ref):
    comps, size_x = grid_ref.shape[0], grid_ref.shape[1] - 2
    size_y, size_z = face_ref.shape[0], grid_ref.shape[3]
    count_x, count_y = size_x // BX, size_y // BY
    for c in range(comps):
        grid_ref[c, size_x + 1, 0:size_y] = from_x_ref[c * size_y : (c + 1) * size_y]
    for q in range(count_y - 1):
        lay_out(grid_ref, lines_ref, count_x - 1, q, size_y, size_z)
    top = jnp.where(lane_ids(size_y) % PACK == size_x, turned(edge_ref[...], size_x), face_ref[...])
    top_ref[0:size_y] = top
    top_ref[size_y:] = jnp.zeros((LANES - size_y, LANES), jnp.float32)
    turned_ref[...] = jnp.transpose(top_ref[...])
    for q in range(count_y - 1):
        lay_out_top(turned_ref, lines_ref, q, comps, count_x, count_y, size_z)


def halo_y_kernel(size_y, grid_in_ref, lines_in_ref, top_in_ref, from_y_ref, grid_ref, lines_ref, turned_ref):
    comps, size_x, size_z = grid_ref.shape[0], grid_ref.shape[1] - 2, grid_ref.shape[3]
    count_x, count_y = size_x // BX, size_y // BY
    inside = lax.axis_index("gy") != lax.axis_size("gy") - 1
    kept = (row_ids(8) == 0) & inside

    def line_at(row):
        return jnp.where(kept, jnp.broadcast_to(from_y_ref[row : row + 1], (8, LANES)), 0.0)

    for c in range(comps):
        for x in range(size_x + 1):
            grid_ref[c, x + 1, size_y:] = line_at(c * size_x + x if x < size_x else comps * size_x + c)
    for p in range(count_x):
        lay_out(grid_ref, lines_ref, p, count_y - 1, size_y, size_z)
    corner = line_at(comps * size_x + comps)
    rest = jnp.zeros((LANES - size_y - 8, LANES), jnp.float32)
    turned_ref[...] = jnp.transpose(jnp.concatenate([top_in_ref[0:size_y], corner, rest], axis=0))
    lay_out_top(turned_ref, lines_ref, count_y - 1, comps, count_x, count_y, size_z)


def blocks_kernel(
    late, comps, count_x, count_y, count_z, rows_z,
    list_ref, brick_ref, lines_ref, table_ref, *refs,
):
    state_ref, deposit_ref, push_ref, spread_ref = refs[-4:]
    nblocks = brick_ref.shape[0]
    room = (list_ref.shape[0] - 2) // 2
    sub = row_ids(8)
    row_y = row_ids(REACH_Y).astype(jnp.float32)
    row_z = row_ids(REACH_Z).astype(jnp.float32)
    lane = lane_ids(REACH_Y)

    def hat(rows, inside, along):
        return jnp.where(rows == inside, 1.0 - along, 0.0) + jnp.where(rows == inside + 1.0, along, 0.0)

    def place_of(at):
        k = list_ref[at]
        brick = jnp.where(k < nblocks, brick_ref[jnp.minimum(k, nblocks - 1)], 0)
        brick_x = lax.div(brick, count_y * count_z)
        brick_y = lax.rem(lax.div(brick, count_z), count_y)
        return k, brick_x * count_y + brick_y, lax.rem(brick, count_z)

    def loaded(at):
        k, pair, brick_z = place_of(at)
        first = pl.multiple_of(pair * comps * rows_z + brick_z * BZ, 8)
        window = jnp.concatenate([lines_ref[pl.ds(first + c * rows_z, REACH_Z)] for c in range(comps)], axis=0)
        table = table_ref[pl.ds(pl.multiple_of(k * TABLE_ROWS, TABLE_ROWS), TABLE_ROWS)]
        return k, window, [table[i : i + 1] for i in range(TABLE_ROWS)]

    def weighted(rows):
        weight_y = hat(row_y, rows[IN_Y], rows[ALONG_Y])
        weight_z = hat(row_z, rows[IN_Z], rows[ALONG_Z])
        weight = jnp.concatenate([rows[WEIGHT + a] * weight_y for a in range(REACH_X)], axis=0)
        return weight_z, *parts_of(weight)

    def stepped(seen, weight_z, rows):
        rate = 1.0 / rows[RESPONSE]
        state, moved, pushed = [], [], []
        for c in range(comps):
            gas_sample = jnp.sum(seen[c * REACH_Z : (c + 1) * REACH_Z] * weight_z, axis=0, keepdims=True)
            drag = (gas_sample - rows[MOVING + c]) * rate
            state.append(rows[MOVING + c] + TIME_STEP * drag)
            moved.append(rows[OFFSET + c] + TIME_STEP * state[c])
            pushed.append(drag * weight_z)
        tile = jnp.broadcast_to(rows[RESPONSE], (STATE, LANES))
        for i, value in enumerate(state + moved):
            tile = jnp.where(sub == i, value, tile)
        gap = jnp.zeros((LANES // 2 - comps * REACH_Z, LANES), jnp.float32)
        main, rest = parts_of(jnp.concatenate(pushed, axis=0))
        return tile, jnp.concatenate([main, gap, rest, gap], axis=0)

    def gathered(one, two):
        tables, windows, weights = [], [], []
        for _, window, rows in (one, two):
            weight_z, main, rest = weighted(rows)
            weights.append((weight_z, main, rest))
            unused = jnp.zeros((LANES - 3 * SPREAD, LANES), jnp.float32)
            tables.append(jnp.concatenate([main, main, rest, unused], axis=0).astype(jnp.bfloat16))
            windows.append(window)
        seen = lax.dot_general(
            jnp.concatenate(windows, axis=0).astype(jnp.bfloat16), jnp.concatenate(tables, axis=1),
            (((1,), (0,)), ((), ())), preferred_element_type=jnp.float32,
        )
        height = comps * REACH_Z
        tiles, pushes, spreads = [], [], []
        for i, (_, _, rows) in enumerate((one, two)):
            mine = seen[i * height : (i + 1) * height, i * LANES : (i + 1) * LANES]
            tile, push = stepped(mine, weights[i][0], rows)
            tiles.append(tile)
            pushes.append(push)
            spreads.extend(weights[i][1:])
        return tiles, jnp.concatenate(pushes, axis=0).astype(jnp.bfloat16), jnp.concatenate(spreads, axis=0).astype(jnp.bfloat16)

    def shared(push, spread):
        shares = lax.dot_general(spread, push, (((1,), (1,)), ((), ())), preferred_element_type=jnp.float32)
        results = []
        for i in (0, 1):
            mine = shares[2 * i * SPREAD : 2 * (i + 1) * SPREAD, i * LANES : (i + 1) * LANES]
            mine = mine[:SPREAD] + mine[SPREAD:]
            results.append(mine + pltpu.roll(mine, LANES // 2, 1))
        return results

    count = list_ref[2 * room + late]
    groups = (count + UNROLL - 1) // UNROLL
    push_ref[...] = jnp.zeros_like(push_ref)
    spread_ref[...] = jnp.zeros_like(spread_ref)

    @pl.loop(0, groups + 1)
    def _(group):
        now = late * room + jnp.maximum(jnp.minimum(group, groups - 1), 0) * UNROLL
        before = late * room + jnp.maximum(group - 1, 0) * UNROLL
        taken = [loaded(now + u) for u in range(UNROLL)]
        old = [(push_ref[i], spread_ref[i]) for i in range(UNROLL // 2)]
        shares = []
        for push, spread in old:
            shares.extend(shared(push, spread))
        tiles, fresh = [], []
        for u in range(0, UNROLL, 2):
            both, push, spread = gathered(taken[u], taken[u + 1])
            tiles.extend(both)
            fresh.append((push, spread))
        sums = []
        for u in range(UNROLL):
            _, pair, brick_z = place_of(before + u)
            first_z = brick_z * BZ
            within = ((lane - first_z) & (LANES - 1)) < REACH_Z
            parts = []
            for c in range(comps):
                shift = (first_z - c * REACH_Z + LANES) & (LANES - 1)
                for a in range(REACH_X):
                    part = pltpu.roll(shares[u][a * REACH_Y : (a + 1) * REACH_Y], shift, 1)
                    parts.append(jnp.where(within, part, 0.0))
            sel = jnp.where(brick_z == count_z - 1, 1, 0)
            start = pl.multiple_of((sel * count_x * count_y + pair) * comps * SPREAD, 8)
            sums.append((start, parts))
        for start, parts in sums:
            spots = [pl.ds(start + i * REACH_Y, REACH_Y) for i in range(comps * REACH_X)]
            totals = [deposit_ref[spot] + part for spot, part in zip(spots, parts)]
            for spot, total in zip(spots, totals):
                deposit_ref[spot] = total
        for (k, _, _), tile in zip(taken, tiles):
            state_ref[pl.ds(pl.multiple_of(STATE * k, STATE), STATE)] = tile
        for i, (push, spread) in enumerate(fresh):
            push_ref[i] = push
            spread_ref[i] = spread


def merge_kernel(tiles_ref, plane_ref):
    _, comps, planes, _, _ = plane_ref.shape
    count_x, count_y = (planes - 1) // BX, tiles_ref.shape[0] // (2 * ((planes - 1) // BX) * comps * SPREAD)
    top = row_ids(REACH_Y) >= BY

    for sel in (0, 1):
        for c in range(comps):
            for x in range(planes):
                bricks = [(x // BX, x % BX)] if x < planes - 1 else []
                if x and x % BX == 0:
                    bricks.append((x // BX - 1, BX))

                def tile(q):
                    total = None
                    for p, a in bricks:
                        at = (((sel * count_x + p) * count_y + q) * comps + c) * SPREAD + a * REACH_Y
                        value = tiles_ref[at : at + REACH_Y]
                        total = value if total is None else total + value
                    return total

                carried = None
                for q in range(0, count_y, 2):
                    here = tile(q)
                    if carried is not None:
                        here = here + carried
                    between = pltpu.roll(tile(q + 1), BY, 0)
                    here = here + jnp.where(top, between, 0.0)
                    carried = jnp.where(top, 0.0, between)
                    plane_ref[sel, c, x, q * BY : q * BY + REACH_Y] = here
                plane_ref[sel, c, x, count_y * BY :] = carried


def leave_kernel(crossing_ref, state_ref, leaving_ref):
    slots = crossing_ref.shape[1]

    for face in range(6):
        tiles = []
        for slot in range(slots):
            block = crossing_ref[face, slot]
            spot = pl.ds(pl.multiple_of(jnp.maximum(block, 0) * STATE, STATE), STATE)
            live = jnp.full((STATE, LANES), block, jnp.int32) >= 0
            tiles.append(jnp.where(live, state_ref[spot], 0.0))
        leaving_ref[face] = jnp.concatenate(tiles, axis=0)


def send_kernel(push, diffuse, leaving_ref, grid_ref, deposit_ref, y_ref, x_ref, z_ref, face_ref):
    comps, size_x = grid_ref.shape[0], grid_ref.shape[1] - 2
    size_y = z_ref.shape[0]
    rows = leaving_ref.shape[1]
    first = jnp.full((rows, LANES), odd("gy")) == 0
    y_ref[0, 0:rows] = jnp.where(first, leaving_ref[2], leaving_ref[3])
    y_ref[1, 0:rows] = jnp.where(first, leaving_ref[3], leaving_ref[2])
    lane = lane_ids(ROWS_Y)
    sub = row_ids(ROWS_Y)
    face_ref[...] = jnp.zeros_like(face_ref)

    @pl.loop(0, comps)
    def _(c):
        face = jnp.zeros((ROWS_Y, LANES), jnp.float32)
        lines = jnp.zeros((ROWS_Y, LANES), jnp.float32)
        for x in range(size_x + 1):
            beyond = push * deposit_ref[1, c, x]
            top = push * deposit_ref[0, c, x, size_y:] + jnp.where(lane[:8] == 0, 0.0, beyond[size_y:])
            if x < size_x:
                here = grid_ref[c, x + 1, 0:size_y]
                beyond = jnp.concatenate([beyond[:size_y] + diffuse * turned(here, 1), beyond[size_y:]], axis=0)
                top = top[0:1] + diffuse * here[size_y - 1 :]
            else:
                here = grid_ref[c, size_x, 0:size_y]
                total = push * deposit_ref[0, c, x, 0:size_y] + jnp.where(lane[:size_y] == 0, 0.0, beyond[:size_y])
                x_ref[pl.ds(pl.multiple_of(c * size_y, 8), size_y)] = diffuse * here + total
                top = top[0:1]
            lines = jnp.where(sub == x, top, lines)
            face = jnp.where(lane == x, turned(beyond, x), face)
        y_ref[0, pl.ds(pl.multiple_of(rows + c * ROWS_Y, 8), ROWS_Y)] = lines
        face_ref[...] = face_ref[...] + pltpu.roll(face, PACK * c, 1)

    z_ref[...] = face_ref[0:size_y]
    y_ref[0, rows + size_x + 1 : rows + size_x + 2] = face_ref[size_y : size_y + 1]
    y_ref[1, rows:] = y_ref[0, rows:]


def base_kernel(push, diffuse, grid_ref, deposit_ref, top_ref, base_ref):
    comps, size_x, size_y, size_z = base_ref.shape
    lane = lane_ids(size_y)
    top = top_ref[0:size_y]
    for c in range(comps):
        for x in range(size_x):
            here = grid_ref[c, x + 1, 0:size_y]
            laplace = grid_ref[c, x + 2, 0:size_y]
            if x:
                laplace = laplace + grid_ref[c, x, 0:size_y]
            before = jnp.where(row_ids(size_y) == 0, 0.0, pltpu.roll(here, 1, 0))
            laplace = laplace + grid_ref[c, x + 1, 1 : size_y + 1] + before
            ahead = jnp.where(lane == size_z - 1, turned(top, size_z - 1 - (PACK * c + x)), turned(here, -1))
            laplace = laplace + ahead + jnp.where(lane == 0, 0.0, turned(here, 1)) - 6.0 * here
            total = deposit_ref[0, c, x, 0:size_y] + jnp.where(lane == 0, 0.0, deposit_ref[1, c, x, 0:size_y])
            base_ref[c, x] = here + diffuse * laplace + push * total


def below(first_ref, second_ref, rows):
    got = jnp.where(odd("gy") == 1, first_ref[rows], second_ref[rows])
    return jnp.where(lax.axis_index("gy") != 0, got, 0.0)


def relay_kernel(size_x, size_y, comps, count, first_ref, second_ref, x_in_ref, z_in_ref, leaving_ref, x_ref, z_ref, edge_ref):
    edge = comps * size_y
    x_ref[0:edge] = x_in_ref[...]
    for c in range(comps):
        at = count + c * ROWS_Y + size_x
        spot = slice(c * size_y, c * size_y + 1)
        x_ref[spot] = x_in_ref[spot] + below(first_ref, second_ref, slice(at, at + 1))
    x_ref[edge : edge + count] = leaving_ref[0]
    if x_ref.shape[0] > edge + count:
        x_ref[edge + count : edge + 2 * count] = leaving_ref[1]
    at = count + size_x + 1
    edge_ref[...] = z_in_ref[...]
    edge_ref[0:1] = z_in_ref[0:1] + below(first_ref, second_ref, slice(at, at + 1))
    up = odd("gz")
    z_ref[up, 0:count] = leaving_ref[4]
    z_ref[up, count : count + size_y] = edge_ref[...]
    z_ref[1 - up, 0:count] = leaving_ref[5]
    z_ref[1 - up, count : count + size_y] = jnp.zeros((size_y, LANES), jnp.float32)


def finish_kernel(
    count, base_ref, y1_ref, y2_ref, x_ref, minus_x_ref, z1_ref, z2_ref, edge_ref, state_ref,
    gas_ref, arrivals_ref, velocity_ref,
):
    comps, size_x, size_y, _ = base_ref.shape
    first_row, first_lane = row_ids(size_y) == 0, lane_ids(size_y) == 0
    rows = slice(count, count + size_y)
    from_first = odd("gz") == 1
    face = jnp.where(from_first, z1_ref[rows], z2_ref[rows])
    corner = edge_ref[...]
    for c in range(comps):
        for x in range(size_x):
            at = count + c * ROWS_Y + x
            line = jnp.broadcast_to(below(y1_ref, y2_ref, slice(at, at + 1)), (size_y, LANES))
            total = base_ref[c, x] + jnp.where(first_row, line, 0.0)
            far = turned(face, -(PACK * c + x))
            if x == 0:
                total = total + x_ref[c * size_y : (c + 1) * size_y]
                far = far + turned(corner, -(PACK * c + size_x))
            gas_ref[c, x] = total + jnp.where(first_lane, far, 0.0)

    slots = arrivals_ref.shape[2]
    lower, upper = lax.axis_index("gy") != 0, lax.axis_index("gy") != lax.axis_size("gy") - 1
    odd_y = odd("gy") == 1
    for i in range(arrivals_ref.shape[1]):

        def rows_of(ref, at=0):
            return ref[pl.ds(at + i, slots, stride=STATE)]

        arrivals_ref[0, i] = rows_of(x_ref, comps * size_y)
        arrivals_ref[1, i] = rows_of(minus_x_ref, minus_x_ref.shape[0] - count)
        y1, y2 = rows_of(y1_ref), rows_of(y2_ref)
        arrivals_ref[2, i] = jnp.where(lower, jnp.where(odd_y, y1, y2), 0.0)
        arrivals_ref[3, i] = jnp.where(upper, jnp.where(odd_y, y2, y1), 0.0)
        z1, z2 = rows_of(z1_ref), rows_of(z2_ref)
        arrivals_ref[4, i] = jnp.where(from_first, z1, z2)
        arrivals_ref[5, i] = jnp.where(from_first, z2, z1)
    for c in range(comps):
        velocity_ref[c] = state_ref[pl.ds(c, velocity_ref.shape[1], stride=STATE)]


def per_device(gas_field, velocity, fraction, response, cell_index, brick_index, crossing):
    comps, size_x, size_y, size_z = gas_field.shape
    nblocks = velocity.shape[0]
    loading = 0.5 * size_x * size_y * size_z / (nblocks * 128)
    push, diffuse = -TIME_STEP * loading, TIME_STEP * VISCOSITY
    velocity = jnp.transpose(velocity, (1, 0, 2))
    fraction = jnp.transpose(fraction, (1, 0, 2))
    spare = nblocks + 8
    rows_z = size_z + 8
    grid_shape = (comps, size_x + 2, ROWS_Y, LANES)
    lines_shape = ((size_x // BX) * (size_y // BY) * comps * rows_z, LANES)
    deposit_shape = (2 * (size_x // BX) * (size_y // BY) * comps * SPREAD, LANES)

    inputs = (gas_field, velocity, fraction, response, cell_index, brick_index, crossing)
    inputs = [pltpu.with_memory_space_constraint(array, pltpu.HBM) for array in inputs]
    grid, face, plane, velocity, fraction, response, cell_index, brick_index, crossing = call(
        begin_kernel,
        [grid_shape, (size_y, LANES), (comps * size_y, LANES)]
        + [jax.ShapeDtypeStruct(array.shape, array.dtype) for array in inputs[1:]],
        *inputs, hbm=range(7), scratch=(pltpu.SemaphoreType.DMA((7,)),), limit=40,
    )
    from_z = moved_along(face, "gz", -1)
    from_x = moved_along(plane, "gx", -1)
    from_xz = moved_diagonally(face, -1)
    lines, deposit, table, ready, blocks = call(
        prepare_kernel,
        [
            lines_shape,
            deposit_shape,
            (TABLE_ROWS * spare, LANES),
            (8, LANES),
            jax.ShapeDtypeStruct((2 * (nblocks + UNROLL) + 2,), jnp.int32),
        ],
        grid, velocity, fraction, response, cell_index, brick_index,
        smem=(5,), smem_outs=(4,), cycles=3000,
    )
    line_rows = -(-(comps * size_x + comps + 1) // 8) * 8
    (y_lines,) = call(y_lines_kernel, [(line_rows, LANES)], grid, from_z, from_x, from_xz, ready)
    from_y = moved_along(y_lines, "gy", -1)
    square = pltpu.VMEM((LANES, LANES), jnp.float32)
    grid, lines, top = call(
        halo_xz_kernel, [grid_shape, lines_shape, (LANES, LANES)], grid, lines, from_z, from_x, from_xz,
        aliases={0: 0, 1: 1}, scratch=(square,), cycles=1000,
    )

    def advance(late, lines, deposit, *state):
        return call(
            functools.partial(blocks_kernel, late, comps, size_x // BX, size_y // BY, size_z // BZ, rows_z),
            [(STATE * spare, LANES), deposit_shape], blocks, brick_index, lines, table, deposit, *state,
            smem=(0, 1), aliases={4: 1, 5: 0} if state else {4: 1}, cycles=6000 - 4000 * late,
            scratch=(
                pltpu.VMEM((UNROLL // 2, 2 * LANES, LANES), jnp.bfloat16),
                pltpu.VMEM((UNROLL // 2, 4 * SPREAD, LANES), jnp.bfloat16),
            ),
        )

    state, deposit = advance(0, lines, deposit)
    grid, lines = call(
        functools.partial(halo_y_kernel, size_y), [grid_shape, lines_shape], grid, lines, top, from_y,
        aliases={0: 0, 1: 1}, scratch=(square,), cycles=1000,
    )
    state, deposit = advance(1, lines, deposit, state)

    (deposit,) = call(merge_kernel, [(2, comps, size_x + 1, ROWS_Y, LANES)], deposit, cycles=500)
    count = STATE * crossing.shape[1]
    (leaving,) = call(leave_kernel, [(6, count, LANES)], crossing, state, smem=(0,), cycles=500)
    to_y, to_x, to_z = call(
        functools.partial(send_kernel, push, diffuse),
        [(2, count + comps * ROWS_Y, LANES), (comps * size_y, LANES), (size_y, LANES)],
        leaving, grid, deposit, cycles=500, scratch=(pltpu.VMEM((ROWS_Y, LANES), jnp.float32),),
    )
    y1, y2 = swapped_y((to_y[0], to_y[1]))
    (base,) = call(
        functools.partial(base_kernel, push, diffuse), [gas_field.shape], grid, deposit, top, cycles=1000,
    )
    edge = comps * size_y
    both = lax.axis_size("gx") == 2
    to_x, to_z, to_xz = call(
        functools.partial(relay_kernel, size_x, size_y, comps, count),
        [(edge + (2 if both else 1) * count, LANES), (2, count + size_y, LANES), (size_y, LANES)],
        y1, y2, to_x, to_z, leaving,
    )
    got_x = moved_along(to_x, "gx", 1)
    z1, z2 = swapped_z((to_z[0], to_z[1]))
    got_xz = moved_diagonally(to_xz, 1)
    got_mx = got_x if both else moved_along(leaving[1], "gx", -1)
    gas_next, arrivals, velocity_next = call(
        functools.partial(finish_kernel, count),
        [gas_field.shape, (6, 7, crossing.shape[1], LANES), (comps, nblocks, LANES)],
        base, y1, y2, got_x, got_mx, z1, z2, got_xz, state,
    )
    return gas_next, jnp.transpose(velocity_next, (1, 0, 2)), jnp.transpose(arrivals, (0, 2, 1, 3))


def solution(mesh):
    owner = ("gx", "gz", "gy")
    in_specs = (
        P(None, "gx", "gy", "gz"),
        P(owner, None, None),
        P(owner, None, None),
        P(owner, None),
        P(owner, None),
        P(owner),
        P(owner, None),
    )
    out_specs = (
        P(None, "gx", "gy", "gz"),
        P(owner, None, None),
        P(owner, None, None, None),
    )
    return jax.shard_map(
        per_device, mesh=mesh, in_specs=in_specs, out_specs=out_specs, check_vma=False
    )
```

```python
import functools

import jax
import jax.numpy as jnp
from jax import lax
from jax.experimental import pallas as pl
from jax.experimental.pallas import tpu as pltpu
from jax.sharding import PartitionSpec as P

BX = 4
BY = 4
BZ = 8

TIME_STEP = 0.25
VISCOSITY = 0.4

LANES = 128
PACK = 32
ROWS_Y = 24
REACH_X = BX + 1
REACH_Y = 8
SPREAD = REACH_X * REACH_Y
REACH_Z = 2 * BZ
UNROLL = 8

WEIGHT, ALONG_Y, IN_Y, ALONG_Z, IN_Z, RESPONSE, MOVING, OFFSET = 0, 5, 6, 7, 8, 9, 10, 13
TABLE_ROWS = 16
STATE = 8

VMEM = pl.BlockSpec(memory_space=pltpu.VMEM)
SMEM = pl.BlockSpec(memory_space=pltpu.SMEM)
HBM = pl.BlockSpec(memory_space=pltpu.HBM)


def moved_along(block, axis, distance):
    count = lax.axis_size(axis)
    return lax.ppermute(block, axis, [(i, (i + distance) % count) for i in range(count)])


def swapped_z(blocks):
    count = lax.axis_size("gz")
    first = [(i, i ^ 1) for i in range(count)]
    second = [(i, (((i + 1) ^ 1) - 1) % count) for i in range(count)]
    return lax.ppermute(blocks[0], "gz", first), lax.ppermute(blocks[1], "gz", second)


def swapped_y(blocks):
    nz, ny = lax.axis_size("gz"), lax.axis_size("gy")
    first = [(j, j ^ 1) for j in range(ny)]
    second = []
    for k in range(nz):
        second.append((k * ny, (k ^ 1) * ny))
        second.append((k * ny + ny - 1, (k ^ 1) * ny + ny - 1))
        second.extend((k * ny + j, k * ny + ((j + 1) ^ 1) - 1) for j in range(1, ny - 1))
    return lax.ppermute(blocks[0], "gy", first), lax.ppermute(blocks[1], ("gz", "gy"), second)


def moved_diagonally(block, distance):
    nx, nz = lax.axis_size("gx"), lax.axis_size("gz")
    route = [(i * nz + k, (i + distance) % nx * nz + (k + distance) % nz) for i in range(nx) for k in range(nz)]
    return lax.ppermute(block, ("gx", "gz"), route)


def call(body, outs, *operands, smem=(), hbm=(), smem_outs=(), scratch=(), aliases=None, cycles=0, limit=40):
    return pl.pallas_call(
        body,
        out_shape=[o if isinstance(o, jax.ShapeDtypeStruct) else jax.ShapeDtypeStruct(o, jnp.float32) for o in outs],
        in_specs=[SMEM if i in smem else HBM if i in hbm else VMEM for i in range(len(operands))],
        out_specs=[SMEM if i in smem_outs else VMEM for i in range(len(outs))],
        scratch_shapes=list(scratch),
        input_output_aliases=aliases or {},
        compiler_params=pltpu.CompilerParams(vmem_limit_bytes=limit * 1024 * 1024),
        cost_estimate=pl.CostEstimate(flops=cycles * 4096, bytes_accessed=cycles * 1024, transcendentals=0),
    )(*operands)


def lane_ids(rows):
    return lax.broadcasted_iota(jnp.int32, (rows, LANES), 1)


def row_ids(rows):
    return lax.broadcasted_iota(jnp.int32, (rows, LANES), 0)


def turned(value, shift):
    shift = shift % LANES
    return pltpu.roll(value, shift, 1) if shift else value


def odd(axis):
    return lax.axis_index(axis) % 2


def begin_kernel(
    gas_ref, velocity_in, fraction_in, response_in, cell_in, brick_in, crossing_in,
    grid_ref, face_ref, plane_ref, velocity_ref, fraction_ref, response_ref, cell_ref, brick_ref, crossing_ref, sems,
):
    comps, size_x, size_y, _ = gas_ref.shape
    pairs = [
        (gas_ref, grid_ref.at[:, 1 : size_x + 1, 0:size_y]),
        (velocity_in, velocity_ref), (fraction_in, fraction_ref), (response_in, response_ref),
        (cell_in, cell_ref), (brick_in, brick_ref), (crossing_in, crossing_ref),
    ]
    copies = [pltpu.make_async_copy(source, target, sems.at[i]) for i, (source, target) in enumerate(pairs)]
    for copy in copies:
        copy.start()
    zeros = jnp.zeros((ROWS_Y, LANES), jnp.float32)
    for c in range(comps):
        grid_ref[c, 0] = zeros
        grid_ref[c, size_x + 1] = zeros
        for x in range(size_x):
            grid_ref[c, x + 1, size_y:] = zeros[size_y:]
    copies[0].wait()
    lane = lane_ids(size_y)
    face = jnp.zeros((size_y, LANES), jnp.float32)
    for c in range(comps):
        plane_ref[c * size_y : (c + 1) * size_y] = grid_ref[c, 1, 0:size_y]
        for x in range(size_x):
            place = PACK * c + x
            face = jnp.where(lane == place, turned(grid_ref[c, x + 1, 0:size_y], place), face)
    face_ref[...] = face
    for copy in copies[1:]:
        copy.wait()


def parts_of(value):
    main = value.astype(jnp.bfloat16).astype(jnp.float32)
    return main, value - main


def lay_out(grid_ref, lines_ref, p, q, size_y, size_z):
    comps = grid_ref.shape[0]
    rows_z = size_z + 8
    count_y = size_y // BY
    for c in range(comps):
        planes = [grid_ref[c, p * BX + a + 1, q * BY : q * BY + REACH_Y] for a in range(REACH_X)]
        main, rest = parts_of(jnp.concatenate(planes, axis=0))
        stack = jnp.concatenate([main, rest, main, jnp.zeros((LANES - 3 * SPREAD, LANES), jnp.float32)], axis=0)
        at = ((p * count_y + q) * comps + c) * rows_z
        lines_ref[at : at + size_z] = jnp.transpose(stack)


def lay_out_top(turned_ref, lines_ref, q, comps, count_x, count_y, size_z):
    lane = lane_ids(count_x)
    rows_z = size_z + 8
    for c in range(comps):
        total = jnp.zeros((count_x, LANES), jnp.float32)
        for a in range(REACH_X):
            rows = turned_ref[pl.ds(PACK * c + a, count_x, stride=BX)]
            total = jnp.where(lane // REACH_Y == a, turned(rows, a * REACH_Y - q * BY), total)
        main, rest = parts_of(total)
        line = main + turned(rest, SPREAD) + turned(main, 2 * SPREAD)
        for p in range(count_x):
            at = ((p * count_y + q) * comps + c) * rows_z + size_z
            lines_ref[at : at + 1] = line[p : p + 1]


def prepare_kernel(
    grid_ref, velocity_ref, fraction_ref, response_ref, cell_ref, brick_ref,
    lines_ref, deposit_ref, table_ref, ready_ref, list_ref,
):
    comps, size_x, size_y, size_z = grid_ref.shape[0], grid_ref.shape[1] - 2, grid_ref.shape[2] - 8, grid_ref.shape[3]
    nblocks = velocity_ref.shape[1]
    count_x, count_y, count_z = size_x // BX, size_y // BY, size_z // BZ
    rows_z = size_z + 8

    room = nblocks + UNROLL

    def visit(k, counts):
        late = jnp.where(lax.rem(lax.div(brick_ref[k], count_z), count_y) == count_y - 1, 1, 0)
        list_ref[jnp.where(late == 1, room + counts[1], counts[0])] = k
        return counts[0] + 1 - late, counts[1] + late

    early, late = lax.fori_loop(0, nblocks, visit, (jnp.int32(0), jnp.int32(0)), unroll=8)
    for base, count in ((0, early), (room, late)):
        for u in range(UNROLL):
            list_ref[base + count + u] = nblocks
    list_ref[2 * room] = early
    list_ref[2 * room + 1] = late
    ready_ref[...] = jnp.zeros_like(ready_ref)

    deposit_ref[...] = jnp.zeros_like(deposit_ref)
    for p in range(count_x):
        for q in range(count_y):
            for c in range(comps):
                at = ((p * count_y + q) * comps + c) * rows_z + size_z
                lines_ref[at : at + 8] = jnp.zeros((8, LANES), jnp.float32)
    for p in range(count_x - 1):
        for q in range(count_y - 1):
            lay_out(grid_ref, lines_ref, p, q, size_y, size_z)

    cells = cell_ref[...]
    cell_x, cell_y, cell_z = cells // (BY * BZ), cells // BZ % BY, cells % BZ
    along_x = fraction_ref[0]

    def put(row, value):
        table_ref[pl.ds(row, nblocks, stride=TABLE_ROWS)] = value

    for a in range(REACH_X):
        put(WEIGHT + a, jnp.where(cell_x == a, 1.0 - along_x, 0.0) + jnp.where(cell_x == a - 1, along_x, 0.0))
    put(ALONG_Y, fraction_ref[1])
    put(IN_Y, cell_y.astype(jnp.float32))
    put(ALONG_Z, fraction_ref[2])
    put(IN_Z, cell_z.astype(jnp.float32))
    put(RESPONSE, response_ref[...])
    for c in range(comps):
        put(MOVING + c, velocity_ref[c])
        put(OFFSET + c, fraction_ref[c])
    spare = table_ref.shape[0] - nblocks * TABLE_ROWS
    row = row_ids(spare)
    table_ref[nblocks * TABLE_ROWS :] = jnp.where(row % TABLE_ROWS == RESPONSE, 1.0, 0.0)


def y_lines_kernel(grid_ref, face_ref, from_x_ref, edge_ref, ready_ref, out_ref):
    comps, size_x = grid_ref.shape[0], grid_ref.shape[1] - 2
    size_y = face_ref.shape[0]
    for c in range(comps):
        out_ref[c * size_x : (c + 1) * size_x] = grid_ref[c, 1 : size_x + 1, 0]
        out_ref[comps * size_x + c : comps * size_x + c + 1] = from_x_ref[c * size_y : c * size_y + 1]
    line = jnp.where(lane_ids(8) % PACK == size_x, turned(edge_ref[0:8], size_x), face_ref[0:8])
    out_ref[comps * size_x + comps : comps * size_x + comps + 1] = line[0:1]


def halo_xz_kernel(grid_in_ref, lines_in_ref, face_ref, from_x_ref, edge_ref, grid_ref, lines_ref, top_ref, turned_ref):
    comps, size_x = grid_ref.shape[0], grid_ref.shape[1] - 2
    size_y, size_z = face_ref.shape[0], grid_ref.shape[3]
    count_x, count_y = size_x // BX, size_y // BY
    for c in range(comps):
        grid_ref[c, size_x + 1, 0:size_y] = from_x_ref[c * size_y : (c + 1) * size_y]
    for q in range(count_y - 1):
        lay_out(grid_ref, lines_ref, count_x - 1, q, size_y, size_z)
    top = jnp.where(lane_ids(size_y) % PACK == size_x, turned(edge_ref[...], size_x), face_ref[...])
    top_ref[0:size_y] = top
    top_ref[size_y:] = jnp.zeros((LANES - size_y, LANES), jnp.float32)
    turned_ref[...] = jnp.transpose(top_ref[...])
    for q in range(count_y - 1):
        lay_out_top(turned_ref, lines_ref, q, comps, count_x, count_y, size_z)


def halo_y_kernel(size_y, grid_in_ref, lines_in_ref, top_in_ref, from_y_ref, grid_ref, lines_ref, turned_ref):
    comps, size_x, size_z = grid_ref.shape[0], grid_ref.shape[1] - 2, grid_ref.shape[3]
    count_x, count_y = size_x // BX, size_y // BY
    inside = lax.axis_index("gy") != lax.axis_size("gy") - 1
    kept = (row_ids(8) == 0) & inside

    def line_at(row):
        return jnp.where(kept, jnp.broadcast_to(from_y_ref[row : row + 1], (8, LANES)), 0.0)

    for c in range(comps):
        for x in range(size_x + 1):
            grid_ref[c, x + 1, size_y:] = line_at(c * size_x + x if x < size_x else comps * size_x + c)
    for p in range(count_x):
        lay_out(grid_ref, lines_ref, p, count_y - 1, size_y, size_z)
    corner = line_at(comps * size_x + comps)
    rest = jnp.zeros((LANES - size_y - 8, LANES), jnp.float32)
    turned_ref[...] = jnp.transpose(jnp.concatenate([top_in_ref[0:size_y], corner, rest], axis=0))
    lay_out_top(turned_ref, lines_ref, count_y - 1, comps, count_x, count_y, size_z)


def block_steps(dims, list_ref, brick_ref):
    comps, count_x, count_y, count_z, rows_z = dims
    nblocks = brick_ref.shape[0]
    sub = row_ids(8)
    row_y = row_ids(REACH_Y).astype(jnp.float32)
    row_z = row_ids(REACH_Z).astype(jnp.float32)
    lane = lane_ids(REACH_Y)

    def hat(rows, inside, along):
        return jnp.where(rows == inside, 1.0 - along, 0.0) + jnp.where(rows == inside + 1.0, along, 0.0)

    def place_of(at):
        k = list_ref[at]
        brick = jnp.where(k < nblocks, brick_ref[jnp.minimum(k, nblocks - 1)], 0)
        brick_x = lax.div(brick, count_y * count_z)
        brick_y = lax.rem(lax.div(brick, count_z), count_y)
        return k, brick_x * count_y + brick_y, lax.rem(brick, count_z)

    def loaded(at, lines_ref, table_ref):
        k, pair, brick_z = place_of(at)
        first = pl.multiple_of(pair * comps * rows_z + brick_z * BZ, 8)
        window = jnp.concatenate([lines_ref[pl.ds(first + c * rows_z, REACH_Z)] for c in range(comps)], axis=0)
        table = table_ref[pl.ds(pl.multiple_of(k * TABLE_ROWS, TABLE_ROWS), TABLE_ROWS)]
        return k, window, [table[i : i + 1] for i in range(TABLE_ROWS)]

    def weighted(rows):
        weight_y = hat(row_y, rows[IN_Y], rows[ALONG_Y])
        weight_z = hat(row_z, rows[IN_Z], rows[ALONG_Z])
        weight = jnp.concatenate([rows[WEIGHT + a] * weight_y for a in range(REACH_X)], axis=0)
        return weight_z, *parts_of(weight)

    def stepped(seen, weight_z, rows):
        rate = 1.0 / rows[RESPONSE]
        state, moved, pushed = [], [], []
        for c in range(comps):
            gas_sample = jnp.sum(seen[c * REACH_Z : (c + 1) * REACH_Z] * weight_z, axis=0, keepdims=True)
            drag = (gas_sample - rows[MOVING + c]) * rate
            state.append(rows[MOVING + c] + TIME_STEP * drag)
            moved.append(rows[OFFSET + c] + TIME_STEP * state[c])
            pushed.append(drag * weight_z)
        tile = jnp.broadcast_to(rows[RESPONSE], (STATE, LANES))
        for i, value in enumerate(state + moved):
            tile = jnp.where(sub == i, value, tile)
        gap = jnp.zeros((LANES // 2 - comps * REACH_Z, LANES), jnp.float32)
        main, rest = parts_of(jnp.concatenate(pushed, axis=0))
        return tile, jnp.concatenate([main, gap, rest, gap], axis=0)

    def gathered(one, two):
        tables, windows, weights = [], [], []
        for _, window, rows in (one, two):
            weight_z, main, rest = weighted(rows)
            weights.append((weight_z, main, rest))
            unused = jnp.zeros((LANES - 3 * SPREAD, LANES), jnp.float32)
            tables.append(jnp.concatenate([main, main, rest, unused], axis=0).astype(jnp.bfloat16))
            windows.append(window)
        seen = lax.dot_general(
            jnp.concatenate(windows, axis=0).astype(jnp.bfloat16), jnp.concatenate(tables, axis=1),
            (((1,), (0,)), ((), ())), preferred_element_type=jnp.float32,
        )
        height = comps * REACH_Z
        tiles, pushes, spreads = [], [], []
        for i, (_, _, rows) in enumerate((one, two)):
            mine = seen[i * height : (i + 1) * height, i * LANES : (i + 1) * LANES]
            tile, push = stepped(mine, weights[i][0], rows)
            tiles.append(tile)
            pushes.append(push)
            spreads.extend(weights[i][1:])
        return tiles, jnp.concatenate(pushes, axis=0).astype(jnp.bfloat16), jnp.concatenate(spreads, axis=0).astype(jnp.bfloat16)

    def shared(push, spread):
        shares = lax.dot_general(spread, push, (((1,), (1,)), ((), ())), preferred_element_type=jnp.float32)
        results = []
        for i in (0, 1):
            mine = shares[2 * i * SPREAD : 2 * (i + 1) * SPREAD, i * LANES : (i + 1) * LANES]
            mine = mine[:SPREAD] + mine[SPREAD:]
            results.append(mine + pltpu.roll(mine, LANES // 2, 1))
        return results

    def add(deposit_ref, at, shares):
        sums = []
        for u, share in enumerate(shares):
            _, pair, brick_z = place_of(at + u)
            first_z = brick_z * BZ
            within = ((lane - first_z) & (LANES - 1)) < REACH_Z
            parts = []
            for c in range(comps):
                shift = (first_z - c * REACH_Z + LANES) & (LANES - 1)
                for a in range(REACH_X):
                    part = pltpu.roll(share[a * REACH_Y : (a + 1) * REACH_Y], shift, 1)
                    parts.append(jnp.where(within, part, 0.0))
            sel = jnp.where(brick_z == count_z - 1, 1, 0)
            start = pl.multiple_of((sel * count_x * count_y + pair) * comps * SPREAD, 8)
            sums.append((start, parts))
        for start, parts in sums:
            spots = [pl.ds(start + i * REACH_Y, REACH_Y) for i in range(comps * REACH_X)]
            totals = [deposit_ref[spot] + part for spot, part in zip(spots, parts)]
            for spot, total in zip(spots, totals):
                deposit_ref[spot] = total

    def group_of(taken):
        tiles, fresh = [], []
        for u in range(0, UNROLL, 2):
            both, push, spread = gathered(taken[u], taken[u + 1])
            tiles.extend(both)
            fresh.append((push, spread))
        return tiles, fresh

    def keep(state_ref, taken, tiles):
        for (k, _, _), tile in zip(taken, tiles):
            state_ref[pl.ds(pl.multiple_of(STATE * k, STATE), STATE)] = tile

    def deposits_of(kept):
        shares = []
        for push, spread in kept:
            shares.extend(shared(push, spread))
        return shares

    return loaded, group_of, keep, deposits_of, add


def groups_in(list_ref, late):
    room = (list_ref.shape[0] - 2) // 2
    return late * room, (list_ref[2 * room + late] + UNROLL - 1) // UNROLL


def gather_kernel(dims, list_ref, brick_ref, lines_ref, table_ref, state_ref, push_ref, spread_ref):
    loaded, group_of, keep, _, _ = block_steps(dims, list_ref, brick_ref)
    base, groups = groups_in(list_ref, 0)

    @pl.loop(0, groups)
    def _(group):
        taken = [loaded(base + group * UNROLL + u, lines_ref, table_ref) for u in range(UNROLL)]
        tiles, fresh = group_of(taken)
        keep(state_ref, taken, tiles)
        for i, (push, spread) in enumerate(fresh):
            push_ref[group * (UNROLL // 2) + i] = push
            spread_ref[group * (UNROLL // 2) + i] = spread


def deposit_kernel(dims, list_ref, brick_ref, push_ref, spread_ref, deposit_in_ref, deposit_ref):
    _, _, _, deposits_of, add = block_steps(dims, list_ref, brick_ref)
    base, groups = groups_in(list_ref, 0)

    @pl.loop(0, groups)
    def _(group):
        pairs = [group * (UNROLL // 2) + i for i in range(UNROLL // 2)]
        add(deposit_ref, base + group * UNROLL, deposits_of([(push_ref[i], spread_ref[i]) for i in pairs]))


def late_kernel(
    dims, slots, list_ref, brick_ref, crossing_ref, lines_ref, table_ref, state_in_ref, deposit_in_ref,
    state_ref, deposit_ref, leaving_ref, push_ref, spread_ref,
):
    loaded, group_of, keep, deposits_of, add = block_steps(dims, list_ref, brick_ref)
    base, groups = groups_in(list_ref, 1)
    push_ref[...] = jnp.zeros_like(push_ref)
    spread_ref[...] = jnp.zeros_like(spread_ref)

    @pl.loop(0, groups + 1)
    def _(group):
        now = base + jnp.maximum(jnp.minimum(group, groups - 1), 0) * UNROLL
        before = base + jnp.maximum(group - 1, 0) * UNROLL
        taken = [loaded(now + u, lines_ref, table_ref) for u in range(UNROLL)]
        shares = deposits_of([(push_ref[i], spread_ref[i]) for i in range(UNROLL // 2)])
        tiles, fresh = group_of(taken)
        add(deposit_ref, before, shares)
        keep(state_ref, taken, tiles)
        for i, (push, spread) in enumerate(fresh):
            push_ref[i] = push
            spread_ref[i] = spread

    rows = leaving_ref.shape[0] // (6 * slots)
    for face in range(6):
        tiles = []
        for slot in range(slots):
            block = crossing_ref[face, slot]
            spot = pl.ds(pl.multiple_of(jnp.maximum(block, 0) * STATE, STATE), STATE)
            live = jnp.full((STATE, LANES), block, jnp.int32) >= 0
            tiles.append(jnp.where(live, state_ref[spot], 0.0))
        for slot, tile in enumerate(tiles):
            leaving_ref[pl.ds(face * rows * slots + slot, rows, stride=slots)] = tile[:rows]


def merge_kernel(tiles_ref, plane_ref):
    _, comps, planes, _, _ = plane_ref.shape
    count_x, count_y = (planes - 1) // BX, tiles_ref.shape[0] // (2 * ((planes - 1) // BX) * comps * SPREAD)
    top = row_ids(REACH_Y) >= BY

    for sel in (0, 1):
        for c in range(comps):
            for x in range(planes):
                bricks = [(x // BX, x % BX)] if x < planes - 1 else []
                if x and x % BX == 0:
                    bricks.append((x // BX - 1, BX))

                def tile(q):
                    total = None
                    for p, a in bricks:
                        at = (((sel * count_x + p) * count_y + q) * comps + c) * SPREAD + a * REACH_Y
                        value = tiles_ref[at : at + REACH_Y]
                        total = value if total is None else total + value
                    return total

                carried = None
                for q in range(0, count_y, 2):
                    here = tile(q)
                    if carried is not None:
                        here = here + carried
                    between = pltpu.roll(tile(q + 1), BY, 0)
                    here = here + jnp.where(top, between, 0.0)
                    carried = jnp.where(top, 0.0, between)
                    plane_ref[sel, c, x, q * BY : q * BY + REACH_Y] = here
                plane_ref[sel, c, x, count_y * BY :] = carried


def send_y_kernel(push, diffuse, leaving_ref, grid_ref, tiles_ref, y_ref, lines_ref):
    comps, size_x, size_y = grid_ref.shape[0], grid_ref.shape[1] - 2, grid_ref.shape[2] - 8
    count_x, count_y = size_x // BX, size_y // BY
    rows = leaving_ref.shape[1]
    first = jnp.full((rows, LANES), odd("gy")) == 0
    y_ref[0, 0:rows] = jnp.where(first, leaving_ref[2], leaving_ref[3])
    y_ref[1, 0:rows] = jnp.where(first, leaving_ref[3], leaving_ref[2])
    lines_ref[...] = jnp.zeros_like(lines_ref)
    for sel in (0, 1):
        for c in range(comps):
            for p in range(count_x):
                at = (((sel * count_x + p) * count_y + count_y - 1) * comps + c) * SPREAD + BY
                spot = slice(c * ROWS_Y + p * BX, c * ROWS_Y + p * BX + REACH_X)
                lines_ref[sel, spot] = lines_ref[sel, spot] + tiles_ref[pl.ds(at, REACH_X, stride=REACH_Y)]
    lane, sub = lane_ids(ROWS_Y), row_ids(ROWS_Y)
    corner = jnp.zeros((1, LANES), jnp.float32)
    for c in range(comps):
        spot = slice(c * ROWS_Y, (c + 1) * ROWS_Y)
        wrapped = lines_ref[1, spot]
        line = push * (lines_ref[0, spot] + jnp.where(lane == 0, 0.0, wrapped))
        beside = jnp.concatenate([grid_ref[c, 1 : size_x + 1, size_y - 1], jnp.zeros((8, LANES), jnp.float32)], axis=0)
        line = line + diffuse * beside
        y_ref[0, rows + c * ROWS_Y : rows + (c + 1) * ROWS_Y] = line
        y_ref[1, rows + c * ROWS_Y : rows + (c + 1) * ROWS_Y] = line
        far = jnp.broadcast_to(push * wrapped[:, 0:1], (ROWS_Y, LANES))
        corner = corner + jnp.sum(jnp.where(lane == sub + PACK * c, far, 0.0), axis=0, keepdims=True)
    at = rows + size_x + 1
    y_ref[0, at : at + 1] = corner
    y_ref[1, at : at + 1] = corner


def send_xz_kernel(push, diffuse, grid_ref, deposit_ref, x_ref, z_ref):
    comps, size_x = grid_ref.shape[0], grid_ref.shape[1] - 2
    size_y = z_ref.shape[0]
    lane = lane_ids(size_y)
    packed = jnp.zeros((size_y, LANES), jnp.float32)
    for c in range(comps):
        face = jnp.zeros((size_y, LANES), jnp.float32)
        for x in range(size_x + 1):
            beyond = push * deposit_ref[1, c, x, 0:size_y]
            if x < size_x:
                beyond = beyond + diffuse * turned(grid_ref[c, x + 1, 0:size_y], 1)
            else:
                total = push * deposit_ref[0, c, x, 0:size_y] + jnp.where(lane == 0, 0.0, beyond)
                x_ref[c * size_y : (c + 1) * size_y] = diffuse * grid_ref[c, size_x, 0:size_y] + total
            face = jnp.where(lane == x, turned(beyond, x), face)
        packed = packed + turned(face, PACK * c)
    z_ref[...] = packed


def base_kernel(push, diffuse, grid_ref, deposit_ref, top_ref, base_ref):
    comps, size_x, size_y, size_z = base_ref.shape
    lane = lane_ids(size_y)
    top = top_ref[0:size_y]
    for c in range(comps):
        for x in range(size_x):
            here = grid_ref[c, x + 1, 0:size_y]
            laplace = grid_ref[c, x + 2, 0:size_y]
            if x:
                laplace = laplace + grid_ref[c, x, 0:size_y]
            before = jnp.where(row_ids(size_y) == 0, 0.0, pltpu.roll(here, 1, 0))
            laplace = laplace + grid_ref[c, x + 1, 1 : size_y + 1] + before
            ahead = jnp.where(lane == size_z - 1, turned(top, size_z - 1 - (PACK * c + x)), turned(here, -1))
            laplace = laplace + ahead + jnp.where(lane == 0, 0.0, turned(here, 1)) - 6.0 * here
            total = deposit_ref[0, c, x, 0:size_y] + jnp.where(lane == 0, 0.0, deposit_ref[1, c, x, 0:size_y])
            base_ref[c, x] = here + diffuse * laplace + push * total


def below(first_ref, second_ref, rows):
    got = jnp.where(odd("gy") == 1, first_ref[rows], second_ref[rows])
    return jnp.where(lax.axis_index("gy") != 0, got, 0.0)


def relay_kernel(size_x, size_y, comps, count, first_ref, second_ref, x_in_ref, z_in_ref, leaving_ref, x_ref, z_ref, edge_ref):
    edge = comps * size_y
    x_ref[0:edge] = x_in_ref[...]
    for c in range(comps):
        at = count + c * ROWS_Y + size_x
        spot = slice(c * size_y, c * size_y + 1)
        x_ref[spot] = x_in_ref[spot] + below(first_ref, second_ref, slice(at, at + 1))
    x_ref[edge : edge + count] = leaving_ref[0]
    if x_ref.shape[0] > edge + count:
        x_ref[edge + count : edge + 2 * count] = leaving_ref[1]
    at = count + size_x + 1
    edge_ref[...] = z_in_ref[...]
    edge_ref[0:1] = z_in_ref[0:1] + below(first_ref, second_ref, slice(at, at + 1))
    up = odd("gz")
    z_ref[up, 0:count] = leaving_ref[4]
    z_ref[up, count : count + size_y] = edge_ref[...]
    z_ref[1 - up, 0:count] = leaving_ref[5]
    z_ref[1 - up, count : count + size_y] = jnp.zeros((size_y, LANES), jnp.float32)


def finish_kernel(
    count, base_ref, y1_ref, y2_ref, x_ref, minus_x_ref, z1_ref, z2_ref, edge_ref, state_ref,
    gas_ref, arrivals_ref, velocity_ref,
):
    comps, size_x, size_y, _ = base_ref.shape
    first_row, first_lane = row_ids(size_y) == 0, lane_ids(size_y) == 0
    rows = slice(count, count + size_y)
    from_first = odd("gz") == 1
    face = jnp.where(from_first, z1_ref[rows], z2_ref[rows])
    corner = edge_ref[...]
    for c in range(comps):
        for x in range(size_x):
            at = count + c * ROWS_Y + x
            line = jnp.broadcast_to(below(y1_ref, y2_ref, slice(at, at + 1)), (size_y, LANES))
            total = base_ref[c, x] + jnp.where(first_row, line, 0.0)
            far = turned(face, -(PACK * c + x))
            if x == 0:
                total = total + x_ref[c * size_y : (c + 1) * size_y]
                far = far + turned(corner, -(PACK * c + size_x))
            gas_ref[c, x] = total + jnp.where(first_lane, far, 0.0)

    slots = arrivals_ref.shape[2]
    lower, upper = lax.axis_index("gy") != 0, lax.axis_index("gy") != lax.axis_size("gy") - 1
    odd_y = odd("gy") == 1
    for i in range(arrivals_ref.shape[1]):

        def rows_of(ref, at=0):
            return ref[at + i * slots : at + (i + 1) * slots]

        arrivals_ref[0, i] = rows_of(x_ref, comps * size_y)
        arrivals_ref[1, i] = rows_of(minus_x_ref, minus_x_ref.shape[0] - count)
        y1, y2 = rows_of(y1_ref), rows_of(y2_ref)
        arrivals_ref[2, i] = jnp.where(lower, jnp.where(odd_y, y1, y2), 0.0)
        arrivals_ref[3, i] = jnp.where(upper, jnp.where(odd_y, y2, y1), 0.0)
        z1, z2 = rows_of(z1_ref), rows_of(z2_ref)
        arrivals_ref[4, i] = jnp.where(from_first, z1, z2)
        arrivals_ref[5, i] = jnp.where(from_first, z2, z1)
    for c in range(comps):
        velocity_ref[c] = state_ref[pl.ds(c, velocity_ref.shape[1], stride=STATE)]


def per_device(gas_field, velocity, fraction, response, cell_index, brick_index, crossing):
    comps, size_x, size_y, size_z = gas_field.shape
    nblocks = velocity.shape[0]
    loading = 0.5 * size_x * size_y * size_z / (nblocks * 128)
    push, diffuse = -TIME_STEP * loading, TIME_STEP * VISCOSITY
    velocity = jnp.transpose(velocity, (1, 0, 2))
    fraction = jnp.transpose(fraction, (1, 0, 2))
    spare = nblocks + 8
    rows_z = size_z + 8
    grid_shape = (comps, size_x + 2, ROWS_Y, LANES)
    lines_shape = ((size_x // BX) * (size_y // BY) * comps * rows_z, LANES)
    deposit_shape = (2 * (size_x // BX) * (size_y // BY) * comps * SPREAD, LANES)

    inputs = (gas_field, velocity, fraction, response, cell_index, brick_index, crossing)
    inputs = [pltpu.with_memory_space_constraint(array, pltpu.HBM) for array in inputs]
    grid, face, plane, velocity, fraction, response, cell_index, brick_index, crossing = call(
        begin_kernel,
        [grid_shape, (size_y, LANES), (comps * size_y, LANES)]
        + [jax.ShapeDtypeStruct(array.shape, array.dtype) for array in inputs[1:]],
        *inputs, hbm=range(7), scratch=(pltpu.SemaphoreType.DMA((7,)),), limit=40,
    )
    from_z = moved_along(face, "gz", -1)
    from_x = moved_along(plane, "gx", -1)
    from_xz = moved_diagonally(face, -1)
    lines, deposit, table, ready, blocks = call(
        prepare_kernel,
        [
            lines_shape,
            deposit_shape,
            (TABLE_ROWS * spare, LANES),
            (8, LANES),
            jax.ShapeDtypeStruct((2 * (nblocks + UNROLL) + 2,), jnp.int32),
        ],
        grid, velocity, fraction, response, cell_index, brick_index,
        smem=(5,), smem_outs=(4,), cycles=3000,
    )
    line_rows = -(-(comps * size_x + comps + 1) // 8) * 8
    (y_lines,) = call(y_lines_kernel, [(line_rows, LANES)], grid, from_z, from_x, from_xz, ready)
    from_y = moved_along(y_lines, "gy", -1)
    square = pltpu.VMEM((LANES, LANES), jnp.float32)
    grid, lines, top = call(
        halo_xz_kernel, [grid_shape, lines_shape, (LANES, LANES)], grid, lines, from_z, from_x, from_xz,
        aliases={0: 0, 1: 1}, scratch=(square,), cycles=1000,
    )

    dims = (comps, size_x // BX, size_y // BY, size_z // BZ, rows_z)
    slots = crossing.shape[1]
    count = 7 * slots

    def parts(pairs):
        return [(pairs, 2 * LANES, LANES), (pairs, 4 * SPREAD, LANES)]

    state, push_parts, spread_parts = call(
        functools.partial(gather_kernel, dims),
        [(STATE * spare, LANES)]
        + [jax.ShapeDtypeStruct(shape, jnp.bfloat16) for shape in parts((nblocks + UNROLL) // 2)],
        blocks, brick_index, lines, table, smem=(0, 1), cycles=4000,
    )
    grid, lines = call(
        functools.partial(halo_y_kernel, size_y), [grid_shape, lines_shape], grid, lines, top, from_y,
        aliases={0: 0, 1: 1}, scratch=(square,), cycles=1000,
    )
    state, deposit, leaving = call(
        functools.partial(late_kernel, dims, slots),
        [(STATE * spare, LANES), deposit_shape, (6 * count, LANES)],
        blocks, brick_index, crossing, lines, table, state, deposit,
        smem=(0, 1, 2), aliases={5: 0, 6: 1}, cycles=2000,
        scratch=[pltpu.VMEM(shape, jnp.bfloat16) for shape in parts(UNROLL // 2)],
    )
    leaving = leaving.reshape(6, count, LANES)
    (to_y,) = call(
        functools.partial(send_y_kernel, push, diffuse), [(2, count + comps * ROWS_Y, LANES)],
        leaving, grid, deposit, cycles=300, scratch=(pltpu.VMEM((2, comps * ROWS_Y, LANES), jnp.float32),),
    )
    y1, y2 = swapped_y((to_y[0], to_y[1]))
    (deposit,) = call(
        functools.partial(deposit_kernel, dims), [deposit_shape], blocks, brick_index, push_parts, spread_parts, deposit,
        smem=(0, 1), aliases={4: 0}, cycles=4000,
    )
    (deposit,) = call(merge_kernel, [(2, comps, size_x + 1, ROWS_Y, LANES)], deposit, cycles=500)
    to_x, to_z = call(
        functools.partial(send_xz_kernel, push, diffuse), [(comps * size_y, LANES), (size_y, LANES)],
        grid, deposit, cycles=500,
    )
    (base,) = call(
        functools.partial(base_kernel, push, diffuse), [gas_field.shape], grid, deposit, top, cycles=1000,
    )
    edge = comps * size_y
    both = lax.axis_size("gx") == 2
    to_x, to_z, to_xz = call(
        functools.partial(relay_kernel, size_x, size_y, comps, count),
        [(edge + (2 if both else 1) * count, LANES), (2, count + size_y, LANES), (size_y, LANES)],
        y1, y2, to_x, to_z, leaving,
    )
    got_x = moved_along(to_x, "gx", 1)
    z1, z2 = swapped_z((to_z[0], to_z[1]))
    got_xz = moved_diagonally(to_xz, 1)
    got_mx = got_x if both else moved_along(leaving[1], "gx", -1)
    gas_next, arrivals, velocity_next = call(
        functools.partial(finish_kernel, count),
        [gas_field.shape, (6, 7, crossing.shape[1], LANES), (comps, nblocks, LANES)],
        base, y1, y2, got_x, got_mx, z1, z2, got_xz, state,
    )
    return gas_next, jnp.transpose(velocity_next, (1, 0, 2)), jnp.transpose(arrivals, (0, 2, 1, 3))


def solution(mesh):
    owner = ("gx", "gz", "gy")
    in_specs = (
        P(None, "gx", "gy", "gz"),
        P(owner, None, None),
        P(owner, None, None),
        P(owner, None),
        P(owner, None),
        P(owner),
        P(owner, None),
    )
    out_specs = (
        P(None, "gx", "gy", "gz"),
        P(owner, None, None),
        P(owner, None, None, None),
    )
    return jax.shard_map(
        per_device, mesh=mesh, in_specs=in_specs, out_specs=out_specs, check_vma=False
    )
```

```python
import functools

import jax
import jax.numpy as jnp
from jax import lax
from jax.experimental import pallas as pl
from jax.experimental.pallas import tpu as pltpu
from jax.sharding import PartitionSpec as P

BX = 4
BY = 4
BZ = 8

TIME_STEP = 0.25
VISCOSITY = 0.4

LANES = 128
PACK = 32
ROWS_Y = 24
REACH_X = BX + 1
REACH_Y = 8
SPREAD = REACH_X * REACH_Y
REACH_Z = 2 * BZ
UNROLL = 8

WEIGHT, ALONG_Y, IN_Y, ALONG_Z, IN_Z, RESPONSE, MOVING, OFFSET = 0, 5, 6, 7, 8, 9, 10, 13
TABLE_ROWS = 16
STATE = 8

VMEM = pl.BlockSpec(memory_space=pltpu.VMEM)
SMEM = pl.BlockSpec(memory_space=pltpu.SMEM)
HBM = pl.BlockSpec(memory_space=pltpu.HBM)


def moved_along(block, axis, distance):
    count = lax.axis_size(axis)
    return lax.ppermute(block, axis, [(i, (i + distance) % count) for i in range(count)])


def swapped_z(blocks):
    count = lax.axis_size("gz")
    first = [(i, i ^ 1) for i in range(count)]
    second = [(i, (((i + 1) ^ 1) - 1) % count) for i in range(count)]
    return lax.ppermute(blocks[0], "gz", first), lax.ppermute(blocks[1], "gz", second)


def swapped_y(blocks):
    nz, ny = lax.axis_size("gz"), lax.axis_size("gy")
    first = [(j, j ^ 1) for j in range(ny)]
    second = []
    for k in range(nz):
        second.append((k * ny, (k ^ 1) * ny))
        second.append((k * ny + ny - 1, (k ^ 1) * ny + ny - 1))
        second.extend((k * ny + j, k * ny + ((j + 1) ^ 1) - 1) for j in range(1, ny - 1))
    return lax.ppermute(blocks[0], "gy", first), lax.ppermute(blocks[1], ("gz", "gy"), second)


def moved_diagonally(block, distance):
    nx, nz = lax.axis_size("gx"), lax.axis_size("gz")
    route = [(i * nz + k, (i + distance) % nx * nz + (k + distance) % nz) for i in range(nx) for k in range(nz)]
    return lax.ppermute(block, ("gx", "gz"), route)


def call(body, outs, *operands, smem=(), hbm=(), smem_outs=(), scratch=(), aliases=None, cycles=0, limit=40):
    return pl.pallas_call(
        body,
        out_shape=[o if isinstance(o, jax.ShapeDtypeStruct) else jax.ShapeDtypeStruct(o, jnp.float32) for o in outs],
        in_specs=[SMEM if i in smem else HBM if i in hbm else VMEM for i in range(len(operands))],
        out_specs=[SMEM if i in smem_outs else VMEM for i in range(len(outs))],
        scratch_shapes=list(scratch),
        input_output_aliases=aliases or {},
        compiler_params=pltpu.CompilerParams(vmem_limit_bytes=limit * 1024 * 1024),
        cost_estimate=pl.CostEstimate(flops=cycles * 4096, bytes_accessed=cycles * 1024, transcendentals=0),
    )(*operands)


def lane_ids(rows):
    return lax.broadcasted_iota(jnp.int32, (rows, LANES), 1)


def row_ids(rows):
    return lax.broadcasted_iota(jnp.int32, (rows, LANES), 0)


def turned(value, shift):
    shift = shift % LANES
    return pltpu.roll(value, shift, 1) if shift else value


def odd(axis):
    return lax.axis_index(axis) % 2


def begin_kernel(
    gas_ref, velocity_in, fraction_in, response_in, cell_in, brick_in, crossing_in,
    grid_ref, face_ref, plane_ref, velocity_ref, fraction_ref, response_ref, cell_ref, brick_ref, crossing_ref, sems,
):
    comps, size_x, size_y, _ = gas_ref.shape
    pairs = [
        (gas_ref, grid_ref.at[:, 1 : size_x + 1, 0:size_y]),
        (velocity_in, velocity_ref), (fraction_in, fraction_ref), (response_in, response_ref),
        (cell_in, cell_ref), (brick_in, brick_ref), (crossing_in, crossing_ref),
    ]
    copies = [pltpu.make_async_copy(source, target, sems.at[i]) for i, (source, target) in enumerate(pairs)]
    for copy in copies:
        copy.start()
    zeros = jnp.zeros((ROWS_Y, LANES), jnp.float32)
    for c in range(comps):
        grid_ref[c, 0] = zeros
        grid_ref[c, size_x + 1] = zeros
        for x in range(size_x):
            grid_ref[c, x + 1, size_y:] = zeros[size_y:]
    copies[0].wait()
    lane = lane_ids(size_y)
    face = jnp.zeros((size_y, LANES), jnp.float32)
    for c in range(comps):
        plane_ref[c * size_y : (c + 1) * size_y] = grid_ref[c, 1, 0:size_y]
        for x in range(size_x):
            place = PACK * c + x
            face = jnp.where(lane == place, turned(grid_ref[c, x + 1, 0:size_y], place), face)
    face_ref[...] = face
    for copy in copies[1:]:
        copy.wait()


def parts_of(value):
    main = value.astype(jnp.bfloat16).astype(jnp.float32)
    return main, value - main


def lay_out(grid_ref, lines_ref, p, q, size_y, size_z):
    comps = grid_ref.shape[0]
    rows_z = size_z + 8
    count_y = size_y // BY
    for c in range(comps):
        planes = [grid_ref[c, p * BX + a + 1, q * BY : q * BY + REACH_Y] for a in range(REACH_X)]
        main, rest = parts_of(jnp.concatenate(planes, axis=0))
        stack = jnp.concatenate([main, rest, main, jnp.zeros((LANES - 3 * SPREAD, LANES), jnp.float32)], axis=0)
        at = ((p * count_y + q) * comps + c) * rows_z
        lines_ref[at : at + size_z] = jnp.transpose(stack)


def lay_out_top(turned_ref, lines_ref, q, comps, count_x, count_y, size_z):
    lane = lane_ids(count_x)
    rows_z = size_z + 8
    for c in range(comps):
        total = jnp.zeros((count_x, LANES), jnp.float32)
        for a in range(REACH_X):
            rows = turned_ref[pl.ds(PACK * c + a, count_x, stride=BX)]
            total = jnp.where(lane // REACH_Y == a, turned(rows, a * REACH_Y - q * BY), total)
        main, rest = parts_of(total)
        line = main + turned(rest, SPREAD) + turned(main, 2 * SPREAD)
        for p in range(count_x):
            at = ((p * count_y + q) * comps + c) * rows_z + size_z
            lines_ref[at : at + 1] = line[p : p + 1]


def prepare_kernel(
    grid_ref, velocity_ref, fraction_ref, response_ref, cell_ref, brick_ref,
    lines_ref, deposit_ref, table_ref, ready_ref, list_ref,
):
    comps, size_x, size_y, size_z = grid_ref.shape[0], grid_ref.shape[1] - 2, grid_ref.shape[2] - 8, grid_ref.shape[3]
    nblocks = velocity_ref.shape[1]
    count_x, count_y, count_z = size_x // BX, size_y // BY, size_z // BZ
    rows_z = size_z + 8

    room = nblocks + UNROLL

    def visit(k, counts):
        late = jnp.where(lax.rem(lax.div(brick_ref[k], count_z), count_y) == count_y - 1, 1, 0)
        list_ref[jnp.where(late == 1, room + counts[1], counts[0])] = k
        return counts[0] + 1 - late, counts[1] + late

    early, late = lax.fori_loop(0, nblocks, visit, (jnp.int32(0), jnp.int32(0)), unroll=8)
    for base, count in ((0, early), (room, late)):
        for u in range(UNROLL):
            list_ref[base + count + u] = nblocks
    list_ref[2 * room] = early
    list_ref[2 * room + 1] = late
    ready_ref[...] = jnp.zeros_like(ready_ref)

    deposit_ref[...] = jnp.zeros_like(deposit_ref)
    for p in range(count_x):
        for q in range(count_y):
            for c in range(comps):
                at = ((p * count_y + q) * comps + c) * rows_z + size_z
                lines_ref[at : at + 8] = jnp.zeros((8, LANES), jnp.float32)
    for p in range(count_x - 1):
        for q in range(count_y - 1):
            lay_out(grid_ref, lines_ref, p, q, size_y, size_z)

    cells = cell_ref[...]
    cell_x, cell_y, cell_z = cells // (BY * BZ), cells // BZ % BY, cells % BZ
    along_x = fraction_ref[0]

    def put(row, value):
        table_ref[pl.ds(row, nblocks, stride=TABLE_ROWS)] = value

    for a in range(REACH_X):
        put(WEIGHT + a, jnp.where(cell_x == a, 1.0 - along_x, 0.0) + jnp.where(cell_x == a - 1, along_x, 0.0))
    put(ALONG_Y, fraction_ref[1])
    put(IN_Y, cell_y.astype(jnp.float32))
    put(ALONG_Z, fraction_ref[2])
    put(IN_Z, cell_z.astype(jnp.float32))
    put(RESPONSE, response_ref[...])
    for c in range(comps):
        put(MOVING + c, velocity_ref[c])
        put(OFFSET + c, fraction_ref[c])
    spare = table_ref.shape[0] - nblocks * TABLE_ROWS
    row = row_ids(spare)
    table_ref[nblocks * TABLE_ROWS :] = jnp.where(row % TABLE_ROWS == RESPONSE, 1.0, 0.0)


def y_lines_kernel(grid_ref, face_ref, from_x_ref, edge_ref, ready_ref, out_ref):
    comps, size_x = grid_ref.shape[0], grid_ref.shape[1] - 2
    size_y = face_ref.shape[0]
    for c in range(comps):
        out_ref[c * size_x : (c + 1) * size_x] = grid_ref[c, 1 : size_x + 1, 0]
        out_ref[comps * size_x + c : comps * size_x + c + 1] = from_x_ref[c * size_y : c * size_y + 1]
    line = jnp.where(lane_ids(8) % PACK == size_x, turned(edge_ref[0:8], size_x), face_ref[0:8])
    out_ref[comps * size_x + comps : comps * size_x + comps + 1] = line[0:1]


def halo_xz_kernel(grid_in_ref, lines_in_ref, face_ref, from_x_ref, edge_ref, grid_ref, lines_ref, top_ref, turned_ref):
    comps, size_x = grid_ref.shape[0], grid_ref.shape[1] - 2
    size_y, size_z = face_ref.shape[0], grid_ref.shape[3]
    count_x, count_y = size_x // BX, size_y // BY
    for c in range(comps):
        grid_ref[c, size_x + 1, 0:size_y] = from_x_ref[c * size_y : (c + 1) * size_y]
    for q in range(count_y - 1):
        lay_out(grid_ref, lines_ref, count_x - 1, q, size_y, size_z)
    top = jnp.where(lane_ids(size_y) % PACK == size_x, turned(edge_ref[...], size_x), face_ref[...])
    top_ref[0:size_y] = top
    top_ref[size_y:] = jnp.zeros((LANES - size_y, LANES), jnp.float32)
    turned_ref[...] = jnp.transpose(top_ref[...])
    for q in range(count_y - 1):
        lay_out_top(turned_ref, lines_ref, q, comps, count_x, count_y, size_z)


def halo_y_kernel(size_y, grid_in_ref, lines_in_ref, top_in_ref, first_ref, second_ref, grid_ref, lines_ref, turned_ref):
    comps, size_x, size_z = grid_ref.shape[0], grid_ref.shape[1] - 2, grid_ref.shape[3]
    count_x, count_y = size_x // BX, size_y // BY
    inside = lax.axis_index("gy") != lax.axis_size("gy") - 1
    kept = (row_ids(8) == 0) & inside
    even = jnp.full((1, LANES), odd("gy")) == 0

    def line_at(row):
        line = jnp.where(even, first_ref[row : row + 1], second_ref[row : row + 1])
        return jnp.where(kept, jnp.broadcast_to(line, (8, LANES)), 0.0)

    for c in range(comps):
        for x in range(size_x + 1):
            grid_ref[c, x + 1, size_y:] = line_at(c * size_x + x if x < size_x else comps * size_x + c)
    for p in range(count_x):
        lay_out(grid_ref, lines_ref, p, count_y - 1, size_y, size_z)
    corner = line_at(comps * size_x + comps)
    rest = jnp.zeros((LANES - size_y - 8, LANES), jnp.float32)
    turned_ref[...] = jnp.transpose(jnp.concatenate([top_in_ref[0:size_y], corner, rest], axis=0))
    lay_out_top(turned_ref, lines_ref, count_y - 1, comps, count_x, count_y, size_z)


def block_steps(dims, list_ref, brick_ref):
    comps, _, count_y, count_z, rows_z = dims
    nblocks = brick_ref.shape[0]
    sub = row_ids(8)
    row_y = row_ids(REACH_Y).astype(jnp.float32)
    row_z = row_ids(REACH_Z).astype(jnp.float32)
    lanes = lane_ids(REACH_Z)

    def hat(rows, inside, along):
        return jnp.where(rows == inside, 1.0 - along, 0.0) + jnp.where(rows == inside + 1.0, along, 0.0)

    def place_of(at):
        k = list_ref[at]
        brick = jnp.where(k < nblocks, brick_ref[jnp.minimum(k, nblocks - 1)], 0)
        brick_x = lax.div(brick, count_y * count_z)
        brick_y = lax.rem(lax.div(brick, count_z), count_y)
        return k, brick_x * count_y + brick_y, lax.rem(brick, count_z)

    def loaded(at, lines_ref, table_ref):
        k, pair, brick_z = place_of(at)
        first = pl.multiple_of(pair * comps * rows_z + brick_z * BZ, 8)
        window = jnp.concatenate([lines_ref[pl.ds(first + c * rows_z, REACH_Z)] for c in range(comps)], axis=0)
        table = table_ref[pl.ds(pl.multiple_of(k * TABLE_ROWS, TABLE_ROWS), TABLE_ROWS)]
        return k, window, [table[i : i + 1] for i in range(TABLE_ROWS)]

    def weighted(rows):
        weight_y = hat(row_y, rows[IN_Y], rows[ALONG_Y])
        weight_z = hat(row_z, rows[IN_Z], rows[ALONG_Z])
        weight = jnp.concatenate([rows[WEIGHT + a] * weight_y for a in range(REACH_X)], axis=0)
        return weight_z, *parts_of(weight)

    def stepped(seen, weight_z, rows):
        rate = 1.0 / rows[RESPONSE]
        state, moved, pushed = [], [], []
        for c in range(comps):
            gas_sample = jnp.sum(seen[c * REACH_Z : (c + 1) * REACH_Z] * weight_z, axis=0, keepdims=True)
            drag = (gas_sample - rows[MOVING + c]) * rate
            state.append(rows[MOVING + c] + TIME_STEP * drag)
            moved.append(rows[OFFSET + c] + TIME_STEP * state[c])
            pushed.append(drag * weight_z)
        tile = jnp.broadcast_to(rows[RESPONSE], (STATE, LANES))
        for i, value in enumerate(state + moved):
            tile = jnp.where(sub == i, value, tile)
        return tile, jnp.concatenate(parts_of(jnp.concatenate(pushed, axis=0)), axis=0)

    def gathered(one, two):
        tables, windows, weights = [], [], []
        for _, window, rows in (one, two):
            weight_z, main, rest = weighted(rows)
            weights.append((weight_z, main, rest))
            unused = jnp.zeros((LANES - 3 * SPREAD, LANES), jnp.float32)
            tables.append(jnp.concatenate([main, main, rest, unused], axis=0).astype(jnp.bfloat16))
            windows.append(window)
        seen = lax.dot_general(
            jnp.concatenate(windows, axis=0).astype(jnp.bfloat16), jnp.concatenate(tables, axis=1),
            (((1,), (0,)), ((), ())), preferred_element_type=jnp.float32,
        )
        height = comps * REACH_Z
        tiles, fresh = [], []
        for i, (_, _, rows) in enumerate((one, two)):
            weight_z, main, rest = weights[i]
            mine = seen[i * height : (i + 1) * height, i * LANES : (i + 1) * LANES]
            tile, push = stepped(mine, weight_z, rows)
            tiles.append(tile)
            unused = jnp.zeros((LANES - comps * SPREAD, LANES), jnp.float32)
            spread = jnp.concatenate([main] * comps + [unused] + [rest] * comps + [unused], axis=0)
            fresh.append((push.astype(jnp.bfloat16), spread.astype(jnp.bfloat16)))
        return tiles, fresh

    def shared(push, spread):
        shares = lax.dot_general(push, spread, (((1,), (1,)), ((), ())), preferred_element_type=jnp.float32)
        height = comps * REACH_Z
        total = shares[:height, :LANES] + shares[:height, LANES:] + shares[height:, :LANES]
        result = jnp.zeros((REACH_Z, LANES), jnp.float32)
        for c in range(comps):
            inside = (lanes >= c * SPREAD) & (lanes < (c + 1) * SPREAD)
            result = jnp.where(inside, total[c * REACH_Z : (c + 1) * REACH_Z], result)
        return result

    def add(deposit_ref, at, shares):
        spots = []
        for u in range(len(shares)):
            _, pair, brick_z = place_of(at + u)
            spots.append(pl.ds(pl.multiple_of(pair * rows_z + brick_z * BZ, 8), REACH_Z))
        for spot, share in zip(spots, shares):
            deposit_ref[spot] = deposit_ref[spot] + share

    def group_of(taken):
        tiles, fresh = [], []
        for u in range(0, UNROLL, 2):
            both, kept = gathered(taken[u], taken[u + 1])
            tiles.extend(both)
            fresh.extend(kept)
        return tiles, fresh

    def keep(state_ref, taken, tiles):
        for (k, _, _), tile in zip(taken, tiles):
            state_ref[pl.ds(pl.multiple_of(STATE * k, STATE), STATE)] = tile

    def deposits_of(kept):
        return [shared(push, spread) for push, spread in kept]

    return loaded, group_of, keep, deposits_of, add


def groups_in(list_ref, late):
    room = (list_ref.shape[0] - 2) // 2
    return late * room, (list_ref[2 * room + late] + UNROLL - 1) // UNROLL


def gather_kernel(dims, list_ref, brick_ref, lines_ref, table_ref, state_ref, push_ref, spread_ref):
    loaded, group_of, keep, _, _ = block_steps(dims, list_ref, brick_ref)
    base, groups = groups_in(list_ref, 0)

    @pl.loop(0, groups)
    def _(group):
        taken = [loaded(base + group * UNROLL + u, lines_ref, table_ref) for u in range(UNROLL)]
        tiles, fresh = group_of(taken)
        keep(state_ref, taken, tiles)
        for i, (push, spread) in enumerate(fresh):
            push_ref[group * UNROLL + i] = push
            spread_ref[group * UNROLL + i] = spread


def deposit_kernel(dims, list_ref, brick_ref, push_ref, spread_ref, deposit_in_ref, deposit_ref):
    _, _, _, deposits_of, add = block_steps(dims, list_ref, brick_ref)
    base, groups = groups_in(list_ref, 0)

    @pl.loop(0, groups)
    def _(group):
        mine = [group * UNROLL + i for i in range(UNROLL)]
        add(deposit_ref, base + group * UNROLL, deposits_of([(push_ref[i], spread_ref[i]) for i in mine]))


def late_kernel(
    dims, slots, list_ref, brick_ref, crossing_ref, lines_ref, table_ref, state_in_ref, deposit_in_ref,
    state_ref, deposit_ref, leaving_ref, push_ref, spread_ref,
):
    loaded, group_of, keep, deposits_of, add = block_steps(dims, list_ref, brick_ref)
    base, groups = groups_in(list_ref, 1)
    push_ref[...] = jnp.zeros_like(push_ref)
    spread_ref[...] = jnp.zeros_like(spread_ref)

    @pl.loop(0, groups + 1)
    def _(group):
        now = base + jnp.maximum(jnp.minimum(group, groups - 1), 0) * UNROLL
        before = base + jnp.maximum(group - 1, 0) * UNROLL
        taken = [loaded(now + u, lines_ref, table_ref) for u in range(UNROLL)]
        shares = deposits_of([(push_ref[i], spread_ref[i]) for i in range(UNROLL)])
        tiles, fresh = group_of(taken)
        add(deposit_ref, before, shares)
        keep(state_ref, taken, tiles)
        for i, (push, spread) in enumerate(fresh):
            push_ref[i] = push
            spread_ref[i] = spread

    rows = leaving_ref.shape[0] // (6 * slots)
    for face in range(6):
        tiles = []
        for slot in range(slots):
            block = crossing_ref[face, slot]
            spot = pl.ds(pl.multiple_of(jnp.maximum(block, 0) * STATE, STATE), STATE)
            live = jnp.full((STATE, LANES), block, jnp.int32) >= 0
            tiles.append(jnp.where(live, state_ref[spot], 0.0))
        for slot, tile in enumerate(tiles):
            leaving_ref[pl.ds(face * rows * slots + slot, rows, stride=slots)] = tile[:rows]


def top_rows(deposit_ref, q, count_x, count_y, rows_z, size_z):
    total = None
    for p in range(count_x):
        at = (p * count_y + q) * rows_z + size_z
        value = pltpu.roll(deposit_ref[at : at + 8], p, 0) if p else deposit_ref[at : at + 8]
        total = value if total is None else total + value
    return total


def send_y_kernel(push, diffuse, leaving_ref, grid_ref, deposit_ref, y_ref, tiles_ref, lines_ref):
    comps, size_x, size_y, size_z = grid_ref.shape[0], grid_ref.shape[1] - 2, grid_ref.shape[2] - 8, grid_ref.shape[3]
    count_x, count_y = size_x // BX, size_y // BY
    rows_z = size_z + 8
    rows = leaving_ref.shape[1]
    height = comps * SPREAD
    for p in range(count_x):
        at = (p * count_y + count_y - 1) * rows_z
        tiles_ref[p * height : (p + 1) * height] = jnp.transpose(deposit_ref[at : at + size_z])[:height]
    first = jnp.full((rows, LANES), odd("gy")) == 0
    y_ref[0, 0:rows] = jnp.where(first, leaving_ref[2], leaving_ref[3])
    y_ref[1, 0:rows] = jnp.where(first, leaving_ref[3], leaving_ref[2])
    lines_ref[...] = jnp.zeros_like(lines_ref)
    for c in range(comps):
        for p in range(count_x):
            spot = slice(c * ROWS_Y + p * BX, c * ROWS_Y + p * BX + REACH_X)
            line = tiles_ref[pl.ds(p * height + c * SPREAD + BY, REACH_X, stride=REACH_Y)]
            lines_ref[spot] = lines_ref[spot] + line
    wrapped = top_rows(deposit_ref, count_y - 1, count_x, count_y, rows_z, size_z)
    lane = lane_ids(8)
    packed = jnp.zeros((8, LANES), jnp.float32)
    for c in range(comps):
        spot = slice(c * ROWS_Y, (c + 1) * ROWS_Y)
        beside = jnp.concatenate([grid_ref[c, 1 : size_x + 1, size_y - 1], jnp.zeros((8, LANES), jnp.float32)], axis=0)
        line = push * lines_ref[spot] + diffuse * beside
        y_ref[0, rows + c * ROWS_Y : rows + (c + 1) * ROWS_Y] = line
        y_ref[1, rows + c * ROWS_Y : rows + (c + 1) * ROWS_Y] = line
        for a in range(REACH_X):
            place = PACK * c + a
            value = turned(wrapped, place - c * SPREAD - a * REACH_Y - BY)
            packed = packed + jnp.where(lane == place, value, 0.0)
    corner = packed[0:1]
    for p in range(1, count_x):
        corner = corner + turned(packed[p : p + 1], p * BX)
    at = rows + size_x + 1
    y_ref[0, at : at + 1] = push * corner
    y_ref[1, at : at + 1] = push * corner


def merge_kernel(deposit_ref, top_tiles_ref, plane_ref, face_ref, tiles_ref, turned_ref):
    comps, planes = plane_ref.shape[:2]
    count_x, size_z = (planes - 1) // BX, plane_ref.shape[3]
    rows_z = size_z + 8
    count_y = deposit_ref.shape[0] // (rows_z * count_x)
    height = comps * SPREAD
    for p in range(count_x):
        for q in range(count_y - 1):
            at = p * count_y + q
            value = jnp.transpose(deposit_ref[at * rows_z : at * rows_z + size_z])
            tiles_ref[at * height : (at + 1) * height] = value[:height]
    top = row_ids(REACH_Y) >= BY
    for c in range(comps):
        for x in range(planes):
            bricks = [(x // BX, x % BX)] if x < planes - 1 else []
            if x and x % BX == 0:
                bricks.append((x // BX - 1, BX))

            def tile(q):
                total = None
                for p, a in bricks:
                    at = c * SPREAD + a * REACH_Y
                    if q < count_y - 1:
                        value = tiles_ref[(p * count_y + q) * height + at : (p * count_y + q) * height + at + REACH_Y]
                    else:
                        value = top_tiles_ref[p * height + at : p * height + at + REACH_Y]
                    total = value if total is None else total + value
                return total

            carried = None
            for q in range(0, count_y, 2):
                here = tile(q)
                if carried is not None:
                    here = here + carried
                between = pltpu.roll(tile(q + 1), BY, 0)
                here = here + jnp.where(top, between, 0.0)
                carried = jnp.where(top, 0.0, between)
                plane_ref[c, x, q * BY : q * BY + REACH_Y] = here
            plane_ref[c, x, count_y * BY :] = carried

    lane = lane_ids(count_x)
    turned_ref[...] = jnp.zeros_like(turned_ref)
    for q in range(count_y):
        wrapped = top_rows(deposit_ref, q, count_x, count_y, rows_z, size_z)[:count_x]
        within = (lane >= q * BY) & (lane <= (q + 1) * BY)
        for c in range(comps):
            for a in range(REACH_X):
                value = turned(wrapped, q * BY - c * SPREAD - a * REACH_Y)
                spot = pl.ds(PACK * c + a, count_x, stride=BX)
                turned_ref[spot] = turned_ref[spot] + jnp.where(within, value, 0.0)
    face_ref[...] = jnp.transpose(turned_ref[...])[: face_ref.shape[0]]


def send_xz_kernel(push, diffuse, grid_ref, deposit_ref, face_ref, x_ref, z_ref):
    comps, size_x = grid_ref.shape[0], grid_ref.shape[1] - 2
    size_y = z_ref.shape[0]
    lane = lane_ids(size_y)
    packed = push * face_ref[0:size_y]
    for c in range(comps):
        for x in range(size_x):
            place = PACK * c + x
            packed = packed + jnp.where(lane == place, diffuse * turned(grid_ref[c, x + 1, 0:size_y], place + 1), 0.0)
        total = push * deposit_ref[c, size_x, 0:size_y]
        x_ref[c * size_y : (c + 1) * size_y] = diffuse * grid_ref[c, size_x, 0:size_y] + total
    z_ref[...] = packed


def base_kernel(push, diffuse, count, grid_ref, deposit_ref, top_ref, y1_ref, y2_ref, state_ref, base_ref, velocity_ref):
    comps, size_x, size_y, size_z = base_ref.shape
    lane, sub = lane_ids(size_y), row_ids(size_y)
    top = top_ref[0:size_y]
    for c in range(comps):
        at = count + c * ROWS_Y
        lines = below(y1_ref, y2_ref, slice(at, at + size_x))
        for x in range(size_x):
            here = grid_ref[c, x + 1, 0:size_y]
            before = jnp.where(sub == 0, 0.0, pltpu.roll(here, 1, 0))
            laplace = grid_ref[c, x, 0:size_y] + grid_ref[c, x + 2, 0:size_y]
            laplace = laplace + grid_ref[c, x + 1, 1 : size_y + 1] + before
            ahead = jnp.where(lane == size_z - 1, turned(top, size_z - 1 - (PACK * c + x)), turned(here, -1))
            laplace = laplace + ahead + jnp.where(lane == 0, 0.0, turned(here, 1)) - 6.0 * here
            total = here + diffuse * laplace + push * deposit_ref[c, x, 0:size_y]
            line = jnp.broadcast_to(lines[x : x + 1], (size_y, LANES))
            base_ref[c, x] = total + jnp.where(sub == 0, line, 0.0)
        velocity_ref[c] = state_ref[pl.ds(c, velocity_ref.shape[1], stride=STATE)]


def below(first_ref, second_ref, rows):
    got = jnp.where(jnp.full((1, LANES), odd("gy")) == 1, first_ref[rows], second_ref[rows])
    return jnp.where(jnp.full((1, LANES), lax.axis_index("gy")) != 0, got, 0.0)


def relay_kernel(size_x, size_y, comps, count, first_ref, second_ref, x_in_ref, z_in_ref, leaving_ref, x_ref, z_ref, edge_ref):
    edge = comps * size_y
    x_ref[0:edge] = x_in_ref[...]
    for c in range(comps):
        at = count + c * ROWS_Y + size_x
        spot = slice(c * size_y, c * size_y + 1)
        x_ref[spot] = x_in_ref[spot] + below(first_ref, second_ref, slice(at, at + 1))
    x_ref[edge : edge + count] = leaving_ref[0]
    if x_ref.shape[0] > edge + count:
        x_ref[edge + count : edge + 2 * count] = leaving_ref[1]
    at = count + size_x + 1
    edge_ref[...] = z_in_ref[...]
    edge_ref[0:1] = z_in_ref[0:1] + below(first_ref, second_ref, slice(at, at + 1))
    up = odd("gz")
    z_ref[up, 0:count] = leaving_ref[4]
    z_ref[up, count : count + size_y] = edge_ref[...]
    z_ref[1 - up, 0:count] = leaving_ref[5]
    z_ref[1 - up, count : count + size_y] = jnp.zeros((size_y, LANES), jnp.float32)


def finish_kernel(
    count, base_ref, y1_ref, y2_ref, x_ref, minus_x_ref, z1_ref, z2_ref, edge_ref, gas_ref, arrivals_ref,
):
    comps, size_x, size_y, _ = base_ref.shape
    first_lane = lane_ids(size_y) == 0
    odd_y, odd_z = jnp.full((1, LANES), odd("gy")) == 1, jnp.full((1, LANES), odd("gz")) == 1
    place = jnp.full((1, LANES), lax.axis_index("gy"))
    lower, upper = place != 0, place != lax.axis_size("gy") - 1
    rows = slice(count, count + size_y)
    face = jnp.where(odd_z, z1_ref[rows], z2_ref[rows])
    corner = edge_ref[...]
    for c in range(comps):
        for x in range(size_x):
            total = base_ref[c, x]
            far = turned(face, -(PACK * c + x))
            if x == 0:
                total = total + x_ref[c * size_y : (c + 1) * size_y]
                far = far + turned(corner, -(PACK * c + size_x))
            gas_ref[c, x] = total + jnp.where(first_lane, far, 0.0)

    slots = arrivals_ref.shape[2]
    for i in range(arrivals_ref.shape[1]):

        def rows_of(ref, at=0):
            return ref[at + i * slots : at + (i + 1) * slots]

        arrivals_ref[0, i] = rows_of(x_ref, comps * size_y)
        arrivals_ref[1, i] = rows_of(minus_x_ref, minus_x_ref.shape[0] - count)
        y1, y2 = rows_of(y1_ref), rows_of(y2_ref)
        arrivals_ref[2, i] = jnp.where(lower, jnp.where(odd_y, y1, y2), 0.0)
        arrivals_ref[3, i] = jnp.where(upper, jnp.where(odd_y, y2, y1), 0.0)
        z1, z2 = rows_of(z1_ref), rows_of(z2_ref)
        arrivals_ref[4, i] = jnp.where(odd_z, z1, z2)
        arrivals_ref[5, i] = jnp.where(odd_z, z2, z1)


def per_device(gas_field, velocity, fraction, response, cell_index, brick_index, crossing):
    comps, size_x, size_y, size_z = gas_field.shape
    nblocks = velocity.shape[0]
    loading = 0.5 * size_x * size_y * size_z / (nblocks * 128)
    push, diffuse = -TIME_STEP * loading, TIME_STEP * VISCOSITY
    velocity = jnp.transpose(velocity, (1, 0, 2))
    fraction = jnp.transpose(fraction, (1, 0, 2))
    spare = nblocks + 8
    rows_z = size_z + 8
    grid_shape = (comps, size_x + 2, ROWS_Y, LANES)
    lines_shape = ((size_x // BX) * (size_y // BY) * comps * rows_z, LANES)
    deposit_shape = ((size_x // BX) * (size_y // BY) * rows_z, LANES)

    inputs = (gas_field, velocity, fraction, response, cell_index, brick_index, crossing)
    inputs = [pltpu.with_memory_space_constraint(array, pltpu.HBM) for array in inputs]
    grid, face, plane, velocity, fraction, response, cell_index, brick_index, crossing = call(
        begin_kernel,
        [grid_shape, (size_y, LANES), (comps * size_y, LANES)]
        + [jax.ShapeDtypeStruct(array.shape, array.dtype) for array in inputs[1:]],
        *inputs, hbm=range(7), scratch=(pltpu.SemaphoreType.DMA((7,)),), limit=40,
    )
    from_z = moved_along(face, "gz", -1)
    from_x = moved_along(plane, "gx", -1)
    from_xz = moved_diagonally(face, -1)
    lines, deposit, table, ready, blocks = call(
        prepare_kernel,
        [
            lines_shape,
            deposit_shape,
            (TABLE_ROWS * spare, LANES),
            (8, LANES),
            jax.ShapeDtypeStruct((2 * (nblocks + UNROLL) + 2,), jnp.int32),
        ],
        grid, velocity, fraction, response, cell_index, brick_index,
        smem=(5,), smem_outs=(4,), cycles=3000,
    )
    line_rows = -(-(comps * size_x + comps + 1) // 8) * 8
    (y_lines,) = call(y_lines_kernel, [(line_rows, LANES)], grid, from_z, from_x, from_xz, ready)
    y1, y2 = swapped_y((y_lines, y_lines))
    square = pltpu.VMEM((LANES, LANES), jnp.float32)
    grid, lines, top = call(
        halo_xz_kernel, [grid_shape, lines_shape, (LANES, LANES)], grid, lines, from_z, from_x, from_xz,
        aliases={0: 0, 1: 1}, scratch=(square,), cycles=1000,
    )

    dims = (comps, size_x // BX, size_y // BY, size_z // BZ, rows_z)
    slots = crossing.shape[1]
    count = 7 * slots

    def parts(many):
        return [(many, 2 * comps * REACH_Z, LANES), (many, 2 * LANES, LANES)]

    state, push_parts, spread_parts = call(
        functools.partial(gather_kernel, dims),
        [(STATE * spare, LANES)]
        + [jax.ShapeDtypeStruct(shape, jnp.bfloat16) for shape in parts(nblocks + UNROLL)],
        blocks, brick_index, lines, table, smem=(0, 1), cycles=4000,
    )
    grid, lines = call(
        functools.partial(halo_y_kernel, size_y), [grid_shape, lines_shape], grid, lines, top, y1, y2,
        aliases={0: 0, 1: 1}, scratch=(square,), cycles=1000,
    )
    state, deposit, leaving = call(
        functools.partial(late_kernel, dims, slots),
        [(STATE * spare, LANES), deposit_shape, (6 * count, LANES)],
        blocks, brick_index, crossing, lines, table, state, deposit,
        smem=(0, 1, 2), aliases={5: 0, 6: 1}, cycles=2000,
        scratch=[pltpu.VMEM(shape, jnp.bfloat16) for shape in parts(UNROLL)],
    )
    leaving = leaving.reshape(6, count, LANES)
    height = comps * SPREAD
    to_y, top_tiles = call(
        functools.partial(send_y_kernel, push, diffuse),
        [(2, count + comps * ROWS_Y, LANES), ((size_x // BX) * height, LANES)],
        leaving, grid, deposit, cycles=300, scratch=(pltpu.VMEM((comps * ROWS_Y, LANES), jnp.float32),),
    )
    y1, y2 = swapped_y((to_y[0], to_y[1]))
    (deposit,) = call(
        functools.partial(deposit_kernel, dims), [deposit_shape], blocks, brick_index, push_parts, spread_parts, deposit,
        smem=(0, 1), aliases={4: 0}, cycles=4000,
    )
    deposit, over = call(
        merge_kernel, [(comps, size_x + 1, ROWS_Y, LANES), (ROWS_Y, LANES)], deposit, top_tiles,
        cycles=1000, scratch=(pltpu.VMEM(((size_x // BX) * (size_y // BY) * height, LANES), jnp.float32), square),
    )
    to_x, to_z = call(
        functools.partial(send_xz_kernel, push, diffuse), [(comps * size_y, LANES), (size_y, LANES)],
        grid, deposit, over, cycles=500,
    )
    base, velocity_next = call(
        functools.partial(base_kernel, push, diffuse, count), [gas_field.shape, (comps, nblocks, LANES)],
        grid, deposit, top, y1, y2, state, cycles=1000,
    )
    edge = comps * size_y
    both = lax.axis_size("gx") == 2
    to_x, to_z, to_xz = call(
        functools.partial(relay_kernel, size_x, size_y, comps, count),
        [(edge + (2 if both else 1) * count, LANES), (2, count + size_y, LANES), (size_y, LANES)],
        y1, y2, to_x, to_z, leaving,
    )
    got_x = moved_along(to_x, "gx", 1)
    z1, z2 = swapped_z((to_z[0], to_z[1]))
    got_xz = moved_diagonally(to_xz, 1)
    got_mx = got_x if both else moved_along(leaving[1], "gx", -1)
    gas_next, arrivals = call(
        functools.partial(finish_kernel, count), [gas_field.shape, (6, 7, slots, LANES)],
        base, y1, y2, got_x, got_mx, z1, z2, got_xz,
    )
    return gas_next, jnp.transpose(velocity_next, (1, 0, 2)), jnp.transpose(arrivals, (0, 2, 1, 3))


def solution(mesh):
    owner = ("gx", "gz", "gy")
    in_specs = (
        P(None, "gx", "gy", "gz"),
        P(owner, None, None),
        P(owner, None, None),
        P(owner, None),
        P(owner, None),
        P(owner),
        P(owner, None),
    )
    out_specs = (
        P(None, "gx", "gy", "gz"),
        P(owner, None, None),
        P(owner, None, None, None),
    )
    return jax.shard_map(
        per_device, mesh=mesh, in_specs=in_specs, out_specs=out_specs, check_vma=False
    )
```

```python
import functools

import jax
import jax.numpy as jnp
from jax import lax
from jax.experimental import pallas as pl
from jax.experimental.pallas import tpu as pltpu
from jax.sharding import PartitionSpec as P

BX = 4
BY = 4
BZ = 8

TIME_STEP = 0.25
VISCOSITY = 0.4

LANES = 128
PACK = 32
ROWS_Y = 24
REACH_X = BX + 1
REACH_Y = 8
SPREAD = REACH_X * REACH_Y
REACH_Z = 2 * BZ
UNROLL = 8

WEIGHT, ALONG_Y, IN_Y, ALONG_Z, IN_Z, RESPONSE, MOVING, OFFSET = 0, 5, 6, 7, 8, 9, 10, 13
TABLE_ROWS = 16
STATE = 8

VMEM = pl.BlockSpec(memory_space=pltpu.VMEM)
SMEM = pl.BlockSpec(memory_space=pltpu.SMEM)
HBM = pl.BlockSpec(memory_space=pltpu.HBM)


def moved_along(block, axis, distance):
    count = lax.axis_size(axis)
    return lax.ppermute(block, axis, [(i, (i + distance) % count) for i in range(count)])


def swapped_z(blocks):
    count = lax.axis_size("gz")
    first = [(i, i ^ 1) for i in range(count)]
    second = [(i, (((i + 1) ^ 1) - 1) % count) for i in range(count)]
    return lax.ppermute(blocks[0], "gz", first), lax.ppermute(blocks[1], "gz", second)


def swapped_y(blocks):
    nz, ny = lax.axis_size("gz"), lax.axis_size("gy")
    first = [(j, j ^ 1) for j in range(ny)]
    second = []
    for k in range(nz):
        second.append((k * ny, (k ^ 1) * ny))
        second.append((k * ny + ny - 1, (k ^ 1) * ny + ny - 1))
        second.extend((k * ny + j, k * ny + ((j + 1) ^ 1) - 1) for j in range(1, ny - 1))
    return lax.ppermute(blocks[0], "gy", first), lax.ppermute(blocks[1], ("gz", "gy"), second)


def moved_diagonally(block, distance):
    nx, nz = lax.axis_size("gx"), lax.axis_size("gz")
    route = [(i * nz + k, (i + distance) % nx * nz + (k + distance) % nz) for i in range(nx) for k in range(nz)]
    return lax.ppermute(block, ("gx", "gz"), route)


def call(body, outs, *operands, smem=(), hbm=(), smem_outs=(), scratch=(), aliases=None, cycles=0, limit=40):
    return pl.pallas_call(
        body,
        out_shape=[o if isinstance(o, jax.ShapeDtypeStruct) else jax.ShapeDtypeStruct(o, jnp.float32) for o in outs],
        in_specs=[SMEM if i in smem else HBM if i in hbm else VMEM for i in range(len(operands))],
        out_specs=[SMEM if i in smem_outs else VMEM for i in range(len(outs))],
        scratch_shapes=list(scratch),
        input_output_aliases=aliases or {},
        compiler_params=pltpu.CompilerParams(vmem_limit_bytes=limit * 1024 * 1024),
        cost_estimate=pl.CostEstimate(flops=cycles * 4096, bytes_accessed=cycles * 1024, transcendentals=0),
    )(*operands)


def lane_ids(rows):
    return lax.broadcasted_iota(jnp.int32, (rows, LANES), 1)


def row_ids(rows):
    return lax.broadcasted_iota(jnp.int32, (rows, LANES), 0)


def turned(value, shift):
    shift = shift % LANES
    return pltpu.roll(value, shift, 1) if shift else value


def odd(axis):
    return lax.axis_index(axis) % 2


def begin_kernel(
    gas_ref, velocity_in, fraction_in, response_in, cell_in, brick_in, crossing_in,
    grid_ref, face_ref, plane_ref, velocity_ref, fraction_ref, response_ref, cell_ref, brick_ref, crossing_ref, sems,
):
    comps, size_x, size_y, _ = gas_ref.shape
    pairs = [
        (gas_ref, grid_ref.at[:, 1 : size_x + 1, 0:size_y]),
        (velocity_in, velocity_ref), (fraction_in, fraction_ref), (response_in, response_ref),
        (cell_in, cell_ref), (brick_in, brick_ref), (crossing_in, crossing_ref),
    ]
    copies = [pltpu.make_async_copy(source, target, sems.at[i]) for i, (source, target) in enumerate(pairs)]
    for copy in copies:
        copy.start()
    zeros = jnp.zeros((ROWS_Y, LANES), jnp.float32)
    for c in range(comps):
        grid_ref[c, 0] = zeros
        grid_ref[c, size_x + 1] = zeros
        for x in range(size_x):
            grid_ref[c, x + 1, size_y:] = zeros[size_y:]
    copies[0].wait()
    lane = lane_ids(size_y)
    face = jnp.zeros((size_y, LANES), jnp.float32)
    for c in range(comps):
        plane_ref[c * size_y : (c + 1) * size_y] = grid_ref[c, 1, 0:size_y]
        for x in range(size_x):
            place = PACK * c + x
            face = jnp.where(lane == place, turned(grid_ref[c, x + 1, 0:size_y], place), face)
    face_ref[...] = face
    for copy in copies[1:]:
        copy.wait()


def parts_of(value):
    main = value.astype(jnp.bfloat16).astype(jnp.float32)
    return main, value - main


def lay_out(grid_ref, lines_ref, p, q, size_y, size_z):
    comps = grid_ref.shape[0]
    rows_z = size_z + 8
    count_y = size_y // BY
    for c in range(comps):
        planes = [grid_ref[c, p * BX + a + 1, q * BY : q * BY + REACH_Y] for a in range(REACH_X)]
        main, rest = parts_of(jnp.concatenate(planes, axis=0))
        stack = jnp.concatenate([main, rest, main, jnp.zeros((LANES - 3 * SPREAD, LANES), jnp.float32)], axis=0)
        at = ((p * count_y + q) * comps + c) * rows_z
        lines_ref[at : at + size_z] = jnp.transpose(stack)


def lay_out_top(turned_ref, lines_ref, q, comps, count_x, count_y, size_z):
    lane = lane_ids(count_x)
    rows_z = size_z + 8
    for c in range(comps):
        total = jnp.zeros((count_x, LANES), jnp.float32)
        for a in range(REACH_X):
            rows = turned_ref[pl.ds(PACK * c + a, count_x, stride=BX)]
            total = jnp.where(lane // REACH_Y == a, turned(rows, a * REACH_Y - q * BY), total)
        main, rest = parts_of(total)
        line = main + turned(rest, SPREAD) + turned(main, 2 * SPREAD)
        for p in range(count_x):
            at = ((p * count_y + q) * comps + c) * rows_z + size_z
            lines_ref[at : at + 1] = line[p : p + 1]


def prepare_kernel(
    grid_ref, velocity_ref, fraction_ref, response_ref, cell_ref, brick_ref,
    lines_ref, deposit_ref, table_ref, ready_ref, list_ref,
):
    comps, size_x, size_y, size_z = grid_ref.shape[0], grid_ref.shape[1] - 2, grid_ref.shape[2] - 8, grid_ref.shape[3]
    nblocks = velocity_ref.shape[1]
    count_x, count_y, count_z = size_x // BX, size_y // BY, size_z // BZ
    rows_z = size_z + 8

    room = nblocks + UNROLL

    def visit(k, counts):
        late = jnp.where(lax.rem(lax.div(brick_ref[k], count_z), count_y) == count_y - 1, 1, 0)
        list_ref[jnp.where(late == 1, room + counts[1], counts[0])] = k
        return counts[0] + 1 - late, counts[1] + late

    early, late = lax.fori_loop(0, nblocks, visit, (jnp.int32(0), jnp.int32(0)), unroll=8)
    for base, count in ((0, early), (room, late)):
        for u in range(UNROLL):
            list_ref[base + count + u] = nblocks
    list_ref[2 * room] = early
    list_ref[2 * room + 1] = late
    ready_ref[...] = jnp.zeros_like(ready_ref)

    deposit_ref[...] = jnp.zeros_like(deposit_ref)
    for p in range(count_x):
        for q in range(count_y):
            for c in range(comps):
                at = ((p * count_y + q) * comps + c) * rows_z + size_z
                lines_ref[at : at + 8] = jnp.zeros((8, LANES), jnp.float32)
    for p in range(count_x - 1):
        for q in range(count_y - 1):
            lay_out(grid_ref, lines_ref, p, q, size_y, size_z)

    cells = cell_ref[...]
    cell_x, cell_y, cell_z = cells // (BY * BZ), cells // BZ % BY, cells % BZ
    along_x = fraction_ref[0]

    def put(row, value):
        table_ref[pl.ds(row, nblocks, stride=TABLE_ROWS)] = value

    for a in range(REACH_X):
        put(WEIGHT + a, jnp.where(cell_x == a, 1.0 - along_x, 0.0) + jnp.where(cell_x == a - 1, along_x, 0.0))
    put(ALONG_Y, fraction_ref[1])
    put(IN_Y, cell_y.astype(jnp.float32))
    put(ALONG_Z, fraction_ref[2])
    put(IN_Z, cell_z.astype(jnp.float32))
    put(RESPONSE, response_ref[...])
    for c in range(comps):
        put(MOVING + c, velocity_ref[c])
        put(OFFSET + c, fraction_ref[c])
    spare = table_ref.shape[0] - nblocks * TABLE_ROWS
    row = row_ids(spare)
    table_ref[nblocks * TABLE_ROWS :] = jnp.where(row % TABLE_ROWS == RESPONSE, 1.0, 0.0)


def y_lines_kernel(grid_ref, face_ref, from_x_ref, edge_ref, ready_ref, out_ref):
    comps, size_x = grid_ref.shape[0], grid_ref.shape[1] - 2
    size_y = face_ref.shape[0]
    for c in range(comps):
        out_ref[c * size_x : (c + 1) * size_x] = grid_ref[c, 1 : size_x + 1, 0]
        out_ref[comps * size_x + c : comps * size_x + c + 1] = from_x_ref[c * size_y : c * size_y + 1]
    line = jnp.where(lane_ids(8) % PACK == size_x, turned(edge_ref[0:8], size_x), face_ref[0:8])
    out_ref[comps * size_x + comps : comps * size_x + comps + 1] = line[0:1]


def halo_xz_kernel(grid_in_ref, lines_in_ref, face_ref, from_x_ref, edge_ref, grid_ref, lines_ref, top_ref, turned_ref):
    comps, size_x = grid_ref.shape[0], grid_ref.shape[1] - 2
    size_y, size_z = face_ref.shape[0], grid_ref.shape[3]
    count_x, count_y = size_x // BX, size_y // BY
    for c in range(comps):
        grid_ref[c, size_x + 1, 0:size_y] = from_x_ref[c * size_y : (c + 1) * size_y]
    for q in range(count_y - 1):
        lay_out(grid_ref, lines_ref, count_x - 1, q, size_y, size_z)
    top = jnp.where(lane_ids(size_y) % PACK == size_x, turned(edge_ref[...], size_x), face_ref[...])
    top_ref[0:size_y] = top
    top_ref[size_y:] = jnp.zeros((LANES - size_y, LANES), jnp.float32)
    turned_ref[...] = jnp.transpose(top_ref[...])
    for q in range(count_y - 1):
        lay_out_top(turned_ref, lines_ref, q, comps, count_x, count_y, size_z)


def halo_y_kernel(size_y, grid_in_ref, lines_in_ref, top_in_ref, first_ref, second_ref, grid_ref, lines_ref, turned_ref):
    comps, size_x, size_z = grid_ref.shape[0], grid_ref.shape[1] - 2, grid_ref.shape[3]
    count_x, count_y = size_x // BX, size_y // BY
    inside = lax.axis_index("gy") != lax.axis_size("gy") - 1
    kept = (row_ids(8) == 0) & inside
    even = jnp.full((1, LANES), odd("gy")) == 0

    def line_at(row):
        line = jnp.where(even, first_ref[row : row + 1], second_ref[row : row + 1])
        return jnp.where(kept, jnp.broadcast_to(line, (8, LANES)), 0.0)

    for c in range(comps):
        for x in range(size_x + 1):
            grid_ref[c, x + 1, size_y:] = line_at(c * size_x + x if x < size_x else comps * size_x + c)
    for p in range(count_x):
        lay_out(grid_ref, lines_ref, p, count_y - 1, size_y, size_z)
    corner = line_at(comps * size_x + comps)
    rest = jnp.zeros((LANES - size_y - 8, LANES), jnp.float32)
    turned_ref[...] = jnp.transpose(jnp.concatenate([top_in_ref[0:size_y], corner, rest], axis=0))
    lay_out_top(turned_ref, lines_ref, count_y - 1, comps, count_x, count_y, size_z)


def block_steps(dims, list_ref, brick_ref):
    comps, _, count_y, count_z, rows_z = dims
    nblocks = brick_ref.shape[0]
    sub = row_ids(8)
    row_y = row_ids(REACH_Y).astype(jnp.float32)
    row_z = row_ids(REACH_Z).astype(jnp.float32)
    lanes = lane_ids(REACH_Z)

    def hat(rows, inside, along):
        return jnp.where(rows == inside, 1.0 - along, 0.0) + jnp.where(rows == inside + 1.0, along, 0.0)

    def place_of(at):
        k = list_ref[at]
        brick = jnp.where(k < nblocks, brick_ref[jnp.minimum(k, nblocks - 1)], 0)
        brick_x = lax.div(brick, count_y * count_z)
        brick_y = lax.rem(lax.div(brick, count_z), count_y)
        return k, brick_x * count_y + brick_y, lax.rem(brick, count_z)

    def loaded(at, lines_ref, table_ref):
        k, pair, brick_z = place_of(at)
        first = pl.multiple_of(pair * comps * rows_z + brick_z * BZ, 8)
        window = jnp.concatenate([lines_ref[pl.ds(first + c * rows_z, REACH_Z)] for c in range(comps)], axis=0)
        table = table_ref[pl.ds(pl.multiple_of(k * TABLE_ROWS, TABLE_ROWS), TABLE_ROWS)]
        return k, window, [table[i : i + 1] for i in range(TABLE_ROWS)]

    def weighted(rows):
        weight_y = hat(row_y, rows[IN_Y], rows[ALONG_Y])
        weight_z = hat(row_z, rows[IN_Z], rows[ALONG_Z])
        weight = jnp.concatenate([rows[WEIGHT + a] * weight_y for a in range(REACH_X)], axis=0)
        return weight_z, *parts_of(weight)

    def stepped(seen, weight_z, rows):
        rate = 1.0 / rows[RESPONSE]
        state, moved, pushed = [], [], []
        for c in range(comps):
            gas_sample = jnp.sum(seen[c * REACH_Z : (c + 1) * REACH_Z] * weight_z, axis=0, keepdims=True)
            drag = (gas_sample - rows[MOVING + c]) * rate
            state.append(rows[MOVING + c] + TIME_STEP * drag)
            moved.append(rows[OFFSET + c] + TIME_STEP * state[c])
            pushed.append(drag * weight_z)
        tile = jnp.broadcast_to(rows[RESPONSE], (STATE, LANES))
        for i, value in enumerate(state + moved):
            tile = jnp.where(sub == i, value, tile)
        return tile, jnp.concatenate(parts_of(jnp.concatenate(pushed, axis=0)), axis=0)

    def gathered(one, two):
        tables, windows, weights = [], [], []
        for _, window, rows in (one, two):
            weight_z, main, rest = weighted(rows)
            weights.append((weight_z, main, rest))
            unused = jnp.zeros((LANES - 3 * SPREAD, LANES), jnp.float32)
            tables.append(jnp.concatenate([main, main, rest, unused], axis=0).astype(jnp.bfloat16))
            windows.append(window)
        seen = lax.dot_general(
            jnp.concatenate(windows, axis=0).astype(jnp.bfloat16), jnp.concatenate(tables, axis=1),
            (((1,), (0,)), ((), ())), preferred_element_type=jnp.float32,
        )
        height = comps * REACH_Z
        tiles, fresh = [], []
        for i, (_, _, rows) in enumerate((one, two)):
            weight_z, main, rest = weights[i]
            mine = seen[i * height : (i + 1) * height, i * LANES : (i + 1) * LANES]
            tile, push = stepped(mine, weight_z, rows)
            tiles.append(tile)
            unused = jnp.zeros((LANES - comps * SPREAD, LANES), jnp.float32)
            spread = jnp.concatenate([main] * comps + [unused] + [rest] * comps + [unused], axis=0)
            fresh.append((push.astype(jnp.bfloat16), spread.astype(jnp.bfloat16)))
        return tiles, fresh

    def shared(push, spread):
        shares = lax.dot_general(push, spread, (((1,), (1,)), ((), ())), preferred_element_type=jnp.float32)
        height = comps * REACH_Z
        total = shares[:height, :LANES] + shares[:height, LANES:] + shares[height:, :LANES]
        result = jnp.zeros((REACH_Z, LANES), jnp.float32)
        for c in range(comps):
            inside = (lanes >= c * SPREAD) & (lanes < (c + 1) * SPREAD)
            result = jnp.where(inside, total[c * REACH_Z : (c + 1) * REACH_Z], result)
        return result

    def add(deposit_ref, at, shares):
        spots = []
        for u in range(len(shares)):
            _, pair, brick_z = place_of(at + u)
            spots.append(pl.ds(pl.multiple_of(pair * rows_z + brick_z * BZ, 8), REACH_Z))
        for spot, share in zip(spots, shares):
            deposit_ref[spot] = deposit_ref[spot] + share

    def group_of(taken):
        tiles, fresh = [], []
        for u in range(0, UNROLL, 2):
            both, kept = gathered(taken[u], taken[u + 1])
            tiles.extend(both)
            fresh.extend(kept)
        return tiles, fresh

    def keep(state_ref, taken, tiles):
        for (k, _, _), tile in zip(taken, tiles):
            state_ref[pl.ds(pl.multiple_of(STATE * k, STATE), STATE)] = tile

    def deposits_of(kept):
        return [shared(push, spread) for push, spread in kept]

    return loaded, group_of, keep, deposits_of, add


def groups_in(list_ref, late):
    room = (list_ref.shape[0] - 2) // 2
    return late * room, (list_ref[2 * room + late] + UNROLL - 1) // UNROLL


def fetched(sems, *pairs):
    copies = [pltpu.make_async_copy(source, target, sems.at[i]) for i, (source, target) in enumerate(pairs)]
    for copy in copies:
        copy.start()
    return copies


def gather_kernel(
    dims, list_in, brick_in, table_ref, grid_in_ref, lines_in_ref, face_ref, from_x_ref, edge_ref,
    state_ref, push_ref, spread_ref, grid_ref, lines_ref, top_ref, list_ref, brick_ref, turned_ref, sems,
):
    copies = fetched(sems, (list_in, list_ref), (brick_in, brick_ref))
    halo_xz_kernel(grid_in_ref, lines_in_ref, face_ref, from_x_ref, edge_ref, grid_ref, lines_ref, top_ref, turned_ref)
    for copy in copies:
        copy.wait()
    loaded, group_of, keep, _, _ = block_steps(dims, list_ref, brick_ref)
    base, groups = groups_in(list_ref, 0)

    @pl.loop(0, groups)
    def _(group):
        taken = [loaded(base + group * UNROLL + u, lines_ref, table_ref) for u in range(UNROLL)]
        tiles, fresh = group_of(taken)
        keep(state_ref, taken, tiles)
        for i, (push, spread) in enumerate(fresh):
            push_ref[group * UNROLL + i] = push
            spread_ref[group * UNROLL + i] = spread


def deposit_kernel(dims, list_ref, brick_ref, push_ref, spread_ref, deposit_in_ref, deposit_ref):
    _, _, _, deposits_of, add = block_steps(dims, list_ref, brick_ref)
    base, groups = groups_in(list_ref, 0)

    @pl.loop(0, groups)
    def _(group):
        mine = [group * UNROLL + i for i in range(UNROLL)]
        add(deposit_ref, base + group * UNROLL, deposits_of([(push_ref[i], spread_ref[i]) for i in mine]))


def late_kernel(
    dims, slots, list_in, brick_in, crossing_in, table_ref, grid_in_ref, lines_in_ref, top_in_ref, first_ref, second_ref,
    state_in_ref, deposit_in_ref,
    grid_ref, lines_ref, state_ref, deposit_ref, leaving_ref,
    push_ref, spread_ref, list_ref, brick_ref, crossing_ref, turned_ref, sems,
):
    copies = fetched(sems, (list_in, list_ref), (brick_in, brick_ref), (crossing_in, crossing_ref))
    halo_y_kernel(
        dims[2] * BY, grid_in_ref, lines_in_ref, top_in_ref, first_ref, second_ref, grid_ref, lines_ref, turned_ref
    )
    for copy in copies:
        copy.wait()
    loaded, group_of, keep, deposits_of, add = block_steps(dims, list_ref, brick_ref)
    base, groups = groups_in(list_ref, 1)
    push_ref[...] = jnp.zeros_like(push_ref)
    spread_ref[...] = jnp.zeros_like(spread_ref)

    @pl.loop(0, groups + 1)
    def _(group):
        now = base + jnp.maximum(jnp.minimum(group, groups - 1), 0) * UNROLL
        before = base + jnp.maximum(group - 1, 0) * UNROLL
        taken = [loaded(now + u, lines_ref, table_ref) for u in range(UNROLL)]
        shares = deposits_of([(push_ref[i], spread_ref[i]) for i in range(UNROLL)])
        tiles, fresh = group_of(taken)
        add(deposit_ref, before, shares)
        keep(state_ref, taken, tiles)
        for i, (push, spread) in enumerate(fresh):
            push_ref[i] = push
            spread_ref[i] = spread

    rows = leaving_ref.shape[0] // (6 * slots)
    for face in range(6):
        tiles = []
        for slot in range(slots):
            block = crossing_ref[face, slot]
            spot = pl.ds(pl.multiple_of(jnp.maximum(block, 0) * STATE, STATE), STATE)
            live = jnp.full((STATE, LANES), block, jnp.int32) >= 0
            tiles.append(jnp.where(live, state_ref[spot], 0.0))
        for slot, tile in enumerate(tiles):
            leaving_ref[pl.ds(face * rows * slots + slot, rows, stride=slots)] = tile[:rows]


def top_rows(deposit_ref, q, count_x, count_y, rows_z, size_z):
    total = None
    for p in range(count_x):
        at = (p * count_y + q) * rows_z + size_z
        value = pltpu.roll(deposit_ref[at : at + 8], p, 0) if p else deposit_ref[at : at + 8]
        total = value if total is None else total + value
    return total


def send_y_kernel(push, diffuse, leaving_ref, grid_ref, deposit_ref, y_ref, tiles_ref, lines_ref):
    comps, size_x, size_y, size_z = grid_ref.shape[0], grid_ref.shape[1] - 2, grid_ref.shape[2] - 8, grid_ref.shape[3]
    count_x, count_y = size_x // BX, size_y // BY
    rows_z = size_z + 8
    rows = leaving_ref.shape[1]
    height = comps * SPREAD
    for p in range(count_x):
        at = (p * count_y + count_y - 1) * rows_z
        tiles_ref[p * height : (p + 1) * height] = jnp.transpose(deposit_ref[at : at + size_z])[:height]
    first = jnp.full((rows, LANES), odd("gy")) == 0
    y_ref[0, 0:rows] = jnp.where(first, leaving_ref[2], leaving_ref[3])
    y_ref[1, 0:rows] = jnp.where(first, leaving_ref[3], leaving_ref[2])
    lines_ref[...] = jnp.zeros_like(lines_ref)
    for c in range(comps):
        for p in range(count_x):
            spot = slice(c * ROWS_Y + p * BX, c * ROWS_Y + p * BX + REACH_X)
            line = tiles_ref[pl.ds(p * height + c * SPREAD + BY, REACH_X, stride=REACH_Y)]
            lines_ref[spot] = lines_ref[spot] + line
    wrapped = top_rows(deposit_ref, count_y - 1, count_x, count_y, rows_z, size_z)
    lane = lane_ids(8)
    packed = jnp.zeros((8, LANES), jnp.float32)
    for c in range(comps):
        spot = slice(c * ROWS_Y, (c + 1) * ROWS_Y)
        beside = jnp.concatenate([grid_ref[c, 1 : size_x + 1, size_y - 1], jnp.zeros((8, LANES), jnp.float32)], axis=0)
        line = push * lines_ref[spot] + diffuse * beside
        y_ref[0, rows + c * ROWS_Y : rows + (c + 1) * ROWS_Y] = line
        y_ref[1, rows + c * ROWS_Y : rows + (c + 1) * ROWS_Y] = line
        for a in range(REACH_X):
            place = PACK * c + a
            value = turned(wrapped, place - c * SPREAD - a * REACH_Y - BY)
            packed = packed + jnp.where(lane == place, value, 0.0)
    corner = packed[0:1]
    for p in range(1, count_x):
        corner = corner + turned(packed[p : p + 1], p * BX)
    at = rows + size_x + 1
    y_ref[0, at : at + 1] = push * corner
    y_ref[1, at : at + 1] = push * corner


def merge_kernel(deposit_ref, top_tiles_ref, plane_ref, face_ref, tiles_ref, turned_ref):
    comps, planes = plane_ref.shape[:2]
    count_x, size_z = (planes - 1) // BX, plane_ref.shape[3]
    rows_z = size_z + 8
    count_y = deposit_ref.shape[0] // (rows_z * count_x)
    height = comps * SPREAD
    for p in range(count_x):
        for q in range(count_y - 1):
            at = p * count_y + q
            value = jnp.transpose(deposit_ref[at * rows_z : at * rows_z + size_z])
            tiles_ref[at * height : (at + 1) * height] = value[:height]
    top = row_ids(REACH_Y) >= BY
    for c in range(comps):
        for x in range(planes):
            bricks = [(x // BX, x % BX)] if x < planes - 1 else []
            if x and x % BX == 0:
                bricks.append((x // BX - 1, BX))

            def tile(q):
                total = None
                for p, a in bricks:
                    at = c * SPREAD + a * REACH_Y
                    if q < count_y - 1:
                        value = tiles_ref[(p * count_y + q) * height + at : (p * count_y + q) * height + at + REACH_Y]
                    else:
                        value = top_tiles_ref[p * height + at : p * height + at + REACH_Y]
                    total = value if total is None else total + value
                return total

            carried = None
            for q in range(0, count_y, 2):
                here = tile(q)
                if carried is not None:
                    here = here + carried
                between = pltpu.roll(tile(q + 1), BY, 0)
                here = here + jnp.where(top, between, 0.0)
                carried = jnp.where(top, 0.0, between)
                plane_ref[c, x, q * BY : q * BY + REACH_Y] = here
            plane_ref[c, x, count_y * BY :] = carried

    lane = lane_ids(count_x)
    turned_ref[...] = jnp.zeros_like(turned_ref)
    for q in range(count_y):
        wrapped = top_rows(deposit_ref, q, count_x, count_y, rows_z, size_z)[:count_x]
        within = (lane >= q * BY) & (lane <= (q + 1) * BY)
        for c in range(comps):
            for a in range(REACH_X):
                value = turned(wrapped, q * BY - c * SPREAD - a * REACH_Y)
                spot = pl.ds(PACK * c + a, count_x, stride=BX)
                turned_ref[spot] = turned_ref[spot] + jnp.where(within, value, 0.0)
    face_ref[...] = jnp.transpose(turned_ref[...])[: face_ref.shape[0]]


def send_xz_kernel(push, diffuse, grid_ref, deposit_ref, face_ref, x_ref, z_ref):
    comps, size_x = grid_ref.shape[0], grid_ref.shape[1] - 2
    size_y = z_ref.shape[0]
    lane = lane_ids(size_y)
    packed = push * face_ref[0:size_y]
    for c in range(comps):
        for x in range(size_x):
            place = PACK * c + x
            packed = packed + jnp.where(lane == place, diffuse * turned(grid_ref[c, x + 1, 0:size_y], place + 1), 0.0)
        total = push * deposit_ref[c, size_x, 0:size_y]
        x_ref[c * size_y : (c + 1) * size_y] = diffuse * grid_ref[c, size_x, 0:size_y] + total
    z_ref[...] = packed


def base_kernel(push, diffuse, count, grid_ref, deposit_ref, top_ref, y1_ref, y2_ref, state_ref, base_ref, velocity_ref):
    comps, size_x, size_y, size_z = base_ref.shape
    lane, sub = lane_ids(size_y), row_ids(size_y)
    top = top_ref[0:size_y]
    for c in range(comps):
        at = count + c * ROWS_Y
        lines = below(y1_ref, y2_ref, slice(at, at + size_x))
        for x in range(size_x):
            here = grid_ref[c, x + 1, 0:size_y]
            before = jnp.where(sub == 0, 0.0, pltpu.roll(here, 1, 0))
            laplace = grid_ref[c, x, 0:size_y] + grid_ref[c, x + 2, 0:size_y]
            laplace = laplace + grid_ref[c, x + 1, 1 : size_y + 1] + before
            ahead = jnp.where(lane == size_z - 1, turned(top, size_z - 1 - (PACK * c + x)), turned(here, -1))
            laplace = laplace + ahead + jnp.where(lane == 0, 0.0, turned(here, 1)) - 6.0 * here
            total = here + diffuse * laplace + push * deposit_ref[c, x, 0:size_y]
            line = jnp.broadcast_to(lines[x : x + 1], (size_y, LANES))
            base_ref[c, x] = total + jnp.where(sub == 0, line, 0.0)
        velocity_ref[c] = state_ref[pl.ds(c, velocity_ref.shape[1], stride=STATE)]


def below(first_ref, second_ref, rows):
    got = jnp.where(jnp.full((1, LANES), odd("gy")) == 1, first_ref[rows], second_ref[rows])
    return jnp.where(jnp.full((1, LANES), lax.axis_index("gy")) != 0, got, 0.0)


def relay_kernel(size_x, size_y, comps, count, first_ref, second_ref, x_in_ref, z_in_ref, leaving_ref, x_ref, z_ref, edge_ref):
    edge = comps * size_y
    x_ref[0:edge] = x_in_ref[...]
    for c in range(comps):
        at = count + c * ROWS_Y + size_x
        spot = slice(c * size_y, c * size_y + 1)
        x_ref[spot] = x_in_ref[spot] + below(first_ref, second_ref, slice(at, at + 1))
    x_ref[edge : edge + count] = leaving_ref[0]
    if x_ref.shape[0] > edge + count:
        x_ref[edge + count : edge + 2 * count] = leaving_ref[1]
    at = count + size_x + 1
    edge_ref[size_y:] = jnp.zeros((edge_ref.shape[0] - size_y, LANES), jnp.float32)
    edge_ref[0:size_y] = z_in_ref[...]
    edge_ref[0:1] = z_in_ref[0:1] + below(first_ref, second_ref, slice(at, at + 1))
    up = odd("gz")
    z_ref[up, 0:count] = leaving_ref[4]
    z_ref[up, count : count + size_y] = edge_ref[0:size_y]
    z_ref[1 - up, 0:count] = leaving_ref[5]
    z_ref[1 - up, count : count + size_y] = jnp.zeros((size_y, LANES), jnp.float32)


def finish_kernel(
    count, base_ref, y1_ref, y2_ref, x_ref, minus_x_ref, z1_ref, z2_ref, edge_ref, gas_ref, arrivals_ref,
):
    comps, size_x, size_y, _ = base_ref.shape
    first_lane = lane_ids(size_y) == 0
    odd_y, odd_z = jnp.full((1, LANES), odd("gy")) == 1, jnp.full((1, LANES), odd("gz")) == 1
    place = jnp.full((1, LANES), lax.axis_index("gy"))
    lower, upper = place != 0, place != lax.axis_size("gy") - 1
    rows = slice(count, count + size_y)
    face = jnp.where(odd_z, z1_ref[rows], z2_ref[rows])
    corner = edge_ref[0:size_y]
    for c in range(comps):
        for x in range(size_x):
            total = base_ref[c, x]
            far = turned(face, -(PACK * c + x))
            if x == 0:
                total = total + x_ref[c * size_y : (c + 1) * size_y]
                far = far + turned(corner, -(PACK * c + size_x))
            gas_ref[c, x] = total + jnp.where(first_lane, far, 0.0)

    slots = arrivals_ref.shape[2]
    for i in range(arrivals_ref.shape[1]):

        def rows_of(ref, at=0):
            return ref[at + i * slots : at + (i + 1) * slots]

        arrivals_ref[0, i] = rows_of(x_ref, comps * size_y)
        arrivals_ref[1, i] = rows_of(minus_x_ref, minus_x_ref.shape[0] - count)
        y1, y2 = rows_of(y1_ref), rows_of(y2_ref)
        arrivals_ref[2, i] = jnp.where(lower, jnp.where(odd_y, y1, y2), 0.0)
        arrivals_ref[3, i] = jnp.where(upper, jnp.where(odd_y, y2, y1), 0.0)
        z1, z2 = rows_of(z1_ref), rows_of(z2_ref)
        arrivals_ref[4, i] = jnp.where(odd_z, z1, z2)
        arrivals_ref[5, i] = jnp.where(odd_z, z2, z1)


def per_device(gas_field, velocity, fraction, response, cell_index, brick_index, crossing):
    comps, size_x, size_y, size_z = gas_field.shape
    nblocks = velocity.shape[0]
    loading = 0.5 * size_x * size_y * size_z / (nblocks * 128)
    push, diffuse = -TIME_STEP * loading, TIME_STEP * VISCOSITY
    velocity = jnp.transpose(velocity, (1, 0, 2))
    fraction = jnp.transpose(fraction, (1, 0, 2))
    spare = nblocks + 8
    rows_z = size_z + 8
    grid_shape = (comps, size_x + 2, ROWS_Y, LANES)
    lines_shape = ((size_x // BX) * (size_y // BY) * comps * rows_z, LANES)
    deposit_shape = ((size_x // BX) * (size_y // BY) * rows_z, LANES)

    inputs = (gas_field, velocity, fraction, response, cell_index, brick_index, crossing)
    inputs = [pltpu.with_memory_space_constraint(array, pltpu.HBM) for array in inputs]
    grid, face, plane, velocity, fraction, response, cell_index, brick_index, crossing = call(
        begin_kernel,
        [grid_shape, (size_y, LANES), (comps * size_y, LANES)]
        + [jax.ShapeDtypeStruct(array.shape, array.dtype) for array in inputs[1:]],
        *inputs, hbm=range(7), scratch=(pltpu.SemaphoreType.DMA((7,)),), limit=40,
    )
    from_z = moved_along(face, "gz", -1)
    from_x = moved_along(plane, "gx", -1)
    from_xz = moved_diagonally(face, -1)
    lines, deposit, table, ready, blocks = call(
        prepare_kernel,
        [
            lines_shape,
            deposit_shape,
            (TABLE_ROWS * spare, LANES),
            (8, LANES),
            jax.ShapeDtypeStruct((2 * (nblocks + UNROLL) + 2,), jnp.int32),
        ],
        grid, velocity, fraction, response, cell_index, brick_index,
        smem=(5,), smem_outs=(4,), cycles=3000,
    )
    line_rows = -(-(comps * size_x + comps + 1) // 8) * 8
    (y_lines,) = call(y_lines_kernel, [(line_rows, LANES)], grid, from_z, from_x, from_xz, ready)
    y1, y2 = swapped_y((y_lines, y_lines))
    square = pltpu.VMEM((LANES, LANES), jnp.float32)
    scalars = (pltpu.SMEM(blocks.shape, jnp.int32), pltpu.SMEM(brick_index.shape, jnp.int32))
    dims = (comps, size_x // BX, size_y // BY, size_z // BZ, rows_z)
    slots = crossing.shape[1]
    count = 7 * slots

    def parts(many):
        return [(many, 2 * comps * REACH_Z, LANES), (many, 2 * LANES, LANES)]

    state, push_parts, spread_parts, grid, lines, top = call(
        functools.partial(gather_kernel, dims),
        [(STATE * spare, LANES)]
        + [jax.ShapeDtypeStruct(shape, jnp.bfloat16) for shape in parts(nblocks + UNROLL)]
        + [grid_shape, lines_shape, (LANES, LANES)],
        blocks, brick_index, table, grid, lines, from_z, from_x, from_xz,
        aliases={3: 3, 4: 4}, cycles=4000, scratch=(*scalars, square, pltpu.SemaphoreType.DMA((2,))),
    )
    grid, lines, state, deposit, leaving = call(
        functools.partial(late_kernel, dims, slots),
        [grid_shape, lines_shape, (STATE * spare, LANES), deposit_shape, (6 * count, LANES)],
        blocks, brick_index, crossing, table, grid, lines, top, y1, y2, state, deposit,
        aliases={4: 0, 5: 1, 9: 2, 10: 3}, cycles=2000,
        scratch=[
            *(pltpu.VMEM(shape, jnp.bfloat16) for shape in parts(UNROLL)),
            *scalars,
            pltpu.SMEM(crossing.shape, jnp.int32),
            square,
            pltpu.SemaphoreType.DMA((3,)),
        ],
    )
    leaving = leaving.reshape(6, count, LANES)
    height = comps * SPREAD
    to_y, top_tiles = call(
        functools.partial(send_y_kernel, push, diffuse),
        [(2, count + comps * ROWS_Y, LANES), ((size_x // BX) * height, LANES)],
        leaving, grid, deposit, cycles=300, scratch=(pltpu.VMEM((comps * ROWS_Y, LANES), jnp.float32),),
    )
    y1, y2 = swapped_y((to_y[0], to_y[1]))
    (deposit,) = call(
        functools.partial(deposit_kernel, dims), [deposit_shape], blocks, brick_index, push_parts, spread_parts, deposit,
        smem=(0, 1), aliases={4: 0}, cycles=4000,
    )
    deposit, over = call(
        merge_kernel, [(comps, size_x + 1, ROWS_Y, LANES), (ROWS_Y, LANES)], deposit, top_tiles,
        cycles=1000, scratch=(pltpu.VMEM(((size_x // BX) * (size_y // BY) * height, LANES), jnp.float32), square),
    )
    to_x, to_z = call(
        functools.partial(send_xz_kernel, push, diffuse), [(comps * size_y, LANES), (size_y, LANES)],
        grid, deposit, over, cycles=500,
    )
    base, velocity_next = call(
        functools.partial(base_kernel, push, diffuse, count), [gas_field.shape, (comps, nblocks, LANES)],
        grid, deposit, top, y1, y2, state, cycles=1000,
    )
    edge = comps * size_y
    both = lax.axis_size("gx") == 2
    to_x, to_z, to_xz = call(
        functools.partial(relay_kernel, size_x, size_y, comps, count),
        [(edge + (2 if both else 1) * count, LANES), (2, count + size_y, LANES), (count + size_y + 8, LANES)],
        y1, y2, to_x, to_z, leaving,
    )
    got_x = moved_along(to_x, "gx", 1)
    z1, z2 = swapped_z((to_z[0], to_z[1]))
    got_xz = moved_diagonally(to_xz, 1)
    got_mx = got_x if both else moved_along(leaving[1], "gx", -1)
    gas_next, arrivals = call(
        functools.partial(finish_kernel, count), [gas_field.shape, (6, 7, slots, LANES)],
        base, y1, y2, got_x, got_mx, z1, z2, got_xz,
    )
    return gas_next, jnp.transpose(velocity_next, (1, 0, 2)), jnp.transpose(arrivals, (0, 2, 1, 3))


def solution(mesh):
    owner = ("gx", "gz", "gy")
    in_specs = (
        P(None, "gx", "gy", "gz"),
        P(owner, None, None),
        P(owner, None, None),
        P(owner, None),
        P(owner, None),
        P(owner),
        P(owner, None),
    )
    out_specs = (
        P(None, "gx", "gy", "gz"),
        P(owner, None, None),
        P(owner, None, None, None),
    )
    return jax.shard_map(
        per_device, mesh=mesh, in_specs=in_specs, out_specs=out_specs, check_vma=False
    )
```

```python
import functools

import jax
import jax.numpy as jnp
from jax import lax
from jax.experimental import pallas as pl
from jax.experimental.pallas import tpu as pltpu
from jax.sharding import PartitionSpec as P

BX = 4
BY = 4
BZ = 8

TIME_STEP = 0.25
VISCOSITY = 0.4

LANES = 128
PACK = 32
ROWS_Y = 24
REACH_X = BX + 1
REACH_Y = 8
SPREAD = REACH_X * REACH_Y
REACH_Z = 2 * BZ
UNROLL = 8

WEIGHT, ALONG_Y, IN_Y, ALONG_Z, IN_Z, RESPONSE, MOVING, OFFSET = 0, 5, 6, 7, 8, 9, 10, 13
TABLE_ROWS = 16
STATE = 8

VMEM = pl.BlockSpec(memory_space=pltpu.VMEM)
SMEM = pl.BlockSpec(memory_space=pltpu.SMEM)
HBM = pl.BlockSpec(memory_space=pltpu.HBM)


def moved_along(block, axis, distance):
    count = lax.axis_size(axis)
    return lax.ppermute(block, axis, [(i, (i + distance) % count) for i in range(count)])


def swapped_z(blocks):
    count = lax.axis_size("gz")
    first = [(i, i ^ 1) for i in range(count)]
    second = [(i, (((i + 1) ^ 1) - 1) % count) for i in range(count)]
    return lax.ppermute(blocks[0], "gz", first), lax.ppermute(blocks[1], "gz", second)


def swapped_y(blocks):
    nz, ny = lax.axis_size("gz"), lax.axis_size("gy")
    first = [(j, j ^ 1) for j in range(ny)]
    second = []
    for k in range(nz):
        second.append((k * ny, (k ^ 1) * ny))
        second.append((k * ny + ny - 1, (k ^ 1) * ny + ny - 1))
        second.extend((k * ny + j, k * ny + ((j + 1) ^ 1) - 1) for j in range(1, ny - 1))
    middle = lax.ppermute(blocks[1], ("gz", "gy"), second)
    return lax.ppermute(blocks[0], "gy", first), middle


def moved_diagonally(block, distance):
    nx, nz = lax.axis_size("gx"), lax.axis_size("gz")
    route = [(i * nz + k, (i + distance) % nx * nz + (k + distance) % nz) for i in range(nx) for k in range(nz)]
    return lax.ppermute(block, ("gx", "gz"), route)


def call(
    body, outs, *operands, smem=(), hbm=(), smem_outs=(), hbm_outs=(), scratch=(), aliases=None, cycles=0, limit=40
):
    return pl.pallas_call(
        body,
        out_shape=[o if isinstance(o, jax.ShapeDtypeStruct) else jax.ShapeDtypeStruct(o, jnp.float32) for o in outs],
        in_specs=[SMEM if i in smem else HBM if i in hbm else VMEM for i in range(len(operands))],
        out_specs=[SMEM if i in smem_outs else HBM if i in hbm_outs else VMEM for i in range(len(outs))],
        scratch_shapes=list(scratch),
        input_output_aliases=aliases or {},
        compiler_params=pltpu.CompilerParams(vmem_limit_bytes=limit * 1024 * 1024),
        cost_estimate=pl.CostEstimate(flops=cycles * 4096, bytes_accessed=cycles * 1024, transcendentals=0),
    )(*operands)


def lane_ids(rows):
    return lax.broadcasted_iota(jnp.int32, (rows, LANES), 1)


def row_ids(rows):
    return lax.broadcasted_iota(jnp.int32, (rows, LANES), 0)


def turned(value, shift):
    shift = shift % LANES
    return pltpu.roll(value, shift, 1) if shift else value


def odd(axis):
    return lax.axis_index(axis) % 2


def begin_kernel(
    gas_ref, velocity_in, fraction_in, response_in, cell_in, brick_in, crossing_in,
    grid_ref, face_ref, plane_ref, velocity_ref, fraction_ref, response_ref, cell_ref, brick_ref, crossing_ref, sems,
):
    comps, size_x, size_y, _ = gas_ref.shape
    pairs = [
        (gas_ref, grid_ref.at[:, 1 : size_x + 1, 0:size_y]),
        (velocity_in, velocity_ref), (fraction_in, fraction_ref), (response_in, response_ref),
        (cell_in, cell_ref), (brick_in, brick_ref), (crossing_in, crossing_ref),
    ]
    copies = [pltpu.make_async_copy(source, target, sems.at[i]) for i, (source, target) in enumerate(pairs)]
    for copy in copies:
        copy.start()
    zeros = jnp.zeros((ROWS_Y, LANES), jnp.float32)
    for c in range(comps):
        grid_ref[c, 0] = zeros
        grid_ref[c, size_x + 1] = zeros
        for x in range(size_x):
            grid_ref[c, x + 1, size_y:] = zeros[size_y:]
    copies[0].wait()
    lane = lane_ids(size_y)
    face = jnp.zeros((size_y, LANES), jnp.float32)
    for c in range(comps):
        plane_ref[c * size_y : (c + 1) * size_y] = grid_ref[c, 1, 0:size_y]
        for x in range(size_x):
            place = PACK * c + x
            face = jnp.where(lane == place, turned(grid_ref[c, x + 1, 0:size_y], place), face)
    face_ref[...] = face
    for copy in copies[1:]:
        copy.wait()


def parts_of(value):
    main = value.astype(jnp.bfloat16).astype(jnp.float32)
    return main, value - main


def lay_out(grid_ref, lines_ref, p, q, size_y, size_z):
    comps = grid_ref.shape[0]
    rows_z = size_z + 8
    count_y = size_y // BY
    for c in range(comps):
        planes = [grid_ref[c, p * BX + a + 1, q * BY : q * BY + REACH_Y] for a in range(REACH_X)]
        main, rest = parts_of(jnp.concatenate(planes, axis=0))
        stack = jnp.concatenate([main, rest, main, jnp.zeros((LANES - 3 * SPREAD, LANES), jnp.float32)], axis=0)
        at = ((p * count_y + q) * comps + c) * rows_z
        lines_ref[at : at + size_z] = jnp.transpose(stack)


def lay_out_top(turned_ref, lines_ref, q, comps, count_x, count_y, size_z):
    lane = lane_ids(count_x)
    rows_z = size_z + 8
    for c in range(comps):
        total = jnp.zeros((count_x, LANES), jnp.float32)
        for a in range(REACH_X):
            rows = turned_ref[pl.ds(PACK * c + a, count_x, stride=BX)]
            total = jnp.where(lane // REACH_Y == a, turned(rows, a * REACH_Y - q * BY), total)
        main, rest = parts_of(total)
        line = main + turned(rest, SPREAD) + turned(main, 2 * SPREAD)
        for p in range(count_x):
            at = ((p * count_y + q) * comps + c) * rows_z + size_z
            lines_ref[at : at + 1] = line[p : p + 1]


def prepare_kernel(
    grid_ref, velocity_ref, fraction_ref, response_ref, cell_ref, brick_ref,
    lines_ref, deposit_ref, table_ref, ready_ref, list_ref,
):
    comps, size_x, size_y, size_z = grid_ref.shape[0], grid_ref.shape[1] - 2, grid_ref.shape[2] - 8, grid_ref.shape[3]
    nblocks = velocity_ref.shape[1]
    count_x, count_y, count_z = size_x // BX, size_y // BY, size_z // BZ
    rows_z = size_z + 8

    room = nblocks + UNROLL

    def visit(k, counts):
        late = jnp.where(lax.rem(lax.div(brick_ref[k], count_z), count_y) == count_y - 1, 1, 0)
        list_ref[jnp.where(late == 1, room + counts[1], counts[0])] = k
        return counts[0] + 1 - late, counts[1] + late

    early, late = lax.fori_loop(0, nblocks, visit, (jnp.int32(0), jnp.int32(0)), unroll=8)
    for base, count in ((0, early), (room, late)):
        for u in range(UNROLL):
            list_ref[base + count + u] = nblocks
    list_ref[2 * room] = early
    list_ref[2 * room + 1] = late
    ready_ref[...] = jnp.zeros_like(ready_ref)

    deposit_ref[...] = jnp.zeros_like(deposit_ref)
    for p in range(count_x):
        for q in range(count_y):
            for c in range(comps):
                at = ((p * count_y + q) * comps + c) * rows_z + size_z
                lines_ref[at : at + 8] = jnp.zeros((8, LANES), jnp.float32)
    for p in range(count_x - 1):
        for q in range(count_y - 1):
            lay_out(grid_ref, lines_ref, p, q, size_y, size_z)

    cells = cell_ref[...]
    cell_x, cell_y, cell_z = cells // (BY * BZ), cells // BZ % BY, cells % BZ
    along_x = fraction_ref[0]

    def put(row, value):
        table_ref[pl.ds(row, nblocks, stride=TABLE_ROWS)] = value

    for a in range(REACH_X):
        put(WEIGHT + a, jnp.where(cell_x == a, 1.0 - along_x, 0.0) + jnp.where(cell_x == a - 1, along_x, 0.0))
    put(ALONG_Y, fraction_ref[1])
    put(IN_Y, cell_y.astype(jnp.float32))
    put(ALONG_Z, fraction_ref[2])
    put(IN_Z, cell_z.astype(jnp.float32))
    put(RESPONSE, response_ref[...])
    for c in range(comps):
        put(MOVING + c, velocity_ref[c])
        put(OFFSET + c, fraction_ref[c])
    spare = table_ref.shape[0] - nblocks * TABLE_ROWS
    row = row_ids(spare)
    table_ref[nblocks * TABLE_ROWS :] = jnp.where(row % TABLE_ROWS == RESPONSE, 1.0, 0.0)


def y_lines_kernel(grid_ref, face_ref, from_x_ref, edge_ref, ready_ref, out_ref):
    comps, size_x = grid_ref.shape[0], grid_ref.shape[1] - 2
    size_y = face_ref.shape[0]
    for c in range(comps):
        out_ref[c * size_x : (c + 1) * size_x] = grid_ref[c, 1 : size_x + 1, 0]
        out_ref[comps * size_x + c : comps * size_x + c + 1] = from_x_ref[c * size_y : c * size_y + 1]
    line = jnp.where(lane_ids(8) % PACK == size_x, turned(edge_ref[0:8], size_x), face_ref[0:8])
    out_ref[comps * size_x + comps : comps * size_x + comps + 1] = line[0:1]


def halo_xz_kernel(grid_in_ref, lines_in_ref, face_ref, from_x_ref, edge_ref, grid_ref, lines_ref, top_ref, turned_ref):
    comps, size_x = grid_ref.shape[0], grid_ref.shape[1] - 2
    size_y, size_z = face_ref.shape[0], grid_ref.shape[3]
    count_x, count_y = size_x // BX, size_y // BY
    for c in range(comps):
        grid_ref[c, size_x + 1, 0:size_y] = from_x_ref[c * size_y : (c + 1) * size_y]
    for q in range(count_y - 1):
        lay_out(grid_ref, lines_ref, count_x - 1, q, size_y, size_z)
    top = jnp.where(lane_ids(size_y) % PACK == size_x, turned(edge_ref[...], size_x), face_ref[...])
    top_ref[0:size_y] = top
    top_ref[size_y:] = jnp.zeros((LANES - size_y, LANES), jnp.float32)
    turned_ref[...] = jnp.transpose(top_ref[...])
    for q in range(count_y - 1):
        lay_out_top(turned_ref, lines_ref, q, comps, count_x, count_y, size_z)


def halo_y_kernel(size_y, grid_in_ref, lines_in_ref, top_in_ref, first_ref, second_ref, grid_ref, lines_ref, turned_ref):
    comps, size_x, size_z = grid_ref.shape[0], grid_ref.shape[1] - 2, grid_ref.shape[3]
    count_x, count_y = size_x // BX, size_y // BY
    inside = lax.axis_index("gy") != lax.axis_size("gy") - 1
    kept = (row_ids(8) == 0) & inside
    even = jnp.full((1, LANES), odd("gy")) == 0

    def line_at(row):
        line = jnp.where(even, first_ref[row : row + 1], second_ref[row : row + 1])
        return jnp.where(kept, jnp.broadcast_to(line, (8, LANES)), 0.0)

    for c in range(comps):
        for x in range(size_x + 1):
            grid_ref[c, x + 1, size_y:] = line_at(c * size_x + x if x < size_x else comps * size_x + c)
    for p in range(count_x):
        lay_out(grid_ref, lines_ref, p, count_y - 1, size_y, size_z)
    corner = line_at(comps * size_x + comps)
    rest = jnp.zeros((LANES - size_y - 8, LANES), jnp.float32)
    turned_ref[...] = jnp.transpose(jnp.concatenate([top_in_ref[0:size_y], corner, rest], axis=0))
    lay_out_top(turned_ref, lines_ref, count_y - 1, comps, count_x, count_y, size_z)


def block_steps(dims, list_ref, brick_ref):
    comps, _, count_y, count_z, rows_z = dims
    nblocks = brick_ref.shape[0]
    sub = row_ids(8)
    row_y = row_ids(REACH_Y).astype(jnp.float32)
    row_z = row_ids(REACH_Z).astype(jnp.float32)
    lanes = lane_ids(REACH_Z)

    def hat(rows, inside, along):
        return jnp.where(rows == inside, 1.0 - along, 0.0) + jnp.where(rows == inside + 1.0, along, 0.0)

    def place_of(at):
        k = list_ref[at]
        brick = jnp.where(k < nblocks, brick_ref[jnp.minimum(k, nblocks - 1)], 0)
        brick_x = lax.div(brick, count_y * count_z)
        brick_y = lax.rem(lax.div(brick, count_z), count_y)
        return k, brick_x * count_y + brick_y, lax.rem(brick, count_z)

    def loaded(at, lines_ref, table_ref):
        k, pair, brick_z = place_of(at)
        first = pl.multiple_of(pair * comps * rows_z + brick_z * BZ, 8)
        window = jnp.concatenate([lines_ref[pl.ds(first + c * rows_z, REACH_Z)] for c in range(comps)], axis=0)
        table = table_ref[pl.ds(pl.multiple_of(k * TABLE_ROWS, TABLE_ROWS), TABLE_ROWS)]
        return k, window, [table[i : i + 1] for i in range(TABLE_ROWS)]

    def weighted(rows):
        weight_y = hat(row_y, rows[IN_Y], rows[ALONG_Y])
        weight_z = hat(row_z, rows[IN_Z], rows[ALONG_Z])
        weight = jnp.concatenate([rows[WEIGHT + a] * weight_y for a in range(REACH_X)], axis=0)
        return weight_z, *parts_of(weight)

    def stepped(seen, weight_z, rows):
        rate = 1.0 / rows[RESPONSE]
        state, moved, pushed = [], [], []
        for c in range(comps):
            gas_sample = jnp.sum(seen[c * REACH_Z : (c + 1) * REACH_Z] * weight_z, axis=0, keepdims=True)
            drag = (gas_sample - rows[MOVING + c]) * rate
            state.append(rows[MOVING + c] + TIME_STEP * drag)
            moved.append(rows[OFFSET + c] + TIME_STEP * state[c])
            pushed.append(drag * weight_z)
        tile = jnp.broadcast_to(rows[RESPONSE], (STATE, LANES))
        for i, value in enumerate(state + moved):
            tile = jnp.where(sub == i, value, tile)
        return tile, jnp.concatenate(parts_of(jnp.concatenate(pushed, axis=0)), axis=0)

    def gathered(one, two):
        tables, windows, weights = [], [], []
        for _, window, rows in (one, two):
            weight_z, main, rest = weighted(rows)
            weights.append((weight_z, main, rest))
            unused = jnp.zeros((LANES - 3 * SPREAD, LANES), jnp.float32)
            tables.append(jnp.concatenate([main, main, rest, unused], axis=0).astype(jnp.bfloat16))
            windows.append(window)
        seen = lax.dot_general(
            jnp.concatenate(windows, axis=0).astype(jnp.bfloat16), jnp.concatenate(tables, axis=1),
            (((1,), (0,)), ((), ())), preferred_element_type=jnp.float32,
        )
        height = comps * REACH_Z
        tiles, fresh = [], []
        for i, (_, _, rows) in enumerate((one, two)):
            weight_z, main, rest = weights[i]
            mine = seen[i * height : (i + 1) * height, i * LANES : (i + 1) * LANES]
            tile, push = stepped(mine, weight_z, rows)
            tiles.append(tile)
            unused = jnp.zeros((LANES - comps * SPREAD, LANES), jnp.float32)
            spread = jnp.concatenate([main] * comps + [unused] + [rest] * comps + [unused], axis=0)
            fresh.append((push.astype(jnp.bfloat16), spread.astype(jnp.bfloat16)))
        return tiles, fresh

    def shared(push, spread):
        shares = lax.dot_general(push, spread, (((1,), (1,)), ((), ())), preferred_element_type=jnp.float32)
        height = comps * REACH_Z
        total = shares[:height, :LANES] + shares[:height, LANES:] + shares[height:, :LANES]
        result = jnp.zeros((REACH_Z, LANES), jnp.float32)
        for c in range(comps):
            inside = (lanes >= c * SPREAD) & (lanes < (c + 1) * SPREAD)
            result = jnp.where(inside, total[c * REACH_Z : (c + 1) * REACH_Z], result)
        return result

    def add(deposit_ref, at, shares):
        spots = []
        for u in range(len(shares)):
            _, pair, brick_z = place_of(at + u)
            spots.append(pl.ds(pl.multiple_of(pair * rows_z + brick_z * BZ, 8), REACH_Z))
        for spot, share in zip(spots, shares):
            deposit_ref[spot] = deposit_ref[spot] + share

    def group_of(taken):
        tiles, fresh = [], []
        for u in range(0, UNROLL, 2):
            both, kept = gathered(taken[u], taken[u + 1])
            tiles.extend(both)
            fresh.extend(kept)
        return tiles, fresh

    def keep(state_ref, taken, tiles):
        for (k, _, _), tile in zip(taken, tiles):
            state_ref[pl.ds(pl.multiple_of(STATE * k, STATE), STATE)] = tile

    def deposits_of(kept):
        return [shared(push, spread) for push, spread in kept]

    return loaded, group_of, keep, deposits_of, add


def groups_in(list_ref, late):
    room = (list_ref.shape[0] - 2) // 2
    return late * room, (list_ref[2 * room + late] + UNROLL - 1) // UNROLL


def fetched(sems, *pairs):
    copies = [pltpu.make_async_copy(source, target, sems.at[i]) for i, (source, target) in enumerate(pairs)]
    for copy in copies:
        copy.start()
    return copies


def gather_kernel(
    dims, list_in, brick_in, table_ref, grid_in_ref, lines_in_ref, face_ref, from_x_ref, edge_ref,
    state_ref, push_ref, spread_ref, grid_ref, lines_ref, top_ref, list_ref, brick_ref, turned_ref, sems,
):
    copies = fetched(sems, (list_in, list_ref), (brick_in, brick_ref))
    halo_xz_kernel(grid_in_ref, lines_in_ref, face_ref, from_x_ref, edge_ref, grid_ref, lines_ref, top_ref, turned_ref)
    for copy in copies:
        copy.wait()
    loaded, group_of, keep, _, _ = block_steps(dims, list_ref, brick_ref)
    base, groups = groups_in(list_ref, 0)

    @pl.loop(0, groups)
    def _(group):
        taken = [loaded(base + group * UNROLL + u, lines_ref, table_ref) for u in range(UNROLL)]
        tiles, fresh = group_of(taken)
        keep(state_ref, taken, tiles)
        for i, (push, spread) in enumerate(fresh):
            push_ref[group * UNROLL + i] = push
            spread_ref[group * UNROLL + i] = spread


def deposit_kernel(dims, list_ref, brick_ref, push_ref, spread_ref, deposit_in_ref, deposit_ref):
    _, _, _, deposits_of, add = block_steps(dims, list_ref, brick_ref)
    base, groups = groups_in(list_ref, 0)

    @pl.loop(0, groups)
    def _(group):
        mine = [group * UNROLL + i for i in range(UNROLL)]
        add(deposit_ref, base + group * UNROLL, deposits_of([(push_ref[i], spread_ref[i]) for i in mine]))


def late_kernel(
    dims, slots, list_in, brick_in, crossing_in, table_ref, grid_in_ref, lines_in_ref, top_in_ref, first_ref, second_ref,
    state_in_ref, deposit_in_ref,
    grid_ref, lines_ref, state_ref, deposit_ref, leaving_ref,
    push_ref, spread_ref, list_ref, brick_ref, crossing_ref, turned_ref, sems,
):
    copies = fetched(sems, (list_in, list_ref), (brick_in, brick_ref), (crossing_in, crossing_ref))
    halo_y_kernel(
        dims[2] * BY, grid_in_ref, lines_in_ref, top_in_ref, first_ref, second_ref, grid_ref, lines_ref, turned_ref
    )
    for copy in copies:
        copy.wait()
    loaded, group_of, keep, deposits_of, add = block_steps(dims, list_ref, brick_ref)
    base, groups = groups_in(list_ref, 1)
    push_ref[...] = jnp.zeros_like(push_ref)
    spread_ref[...] = jnp.zeros_like(spread_ref)

    @pl.loop(0, groups + 1)
    def _(group):
        now = base + jnp.maximum(jnp.minimum(group, groups - 1), 0) * UNROLL
        before = base + jnp.maximum(group - 1, 0) * UNROLL
        taken = [loaded(now + u, lines_ref, table_ref) for u in range(UNROLL)]
        shares = deposits_of([(push_ref[i], spread_ref[i]) for i in range(UNROLL)])
        tiles, fresh = group_of(taken)
        add(deposit_ref, before, shares)
        keep(state_ref, taken, tiles)
        for i, (push, spread) in enumerate(fresh):
            push_ref[i] = push
            spread_ref[i] = spread

    rows = leaving_ref.shape[0] // (6 * slots)
    for face in range(6):
        tiles = []
        for slot in range(slots):
            block = crossing_ref[face, slot]
            spot = pl.ds(pl.multiple_of(jnp.maximum(block, 0) * STATE, STATE), STATE)
            live = jnp.full((STATE, LANES), block, jnp.int32) >= 0
            tiles.append(jnp.where(live, state_ref[spot], 0.0))
        for slot, tile in enumerate(tiles):
            leaving_ref[pl.ds(face * rows * slots + slot, rows, stride=slots)] = tile[:rows]


def top_rows(deposit_ref, q, count_x, count_y, rows_z, size_z):
    total = None
    for p in range(count_x):
        at = (p * count_y + q) * rows_z + size_z
        value = pltpu.roll(deposit_ref[at : at + 8], p, 0) if p else deposit_ref[at : at + 8]
        total = value if total is None else total + value
    return total


def send_y_kernel(push, diffuse, leaving_ref, grid_ref, deposit_ref, y_ref, tiles_ref, lines_ref):
    comps, size_x, size_y, size_z = grid_ref.shape[0], grid_ref.shape[1] - 2, grid_ref.shape[2] - 8, grid_ref.shape[3]
    count_x, count_y = size_x // BX, size_y // BY
    rows_z = size_z + 8
    rows = leaving_ref.shape[1]
    height = comps * SPREAD
    for p in range(count_x):
        at = (p * count_y + count_y - 1) * rows_z
        tiles_ref[p * height : (p + 1) * height] = jnp.transpose(deposit_ref[at : at + size_z])[:height]
    first = jnp.full((rows, LANES), odd("gy")) == 0
    y_ref[0, 0:rows] = jnp.where(first, leaving_ref[2], leaving_ref[3])
    y_ref[1, 0:rows] = jnp.where(first, leaving_ref[3], leaving_ref[2])
    lines_ref[...] = jnp.zeros_like(lines_ref)
    for c in range(comps):
        for p in range(count_x):
            spot = slice(c * ROWS_Y + p * BX, c * ROWS_Y + p * BX + REACH_X)
            line = tiles_ref[pl.ds(p * height + c * SPREAD + BY, REACH_X, stride=REACH_Y)]
            lines_ref[spot] = lines_ref[spot] + line
    wrapped = top_rows(deposit_ref, count_y - 1, count_x, count_y, rows_z, size_z)
    lane = lane_ids(8)
    packed = jnp.zeros((8, LANES), jnp.float32)
    for c in range(comps):
        spot = slice(c * ROWS_Y, (c + 1) * ROWS_Y)
        beside = jnp.concatenate([grid_ref[c, 1 : size_x + 1, size_y - 1], jnp.zeros((8, LANES), jnp.float32)], axis=0)
        line = push * lines_ref[spot] + diffuse * beside
        y_ref[0, rows + c * ROWS_Y : rows + (c + 1) * ROWS_Y] = line
        y_ref[1, rows + c * ROWS_Y : rows + (c + 1) * ROWS_Y] = line
        for a in range(REACH_X):
            place = PACK * c + a
            value = turned(wrapped, place - c * SPREAD - a * REACH_Y - BY)
            packed = packed + jnp.where(lane == place, value, 0.0)
    corner = packed[0:1]
    for p in range(1, count_x):
        corner = corner + turned(packed[p : p + 1], p * BX)
    at = rows + size_x + 1
    y_ref[0, at : at + 1] = push * corner
    y_ref[1, at : at + 1] = push * corner


def merge_kernel(deposit_ref, top_tiles_ref, plane_ref, face_ref, tiles_ref, turned_ref):
    comps, planes = plane_ref.shape[:2]
    count_x, size_z = (planes - 1) // BX, plane_ref.shape[3]
    rows_z = size_z + 8
    count_y = deposit_ref.shape[0] // (rows_z * count_x)
    height = comps * SPREAD
    for p in range(count_x):
        for q in range(count_y - 1):
            at = p * count_y + q
            value = jnp.transpose(deposit_ref[at * rows_z : at * rows_z + size_z])
            tiles_ref[at * height : (at + 1) * height] = value[:height]
    top = row_ids(REACH_Y) >= BY
    for c in range(comps):
        for x in range(planes):
            bricks = [(x // BX, x % BX)] if x < planes - 1 else []
            if x and x % BX == 0:
                bricks.append((x // BX - 1, BX))

            def tile(q):
                total = None
                for p, a in bricks:
                    at = c * SPREAD + a * REACH_Y
                    if q < count_y - 1:
                        value = tiles_ref[(p * count_y + q) * height + at : (p * count_y + q) * height + at + REACH_Y]
                    else:
                        value = top_tiles_ref[p * height + at : p * height + at + REACH_Y]
                    total = value if total is None else total + value
                return total

            carried = None
            for q in range(0, count_y, 2):
                here = tile(q)
                if carried is not None:
                    here = here + carried
                between = pltpu.roll(tile(q + 1), BY, 0)
                here = here + jnp.where(top, between, 0.0)
                carried = jnp.where(top, 0.0, between)
                plane_ref[c, x, q * BY : q * BY + REACH_Y] = here
            plane_ref[c, x, count_y * BY :] = carried

    lane = lane_ids(count_x)
    turned_ref[...] = jnp.zeros_like(turned_ref)
    for q in range(count_y):
        wrapped = top_rows(deposit_ref, q, count_x, count_y, rows_z, size_z)[:count_x]
        within = (lane >= q * BY) & (lane <= (q + 1) * BY)
        for c in range(comps):
            for a in range(REACH_X):
                value = turned(wrapped, q * BY - c * SPREAD - a * REACH_Y)
                spot = pl.ds(PACK * c + a, count_x, stride=BX)
                turned_ref[spot] = turned_ref[spot] + jnp.where(within, value, 0.0)
    face_ref[...] = jnp.transpose(turned_ref[...])[: face_ref.shape[0]]


def send_xz_kernel(push, diffuse, grid_ref, deposit_ref, face_ref, x_ref, z_ref):
    comps, size_x = grid_ref.shape[0], grid_ref.shape[1] - 2
    size_y = z_ref.shape[0]
    lane = lane_ids(size_y)
    packed = push * face_ref[0:size_y]
    for c in range(comps):
        for x in range(size_x):
            place = PACK * c + x
            packed = packed + jnp.where(lane == place, diffuse * turned(grid_ref[c, x + 1, 0:size_y], place + 1), 0.0)
        total = push * deposit_ref[c, size_x, 0:size_y]
        x_ref[c * size_y : (c + 1) * size_y] = diffuse * grid_ref[c, size_x, 0:size_y] + total
    z_ref[...] = packed


def base_kernel(push, diffuse, count, grid_ref, deposit_ref, top_ref, y1_ref, y2_ref, state_ref, base_ref, velocity_ref):
    comps, size_x, size_y, size_z = base_ref.shape
    lane, sub = lane_ids(size_y), row_ids(size_y)
    top = top_ref[0:size_y]
    for c in range(comps):
        at = count + c * ROWS_Y
        lines = below(y1_ref, y2_ref, slice(at, at + size_x))
        for x in range(size_x):
            here = grid_ref[c, x + 1, 0:size_y]
            before = jnp.where(sub == 0, 0.0, pltpu.roll(here, 1, 0))
            laplace = grid_ref[c, x, 0:size_y] + grid_ref[c, x + 2, 0:size_y]
            laplace = laplace + grid_ref[c, x + 1, 1 : size_y + 1] + before
            ahead = jnp.where(lane == size_z - 1, turned(top, size_z - 1 - (PACK * c + x)), turned(here, -1))
            laplace = laplace + ahead + jnp.where(lane == 0, 0.0, turned(here, 1)) - 6.0 * here
            total = here + diffuse * laplace + push * deposit_ref[c, x, 0:size_y]
            line = jnp.broadcast_to(lines[x : x + 1], (size_y, LANES))
            base_ref[c, x] = total + jnp.where(sub == 0, line, 0.0)
        velocity_ref[c] = state_ref[pl.ds(c, velocity_ref.shape[1], stride=STATE)]


def below(first_ref, second_ref, rows):
    got = jnp.where(jnp.full((1, LANES), odd("gy")) == 1, first_ref[rows], second_ref[rows])
    return jnp.where(jnp.full((1, LANES), lax.axis_index("gy")) != 0, got, 0.0)


def relay_kernel(size_x, size_y, comps, count, first_ref, second_ref, x_in_ref, z_in_ref, leaving_ref, x_ref, z_ref, edge_ref):
    edge = comps * size_y
    x_ref[0:edge] = x_in_ref[...]
    for c in range(comps):
        at = count + c * ROWS_Y + size_x
        spot = slice(c * size_y, c * size_y + 1)
        x_ref[spot] = x_in_ref[spot] + below(first_ref, second_ref, slice(at, at + 1))
    x_ref[edge : edge + count] = leaving_ref[0]
    if x_ref.shape[0] > edge + count:
        x_ref[edge + count : edge + 2 * count] = leaving_ref[1]
    at = count + size_x + 1
    edge_ref[size_y:] = jnp.zeros((edge_ref.shape[0] - size_y, LANES), jnp.float32)
    edge_ref[0:size_y] = z_in_ref[...]
    edge_ref[0:1] = z_in_ref[0:1] + below(first_ref, second_ref, slice(at, at + 1))
    up = odd("gz")
    z_ref[up, 0:count] = leaving_ref[4]
    z_ref[up, count : count + size_y] = edge_ref[0:size_y]
    z_ref[1 - up, 0:count] = leaving_ref[5]
    z_ref[1 - up, count : count + size_y] = jnp.zeros((size_y, LANES), jnp.float32)


def finish_kernel(
    count, base_ref, y1_ref, y2_ref, x_ref, minus_x_ref, z1_ref, z2_ref, edge_ref, gas_out, arrivals_out,
    gas_ref, arrivals_ref, sems,
):
    comps, size_x, size_y, _ = base_ref.shape
    first_lane = lane_ids(size_y) == 0
    odd_y, odd_z = jnp.full((1, LANES), odd("gy")) == 1, jnp.full((1, LANES), odd("gz")) == 1
    place = jnp.full((1, LANES), lax.axis_index("gy"))
    lower, upper = place != 0, place != lax.axis_size("gy") - 1
    rows = slice(count, count + size_y)
    slots = arrivals_ref.shape[2]
    for i in range(arrivals_ref.shape[1]):

        def rows_of(ref, at=0):
            return ref[at + i * slots : at + (i + 1) * slots]

        arrivals_ref[0, i] = rows_of(x_ref, comps * size_y)
        arrivals_ref[1, i] = rows_of(minus_x_ref, minus_x_ref.shape[0] - count)
        y1, y2 = rows_of(y1_ref), rows_of(y2_ref)
        arrivals_ref[2, i] = jnp.where(lower, jnp.where(odd_y, y1, y2), 0.0)
        arrivals_ref[3, i] = jnp.where(upper, jnp.where(odd_y, y2, y1), 0.0)
        z1, z2 = rows_of(z1_ref), rows_of(z2_ref)
        arrivals_ref[4, i] = jnp.where(odd_z, z1, z2)
        arrivals_ref[5, i] = jnp.where(odd_z, z2, z1)
    copies = [pltpu.make_async_copy(arrivals_ref, arrivals_out, sems.at[comps])]
    copies[0].start()
    face = jnp.where(odd_z, z1_ref[rows], z2_ref[rows])
    corner = edge_ref[0:size_y]
    for c in range(comps):
        for x in range(size_x):
            total = base_ref[c, x]
            far = turned(face, -(PACK * c + x))
            if x == 0:
                total = total + x_ref[c * size_y : (c + 1) * size_y]
                far = far + turned(corner, -(PACK * c + size_x))
            gas_ref[c, x] = total + jnp.where(first_lane, far, 0.0)
        copies.append(pltpu.make_async_copy(gas_ref.at[c], gas_out.at[c], sems.at[c]))
        copies[-1].start()
    for copy in copies:
        copy.wait()


def per_device(gas_field, velocity, fraction, response, cell_index, brick_index, crossing):
    comps, size_x, size_y, size_z = gas_field.shape
    nblocks = velocity.shape[0]
    loading = 0.5 * size_x * size_y * size_z / (nblocks * 128)
    push, diffuse = -TIME_STEP * loading, TIME_STEP * VISCOSITY
    velocity = jnp.transpose(velocity, (1, 0, 2))
    fraction = jnp.transpose(fraction, (1, 0, 2))
    spare = nblocks + 8
    rows_z = size_z + 8
    grid_shape = (comps, size_x + 2, ROWS_Y, LANES)
    lines_shape = ((size_x // BX) * (size_y // BY) * comps * rows_z, LANES)
    deposit_shape = ((size_x // BX) * (size_y // BY) * rows_z, LANES)

    inputs = (gas_field, velocity, fraction, response, cell_index, brick_index, crossing)
    inputs = [pltpu.with_memory_space_constraint(array, pltpu.HBM) for array in inputs]
    grid, face, plane, velocity, fraction, response, cell_index, brick_index, crossing = call(
        begin_kernel,
        [grid_shape, (size_y, LANES), (comps * size_y, LANES)]
        + [jax.ShapeDtypeStruct(array.shape, array.dtype) for array in inputs[1:]],
        *inputs, hbm=range(7), scratch=(pltpu.SemaphoreType.DMA((7,)),), limit=40,
    )
    from_z = moved_along(face, "gz", -1)
    from_x = moved_along(plane, "gx", -1)
    from_xz = moved_diagonally(face, -1)
    lines, deposit, table, ready, blocks = call(
        prepare_kernel,
        [
            lines_shape,
            deposit_shape,
            (TABLE_ROWS * spare, LANES),
            (8, LANES),
            jax.ShapeDtypeStruct((2 * (nblocks + UNROLL) + 2,), jnp.int32),
        ],
        grid, velocity, fraction, response, cell_index, brick_index,
        smem=(5,), smem_outs=(4,), cycles=3000,
    )
    line_rows = -(-(comps * size_x + comps + 1) // 8) * 8
    (y_lines,) = call(y_lines_kernel, [(line_rows, LANES)], grid, from_z, from_x, from_xz, ready)
    y1, y2 = swapped_y((y_lines, y_lines))
    square = pltpu.VMEM((LANES, LANES), jnp.float32)
    scalars = (pltpu.SMEM(blocks.shape, jnp.int32), pltpu.SMEM(brick_index.shape, jnp.int32))
    dims = (comps, size_x // BX, size_y // BY, size_z // BZ, rows_z)
    slots = crossing.shape[1]
    count = 7 * slots

    def parts(many):
        return [(many, 2 * comps * REACH_Z, LANES), (many, 2 * LANES, LANES)]

    state, push_parts, spread_parts, grid, lines, top = call(
        functools.partial(gather_kernel, dims),
        [(STATE * spare, LANES)]
        + [jax.ShapeDtypeStruct(shape, jnp.bfloat16) for shape in parts(nblocks + UNROLL)]
        + [grid_shape, lines_shape, (LANES, LANES)],
        blocks, brick_index, table, grid, lines, from_z, from_x, from_xz,
        aliases={3: 3, 4: 4}, cycles=4000, scratch=(*scalars, square, pltpu.SemaphoreType.DMA((2,))),
    )
    grid, lines, state, deposit, leaving = call(
        functools.partial(late_kernel, dims, slots),
        [grid_shape, lines_shape, (STATE * spare, LANES), deposit_shape, (6 * count, LANES)],
        blocks, brick_index, crossing, table, grid, lines, top, y1, y2, state, deposit,
        aliases={4: 0, 5: 1, 9: 2, 10: 3}, cycles=2000,
        scratch=[
            *(pltpu.VMEM(shape, jnp.bfloat16) for shape in parts(UNROLL)),
            *scalars,
            pltpu.SMEM(crossing.shape, jnp.int32),
            square,
            pltpu.SemaphoreType.DMA((3,)),
        ],
    )
    leaving = leaving.reshape(6, count, LANES)
    height = comps * SPREAD
    to_y, top_tiles = call(
        functools.partial(send_y_kernel, push, diffuse),
        [(2, count + comps * ROWS_Y, LANES), ((size_x // BX) * height, LANES)],
        leaving, grid, deposit, cycles=300, scratch=(pltpu.VMEM((comps * ROWS_Y, LANES), jnp.float32),),
    )
    y1, y2 = swapped_y((to_y[0], to_y[1]))
    (deposit,) = call(
        functools.partial(deposit_kernel, dims), [deposit_shape], blocks, brick_index, push_parts, spread_parts, deposit,
        smem=(0, 1), aliases={4: 0}, cycles=4000,
    )
    deposit, over = call(
        merge_kernel, [(comps, size_x + 1, ROWS_Y, LANES), (ROWS_Y, LANES)], deposit, top_tiles,
        cycles=1000, scratch=(pltpu.VMEM(((size_x // BX) * (size_y // BY) * height, LANES), jnp.float32), square),
    )
    to_x, to_z = call(
        functools.partial(send_xz_kernel, push, diffuse), [(comps * size_y, LANES), (size_y, LANES)],
        grid, deposit, over, cycles=500,
    )
    base, velocity_next = call(
        functools.partial(base_kernel, push, diffuse, count), [gas_field.shape, (comps, nblocks, LANES)],
        grid, deposit, top, y1, y2, state, cycles=1000,
    )
    edge = comps * size_y
    both = lax.axis_size("gx") == 2
    to_x, to_z, to_xz = call(
        functools.partial(relay_kernel, size_x, size_y, comps, count),
        [(edge + (2 if both else 1) * count, LANES), (2, count + size_y, LANES), (count + size_y + 8, LANES)],
        y1, y2, to_x, to_z, leaving,
    )
    got_x = moved_along(to_x, "gx", 1)
    z1, z2 = swapped_z((to_z[0], to_z[1]))
    got_xz = moved_diagonally(to_xz, 1)
    got_mx = got_x if both else moved_along(leaving[1], "gx", -1)
    gas_next, arrivals = call(
        functools.partial(finish_kernel, count), [gas_field.shape, (6, 7, slots, LANES)],
        base, y1, y2, got_x, got_mx, z1, z2, got_xz, hbm_outs=(0, 1),
        scratch=(
            pltpu.VMEM(gas_field.shape, jnp.float32),
            pltpu.VMEM((6, 7, slots, LANES), jnp.float32),
            pltpu.SemaphoreType.DMA((comps + 1,)),
        ),
    )
    return gas_next, jnp.transpose(velocity_next, (1, 0, 2)), jnp.transpose(arrivals, (0, 2, 1, 3))


def solution(mesh):
    owner = ("gx", "gz", "gy")
    in_specs = (
        P(None, "gx", "gy", "gz"),
        P(owner, None, None),
        P(owner, None, None),
        P(owner, None),
        P(owner, None),
        P(owner),
        P(owner, None),
    )
    out_specs = (
        P(None, "gx", "gy", "gz"),
        P(owner, None, None),
        P(owner, None, None, None),
    )
    return jax.shard_map(
        per_device, mesh=mesh, in_specs=in_specs, out_specs=out_specs, check_vma=False
    )
```

```python
import functools

import jax
import jax.numpy as jnp
from jax import lax
from jax.experimental import pallas as pl
from jax.experimental.pallas import tpu as pltpu
from jax.sharding import PartitionSpec as P

BX = 4
BY = 4
BZ = 8

TIME_STEP = 0.25
VISCOSITY = 0.4

LANES = 128
PACK = 32
ROWS_Y = 24
REACH_X = BX + 1
REACH_Y = 8
SPREAD = REACH_X * REACH_Y
REACH_Z = 2 * BZ
UNROLL = 8

WEIGHT, ALONG_Y, IN_Y, ALONG_Z, IN_Z, RESPONSE, MOVING, OFFSET = 0, 5, 6, 7, 8, 9, 10, 13
TABLE_ROWS = 16
STATE = 8

VMEM = pl.BlockSpec(memory_space=pltpu.VMEM)
SMEM = pl.BlockSpec(memory_space=pltpu.SMEM)
HBM = pl.BlockSpec(memory_space=pltpu.HBM)


def moved_along(block, axis, distance):
    count = lax.axis_size(axis)
    return lax.ppermute(block, axis, [(i, (i + distance) % count) for i in range(count)])


def swapped_z(blocks):
    count = lax.axis_size("gz")
    first = [(i, i ^ 1) for i in range(count)]
    second = [(i, (((i + 1) ^ 1) - 1) % count) for i in range(count)]
    return lax.ppermute(blocks[0], "gz", first), lax.ppermute(blocks[1], "gz", second)


def swapped_y(blocks):
    nz, ny = lax.axis_size("gz"), lax.axis_size("gy")
    first = [(j, j ^ 1) for j in range(ny)]
    second = []
    for k in range(nz):
        second.append((k * ny, (k ^ 1) * ny))
        second.append((k * ny + ny - 1, (k ^ 1) * ny + ny - 1))
        second.extend((k * ny + j, k * ny + ((j + 1) ^ 1) - 1) for j in range(1, ny - 1))
    middle = lax.ppermute(blocks[1], ("gz", "gy"), second)
    return lax.ppermute(blocks[0], "gy", first), middle


def moved_diagonally(block, distance):
    nx, nz = lax.axis_size("gx"), lax.axis_size("gz")
    route = [(i * nz + k, (i + distance) % nx * nz + (k + distance) % nz) for i in range(nx) for k in range(nz)]
    return lax.ppermute(block, ("gx", "gz"), route)


def call(
    body, outs, *operands, smem=(), hbm=(), smem_outs=(), hbm_outs=(), scratch=(), aliases=None, cycles=0, limit=40
):
    return pl.pallas_call(
        body,
        out_shape=[o if isinstance(o, jax.ShapeDtypeStruct) else jax.ShapeDtypeStruct(o, jnp.float32) for o in outs],
        in_specs=[SMEM if i in smem else HBM if i in hbm else VMEM for i in range(len(operands))],
        out_specs=[SMEM if i in smem_outs else HBM if i in hbm_outs else VMEM for i in range(len(outs))],
        scratch_shapes=list(scratch),
        input_output_aliases=aliases or {},
        compiler_params=pltpu.CompilerParams(vmem_limit_bytes=limit * 1024 * 1024),
        cost_estimate=pl.CostEstimate(flops=cycles * 4096, bytes_accessed=cycles * 1024, transcendentals=0),
    )(*operands)


def lane_ids(rows):
    return lax.broadcasted_iota(jnp.int32, (rows, LANES), 1)


def row_ids(rows):
    return lax.broadcasted_iota(jnp.int32, (rows, LANES), 0)


def turned(value, shift):
    shift = shift % LANES
    return pltpu.roll(value, shift, 1) if shift else value


def odd(axis):
    return lax.axis_index(axis) % 2


def begin_kernel(
    gas_ref, velocity_in, fraction_in, response_in, cell_in, brick_in, crossing_in,
    grid_ref, face_ref, plane_ref, velocity_ref, fraction_ref, response_ref, cell_ref, brick_ref, crossing_ref, sems,
):
    comps, size_x, size_y, _ = gas_ref.shape
    pairs = [
        (gas_ref, grid_ref.at[:, 1 : size_x + 1, 0:size_y]),
        (velocity_in, velocity_ref), (fraction_in, fraction_ref), (response_in, response_ref),
        (cell_in, cell_ref), (brick_in, brick_ref), (crossing_in, crossing_ref),
    ]
    copies = [pltpu.make_async_copy(source, target, sems.at[i]) for i, (source, target) in enumerate(pairs)]
    for copy in copies:
        copy.start()
    zeros = jnp.zeros((ROWS_Y, LANES), jnp.float32)
    for c in range(comps):
        grid_ref[c, 0] = zeros
        grid_ref[c, size_x + 1] = zeros
        for x in range(size_x):
            grid_ref[c, x + 1, size_y:] = zeros[size_y:]
    copies[0].wait()
    lane = lane_ids(size_y)
    face = jnp.zeros((size_y, LANES), jnp.float32)
    for c in range(comps):
        plane_ref[c * size_y : (c + 1) * size_y] = grid_ref[c, 1, 0:size_y]
        for x in range(size_x):
            place = PACK * c + x
            face = jnp.where(lane == place, turned(grid_ref[c, x + 1, 0:size_y], place), face)
    face_ref[...] = face
    for copy in copies[1:]:
        copy.wait()


def parts_of(value):
    main = value.astype(jnp.bfloat16).astype(jnp.float32)
    return main, value - main


def lay_out(grid_ref, lines_ref, p, q, size_y, size_z):
    comps = grid_ref.shape[0]
    rows_z = size_z + 8
    count_y = size_y // BY
    for c in range(comps):
        planes = [grid_ref[c, p * BX + a + 1, q * BY : q * BY + REACH_Y] for a in range(REACH_X)]
        main, rest = parts_of(jnp.concatenate(planes, axis=0))
        stack = jnp.concatenate([main, rest, main, jnp.zeros((LANES - 3 * SPREAD, LANES), jnp.float32)], axis=0)
        at = ((p * count_y + q) * comps + c) * rows_z
        lines_ref[at : at + size_z] = jnp.transpose(stack)


def lay_out_top(turned_ref, lines_ref, q, comps, count_x, count_y, size_z):
    lane = lane_ids(count_x)
    rows_z = size_z + 8
    for c in range(comps):
        total = jnp.zeros((count_x, LANES), jnp.float32)
        for a in range(REACH_X):
            rows = turned_ref[pl.ds(PACK * c + a, count_x, stride=BX)]
            total = jnp.where(lane // REACH_Y == a, turned(rows, a * REACH_Y - q * BY), total)
        main, rest = parts_of(total)
        line = main + turned(rest, SPREAD) + turned(main, 2 * SPREAD)
        for p in range(count_x):
            at = ((p * count_y + q) * comps + c) * rows_z + size_z
            lines_ref[at : at + 1] = line[p : p + 1]


def prepare_kernel(
    grid_ref, velocity_ref, fraction_ref, response_ref, cell_ref, brick_ref,
    lines_ref, deposit_ref, table_ref, ready_ref, list_ref,
):
    comps, size_x, size_y, size_z = grid_ref.shape[0], grid_ref.shape[1] - 2, grid_ref.shape[2] - 8, grid_ref.shape[3]
    nblocks = velocity_ref.shape[1]
    count_x, count_y, count_z = size_x // BX, size_y // BY, size_z // BZ
    rows_z = size_z + 8

    room = nblocks + UNROLL

    def visit(k, counts):
        late = jnp.where(lax.rem(lax.div(brick_ref[k], count_z), count_y) == count_y - 1, 1, 0)
        list_ref[jnp.where(late == 1, room + counts[1], counts[0])] = k
        return counts[0] + 1 - late, counts[1] + late

    early, late = lax.fori_loop(0, nblocks, visit, (jnp.int32(0), jnp.int32(0)), unroll=8)
    for base, count in ((0, early), (room, late)):
        for u in range(UNROLL):
            list_ref[base + count + u] = nblocks
    list_ref[2 * room] = early
    list_ref[2 * room + 1] = late
    ready_ref[...] = jnp.zeros_like(ready_ref)

    deposit_ref[...] = jnp.zeros_like(deposit_ref)
    for p in range(count_x):
        for q in range(count_y):
            for c in range(comps):
                at = ((p * count_y + q) * comps + c) * rows_z + size_z
                lines_ref[at : at + 8] = jnp.zeros((8, LANES), jnp.float32)
    for p in range(count_x - 1):
        for q in range(count_y - 1):
            lay_out(grid_ref, lines_ref, p, q, size_y, size_z)

    cells = cell_ref[...]
    cell_x, cell_y, cell_z = cells // (BY * BZ), cells // BZ % BY, cells % BZ
    along_x = fraction_ref[0]

    def put(row, value):
        table_ref[pl.ds(row, nblocks, stride=TABLE_ROWS)] = value

    for a in range(REACH_X):
        put(WEIGHT + a, jnp.where(cell_x == a, 1.0 - along_x, 0.0) + jnp.where(cell_x == a - 1, along_x, 0.0))
    put(ALONG_Y, fraction_ref[1])
    put(IN_Y, cell_y.astype(jnp.float32))
    put(ALONG_Z, fraction_ref[2])
    put(IN_Z, cell_z.astype(jnp.float32))
    put(RESPONSE, response_ref[...])
    for c in range(comps):
        put(MOVING + c, velocity_ref[c])
        put(OFFSET + c, fraction_ref[c])
    spare = table_ref.shape[0] - nblocks * TABLE_ROWS
    row = row_ids(spare)
    table_ref[nblocks * TABLE_ROWS :] = jnp.where(row % TABLE_ROWS == RESPONSE, 1.0, 0.0)


def y_lines_kernel(grid_ref, face_ref, from_x_ref, edge_ref, ready_ref, first_ref, second_ref):
    comps, size_x = grid_ref.shape[0], grid_ref.shape[1] - 2
    size_y = face_ref.shape[0]
    for out_ref in (first_ref, second_ref):
        for c in range(comps):
            out_ref[c * size_x : (c + 1) * size_x] = grid_ref[c, 1 : size_x + 1, 0]
            out_ref[comps * size_x + c : comps * size_x + c + 1] = from_x_ref[c * size_y : c * size_y + 1]
        line = jnp.where(lane_ids(8) % PACK == size_x, turned(edge_ref[0:8], size_x), face_ref[0:8])
        out_ref[comps * size_x + comps : comps * size_x + comps + 1] = line[0:1]


def halo_xz_kernel(grid_in_ref, lines_in_ref, face_ref, from_x_ref, edge_ref, grid_ref, lines_ref, top_ref, turned_ref):
    comps, size_x = grid_ref.shape[0], grid_ref.shape[1] - 2
    size_y, size_z = face_ref.shape[0], grid_ref.shape[3]
    count_x, count_y = size_x // BX, size_y // BY
    for c in range(comps):
        grid_ref[c, size_x + 1, 0:size_y] = from_x_ref[c * size_y : (c + 1) * size_y]
    for q in range(count_y - 1):
        lay_out(grid_ref, lines_ref, count_x - 1, q, size_y, size_z)
    top = jnp.where(lane_ids(size_y) % PACK == size_x, turned(edge_ref[...], size_x), face_ref[...])
    top_ref[0:size_y] = top
    top_ref[size_y:] = jnp.zeros((LANES - size_y, LANES), jnp.float32)
    turned_ref[...] = jnp.transpose(top_ref[...])
    for q in range(count_y - 1):
        lay_out_top(turned_ref, lines_ref, q, comps, count_x, count_y, size_z)


def halo_y_kernel(size_y, grid_in_ref, lines_in_ref, top_in_ref, first_ref, second_ref, grid_ref, lines_ref, turned_ref):
    comps, size_x, size_z = grid_ref.shape[0], grid_ref.shape[1] - 2, grid_ref.shape[3]
    count_x, count_y = size_x // BX, size_y // BY
    inside = lax.axis_index("gy") != lax.axis_size("gy") - 1
    kept = (row_ids(8) == 0) & inside
    even = jnp.full((1, LANES), odd("gy")) == 0

    def line_at(row):
        line = jnp.where(even, first_ref[row : row + 1], second_ref[row : row + 1])
        return jnp.where(kept, jnp.broadcast_to(line, (8, LANES)), 0.0)

    for c in range(comps):
        for x in range(size_x + 1):
            grid_ref[c, x + 1, size_y:] = line_at(c * size_x + x if x < size_x else comps * size_x + c)
    for p in range(count_x):
        lay_out(grid_ref, lines_ref, p, count_y - 1, size_y, size_z)
    corner = line_at(comps * size_x + comps)
    rest = jnp.zeros((LANES - size_y - 8, LANES), jnp.float32)
    turned_ref[...] = jnp.transpose(jnp.concatenate([top_in_ref[0:size_y], corner, rest], axis=0))
    lay_out_top(turned_ref, lines_ref, count_y - 1, comps, count_x, count_y, size_z)


def block_steps(dims, list_ref, brick_ref):
    comps, _, count_y, count_z, rows_z = dims
    nblocks = brick_ref.shape[0]
    sub = row_ids(8)
    row_y = row_ids(REACH_Y).astype(jnp.float32)
    row_z = row_ids(REACH_Z).astype(jnp.float32)
    lanes = lane_ids(REACH_Z)

    def hat(rows, inside, along):
        return jnp.where(rows == inside, 1.0 - along, 0.0) + jnp.where(rows == inside + 1.0, along, 0.0)

    def place_of(at):
        k = list_ref[at]
        brick = jnp.where(k < nblocks, brick_ref[jnp.minimum(k, nblocks - 1)], 0)
        brick_x = lax.div(brick, count_y * count_z)
        brick_y = lax.rem(lax.div(brick, count_z), count_y)
        return k, brick_x * count_y + brick_y, lax.rem(brick, count_z)

    def loaded(at, lines_ref, table_ref):
        k, pair, brick_z = place_of(at)
        first = pl.multiple_of(pair * comps * rows_z + brick_z * BZ, 8)
        window = jnp.concatenate([lines_ref[pl.ds(first + c * rows_z, REACH_Z)] for c in range(comps)], axis=0)
        table = table_ref[pl.ds(pl.multiple_of(k * TABLE_ROWS, TABLE_ROWS), TABLE_ROWS)]
        return k, window, [table[i : i + 1] for i in range(TABLE_ROWS)]

    def weighted(rows):
        weight_y = hat(row_y, rows[IN_Y], rows[ALONG_Y])
        weight_z = hat(row_z, rows[IN_Z], rows[ALONG_Z])
        weight = jnp.concatenate([rows[WEIGHT + a] * weight_y for a in range(REACH_X)], axis=0)
        return weight_z, *parts_of(weight)

    def stepped(seen, weight_z, rows):
        rate = 1.0 / rows[RESPONSE]
        state, moved, pushed = [], [], []
        for c in range(comps):
            gas_sample = jnp.sum(seen[c * REACH_Z : (c + 1) * REACH_Z] * weight_z, axis=0, keepdims=True)
            drag = (gas_sample - rows[MOVING + c]) * rate
            state.append(rows[MOVING + c] + TIME_STEP * drag)
            moved.append(rows[OFFSET + c] + TIME_STEP * state[c])
            pushed.append(drag * weight_z)
        tile = jnp.broadcast_to(rows[RESPONSE], (STATE, LANES))
        for i, value in enumerate(state + moved):
            tile = jnp.where(sub == i, value, tile)
        return tile, jnp.concatenate(parts_of(jnp.concatenate(pushed, axis=0)), axis=0)

    def gathered(one, two):
        tables, windows, weights = [], [], []
        for _, window, rows in (one, two):
            weight_z, main, rest = weighted(rows)
            weights.append((weight_z, main, rest))
            unused = jnp.zeros((LANES - 3 * SPREAD, LANES), jnp.float32)
            tables.append(jnp.concatenate([main, main, rest, unused], axis=0).astype(jnp.bfloat16))
            windows.append(window)
        seen = lax.dot_general(
            jnp.concatenate(windows, axis=0).astype(jnp.bfloat16), jnp.concatenate(tables, axis=1),
            (((1,), (0,)), ((), ())), preferred_element_type=jnp.float32,
        )
        height = comps * REACH_Z
        tiles, fresh = [], []
        for i, (_, _, rows) in enumerate((one, two)):
            weight_z, main, rest = weights[i]
            mine = seen[i * height : (i + 1) * height, i * LANES : (i + 1) * LANES]
            tile, push = stepped(mine, weight_z, rows)
            tiles.append(tile)
            fresh.append((push.astype(jnp.bfloat16), jnp.concatenate([main, rest], axis=0).astype(jnp.bfloat16)))
        return tiles, fresh

    def shared(one, two):
        gap = jnp.zeros((LANES - 2 * SPREAD, LANES), jnp.bfloat16)
        shares = lax.dot_general(
            jnp.concatenate([one[0], two[0]], axis=0), jnp.concatenate([one[1], gap, two[1], gap], axis=0),
            (((1,), (1,)), ((), ())), preferred_element_type=jnp.float32,
        )
        height = comps * REACH_Z
        results = []
        for i in (0, 1):
            mine = shares[2 * i * height : 2 * (i + 1) * height, i * LANES : (i + 1) * LANES]
            mine = mine[:height] + mine[height:]
            first, second, third = (mine[c * REACH_Z : (c + 1) * REACH_Z] for c in range(comps))
            across = turned(jnp.where(lanes < SPREAD, second, third), SPREAD)
            far = jnp.where(lanes < 2 * SPREAD, second, turned(third, 2 * SPREAD)) + across
            results.append(jnp.where(lanes < SPREAD, first + turned(first, -SPREAD), far))
        return results

    def add(deposit_ref, at, shares):
        spots = []
        for u in range(len(shares)):
            _, pair, brick_z = place_of(at + u)
            spots.append(pl.ds(pl.multiple_of(pair * rows_z + brick_z * BZ, 8), REACH_Z))
        for spot, share in zip(spots, shares):
            deposit_ref[spot] = deposit_ref[spot] + share

    def group_of(taken):
        tiles, fresh = [], []
        for u in range(0, UNROLL, 2):
            both, kept = gathered(taken[u], taken[u + 1])
            tiles.extend(both)
            fresh.extend(kept)
        return tiles, fresh

    def keep(state_ref, taken, tiles):
        for (k, _, _), tile in zip(taken, tiles):
            state_ref[pl.ds(pl.multiple_of(STATE * k, STATE), STATE)] = tile

    def deposits_of(kept):
        results = []
        for u in range(0, UNROLL, 2):
            results.extend(shared(kept[u], kept[u + 1]))
        return results

    return loaded, group_of, keep, deposits_of, add


def groups_in(list_ref, late):
    room = (list_ref.shape[0] - 2) // 2
    return late * room, (list_ref[2 * room + late] + UNROLL - 1) // UNROLL


def fetched(sems, *pairs):
    copies = [pltpu.make_async_copy(source, target, sems.at[i]) for i, (source, target) in enumerate(pairs)]
    for copy in copies:
        copy.start()
    return copies


def gather_kernel(
    dims, list_in, brick_in, table_ref, grid_in_ref, lines_in_ref, face_ref, from_x_ref, edge_ref,
    state_ref, push_ref, spread_ref, grid_ref, lines_ref, top_ref, list_ref, brick_ref, turned_ref, sems,
):
    copies = fetched(sems, (list_in, list_ref), (brick_in, brick_ref))
    halo_xz_kernel(grid_in_ref, lines_in_ref, face_ref, from_x_ref, edge_ref, grid_ref, lines_ref, top_ref, turned_ref)
    for copy in copies:
        copy.wait()
    loaded, group_of, keep, _, _ = block_steps(dims, list_ref, brick_ref)
    base, groups = groups_in(list_ref, 0)

    @pl.loop(0, groups)
    def _(group):
        taken = [loaded(base + group * UNROLL + u, lines_ref, table_ref) for u in range(UNROLL)]
        tiles, fresh = group_of(taken)
        keep(state_ref, taken, tiles)
        for i, (push, spread) in enumerate(fresh):
            push_ref[group * UNROLL + i] = push
            spread_ref[group * UNROLL + i] = spread


def deposit_kernel(dims, list_ref, brick_ref, push_ref, spread_ref, deposit_in_ref, deposit_ref):
    _, _, _, deposits_of, add = block_steps(dims, list_ref, brick_ref)
    base, groups = groups_in(list_ref, 0)

    @pl.loop(0, groups)
    def _(group):
        mine = [group * UNROLL + i for i in range(UNROLL)]
        add(deposit_ref, base + group * UNROLL, deposits_of([(push_ref[i], spread_ref[i]) for i in mine]))


def late_kernel(
    dims, slots, list_in, brick_in, crossing_in, table_ref, grid_in_ref, lines_in_ref, top_in_ref, first_ref, second_ref,
    state_in_ref, deposit_in_ref,
    grid_ref, lines_ref, state_ref, deposit_ref, leaving_ref,
    push_ref, spread_ref, list_ref, brick_ref, crossing_ref, turned_ref, sems,
):
    copies = fetched(sems, (list_in, list_ref), (brick_in, brick_ref), (crossing_in, crossing_ref))
    halo_y_kernel(
        dims[2] * BY, grid_in_ref, lines_in_ref, top_in_ref, first_ref, second_ref, grid_ref, lines_ref, turned_ref
    )
    for copy in copies:
        copy.wait()
    loaded, group_of, keep, deposits_of, add = block_steps(dims, list_ref, brick_ref)
    base, groups = groups_in(list_ref, 1)
    push_ref[...] = jnp.zeros_like(push_ref)
    spread_ref[...] = jnp.zeros_like(spread_ref)

    @pl.loop(0, groups + 1)
    def _(group):
        now = base + jnp.maximum(jnp.minimum(group, groups - 1), 0) * UNROLL
        before = base + jnp.maximum(group - 1, 0) * UNROLL
        taken = [loaded(now + u, lines_ref, table_ref) for u in range(UNROLL)]
        shares = deposits_of([(push_ref[i], spread_ref[i]) for i in range(UNROLL)])
        tiles, fresh = group_of(taken)
        add(deposit_ref, before, shares)
        keep(state_ref, taken, tiles)
        for i, (push, spread) in enumerate(fresh):
            push_ref[i] = push
            spread_ref[i] = spread

    rows = leaving_ref.shape[0] // (6 * slots)
    for face in range(6):
        tiles = []
        for slot in range(slots):
            block = crossing_ref[face, slot]
            spot = pl.ds(pl.multiple_of(jnp.maximum(block, 0) * STATE, STATE), STATE)
            live = jnp.full((STATE, LANES), block, jnp.int32) >= 0
            tiles.append(jnp.where(live, state_ref[spot], 0.0))
        for slot, tile in enumerate(tiles):
            leaving_ref[pl.ds(face * rows * slots + slot, rows, stride=slots)] = tile[:rows]


def top_rows(deposit_ref, q, count_x, count_y, rows_z, size_z):
    total = None
    for p in range(count_x):
        at = (p * count_y + q) * rows_z + size_z
        value = pltpu.roll(deposit_ref[at : at + 8], p, 0) if p else deposit_ref[at : at + 8]
        total = value if total is None else total + value
    return total


def send_y_kernel(push, diffuse, leaving_ref, grid_ref, deposit_ref, y1_ref, y2_ref, tiles_ref, lines_ref):
    comps, size_x, size_y, size_z = grid_ref.shape[0], grid_ref.shape[1] - 2, grid_ref.shape[2] - 8, grid_ref.shape[3]
    count_x, count_y = size_x // BX, size_y // BY
    rows_z = size_z + 8
    rows = leaving_ref.shape[1]
    height = comps * SPREAD
    for p in range(count_x):
        at = (p * count_y + count_y - 1) * rows_z
        tiles_ref[p * height : (p + 1) * height] = jnp.transpose(deposit_ref[at : at + size_z])[:height]
    first = jnp.full((rows, LANES), odd("gy")) == 0
    y1_ref[0:rows] = jnp.where(first, leaving_ref[2], leaving_ref[3])
    y2_ref[0:rows] = jnp.where(first, leaving_ref[3], leaving_ref[2])
    lines_ref[...] = jnp.zeros_like(lines_ref)
    for c in range(comps):
        for p in range(count_x):
            spot = slice(c * ROWS_Y + p * BX, c * ROWS_Y + p * BX + REACH_X)
            line = tiles_ref[pl.ds(p * height + c * SPREAD + BY, REACH_X, stride=REACH_Y)]
            lines_ref[spot] = lines_ref[spot] + line
    wrapped = top_rows(deposit_ref, count_y - 1, count_x, count_y, rows_z, size_z)
    lane = lane_ids(8)
    packed = jnp.zeros((8, LANES), jnp.float32)
    for c in range(comps):
        spot = slice(c * ROWS_Y, (c + 1) * ROWS_Y)
        beside = jnp.concatenate([grid_ref[c, 1 : size_x + 1, size_y - 1], jnp.zeros((8, LANES), jnp.float32)], axis=0)
        line = push * lines_ref[spot] + diffuse * beside
        for y_ref in (y1_ref, y2_ref):
            y_ref[rows + c * ROWS_Y : rows + (c + 1) * ROWS_Y] = line
        for a in range(REACH_X):
            place = PACK * c + a
            value = turned(wrapped, place - c * SPREAD - a * REACH_Y - BY)
            packed = packed + jnp.where(lane == place, value, 0.0)
    corner = packed[0:1]
    for p in range(1, count_x):
        corner = corner + turned(packed[p : p + 1], p * BX)
    at = rows + size_x + 1
    for y_ref in (y1_ref, y2_ref):
        y_ref[at : at + 1] = push * corner
    y1_ref[y2_ref.shape[0] :] = jnp.zeros((8, LANES), jnp.float32)


def merge_kernel(deposit_ref, top_tiles_ref, plane_ref, face_ref, tiles_ref, turned_ref):
    comps, planes = plane_ref.shape[:2]
    count_x, size_z = (planes - 1) // BX, plane_ref.shape[3]
    rows_z = size_z + 8
    count_y = deposit_ref.shape[0] // (rows_z * count_x)
    height = comps * SPREAD
    for p in range(count_x):
        for q in range(count_y - 1):
            at = p * count_y + q
            value = jnp.transpose(deposit_ref[at * rows_z : at * rows_z + size_z])
            tiles_ref[at * height : (at + 1) * height] = value[:height]
    top = row_ids(REACH_Y) >= BY
    for c in range(comps):
        for x in range(planes):
            bricks = [(x // BX, x % BX)] if x < planes - 1 else []
            if x and x % BX == 0:
                bricks.append((x // BX - 1, BX))

            def tile(q):
                total = None
                for p, a in bricks:
                    at = c * SPREAD + a * REACH_Y
                    if q < count_y - 1:
                        value = tiles_ref[(p * count_y + q) * height + at : (p * count_y + q) * height + at + REACH_Y]
                    else:
                        value = top_tiles_ref[p * height + at : p * height + at + REACH_Y]
                    total = value if total is None else total + value
                return total

            carried = None
            for q in range(0, count_y, 2):
                here = tile(q)
                if carried is not None:
                    here = here + carried
                between = pltpu.roll(tile(q + 1), BY, 0)
                here = here + jnp.where(top, between, 0.0)
                carried = jnp.where(top, 0.0, between)
                plane_ref[c, x, q * BY : q * BY + REACH_Y] = here
            plane_ref[c, x, count_y * BY :] = carried

    lane = lane_ids(count_x)
    turned_ref[...] = jnp.zeros_like(turned_ref)
    for q in range(count_y):
        wrapped = top_rows(deposit_ref, q, count_x, count_y, rows_z, size_z)[:count_x]
        within = (lane >= q * BY) & (lane <= (q + 1) * BY)
        for c in range(comps):
            for a in range(REACH_X):
                value = turned(wrapped, q * BY - c * SPREAD - a * REACH_Y)
                spot = pl.ds(PACK * c + a, count_x, stride=BX)
                turned_ref[spot] = turned_ref[spot] + jnp.where(within, value, 0.0)
    face_ref[...] = jnp.transpose(turned_ref[...])[: face_ref.shape[0]]


def send_xz_kernel(push, diffuse, grid_ref, deposit_ref, face_ref, x_ref, z_ref):
    comps, size_x = grid_ref.shape[0], grid_ref.shape[1] - 2
    size_y = z_ref.shape[0]
    lane = lane_ids(size_y)
    packed = push * face_ref[0:size_y]
    for c in range(comps):
        for x in range(size_x):
            place = PACK * c + x
            packed = packed + jnp.where(lane == place, diffuse * turned(grid_ref[c, x + 1, 0:size_y], place + 1), 0.0)
        total = push * deposit_ref[c, size_x, 0:size_y]
        x_ref[c * size_y : (c + 1) * size_y] = diffuse * grid_ref[c, size_x, 0:size_y] + total
    z_ref[...] = packed


def base_kernel(push, diffuse, count, grid_ref, deposit_ref, top_ref, y1_ref, y2_ref, state_ref, base_ref, velocity_ref):
    comps, size_x, size_y, size_z = base_ref.shape
    lane, sub = lane_ids(size_y), row_ids(size_y)
    top = top_ref[0:size_y]
    for c in range(comps):
        at = count + c * ROWS_Y
        lines = below(y1_ref, y2_ref, slice(at, at + size_x))
        for x in range(size_x):
            here = grid_ref[c, x + 1, 0:size_y]
            before = jnp.where(sub == 0, 0.0, pltpu.roll(here, 1, 0))
            laplace = grid_ref[c, x, 0:size_y] + grid_ref[c, x + 2, 0:size_y]
            laplace = laplace + grid_ref[c, x + 1, 1 : size_y + 1] + before
            ahead = jnp.where(lane == size_z - 1, turned(top, size_z - 1 - (PACK * c + x)), turned(here, -1))
            laplace = laplace + ahead + jnp.where(lane == 0, 0.0, turned(here, 1)) - 6.0 * here
            total = here + diffuse * laplace + push * deposit_ref[c, x, 0:size_y]
            line = jnp.broadcast_to(lines[x : x + 1], (size_y, LANES))
            base_ref[c, x] = total + jnp.where(sub == 0, line, 0.0)
        velocity_ref[c] = state_ref[pl.ds(c, velocity_ref.shape[1], stride=STATE)]


def below(first_ref, second_ref, rows):
    got = jnp.where(jnp.full((1, LANES), odd("gy")) == 1, first_ref[rows], second_ref[rows])
    return jnp.where(jnp.full((1, LANES), lax.axis_index("gy")) != 0, got, 0.0)


def relay_kernel(size_x, size_y, comps, count, first_ref, second_ref, x_in_ref, z_in_ref, leaving_ref, x_ref, z_ref, edge_ref):
    edge = comps * size_y
    x_ref[0:edge] = x_in_ref[...]
    for c in range(comps):
        at = count + c * ROWS_Y + size_x
        spot = slice(c * size_y, c * size_y + 1)
        x_ref[spot] = x_in_ref[spot] + below(first_ref, second_ref, slice(at, at + 1))
    x_ref[edge : edge + count] = leaving_ref[0]
    if x_ref.shape[0] > edge + count:
        x_ref[edge + count : edge + 2 * count] = leaving_ref[1]
    at = count + size_x + 1
    edge_ref[size_y:] = jnp.zeros((edge_ref.shape[0] - size_y, LANES), jnp.float32)
    edge_ref[0:size_y] = z_in_ref[...]
    edge_ref[0:1] = z_in_ref[0:1] + below(first_ref, second_ref, slice(at, at + 1))
    up = odd("gz")
    z_ref[up, 0:count] = leaving_ref[4]
    z_ref[up, count : count + size_y] = edge_ref[0:size_y]
    z_ref[1 - up, 0:count] = leaving_ref[5]
    z_ref[1 - up, count : count + size_y] = jnp.zeros((size_y, LANES), jnp.float32)


def finish_kernel(
    count, base_ref, y1_ref, y2_ref, x_ref, minus_x_ref, z1_ref, z2_ref, edge_ref, gas_out, arrivals_out,
    gas_ref, arrivals_ref, sems,
):
    comps, size_x, size_y, _ = base_ref.shape
    first_lane = lane_ids(size_y) == 0
    odd_y, odd_z = jnp.full((1, LANES), odd("gy")) == 1, jnp.full((1, LANES), odd("gz")) == 1
    place = jnp.full((1, LANES), lax.axis_index("gy"))
    lower, upper = place != 0, place != lax.axis_size("gy") - 1
    rows = slice(count, count + size_y)
    slots = arrivals_ref.shape[2]
    for i in range(arrivals_ref.shape[1]):

        def rows_of(ref, at=0):
            return ref[at + i * slots : at + (i + 1) * slots]

        arrivals_ref[0, i] = rows_of(x_ref, comps * size_y)
        arrivals_ref[1, i] = rows_of(minus_x_ref, minus_x_ref.shape[0] - count)
        y1, y2 = rows_of(y1_ref), rows_of(y2_ref)
        arrivals_ref[2, i] = jnp.where(lower, jnp.where(odd_y, y1, y2), 0.0)
        arrivals_ref[3, i] = jnp.where(upper, jnp.where(odd_y, y2, y1), 0.0)
        z1, z2 = rows_of(z1_ref), rows_of(z2_ref)
        arrivals_ref[4, i] = jnp.where(odd_z, z1, z2)
        arrivals_ref[5, i] = jnp.where(odd_z, z2, z1)
    copies = [pltpu.make_async_copy(arrivals_ref, arrivals_out, sems.at[comps])]
    copies[0].start()
    face = jnp.where(odd_z, z1_ref[rows], z2_ref[rows])
    corner = edge_ref[0:size_y]
    for c in range(comps):
        for x in range(size_x):
            total = base_ref[c, x]
            far = turned(face, -(PACK * c + x))
            if x == 0:
                total = total + x_ref[c * size_y : (c + 1) * size_y]
                far = far + turned(corner, -(PACK * c + size_x))
            gas_ref[c, x] = total + jnp.where(first_lane, far, 0.0)
        copies.append(pltpu.make_async_copy(gas_ref.at[c], gas_out.at[c], sems.at[c]))
        copies[-1].start()
    for copy in copies:
        copy.wait()


def per_device(gas_field, velocity, fraction, response, cell_index, brick_index, crossing):
    comps, size_x, size_y, size_z = gas_field.shape
    nblocks = velocity.shape[0]
    loading = 0.5 * size_x * size_y * size_z / (nblocks * 128)
    push, diffuse = -TIME_STEP * loading, TIME_STEP * VISCOSITY
    velocity = jnp.transpose(velocity, (1, 0, 2))
    fraction = jnp.transpose(fraction, (1, 0, 2))
    spare = nblocks + 8
    rows_z = size_z + 8
    grid_shape = (comps, size_x + 2, ROWS_Y, LANES)
    lines_shape = ((size_x // BX) * (size_y // BY) * comps * rows_z, LANES)
    deposit_shape = ((size_x // BX) * (size_y // BY) * rows_z, LANES)

    inputs = (gas_field, velocity, fraction, response, cell_index, brick_index, crossing)
    inputs = [pltpu.with_memory_space_constraint(array, pltpu.HBM) for array in inputs]
    grid, face, plane, velocity, fraction, response, cell_index, brick_index, crossing = call(
        begin_kernel,
        [grid_shape, (size_y, LANES), (comps * size_y, LANES)]
        + [jax.ShapeDtypeStruct(array.shape, array.dtype) for array in inputs[1:]],
        *inputs, hbm=range(7), scratch=(pltpu.SemaphoreType.DMA((7,)),), limit=40,
    )
    from_z = moved_along(face, "gz", -1)
    from_x = moved_along(plane, "gx", -1)
    from_xz = moved_diagonally(face, -1)
    lines, deposit, table, ready, blocks = call(
        prepare_kernel,
        [
            lines_shape,
            deposit_shape,
            (TABLE_ROWS * spare, LANES),
            (8, LANES),
            jax.ShapeDtypeStruct((2 * (nblocks + UNROLL) + 2,), jnp.int32),
        ],
        grid, velocity, fraction, response, cell_index, brick_index,
        smem=(5,), smem_outs=(4,), cycles=3000,
    )
    line_rows = -(-(comps * size_x + comps + 1) // 8) * 8
    y_lines = call(
        y_lines_kernel, [(line_rows + 8, LANES), (line_rows, LANES)], grid, from_z, from_x, from_xz, ready
    )
    y1, y2 = swapped_y(y_lines)
    square = pltpu.VMEM((LANES, LANES), jnp.float32)
    scalars = (pltpu.SMEM(blocks.shape, jnp.int32), pltpu.SMEM(brick_index.shape, jnp.int32))
    dims = (comps, size_x // BX, size_y // BY, size_z // BZ, rows_z)
    slots = crossing.shape[1]
    count = 7 * slots

    def parts(many):
        return [(many, 2 * comps * REACH_Z, LANES), (many, 2 * SPREAD, LANES)]

    state, push_parts, spread_parts, grid, lines, top = call(
        functools.partial(gather_kernel, dims),
        [(STATE * spare, LANES)]
        + [jax.ShapeDtypeStruct(shape, jnp.bfloat16) for shape in parts(nblocks + UNROLL)]
        + [grid_shape, lines_shape, (LANES, LANES)],
        blocks, brick_index, table, grid, lines, from_z, from_x, from_xz,
        aliases={3: 3, 4: 4}, cycles=4000, scratch=(*scalars, square, pltpu.SemaphoreType.DMA((2,))),
    )
    grid, lines, state, deposit, leaving = call(
        functools.partial(late_kernel, dims, slots),
        [grid_shape, lines_shape, (STATE * spare, LANES), deposit_shape, (6 * count, LANES)],
        blocks, brick_index, crossing, table, grid, lines, top, y1, y2, state, deposit,
        aliases={4: 0, 5: 1, 9: 2, 10: 3}, cycles=2000,
        scratch=[
            *(pltpu.VMEM(shape, jnp.bfloat16) for shape in parts(UNROLL)),
            *scalars,
            pltpu.SMEM(crossing.shape, jnp.int32),
            square,
            pltpu.SemaphoreType.DMA((3,)),
        ],
    )
    leaving = leaving.reshape(6, count, LANES)
    height = comps * SPREAD
    to_y1, to_y2, top_tiles = call(
        functools.partial(send_y_kernel, push, diffuse),
        [
            (count + comps * ROWS_Y + 8, LANES),
            (count + comps * ROWS_Y, LANES),
            ((size_x // BX) * height, LANES),
        ],
        leaving, grid, deposit, cycles=300, scratch=(pltpu.VMEM((comps * ROWS_Y, LANES), jnp.float32),),
    )
    y1, y2 = swapped_y((to_y1, to_y2))
    (deposit,) = call(
        functools.partial(deposit_kernel, dims), [deposit_shape], blocks, brick_index, push_parts, spread_parts, deposit,
        smem=(0, 1), aliases={4: 0}, cycles=4000,
    )
    deposit, over = call(
        merge_kernel, [(comps, size_x + 1, ROWS_Y, LANES), (ROWS_Y, LANES)], deposit, top_tiles,
        cycles=1000, scratch=(pltpu.VMEM(((size_x // BX) * (size_y // BY) * height, LANES), jnp.float32), square),
    )
    to_x, to_z = call(
        functools.partial(send_xz_kernel, push, diffuse), [(comps * size_y, LANES), (size_y, LANES)],
        grid, deposit, over, cycles=500,
    )
    base, velocity_next = call(
        functools.partial(base_kernel, push, diffuse, count), [gas_field.shape, (comps, nblocks, LANES)],
        grid, deposit, top, y1, y2, state, cycles=1000,
    )
    edge = comps * size_y
    both = lax.axis_size("gx") == 2
    to_x, to_z, to_xz = call(
        functools.partial(relay_kernel, size_x, size_y, comps, count),
        [(edge + (2 if both else 1) * count, LANES), (2, count + size_y, LANES), (count + size_y + 8, LANES)],
        y1, y2, to_x, to_z, leaving,
    )
    got_x = moved_along(to_x, "gx", 1)
    z1, z2 = swapped_z((to_z[0], to_z[1]))
    got_xz = moved_diagonally(to_xz, 1)
    got_mx = got_x if both else moved_along(leaving[1], "gx", -1)
    gas_next, arrivals = call(
        functools.partial(finish_kernel, count), [gas_field.shape, (6, 7, slots, LANES)],
        base, y1, y2, got_x, got_mx, z1, z2, got_xz, hbm_outs=(0, 1),
        scratch=(
            pltpu.VMEM(gas_field.shape, jnp.float32),
            pltpu.VMEM((6, 7, slots, LANES), jnp.float32),
            pltpu.SemaphoreType.DMA((comps + 1,)),
        ),
    )
    return gas_next, jnp.transpose(velocity_next, (1, 0, 2)), jnp.transpose(arrivals, (0, 2, 1, 3))


def solution(mesh):
    owner = ("gx", "gz", "gy")
    in_specs = (
        P(None, "gx", "gy", "gz"),
        P(owner, None, None),
        P(owner, None, None),
        P(owner, None),
        P(owner, None),
        P(owner),
        P(owner, None),
    )
    out_specs = (
        P(None, "gx", "gy", "gz"),
        P(owner, None, None),
        P(owner, None, None, None),
    )
    return jax.shard_map(
        per_device, mesh=mesh, in_specs=in_specs, out_specs=out_specs, check_vma=False
    )
```

```python
import functools

import jax
import jax.numpy as jnp
from jax import lax
from jax.experimental import pallas as pl
from jax.experimental.pallas import tpu as pltpu
from jax.sharding import PartitionSpec as P

BX = 4
BY = 4
BZ = 8

TIME_STEP = 0.25
VISCOSITY = 0.4

LANES = 128
PACK = 32
ROWS_Y = 24
REACH_X = BX + 1
REACH_Y = 8
SPREAD = REACH_X * REACH_Y
REACH_Z = 2 * BZ
UNROLL = 8

WEIGHT, ALONG_Y, IN_Y, ALONG_Z, IN_Z, RESPONSE, MOVING, OFFSET = 0, 5, 6, 7, 8, 9, 10, 13
TABLE_ROWS = 16
STATE = 8

VMEM = pl.BlockSpec(memory_space=pltpu.VMEM)
SMEM = pl.BlockSpec(memory_space=pltpu.SMEM)
HBM = pl.BlockSpec(memory_space=pltpu.HBM)


def moved_along(block, axis, distance):
    count = lax.axis_size(axis)
    return lax.ppermute(block, axis, [(i, (i + distance) % count) for i in range(count)])


def swapped_z(blocks):
    count = lax.axis_size("gz")
    first = [(i, i ^ 1) for i in range(count)]
    second = [(i, (((i + 1) ^ 1) - 1) % count) for i in range(count)]
    return lax.ppermute(blocks[0], "gz", first), lax.ppermute(blocks[1], "gz", second)


def swapped_y(blocks):
    nz, ny = lax.axis_size("gz"), lax.axis_size("gy")
    first = [(j, j ^ 1) for j in range(ny)]
    second = []
    for k in range(nz):
        second.append((k * ny, (k ^ 1) * ny))
        second.append((k * ny + ny - 1, (k ^ 1) * ny + ny - 1))
        second.extend((k * ny + j, k * ny + ((j + 1) ^ 1) - 1) for j in range(1, ny - 1))
    middle = lax.ppermute(blocks[1], ("gz", "gy"), second)
    return lax.ppermute(blocks[0], "gy", first), middle


def moved_diagonally(block, distance):
    nx, nz = lax.axis_size("gx"), lax.axis_size("gz")
    route = [(i * nz + k, (i + distance) % nx * nz + (k + distance) % nz) for i in range(nx) for k in range(nz)]
    return lax.ppermute(block, ("gx", "gz"), route)


def call(
    body, outs, *operands, smem=(), hbm=(), smem_outs=(), hbm_outs=(), scratch=(), aliases=None, cycles=0, limit=40
):
    return pl.pallas_call(
        body,
        out_shape=[o if isinstance(o, jax.ShapeDtypeStruct) else jax.ShapeDtypeStruct(o, jnp.float32) for o in outs],
        in_specs=[SMEM if i in smem else HBM if i in hbm else VMEM for i in range(len(operands))],
        out_specs=[SMEM if i in smem_outs else HBM if i in hbm_outs else VMEM for i in range(len(outs))],
        scratch_shapes=list(scratch),
        input_output_aliases=aliases or {},
        compiler_params=pltpu.CompilerParams(vmem_limit_bytes=limit * 1024 * 1024),
        cost_estimate=pl.CostEstimate(flops=cycles * 4096, bytes_accessed=cycles * 1024, transcendentals=0),
    )(*operands)


def lane_ids(rows):
    return lax.broadcasted_iota(jnp.int32, (rows, LANES), 1)


def row_ids(rows):
    return lax.broadcasted_iota(jnp.int32, (rows, LANES), 0)


def turned(value, shift):
    shift = shift % LANES
    return pltpu.roll(value, shift, 1) if shift else value


def odd(axis):
    return lax.axis_index(axis) % 2


def begin_kernel(
    gas_ref, velocity_in, fraction_in, response_in, cell_in, brick_in, crossing_in,
    grid_ref, face_ref, plane_ref, velocity_ref, fraction_ref, response_ref, cell_ref, brick_ref, crossing_ref, sems,
):
    comps, size_x, size_y, _ = gas_ref.shape
    pairs = [
        (gas_ref, grid_ref.at[:, 1 : size_x + 1, 0:size_y]),
        (velocity_in, velocity_ref), (fraction_in, fraction_ref), (response_in, response_ref),
        (cell_in, cell_ref), (brick_in, brick_ref), (crossing_in, crossing_ref),
    ]
    copies = [pltpu.make_async_copy(source, target, sems.at[i]) for i, (source, target) in enumerate(pairs)]
    for copy in copies:
        copy.start()
    zeros = jnp.zeros((ROWS_Y, LANES), jnp.float32)
    for c in range(comps):
        grid_ref[c, 0] = zeros
        grid_ref[c, size_x + 1] = zeros
        for x in range(size_x):
            grid_ref[c, x + 1, size_y:] = zeros[size_y:]
    copies[0].wait()
    lane = lane_ids(size_y)
    face = jnp.zeros((size_y, LANES), jnp.float32)
    for c in range(comps):
        plane_ref[c * size_y : (c + 1) * size_y] = grid_ref[c, 1, 0:size_y]
        for x in range(size_x):
            place = PACK * c + x
            face = jnp.where(lane == place, turned(grid_ref[c, x + 1, 0:size_y], place), face)
    face_ref[...] = face
    for copy in copies[1:]:
        copy.wait()


def parts_of(value):
    main = value.astype(jnp.bfloat16).astype(jnp.float32)
    return main, value - main


def lay_out(grid_ref, lines_ref, p, q, size_y, size_z):
    comps = grid_ref.shape[0]
    rows_z = size_z + 8
    count_y = size_y // BY
    for c in range(comps):
        planes = [grid_ref[c, p * BX + a + 1, q * BY : q * BY + REACH_Y] for a in range(REACH_X)]
        main, rest = parts_of(jnp.concatenate(planes, axis=0))
        stack = jnp.concatenate([main, rest, main, jnp.zeros((LANES - 3 * SPREAD, LANES), jnp.float32)], axis=0)
        at = ((p * count_y + q) * comps + c) * rows_z
        lines_ref[at : at + size_z] = jnp.transpose(stack)


def lay_out_top(turned_ref, lines_ref, q, comps, count_x, count_y, size_z):
    lane = lane_ids(count_x)
    rows_z = size_z + 8
    for c in range(comps):
        total = jnp.zeros((count_x, LANES), jnp.float32)
        for a in range(REACH_X):
            rows = turned_ref[pl.ds(PACK * c + a, count_x, stride=BX)]
            total = jnp.where(lane // REACH_Y == a, turned(rows, a * REACH_Y - q * BY), total)
        main, rest = parts_of(total)
        line = main + turned(rest, SPREAD) + turned(main, 2 * SPREAD)
        for p in range(count_x):
            at = ((p * count_y + q) * comps + c) * rows_z + size_z
            lines_ref[at : at + 1] = line[p : p + 1]


def prepare_kernel(
    grid_ref, velocity_ref, fraction_ref, response_ref, cell_ref, brick_ref,
    lines_ref, deposit_ref, table_ref, ready_ref, list_ref,
):
    comps, size_x, size_y, size_z = grid_ref.shape[0], grid_ref.shape[1] - 2, grid_ref.shape[2] - 8, grid_ref.shape[3]
    nblocks = velocity_ref.shape[1]
    count_x, count_y, count_z = size_x // BX, size_y // BY, size_z // BZ
    rows_z = size_z + 8

    room = nblocks + UNROLL

    def visit(k, counts):
        late = jnp.where(lax.rem(lax.div(brick_ref[k], count_z), count_y) == count_y - 1, 1, 0)
        list_ref[jnp.where(late == 1, room + counts[1], counts[0])] = k
        return counts[0] + 1 - late, counts[1] + late

    early, late = lax.fori_loop(0, nblocks, visit, (jnp.int32(0), jnp.int32(0)), unroll=8)
    for base, count in ((0, early), (room, late)):
        for u in range(UNROLL):
            list_ref[base + count + u] = nblocks
    list_ref[2 * room] = early
    list_ref[2 * room + 1] = late
    ready_ref[...] = jnp.zeros_like(ready_ref)

    deposit_ref[...] = jnp.zeros_like(deposit_ref)
    for p in range(count_x):
        for q in range(count_y):
            for c in range(comps):
                at = ((p * count_y + q) * comps + c) * rows_z + size_z
                lines_ref[at : at + 8] = jnp.zeros((8, LANES), jnp.float32)
    for p in range(count_x - 1):
        for q in range(count_y - 1):
            lay_out(grid_ref, lines_ref, p, q, size_y, size_z)

    cells = cell_ref[...]
    cell_x, cell_y, cell_z = cells // (BY * BZ), cells // BZ % BY, cells % BZ
    along_x = fraction_ref[0]

    def put(row, value):
        table_ref[pl.ds(row, nblocks, stride=TABLE_ROWS)] = value

    for a in range(REACH_X):
        put(WEIGHT + a, jnp.where(cell_x == a, 1.0 - along_x, 0.0) + jnp.where(cell_x == a - 1, along_x, 0.0))
    put(ALONG_Y, fraction_ref[1])
    put(IN_Y, cell_y.astype(jnp.float32))
    put(ALONG_Z, fraction_ref[2])
    put(IN_Z, cell_z.astype(jnp.float32))
    put(RESPONSE, response_ref[...])
    for c in range(comps):
        put(MOVING + c, velocity_ref[c])
        put(OFFSET + c, fraction_ref[c])
    spare = table_ref.shape[0] - nblocks * TABLE_ROWS
    row = row_ids(spare)
    table_ref[nblocks * TABLE_ROWS :] = jnp.where(row % TABLE_ROWS == RESPONSE, 1.0, 0.0)


def upper_faces(faces_ref):
    nx, nz = lax.axis_size("gx"), lax.axis_size("gz")
    i, k = lax.axis_index("gx"), lax.axis_index("gz")
    above = lax.rem(k + 1, nz)
    return faces_ref.at[i * nz + above], faces_ref.at[lax.rem(i + 1, nx) * nz + above]


def y_lines_kernel(grid_ref, faces_ref, from_x_ref, ready_ref, out_ref):
    face_ref, edge_ref = upper_faces(faces_ref)
    comps, size_x = grid_ref.shape[0], grid_ref.shape[1] - 2
    size_y = face_ref.shape[0]
    for c in range(comps):
        out_ref[c * size_x : (c + 1) * size_x] = grid_ref[c, 1 : size_x + 1, 0]
        out_ref[comps * size_x + c : comps * size_x + c + 1] = from_x_ref[c * size_y : c * size_y + 1]
    line = jnp.where(lane_ids(8) % PACK == size_x, turned(edge_ref[0:8], size_x), face_ref[0:8])
    out_ref[comps * size_x + comps : comps * size_x + comps + 1] = line[0:1]


def halo_xz_kernel(grid_in_ref, lines_in_ref, face_ref, from_x_ref, edge_ref, grid_ref, lines_ref, top_ref, turned_ref):
    comps, size_x = grid_ref.shape[0], grid_ref.shape[1] - 2
    size_y, size_z = face_ref.shape[0], grid_ref.shape[3]
    count_x, count_y = size_x // BX, size_y // BY
    for c in range(comps):
        grid_ref[c, size_x + 1, 0:size_y] = from_x_ref[c * size_y : (c + 1) * size_y]
    for q in range(count_y - 1):
        lay_out(grid_ref, lines_ref, count_x - 1, q, size_y, size_z)
    top = jnp.where(lane_ids(size_y) % PACK == size_x, turned(edge_ref[...], size_x), face_ref[...])
    top_ref[0:size_y] = top
    top_ref[size_y:] = jnp.zeros((LANES - size_y, LANES), jnp.float32)
    turned_ref[...] = jnp.transpose(top_ref[...])
    for q in range(count_y - 1):
        lay_out_top(turned_ref, lines_ref, q, comps, count_x, count_y, size_z)


def halo_y_kernel(size_y, grid_in_ref, lines_in_ref, top_in_ref, first_ref, second_ref, grid_ref, lines_ref, turned_ref):
    comps, size_x, size_z = grid_ref.shape[0], grid_ref.shape[1] - 2, grid_ref.shape[3]
    count_x, count_y = size_x // BX, size_y // BY
    inside = lax.axis_index("gy") != lax.axis_size("gy") - 1
    kept = (row_ids(8) == 0) & inside
    even = jnp.full((1, LANES), odd("gy")) == 0

    def line_at(row):
        line = jnp.where(even, first_ref[row : row + 1], second_ref[row : row + 1])
        return jnp.where(kept, jnp.broadcast_to(line, (8, LANES)), 0.0)

    for c in range(comps):
        for x in range(size_x + 1):
            grid_ref[c, x + 1, size_y:] = line_at(c * size_x + x if x < size_x else comps * size_x + c)
    for p in range(count_x):
        lay_out(grid_ref, lines_ref, p, count_y - 1, size_y, size_z)
    corner = line_at(comps * size_x + comps)
    rest = jnp.zeros((LANES - size_y - 8, LANES), jnp.float32)
    turned_ref[...] = jnp.transpose(jnp.concatenate([top_in_ref[0:size_y], corner, rest], axis=0))
    lay_out_top(turned_ref, lines_ref, count_y - 1, comps, count_x, count_y, size_z)


def block_steps(dims, list_ref, brick_ref):
    comps, _, count_y, count_z, rows_z = dims
    nblocks = brick_ref.shape[0]
    sub = row_ids(8)
    row_y = row_ids(REACH_Y).astype(jnp.float32)
    row_z = row_ids(REACH_Z).astype(jnp.float32)
    lanes = lane_ids(REACH_Z)

    def hat(rows, inside, along):
        return jnp.where(rows == inside, 1.0 - along, 0.0) + jnp.where(rows == inside + 1.0, along, 0.0)

    def place_of(at):
        k = list_ref[at]
        brick = jnp.where(k < nblocks, brick_ref[jnp.minimum(k, nblocks - 1)], 0)
        brick_x = lax.div(brick, count_y * count_z)
        brick_y = lax.rem(lax.div(brick, count_z), count_y)
        return k, brick_x * count_y + brick_y, lax.rem(brick, count_z)

    def loaded(at, lines_ref, table_ref):
        k, pair, brick_z = place_of(at)
        first = pl.multiple_of(pair * comps * rows_z + brick_z * BZ, 8)
        window = jnp.concatenate([lines_ref[pl.ds(first + c * rows_z, REACH_Z)] for c in range(comps)], axis=0)
        table = table_ref[pl.ds(pl.multiple_of(k * TABLE_ROWS, TABLE_ROWS), TABLE_ROWS)]
        return k, window, [table[i : i + 1] for i in range(TABLE_ROWS)]

    def weighted(rows):
        weight_y = hat(row_y, rows[IN_Y], rows[ALONG_Y])
        weight_z = hat(row_z, rows[IN_Z], rows[ALONG_Z])
        weight = jnp.concatenate([rows[WEIGHT + a] * weight_y for a in range(REACH_X)], axis=0)
        return weight_z, *parts_of(weight)

    def stepped(seen, weight_z, rows):
        rate = 1.0 / rows[RESPONSE]
        state, moved, pushed = [], [], []
        for c in range(comps):
            gas_sample = jnp.sum(seen[c * REACH_Z : (c + 1) * REACH_Z] * weight_z, axis=0, keepdims=True)
            drag = (gas_sample - rows[MOVING + c]) * rate
            state.append(rows[MOVING + c] + TIME_STEP * drag)
            moved.append(rows[OFFSET + c] + TIME_STEP * state[c])
            pushed.append(drag * weight_z)
        tile = jnp.broadcast_to(rows[RESPONSE], (STATE, LANES))
        for i, value in enumerate(state + moved):
            tile = jnp.where(sub == i, value, tile)
        return tile, jnp.concatenate(parts_of(jnp.concatenate(pushed, axis=0)), axis=0)

    def gathered(one, two):
        tables, windows, weights = [], [], []
        for _, window, rows in (one, two):
            weight_z, main, rest = weighted(rows)
            weights.append((weight_z, main, rest))
            unused = jnp.zeros((LANES - 3 * SPREAD, LANES), jnp.float32)
            tables.append(jnp.concatenate([main, main, rest, unused], axis=0).astype(jnp.bfloat16))
            windows.append(window)
        seen = lax.dot_general(
            jnp.concatenate(windows, axis=0).astype(jnp.bfloat16), jnp.concatenate(tables, axis=1),
            (((1,), (0,)), ((), ())), preferred_element_type=jnp.float32,
        )
        height = comps * REACH_Z
        tiles, fresh = [], []
        for i, (_, _, rows) in enumerate((one, two)):
            weight_z, main, rest = weights[i]
            mine = seen[i * height : (i + 1) * height, i * LANES : (i + 1) * LANES]
            tile, push = stepped(mine, weight_z, rows)
            tiles.append(tile)
            unused = jnp.zeros((LANES - comps * SPREAD, LANES), jnp.float32)
            spread = jnp.concatenate([main] * comps + [unused] + [rest] * comps + [unused], axis=0)
            fresh.append((push.astype(jnp.bfloat16), spread.astype(jnp.bfloat16)))
        return tiles, fresh

    def shared(push, spread):
        shares = lax.dot_general(push, spread, (((1,), (1,)), ((), ())), preferred_element_type=jnp.float32)
        height = comps * REACH_Z
        total = shares[:height, :LANES] + shares[:height, LANES:] + shares[height:, :LANES]
        result = jnp.zeros((REACH_Z, LANES), jnp.float32)
        for c in range(comps):
            inside = (lanes >= c * SPREAD) & (lanes < (c + 1) * SPREAD)
            result = jnp.where(inside, total[c * REACH_Z : (c + 1) * REACH_Z], result)
        return result

    def add(deposit_ref, at, shares):
        spots = []
        for u in range(len(shares)):
            _, pair, brick_z = place_of(at + u)
            spots.append(pl.ds(pl.multiple_of(pair * rows_z + brick_z * BZ, 8), REACH_Z))
        for spot, share in zip(spots, shares):
            deposit_ref[spot] = deposit_ref[spot] + share

    def group_of(taken):
        tiles, fresh = [], []
        for u in range(0, UNROLL, 2):
            both, kept = gathered(taken[u], taken[u + 1])
            tiles.extend(both)
            fresh.extend(kept)
        return tiles, fresh

    def keep(state_ref, taken, tiles):
        for (k, _, _), tile in zip(taken, tiles):
            state_ref[pl.ds(pl.multiple_of(STATE * k, STATE), STATE)] = tile

    def deposits_of(kept):
        return [shared(push, spread) for push, spread in kept]

    return loaded, group_of, keep, deposits_of, add


def groups_in(list_ref, late):
    room = (list_ref.shape[0] - 2) // 2
    return late * room, (list_ref[2 * room + late] + UNROLL - 1) // UNROLL


def fetched(sems, *pairs):
    copies = [pltpu.make_async_copy(source, target, sems.at[i]) for i, (source, target) in enumerate(pairs)]
    for copy in copies:
        copy.start()
    return copies


def gather_kernel(
    dims, list_in, brick_in, table_ref, grid_in_ref, lines_in_ref, faces_ref, from_x_ref,
    state_ref, push_ref, spread_ref, grid_ref, lines_ref, top_ref, list_ref, brick_ref, turned_ref, sems,
):
    copies = fetched(sems, (list_in, list_ref), (brick_in, brick_ref))
    face_ref, edge_ref = upper_faces(faces_ref)
    halo_xz_kernel(grid_in_ref, lines_in_ref, face_ref, from_x_ref, edge_ref, grid_ref, lines_ref, top_ref, turned_ref)
    for copy in copies:
        copy.wait()
    loaded, group_of, keep, _, _ = block_steps(dims, list_ref, brick_ref)
    base, groups = groups_in(list_ref, 0)

    @pl.loop(0, groups)
    def _(group):
        taken = [loaded(base + group * UNROLL + u, lines_ref, table_ref) for u in range(UNROLL)]
        tiles, fresh = group_of(taken)
        keep(state_ref, taken, tiles)
        for i, (push, spread) in enumerate(fresh):
            push_ref[group * UNROLL + i] = push
            spread_ref[group * UNROLL + i] = spread


def deposit_kernel(dims, list_ref, brick_ref, push_ref, spread_ref, deposit_in_ref, deposit_ref):
    _, _, _, deposits_of, add = block_steps(dims, list_ref, brick_ref)
    base, groups = groups_in(list_ref, 0)

    @pl.loop(0, groups)
    def _(group):
        mine = [group * UNROLL + i for i in range(UNROLL)]
        add(deposit_ref, base + group * UNROLL, deposits_of([(push_ref[i], spread_ref[i]) for i in mine]))


def late_kernel(
    dims, slots, list_in, brick_in, crossing_in, table_ref, grid_in_ref, lines_in_ref, top_in_ref, first_ref, second_ref,
    state_in_ref, deposit_in_ref,
    grid_ref, lines_ref, state_ref, deposit_ref, leaving_ref,
    push_ref, spread_ref, list_ref, brick_ref, crossing_ref, turned_ref, sems,
):
    copies = fetched(sems, (list_in, list_ref), (brick_in, brick_ref), (crossing_in, crossing_ref))
    halo_y_kernel(
        dims[2] * BY, grid_in_ref, lines_in_ref, top_in_ref, first_ref, second_ref, grid_ref, lines_ref, turned_ref
    )
    for copy in copies:
        copy.wait()
    loaded, group_of, keep, deposits_of, add = block_steps(dims, list_ref, brick_ref)
    base, groups = groups_in(list_ref, 1)
    push_ref[...] = jnp.zeros_like(push_ref)
    spread_ref[...] = jnp.zeros_like(spread_ref)

    @pl.loop(0, groups + 1)
    def _(group):
        now = base + jnp.maximum(jnp.minimum(group, groups - 1), 0) * UNROLL
        before = base + jnp.maximum(group - 1, 0) * UNROLL
        taken = [loaded(now + u, lines_ref, table_ref) for u in range(UNROLL)]
        shares = deposits_of([(push_ref[i], spread_ref[i]) for i in range(UNROLL)])
        tiles, fresh = group_of(taken)
        add(deposit_ref, before, shares)
        keep(state_ref, taken, tiles)
        for i, (push, spread) in enumerate(fresh):
            push_ref[i] = push
            spread_ref[i] = spread

    rows = leaving_ref.shape[0] // (6 * slots)
    for face in range(6):
        tiles = []
        for slot in range(slots):
            block = crossing_ref[face, slot]
            spot = pl.ds(pl.multiple_of(jnp.maximum(block, 0) * STATE, STATE), STATE)
            live = jnp.full((STATE, LANES), block, jnp.int32) >= 0
            tiles.append(jnp.where(live, state_ref[spot], 0.0))
        for slot, tile in enumerate(tiles):
            leaving_ref[pl.ds(face * rows * slots + slot, rows, stride=slots)] = tile[:rows]


def top_rows(deposit_ref, q, count_x, count_y, rows_z, size_z):
    total = None
    for p in range(count_x):
        at = (p * count_y + q) * rows_z + size_z
        value = pltpu.roll(deposit_ref[at : at + 8], p, 0) if p else deposit_ref[at : at + 8]
        total = value if total is None else total + value
    return total


def send_y_kernel(push, diffuse, leaving_ref, grid_ref, deposit_ref, y_ref, tiles_ref, lines_ref):
    comps, size_x, size_y, size_z = grid_ref.shape[0], grid_ref.shape[1] - 2, grid_ref.shape[2] - 8, grid_ref.shape[3]
    count_x, count_y = size_x // BX, size_y // BY
    rows_z = size_z + 8
    rows = leaving_ref.shape[1]
    height = comps * SPREAD
    for p in range(count_x):
        at = (p * count_y + count_y - 1) * rows_z
        tiles_ref[p * height : (p + 1) * height] = jnp.transpose(deposit_ref[at : at + size_z])[:height]
    first = jnp.full((rows, LANES), odd("gy")) == 0
    y_ref[0, 0:rows] = jnp.where(first, leaving_ref[2], leaving_ref[3])
    y_ref[1, 0:rows] = jnp.where(first, leaving_ref[3], leaving_ref[2])
    lines_ref[...] = jnp.zeros_like(lines_ref)
    for c in range(comps):
        for p in range(count_x):
            spot = slice(c * ROWS_Y + p * BX, c * ROWS_Y + p * BX + REACH_X)
            line = tiles_ref[pl.ds(p * height + c * SPREAD + BY, REACH_X, stride=REACH_Y)]
            lines_ref[spot] = lines_ref[spot] + line
    wrapped = top_rows(deposit_ref, count_y - 1, count_x, count_y, rows_z, size_z)
    lane = lane_ids(8)
    packed = jnp.zeros((8, LANES), jnp.float32)
    for c in range(comps):
        spot = slice(c * ROWS_Y, (c + 1) * ROWS_Y)
        beside = jnp.concatenate([grid_ref[c, 1 : size_x + 1, size_y - 1], jnp.zeros((8, LANES), jnp.float32)], axis=0)
        line = push * lines_ref[spot] + diffuse * beside
        y_ref[0, rows + c * ROWS_Y : rows + (c + 1) * ROWS_Y] = line
        y_ref[1, rows + c * ROWS_Y : rows + (c + 1) * ROWS_Y] = line
        for a in range(REACH_X):
            place = PACK * c + a
            value = turned(wrapped, place - c * SPREAD - a * REACH_Y - BY)
            packed = packed + jnp.where(lane == place, value, 0.0)
    corner = packed[0:1]
    for p in range(1, count_x):
        corner = corner + turned(packed[p : p + 1], p * BX)
    at = rows + size_x + 1
    y_ref[0, at : at + 1] = push * corner
    y_ref[1, at : at + 1] = push * corner


def merge_kernel(deposit_ref, top_tiles_ref, plane_ref, face_ref, tiles_ref, turned_ref):
    comps, planes = plane_ref.shape[:2]
    count_x, size_z = (planes - 1) // BX, plane_ref.shape[3]
    rows_z = size_z + 8
    count_y = deposit_ref.shape[0] // (rows_z * count_x)
    height = comps * SPREAD
    for p in range(count_x):
        for q in range(count_y - 1):
            at = p * count_y + q
            value = jnp.transpose(deposit_ref[at * rows_z : at * rows_z + size_z])
            tiles_ref[at * height : (at + 1) * height] = value[:height]
    top = row_ids(REACH_Y) >= BY
    for c in range(comps):
        for x in range(planes):
            bricks = [(x // BX, x % BX)] if x < planes - 1 else []
            if x and x % BX == 0:
                bricks.append((x // BX - 1, BX))

            def tile(q):
                total = None
                for p, a in bricks:
                    at = c * SPREAD + a * REACH_Y
                    if q < count_y - 1:
                        value = tiles_ref[(p * count_y + q) * height + at : (p * count_y + q) * height + at + REACH_Y]
                    else:
                        value = top_tiles_ref[p * height + at : p * height + at + REACH_Y]
                    total = value if total is None else total + value
                return total

            carried = None
            for q in range(0, count_y, 2):
                here = tile(q)
                if carried is not None:
                    here = here + carried
                between = pltpu.roll(tile(q + 1), BY, 0)
                here = here + jnp.where(top, between, 0.0)
                carried = jnp.where(top, 0.0, between)
                plane_ref[c, x, q * BY : q * BY + REACH_Y] = here
            plane_ref[c, x, count_y * BY :] = carried

    lane = lane_ids(count_x)
    turned_ref[...] = jnp.zeros_like(turned_ref)
    for q in range(count_y):
        wrapped = top_rows(deposit_ref, q, count_x, count_y, rows_z, size_z)[:count_x]
        within = (lane >= q * BY) & (lane <= (q + 1) * BY)
        for c in range(comps):
            for a in range(REACH_X):
                value = turned(wrapped, q * BY - c * SPREAD - a * REACH_Y)
                spot = pl.ds(PACK * c + a, count_x, stride=BX)
                turned_ref[spot] = turned_ref[spot] + jnp.where(within, value, 0.0)
    face_ref[...] = jnp.transpose(turned_ref[...])[: face_ref.shape[0]]


def send_xz_kernel(push, diffuse, grid_ref, deposit_ref, face_ref, x_ref, z_ref):
    comps, size_x = grid_ref.shape[0], grid_ref.shape[1] - 2
    size_y = z_ref.shape[0]
    lane = lane_ids(size_y)
    packed = push * face_ref[0:size_y]
    for c in range(comps):
        for x in range(size_x):
            place = PACK * c + x
            packed = packed + jnp.where(lane == place, diffuse * turned(grid_ref[c, x + 1, 0:size_y], place + 1), 0.0)
        total = push * deposit_ref[c, size_x, 0:size_y]
        x_ref[c * size_y : (c + 1) * size_y] = diffuse * grid_ref[c, size_x, 0:size_y] + total
    z_ref[...] = packed


def base_kernel(push, diffuse, count, grid_ref, deposit_ref, top_ref, y1_ref, y2_ref, state_ref, base_ref, velocity_ref):
    comps, size_x, size_y, size_z = base_ref.shape
    lane, sub = lane_ids(size_y), row_ids(size_y)
    top = top_ref[0:size_y]
    for c in range(comps):
        at = count + c * ROWS_Y
        lines = below(y1_ref, y2_ref, slice(at, at + size_x))
        for x in range(size_x):
            here = grid_ref[c, x + 1, 0:size_y]
            before = jnp.where(sub == 0, 0.0, pltpu.roll(here, 1, 0))
            laplace = grid_ref[c, x, 0:size_y] + grid_ref[c, x + 2, 0:size_y]
            laplace = laplace + grid_ref[c, x + 1, 1 : size_y + 1] + before
            ahead = jnp.where(lane == size_z - 1, turned(top, size_z - 1 - (PACK * c + x)), turned(here, -1))
            laplace = laplace + ahead + jnp.where(lane == 0, 0.0, turned(here, 1)) - 6.0 * here
            total = here + diffuse * laplace + push * deposit_ref[c, x, 0:size_y]
            line = jnp.broadcast_to(lines[x : x + 1], (size_y, LANES))
            base_ref[c, x] = total + jnp.where(sub == 0, line, 0.0)
        velocity_ref[c] = state_ref[pl.ds(c, velocity_ref.shape[1], stride=STATE)]


def below(first_ref, second_ref, rows):
    got = jnp.where(jnp.full((1, LANES), odd("gy")) == 1, first_ref[rows], second_ref[rows])
    return jnp.where(jnp.full((1, LANES), lax.axis_index("gy")) != 0, got, 0.0)


def relay_kernel(size_x, size_y, comps, count, first_ref, second_ref, x_in_ref, z_in_ref, leaving_ref, x_ref, z_ref, edge_ref):
    edge = comps * size_y
    x_ref[0:edge] = x_in_ref[...]
    for c in range(comps):
        at = count + c * ROWS_Y + size_x
        spot = slice(c * size_y, c * size_y + 1)
        x_ref[spot] = x_in_ref[spot] + below(first_ref, second_ref, slice(at, at + 1))
    x_ref[edge : edge + count] = leaving_ref[0]
    if x_ref.shape[0] > edge + count:
        x_ref[edge + count : edge + 2 * count] = leaving_ref[1]
    at = count + size_x + 1
    edge_ref[size_y:] = jnp.zeros((edge_ref.shape[0] - size_y, LANES), jnp.float32)
    edge_ref[0:size_y] = z_in_ref[...]
    edge_ref[0:1] = z_in_ref[0:1] + below(first_ref, second_ref, slice(at, at + 1))
    up = odd("gz")
    z_ref[up, 0:count] = leaving_ref[4]
    z_ref[up, count : count + size_y] = edge_ref[0:size_y]
    z_ref[1 - up, 0:count] = leaving_ref[5]
    z_ref[1 - up, count : count + size_y] = jnp.zeros((size_y, LANES), jnp.float32)


def finish_kernel(
    count, base_ref, y1_ref, y2_ref, x_ref, minus_x_ref, z1_ref, z2_ref, edge_ref, gas_out, arrivals_out,
    gas_ref, arrivals_ref, sems,
):
    comps, size_x, size_y, _ = base_ref.shape
    first_lane = lane_ids(size_y) == 0
    odd_y, odd_z = jnp.full((1, LANES), odd("gy")) == 1, jnp.full((1, LANES), odd("gz")) == 1
    place = jnp.full((1, LANES), lax.axis_index("gy"))
    lower, upper = place != 0, place != lax.axis_size("gy") - 1
    rows = slice(count, count + size_y)
    slots = arrivals_ref.shape[2]
    for i in range(arrivals_ref.shape[1]):

        def rows_of(ref, at=0):
            return ref[at + i * slots : at + (i + 1) * slots]

        arrivals_ref[0, i] = rows_of(x_ref, comps * size_y)
        arrivals_ref[1, i] = rows_of(minus_x_ref, minus_x_ref.shape[0] - count)
        y1, y2 = rows_of(y1_ref), rows_of(y2_ref)
        arrivals_ref[2, i] = jnp.where(lower, jnp.where(odd_y, y1, y2), 0.0)
        arrivals_ref[3, i] = jnp.where(upper, jnp.where(odd_y, y2, y1), 0.0)
        z1, z2 = rows_of(z1_ref), rows_of(z2_ref)
        arrivals_ref[4, i] = jnp.where(odd_z, z1, z2)
        arrivals_ref[5, i] = jnp.where(odd_z, z2, z1)
    copies = [pltpu.make_async_copy(arrivals_ref, arrivals_out, sems.at[comps])]
    copies[0].start()
    face = jnp.where(odd_z, z1_ref[rows], z2_ref[rows])
    corner = edge_ref[0:size_y]
    for c in range(comps):
        for x in range(size_x):
            total = base_ref[c, x]
            far = turned(face, -(PACK * c + x))
            if x == 0:
                total = total + x_ref[c * size_y : (c + 1) * size_y]
                far = far + turned(corner, -(PACK * c + size_x))
            gas_ref[c, x] = total + jnp.where(first_lane, far, 0.0)
        copies.append(pltpu.make_async_copy(gas_ref.at[c], gas_out.at[c], sems.at[c]))
        copies[-1].start()
    for copy in copies:
        copy.wait()


def per_device(gas_field, velocity, fraction, response, cell_index, brick_index, crossing):
    comps, size_x, size_y, size_z = gas_field.shape
    nblocks = velocity.shape[0]
    loading = 0.5 * size_x * size_y * size_z / (nblocks * 128)
    push, diffuse = -TIME_STEP * loading, TIME_STEP * VISCOSITY
    velocity = jnp.transpose(velocity, (1, 0, 2))
    fraction = jnp.transpose(fraction, (1, 0, 2))
    spare = nblocks + 8
    rows_z = size_z + 8
    grid_shape = (comps, size_x + 2, ROWS_Y, LANES)
    lines_shape = ((size_x // BX) * (size_y // BY) * comps * rows_z, LANES)
    deposit_shape = ((size_x // BX) * (size_y // BY) * rows_z, LANES)

    inputs = (gas_field, velocity, fraction, response, cell_index, brick_index, crossing)
    inputs = [pltpu.with_memory_space_constraint(array, pltpu.HBM) for array in inputs]
    grid, face, plane, velocity, fraction, response, cell_index, brick_index, crossing = call(
        begin_kernel,
        [grid_shape, (size_y, LANES), (comps * size_y, LANES)]
        + [jax.ShapeDtypeStruct(array.shape, array.dtype) for array in inputs[1:]],
        *inputs, hbm=range(7), scratch=(pltpu.SemaphoreType.DMA((7,)),), limit=40,
    )
    from_x = moved_along(plane, "gx", -1)
    faces = lax.all_gather(face, ("gx", "gz"))
    lines, deposit, table, ready, blocks = call(
        prepare_kernel,
        [
            lines_shape,
            deposit_shape,
            (TABLE_ROWS * spare, LANES),
            (8, LANES),
            jax.ShapeDtypeStruct((2 * (nblocks + UNROLL) + 2,), jnp.int32),
        ],
        grid, velocity, fraction, response, cell_index, brick_index,
        smem=(5,), smem_outs=(4,), cycles=3000,
    )
    line_rows = -(-(comps * size_x + comps + 1) // 8) * 8
    (y_lines,) = call(y_lines_kernel, [(line_rows, LANES)], grid, faces, from_x, ready)
    y1, y2 = swapped_y((y_lines, y_lines))
    square = pltpu.VMEM((LANES, LANES), jnp.float32)
    scalars = (pltpu.SMEM(blocks.shape, jnp.int32), pltpu.SMEM(brick_index.shape, jnp.int32))
    dims = (comps, size_x // BX, size_y // BY, size_z // BZ, rows_z)
    slots = crossing.shape[1]
    count = 7 * slots

    def parts(many):
        return [(many, 2 * comps * REACH_Z, LANES), (many, 2 * LANES, LANES)]

    state, push_parts, spread_parts, grid, lines, top = call(
        functools.partial(gather_kernel, dims),
        [(STATE * spare, LANES)]
        + [jax.ShapeDtypeStruct(shape, jnp.bfloat16) for shape in parts(nblocks + UNROLL)]
        + [grid_shape, lines_shape, (LANES, LANES)],
        blocks, brick_index, table, grid, lines, faces, from_x,
        aliases={3: 3, 4: 4}, cycles=4000, scratch=(*scalars, square, pltpu.SemaphoreType.DMA((2,))),
    )
    grid, lines, state, deposit, leaving = call(
        functools.partial(late_kernel, dims, slots),
        [grid_shape, lines_shape, (STATE * spare, LANES), deposit_shape, (6 * count, LANES)],
        blocks, brick_index, crossing, table, grid, lines, top, y1, y2, state, deposit,
        aliases={4: 0, 5: 1, 9: 2, 10: 3}, cycles=2000,
        scratch=[
            *(pltpu.VMEM(shape, jnp.bfloat16) for shape in parts(UNROLL)),
            *scalars,
            pltpu.SMEM(crossing.shape, jnp.int32),
            square,
            pltpu.SemaphoreType.DMA((3,)),
        ],
    )
    leaving = leaving.reshape(6, count, LANES)
    height = comps * SPREAD
    to_y, top_tiles = call(
        functools.partial(send_y_kernel, push, diffuse),
        [(2, count + comps * ROWS_Y, LANES), ((size_x // BX) * height, LANES)],
        leaving, grid, deposit, cycles=300, scratch=(pltpu.VMEM((comps * ROWS_Y, LANES), jnp.float32),),
    )
    y1, y2 = swapped_y((to_y[0], to_y[1]))
    (deposit,) = call(
        functools.partial(deposit_kernel, dims), [deposit_shape], blocks, brick_index, push_parts, spread_parts, deposit,
        smem=(0, 1), aliases={4: 0}, cycles=4000,
    )
    deposit, over = call(
        merge_kernel, [(comps, size_x + 1, ROWS_Y, LANES), (ROWS_Y, LANES)], deposit, top_tiles,
        cycles=1000, scratch=(pltpu.VMEM(((size_x // BX) * (size_y // BY) * height, LANES), jnp.float32), square),
    )
    to_x, to_z = call(
        functools.partial(send_xz_kernel, push, diffuse), [(comps * size_y, LANES), (size_y, LANES)],
        grid, deposit, over, cycles=500,
    )
    base, velocity_next = call(
        functools.partial(base_kernel, push, diffuse, count), [gas_field.shape, (comps, nblocks, LANES)],
        grid, deposit, top, y1, y2, state, cycles=1000,
    )
    edge = comps * size_y
    both = lax.axis_size("gx") == 2
    to_x, to_z, to_xz = call(
        functools.partial(relay_kernel, size_x, size_y, comps, count),
        [(edge + (2 if both else 1) * count, LANES), (2, count + size_y, LANES), (count + size_y + 8, LANES)],
        y1, y2, to_x, to_z, leaving,
    )
    got_x = moved_along(to_x, "gx", 1)
    z1, z2 = swapped_z((to_z[0], to_z[1]))
    got_xz = moved_diagonally(to_xz, 1)
    got_mx = got_x if both else moved_along(leaving[1], "gx", -1)
    gas_next, arrivals = call(
        functools.partial(finish_kernel, count), [gas_field.shape, (6, 7, slots, LANES)],
        base, y1, y2, got_x, got_mx, z1, z2, got_xz, hbm_outs=(0, 1),
        scratch=(
            pltpu.VMEM(gas_field.shape, jnp.float32),
            pltpu.VMEM((6, 7, slots, LANES), jnp.float32),
            pltpu.SemaphoreType.DMA((comps + 1,)),
        ),
    )
    return gas_next, jnp.transpose(velocity_next, (1, 0, 2)), jnp.transpose(arrivals, (0, 2, 1, 3))


def solution(mesh):
    owner = ("gx", "gz", "gy")
    in_specs = (
        P(None, "gx", "gy", "gz"),
        P(owner, None, None),
        P(owner, None, None),
        P(owner, None),
        P(owner, None),
        P(owner),
        P(owner, None),
    )
    out_specs = (
        P(None, "gx", "gy", "gz"),
        P(owner, None, None),
        P(owner, None, None, None),
    )
    return jax.shard_map(
        per_device, mesh=mesh, in_specs=in_specs, out_specs=out_specs, check_vma=False
    )
```

```python
import functools

import jax
import jax.numpy as jnp
from jax import lax
from jax.experimental import pallas as pl
from jax.experimental.pallas import tpu as pltpu
from jax.sharding import PartitionSpec as P

BX = 4
BY = 4
BZ = 8

TIME_STEP = 0.25
VISCOSITY = 0.4

LANES = 128
PACK = 32
ROWS_Y = 24
REACH_X = BX + 1
REACH_Y = 8
SPREAD = REACH_X * REACH_Y
REACH_Z = 2 * BZ
UNROLL = 8
WIDE = 16

WEIGHT, ALONG_Y, IN_Y, ALONG_Z, IN_Z, RESPONSE, MOVING, OFFSET = 0, 5, 6, 7, 8, 9, 10, 13
TABLE_ROWS = 16
STATE = 8

VMEM = pl.BlockSpec(memory_space=pltpu.VMEM)
SMEM = pl.BlockSpec(memory_space=pltpu.SMEM)
HBM = pl.BlockSpec(memory_space=pltpu.HBM)


def moved_along(block, axis, distance):
    count = lax.axis_size(axis)
    return lax.ppermute(block, axis, [(i, (i + distance) % count) for i in range(count)])


def swapped_z(blocks):
    count = lax.axis_size("gz")
    first = [(i, i ^ 1) for i in range(count)]
    second = [(i, (((i + 1) ^ 1) - 1) % count) for i in range(count)]
    return lax.ppermute(blocks[0], "gz", first), lax.ppermute(blocks[1], "gz", second)


def swapped_y(blocks):
    nz, ny = lax.axis_size("gz"), lax.axis_size("gy")
    first = [(j, j ^ 1) for j in range(ny)]
    second = []
    for k in range(nz):
        second.append((k * ny, (k ^ 1) * ny))
        second.append((k * ny + ny - 1, (k ^ 1) * ny + ny - 1))
        second.extend((k * ny + j, k * ny + ((j + 1) ^ 1) - 1) for j in range(1, ny - 1))
    middle = lax.ppermute(blocks[1], ("gz", "gy"), second)
    return lax.ppermute(blocks[0], "gy", first), middle


def moved_diagonally(block, distance):
    nx, nz = lax.axis_size("gx"), lax.axis_size("gz")
    route = [(i * nz + k, (i + distance) % nx * nz + (k + distance) % nz) for i in range(nx) for k in range(nz)]
    return lax.ppermute(block, ("gx", "gz"), route)


def call(
    body, outs, *operands, smem=(), hbm=(), smem_outs=(), hbm_outs=(), scratch=(), aliases=None, cycles=0, limit=40
):
    return pl.pallas_call(
        body,
        out_shape=[o if isinstance(o, jax.ShapeDtypeStruct) else jax.ShapeDtypeStruct(o, jnp.float32) for o in outs],
        in_specs=[SMEM if i in smem else HBM if i in hbm else VMEM for i in range(len(operands))],
        out_specs=[SMEM if i in smem_outs else HBM if i in hbm_outs else VMEM for i in range(len(outs))],
        scratch_shapes=list(scratch),
        input_output_aliases=aliases or {},
        compiler_params=pltpu.CompilerParams(vmem_limit_bytes=limit * 1024 * 1024),
        cost_estimate=pl.CostEstimate(flops=cycles * 4096, bytes_accessed=cycles * 1024, transcendentals=0),
    )(*operands)


def lane_ids(rows):
    return lax.broadcasted_iota(jnp.int32, (rows, LANES), 1)


def row_ids(rows):
    return lax.broadcasted_iota(jnp.int32, (rows, LANES), 0)


def turned(value, shift):
    shift = shift % LANES
    return pltpu.roll(value, shift, 1) if shift else value


def odd(axis):
    return lax.axis_index(axis) % 2


def begin_kernel(
    gas_ref, velocity_in, fraction_in, response_in, cell_in, brick_in, crossing_in,
    grid_ref, face_ref, plane_ref, velocity_ref, fraction_ref, response_ref, cell_ref, brick_ref, crossing_ref, sems,
):
    comps, size_x, size_y, _ = gas_ref.shape
    pairs = [
        *((gas_ref.at[c], grid_ref.at[c, 1 : size_x + 1, 0:size_y]) for c in range(comps)),
        (velocity_in, velocity_ref), (fraction_in, fraction_ref), (response_in, response_ref),
        (cell_in, cell_ref), (brick_in, brick_ref), (crossing_in, crossing_ref),
    ]
    copies = [pltpu.make_async_copy(source, target, sems.at[i]) for i, (source, target) in enumerate(pairs)]
    for copy in copies:
        copy.start()
    zeros = jnp.zeros((ROWS_Y, LANES), jnp.float32)
    for c in range(comps):
        grid_ref[c, 0] = zeros
        grid_ref[c, size_x + 1] = zeros
        for x in range(size_x):
            grid_ref[c, x + 1, size_y:] = zeros[size_y:]
    lane = lane_ids(size_y)
    face = jnp.zeros((size_y, LANES), jnp.float32)
    for c in range(comps):
        copies[c].wait()
        plane_ref[c * size_y : (c + 1) * size_y] = grid_ref[c, 1, 0:size_y]
        for x in range(size_x):
            place = PACK * c + x
            face = jnp.where(lane == place, turned(grid_ref[c, x + 1, 0:size_y], place), face)
    face_ref[...] = face
    for copy in copies[comps:]:
        copy.wait()


def parts_of(value):
    main = value.astype(jnp.bfloat16).astype(jnp.float32)
    return main, value - main


def lay_out(grid_ref, lines_ref, p, q, size_y, size_z):
    comps = grid_ref.shape[0]
    rows_z = size_z + 8
    count_y = size_y // BY
    for c in range(comps):
        planes = [grid_ref[c, p * BX + a + 1, q * BY : q * BY + REACH_Y] for a in range(REACH_X)]
        main, rest = parts_of(jnp.concatenate(planes, axis=0))
        stack = jnp.concatenate([main, rest, main, jnp.zeros((LANES - 3 * SPREAD, LANES), jnp.float32)], axis=0)
        at = ((p * count_y + q) * comps + c) * rows_z
        lines_ref[at : at + size_z] = jnp.transpose(stack)


def lay_out_top(turned_ref, lines_ref, q, comps, count_x, count_y, size_z):
    lane = lane_ids(count_x)
    rows_z = size_z + 8
    for c in range(comps):
        total = jnp.zeros((count_x, LANES), jnp.float32)
        for a in range(REACH_X):
            rows = turned_ref[pl.ds(PACK * c + a, count_x, stride=BX)]
            total = jnp.where(lane // REACH_Y == a, turned(rows, a * REACH_Y - q * BY), total)
        main, rest = parts_of(total)
        line = main + turned(rest, SPREAD) + turned(main, 2 * SPREAD)
        for p in range(count_x):
            at = ((p * count_y + q) * comps + c) * rows_z + size_z
            lines_ref[at : at + 1] = line[p : p + 1]


def prepare_kernel(
    grid_ref, velocity_ref, fraction_ref, response_ref, cell_ref, brick_ref,
    lines_ref, deposit_ref, table_ref, ready_ref, list_ref,
):
    comps, size_x, size_y, size_z = grid_ref.shape[0], grid_ref.shape[1] - 2, grid_ref.shape[2] - 8, grid_ref.shape[3]
    nblocks = velocity_ref.shape[1]
    count_x, count_y, count_z = size_x // BX, size_y // BY, size_z // BZ
    rows_z = size_z + 8

    room = nblocks + WIDE

    def visit(k, counts):
        late = jnp.where(lax.rem(lax.div(brick_ref[k], count_z), count_y) == count_y - 1, 1, 0)
        list_ref[jnp.where(late == 1, room + counts[1], counts[0])] = k
        return counts[0] + 1 - late, counts[1] + late

    early, late = lax.fori_loop(0, nblocks, visit, (jnp.int32(0), jnp.int32(0)), unroll=8)
    for base, count in ((0, early), (room, late)):
        for u in range(WIDE):
            list_ref[base + count + u] = nblocks
    list_ref[2 * room] = early
    list_ref[2 * room + 1] = late
    ready_ref[...] = jnp.zeros_like(ready_ref)

    deposit_ref[...] = jnp.zeros_like(deposit_ref)
    for p in range(count_x):
        for q in range(count_y):
            for c in range(comps):
                at = ((p * count_y + q) * comps + c) * rows_z + size_z
                lines_ref[at : at + 8] = jnp.zeros((8, LANES), jnp.float32)
    for p in range(count_x - 1):
        for q in range(count_y - 1):
            lay_out(grid_ref, lines_ref, p, q, size_y, size_z)

    cells = cell_ref[...]
    cell_x, cell_y, cell_z = cells // (BY * BZ), cells // BZ % BY, cells % BZ
    along_x = fraction_ref[0]

    def put(row, value):
        table_ref[pl.ds(row, nblocks, stride=TABLE_ROWS)] = value

    for a in range(REACH_X):
        put(WEIGHT + a, jnp.where(cell_x == a, 1.0 - along_x, 0.0) + jnp.where(cell_x == a - 1, along_x, 0.0))
    put(ALONG_Y, fraction_ref[1])
    put(IN_Y, cell_y.astype(jnp.float32))
    put(ALONG_Z, fraction_ref[2])
    put(IN_Z, cell_z.astype(jnp.float32))
    put(RESPONSE, response_ref[...])
    for c in range(comps):
        put(MOVING + c, velocity_ref[c])
        put(OFFSET + c, fraction_ref[c])
    spare = table_ref.shape[0] - nblocks * TABLE_ROWS
    row = row_ids(spare)
    table_ref[nblocks * TABLE_ROWS :] = jnp.where(row % TABLE_ROWS == RESPONSE, 1.0, 0.0)


def y_lines_kernel(grid_ref, face_ref, from_x_ref, edge_ref, ready_ref, out_ref):
    comps, size_x = grid_ref.shape[0], grid_ref.shape[1] - 2
    size_y = face_ref.shape[0]
    for c in range(comps):
        out_ref[c * size_x : (c + 1) * size_x] = grid_ref[c, 1 : size_x + 1, 0]
        out_ref[comps * size_x + c : comps * size_x + c + 1] = from_x_ref[c * size_y : c * size_y + 1]
    line = jnp.where(lane_ids(8) % PACK == size_x, turned(edge_ref[0:8], size_x), face_ref[0:8])
    out_ref[comps * size_x + comps : comps * size_x + comps + 1] = line[0:1]


def halo_xz_kernel(grid_in_ref, lines_in_ref, face_ref, from_x_ref, edge_ref, grid_ref, lines_ref, top_ref, turned_ref):
    comps, size_x = grid_ref.shape[0], grid_ref.shape[1] - 2
    size_y, size_z = face_ref.shape[0], grid_ref.shape[3]
    count_x, count_y = size_x // BX, size_y // BY
    for c in range(comps):
        grid_ref[c, size_x + 1, 0:size_y] = from_x_ref[c * size_y : (c + 1) * size_y]
    for q in range(count_y - 1):
        lay_out(grid_ref, lines_ref, count_x - 1, q, size_y, size_z)
    top = jnp.where(lane_ids(size_y) % PACK == size_x, turned(edge_ref[...], size_x), face_ref[...])
    top_ref[0:size_y] = top
    top_ref[size_y:] = jnp.zeros((LANES - size_y, LANES), jnp.float32)
    turned_ref[...] = jnp.transpose(top_ref[...])
    for q in range(count_y - 1):
        lay_out_top(turned_ref, lines_ref, q, comps, count_x, count_y, size_z)


def halo_y_kernel(size_y, grid_in_ref, lines_in_ref, top_in_ref, first_ref, second_ref, grid_ref, lines_ref, turned_ref):
    comps, size_x, size_z = grid_ref.shape[0], grid_ref.shape[1] - 2, grid_ref.shape[3]
    count_x, count_y = size_x // BX, size_y // BY
    inside = lax.axis_index("gy") != lax.axis_size("gy") - 1
    kept = (row_ids(8) == 0) & inside
    even = jnp.full((1, LANES), odd("gy")) == 0

    def line_at(row):
        line = jnp.where(even, first_ref[row : row + 1], second_ref[row : row + 1])
        return jnp.where(kept, jnp.broadcast_to(line, (8, LANES)), 0.0)

    for c in range(comps):
        for x in range(size_x + 1):
            grid_ref[c, x + 1, size_y:] = line_at(c * size_x + x if x < size_x else comps * size_x + c)
    for p in range(count_x):
        lay_out(grid_ref, lines_ref, p, count_y - 1, size_y, size_z)
    corner = line_at(comps * size_x + comps)
    rest = jnp.zeros((LANES - size_y - 8, LANES), jnp.float32)
    turned_ref[...] = jnp.transpose(jnp.concatenate([top_in_ref[0:size_y], corner, rest], axis=0))
    lay_out_top(turned_ref, lines_ref, count_y - 1, comps, count_x, count_y, size_z)


def block_steps(dims, list_ref, brick_ref):
    comps, _, count_y, count_z, rows_z = dims
    nblocks = brick_ref.shape[0]
    sub = row_ids(8)
    row_y = row_ids(REACH_Y).astype(jnp.float32)
    row_z = row_ids(REACH_Z).astype(jnp.float32)
    lanes = lane_ids(REACH_Z)

    def hat(rows, inside, along):
        return jnp.where(rows == inside, 1.0 - along, 0.0) + jnp.where(rows == inside + 1.0, along, 0.0)

    def place_of(at):
        k = list_ref[at]
        brick = jnp.where(k < nblocks, brick_ref[jnp.minimum(k, nblocks - 1)], 0)
        brick_x = lax.div(brick, count_y * count_z)
        brick_y = lax.rem(lax.div(brick, count_z), count_y)
        return k, brick_x * count_y + brick_y, lax.rem(brick, count_z)

    def loaded(at, lines_ref, table_ref):
        k, pair, brick_z = place_of(at)
        first = pl.multiple_of(pair * comps * rows_z + brick_z * BZ, 8)
        window = jnp.concatenate([lines_ref[pl.ds(first + c * rows_z, REACH_Z)] for c in range(comps)], axis=0)
        table = table_ref[pl.ds(pl.multiple_of(k * TABLE_ROWS, TABLE_ROWS), TABLE_ROWS)]
        return k, window, [table[i : i + 1] for i in range(TABLE_ROWS)]

    def weighted(rows):
        weight_y = hat(row_y, rows[IN_Y], rows[ALONG_Y])
        weight_z = hat(row_z, rows[IN_Z], rows[ALONG_Z])
        weight = jnp.concatenate([rows[WEIGHT + a] * weight_y for a in range(REACH_X)], axis=0)
        return weight_z, *parts_of(weight)

    def stepped(seen, weight_z, rows):
        rate = 1.0 / rows[RESPONSE]
        state, moved, pushed = [], [], []
        for c in range(comps):
            gas_sample = jnp.sum(seen[c * REACH_Z : (c + 1) * REACH_Z] * weight_z, axis=0, keepdims=True)
            drag = (gas_sample - rows[MOVING + c]) * rate
            state.append(rows[MOVING + c] + TIME_STEP * drag)
            moved.append(rows[OFFSET + c] + TIME_STEP * state[c])
            pushed.append(drag * weight_z)
        tile = jnp.broadcast_to(rows[RESPONSE], (STATE, LANES))
        for i, value in enumerate(state + moved):
            tile = jnp.where(sub == i, value, tile)
        return tile, jnp.concatenate(parts_of(jnp.concatenate(pushed, axis=0)), axis=0)

    def gathered(one, two):
        tables, windows, weights = [], [], []
        for _, window, rows in (one, two):
            weight_z, main, rest = weighted(rows)
            weights.append((weight_z, main, rest))
            unused = jnp.zeros((LANES - 3 * SPREAD, LANES), jnp.float32)
            tables.append(jnp.concatenate([main, main, rest, unused], axis=0).astype(jnp.bfloat16))
            windows.append(window)
        seen = lax.dot_general(
            jnp.concatenate(windows, axis=0).astype(jnp.bfloat16), jnp.concatenate(tables, axis=1),
            (((1,), (0,)), ((), ())), preferred_element_type=jnp.float32,
        )
        height = comps * REACH_Z
        tiles, fresh = [], []
        for i, (_, _, rows) in enumerate((one, two)):
            weight_z, main, rest = weights[i]
            mine = seen[i * height : (i + 1) * height, i * LANES : (i + 1) * LANES]
            tile, push = stepped(mine, weight_z, rows)
            tiles.append(tile)
            unused = jnp.zeros((LANES - comps * SPREAD, LANES), jnp.float32)
            spread = jnp.concatenate([main] * comps + [unused] + [rest] * comps + [unused], axis=0)
            fresh.append((push.astype(jnp.bfloat16), spread.astype(jnp.bfloat16)))
        return tiles, fresh

    def shared(push, spread):
        shares = lax.dot_general(push, spread, (((1,), (1,)), ((), ())), preferred_element_type=jnp.float32)
        height = comps * REACH_Z
        total = shares[:height, :LANES] + shares[:height, LANES:] + shares[height:, :LANES]
        result = jnp.zeros((REACH_Z, LANES), jnp.float32)
        for c in range(comps):
            inside = (lanes >= c * SPREAD) & (lanes < (c + 1) * SPREAD)
            result = jnp.where(inside, total[c * REACH_Z : (c + 1) * REACH_Z], result)
        return result

    def add(deposit_ref, at, shares):
        spots = []
        for u in range(len(shares)):
            _, pair, brick_z = place_of(at + u)
            spots.append(pl.ds(pl.multiple_of(pair * rows_z + brick_z * BZ, 8), REACH_Z))
        for spot, share in zip(spots, shares):
            deposit_ref[spot] = deposit_ref[spot] + share

    def group_of(taken):
        tiles, fresh = [], []
        for u in range(0, len(taken), 2):
            both, kept = gathered(taken[u], taken[u + 1])
            tiles.extend(both)
            fresh.extend(kept)
        return tiles, fresh

    def keep(state_ref, taken, tiles):
        for (k, _, _), tile in zip(taken, tiles):
            state_ref[pl.ds(pl.multiple_of(STATE * k, STATE), STATE)] = tile

    def deposits_of(kept):
        return [shared(push, spread) for push, spread in kept]

    return loaded, group_of, keep, deposits_of, add


def groups_in(list_ref, late, many=UNROLL):
    room = (list_ref.shape[0] - 2) // 2
    return late * room, (list_ref[2 * room + late] + many - 1) // many


def leave(crossing_ref, state_ref, leaving_ref, faces):
    slots = crossing_ref.shape[1]
    rows = leaving_ref.shape[0] // (len(faces) * slots)
    for i, face in enumerate(faces):
        tiles = []
        for slot in range(slots):
            block = crossing_ref[face, slot]
            spot = pl.ds(pl.multiple_of(jnp.maximum(block, 0) * STATE, STATE), STATE)
            live = jnp.full((STATE, LANES), block, jnp.int32) >= 0
            tiles.append(jnp.where(live, state_ref[spot], 0.0))
        for slot, tile in enumerate(tiles):
            leaving_ref[pl.ds(i * rows * slots + slot, rows, stride=slots)] = tile[:rows]


def fetched(sems, *pairs):
    copies = [pltpu.make_async_copy(source, target, sems.at[i]) for i, (source, target) in enumerate(pairs)]
    for copy in copies:
        copy.start()
    return copies


def gather_kernel(
    dims, list_in, brick_in, table_ref, grid_in_ref, lines_in_ref, face_ref, from_x_ref, edge_ref,
    state_ref, push_ref, spread_ref, grid_ref, lines_ref, top_ref, list_ref, brick_ref, turned_ref, sems,
):
    copies = fetched(sems, (list_in, list_ref), (brick_in, brick_ref))
    halo_xz_kernel(grid_in_ref, lines_in_ref, face_ref, from_x_ref, edge_ref, grid_ref, lines_ref, top_ref, turned_ref)
    for copy in copies:
        copy.wait()
    loaded, group_of, keep, _, _ = block_steps(dims, list_ref, brick_ref)
    base, groups = groups_in(list_ref, 0)

    @pl.loop(0, groups)
    def _(group):
        taken = [loaded(base + group * UNROLL + u, lines_ref, table_ref) for u in range(UNROLL)]
        tiles, fresh = group_of(taken)
        keep(state_ref, taken, tiles)
        for i, (push, spread) in enumerate(fresh):
            push_ref[group * UNROLL + i] = push
            spread_ref[group * UNROLL + i] = spread

    for i in range(UNROLL):
        push_ref[groups * UNROLL + i] = jnp.zeros(push_ref.shape[1:], push_ref.dtype)
        spread_ref[groups * UNROLL + i] = jnp.zeros(spread_ref.shape[1:], spread_ref.dtype)


def deposit_kernel(
    dims, list_ref, brick_ref, crossing_ref, push_ref, spread_ref, state_ref, deposit_in_ref, deposit_ref, leaving_ref
):
    _, _, _, deposits_of, add = block_steps(dims, list_ref, brick_ref)
    base, groups = groups_in(list_ref, 0, WIDE)
    leave(crossing_ref, state_ref, leaving_ref, (0, 1, 4, 5))

    @pl.loop(0, groups)
    def _(group):
        mine = [group * WIDE + i for i in range(WIDE)]
        add(deposit_ref, base + group * WIDE, deposits_of([(push_ref[i], spread_ref[i]) for i in mine]))


def late_kernel(
    dims, list_in, brick_in, crossing_in, table_ref, grid_in_ref, lines_in_ref, top_in_ref, first_ref, second_ref,
    state_in_ref, deposit_in_ref,
    grid_ref, lines_ref, state_ref, deposit_ref, leaving_ref,
    push_ref, spread_ref, list_ref, brick_ref, crossing_ref, turned_ref, sems,
):
    copies = fetched(sems, (list_in, list_ref), (brick_in, brick_ref), (crossing_in, crossing_ref))
    halo_y_kernel(
        dims[2] * BY, grid_in_ref, lines_in_ref, top_in_ref, first_ref, second_ref, grid_ref, lines_ref, turned_ref
    )
    for copy in copies:
        copy.wait()
    loaded, group_of, keep, deposits_of, add = block_steps(dims, list_ref, brick_ref)
    base, groups = groups_in(list_ref, 1)
    push_ref[...] = jnp.zeros_like(push_ref)
    spread_ref[...] = jnp.zeros_like(spread_ref)

    @pl.loop(0, groups + 1)
    def _(group):
        now = base + jnp.maximum(jnp.minimum(group, groups - 1), 0) * UNROLL
        before = base + jnp.maximum(group - 1, 0) * UNROLL
        taken = [loaded(now + u, lines_ref, table_ref) for u in range(UNROLL)]
        shares = deposits_of([(push_ref[i], spread_ref[i]) for i in range(UNROLL)])
        tiles, fresh = group_of(taken)
        add(deposit_ref, before, shares)
        keep(state_ref, taken, tiles)
        for i, (push, spread) in enumerate(fresh):
            push_ref[i] = push
            spread_ref[i] = spread

    leave(crossing_ref, state_ref, leaving_ref, (2, 3))


def top_rows(deposit_ref, q, count_x, count_y, rows_z, size_z):
    total = None
    for p in range(count_x):
        at = (p * count_y + q) * rows_z + size_z
        value = pltpu.roll(deposit_ref[at : at + 8], p, 0) if p else deposit_ref[at : at + 8]
        total = value if total is None else total + value
    return total


def send_y_kernel(push, diffuse, leaving_ref, grid_ref, deposit_ref, y_ref, tiles_ref, lines_ref):
    comps, size_x, size_y, size_z = grid_ref.shape[0], grid_ref.shape[1] - 2, grid_ref.shape[2] - 8, grid_ref.shape[3]
    count_x, count_y = size_x // BX, size_y // BY
    rows_z = size_z + 8
    rows = leaving_ref.shape[1]
    height = comps * SPREAD
    for p in range(count_x):
        at = (p * count_y + count_y - 1) * rows_z
        tiles_ref[p * height : (p + 1) * height] = jnp.transpose(deposit_ref[at : at + size_z])[:height]
    first = jnp.full((rows, LANES), odd("gy")) == 0
    y_ref[0, 0:rows] = jnp.where(first, leaving_ref[0], leaving_ref[1])
    y_ref[1, 0:rows] = jnp.where(first, leaving_ref[1], leaving_ref[0])
    lines_ref[...] = jnp.zeros_like(lines_ref)
    for c in range(comps):
        for p in range(count_x):
            spot = slice(c * ROWS_Y + p * BX, c * ROWS_Y + p * BX + REACH_X)
            line = tiles_ref[pl.ds(p * height + c * SPREAD + BY, REACH_X, stride=REACH_Y)]
            lines_ref[spot] = lines_ref[spot] + line
    wrapped = top_rows(deposit_ref, count_y - 1, count_x, count_y, rows_z, size_z)
    lane = lane_ids(8)
    packed = jnp.zeros((8, LANES), jnp.float32)
    for c in range(comps):
        spot = slice(c * ROWS_Y, (c + 1) * ROWS_Y)
        beside = jnp.concatenate([grid_ref[c, 1 : size_x + 1, size_y - 1], jnp.zeros((8, LANES), jnp.float32)], axis=0)
        line = push * lines_ref[spot] + diffuse * beside
        at = rows + c * (size_x + 1)
        y_ref[0, at : at + size_x + 1] = line[: size_x + 1]
        y_ref[1, at : at + size_x + 1] = line[: size_x + 1]
        for a in range(REACH_X):
            place = PACK * c + a
            value = turned(wrapped, place - c * SPREAD - a * REACH_Y - BY)
            packed = packed + jnp.where(lane == place, value, 0.0)
    corner = packed[0:1]
    for p in range(1, count_x):
        corner = corner + turned(packed[p : p + 1], p * BX)
    at = rows + comps * (size_x + 1)
    y_ref[0, at : at + 1] = push * corner
    y_ref[1, at : at + 1] = push * corner


def merge_kernel(deposit_ref, top_tiles_ref, plane_ref, face_ref, tiles_ref, turned_ref):
    comps, planes = plane_ref.shape[:2]
    count_x, size_z = (planes - 1) // BX, plane_ref.shape[3]
    rows_z = size_z + 8
    count_y = deposit_ref.shape[0] // (rows_z * count_x)
    height = comps * SPREAD
    for p in range(count_x):
        for q in range(count_y - 1):
            at = p * count_y + q
            value = jnp.transpose(deposit_ref[at * rows_z : at * rows_z + size_z])
            tiles_ref[at * height : (at + 1) * height] = value[:height]
    top = row_ids(REACH_Y) >= BY
    for c in range(comps):
        for x in range(planes):
            bricks = [(x // BX, x % BX)] if x < planes - 1 else []
            if x and x % BX == 0:
                bricks.append((x // BX - 1, BX))

            def tile(q):
                total = None
                for p, a in bricks:
                    at = c * SPREAD + a * REACH_Y
                    if q < count_y - 1:
                        value = tiles_ref[(p * count_y + q) * height + at : (p * count_y + q) * height + at + REACH_Y]
                    else:
                        value = top_tiles_ref[p * height + at : p * height + at + REACH_Y]
                    total = value if total is None else total + value
                return total

            carried = None
            for q in range(0, count_y, 2):
                here = tile(q)
                if carried is not None:
                    here = here + carried
                between = pltpu.roll(tile(q + 1), BY, 0)
                here = here + jnp.where(top, between, 0.0)
                carried = jnp.where(top, 0.0, between)
                plane_ref[c, x, q * BY : q * BY + REACH_Y] = here
            plane_ref[c, x, count_y * BY :] = carried

    lane = lane_ids(count_x)
    turned_ref[...] = jnp.zeros_like(turned_ref)
    for q in range(count_y):
        wrapped = top_rows(deposit_ref, q, count_x, count_y, rows_z, size_z)[:count_x]
        within = (lane >= q * BY) & (lane <= (q + 1) * BY)
        for c in range(comps):
            for a in range(REACH_X):
                value = turned(wrapped, q * BY - c * SPREAD - a * REACH_Y)
                spot = pl.ds(PACK * c + a, count_x, stride=BX)
                turned_ref[spot] = turned_ref[spot] + jnp.where(within, value, 0.0)
    face_ref[...] = jnp.transpose(turned_ref[...])[: face_ref.shape[0]]


def send_xz_kernel(push, diffuse, grid_ref, deposit_ref, face_ref, x_ref, z_ref):
    comps, size_x = grid_ref.shape[0], grid_ref.shape[1] - 2
    size_y = z_ref.shape[0]
    lane = lane_ids(size_y)
    packed = push * face_ref[0:size_y]
    for c in range(comps):
        for x in range(size_x):
            place = PACK * c + x
            packed = packed + jnp.where(lane == place, diffuse * turned(grid_ref[c, x + 1, 0:size_y], place + 1), 0.0)
        total = push * deposit_ref[c, size_x, 0:size_y]
        x_ref[c * size_y : (c + 1) * size_y] = diffuse * grid_ref[c, size_x, 0:size_y] + total
    z_ref[...] = packed


def base_kernel(push, diffuse, count, grid_ref, deposit_ref, top_ref, y1_ref, y2_ref, state_ref, base_ref, velocity_ref):
    comps, size_x, size_y, size_z = base_ref.shape
    lane, sub = lane_ids(size_y), row_ids(size_y)
    top = top_ref[0:size_y]
    for c in range(comps):
        at = count + c * (size_x + 1)
        lines = below(y1_ref, y2_ref, slice(at, at + size_x))
        for x in range(size_x):
            here = grid_ref[c, x + 1, 0:size_y]
            before = jnp.where(sub == 0, 0.0, pltpu.roll(here, 1, 0))
            laplace = grid_ref[c, x, 0:size_y] + grid_ref[c, x + 2, 0:size_y]
            laplace = laplace + grid_ref[c, x + 1, 1 : size_y + 1] + before
            ahead = jnp.where(lane == size_z - 1, turned(top, size_z - 1 - (PACK * c + x)), turned(here, -1))
            laplace = laplace + ahead + jnp.where(lane == 0, 0.0, turned(here, 1)) - 6.0 * here
            total = here + diffuse * laplace + push * deposit_ref[c, x, 0:size_y]
            line = jnp.broadcast_to(lines[x : x + 1], (size_y, LANES))
            base_ref[c, x] = total + jnp.where(sub == 0, line, 0.0)
        velocity_ref[c] = state_ref[pl.ds(c, velocity_ref.shape[1], stride=STATE)]


def below(first_ref, second_ref, rows):
    got = jnp.where(jnp.full((1, LANES), odd("gy")) == 1, first_ref[rows], second_ref[rows])
    return jnp.where(jnp.full((1, LANES), lax.axis_index("gy")) != 0, got, 0.0)


def relay_kernel(size_x, size_y, comps, count, first_ref, second_ref, x_in_ref, z_in_ref, leaving_ref, x_ref, z_ref, edge_ref):
    edge = comps * size_y
    x_ref[0:edge] = x_in_ref[...]
    for c in range(comps):
        at = count + c * (size_x + 1) + size_x
        spot = slice(c * size_y, c * size_y + 1)
        x_ref[spot] = x_in_ref[spot] + below(first_ref, second_ref, slice(at, at + 1))
    x_ref[edge : edge + count] = leaving_ref[0]
    if x_ref.shape[0] > edge + count:
        x_ref[edge + count : edge + 2 * count] = leaving_ref[1]
    at = count + comps * (size_x + 1)
    edge_ref[size_y:] = jnp.zeros((edge_ref.shape[0] - size_y, LANES), jnp.float32)
    edge_ref[0:size_y] = z_in_ref[...]
    edge_ref[0:1] = z_in_ref[0:1] + below(first_ref, second_ref, slice(at, at + 1))
    up = odd("gz")
    z_ref[up, 0:count] = leaving_ref[2]
    z_ref[up, count : count + size_y] = edge_ref[0:size_y]
    z_ref[1 - up, 0:count] = leaving_ref[3]
    z_ref[1 - up, count : count + size_y] = jnp.zeros((size_y, LANES), jnp.float32)


def finish_kernel(
    count, base_ref, y1_ref, y2_ref, x_ref, minus_x_ref, z1_ref, z2_ref, edge_ref, gas_out, arrivals_out,
    gas_ref, arrivals_ref, sems,
):
    comps, size_x, size_y, _ = base_ref.shape
    first_lane = lane_ids(size_y) == 0
    odd_y, odd_z = jnp.full((1, LANES), odd("gy")) == 1, jnp.full((1, LANES), odd("gz")) == 1
    place = jnp.full((1, LANES), lax.axis_index("gy"))
    lower, upper = place != 0, place != lax.axis_size("gy") - 1
    rows = slice(count, count + size_y)
    slots = arrivals_ref.shape[2]
    for i in range(arrivals_ref.shape[1]):

        def rows_of(ref, at=0):
            return ref[at + i * slots : at + (i + 1) * slots]

        arrivals_ref[0, i] = rows_of(x_ref, comps * size_y)
        arrivals_ref[1, i] = rows_of(minus_x_ref, minus_x_ref.shape[0] - count)
        y1, y2 = rows_of(y1_ref), rows_of(y2_ref)
        arrivals_ref[2, i] = jnp.where(lower, jnp.where(odd_y, y1, y2), 0.0)
        arrivals_ref[3, i] = jnp.where(upper, jnp.where(odd_y, y2, y1), 0.0)
        z1, z2 = rows_of(z1_ref), rows_of(z2_ref)
        arrivals_ref[4, i] = jnp.where(odd_z, z1, z2)
        arrivals_ref[5, i] = jnp.where(odd_z, z2, z1)
    copies = [pltpu.make_async_copy(arrivals_ref, arrivals_out, sems.at[comps])]
    copies[0].start()
    face = jnp.where(odd_z, z1_ref[rows], z2_ref[rows])
    corner = edge_ref[0:size_y]
    for c in range(comps):
        for x in range(size_x):
            total = base_ref[c, x]
            far = turned(face, -(PACK * c + x))
            if x == 0:
                total = total + x_ref[c * size_y : (c + 1) * size_y]
                far = far + turned(corner, -(PACK * c + size_x))
            gas_ref[c, x] = total + jnp.where(first_lane, far, 0.0)
        copies.append(pltpu.make_async_copy(gas_ref.at[c], gas_out.at[c], sems.at[c]))
        copies[-1].start()
    for copy in copies:
        copy.wait()


def per_device(gas_field, velocity, fraction, response, cell_index, brick_index, crossing):
    comps, size_x, size_y, size_z = gas_field.shape
    nblocks = velocity.shape[0]
    loading = 0.5 * size_x * size_y * size_z / (nblocks * 128)
    push, diffuse = -TIME_STEP * loading, TIME_STEP * VISCOSITY
    velocity = jnp.transpose(velocity, (1, 0, 2))
    fraction = jnp.transpose(fraction, (1, 0, 2))
    spare = nblocks + 8
    rows_z = size_z + 8
    grid_shape = (comps, size_x + 2, ROWS_Y, LANES)
    lines_shape = ((size_x // BX) * (size_y // BY) * comps * rows_z, LANES)
    deposit_shape = ((size_x // BX) * (size_y // BY) * rows_z, LANES)

    inputs = (gas_field, velocity, fraction, response, cell_index, brick_index, crossing)
    inputs = [pltpu.with_memory_space_constraint(array, pltpu.HBM) for array in inputs]
    grid, face, plane, velocity, fraction, response, cell_index, brick_index, crossing = call(
        begin_kernel,
        [grid_shape, (size_y, LANES), (comps * size_y, LANES)]
        + [jax.ShapeDtypeStruct(array.shape, array.dtype) for array in inputs[1:]],
        *inputs, hbm=range(7), scratch=(pltpu.SemaphoreType.DMA((comps + 6,)),),
    )
    from_z = moved_along(face, "gz", -1)
    from_x = moved_along(plane, "gx", -1)
    from_xz = moved_diagonally(face, -1)
    lines, deposit, table, ready, blocks = call(
        prepare_kernel,
        [
            lines_shape,
            deposit_shape,
            (TABLE_ROWS * spare, LANES),
            (8, LANES),
            jax.ShapeDtypeStruct((2 * (nblocks + WIDE) + 2,), jnp.int32),
        ],
        grid, velocity, fraction, response, cell_index, brick_index,
        smem=(5,), smem_outs=(4,), cycles=3000,
    )
    line_rows = -(-(comps * size_x + comps + 1) // 8) * 8
    (y_lines,) = call(y_lines_kernel, [(line_rows, LANES)], grid, from_z, from_x, from_xz, ready)
    y1, y2 = swapped_y((y_lines, y_lines))
    square = pltpu.VMEM((LANES, LANES), jnp.float32)
    scalars = (pltpu.SMEM(blocks.shape, jnp.int32), pltpu.SMEM(brick_index.shape, jnp.int32))
    dims = (comps, size_x // BX, size_y // BY, size_z // BZ, rows_z)
    slots = crossing.shape[1]
    count = 7 * slots

    def parts(many):
        return [(many, 2 * comps * REACH_Z, LANES), (many, 2 * LANES, LANES)]

    state, push_parts, spread_parts, grid, lines, top = call(
        functools.partial(gather_kernel, dims),
        [(STATE * spare, LANES)]
        + [jax.ShapeDtypeStruct(shape, jnp.bfloat16) for shape in parts(nblocks + 2 * UNROLL)]
        + [grid_shape, lines_shape, (LANES, LANES)],
        blocks, brick_index, table, grid, lines, from_z, from_x, from_xz,
        aliases={3: 3, 4: 4}, cycles=4000, scratch=(*scalars, square, pltpu.SemaphoreType.DMA((2,))),
    )
    grid, lines, state, deposit, leaving = call(
        functools.partial(late_kernel, dims),
        [grid_shape, lines_shape, (STATE * spare, LANES), deposit_shape, (2 * count, LANES)],
        blocks, brick_index, crossing, table, grid, lines, top, y1, y2, state, deposit,
        aliases={4: 0, 5: 1, 9: 2, 10: 3}, cycles=2000,
        scratch=[
            *(pltpu.VMEM(shape, jnp.bfloat16) for shape in parts(UNROLL)),
            *scalars,
            pltpu.SMEM(crossing.shape, jnp.int32),
            square,
            pltpu.SemaphoreType.DMA((3,)),
        ],
    )
    leaving = leaving.reshape(2, count, LANES)
    height = comps * SPREAD
    to_y, top_tiles = call(
        functools.partial(send_y_kernel, push, diffuse),
        [(2, count + line_rows, LANES), ((size_x // BX) * height, LANES)],
        leaving, grid, deposit, cycles=300, scratch=(pltpu.VMEM((comps * ROWS_Y, LANES), jnp.float32),),
    )
    y1, y2 = swapped_y((to_y[0], to_y[1]))
    deposit, leaving = call(
        functools.partial(deposit_kernel, dims), [deposit_shape, (4 * count, LANES)],
        blocks, brick_index, crossing, push_parts, spread_parts, state, deposit,
        smem=(0, 1, 2), aliases={6: 0}, cycles=4000,
    )
    leaving = leaving.reshape(4, count, LANES)
    deposit, over = call(
        merge_kernel, [(comps, size_x + 1, ROWS_Y, LANES), (ROWS_Y, LANES)], deposit, top_tiles,
        cycles=1000, scratch=(pltpu.VMEM(((size_x // BX) * (size_y // BY) * height, LANES), jnp.float32), square),
    )
    to_x, to_z = call(
        functools.partial(send_xz_kernel, push, diffuse), [(comps * size_y, LANES), (size_y, LANES)],
        grid, deposit, over, cycles=500,
    )
    base, velocity_next = call(
        functools.partial(base_kernel, push, diffuse, count), [gas_field.shape, (comps, nblocks, LANES)],
        grid, deposit, top, y1, y2, state, cycles=1000,
    )
    edge = comps * size_y
    both = lax.axis_size("gx") == 2
    to_x, to_z, to_xz = call(
        functools.partial(relay_kernel, size_x, size_y, comps, count),
        [(edge + (2 if both else 1) * count, LANES), (2, count + size_y, LANES), (count + size_y + 8, LANES)],
        y1, y2, to_x, to_z, leaving,
    )
    got_x = moved_along(to_x, "gx", 1)
    z1, z2 = swapped_z((to_z[0], to_z[1]))
    got_xz = moved_diagonally(to_xz, 1)
    got_mx = got_x if both else moved_along(leaving[1], "gx", -1)
    gas_next, arrivals = call(
        functools.partial(finish_kernel, count), [gas_field.shape, (6, 7, slots, LANES)],
        base, y1, y2, got_x, got_mx, z1, z2, got_xz, hbm_outs=(0, 1),
        scratch=(
            pltpu.VMEM(gas_field.shape, jnp.float32),
            pltpu.VMEM((6, 7, slots, LANES), jnp.float32),
            pltpu.SemaphoreType.DMA((comps + 1,)),
        ),
    )
    return gas_next, jnp.transpose(velocity_next, (1, 0, 2)), jnp.transpose(arrivals, (0, 2, 1, 3))


def solution(mesh):
    owner = ("gx", "gz", "gy")
    in_specs = (
        P(None, "gx", "gy", "gz"),
        P(owner, None, None),
        P(owner, None, None),
        P(owner, None),
        P(owner, None),
        P(owner),
        P(owner, None),
    )
    out_specs = (
        P(None, "gx", "gy", "gz"),
        P(owner, None, None),
        P(owner, None, None, None),
    )
    return jax.shard_map(
        per_device, mesh=mesh, in_specs=in_specs, out_specs=out_specs, check_vma=False
    )
```

```python
import functools

import jax
import jax.numpy as jnp
from jax import lax
from jax.experimental import pallas as pl
from jax.experimental.pallas import tpu as pltpu
from jax.sharding import PartitionSpec as P

BX = 4
BY = 4
BZ = 8

TIME_STEP = 0.25
VISCOSITY = 0.4

LANES = 128
PACK = 32
ROWS_Y = 24
REACH_X = BX + 1
REACH_Y = 8
SPREAD = REACH_X * REACH_Y
REACH_Z = 2 * BZ
UNROLL = 8
WIDE = 16

WEIGHT, ALONG_Y, IN_Y, ALONG_Z, IN_Z, RESPONSE, MOVING, OFFSET = 0, 5, 6, 7, 8, 9, 10, 13
TABLE_ROWS = 16
STATE = 8

VMEM = pl.BlockSpec(memory_space=pltpu.VMEM)
SMEM = pl.BlockSpec(memory_space=pltpu.SMEM)
HBM = pl.BlockSpec(memory_space=pltpu.HBM)


def moved_along(block, axis, distance):
    count = lax.axis_size(axis)
    return lax.ppermute(block, axis, [(i, (i + distance) % count) for i in range(count)])


def swapped_z(blocks):
    count = lax.axis_size("gz")
    first = [(i, i ^ 1) for i in range(count)]
    second = [(i, (((i + 1) ^ 1) - 1) % count) for i in range(count)]
    return lax.ppermute(blocks[0], "gz", first), lax.ppermute(blocks[1], "gz", second)


def swapped_y(blocks):
    nz, ny = lax.axis_size("gz"), lax.axis_size("gy")
    first = [(j, j ^ 1) for j in range(ny)]
    second = []
    for k in range(nz):
        second.append((k * ny, (k ^ 1) * ny))
        second.append((k * ny + ny - 1, (k ^ 1) * ny + ny - 1))
        second.extend((k * ny + j, k * ny + ((j + 1) ^ 1) - 1) for j in range(1, ny - 1))
    middle = lax.ppermute(blocks[1], ("gz", "gy"), second)
    return lax.ppermute(blocks[0], "gy", first), middle


def moved_diagonally(block, distance):
    nx, nz = lax.axis_size("gx"), lax.axis_size("gz")
    route = [(i * nz + k, (i + distance) % nx * nz + (k + distance) % nz) for i in range(nx) for k in range(nz)]
    return lax.ppermute(block, ("gx", "gz"), route)


def call(
    body, outs, *operands, smem=(), hbm=(), smem_outs=(), hbm_outs=(), scratch=(), aliases=None, cycles=0, limit=40
):
    return pl.pallas_call(
        body,
        out_shape=[o if isinstance(o, jax.ShapeDtypeStruct) else jax.ShapeDtypeStruct(o, jnp.float32) for o in outs],
        in_specs=[SMEM if i in smem else HBM if i in hbm else VMEM for i in range(len(operands))],
        out_specs=[SMEM if i in smem_outs else HBM if i in hbm_outs else VMEM for i in range(len(outs))],
        scratch_shapes=list(scratch),
        input_output_aliases=aliases or {},
        compiler_params=pltpu.CompilerParams(vmem_limit_bytes=limit * 1024 * 1024),
        cost_estimate=pl.CostEstimate(flops=cycles * 4096, bytes_accessed=cycles * 1024, transcendentals=0),
    )(*operands)


def lane_ids(rows):
    return lax.broadcasted_iota(jnp.int32, (rows, LANES), 1)


def row_ids(rows):
    return lax.broadcasted_iota(jnp.int32, (rows, LANES), 0)


def turned(value, shift):
    shift = shift % LANES
    return pltpu.roll(value, shift, 1) if shift else value


def odd(axis):
    return lax.axis_index(axis) % 2


def begin_kernel(
    gas_ref, velocity_in, fraction_in, response_in, cell_in, brick_in, crossing_in,
    grid_ref, face_ref, plane_ref, velocity_ref, fraction_ref, response_ref, cell_ref, brick_ref, crossing_ref, sems,
):
    comps, size_x, size_y, _ = gas_ref.shape
    pairs = [
        (gas_ref, grid_ref.at[:, 1 : size_x + 1, 0:size_y]),
        (velocity_in, velocity_ref), (fraction_in, fraction_ref), (response_in, response_ref),
        (cell_in, cell_ref), (brick_in, brick_ref), (crossing_in, crossing_ref),
    ]
    copies = [pltpu.make_async_copy(source, target, sems.at[i]) for i, (source, target) in enumerate(pairs)]
    for copy in copies:
        copy.start()
    zeros = jnp.zeros((ROWS_Y, LANES), jnp.float32)
    for c in range(comps):
        grid_ref[c, 0] = zeros
        grid_ref[c, size_x + 1] = zeros
        for x in range(size_x):
            grid_ref[c, x + 1, size_y:] = zeros[size_y:]
    copies[0].wait()
    lane = lane_ids(size_y)
    face = jnp.zeros((size_y, LANES), jnp.float32)
    for c in range(comps):
        plane_ref[c * size_y : (c + 1) * size_y] = grid_ref[c, 1, 0:size_y]
        for x in range(size_x):
            place = PACK * c + x
            face = jnp.where(lane == place, turned(grid_ref[c, x + 1, 0:size_y], place), face)
    face_ref[...] = face
    for copy in copies[1:]:
        copy.wait()


def parts_of(value):
    main = value.astype(jnp.bfloat16).astype(jnp.float32)
    return main, value - main


def lay_out(grid_ref, lines_ref, p, q, size_y, size_z):
    comps = grid_ref.shape[0]
    rows_z = size_z + 8
    count_y = size_y // BY
    for c in range(comps):
        planes = [grid_ref[c, p * BX + a + 1, q * BY : q * BY + REACH_Y] for a in range(REACH_X)]
        main, rest = parts_of(jnp.concatenate(planes, axis=0))
        stack = jnp.concatenate([main, rest, main, jnp.zeros((LANES - 3 * SPREAD, LANES), jnp.float32)], axis=0)
        at = ((p * count_y + q) * comps + c) * rows_z
        lines_ref[at : at + size_z] = jnp.transpose(stack)


def lay_out_top(turned_ref, lines_ref, q, comps, count_x, count_y, size_z):
    lane = lane_ids(count_x)
    rows_z = size_z + 8
    for c in range(comps):
        total = jnp.zeros((count_x, LANES), jnp.float32)
        for a in range(REACH_X):
            rows = turned_ref[pl.ds(PACK * c + a, count_x, stride=BX)]
            total = jnp.where(lane // REACH_Y == a, turned(rows, a * REACH_Y - q * BY), total)
        main, rest = parts_of(total)
        line = main + turned(rest, SPREAD) + turned(main, 2 * SPREAD)
        for p in range(count_x):
            at = ((p * count_y + q) * comps + c) * rows_z + size_z
            lines_ref[at : at + 1] = line[p : p + 1]


def prepare_kernel(
    grid_ref, velocity_ref, fraction_ref, response_ref, cell_ref, brick_ref,
    lines_ref, deposit_ref, table_ref, ready_ref, list_ref,
):
    comps, size_x, size_y, size_z = grid_ref.shape[0], grid_ref.shape[1] - 2, grid_ref.shape[2] - 8, grid_ref.shape[3]
    nblocks = velocity_ref.shape[1]
    count_x, count_y, count_z = size_x // BX, size_y // BY, size_z // BZ
    rows_z = size_z + 8


    def visit(k, counts):
        late = jnp.where(lax.rem(lax.div(brick_ref[k], count_z), count_y) == count_y - 1, 1, 0)
        list_ref[jnp.where(late == 1, nblocks + counts[1], counts[0])] = k
        return counts[0] + 1 - late, counts[1] + late

    early, late = lax.fori_loop(0, nblocks, visit, (jnp.int32(0), jnp.int32(0)), unroll=8)
    list_ref[2 * nblocks] = early
    list_ref[2 * nblocks + 1] = late
    ready_ref[...] = jnp.zeros_like(ready_ref)

    deposit_ref[...] = jnp.zeros_like(deposit_ref)
    for p in range(count_x):
        for q in range(count_y):
            for c in range(comps):
                at = ((p * count_y + q) * comps + c) * rows_z + size_z
                lines_ref[at : at + 8] = jnp.zeros((8, LANES), jnp.float32)
    for p in range(count_x - 1):
        for q in range(count_y - 1):
            lay_out(grid_ref, lines_ref, p, q, size_y, size_z)

    cells = cell_ref[...]
    cell_x, cell_y, cell_z = cells // (BY * BZ), cells // BZ % BY, cells % BZ
    along_x = fraction_ref[0]

    def put(row, value):
        table_ref[pl.ds(row, nblocks, stride=TABLE_ROWS)] = value

    for a in range(REACH_X):
        put(WEIGHT + a, jnp.where(cell_x == a, 1.0 - along_x, 0.0) + jnp.where(cell_x == a - 1, along_x, 0.0))
    put(ALONG_Y, fraction_ref[1])
    put(IN_Y, cell_y.astype(jnp.float32))
    put(ALONG_Z, fraction_ref[2])
    put(IN_Z, cell_z.astype(jnp.float32))
    put(RESPONSE, response_ref[...])
    for c in range(comps):
        put(MOVING + c, velocity_ref[c])
        put(OFFSET + c, fraction_ref[c])
    spare = table_ref.shape[0] - nblocks * TABLE_ROWS
    row = row_ids(spare)
    table_ref[nblocks * TABLE_ROWS :] = jnp.where(row % TABLE_ROWS == RESPONSE, 1.0, 0.0)


def y_lines_kernel(grid_ref, face_ref, from_x_ref, edge_ref, ready_ref, out_ref):
    comps, size_x = grid_ref.shape[0], grid_ref.shape[1] - 2
    size_y = face_ref.shape[0]
    for c in range(comps):
        out_ref[c * size_x : (c + 1) * size_x] = grid_ref[c, 1 : size_x + 1, 0]
        out_ref[comps * size_x + c : comps * size_x + c + 1] = from_x_ref[c * size_y : c * size_y + 1]
    line = jnp.where(lane_ids(8) % PACK == size_x, turned(edge_ref[0:8], size_x), face_ref[0:8])
    out_ref[comps * size_x + comps : comps * size_x + comps + 1] = line[0:1]


def halo_xz_kernel(grid_in_ref, lines_in_ref, face_ref, from_x_ref, edge_ref, grid_ref, lines_ref, top_ref, turned_ref):
    comps, size_x = grid_ref.shape[0], grid_ref.shape[1] - 2
    size_y, size_z = face_ref.shape[0], grid_ref.shape[3]
    count_x, count_y = size_x // BX, size_y // BY
    for c in range(comps):
        grid_ref[c, size_x + 1, 0:size_y] = from_x_ref[c * size_y : (c + 1) * size_y]
    for q in range(count_y - 1):
        lay_out(grid_ref, lines_ref, count_x - 1, q, size_y, size_z)
    top = jnp.where(lane_ids(size_y) % PACK == size_x, turned(edge_ref[...], size_x), face_ref[...])
    top_ref[0:size_y] = top
    top_ref[size_y:] = jnp.zeros((LANES - size_y, LANES), jnp.float32)
    turned_ref[...] = jnp.transpose(top_ref[...])
    for q in range(count_y - 1):
        lay_out_top(turned_ref, lines_ref, q, comps, count_x, count_y, size_z)


def halo_y_kernel(size_y, grid_in_ref, lines_in_ref, top_in_ref, first_ref, second_ref, grid_ref, lines_ref, turned_ref):
    comps, size_x, size_z = grid_ref.shape[0], grid_ref.shape[1] - 2, grid_ref.shape[3]
    count_x, count_y = size_x // BX, size_y // BY
    inside = lax.axis_index("gy") != lax.axis_size("gy") - 1
    kept = (row_ids(8) == 0) & inside
    even = jnp.full((1, LANES), odd("gy")) == 0

    def line_at(row):
        line = jnp.where(even, first_ref[row : row + 1], second_ref[row : row + 1])
        return jnp.where(kept, jnp.broadcast_to(line, (8, LANES)), 0.0)

    for c in range(comps):
        for x in range(size_x + 1):
            grid_ref[c, x + 1, size_y:] = line_at(c * size_x + x if x < size_x else comps * size_x + c)
    for p in range(count_x):
        lay_out(grid_ref, lines_ref, p, count_y - 1, size_y, size_z)
    corner = line_at(comps * size_x + comps)
    rest = jnp.zeros((LANES - size_y - 8, LANES), jnp.float32)
    turned_ref[...] = jnp.transpose(jnp.concatenate([top_in_ref[0:size_y], corner, rest], axis=0))
    lay_out_top(turned_ref, lines_ref, count_y - 1, comps, count_x, count_y, size_z)


def block_steps(dims, list_ref, brick_ref, end):
    comps, _, count_y, count_z, rows_z = dims
    nblocks = brick_ref.shape[0]
    sub = row_ids(8)
    row_y = row_ids(REACH_Y).astype(jnp.float32)
    row_z = row_ids(REACH_Z).astype(jnp.float32)
    lanes = lane_ids(REACH_Z)

    def hat(rows, inside, along):
        return jnp.where(rows == inside, 1.0 - along, 0.0) + jnp.where(rows == inside + 1.0, along, 0.0)

    def place_of(at):
        k = jnp.where(at < end, list_ref[jnp.minimum(at, 2 * nblocks + 1)], nblocks)
        brick = jnp.where(k < nblocks, brick_ref[jnp.minimum(k, nblocks - 1)], 0)
        brick_x = lax.div(brick, count_y * count_z)
        brick_y = lax.rem(lax.div(brick, count_z), count_y)
        return k, brick_x * count_y + brick_y, lax.rem(brick, count_z)

    def loaded(at, lines_ref, table_ref):
        k, pair, brick_z = place_of(at)
        first = pl.multiple_of(pair * comps * rows_z + brick_z * BZ, 8)
        window = jnp.concatenate([lines_ref[pl.ds(first + c * rows_z, REACH_Z)] for c in range(comps)], axis=0)
        table = table_ref[pl.ds(pl.multiple_of(k * TABLE_ROWS, TABLE_ROWS), TABLE_ROWS)]
        return k, window, [table[i : i + 1] for i in range(TABLE_ROWS)]

    def weighted(rows):
        weight_y = hat(row_y, rows[IN_Y], rows[ALONG_Y])
        weight_z = hat(row_z, rows[IN_Z], rows[ALONG_Z])
        weight = jnp.concatenate([rows[WEIGHT + a] * weight_y for a in range(REACH_X)], axis=0)
        return weight_z, *parts_of(weight)

    def stepped(seen, weight_z, rows):
        rate = 1.0 / rows[RESPONSE]
        state, moved, pushed = [], [], []
        for c in range(comps):
            gas_sample = jnp.sum(seen[c * REACH_Z : (c + 1) * REACH_Z] * weight_z, axis=0, keepdims=True)
            drag = (gas_sample - rows[MOVING + c]) * rate
            state.append(rows[MOVING + c] + TIME_STEP * drag)
            moved.append(rows[OFFSET + c] + TIME_STEP * state[c])
            pushed.append(drag * weight_z)
        tile = jnp.broadcast_to(rows[RESPONSE], (STATE, LANES))
        for i, value in enumerate(state + moved):
            tile = jnp.where(sub == i, value, tile)
        return tile, jnp.concatenate(parts_of(jnp.concatenate(pushed, axis=0)), axis=0)

    def gathered(one, two):
        tables, windows, weights = [], [], []
        for _, window, rows in (one, two):
            weight_z, main, rest = weighted(rows)
            weights.append((weight_z, main, rest))
            unused = jnp.zeros((LANES - 3 * SPREAD, LANES), jnp.float32)
            tables.append(jnp.concatenate([main, main, rest, unused], axis=0).astype(jnp.bfloat16))
            windows.append(window)
        seen = lax.dot_general(
            jnp.concatenate(windows, axis=0).astype(jnp.bfloat16), jnp.concatenate(tables, axis=1),
            (((1,), (0,)), ((), ())), preferred_element_type=jnp.float32,
        )
        height = comps * REACH_Z
        tiles, fresh = [], []
        for i, (_, _, rows) in enumerate((one, two)):
            weight_z, main, rest = weights[i]
            mine = seen[i * height : (i + 1) * height, i * LANES : (i + 1) * LANES]
            tile, push = stepped(mine, weight_z, rows)
            tiles.append(tile)
            unused = jnp.zeros((LANES - comps * SPREAD, LANES), jnp.float32)
            spread = jnp.concatenate([main] * comps + [unused] + [rest] * comps + [unused], axis=0)
            fresh.append((push.astype(jnp.bfloat16), spread.astype(jnp.bfloat16)))
        return tiles, fresh

    def shared(push, spread):
        shares = lax.dot_general(push, spread, (((1,), (1,)), ((), ())), preferred_element_type=jnp.float32)
        height = comps * REACH_Z
        total = shares[:height, :LANES] + shares[:height, LANES:] + shares[height:, :LANES]
        result = jnp.zeros((REACH_Z, LANES), jnp.float32)
        for c in range(comps):
            inside = (lanes >= c * SPREAD) & (lanes < (c + 1) * SPREAD)
            result = jnp.where(inside, total[c * REACH_Z : (c + 1) * REACH_Z], result)
        return result

    def add(deposit_ref, at, shares):
        spots = []
        for u in range(len(shares)):
            _, pair, brick_z = place_of(at + u)
            spots.append(pl.ds(pl.multiple_of(pair * rows_z + brick_z * BZ, 8), REACH_Z))
        for spot, share in zip(spots, shares):
            deposit_ref[spot] = deposit_ref[spot] + share

    def group_of(taken):
        tiles, fresh = [], []
        for u in range(0, len(taken), 2):
            both, kept = gathered(taken[u], taken[u + 1])
            tiles.extend(both)
            fresh.extend(kept)
        return tiles, fresh

    def keep(state_ref, taken, tiles):
        for (k, _, _), tile in zip(taken, tiles):
            state_ref[pl.ds(pl.multiple_of(STATE * k, STATE), STATE)] = tile

    def deposits_of(kept):
        return [shared(push, spread) for push, spread in kept]

    return loaded, group_of, keep, deposits_of, add


def groups_in(list_ref, late, many=UNROLL):
    room = (list_ref.shape[0] - 2) // 2
    count = list_ref[2 * room + late]
    return late * room, (count + many - 1) // many, late * room + count


def leave(crossing_ref, state_ref, leaving_ref, faces):
    slots = crossing_ref.shape[1]
    rows = leaving_ref.shape[0] // (len(faces) * slots)
    for i, face in enumerate(faces):
        tiles = []
        for slot in range(slots):
            block = crossing_ref[face, slot]
            spot = pl.ds(pl.multiple_of(jnp.maximum(block, 0) * STATE, STATE), STATE)
            live = jnp.full((STATE, LANES), block, jnp.int32) >= 0
            tiles.append(jnp.where(live, state_ref[spot], 0.0))
        for slot, tile in enumerate(tiles):
            leaving_ref[pl.ds(i * rows * slots + slot, rows, stride=slots)] = tile[:rows]


def fetched(sems, *pairs):
    copies = [pltpu.make_async_copy(source, target, sems.at[i]) for i, (source, target) in enumerate(pairs)]
    for copy in copies:
        copy.start()
    return copies


def gather_kernel(
    dims, list_in, brick_in, table_ref, grid_in_ref, lines_in_ref, face_ref, from_x_ref, edge_ref,
    state_ref, push_ref, spread_ref, grid_ref, lines_ref, top_ref, list_ref, brick_ref, turned_ref, sems,
):
    copies = fetched(sems, (list_in, list_ref), (brick_in, brick_ref))
    halo_xz_kernel(grid_in_ref, lines_in_ref, face_ref, from_x_ref, edge_ref, grid_ref, lines_ref, top_ref, turned_ref)
    for copy in copies:
        copy.wait()
    base, groups, end = groups_in(list_ref, 0)
    loaded, group_of, keep, _, _ = block_steps(dims, list_ref, brick_ref, end)

    @pl.loop(0, groups)
    def _(group):
        taken = [loaded(base + group * UNROLL + u, lines_ref, table_ref) for u in range(UNROLL)]
        tiles, fresh = group_of(taken)
        keep(state_ref, taken, tiles)
        for i, (push, spread) in enumerate(fresh):
            push_ref[group * UNROLL + i] = push
            spread_ref[group * UNROLL + i] = spread

    for i in range(UNROLL):
        push_ref[groups * UNROLL + i] = jnp.zeros(push_ref.shape[1:], push_ref.dtype)
        spread_ref[groups * UNROLL + i] = jnp.zeros(spread_ref.shape[1:], spread_ref.dtype)


def deposit_kernel(
    dims, list_ref, brick_ref, crossing_ref, push_ref, spread_ref, state_ref, deposit_in_ref, deposit_ref, leaving_ref
):
    base, groups, end = groups_in(list_ref, 0, WIDE)
    _, _, _, deposits_of, add = block_steps(dims, list_ref, brick_ref, end)
    leave(crossing_ref, state_ref, leaving_ref, (0, 1, 4, 5))

    @pl.loop(0, groups)
    def _(group):
        mine = [group * WIDE + i for i in range(WIDE)]
        add(deposit_ref, base + group * WIDE, deposits_of([(push_ref[i], spread_ref[i]) for i in mine]))


def late_kernel(
    dims, list_in, brick_in, crossing_in, table_ref, grid_in_ref, lines_in_ref, top_in_ref, first_ref, second_ref,
    state_in_ref, deposit_in_ref,
    grid_ref, lines_ref, state_ref, deposit_ref, leaving_ref,
    push_ref, spread_ref, list_ref, brick_ref, crossing_ref, turned_ref, sems,
):
    copies = fetched(sems, (list_in, list_ref), (brick_in, brick_ref), (crossing_in, crossing_ref))
    halo_y_kernel(
        dims[2] * BY, grid_in_ref, lines_in_ref, top_in_ref, first_ref, second_ref, grid_ref, lines_ref, turned_ref
    )
    for copy in copies:
        copy.wait()
    base, groups, end = groups_in(list_ref, 1)
    loaded, group_of, keep, deposits_of, add = block_steps(dims, list_ref, brick_ref, end)
    push_ref[...] = jnp.zeros_like(push_ref)
    spread_ref[...] = jnp.zeros_like(spread_ref)

    @pl.loop(0, groups + 1)
    def _(group):
        now = base + jnp.maximum(jnp.minimum(group, groups - 1), 0) * UNROLL
        before = base + jnp.maximum(group - 1, 0) * UNROLL
        taken = [loaded(now + u, lines_ref, table_ref) for u in range(UNROLL)]
        shares = deposits_of([(push_ref[i], spread_ref[i]) for i in range(UNROLL)])
        tiles, fresh = group_of(taken)
        add(deposit_ref, before, shares)
        keep(state_ref, taken, tiles)
        for i, (push, spread) in enumerate(fresh):
            push_ref[i] = push
            spread_ref[i] = spread

    leave(crossing_ref, state_ref, leaving_ref, (2, 3))


def top_rows(deposit_ref, q, count_x, count_y, rows_z, size_z):
    total = None
    for p in range(count_x):
        at = (p * count_y + q) * rows_z + size_z
        value = pltpu.roll(deposit_ref[at : at + 8], p, 0) if p else deposit_ref[at : at + 8]
        total = value if total is None else total + value
    return total


def send_y_kernel(push, diffuse, leaving_ref, grid_ref, deposit_ref, y_ref, tiles_ref, lines_ref):
    comps, size_x, size_y, size_z = grid_ref.shape[0], grid_ref.shape[1] - 2, grid_ref.shape[2] - 8, grid_ref.shape[3]
    count_x, count_y = size_x // BX, size_y // BY
    rows_z = size_z + 8
    rows = leaving_ref.shape[1]
    height = comps * SPREAD
    for p in range(count_x):
        at = (p * count_y + count_y - 1) * rows_z
        tiles_ref[p * height : (p + 1) * height] = jnp.transpose(deposit_ref[at : at + size_z])[:height]
    first = jnp.full((rows, LANES), odd("gy")) == 0
    y_ref[0, 0:rows] = jnp.where(first, leaving_ref[0], leaving_ref[1])
    y_ref[1, 0:rows] = jnp.where(first, leaving_ref[1], leaving_ref[0])
    lines_ref[...] = jnp.zeros_like(lines_ref)
    for c in range(comps):
        for p in range(count_x):
            spot = slice(c * ROWS_Y + p * BX, c * ROWS_Y + p * BX + REACH_X)
            line = tiles_ref[pl.ds(p * height + c * SPREAD + BY, REACH_X, stride=REACH_Y)]
            lines_ref[spot] = lines_ref[spot] + line
    wrapped = top_rows(deposit_ref, count_y - 1, count_x, count_y, rows_z, size_z)
    lane = lane_ids(8)
    packed = jnp.zeros((8, LANES), jnp.float32)
    for c in range(comps):
        spot = slice(c * ROWS_Y, (c + 1) * ROWS_Y)
        beside = jnp.concatenate([grid_ref[c, 1 : size_x + 1, size_y - 1], jnp.zeros((8, LANES), jnp.float32)], axis=0)
        line = push * lines_ref[spot] + diffuse * beside
        at = rows + c * (size_x + 1)
        y_ref[0, at : at + size_x + 1] = line[: size_x + 1]
        y_ref[1, at : at + size_x + 1] = line[: size_x + 1]
        for a in range(REACH_X):
            place = PACK * c + a
            value = turned(wrapped, place - c * SPREAD - a * REACH_Y - BY)
            packed = packed + jnp.where(lane == place, value, 0.0)
    corner = packed[0:1]
    for p in range(1, count_x):
        corner = corner + turned(packed[p : p + 1], p * BX)
    at = rows + comps * (size_x + 1)
    y_ref[0, at : at + 1] = push * corner
    y_ref[1, at : at + 1] = push * corner


def merge_kernel(deposit_ref, top_tiles_ref, plane_ref, face_ref, tiles_ref, turned_ref):
    comps, planes = plane_ref.shape[:2]
    count_x, size_z = (planes - 1) // BX, plane_ref.shape[3]
    rows_z = size_z + 8
    count_y = deposit_ref.shape[0] // (rows_z * count_x)
    height = comps * SPREAD
    for p in range(count_x):
        for q in range(count_y - 1):
            at = p * count_y + q
            value = jnp.transpose(deposit_ref[at * rows_z : at * rows_z + size_z])
            tiles_ref[at * height : (at + 1) * height] = value[:height]
    top = row_ids(REACH_Y) >= BY
    for c in range(comps):
        for x in range(planes):
            bricks = [(x // BX, x % BX)] if x < planes - 1 else []
            if x and x % BX == 0:
                bricks.append((x // BX - 1, BX))

            def tile(q):
                total = None
                for p, a in bricks:
                    at = c * SPREAD + a * REACH_Y
                    if q < count_y - 1:
                        value = tiles_ref[(p * count_y + q) * height + at : (p * count_y + q) * height + at + REACH_Y]
                    else:
                        value = top_tiles_ref[p * height + at : p * height + at + REACH_Y]
                    total = value if total is None else total + value
                return total

            carried = None
            for q in range(0, count_y, 2):
                here = tile(q)
                if carried is not None:
                    here = here + carried
                between = pltpu.roll(tile(q + 1), BY, 0)
                here = here + jnp.where(top, between, 0.0)
                carried = jnp.where(top, 0.0, between)
                plane_ref[c, x, q * BY : q * BY + REACH_Y] = here
            plane_ref[c, x, count_y * BY :] = carried

    lane = lane_ids(count_x)
    turned_ref[...] = jnp.zeros_like(turned_ref)
    for q in range(count_y):
        wrapped = top_rows(deposit_ref, q, count_x, count_y, rows_z, size_z)[:count_x]
        within = (lane >= q * BY) & (lane <= (q + 1) * BY)
        for c in range(comps):
            for a in range(REACH_X):
                value = turned(wrapped, q * BY - c * SPREAD - a * REACH_Y)
                spot = pl.ds(PACK * c + a, count_x, stride=BX)
                turned_ref[spot] = turned_ref[spot] + jnp.where(within, value, 0.0)
    face_ref[...] = jnp.transpose(turned_ref[...])[: face_ref.shape[0]]


def send_xz_kernel(push, diffuse, grid_ref, deposit_ref, face_ref, x_ref, z_ref):
    comps, size_x = grid_ref.shape[0], grid_ref.shape[1] - 2
    size_y = z_ref.shape[0]
    lane = lane_ids(size_y)
    packed = push * face_ref[0:size_y]
    for c in range(comps):
        for x in range(size_x):
            place = PACK * c + x
            packed = packed + jnp.where(lane == place, diffuse * turned(grid_ref[c, x + 1, 0:size_y], place + 1), 0.0)
        total = push * deposit_ref[c, size_x, 0:size_y]
        x_ref[c * size_y : (c + 1) * size_y] = diffuse * grid_ref[c, size_x, 0:size_y] + total
    z_ref[...] = packed


def base_kernel(push, diffuse, count, grid_ref, deposit_ref, top_ref, y1_ref, y2_ref, state_ref, base_ref, velocity_ref):
    comps, size_x, size_y, size_z = base_ref.shape
    lane, sub = lane_ids(size_y), row_ids(size_y)
    top = top_ref[0:size_y]
    for c in range(comps):
        at = count + c * (size_x + 1)
        lines = below(y1_ref, y2_ref, slice(at, at + size_x))
        for x in range(size_x):
            here = grid_ref[c, x + 1, 0:size_y]
            before = jnp.where(sub == 0, 0.0, pltpu.roll(here, 1, 0))
            laplace = grid_ref[c, x, 0:size_y] + grid_ref[c, x + 2, 0:size_y]
            laplace = laplace + grid_ref[c, x + 1, 1 : size_y + 1] + before
            ahead = jnp.where(lane == size_z - 1, turned(top, size_z - 1 - (PACK * c + x)), turned(here, -1))
            laplace = laplace + ahead + jnp.where(lane == 0, 0.0, turned(here, 1)) - 6.0 * here
            total = here + diffuse * laplace + push * deposit_ref[c, x, 0:size_y]
            line = jnp.broadcast_to(lines[x : x + 1], (size_y, LANES))
            base_ref[c, x] = total + jnp.where(sub == 0, line, 0.0)
        velocity_ref[c] = state_ref[pl.ds(c, velocity_ref.shape[1], stride=STATE)]


def below(first_ref, second_ref, rows):
    got = jnp.where(jnp.full((1, LANES), odd("gy")) == 1, first_ref[rows], second_ref[rows])
    return jnp.where(jnp.full((1, LANES), lax.axis_index("gy")) != 0, got, 0.0)


def relay_kernel(size_x, size_y, comps, count, first_ref, second_ref, x_in_ref, z_in_ref, leaving_ref, x_ref, z_ref, edge_ref):
    edge = comps * size_y
    x_ref[0:edge] = x_in_ref[...]
    for c in range(comps):
        at = count + c * (size_x + 1) + size_x
        spot = slice(c * size_y, c * size_y + 1)
        x_ref[spot] = x_in_ref[spot] + below(first_ref, second_ref, slice(at, at + 1))
    x_ref[edge : edge + count] = leaving_ref[0]
    if x_ref.shape[0] > edge + count:
        x_ref[edge + count : edge + 2 * count] = leaving_ref[1]
    at = count + comps * (size_x + 1)
    edge_ref[size_y:] = jnp.zeros((edge_ref.shape[0] - size_y, LANES), jnp.float32)
    edge_ref[0:size_y] = z_in_ref[...]
    edge_ref[0:1] = z_in_ref[0:1] + below(first_ref, second_ref, slice(at, at + 1))
    up = odd("gz")
    z_ref[up, 0:count] = leaving_ref[2]
    z_ref[up, count : count + size_y] = edge_ref[0:size_y]
    z_ref[1 - up, 0:count] = leaving_ref[3]
    z_ref[1 - up, count : count + size_y] = jnp.zeros((size_y, LANES), jnp.float32)


def finish_kernel(
    count, base_ref, y1_ref, y2_ref, x_ref, minus_x_ref, z1_ref, z2_ref, edge_ref, gas_out, arrivals_out,
    gas_ref, arrivals_ref, sems,
):
    comps, size_x, size_y, _ = base_ref.shape
    first_lane = lane_ids(size_y) == 0
    odd_y, odd_z = jnp.full((1, LANES), odd("gy")) == 1, jnp.full((1, LANES), odd("gz")) == 1
    place = jnp.full((1, LANES), lax.axis_index("gy"))
    lower, upper = place != 0, place != lax.axis_size("gy") - 1
    rows = slice(count, count + size_y)
    slots = arrivals_ref.shape[2]
    for i in range(arrivals_ref.shape[1]):

        def rows_of(ref, at=0):
            return ref[at + i * slots : at + (i + 1) * slots]

        arrivals_ref[0, i] = rows_of(x_ref, comps * size_y)
        arrivals_ref[1, i] = rows_of(minus_x_ref, minus_x_ref.shape[0] - count)
        y1, y2 = rows_of(y1_ref), rows_of(y2_ref)
        arrivals_ref[2, i] = jnp.where(lower, jnp.where(odd_y, y1, y2), 0.0)
        arrivals_ref[3, i] = jnp.where(upper, jnp.where(odd_y, y2, y1), 0.0)
        z1, z2 = rows_of(z1_ref), rows_of(z2_ref)
        arrivals_ref[4, i] = jnp.where(odd_z, z1, z2)
        arrivals_ref[5, i] = jnp.where(odd_z, z2, z1)
    copies = [pltpu.make_async_copy(arrivals_ref, arrivals_out, sems.at[comps])]
    copies[0].start()
    face = jnp.where(odd_z, z1_ref[rows], z2_ref[rows])
    corner = edge_ref[0:size_y]
    for c in range(comps):
        for x in range(size_x):
            total = base_ref[c, x]
            far = turned(face, -(PACK * c + x))
            if x == 0:
                total = total + x_ref[c * size_y : (c + 1) * size_y]
                far = far + turned(corner, -(PACK * c + size_x))
            gas_ref[c, x] = total + jnp.where(first_lane, far, 0.0)
        copies.append(pltpu.make_async_copy(gas_ref.at[c], gas_out.at[c], sems.at[c]))
        copies[-1].start()
    for copy in copies:
        copy.wait()


def per_device(gas_field, velocity, fraction, response, cell_index, brick_index, crossing):
    comps, size_x, size_y, size_z = gas_field.shape
    nblocks = velocity.shape[0]
    loading = 0.5 * size_x * size_y * size_z / (nblocks * 128)
    push, diffuse = -TIME_STEP * loading, TIME_STEP * VISCOSITY
    velocity = jnp.transpose(velocity, (1, 0, 2))
    fraction = jnp.transpose(fraction, (1, 0, 2))
    spare = nblocks + 8
    rows_z = size_z + 8
    grid_shape = (comps, size_x + 2, ROWS_Y, LANES)
    lines_shape = ((size_x // BX) * (size_y // BY) * comps * rows_z, LANES)
    deposit_shape = ((size_x // BX) * (size_y // BY) * rows_z, LANES)

    inputs = (gas_field, velocity, fraction, response, cell_index, brick_index, crossing)
    inputs = [pltpu.with_memory_space_constraint(array, pltpu.HBM) for array in inputs]
    grid, face, plane, velocity, fraction, response, cell_index, brick_index, crossing = call(
        begin_kernel,
        [grid_shape, (size_y, LANES), (comps * size_y, LANES)]
        + [jax.ShapeDtypeStruct(array.shape, array.dtype) for array in inputs[1:]],
        *inputs, hbm=range(7), scratch=(pltpu.SemaphoreType.DMA((7,)),),
    )
    from_z = moved_along(face, "gz", -1)
    from_x = moved_along(plane, "gx", -1)
    from_xz = moved_diagonally(face, -1)
    lines, deposit, table, ready, blocks = call(
        prepare_kernel,
        [
            lines_shape,
            deposit_shape,
            (TABLE_ROWS * spare, LANES),
            (8, LANES),
            jax.ShapeDtypeStruct((2 * nblocks + 2,), jnp.int32),
        ],
        grid, velocity, fraction, response, cell_index, brick_index,
        smem=(5,), smem_outs=(4,), cycles=3000,
    )
    line_rows = -(-(comps * size_x + comps + 1) // 8) * 8
    (y_lines,) = call(y_lines_kernel, [(line_rows, LANES)], grid, from_z, from_x, from_xz, ready)
    y1, y2 = swapped_y((y_lines, y_lines))
    square = pltpu.VMEM((LANES, LANES), jnp.float32)
    scalars = (pltpu.SMEM(blocks.shape, jnp.int32), pltpu.SMEM(brick_index.shape, jnp.int32))
    dims = (comps, size_x // BX, size_y // BY, size_z // BZ, rows_z)
    slots = crossing.shape[1]
    count = 7 * slots

    def parts(many):
        return [(many, 2 * comps * REACH_Z, LANES), (many, 2 * LANES, LANES)]

    state, push_parts, spread_parts, grid, lines, top = call(
        functools.partial(gather_kernel, dims),
        [(STATE * spare, LANES)]
        + [jax.ShapeDtypeStruct(shape, jnp.bfloat16) for shape in parts(nblocks + 2 * UNROLL)]
        + [grid_shape, lines_shape, (LANES, LANES)],
        blocks, brick_index, table, grid, lines, from_z, from_x, from_xz,
        aliases={3: 3, 4: 4}, cycles=4000, scratch=(*scalars, square, pltpu.SemaphoreType.DMA((2,))),
    )
    grid, lines, state, deposit, leaving = call(
        functools.partial(late_kernel, dims),
        [grid_shape, lines_shape, (STATE * spare, LANES), deposit_shape, (2 * count, LANES)],
        blocks, brick_index, crossing, table, grid, lines, top, y1, y2, state, deposit,
        aliases={4: 0, 5: 1, 9: 2, 10: 3}, cycles=2000,
        scratch=[
            *(pltpu.VMEM(shape, jnp.bfloat16) for shape in parts(UNROLL)),
            *scalars,
            pltpu.SMEM(crossing.shape, jnp.int32),
            square,
            pltpu.SemaphoreType.DMA((3,)),
        ],
    )
    leaving = leaving.reshape(2, count, LANES)
    height = comps * SPREAD
    to_y, top_tiles = call(
        functools.partial(send_y_kernel, push, diffuse),
        [(2, count + line_rows, LANES), ((size_x // BX) * height, LANES)],
        leaving, grid, deposit, cycles=300, scratch=(pltpu.VMEM((comps * ROWS_Y, LANES), jnp.float32),),
    )
    y1, y2 = swapped_y((to_y[0], to_y[1]))
    deposit, leaving = call(
        functools.partial(deposit_kernel, dims), [deposit_shape, (4 * count, LANES)],
        blocks, brick_index, crossing, push_parts, spread_parts, state, deposit,
        smem=(0, 1, 2), aliases={6: 0}, cycles=4000,
    )
    leaving = leaving.reshape(4, count, LANES)
    deposit, over = call(
        merge_kernel, [(comps, size_x + 1, ROWS_Y, LANES), (ROWS_Y, LANES)], deposit, top_tiles,
        cycles=1000, scratch=(pltpu.VMEM(((size_x // BX) * (size_y // BY) * height, LANES), jnp.float32), square),
    )
    to_x, to_z = call(
        functools.partial(send_xz_kernel, push, diffuse), [(comps * size_y, LANES), (size_y, LANES)],
        grid, deposit, over, cycles=500,
    )
    base, velocity_next = call(
        functools.partial(base_kernel, push, diffuse, count), [gas_field.shape, (comps, nblocks, LANES)],
        grid, deposit, top, y1, y2, state, cycles=1000,
    )
    edge = comps * size_y
    both = lax.axis_size("gx") == 2
    to_x, to_z, to_xz = call(
        functools.partial(relay_kernel, size_x, size_y, comps, count),
        [(edge + (2 if both else 1) * count, LANES), (2, count + size_y, LANES), (count + size_y, LANES)],
        y1, y2, to_x, to_z, leaving,
    )
    got_x = moved_along(to_x, "gx", 1)
    z1, z2 = swapped_z((to_z[0], to_z[1]))
    got_xz = moved_diagonally(to_xz, 1)
    got_mx = got_x if both else moved_along(leaving[1], "gx", -1)
    gas_next, arrivals = call(
        functools.partial(finish_kernel, count), [gas_field.shape, (6, 7, slots, LANES)],
        base, y1, y2, got_x, got_mx, z1, z2, got_xz, hbm_outs=(0, 1),
        scratch=(
            pltpu.VMEM(gas_field.shape, jnp.float32),
            pltpu.VMEM((6, 7, slots, LANES), jnp.float32),
            pltpu.SemaphoreType.DMA((comps + 1,)),
        ),
    )
    return gas_next, jnp.transpose(velocity_next, (1, 0, 2)), jnp.transpose(arrivals, (0, 2, 1, 3))


def solution(mesh):
    owner = ("gx", "gz", "gy")
    in_specs = (
        P(None, "gx", "gy", "gz"),
        P(owner, None, None),
        P(owner, None, None),
        P(owner, None),
        P(owner, None),
        P(owner),
        P(owner, None),
    )
    out_specs = (
        P(None, "gx", "gy", "gz"),
        P(owner, None, None),
        P(owner, None, None, None),
    )
    return jax.shard_map(
        per_device, mesh=mesh, in_specs=in_specs, out_specs=out_specs, check_vma=False
    )
```

```python
import functools

import jax
import jax.numpy as jnp
from jax import lax
from jax.experimental import pallas as pl
from jax.experimental.pallas import tpu as pltpu
from jax.sharding import PartitionSpec as P

BX = 4
BY = 4
BZ = 8

TIME_STEP = 0.25
VISCOSITY = 0.4

LANES = 128
PACK = 32
ROWS_Y = 24
REACH_X = BX + 1
REACH_Y = 8
SPREAD = REACH_X * REACH_Y
REACH_Z = 2 * BZ
UNROLL = 8
WIDE = 16

WEIGHT, ALONG_Y, IN_Y, ALONG_Z, IN_Z, RESPONSE, MOVING, OFFSET = 0, 5, 6, 7, 8, 9, 10, 13
TABLE_ROWS = 16
STATE = 8

VMEM = pl.BlockSpec(memory_space=pltpu.VMEM)
SMEM = pl.BlockSpec(memory_space=pltpu.SMEM)
HBM = pl.BlockSpec(memory_space=pltpu.HBM)


def moved_along(block, axis, distance):
    count = lax.axis_size(axis)
    return lax.ppermute(block, axis, [(i, (i + distance) % count) for i in range(count)])


def swapped_z(blocks):
    count = lax.axis_size("gz")
    first = [(i, i ^ 1) for i in range(count)]
    second = [(i, (((i + 1) ^ 1) - 1) % count) for i in range(count)]
    return lax.ppermute(blocks[0], "gz", first), lax.ppermute(blocks[1], "gz", second)


def swapped_y(blocks):
    nz, ny = lax.axis_size("gz"), lax.axis_size("gy")
    first = [(j, j ^ 1) for j in range(ny)]
    second = []
    for k in range(nz):
        second.append((k * ny, (k ^ 1) * ny))
        second.append((k * ny + ny - 1, (k ^ 1) * ny + ny - 1))
        second.extend((k * ny + j, k * ny + ((j + 1) ^ 1) - 1) for j in range(1, ny - 1))
    middle = lax.ppermute(blocks[1], ("gz", "gy"), second)
    return lax.ppermute(blocks[0], "gy", first), middle


def moved_diagonally(block, distance):
    nx, nz = lax.axis_size("gx"), lax.axis_size("gz")
    route = [(i * nz + k, (i + distance) % nx * nz + (k + distance) % nz) for i in range(nx) for k in range(nz)]
    return lax.ppermute(block, ("gx", "gz"), route)


def call(
    body, outs, *operands, smem=(), hbm=(), smem_outs=(), hbm_outs=(), scratch=(), aliases=None, cycles=0, limit=40
):
    return pl.pallas_call(
        body,
        out_shape=[o if isinstance(o, jax.ShapeDtypeStruct) else jax.ShapeDtypeStruct(o, jnp.float32) for o in outs],
        in_specs=[SMEM if i in smem else HBM if i in hbm else VMEM for i in range(len(operands))],
        out_specs=[SMEM if i in smem_outs else HBM if i in hbm_outs else VMEM for i in range(len(outs))],
        scratch_shapes=list(scratch),
        input_output_aliases=aliases or {},
        compiler_params=pltpu.CompilerParams(vmem_limit_bytes=limit * 1024 * 1024),
        cost_estimate=pl.CostEstimate(flops=cycles * 4096, bytes_accessed=cycles * 1024, transcendentals=0),
    )(*operands)


def lane_ids(rows):
    return lax.broadcasted_iota(jnp.int32, (rows, LANES), 1)


def row_ids(rows):
    return lax.broadcasted_iota(jnp.int32, (rows, LANES), 0)


def turned(value, shift):
    shift = shift % LANES
    return pltpu.roll(value, shift, 1) if shift else value


def odd(axis):
    return lax.axis_index(axis) % 2


def begin_kernel(
    gas_ref, velocity_in, fraction_in, response_in, cell_in, brick_in, crossing_in,
    grid_ref, face_ref, plane_ref, velocity_ref, fraction_ref, response_ref, cell_ref, brick_ref, crossing_ref, sems,
):
    comps, size_x, size_y, _ = gas_ref.shape
    pairs = [
        (gas_ref, grid_ref.at[:, 1 : size_x + 1, 0:size_y]),
        (velocity_in, velocity_ref), (fraction_in, fraction_ref), (response_in, response_ref),
        (cell_in, cell_ref), (brick_in, brick_ref), (crossing_in, crossing_ref),
    ]
    copies = [pltpu.make_async_copy(source, target, sems.at[i]) for i, (source, target) in enumerate(pairs)]
    for copy in copies:
        copy.start()
    zeros = jnp.zeros((ROWS_Y, LANES), jnp.float32)
    for c in range(comps):
        grid_ref[c, 0] = zeros
        grid_ref[c, size_x + 1] = zeros
        for x in range(size_x):
            grid_ref[c, x + 1, size_y:] = zeros[size_y:]
    copies[0].wait()
    lane = lane_ids(size_y)
    face = jnp.zeros((size_y, LANES), jnp.float32)
    for c in range(comps):
        plane_ref[c * size_y : (c + 1) * size_y] = grid_ref[c, 1, 0:size_y]
        for x in range(size_x):
            place = PACK * c + x
            face = jnp.where(lane == place, turned(grid_ref[c, x + 1, 0:size_y], place), face)
    face_ref[...] = face
    for copy in copies[1:]:
        copy.wait()


def parts_of(value):
    main = value.astype(jnp.bfloat16).astype(jnp.float32)
    return main, value - main


def lay_out(grid_ref, lines_ref, p, q, size_y, size_z):
    comps = grid_ref.shape[0]
    rows_z = size_z + 8
    count_y = size_y // BY
    for c in range(comps):
        planes = [grid_ref[c, p * BX + a + 1, q * BY : q * BY + REACH_Y] for a in range(REACH_X)]
        main, rest = parts_of(jnp.concatenate(planes, axis=0))
        stack = jnp.concatenate([main, rest, main, jnp.zeros((LANES - 3 * SPREAD, LANES), jnp.float32)], axis=0)
        at = ((p * count_y + q) * comps + c) * rows_z
        lines_ref[at : at + size_z] = jnp.transpose(stack)


def lay_out_top(turned_ref, lines_ref, q, comps, count_x, count_y, size_z):
    lane = lane_ids(count_x)
    rows_z = size_z + 8
    for c in range(comps):
        total = jnp.zeros((count_x, LANES), jnp.float32)
        for a in range(REACH_X):
            rows = turned_ref[pl.ds(PACK * c + a, count_x, stride=BX)]
            total = jnp.where(lane // REACH_Y == a, turned(rows, a * REACH_Y - q * BY), total)
        main, rest = parts_of(total)
        line = main + turned(rest, SPREAD) + turned(main, 2 * SPREAD)
        for p in range(count_x):
            at = ((p * count_y + q) * comps + c) * rows_z + size_z
            lines_ref[at : at + 1] = line[p : p + 1]


def prepare_kernel(
    grid_ref, velocity_ref, fraction_ref, response_ref, cell_ref, brick_ref,
    lines_ref, deposit_ref, table_ref, ready_ref, list_ref,
):
    comps, size_x, size_y, size_z = grid_ref.shape[0], grid_ref.shape[1] - 2, grid_ref.shape[2] - 8, grid_ref.shape[3]
    nblocks = velocity_ref.shape[1]
    count_x, count_y, count_z = size_x // BX, size_y // BY, size_z // BZ
    rows_z = size_z + 8


    def visit(k, counts):
        late = jnp.where(lax.rem(lax.div(brick_ref[k], count_z), count_y) == count_y - 1, 1, 0)
        list_ref[jnp.where(late == 1, nblocks + counts[1], counts[0])] = k
        return counts[0] + 1 - late, counts[1] + late

    early, late = lax.fori_loop(0, nblocks, visit, (jnp.int32(0), jnp.int32(0)), unroll=8)
    list_ref[2 * nblocks] = early
    list_ref[2 * nblocks + 1] = late
    ready_ref[...] = jnp.zeros_like(ready_ref)

    deposit_ref[...] = jnp.zeros_like(deposit_ref)
    for p in range(count_x):
        for q in range(count_y):
            for c in range(comps):
                at = ((p * count_y + q) * comps + c) * rows_z + size_z
                lines_ref[at : at + 8] = jnp.zeros((8, LANES), jnp.float32)
    for p in range(count_x - 1):
        for q in range(count_y - 1):
            lay_out(grid_ref, lines_ref, p, q, size_y, size_z)

    cells = cell_ref[...]
    cell_x, cell_y, cell_z = cells // (BY * BZ), cells // BZ % BY, cells % BZ
    along_x = fraction_ref[0]

    def put(row, value):
        table_ref[pl.ds(row, nblocks, stride=TABLE_ROWS)] = value

    for a in range(REACH_X):
        put(WEIGHT + a, jnp.where(cell_x == a, 1.0 - along_x, 0.0) + jnp.where(cell_x == a - 1, along_x, 0.0))
    put(ALONG_Y, fraction_ref[1])
    put(IN_Y, cell_y.astype(jnp.float32))
    put(ALONG_Z, fraction_ref[2])
    put(IN_Z, cell_z.astype(jnp.float32))
    put(RESPONSE, response_ref[...])
    for c in range(comps):
        put(MOVING + c, velocity_ref[c])
        put(OFFSET + c, fraction_ref[c])
    spare = table_ref.shape[0] - nblocks * TABLE_ROWS
    row = row_ids(spare)
    table_ref[nblocks * TABLE_ROWS :] = jnp.where(row % TABLE_ROWS == RESPONSE, 1.0, 0.0)


def y_lines_kernel(grid_ref, face_ref, from_x_ref, edge_ref, ready_ref, out_ref):
    comps, size_x = grid_ref.shape[0], grid_ref.shape[1] - 2
    size_y = face_ref.shape[0]
    for c in range(comps):
        out_ref[c * size_x : (c + 1) * size_x] = grid_ref[c, 1 : size_x + 1, 0]
        out_ref[comps * size_x + c : comps * size_x + c + 1] = from_x_ref[c * size_y : c * size_y + 1]
    line = jnp.where(lane_ids(8) % PACK == size_x, turned(edge_ref[0:8], size_x), face_ref[0:8])
    out_ref[comps * size_x + comps : comps * size_x + comps + 1] = line[0:1]


def halo_xz_kernel(grid_in_ref, lines_in_ref, face_ref, from_x_ref, edge_ref, grid_ref, lines_ref, top_ref, turned_ref):
    comps, size_x = grid_ref.shape[0], grid_ref.shape[1] - 2
    size_y, size_z = face_ref.shape[0], grid_ref.shape[3]
    count_x, count_y = size_x // BX, size_y // BY
    for c in range(comps):
        grid_ref[c, size_x + 1, 0:size_y] = from_x_ref[c * size_y : (c + 1) * size_y]
    for q in range(count_y - 1):
        lay_out(grid_ref, lines_ref, count_x - 1, q, size_y, size_z)
    top = jnp.where(lane_ids(size_y) % PACK == size_x, turned(edge_ref[...], size_x), face_ref[...])
    top_ref[0:size_y] = top
    top_ref[size_y:] = jnp.zeros((LANES - size_y, LANES), jnp.float32)
    turned_ref[...] = jnp.transpose(top_ref[...])
    for q in range(count_y - 1):
        lay_out_top(turned_ref, lines_ref, q, comps, count_x, count_y, size_z)


def halo_y_kernel(size_y, grid_in_ref, lines_in_ref, top_in_ref, first_ref, second_ref, grid_ref, lines_ref, turned_ref):
    comps, size_x, size_z = grid_ref.shape[0], grid_ref.shape[1] - 2, grid_ref.shape[3]
    count_x, count_y = size_x // BX, size_y // BY
    inside = lax.axis_index("gy") != lax.axis_size("gy") - 1
    kept = (row_ids(8) == 0) & inside
    even = jnp.full((1, LANES), odd("gy")) == 0

    def line_at(row):
        line = jnp.where(even, first_ref[row : row + 1], second_ref[row : row + 1])
        return jnp.where(kept, jnp.broadcast_to(line, (8, LANES)), 0.0)

    for c in range(comps):
        for x in range(size_x + 1):
            grid_ref[c, x + 1, size_y:] = line_at(c * size_x + x if x < size_x else comps * size_x + c)
    for p in range(count_x):
        lay_out(grid_ref, lines_ref, p, count_y - 1, size_y, size_z)
    corner = line_at(comps * size_x + comps)
    rest = jnp.zeros((LANES - size_y - 8, LANES), jnp.float32)
    turned_ref[...] = jnp.transpose(jnp.concatenate([top_in_ref[0:size_y], corner, rest], axis=0))
    lay_out_top(turned_ref, lines_ref, count_y - 1, comps, count_x, count_y, size_z)


def block_steps(dims, list_ref, brick_ref, end):
    comps, _, count_y, count_z, rows_z = dims
    nblocks = brick_ref.shape[0]
    sub = row_ids(8)
    row_y = row_ids(REACH_Y).astype(jnp.float32)
    row_z = row_ids(REACH_Z).astype(jnp.float32)
    lanes = lane_ids(REACH_Z)

    def hat(rows, inside, along):
        return jnp.where(rows == inside, 1.0 - along, 0.0) + jnp.where(rows == inside + 1.0, along, 0.0)

    def place_of(at):
        k = jnp.where(at < end, list_ref[jnp.minimum(at, 2 * nblocks + 1)], nblocks)
        brick = jnp.where(k < nblocks, brick_ref[jnp.minimum(k, nblocks - 1)], 0)
        brick_x = lax.div(brick, count_y * count_z)
        brick_y = lax.rem(lax.div(brick, count_z), count_y)
        return k, brick_x * count_y + brick_y, lax.rem(brick, count_z)

    def loaded(at, lines_ref, table_ref):
        k, pair, brick_z = place_of(at)
        first = pl.multiple_of(pair * comps * rows_z + brick_z * BZ, 8)
        window = jnp.concatenate([lines_ref[pl.ds(first + c * rows_z, REACH_Z)] for c in range(comps)], axis=0)
        table = table_ref[pl.ds(pl.multiple_of(k * TABLE_ROWS, TABLE_ROWS), TABLE_ROWS)]
        return k, window, [table[i : i + 1] for i in range(TABLE_ROWS)]

    def weighted(rows):
        weight_y = hat(row_y, rows[IN_Y], rows[ALONG_Y])
        weight_z = hat(row_z, rows[IN_Z], rows[ALONG_Z])
        weight = jnp.concatenate([rows[WEIGHT + a] * weight_y for a in range(REACH_X)], axis=0)
        return weight_z, *parts_of(weight)

    def stepped(seen, weight_z, rows):
        rate = 1.0 / rows[RESPONSE]
        state, moved, pushed = [], [], []
        for c in range(comps):
            gas_sample = jnp.sum(seen[c * REACH_Z : (c + 1) * REACH_Z] * weight_z, axis=0, keepdims=True)
            drag = (gas_sample - rows[MOVING + c]) * rate
            state.append(rows[MOVING + c] + TIME_STEP * drag)
            moved.append(rows[OFFSET + c] + TIME_STEP * state[c])
            pushed.append(drag * weight_z)
        tile = jnp.broadcast_to(rows[RESPONSE], (STATE, LANES))
        for i, value in enumerate(state + moved):
            tile = jnp.where(sub == i, value, tile)
        return tile, jnp.concatenate(parts_of(jnp.concatenate(pushed, axis=0)), axis=0)

    def gathered(one, two):
        tables, windows, weights = [], [], []
        for _, window, rows in (one, two):
            weight_z, main, rest = weighted(rows)
            weights.append((weight_z, main, rest))
            unused = jnp.zeros((LANES - 3 * SPREAD, LANES), jnp.float32)
            tables.append(jnp.concatenate([main, main, rest, unused], axis=0).astype(jnp.bfloat16))
            windows.append(window)
        seen = lax.dot_general(
            jnp.concatenate(windows, axis=0).astype(jnp.bfloat16), jnp.concatenate(tables, axis=1),
            (((1,), (0,)), ((), ())), preferred_element_type=jnp.float32,
        )
        height = comps * REACH_Z
        tiles, fresh = [], []
        for i, (_, _, rows) in enumerate((one, two)):
            weight_z, main, rest = weights[i]
            mine = seen[i * height : (i + 1) * height, i * LANES : (i + 1) * LANES]
            tile, push = stepped(mine, weight_z, rows)
            tiles.append(tile)
            unused = jnp.zeros((LANES - comps * SPREAD, LANES), jnp.float32)
            spread = jnp.concatenate([main] * comps + [unused] + [rest] * comps + [unused], axis=0)
            fresh.append((push.astype(jnp.bfloat16), spread.astype(jnp.bfloat16)))
        return tiles, fresh

    def shared(push, spread):
        shares = lax.dot_general(push, spread, (((1,), (1,)), ((), ())), preferred_element_type=jnp.float32)
        height = comps * REACH_Z
        total = shares[:height, :LANES] + shares[:height, LANES:] + shares[height:, :LANES]
        result = jnp.zeros((REACH_Z, LANES), jnp.float32)
        for c in range(comps):
            inside = (lanes >= c * SPREAD) & (lanes < (c + 1) * SPREAD)
            result = jnp.where(inside, total[c * REACH_Z : (c + 1) * REACH_Z], result)
        return result

    def add(deposit_ref, at, shares):
        spots = []
        for u in range(len(shares)):
            _, pair, brick_z = place_of(at + u)
            spots.append(pl.ds(pl.multiple_of(pair * rows_z + brick_z * BZ, 8), REACH_Z))
        for spot, share in zip(spots, shares):
            deposit_ref[spot] = deposit_ref[spot] + share

    def group_of(taken):
        tiles, fresh = [], []
        for u in range(0, len(taken), 2):
            both, kept = gathered(taken[u], taken[u + 1])
            tiles.extend(both)
            fresh.extend(kept)
        return tiles, fresh

    def keep(state_ref, taken, tiles):
        for (k, _, _), tile in zip(taken, tiles):
            state_ref[pl.ds(pl.multiple_of(STATE * k, STATE), STATE)] = tile

    def deposits_of(kept):
        return [shared(push, spread) for push, spread in kept]

    return loaded, group_of, keep, deposits_of, add


def groups_in(list_ref, late, many=UNROLL):
    room = (list_ref.shape[0] - 2) // 2
    count = list_ref[2 * room + late]
    return late * room, (count + many - 1) // many, late * room + count


def leave(crossing_ref, state_ref, leaving_ref, faces):
    slots = crossing_ref.shape[1]
    rows = leaving_ref.shape[0] // (len(faces) * slots)
    for i, face in enumerate(faces):
        tiles = []
        for slot in range(slots):
            block = crossing_ref[face, slot]
            spot = pl.ds(pl.multiple_of(jnp.maximum(block, 0) * STATE, STATE), STATE)
            live = jnp.full((STATE, LANES), block, jnp.int32) >= 0
            tiles.append(jnp.where(live, state_ref[spot], 0.0))
        for slot, tile in enumerate(tiles):
            leaving_ref[pl.ds(i * rows * slots + slot, rows, stride=slots)] = tile[:rows]


def fetched(sems, *pairs):
    copies = [pltpu.make_async_copy(source, target, sems.at[i]) for i, (source, target) in enumerate(pairs)]
    for copy in copies:
        copy.start()
    return copies


def gather_kernel(
    dims, list_in, brick_in, table_ref, grid_in_ref, lines_in_ref, face_ref, from_x_ref, edge_ref,
    state_ref, push_ref, spread_ref, grid_ref, lines_ref, top_ref, list_ref, brick_ref, turned_ref, sems,
):
    copies = fetched(sems, (list_in, list_ref), (brick_in, brick_ref))
    halo_xz_kernel(grid_in_ref, lines_in_ref, face_ref, from_x_ref, edge_ref, grid_ref, lines_ref, top_ref, turned_ref)
    for copy in copies:
        copy.wait()
    base, groups, end = groups_in(list_ref, 0)
    loaded, group_of, keep, _, _ = block_steps(dims, list_ref, brick_ref, end)

    @pl.loop(0, groups)
    def _(group):
        taken = [loaded(base + group * UNROLL + u, lines_ref, table_ref) for u in range(UNROLL)]
        tiles, fresh = group_of(taken)
        keep(state_ref, taken, tiles)
        for i, (push, spread) in enumerate(fresh):
            push_ref[group * UNROLL + i] = push
            spread_ref[group * UNROLL + i] = spread

    for i in range(UNROLL):
        push_ref[groups * UNROLL + i] = jnp.zeros(push_ref.shape[1:], push_ref.dtype)
        spread_ref[groups * UNROLL + i] = jnp.zeros(spread_ref.shape[1:], spread_ref.dtype)


def deposit_kernel(
    dims, list_ref, brick_ref, crossing_ref, push_ref, spread_ref, state_ref, deposit_in_ref, deposit_ref, leaving_ref
):
    base, groups, end = groups_in(list_ref, 0, WIDE)
    _, _, _, deposits_of, add = block_steps(dims, list_ref, brick_ref, end)
    leave(crossing_ref, state_ref, leaving_ref, (0, 1, 4, 5))

    @pl.loop(0, groups)
    def _(group):
        mine = [group * WIDE + i for i in range(WIDE)]
        add(deposit_ref, base + group * WIDE, deposits_of([(push_ref[i], spread_ref[i]) for i in mine]))


def late_kernel(
    dims, list_in, brick_in, crossing_in, table_ref, grid_in_ref, lines_in_ref, top_in_ref, first_ref, second_ref,
    state_in_ref, deposit_in_ref,
    grid_ref, lines_ref, state_ref, deposit_ref, leaving_ref,
    push_ref, spread_ref, list_ref, brick_ref, crossing_ref, turned_ref, sems,
):
    copies = fetched(sems, (list_in, list_ref), (brick_in, brick_ref), (crossing_in, crossing_ref))
    halo_y_kernel(
        dims[2] * BY, grid_in_ref, lines_in_ref, top_in_ref, first_ref, second_ref, grid_ref, lines_ref, turned_ref
    )
    for copy in copies:
        copy.wait()
    base, groups, end = groups_in(list_ref, 1)
    loaded, group_of, keep, deposits_of, add = block_steps(dims, list_ref, brick_ref, end)
    push_ref[...] = jnp.zeros_like(push_ref)
    spread_ref[...] = jnp.zeros_like(spread_ref)

    @pl.loop(0, groups + 1)
    def _(group):
        now = base + jnp.maximum(jnp.minimum(group, groups - 1), 0) * UNROLL
        before = base + jnp.maximum(group - 1, 0) * UNROLL
        taken = [loaded(now + u, lines_ref, table_ref) for u in range(UNROLL)]
        shares = deposits_of([(push_ref[i], spread_ref[i]) for i in range(UNROLL)])
        tiles, fresh = group_of(taken)
        add(deposit_ref, before, shares)
        keep(state_ref, taken, tiles)
        for i, (push, spread) in enumerate(fresh):
            push_ref[i] = push
            spread_ref[i] = spread

    leave(crossing_ref, state_ref, leaving_ref, (2, 3))


def top_rows(deposit_ref, q, count_x, count_y, rows_z, size_z):
    total = None
    for p in range(count_x):
        at = (p * count_y + q) * rows_z + size_z
        value = pltpu.roll(deposit_ref[at : at + 8], p, 0) if p else deposit_ref[at : at + 8]
        total = value if total is None else total + value
    return total


def send_y_kernel(push, diffuse, leaving_ref, grid_ref, deposit_ref, y1_ref, y2_ref, tiles_ref, lines_ref):
    comps, size_x, size_y, size_z = grid_ref.shape[0], grid_ref.shape[1] - 2, grid_ref.shape[2] - 8, grid_ref.shape[3]
    count_x, count_y = size_x // BX, size_y // BY
    rows_z = size_z + 8
    rows = leaving_ref.shape[1]
    height = comps * SPREAD
    for p in range(count_x):
        at = (p * count_y + count_y - 1) * rows_z
        tiles_ref[p * height : (p + 1) * height] = jnp.transpose(deposit_ref[at : at + size_z])[:height]
    first = jnp.full((rows, LANES), odd("gy")) == 0
    y1_ref[0:rows] = jnp.where(first, leaving_ref[0], leaving_ref[1])
    y2_ref[0:rows] = jnp.where(first, leaving_ref[1], leaving_ref[0])
    lines_ref[...] = jnp.zeros_like(lines_ref)
    for c in range(comps):
        for p in range(count_x):
            spot = slice(c * ROWS_Y + p * BX, c * ROWS_Y + p * BX + REACH_X)
            line = tiles_ref[pl.ds(p * height + c * SPREAD + BY, REACH_X, stride=REACH_Y)]
            lines_ref[spot] = lines_ref[spot] + line
    wrapped = top_rows(deposit_ref, count_y - 1, count_x, count_y, rows_z, size_z)
    lane = lane_ids(8)
    packed = jnp.zeros((8, LANES), jnp.float32)
    for c in range(comps):
        spot = slice(c * ROWS_Y, (c + 1) * ROWS_Y)
        beside = jnp.concatenate([grid_ref[c, 1 : size_x + 1, size_y - 1], jnp.zeros((8, LANES), jnp.float32)], axis=0)
        line = push * lines_ref[spot] + diffuse * beside
        at = rows + c * (size_x + 1)
        y1_ref[at : at + size_x + 1] = line[: size_x + 1]
        y2_ref[at : at + size_x + 1] = line[: size_x + 1]
        for a in range(REACH_X):
            place = PACK * c + a
            value = turned(wrapped, place - c * SPREAD - a * REACH_Y - BY)
            packed = packed + jnp.where(lane == place, value, 0.0)
    corner = packed[0:1]
    for p in range(1, count_x):
        corner = corner + turned(packed[p : p + 1], p * BX)
    at = rows + comps * (size_x + 1)
    y1_ref[at : at + 1] = push * corner
    y2_ref[at : at + 1] = push * corner


def merge_kernel(deposit_ref, top_tiles_ref, plane_ref, face_ref, tiles_ref, turned_ref):
    comps, planes = plane_ref.shape[:2]
    count_x, size_z = (planes - 1) // BX, plane_ref.shape[3]
    rows_z = size_z + 8
    count_y = deposit_ref.shape[0] // (rows_z * count_x)
    height = comps * SPREAD
    for p in range(count_x):
        for q in range(count_y - 1):
            at = p * count_y + q
            value = jnp.transpose(deposit_ref[at * rows_z : at * rows_z + size_z])
            tiles_ref[at * height : (at + 1) * height] = value[:height]
    top = row_ids(REACH_Y) >= BY
    for c in range(comps):
        for x in range(planes):
            bricks = [(x // BX, x % BX)] if x < planes - 1 else []
            if x and x % BX == 0:
                bricks.append((x // BX - 1, BX))

            def tile(q):
                total = None
                for p, a in bricks:
                    at = c * SPREAD + a * REACH_Y
                    if q < count_y - 1:
                        value = tiles_ref[(p * count_y + q) * height + at : (p * count_y + q) * height + at + REACH_Y]
                    else:
                        value = top_tiles_ref[p * height + at : p * height + at + REACH_Y]
                    total = value if total is None else total + value
                return total

            carried = None
            for q in range(0, count_y, 2):
                here = tile(q)
                if carried is not None:
                    here = here + carried
                between = pltpu.roll(tile(q + 1), BY, 0)
                here = here + jnp.where(top, between, 0.0)
                carried = jnp.where(top, 0.0, between)
                plane_ref[c, x, q * BY : q * BY + REACH_Y] = here
            plane_ref[c, x, count_y * BY :] = carried

    lane = lane_ids(count_x)
    turned_ref[...] = jnp.zeros_like(turned_ref)
    for q in range(count_y):
        wrapped = top_rows(deposit_ref, q, count_x, count_y, rows_z, size_z)[:count_x]
        within = (lane >= q * BY) & (lane <= (q + 1) * BY)
        for c in range(comps):
            for a in range(REACH_X):
                value = turned(wrapped, q * BY - c * SPREAD - a * REACH_Y)
                spot = pl.ds(PACK * c + a, count_x, stride=BX)
                turned_ref[spot] = turned_ref[spot] + jnp.where(within, value, 0.0)
    face_ref[...] = jnp.transpose(turned_ref[...])[: face_ref.shape[0]]


def send_xz_kernel(push, diffuse, grid_ref, deposit_ref, face_ref, x_ref, z_ref):
    comps, size_x = grid_ref.shape[0], grid_ref.shape[1] - 2
    size_y = z_ref.shape[0]
    lane = lane_ids(size_y)
    packed = push * face_ref[0:size_y]
    for c in range(comps):
        for x in range(size_x):
            place = PACK * c + x
            packed = packed + jnp.where(lane == place, diffuse * turned(grid_ref[c, x + 1, 0:size_y], place + 1), 0.0)
        total = push * deposit_ref[c, size_x, 0:size_y]
        x_ref[c * size_y : (c + 1) * size_y] = diffuse * grid_ref[c, size_x, 0:size_y] + total
    z_ref[...] = packed


def base_kernel(push, diffuse, count, grid_ref, deposit_ref, top_ref, y1_ref, y2_ref, state_ref, base_ref, velocity_ref):
    comps, size_x, size_y, size_z = base_ref.shape
    lane, sub = lane_ids(size_y), row_ids(size_y)
    top = top_ref[0:size_y]
    for c in range(comps):
        at = count + c * (size_x + 1)
        lines = below(y1_ref, y2_ref, slice(at, at + size_x))
        for x in range(size_x):
            here = grid_ref[c, x + 1, 0:size_y]
            before = jnp.where(sub == 0, 0.0, pltpu.roll(here, 1, 0))
            laplace = grid_ref[c, x, 0:size_y] + grid_ref[c, x + 2, 0:size_y]
            laplace = laplace + grid_ref[c, x + 1, 1 : size_y + 1] + before
            ahead = jnp.where(lane == size_z - 1, turned(top, size_z - 1 - (PACK * c + x)), turned(here, -1))
            laplace = laplace + ahead + jnp.where(lane == 0, 0.0, turned(here, 1)) - 6.0 * here
            total = here + diffuse * laplace + push * deposit_ref[c, x, 0:size_y]
            line = jnp.broadcast_to(lines[x : x + 1], (size_y, LANES))
            base_ref[c, x] = total + jnp.where(sub == 0, line, 0.0)
        velocity_ref[c] = state_ref[pl.ds(c, velocity_ref.shape[1], stride=STATE)]


def below(first_ref, second_ref, rows):
    got = jnp.where(jnp.full((1, LANES), odd("gy")) == 1, first_ref[rows], second_ref[rows])
    return jnp.where(jnp.full((1, LANES), lax.axis_index("gy")) != 0, got, 0.0)


def relay_kernel(size_x, size_y, comps, count, first_ref, second_ref, x_in_ref, z_in_ref, leaving_ref, x_ref, z1_ref, z2_ref, edge_ref):
    edge = comps * size_y
    x_ref[0:edge] = x_in_ref[...]
    for c in range(comps):
        at = count + c * (size_x + 1) + size_x
        spot = slice(c * size_y, c * size_y + 1)
        x_ref[spot] = x_in_ref[spot] + below(first_ref, second_ref, slice(at, at + 1))
    x_ref[edge : edge + count] = leaving_ref[0]
    if x_ref.shape[0] > edge + count:
        x_ref[edge + count : edge + 2 * count] = leaving_ref[1]
    at = count + comps * (size_x + 1)
    edge_ref[size_y:] = jnp.zeros((edge_ref.shape[0] - size_y, LANES), jnp.float32)
    edge_ref[0:size_y] = z_in_ref[...]
    edge_ref[0:1] = z_in_ref[0:1] + below(first_ref, second_ref, slice(at, at + 1))
    first = jnp.full((1, LANES), odd("gz")) == 0
    plus = jnp.concatenate([leaving_ref[2], edge_ref[0:size_y]], axis=0)
    minus = jnp.concatenate([leaving_ref[3], jnp.zeros((size_y, LANES), jnp.float32)], axis=0)
    z1_ref[...] = jnp.where(first, plus, minus)
    z2_ref[0 : count + size_y] = jnp.where(first, minus, plus)
    z2_ref[count + size_y :] = jnp.zeros((z2_ref.shape[0] - count - size_y, LANES), jnp.float32)


def finish_kernel(
    count, base_ref, y1_ref, y2_ref, x_ref, minus_x_ref, z1_ref, z2_ref, edge_ref, gas_out, arrivals_out,
    gas_ref, arrivals_ref, sems,
):
    comps, size_x, size_y, _ = base_ref.shape
    first_lane = lane_ids(size_y) == 0
    odd_y, odd_z = jnp.full((1, LANES), odd("gy")) == 1, jnp.full((1, LANES), odd("gz")) == 1
    place = jnp.full((1, LANES), lax.axis_index("gy"))
    lower, upper = place != 0, place != lax.axis_size("gy") - 1
    rows = slice(count, count + size_y)
    slots = arrivals_ref.shape[2]
    for i in range(arrivals_ref.shape[1]):

        def rows_of(ref, at=0):
            return ref[at + i * slots : at + (i + 1) * slots]

        arrivals_ref[0, i] = rows_of(x_ref, comps * size_y)
        arrivals_ref[1, i] = rows_of(minus_x_ref, minus_x_ref.shape[0] - count)
        y1, y2 = rows_of(y1_ref), rows_of(y2_ref)
        arrivals_ref[2, i] = jnp.where(lower, jnp.where(odd_y, y1, y2), 0.0)
        arrivals_ref[3, i] = jnp.where(upper, jnp.where(odd_y, y2, y1), 0.0)
        z1, z2 = rows_of(z1_ref), rows_of(z2_ref)
        arrivals_ref[4, i] = jnp.where(odd_z, z1, z2)
        arrivals_ref[5, i] = jnp.where(odd_z, z2, z1)
    copies = [pltpu.make_async_copy(arrivals_ref, arrivals_out, sems.at[comps])]
    copies[0].start()
    face = jnp.where(odd_z, z1_ref[rows], z2_ref[rows])
    corner = edge_ref[0:size_y]
    for c in range(comps):
        for x in range(size_x):
            total = base_ref[c, x]
            far = turned(face, -(PACK * c + x))
            if x == 0:
                total = total + x_ref[c * size_y : (c + 1) * size_y]
                far = far + turned(corner, -(PACK * c + size_x))
            gas_ref[c, x] = total + jnp.where(first_lane, far, 0.0)
        copies.append(pltpu.make_async_copy(gas_ref.at[c], gas_out.at[c], sems.at[c]))
        copies[-1].start()
    for copy in copies:
        copy.wait()


def per_device(gas_field, velocity, fraction, response, cell_index, brick_index, crossing):
    comps, size_x, size_y, size_z = gas_field.shape
    nblocks = velocity.shape[0]
    loading = 0.5 * size_x * size_y * size_z / (nblocks * 128)
    push, diffuse = -TIME_STEP * loading, TIME_STEP * VISCOSITY
    velocity = jnp.transpose(velocity, (1, 0, 2))
    fraction = jnp.transpose(fraction, (1, 0, 2))
    spare = nblocks + 8
    rows_z = size_z + 8
    grid_shape = (comps, size_x + 2, ROWS_Y, LANES)
    lines_shape = ((size_x // BX) * (size_y // BY) * comps * rows_z, LANES)
    deposit_shape = ((size_x // BX) * (size_y // BY) * rows_z, LANES)

    inputs = (gas_field, velocity, fraction, response, cell_index, brick_index, crossing)
    inputs = [pltpu.with_memory_space_constraint(array, pltpu.HBM) for array in inputs]
    grid, face, plane, velocity, fraction, response, cell_index, brick_index, crossing = call(
        begin_kernel,
        [grid_shape, (size_y, LANES), (comps * size_y, LANES)]
        + [jax.ShapeDtypeStruct(array.shape, array.dtype) for array in inputs[1:]],
        *inputs, hbm=range(7), scratch=(pltpu.SemaphoreType.DMA((7,)),),
    )
    from_z = moved_along(face, "gz", -1)
    from_x = moved_along(plane, "gx", -1)
    from_xz = moved_diagonally(face, -1)
    lines, deposit, table, ready, blocks = call(
        prepare_kernel,
        [
            lines_shape,
            deposit_shape,
            (TABLE_ROWS * spare, LANES),
            (8, LANES),
            jax.ShapeDtypeStruct((2 * nblocks + 2,), jnp.int32),
        ],
        grid, velocity, fraction, response, cell_index, brick_index,
        smem=(5,), smem_outs=(4,), cycles=3000,
    )
    line_rows = -(-(comps * size_x + comps + 1) // 8) * 8
    (y_lines,) = call(y_lines_kernel, [(line_rows, LANES)], grid, from_z, from_x, from_xz, ready)
    y1, y2 = swapped_y((y_lines, y_lines))
    square = pltpu.VMEM((LANES, LANES), jnp.float32)
    scalars = (pltpu.SMEM(blocks.shape, jnp.int32), pltpu.SMEM(brick_index.shape, jnp.int32))
    dims = (comps, size_x // BX, size_y // BY, size_z // BZ, rows_z)
    slots = crossing.shape[1]
    count = 7 * slots

    def parts(many):
        return [(many, 2 * comps * REACH_Z, LANES), (many, 2 * LANES, LANES)]

    state, push_parts, spread_parts, grid, lines, top = call(
        functools.partial(gather_kernel, dims),
        [(STATE * spare, LANES)]
        + [jax.ShapeDtypeStruct(shape, jnp.bfloat16) for shape in parts(nblocks + 2 * UNROLL)]
        + [grid_shape, lines_shape, (LANES, LANES)],
        blocks, brick_index, table, grid, lines, from_z, from_x, from_xz,
        aliases={3: 3, 4: 4}, cycles=4000, scratch=(*scalars, square, pltpu.SemaphoreType.DMA((2,))),
    )
    grid, lines, state, deposit, leaving = call(
        functools.partial(late_kernel, dims),
        [grid_shape, lines_shape, (STATE * spare, LANES), deposit_shape, (2 * count, LANES)],
        blocks, brick_index, crossing, table, grid, lines, top, y1, y2, state, deposit,
        aliases={4: 0, 5: 1, 9: 2, 10: 3}, cycles=2000,
        scratch=[
            *(pltpu.VMEM(shape, jnp.bfloat16) for shape in parts(UNROLL)),
            *scalars,
            pltpu.SMEM(crossing.shape, jnp.int32),
            square,
            pltpu.SemaphoreType.DMA((3,)),
        ],
    )
    leaving = leaving.reshape(2, count, LANES)
    height = comps * SPREAD
    to_y1, to_y2, top_tiles = call(
        functools.partial(send_y_kernel, push, diffuse),
        [(count + line_rows, LANES), (count + line_rows, LANES), ((size_x // BX) * height, LANES)],
        leaving, grid, deposit, cycles=300, scratch=(pltpu.VMEM((comps * ROWS_Y, LANES), jnp.float32),),
    )
    y1, y2 = swapped_y((to_y1, to_y2))
    deposit, leaving = call(
        functools.partial(deposit_kernel, dims), [deposit_shape, (4 * count, LANES)],
        blocks, brick_index, crossing, push_parts, spread_parts, state, deposit,
        smem=(0, 1, 2), aliases={6: 0}, cycles=4000,
    )
    leaving = leaving.reshape(4, count, LANES)
    deposit, over = call(
        merge_kernel, [(comps, size_x + 1, ROWS_Y, LANES), (ROWS_Y, LANES)], deposit, top_tiles,
        cycles=1000, scratch=(pltpu.VMEM(((size_x // BX) * (size_y // BY) * height, LANES), jnp.float32), square),
    )
    to_x, to_z = call(
        functools.partial(send_xz_kernel, push, diffuse), [(comps * size_y, LANES), (size_y, LANES)],
        grid, deposit, over, cycles=500,
    )
    base, velocity_next = call(
        functools.partial(base_kernel, push, diffuse, count), [gas_field.shape, (comps, nblocks, LANES)],
        grid, deposit, top, y1, y2, state, cycles=1000,
    )
    edge = comps * size_y
    both = lax.axis_size("gx") == 2
    to_x, to_z1, to_z2, to_xz = call(
        functools.partial(relay_kernel, size_x, size_y, comps, count),
        [(edge + (2 if both else 1) * count, LANES), *[(count + size_y + 8 * more, LANES) for more in range(3)]],
        y1, y2, to_x, to_z, leaving,
    )
    got_x = moved_along(to_x, "gx", 1)
    z1, z2 = swapped_z((to_z1, to_z2))
    got_xz = moved_diagonally(to_xz, 1)
    got_mx = got_x if both else moved_along(leaving[1], "gx", -1)
    gas_next, arrivals = call(
        functools.partial(finish_kernel, count), [gas_field.shape, (6, 7, slots, LANES)],
        base, y1, y2, got_x, got_mx, z1, z2, got_xz, hbm_outs=(0, 1),
        scratch=(
            pltpu.VMEM(gas_field.shape, jnp.float32),
            pltpu.VMEM((6, 7, slots, LANES), jnp.float32),
            pltpu.SemaphoreType.DMA((comps + 1,)),
        ),
    )
    return gas_next, jnp.transpose(velocity_next, (1, 0, 2)), jnp.transpose(arrivals, (0, 2, 1, 3))


def solution(mesh):
    owner = ("gx", "gz", "gy")
    in_specs = (
        P(None, "gx", "gy", "gz"),
        P(owner, None, None),
        P(owner, None, None),
        P(owner, None),
        P(owner, None),
        P(owner),
        P(owner, None),
    )
    out_specs = (
        P(None, "gx", "gy", "gz"),
        P(owner, None, None),
        P(owner, None, None, None),
    )
    return jax.shard_map(
        per_device, mesh=mesh, in_specs=in_specs, out_specs=out_specs, check_vma=False
    )
```

```python
import functools

import jax
import jax.numpy as jnp
from jax import lax
from jax.experimental import pallas as pl
from jax.experimental.pallas import tpu as pltpu
from jax.sharding import PartitionSpec as P

BX = 4
BY = 4
BZ = 8

TIME_STEP = 0.25
VISCOSITY = 0.4

LANES = 128
PACK = 32
ROWS_Y = 24
REACH_X = BX + 1
REACH_Y = 8
SPREAD = REACH_X * REACH_Y
REACH_Z = 2 * BZ
UNROLL = 8
WIDE = 16

WEIGHT, ALONG_Y, IN_Y, ALONG_Z, IN_Z, RESPONSE, MOVING, OFFSET = 0, 5, 6, 7, 8, 9, 10, 13
TABLE_ROWS = 16
STATE = 8

VMEM = pl.BlockSpec(memory_space=pltpu.VMEM)
SMEM = pl.BlockSpec(memory_space=pltpu.SMEM)
HBM = pl.BlockSpec(memory_space=pltpu.HBM)


def moved_along(block, axis, distance):
    count = lax.axis_size(axis)
    return lax.ppermute(block, axis, [(i, (i + distance) % count) for i in range(count)])


def swapped_z(blocks):
    count = lax.axis_size("gz")
    first = [(i, i ^ 1) for i in range(count)]
    second = [(i, (((i + 1) ^ 1) - 1) % count) for i in range(count)]
    return lax.ppermute(blocks[0], "gz", first), lax.ppermute(blocks[1], "gz", second)


def swapped_y(blocks):
    nz, ny = lax.axis_size("gz"), lax.axis_size("gy")
    first = [(j, j ^ 1) for j in range(ny)]
    second = []
    for k in range(nz):
        second.append((k * ny, (k ^ 1) * ny))
        second.append((k * ny + ny - 1, (k ^ 1) * ny + ny - 1))
        second.extend((k * ny + j, k * ny + ((j + 1) ^ 1) - 1) for j in range(1, ny - 1))
    middle = lax.ppermute(blocks[1], ("gz", "gy"), second)
    return lax.ppermute(blocks[0], "gy", first), middle


def moved_diagonally(block, distance):
    nx, nz = lax.axis_size("gx"), lax.axis_size("gz")
    route = [(i * nz + k, (i + distance) % nx * nz + (k + distance) % nz) for i in range(nx) for k in range(nz)]
    return lax.ppermute(block, ("gx", "gz"), route)


def call(
    body, outs, *operands, smem=(), hbm=(), smem_outs=(), hbm_outs=(), scratch=(), aliases=None, cycles=0, limit=40
):
    return pl.pallas_call(
        body,
        out_shape=[o if isinstance(o, jax.ShapeDtypeStruct) else jax.ShapeDtypeStruct(o, jnp.float32) for o in outs],
        in_specs=[SMEM if i in smem else HBM if i in hbm else VMEM for i in range(len(operands))],
        out_specs=[SMEM if i in smem_outs else HBM if i in hbm_outs else VMEM for i in range(len(outs))],
        scratch_shapes=list(scratch),
        input_output_aliases=aliases or {},
        compiler_params=pltpu.CompilerParams(vmem_limit_bytes=limit * 1024 * 1024),
        cost_estimate=pl.CostEstimate(flops=cycles * 4096, bytes_accessed=cycles * 1024, transcendentals=0),
    )(*operands)


def lane_ids(rows):
    return lax.broadcasted_iota(jnp.int32, (rows, LANES), 1)


def row_ids(rows):
    return lax.broadcasted_iota(jnp.int32, (rows, LANES), 0)


def turned(value, shift):
    shift = shift % LANES
    return pltpu.roll(value, shift, 1) if shift else value


def odd(axis):
    return lax.axis_index(axis) % 2


def begin_kernel(
    gas_ref, velocity_in, fraction_in, response_in, cell_in, brick_in, crossing_in,
    grid_ref, face_ref, plane_ref, velocity_ref, fraction_ref, response_ref, cell_ref, brick_ref, crossing_ref, sems,
):
    comps, size_x, size_y, _ = gas_ref.shape
    pairs = [
        (gas_ref, grid_ref.at[:, 1 : size_x + 1, 0:size_y]),
        (velocity_in, velocity_ref), (fraction_in, fraction_ref), (response_in, response_ref),
        (cell_in, cell_ref), (brick_in, brick_ref), (crossing_in, crossing_ref),
    ]
    copies = [pltpu.make_async_copy(source, target, sems.at[i]) for i, (source, target) in enumerate(pairs)]
    for copy in copies:
        copy.start()
    zeros = jnp.zeros((ROWS_Y, LANES), jnp.float32)
    for c in range(comps):
        grid_ref[c, 0] = zeros
        grid_ref[c, size_x + 1] = zeros
        for x in range(size_x):
            grid_ref[c, x + 1, size_y:] = zeros[size_y:]
    copies[0].wait()
    lane = lane_ids(size_y)
    face = jnp.zeros((size_y, LANES), jnp.float32)
    for c in range(comps):
        plane_ref[c * size_y : (c + 1) * size_y] = grid_ref[c, 1, 0:size_y]
        for x in range(size_x):
            place = PACK * c + x
            face = jnp.where(lane == place, turned(grid_ref[c, x + 1, 0:size_y], place), face)
    face_ref[...] = face
    for copy in copies[1:]:
        copy.wait()


def parts_of(value):
    main = value.astype(jnp.bfloat16).astype(jnp.float32)
    return main, value - main


def lay_out(grid_ref, lines_ref, p, q, size_y, size_z):
    comps = grid_ref.shape[0]
    rows_z = size_z + 8
    count_y = size_y // BY
    for c in range(comps):
        planes = [grid_ref[c, p * BX + a + 1, q * BY : q * BY + REACH_Y] for a in range(REACH_X)]
        main, rest = parts_of(jnp.concatenate(planes, axis=0))
        stack = jnp.concatenate([main, rest, main, jnp.zeros((LANES - 3 * SPREAD, LANES), jnp.float32)], axis=0)
        at = ((p * count_y + q) * comps + c) * rows_z
        lines_ref[at : at + size_z] = jnp.transpose(stack)


def lay_out_top(turned_ref, lines_ref, q, comps, count_x, count_y, size_z):
    lane = lane_ids(count_x)
    rows_z = size_z + 8
    for c in range(comps):
        total = jnp.zeros((count_x, LANES), jnp.float32)
        for a in range(REACH_X):
            rows = turned_ref[pl.ds(PACK * c + a, count_x, stride=BX)]
            total = jnp.where(lane // REACH_Y == a, turned(rows, a * REACH_Y - q * BY), total)
        main, rest = parts_of(total)
        line = main + turned(rest, SPREAD) + turned(main, 2 * SPREAD)
        for p in range(count_x):
            at = ((p * count_y + q) * comps + c) * rows_z + size_z
            lines_ref[at : at + 1] = line[p : p + 1]


def prepare_kernel(
    grid_ref, velocity_ref, fraction_ref, response_ref, cell_ref, brick_ref,
    lines_ref, deposit_ref, table_ref, ready_ref, list_ref,
):
    comps, size_x, size_y, size_z = grid_ref.shape[0], grid_ref.shape[1] - 2, grid_ref.shape[2] - 8, grid_ref.shape[3]
    nblocks = velocity_ref.shape[1]
    count_x, count_y, count_z = size_x // BX, size_y // BY, size_z // BZ
    rows_z = size_z + 8


    def visit(k, counts):
        late = jnp.where(lax.rem(lax.div(brick_ref[k], count_z), count_y) == count_y - 1, 1, 0)
        list_ref[jnp.where(late == 1, nblocks + counts[1], counts[0])] = k
        return counts[0] + 1 - late, counts[1] + late

    early, late = lax.fori_loop(0, nblocks, visit, (jnp.int32(0), jnp.int32(0)), unroll=8)
    list_ref[2 * nblocks] = early
    list_ref[2 * nblocks + 1] = late
    ready_ref[...] = jnp.zeros_like(ready_ref)

    deposit_ref[...] = jnp.zeros_like(deposit_ref)
    for p in range(count_x):
        for q in range(count_y):
            for c in range(comps):
                at = ((p * count_y + q) * comps + c) * rows_z + size_z
                lines_ref[at : at + 8] = jnp.zeros((8, LANES), jnp.float32)
    for p in range(count_x - 1):
        for q in range(count_y - 1):
            lay_out(grid_ref, lines_ref, p, q, size_y, size_z)

    cells = cell_ref[...]
    cell_x, cell_y, cell_z = cells // (BY * BZ), cells // BZ % BY, cells % BZ
    along_x = fraction_ref[0]

    def put(row, value):
        table_ref[pl.ds(row, nblocks, stride=TABLE_ROWS)] = value

    for a in range(REACH_X):
        put(WEIGHT + a, jnp.where(cell_x == a, 1.0 - along_x, 0.0) + jnp.where(cell_x == a - 1, along_x, 0.0))
    put(ALONG_Y, fraction_ref[1])
    put(IN_Y, cell_y.astype(jnp.float32))
    put(ALONG_Z, fraction_ref[2])
    put(IN_Z, cell_z.astype(jnp.float32))
    put(RESPONSE, response_ref[...])
    for c in range(comps):
        put(MOVING + c, velocity_ref[c])
        put(OFFSET + c, fraction_ref[c])
    spare = table_ref.shape[0] - nblocks * TABLE_ROWS
    row = row_ids(spare)
    table_ref[nblocks * TABLE_ROWS :] = jnp.where(row % TABLE_ROWS == RESPONSE, 1.0, 0.0)


def y_lines_kernel(grid_ref, face_ref, from_x_ref, edge_ref, ready_ref, out_ref):
    comps, size_x = grid_ref.shape[0], grid_ref.shape[1] - 2
    size_y = face_ref.shape[0]
    for c in range(comps):
        out_ref[c * size_x : (c + 1) * size_x] = grid_ref[c, 1 : size_x + 1, 0]
        out_ref[comps * size_x + c : comps * size_x + c + 1] = from_x_ref[c * size_y : c * size_y + 1]
    line = jnp.where(lane_ids(8) % PACK == size_x, turned(edge_ref[0:8], size_x), face_ref[0:8])
    out_ref[comps * size_x + comps : comps * size_x + comps + 1] = line[0:1]


def halo_xz_kernel(grid_in_ref, lines_in_ref, face_ref, from_x_ref, edge_ref, grid_ref, lines_ref, top_ref, turned_ref):
    comps, size_x = grid_ref.shape[0], grid_ref.shape[1] - 2
    size_y, size_z = face_ref.shape[0], grid_ref.shape[3]
    count_x, count_y = size_x // BX, size_y // BY
    for c in range(comps):
        grid_ref[c, size_x + 1, 0:size_y] = from_x_ref[c * size_y : (c + 1) * size_y]
    for q in range(count_y - 1):
        lay_out(grid_ref, lines_ref, count_x - 1, q, size_y, size_z)
    top = jnp.where(lane_ids(size_y) % PACK == size_x, turned(edge_ref[...], size_x), face_ref[...])
    top_ref[0:size_y] = top
    top_ref[size_y:] = jnp.zeros((LANES - size_y, LANES), jnp.float32)
    turned_ref[...] = jnp.transpose(top_ref[...])
    for q in range(count_y - 1):
        lay_out_top(turned_ref, lines_ref, q, comps, count_x, count_y, size_z)


def halo_y_kernel(size_y, grid_in_ref, lines_in_ref, top_in_ref, first_ref, second_ref, grid_ref, lines_ref, turned_ref):
    comps, size_x, size_z = grid_ref.shape[0], grid_ref.shape[1] - 2, grid_ref.shape[3]
    count_x, count_y = size_x // BX, size_y // BY
    inside = lax.axis_index("gy") != lax.axis_size("gy") - 1
    kept = (row_ids(8) == 0) & inside
    even = jnp.full((1, LANES), odd("gy")) == 0

    def line_at(row):
        line = jnp.where(even, first_ref[row : row + 1], second_ref[row : row + 1])
        return jnp.where(kept, jnp.broadcast_to(line, (8, LANES)), 0.0)

    for c in range(comps):
        for x in range(size_x + 1):
            grid_ref[c, x + 1, size_y:] = line_at(c * size_x + x if x < size_x else comps * size_x + c)
    for p in range(count_x):
        lay_out(grid_ref, lines_ref, p, count_y - 1, size_y, size_z)
    corner = line_at(comps * size_x + comps)
    rest = jnp.zeros((LANES - size_y - 8, LANES), jnp.float32)
    turned_ref[...] = jnp.transpose(jnp.concatenate([top_in_ref[0:size_y], corner, rest], axis=0))
    lay_out_top(turned_ref, lines_ref, count_y - 1, comps, count_x, count_y, size_z)


def block_steps(dims, list_ref, brick_ref, end):
    comps, _, count_y, count_z, rows_z = dims
    nblocks = brick_ref.shape[0]
    sub = row_ids(8)
    row_y = row_ids(REACH_Y).astype(jnp.float32)
    row_z = row_ids(REACH_Z).astype(jnp.float32)
    lanes = lane_ids(REACH_Z)

    def hat(rows, inside, along):
        return jnp.where(rows == inside, 1.0 - along, 0.0) + jnp.where(rows == inside + 1.0, along, 0.0)

    def place_of(at):
        k = jnp.where(at < end, list_ref[jnp.minimum(at, 2 * nblocks + 1)], nblocks)
        brick = jnp.where(k < nblocks, brick_ref[jnp.minimum(k, nblocks - 1)], 0)
        brick_x = lax.div(brick, count_y * count_z)
        brick_y = lax.rem(lax.div(brick, count_z), count_y)
        return k, brick_x * count_y + brick_y, lax.rem(brick, count_z)

    def loaded(at, lines_ref, table_ref):
        k, pair, brick_z = place_of(at)
        first = pl.multiple_of(pair * comps * rows_z + brick_z * BZ, 8)
        window = jnp.concatenate([lines_ref[pl.ds(first + c * rows_z, REACH_Z)] for c in range(comps)], axis=0)
        table = table_ref[pl.ds(pl.multiple_of(k * TABLE_ROWS, TABLE_ROWS), TABLE_ROWS)]
        return k, window, [table[i : i + 1] for i in range(TABLE_ROWS)]

    def weighted(rows):
        weight_y = hat(row_y, rows[IN_Y], rows[ALONG_Y])
        weight_z = hat(row_z, rows[IN_Z], rows[ALONG_Z])
        weight = jnp.concatenate([rows[WEIGHT + a] * weight_y for a in range(REACH_X)], axis=0)
        return weight_z, *parts_of(weight)

    def stepped(seen, weight_z, rows):
        rate = 1.0 / rows[RESPONSE]
        state, moved, pushed = [], [], []
        for c in range(comps):
            gas_sample = jnp.sum(seen[c * REACH_Z : (c + 1) * REACH_Z] * weight_z, axis=0, keepdims=True)
            drag = (gas_sample - rows[MOVING + c]) * rate
            state.append(rows[MOVING + c] + TIME_STEP * drag)
            moved.append(rows[OFFSET + c] + TIME_STEP * state[c])
            pushed.append(drag * weight_z)
        tile = jnp.broadcast_to(rows[RESPONSE], (STATE, LANES))
        for i, value in enumerate(state + moved):
            tile = jnp.where(sub == i, value, tile)
        return tile, jnp.concatenate(parts_of(jnp.concatenate(pushed, axis=0)), axis=0)

    def gathered(one, two):
        tables, windows, weights = [], [], []
        for _, window, rows in (one, two):
            weight_z, main, rest = weighted(rows)
            weights.append((weight_z, main, rest))
            unused = jnp.zeros((LANES - 3 * SPREAD, LANES), jnp.float32)
            tables.append(jnp.concatenate([main, main, rest, unused], axis=0).astype(jnp.bfloat16))
            windows.append(window)
        seen = lax.dot_general(
            jnp.concatenate(windows, axis=0).astype(jnp.bfloat16), jnp.concatenate(tables, axis=1),
            (((1,), (0,)), ((), ())), preferred_element_type=jnp.float32,
        )
        height = comps * REACH_Z
        tiles, fresh = [], []
        for i, (_, _, rows) in enumerate((one, two)):
            weight_z, main, rest = weights[i]
            mine = seen[i * height : (i + 1) * height, i * LANES : (i + 1) * LANES]
            tile, push = stepped(mine, weight_z, rows)
            tiles.append(tile)
            unused = jnp.zeros((LANES - comps * SPREAD, LANES), jnp.float32)
            spread = jnp.concatenate([main] * comps + [unused] + [rest] * comps + [unused], axis=0)
            fresh.append((push.astype(jnp.bfloat16), spread.astype(jnp.bfloat16)))
        return tiles, fresh

    def shared(push, spread):
        shares = lax.dot_general(push, spread, (((1,), (1,)), ((), ())), preferred_element_type=jnp.float32)
        height = comps * REACH_Z
        total = shares[:height, :LANES] + shares[:height, LANES:] + shares[height:, :LANES]
        result = jnp.zeros((REACH_Z, LANES), jnp.float32)
        for c in range(comps):
            inside = (lanes >= c * SPREAD) & (lanes < (c + 1) * SPREAD)
            result = jnp.where(inside, total[c * REACH_Z : (c + 1) * REACH_Z], result)
        return result

    def add(deposit_ref, at, shares):
        spots = []
        for u in range(len(shares)):
            _, pair, brick_z = place_of(at + u)
            spots.append(pl.ds(pl.multiple_of(pair * rows_z + brick_z * BZ, 8), REACH_Z))
        for spot, share in zip(spots, shares):
            deposit_ref[spot] = deposit_ref[spot] + share

    def group_of(taken):
        tiles, fresh = [], []
        for u in range(0, len(taken), 2):
            both, kept = gathered(taken[u], taken[u + 1])
            tiles.extend(both)
            fresh.extend(kept)
        return tiles, fresh

    def keep(state_ref, taken, tiles):
        for (k, _, _), tile in zip(taken, tiles):
            state_ref[pl.ds(pl.multiple_of(STATE * k, STATE), STATE)] = tile

    def deposits_of(kept):
        return [shared(push, spread) for push, spread in kept]

    return loaded, group_of, keep, deposits_of, add


def groups_in(list_ref, late, many=UNROLL):
    room = (list_ref.shape[0] - 2) // 2
    count = list_ref[2 * room + late]
    return late * room, (count + many - 1) // many, late * room + count


def leave(crossing_ref, state_ref, leaving_ref, faces):
    slots = crossing_ref.shape[1]
    rows = leaving_ref.shape[0] // (len(faces) * slots)
    for i, face in enumerate(faces):
        tiles = []
        for slot in range(slots):
            block = crossing_ref[face, slot]
            spot = pl.ds(pl.multiple_of(jnp.maximum(block, 0) * STATE, STATE), STATE)
            live = jnp.full((STATE, LANES), block, jnp.int32) >= 0
            tiles.append(jnp.where(live, state_ref[spot], 0.0))
        for slot, tile in enumerate(tiles):
            leaving_ref[pl.ds(i * rows * slots + slot, rows, stride=slots)] = tile[:rows]


def fetched(sems, *pairs):
    copies = [pltpu.make_async_copy(source, target, sems.at[i]) for i, (source, target) in enumerate(pairs)]
    for copy in copies:
        copy.start()
    return copies


def gather_kernel(
    dims, list_in, brick_in, table_ref, grid_in_ref, lines_in_ref, face_ref, from_x_ref, edge_ref,
    state_ref, push_ref, spread_ref, grid_ref, lines_ref, top_ref, list_ref, brick_ref, turned_ref, sems,
):
    copies = fetched(sems, (list_in, list_ref), (brick_in, brick_ref))
    halo_xz_kernel(grid_in_ref, lines_in_ref, face_ref, from_x_ref, edge_ref, grid_ref, lines_ref, top_ref, turned_ref)
    for copy in copies:
        copy.wait()
    base, groups, end = groups_in(list_ref, 0, WIDE)
    loaded, group_of, keep, _, _ = block_steps(dims, list_ref, brick_ref, end)

    @pl.loop(0, groups)
    def _(group):
        taken = [loaded(base + group * WIDE + u, lines_ref, table_ref) for u in range(WIDE)]
        tiles, fresh = group_of(taken)
        keep(state_ref, taken, tiles)
        for i, (push, spread) in enumerate(fresh):
            push_ref[group * WIDE + i] = push
            spread_ref[group * WIDE + i] = spread


def deposit_kernel(
    dims, list_ref, brick_ref, crossing_ref, push_ref, spread_ref, state_ref, deposit_in_ref, deposit_ref, leaving_ref
):
    base, groups, end = groups_in(list_ref, 0, WIDE)
    _, _, _, deposits_of, add = block_steps(dims, list_ref, brick_ref, end)
    leave(crossing_ref, state_ref, leaving_ref, (0, 1, 4, 5))

    @pl.loop(0, groups)
    def _(group):
        mine = [group * WIDE + i for i in range(WIDE)]
        add(deposit_ref, base + group * WIDE, deposits_of([(push_ref[i], spread_ref[i]) for i in mine]))


def late_kernel(
    dims, list_in, brick_in, crossing_in, table_ref, grid_in_ref, lines_in_ref, top_in_ref, first_ref, second_ref,
    state_in_ref, deposit_in_ref,
    grid_ref, lines_ref, state_ref, deposit_ref, leaving_ref,
    push_ref, spread_ref, list_ref, brick_ref, crossing_ref, turned_ref, sems,
):
    copies = fetched(sems, (list_in, list_ref), (brick_in, brick_ref), (crossing_in, crossing_ref))
    halo_y_kernel(
        dims[2] * BY, grid_in_ref, lines_in_ref, top_in_ref, first_ref, second_ref, grid_ref, lines_ref, turned_ref
    )
    for copy in copies:
        copy.wait()
    base, groups, end = groups_in(list_ref, 1)
    loaded, group_of, keep, deposits_of, add = block_steps(dims, list_ref, brick_ref, end)
    push_ref[...] = jnp.zeros_like(push_ref)
    spread_ref[...] = jnp.zeros_like(spread_ref)

    @pl.loop(0, groups + 1)
    def _(group):
        now = base + jnp.maximum(jnp.minimum(group, groups - 1), 0) * UNROLL
        before = base + jnp.maximum(group - 1, 0) * UNROLL
        taken = [loaded(now + u, lines_ref, table_ref) for u in range(UNROLL)]
        shares = deposits_of([(push_ref[i], spread_ref[i]) for i in range(UNROLL)])
        tiles, fresh = group_of(taken)
        add(deposit_ref, before, shares)
        keep(state_ref, taken, tiles)
        for i, (push, spread) in enumerate(fresh):
            push_ref[i] = push
            spread_ref[i] = spread

    leave(crossing_ref, state_ref, leaving_ref, (2, 3))


def top_rows(deposit_ref, q, count_x, count_y, rows_z, size_z):
    total = None
    for p in range(count_x):
        at = (p * count_y + q) * rows_z + size_z
        value = pltpu.roll(deposit_ref[at : at + 8], p, 0) if p else deposit_ref[at : at + 8]
        total = value if total is None else total + value
    return total


def send_y_kernel(push, diffuse, leaving_ref, grid_ref, deposit_ref, y1_ref, y2_ref, tiles_ref, lines_ref):
    comps, size_x, size_y, size_z = grid_ref.shape[0], grid_ref.shape[1] - 2, grid_ref.shape[2] - 8, grid_ref.shape[3]
    count_x, count_y = size_x // BX, size_y // BY
    rows_z = size_z + 8
    rows = leaving_ref.shape[1]
    height = comps * SPREAD
    for p in range(count_x):
        at = (p * count_y + count_y - 1) * rows_z
        tiles_ref[p * height : (p + 1) * height] = jnp.transpose(deposit_ref[at : at + size_z])[:height]
    first = jnp.full((rows, LANES), odd("gy")) == 0
    y1_ref[0:rows] = jnp.where(first, leaving_ref[0], leaving_ref[1])
    y2_ref[0:rows] = jnp.where(first, leaving_ref[1], leaving_ref[0])
    lines_ref[...] = jnp.zeros_like(lines_ref)
    for c in range(comps):
        for p in range(count_x):
            spot = slice(c * ROWS_Y + p * BX, c * ROWS_Y + p * BX + REACH_X)
            line = tiles_ref[pl.ds(p * height + c * SPREAD + BY, REACH_X, stride=REACH_Y)]
            lines_ref[spot] = lines_ref[spot] + line
    wrapped = top_rows(deposit_ref, count_y - 1, count_x, count_y, rows_z, size_z)
    lane = lane_ids(8)
    packed = jnp.zeros((8, LANES), jnp.float32)
    for c in range(comps):
        spot = slice(c * ROWS_Y, (c + 1) * ROWS_Y)
        beside = jnp.concatenate([grid_ref[c, 1 : size_x + 1, size_y - 1], jnp.zeros((8, LANES), jnp.float32)], axis=0)
        line = push * lines_ref[spot] + diffuse * beside
        at = rows + c * (size_x + 1)
        y1_ref[at : at + size_x + 1] = line[: size_x + 1]
        y2_ref[at : at + size_x + 1] = line[: size_x + 1]
        for a in range(REACH_X):
            place = PACK * c + a
            value = turned(wrapped, place - c * SPREAD - a * REACH_Y - BY)
            packed = packed + jnp.where(lane == place, value, 0.0)
    corner = packed[0:1]
    for p in range(1, count_x):
        corner = corner + turned(packed[p : p + 1], p * BX)
    at = rows + comps * (size_x + 1)
    y1_ref[at : at + 1] = push * corner
    y2_ref[at : at + 1] = push * corner


def merge_kernel(deposit_ref, top_tiles_ref, plane_ref, face_ref, tiles_ref, turned_ref):
    comps, planes = plane_ref.shape[:2]
    count_x, size_z = (planes - 1) // BX, plane_ref.shape[3]
    rows_z = size_z + 8
    count_y = deposit_ref.shape[0] // (rows_z * count_x)
    height = comps * SPREAD
    for p in range(count_x):
        for q in range(count_y - 1):
            at = p * count_y + q
            value = jnp.transpose(deposit_ref[at * rows_z : at * rows_z + size_z])
            tiles_ref[at * height : (at + 1) * height] = value[:height]
    top = row_ids(REACH_Y) >= BY
    for c in range(comps):
        for x in range(planes):
            bricks = [(x // BX, x % BX)] if x < planes - 1 else []
            if x and x % BX == 0:
                bricks.append((x // BX - 1, BX))

            def tile(q):
                total = None
                for p, a in bricks:
                    at = c * SPREAD + a * REACH_Y
                    if q < count_y - 1:
                        value = tiles_ref[(p * count_y + q) * height + at : (p * count_y + q) * height + at + REACH_Y]
                    else:
                        value = top_tiles_ref[p * height + at : p * height + at + REACH_Y]
                    total = value if total is None else total + value
                return total

            carried = None
            for q in range(0, count_y, 2):
                here = tile(q)
                if carried is not None:
                    here = here + carried
                between = pltpu.roll(tile(q + 1), BY, 0)
                here = here + jnp.where(top, between, 0.0)
                carried = jnp.where(top, 0.0, between)
                plane_ref[c, x, q * BY : q * BY + REACH_Y] = here
            plane_ref[c, x, count_y * BY :] = carried

    lane = lane_ids(count_x)
    turned_ref[...] = jnp.zeros_like(turned_ref)
    for q in range(count_y):
        wrapped = top_rows(deposit_ref, q, count_x, count_y, rows_z, size_z)[:count_x]
        within = (lane >= q * BY) & (lane <= (q + 1) * BY)
        for c in range(comps):
            for a in range(REACH_X):
                value = turned(wrapped, q * BY - c * SPREAD - a * REACH_Y)
                spot = pl.ds(PACK * c + a, count_x, stride=BX)
                turned_ref[spot] = turned_ref[spot] + jnp.where(within, value, 0.0)
    face_ref[...] = jnp.transpose(turned_ref[...])[: face_ref.shape[0]]


def send_xz_kernel(push, diffuse, grid_ref, deposit_ref, face_ref, x_ref, z_ref):
    comps, size_x = grid_ref.shape[0], grid_ref.shape[1] - 2
    size_y = z_ref.shape[0]
    lane = lane_ids(size_y)
    packed = push * face_ref[0:size_y]
    for c in range(comps):
        for x in range(size_x):
            place = PACK * c + x
            packed = packed + jnp.where(lane == place, diffuse * turned(grid_ref[c, x + 1, 0:size_y], place + 1), 0.0)
        total = push * deposit_ref[c, size_x, 0:size_y]
        x_ref[c * size_y : (c + 1) * size_y] = diffuse * grid_ref[c, size_x, 0:size_y] + total
    z_ref[...] = packed


def base_kernel(push, diffuse, count, grid_ref, deposit_ref, top_ref, y1_ref, y2_ref, state_ref, base_ref, velocity_ref):
    comps, size_x, size_y, size_z = base_ref.shape
    lane, sub = lane_ids(size_y), row_ids(size_y)
    top = top_ref[0:size_y]
    for c in range(comps):
        at = count + c * (size_x + 1)
        lines = below(y1_ref, y2_ref, slice(at, at + size_x))
        for x in range(size_x):
            here = grid_ref[c, x + 1, 0:size_y]
            before = jnp.where(sub == 0, 0.0, pltpu.roll(here, 1, 0))
            laplace = grid_ref[c, x, 0:size_y] + grid_ref[c, x + 2, 0:size_y]
            laplace = laplace + grid_ref[c, x + 1, 1 : size_y + 1] + before
            ahead = jnp.where(lane == size_z - 1, turned(top, size_z - 1 - (PACK * c + x)), turned(here, -1))
            laplace = laplace + ahead + jnp.where(lane == 0, 0.0, turned(here, 1)) - 6.0 * here
            total = here + diffuse * laplace + push * deposit_ref[c, x, 0:size_y]
            line = jnp.broadcast_to(lines[x : x + 1], (size_y, LANES))
            base_ref[c, x] = total + jnp.where(sub == 0, line, 0.0)
        velocity_ref[c] = state_ref[pl.ds(c, velocity_ref.shape[1], stride=STATE)]


def below(first_ref, second_ref, rows):
    got = jnp.where(jnp.full((1, LANES), odd("gy")) == 1, first_ref[rows], second_ref[rows])
    return jnp.where(jnp.full((1, LANES), lax.axis_index("gy")) != 0, got, 0.0)


def relay_kernel(size_x, size_y, comps, count, first_ref, second_ref, x_in_ref, z_in_ref, leaving_ref, x_ref, z1_ref, z2_ref, edge_ref):
    edge = comps * size_y
    x_ref[0:edge] = x_in_ref[...]
    for c in range(comps):
        at = count + c * (size_x + 1) + size_x
        spot = slice(c * size_y, c * size_y + 1)
        x_ref[spot] = x_in_ref[spot] + below(first_ref, second_ref, slice(at, at + 1))
    x_ref[edge : edge + count] = leaving_ref[0]
    if x_ref.shape[0] > edge + count:
        x_ref[edge + count : edge + 2 * count] = leaving_ref[1]
    at = count + comps * (size_x + 1)
    edge_ref[size_y:] = jnp.zeros((edge_ref.shape[0] - size_y, LANES), jnp.float32)
    edge_ref[0:size_y] = z_in_ref[...]
    edge_ref[0:1] = z_in_ref[0:1] + below(first_ref, second_ref, slice(at, at + 1))
    first = jnp.full((1, LANES), odd("gz")) == 0
    plus = jnp.concatenate([leaving_ref[2], edge_ref[0:size_y]], axis=0)
    minus = jnp.concatenate([leaving_ref[3], jnp.zeros((size_y, LANES), jnp.float32)], axis=0)
    z1_ref[...] = jnp.where(first, plus, minus)
    z2_ref[0 : count + size_y] = jnp.where(first, minus, plus)
    z2_ref[count + size_y :] = jnp.zeros((z2_ref.shape[0] - count - size_y, LANES), jnp.float32)


def finish_kernel(
    count, base_ref, y1_ref, y2_ref, x_ref, minus_x_ref, z1_ref, z2_ref, edge_ref, gas_out, arrivals_out,
    gas_ref, arrivals_ref, sems,
):
    comps, size_x, size_y, _ = base_ref.shape
    first_lane = lane_ids(size_y) == 0
    odd_y, odd_z = jnp.full((1, LANES), odd("gy")) == 1, jnp.full((1, LANES), odd("gz")) == 1
    place = jnp.full((1, LANES), lax.axis_index("gy"))
    lower, upper = place != 0, place != lax.axis_size("gy") - 1
    rows = slice(count, count + size_y)
    slots = arrivals_ref.shape[2]
    for i in range(arrivals_ref.shape[1]):

        def rows_of(ref, at=0):
            return ref[at + i * slots : at + (i + 1) * slots]

        arrivals_ref[0, i] = rows_of(x_ref, comps * size_y)
        arrivals_ref[1, i] = rows_of(minus_x_ref, minus_x_ref.shape[0] - count)
        y1, y2 = rows_of(y1_ref), rows_of(y2_ref)
        arrivals_ref[2, i] = jnp.where(lower, jnp.where(odd_y, y1, y2), 0.0)
        arrivals_ref[3, i] = jnp.where(upper, jnp.where(odd_y, y2, y1), 0.0)
        z1, z2 = rows_of(z1_ref), rows_of(z2_ref)
        arrivals_ref[4, i] = jnp.where(odd_z, z1, z2)
        arrivals_ref[5, i] = jnp.where(odd_z, z2, z1)
    copies = [pltpu.make_async_copy(arrivals_ref, arrivals_out, sems.at[comps])]
    copies[0].start()
    face = jnp.where(odd_z, z1_ref[rows], z2_ref[rows])
    corner = edge_ref[0:size_y]
    for c in range(comps):
        for x in range(size_x):
            total = base_ref[c, x]
            far = turned(face, -(PACK * c + x))
            if x == 0:
                total = total + x_ref[c * size_y : (c + 1) * size_y]
                far = far + turned(corner, -(PACK * c + size_x))
            gas_ref[c, x] = total + jnp.where(first_lane, far, 0.0)
        copies.append(pltpu.make_async_copy(gas_ref.at[c], gas_out.at[c], sems.at[c]))
        copies[-1].start()
    for copy in copies:
        copy.wait()


def per_device(gas_field, velocity, fraction, response, cell_index, brick_index, crossing):
    comps, size_x, size_y, size_z = gas_field.shape
    nblocks = velocity.shape[0]
    loading = 0.5 * size_x * size_y * size_z / (nblocks * 128)
    push, diffuse = -TIME_STEP * loading, TIME_STEP * VISCOSITY
    velocity = jnp.transpose(velocity, (1, 0, 2))
    fraction = jnp.transpose(fraction, (1, 0, 2))
    spare = nblocks + 8
    rows_z = size_z + 8
    grid_shape = (comps, size_x + 2, ROWS_Y, LANES)
    lines_shape = ((size_x // BX) * (size_y // BY) * comps * rows_z, LANES)
    deposit_shape = ((size_x // BX) * (size_y // BY) * rows_z, LANES)

    inputs = (gas_field, velocity, fraction, response, cell_index, brick_index, crossing)
    inputs = [pltpu.with_memory_space_constraint(array, pltpu.HBM) for array in inputs]
    grid, face, plane, velocity, fraction, response, cell_index, brick_index, crossing = call(
        begin_kernel,
        [grid_shape, (size_y, LANES), (comps * size_y, LANES)]
        + [jax.ShapeDtypeStruct(array.shape, array.dtype) for array in inputs[1:]],
        *inputs, hbm=range(7), scratch=(pltpu.SemaphoreType.DMA((7,)),),
    )
    from_z = moved_along(face, "gz", -1)
    from_x = moved_along(plane, "gx", -1)
    from_xz = moved_diagonally(face, -1)
    lines, deposit, table, ready, blocks = call(
        prepare_kernel,
        [
            lines_shape,
            deposit_shape,
            (TABLE_ROWS * spare, LANES),
            (8, LANES),
            jax.ShapeDtypeStruct((2 * nblocks + 2,), jnp.int32),
        ],
        grid, velocity, fraction, response, cell_index, brick_index,
        smem=(5,), smem_outs=(4,), cycles=3000,
    )
    line_rows = -(-(comps * size_x + comps + 1) // 8) * 8
    (y_lines,) = call(y_lines_kernel, [(line_rows, LANES)], grid, from_z, from_x, from_xz, ready)
    y1, y2 = swapped_y((y_lines, y_lines))
    square = pltpu.VMEM((LANES, LANES), jnp.float32)
    scalars = (pltpu.SMEM(blocks.shape, jnp.int32), pltpu.SMEM(brick_index.shape, jnp.int32))
    dims = (comps, size_x // BX, size_y // BY, size_z // BZ, rows_z)
    slots = crossing.shape[1]
    count = 7 * slots

    def parts(many):
        return [(many, 2 * comps * REACH_Z, LANES), (many, 2 * LANES, LANES)]

    state, push_parts, spread_parts, grid, lines, top = call(
        functools.partial(gather_kernel, dims),
        [(STATE * spare, LANES)]
        + [jax.ShapeDtypeStruct(shape, jnp.bfloat16) for shape in parts(-(-nblocks // WIDE) * WIDE)]
        + [grid_shape, lines_shape, (LANES, LANES)],
        blocks, brick_index, table, grid, lines, from_z, from_x, from_xz,
        aliases={3: 3, 4: 4}, cycles=4000, scratch=(*scalars, square, pltpu.SemaphoreType.DMA((2,))),
    )
    grid, lines, state, deposit, leaving = call(
        functools.partial(late_kernel, dims),
        [grid_shape, lines_shape, (STATE * spare, LANES), deposit_shape, (2 * count, LANES)],
        blocks, brick_index, crossing, table, grid, lines, top, y1, y2, state, deposit,
        aliases={4: 0, 5: 1, 9: 2, 10: 3}, cycles=2000,
        scratch=[
            *(pltpu.VMEM(shape, jnp.bfloat16) for shape in parts(UNROLL)),
            *scalars,
            pltpu.SMEM(crossing.shape, jnp.int32),
            square,
            pltpu.SemaphoreType.DMA((3,)),
        ],
    )
    leaving = leaving.reshape(2, count, LANES)
    height = comps * SPREAD
    to_y1, to_y2, top_tiles = call(
        functools.partial(send_y_kernel, push, diffuse),
        [(count + line_rows, LANES), (count + line_rows, LANES), ((size_x // BX) * height, LANES)],
        leaving, grid, deposit, cycles=300, scratch=(pltpu.VMEM((comps * ROWS_Y, LANES), jnp.float32),),
    )
    y1, y2 = swapped_y((to_y1, to_y2))
    deposit, leaving = call(
        functools.partial(deposit_kernel, dims), [deposit_shape, (4 * count, LANES)],
        blocks, brick_index, crossing, push_parts, spread_parts, state, deposit,
        smem=(0, 1, 2), aliases={6: 0}, cycles=4000,
    )
    leaving = leaving.reshape(4, count, LANES)
    deposit, over = call(
        merge_kernel, [(comps, size_x + 1, ROWS_Y, LANES), (ROWS_Y, LANES)], deposit, top_tiles,
        cycles=1000, scratch=(pltpu.VMEM(((size_x // BX) * (size_y // BY) * height, LANES), jnp.float32), square),
    )
    to_x, to_z = call(
        functools.partial(send_xz_kernel, push, diffuse), [(comps * size_y, LANES), (size_y, LANES)],
        grid, deposit, over, cycles=500,
    )
    base, velocity_next = call(
        functools.partial(base_kernel, push, diffuse, count), [gas_field.shape, (comps, nblocks, LANES)],
        grid, deposit, top, y1, y2, state, cycles=1000,
    )
    edge = comps * size_y
    both = lax.axis_size("gx") == 2
    to_x, to_z1, to_z2, to_xz = call(
        functools.partial(relay_kernel, size_x, size_y, comps, count),
        [(edge + (2 if both else 1) * count, LANES), *[(count + size_y + 8 * more, LANES) for more in range(3)]],
        y1, y2, to_x, to_z, leaving,
    )
    got_x = moved_along(to_x, "gx", 1)
    z1, z2 = swapped_z((to_z1, to_z2))
    got_xz = moved_diagonally(to_xz, 1)
    got_mx = got_x if both else moved_along(leaving[1], "gx", -1)
    gas_next, arrivals = call(
        functools.partial(finish_kernel, count), [gas_field.shape, (6, 7, slots, LANES)],
        base, y1, y2, got_x, got_mx, z1, z2, got_xz, hbm_outs=(0, 1),
        scratch=(
            pltpu.VMEM(gas_field.shape, jnp.float32),
            pltpu.VMEM((6, 7, slots, LANES), jnp.float32),
            pltpu.SemaphoreType.DMA((comps + 1,)),
        ),
    )
    return gas_next, jnp.transpose(velocity_next, (1, 0, 2)), jnp.transpose(arrivals, (0, 2, 1, 3))


def solution(mesh):
    owner = ("gx", "gz", "gy")
    in_specs = (
        P(None, "gx", "gy", "gz"),
        P(owner, None, None),
        P(owner, None, None),
        P(owner, None),
        P(owner, None),
        P(owner),
        P(owner, None),
    )
    out_specs = (
        P(None, "gx", "gy", "gz"),
        P(owner, None, None),
        P(owner, None, None, None),
    )
    return jax.shard_map(
        per_device, mesh=mesh, in_specs=in_specs, out_specs=out_specs, check_vma=False
    )
```

```python
import functools

import jax
import jax.numpy as jnp
from jax import lax
from jax.experimental import pallas as pl
from jax.experimental.pallas import tpu as pltpu
from jax.sharding import PartitionSpec as P

BX = 4
BY = 4
BZ = 8

TIME_STEP = 0.25
VISCOSITY = 0.4

LANES = 128
PACK = 32
ROWS_Y = 24
REACH_X = BX + 1
REACH_Y = 8
SPREAD = REACH_X * REACH_Y
REACH_Z = 2 * BZ
UNROLL = 8
WIDE = 16

WEIGHT, ALONG_Y, IN_Y, ALONG_Z, IN_Z, RESPONSE, MOVING, OFFSET = 0, 5, 6, 7, 8, 9, 10, 13
TABLE_ROWS = 16
STATE = 8

VMEM = pl.BlockSpec(memory_space=pltpu.VMEM)
SMEM = pl.BlockSpec(memory_space=pltpu.SMEM)
HBM = pl.BlockSpec(memory_space=pltpu.HBM)


def moved_along(block, axis, distance):
    count = lax.axis_size(axis)
    return lax.ppermute(block, axis, [(i, (i + distance) % count) for i in range(count)])


def swapped_z(blocks):
    count = lax.axis_size("gz")
    first = [(i, i ^ 1) for i in range(count)]
    second = [(i, (((i + 1) ^ 1) - 1) % count) for i in range(count)]
    return lax.ppermute(blocks[0], "gz", first), lax.ppermute(blocks[1], "gz", second)


def swapped_y(blocks):
    nz, ny = lax.axis_size("gz"), lax.axis_size("gy")
    first = [(j, j ^ 1) for j in range(ny)]
    second = []
    for k in range(nz):
        second.append((k * ny, (k ^ 1) * ny))
        second.append((k * ny + ny - 1, (k ^ 1) * ny + ny - 1))
        second.extend((k * ny + j, k * ny + ((j + 1) ^ 1) - 1) for j in range(1, ny - 1))
    middle = lax.ppermute(blocks[1], ("gz", "gy"), second)
    return lax.ppermute(blocks[0], "gy", first), middle


def moved_diagonally(block, distance):
    nx, nz = lax.axis_size("gx"), lax.axis_size("gz")
    route = [(i * nz + k, (i + distance) % nx * nz + (k + distance) % nz) for i in range(nx) for k in range(nz)]
    return lax.ppermute(block, ("gx", "gz"), route)


def call(
    body, outs, *operands, smem=(), hbm=(), smem_outs=(), hbm_outs=(), scratch=(), aliases=None, cycles=0, limit=40
):
    return pl.pallas_call(
        body,
        out_shape=[o if isinstance(o, jax.ShapeDtypeStruct) else jax.ShapeDtypeStruct(o, jnp.float32) for o in outs],
        in_specs=[SMEM if i in smem else HBM if i in hbm else VMEM for i in range(len(operands))],
        out_specs=[SMEM if i in smem_outs else HBM if i in hbm_outs else VMEM for i in range(len(outs))],
        scratch_shapes=list(scratch),
        input_output_aliases=aliases or {},
        compiler_params=pltpu.CompilerParams(vmem_limit_bytes=limit * 1024 * 1024),
        cost_estimate=pl.CostEstimate(flops=cycles * 4096, bytes_accessed=cycles * 1024, transcendentals=0),
    )(*operands)


def lane_ids(rows):
    return lax.broadcasted_iota(jnp.int32, (rows, LANES), 1)


def row_ids(rows):
    return lax.broadcasted_iota(jnp.int32, (rows, LANES), 0)


def turned(value, shift):
    shift = shift % LANES
    return pltpu.roll(value, shift, 1) if shift else value


def odd(axis):
    return lax.axis_index(axis) % 2


def begin_kernel(
    gas_ref, velocity_in, fraction_in, response_in, cell_in, brick_in, crossing_in,
    grid_ref, face_ref, plane_ref, velocity_ref, fraction_ref, response_ref, cell_ref, brick_ref, crossing_ref, sems,
):
    comps, size_x, size_y, _ = gas_ref.shape
    pairs = [
        (gas_ref, grid_ref.at[:, 1 : size_x + 1, 0:size_y]),
        (velocity_in, velocity_ref), (fraction_in, fraction_ref), (response_in, response_ref),
        (cell_in, cell_ref), (brick_in, brick_ref), (crossing_in, crossing_ref),
    ]
    copies = [pltpu.make_async_copy(source, target, sems.at[i]) for i, (source, target) in enumerate(pairs)]
    for copy in copies:
        copy.start()
    zeros = jnp.zeros((ROWS_Y, LANES), jnp.float32)
    for c in range(comps):
        grid_ref[c, 0] = zeros
        grid_ref[c, size_x + 1] = zeros
        for x in range(size_x):
            grid_ref[c, x + 1, size_y:] = zeros[size_y:]
    copies[0].wait()
    lane = lane_ids(size_y)
    face = jnp.zeros((size_y, LANES), jnp.float32)
    for c in range(comps):
        plane_ref[c * size_y : (c + 1) * size_y] = grid_ref[c, 1, 0:size_y]
        for x in range(size_x):
            place = PACK * c + x
            face = jnp.where(lane == place, turned(grid_ref[c, x + 1, 0:size_y], place), face)
    face_ref[...] = face
    for copy in copies[1:]:
        copy.wait()


def parts_of(value):
    main = value.astype(jnp.bfloat16).astype(jnp.float32)
    return main, value - main


def lay_out(grid_ref, lines_ref, p, q, size_y, size_z):
    comps = grid_ref.shape[0]
    rows_z = size_z + 8
    count_y = size_y // BY
    for c in range(comps):
        planes = [grid_ref[c, p * BX + a + 1, q * BY : q * BY + REACH_Y] for a in range(REACH_X)]
        main, rest = parts_of(jnp.concatenate(planes, axis=0))
        stack = jnp.concatenate([main, rest, main, jnp.zeros((LANES - 3 * SPREAD, LANES), jnp.float32)], axis=0)
        at = ((p * count_y + q) * comps + c) * rows_z
        lines_ref[at : at + size_z] = jnp.transpose(stack)


def lay_out_top(turned_ref, lines_ref, q, comps, count_x, count_y, size_z):
    lane = lane_ids(count_x)
    rows_z = size_z + 8
    for c in range(comps):
        total = jnp.zeros((count_x, LANES), jnp.float32)
        for a in range(REACH_X):
            rows = turned_ref[pl.ds(PACK * c + a, count_x, stride=BX)]
            total = jnp.where(lane // REACH_Y == a, turned(rows, a * REACH_Y - q * BY), total)
        main, rest = parts_of(total)
        line = main + turned(rest, SPREAD) + turned(main, 2 * SPREAD)
        for p in range(count_x):
            at = ((p * count_y + q) * comps + c) * rows_z + size_z
            lines_ref[at : at + 1] = line[p : p + 1]


def prepare_kernel(
    grid_ref, velocity_ref, fraction_ref, response_ref, cell_ref, brick_ref,
    lines_ref, deposit_ref, table_ref, ready_ref, list_ref,
):
    comps, size_x, size_y, size_z = grid_ref.shape[0], grid_ref.shape[1] - 2, grid_ref.shape[2] - 8, grid_ref.shape[3]
    nblocks = velocity_ref.shape[1]
    count_x, count_y, count_z = size_x // BX, size_y // BY, size_z // BZ
    rows_z = size_z + 8


    def visit(k, counts):
        late = jnp.where(lax.rem(lax.div(brick_ref[k], count_z), count_y) == count_y - 1, 1, 0)
        list_ref[jnp.where(late == 1, nblocks + counts[1], counts[0])] = k
        return counts[0] + 1 - late, counts[1] + late

    early, late = lax.fori_loop(0, nblocks, visit, (jnp.int32(0), jnp.int32(0)), unroll=8)
    list_ref[2 * nblocks] = early
    list_ref[2 * nblocks + 1] = late
    ready_ref[...] = jnp.zeros_like(ready_ref)

    deposit_ref[...] = jnp.zeros_like(deposit_ref)
    for p in range(count_x):
        for q in range(count_y):
            for c in range(comps):
                at = ((p * count_y + q) * comps + c) * rows_z + size_z
                lines_ref[at : at + 8] = jnp.zeros((8, LANES), jnp.float32)
    for p in range(count_x - 1):
        for q in range(count_y - 1):
            lay_out(grid_ref, lines_ref, p, q, size_y, size_z)

    cells = cell_ref[...]
    cell_x, cell_y, cell_z = cells // (BY * BZ), cells // BZ % BY, cells % BZ
    along_x = fraction_ref[0]

    def put(row, value):
        table_ref[pl.ds(row, nblocks, stride=TABLE_ROWS)] = value

    for a in range(REACH_X):
        put(WEIGHT + a, jnp.where(cell_x == a, 1.0 - along_x, 0.0) + jnp.where(cell_x == a - 1, along_x, 0.0))
    put(ALONG_Y, fraction_ref[1])
    put(IN_Y, cell_y.astype(jnp.float32))
    put(ALONG_Z, fraction_ref[2])
    put(IN_Z, cell_z.astype(jnp.float32))
    put(RESPONSE, response_ref[...])
    for c in range(comps):
        put(MOVING + c, velocity_ref[c])
        put(OFFSET + c, fraction_ref[c])
    spare = table_ref.shape[0] - nblocks * TABLE_ROWS
    row = row_ids(spare)
    table_ref[nblocks * TABLE_ROWS :] = jnp.where(row % TABLE_ROWS == RESPONSE, 1.0, 0.0)


def y_lines_kernel(grid_ref, face_ref, from_x_ref, edge_ref, ready_ref, out_ref):
    comps, size_x = grid_ref.shape[0], grid_ref.shape[1] - 2
    size_y = face_ref.shape[0]
    for c in range(comps):
        out_ref[c * size_x : (c + 1) * size_x] = grid_ref[c, 1 : size_x + 1, 0]
        out_ref[comps * size_x + c : comps * size_x + c + 1] = from_x_ref[c * size_y : c * size_y + 1]
    line = jnp.where(lane_ids(8) % PACK == size_x, turned(edge_ref[0:8], size_x), face_ref[0:8])
    out_ref[comps * size_x + comps : comps * size_x + comps + 1] = line[0:1]


def halo_xz_kernel(grid_in_ref, lines_in_ref, face_ref, from_x_ref, edge_ref, grid_ref, lines_ref, top_ref, turned_ref):
    comps, size_x = grid_ref.shape[0], grid_ref.shape[1] - 2
    size_y, size_z = face_ref.shape[0], grid_ref.shape[3]
    count_x, count_y = size_x // BX, size_y // BY
    for c in range(comps):
        grid_ref[c, size_x + 1, 0:size_y] = from_x_ref[c * size_y : (c + 1) * size_y]
    for q in range(count_y - 1):
        lay_out(grid_ref, lines_ref, count_x - 1, q, size_y, size_z)
    top = jnp.where(lane_ids(size_y) % PACK == size_x, turned(edge_ref[...], size_x), face_ref[...])
    top_ref[0:size_y] = top
    top_ref[size_y:] = jnp.zeros((LANES - size_y, LANES), jnp.float32)
    turned_ref[...] = jnp.transpose(top_ref[...])
    for q in range(count_y - 1):
        lay_out_top(turned_ref, lines_ref, q, comps, count_x, count_y, size_z)


def halo_y_kernel(size_y, grid_in_ref, lines_in_ref, top_in_ref, first_ref, second_ref, grid_ref, lines_ref, turned_ref):
    comps, size_x, size_z = grid_ref.shape[0], grid_ref.shape[1] - 2, grid_ref.shape[3]
    count_x, count_y = size_x // BX, size_y // BY
    inside = lax.axis_index("gy") != lax.axis_size("gy") - 1
    kept = (row_ids(8) == 0) & inside
    even = jnp.full((1, LANES), odd("gy")) == 0

    def line_at(row):
        line = jnp.where(even, first_ref[row : row + 1], second_ref[row : row + 1])
        return jnp.where(kept, jnp.broadcast_to(line, (8, LANES)), 0.0)

    for c in range(comps):
        for x in range(size_x + 1):
            grid_ref[c, x + 1, size_y:] = line_at(c * size_x + x if x < size_x else comps * size_x + c)
    for p in range(count_x):
        lay_out(grid_ref, lines_ref, p, count_y - 1, size_y, size_z)
    corner = line_at(comps * size_x + comps)
    rest = jnp.zeros((LANES - size_y - 8, LANES), jnp.float32)
    turned_ref[...] = jnp.transpose(jnp.concatenate([top_in_ref[0:size_y], corner, rest], axis=0))
    lay_out_top(turned_ref, lines_ref, count_y - 1, comps, count_x, count_y, size_z)


def block_steps(dims, list_ref, brick_ref, end):
    comps, _, count_y, count_z, rows_z = dims
    nblocks = brick_ref.shape[0]
    sub = row_ids(8)
    row_y = row_ids(REACH_Y).astype(jnp.float32)
    row_z = row_ids(REACH_Z).astype(jnp.float32)
    lanes = lane_ids(REACH_Z)

    def hat(rows, inside, along):
        return jnp.where(rows == inside, 1.0 - along, 0.0) + jnp.where(rows == inside + 1.0, along, 0.0)

    def place_of(at):
        k = jnp.where(at < end, list_ref[jnp.minimum(at, 2 * nblocks + 1)], nblocks)
        brick = jnp.where(k < nblocks, brick_ref[jnp.minimum(k, nblocks - 1)], 0)
        brick_x = lax.div(brick, count_y * count_z)
        brick_y = lax.rem(lax.div(brick, count_z), count_y)
        return k, brick_x * count_y + brick_y, lax.rem(brick, count_z)

    def loaded(at, lines_ref, table_ref):
        k, pair, brick_z = place_of(at)
        first = pl.multiple_of(pair * comps * rows_z + brick_z * BZ, 8)
        window = jnp.concatenate([lines_ref[pl.ds(first + c * rows_z, REACH_Z)] for c in range(comps)], axis=0)
        table = table_ref[pl.ds(pl.multiple_of(k * TABLE_ROWS, TABLE_ROWS), TABLE_ROWS)]
        return k, window, [table[i : i + 1] for i in range(TABLE_ROWS)]

    def weighted(rows):
        weight_y = hat(row_y, rows[IN_Y], rows[ALONG_Y])
        weight_z = hat(row_z, rows[IN_Z], rows[ALONG_Z])
        weight = jnp.concatenate([rows[WEIGHT + a] * weight_y for a in range(REACH_X)], axis=0)
        return weight_z, *parts_of(weight)

    def stepped(seen, weight_z, rows):
        rate = 1.0 / rows[RESPONSE]
        state, moved, pushed = [], [], []
        for c in range(comps):
            gas_sample = jnp.sum(seen[c * REACH_Z : (c + 1) * REACH_Z] * weight_z, axis=0, keepdims=True)
            drag = (gas_sample - rows[MOVING + c]) * rate
            state.append(rows[MOVING + c] + TIME_STEP * drag)
            moved.append(rows[OFFSET + c] + TIME_STEP * state[c])
            pushed.append(drag * weight_z)
        tile = jnp.broadcast_to(rows[RESPONSE], (STATE, LANES))
        for i, value in enumerate(state + moved):
            tile = jnp.where(sub == i, value, tile)
        return tile, jnp.concatenate(parts_of(jnp.concatenate(pushed, axis=0)), axis=0)

    def gathered(one, two):
        tables, windows, weights = [], [], []
        for _, window, rows in (one, two):
            weight_z, main, rest = weighted(rows)
            weights.append((weight_z, main, rest))
            unused = jnp.zeros((LANES - 3 * SPREAD, LANES), jnp.float32)
            tables.append(jnp.concatenate([main, main, rest, unused], axis=0).astype(jnp.bfloat16))
            windows.append(window)
        seen = lax.dot_general(
            jnp.concatenate(windows, axis=0).astype(jnp.bfloat16), jnp.concatenate(tables, axis=1),
            (((1,), (0,)), ((), ())), preferred_element_type=jnp.float32,
        )
        height = comps * REACH_Z
        tiles, fresh = [], []
        for i, (_, _, rows) in enumerate((one, two)):
            weight_z, main, rest = weights[i]
            mine = seen[i * height : (i + 1) * height, i * LANES : (i + 1) * LANES]
            tile, push = stepped(mine, weight_z, rows)
            tiles.append(tile)
            unused = jnp.zeros((LANES - comps * SPREAD, LANES), jnp.float32)
            spread = jnp.concatenate([main] * comps + [unused] + [rest] * comps + [unused], axis=0)
            fresh.append((push.astype(jnp.bfloat16), spread.astype(jnp.bfloat16)))
        return tiles, fresh

    def shared(push, spread):
        shares = lax.dot_general(push, spread, (((1,), (1,)), ((), ())), preferred_element_type=jnp.float32)
        height = comps * REACH_Z
        total = shares[:height, :LANES] + shares[:height, LANES:] + shares[height:, :LANES]
        result = jnp.zeros((REACH_Z, LANES), jnp.float32)
        for c in range(comps):
            inside = (lanes >= c * SPREAD) & (lanes < (c + 1) * SPREAD)
            result = jnp.where(inside, total[c * REACH_Z : (c + 1) * REACH_Z], result)
        return result

    def add(deposit_ref, at, shares):
        spots = []
        for u in range(len(shares)):
            _, pair, brick_z = place_of(at + u)
            spots.append(pl.ds(pl.multiple_of(pair * rows_z + brick_z * BZ, 8), REACH_Z))
        for spot, share in zip(spots, shares):
            deposit_ref[spot] = deposit_ref[spot] + share

    def group_of(taken):
        tiles, fresh = [], []
        for u in range(0, len(taken), 2):
            both, kept = gathered(taken[u], taken[u + 1])
            tiles.extend(both)
            fresh.extend(kept)
        return tiles, fresh

    def keep(state_ref, taken, tiles):
        for (k, _, _), tile in zip(taken, tiles):
            state_ref[pl.ds(pl.multiple_of(STATE * k, STATE), STATE)] = tile

    def deposits_of(kept):
        return [shared(push, spread) for push, spread in kept]

    return loaded, group_of, keep, deposits_of, add


def groups_in(list_ref, late, many=UNROLL):
    room = (list_ref.shape[0] - 2) // 2
    count = list_ref[2 * room + late]
    return late * room, (count + many - 1) // many, late * room + count


def leave(crossing_ref, state_ref, leaving_ref, faces):
    slots = crossing_ref.shape[1]
    rows = (leaving_ref.shape[0] - 8) // (len(faces) * slots)
    for i, face in enumerate(faces):
        tiles = []
        for slot in range(slots):
            block = crossing_ref[face, slot]
            spot = pl.ds(pl.multiple_of(jnp.maximum(block, 0) * STATE, STATE), STATE)
            live = jnp.full((STATE, LANES), block, jnp.int32) >= 0
            tiles.append(jnp.where(live, state_ref[spot], 0.0))
        for slot, tile in enumerate(tiles):
            leaving_ref[pl.ds(i * rows * slots + slot, rows, stride=slots)] = tile[:rows]


def fetched(sems, *pairs):
    copies = [pltpu.make_async_copy(source, target, sems.at[i]) for i, (source, target) in enumerate(pairs)]
    for copy in copies:
        copy.start()
    return copies


def gather_kernel(
    dims, list_in, brick_in, table_ref, grid_in_ref, lines_in_ref, face_ref, from_x_ref, edge_ref,
    state_ref, push_ref, spread_ref, grid_ref, lines_ref, top_ref, list_ref, brick_ref, turned_ref, sems,
):
    copies = fetched(sems, (list_in, list_ref), (brick_in, brick_ref))
    halo_xz_kernel(grid_in_ref, lines_in_ref, face_ref, from_x_ref, edge_ref, grid_ref, lines_ref, top_ref, turned_ref)
    for copy in copies:
        copy.wait()
    base, groups, end = groups_in(list_ref, 0, WIDE)
    loaded, group_of, keep, _, _ = block_steps(dims, list_ref, brick_ref, end)

    @pl.loop(0, groups)
    def _(group):
        taken = [loaded(base + group * WIDE + u, lines_ref, table_ref) for u in range(WIDE)]
        tiles, fresh = group_of(taken)
        keep(state_ref, taken, tiles)
        for i, (push, spread) in enumerate(fresh):
            push_ref[group * WIDE + i] = push
            spread_ref[group * WIDE + i] = spread


def deposit_kernel(
    dims, list_ref, brick_ref, crossing_ref, push_ref, spread_ref, state_ref, deposit_in_ref, deposit_ref, leaving_ref
):
    base, groups, end = groups_in(list_ref, 0, WIDE)
    _, _, _, deposits_of, add = block_steps(dims, list_ref, brick_ref, end)
    leave(crossing_ref, state_ref, leaving_ref, (0, 1, 4, 5))

    @pl.loop(0, groups)
    def _(group):
        mine = [group * WIDE + i for i in range(WIDE)]
        add(deposit_ref, base + group * WIDE, deposits_of([(push_ref[i], spread_ref[i]) for i in mine]))


def late_kernel(
    dims, list_in, brick_in, crossing_in, table_ref, grid_in_ref, lines_in_ref, top_in_ref, first_ref, second_ref,
    state_in_ref, deposit_in_ref,
    grid_ref, lines_ref, state_ref, deposit_ref, leaving_ref,
    push_ref, spread_ref, list_ref, brick_ref, crossing_ref, turned_ref, sems,
):
    copies = fetched(sems, (list_in, list_ref), (brick_in, brick_ref), (crossing_in, crossing_ref))
    halo_y_kernel(
        dims[2] * BY, grid_in_ref, lines_in_ref, top_in_ref, first_ref, second_ref, grid_ref, lines_ref, turned_ref
    )
    for copy in copies:
        copy.wait()
    base, groups, end = groups_in(list_ref, 1)
    loaded, group_of, keep, deposits_of, add = block_steps(dims, list_ref, brick_ref, end)
    push_ref[...] = jnp.zeros_like(push_ref)
    spread_ref[...] = jnp.zeros_like(spread_ref)

    @pl.loop(0, groups + 1)
    def _(group):
        now = base + jnp.maximum(jnp.minimum(group, groups - 1), 0) * UNROLL
        before = base + jnp.maximum(group - 1, 0) * UNROLL
        taken = [loaded(now + u, lines_ref, table_ref) for u in range(UNROLL)]
        shares = deposits_of([(push_ref[i], spread_ref[i]) for i in range(UNROLL)])
        tiles, fresh = group_of(taken)
        add(deposit_ref, before, shares)
        keep(state_ref, taken, tiles)
        for i, (push, spread) in enumerate(fresh):
            push_ref[i] = push
            spread_ref[i] = spread

    leave(crossing_ref, state_ref, leaving_ref, (2, 3))


def top_rows(deposit_ref, q, count_x, count_y, rows_z, size_z):
    total = None
    for p in range(count_x):
        at = (p * count_y + q) * rows_z + size_z
        value = pltpu.roll(deposit_ref[at : at + 8], p, 0) if p else deposit_ref[at : at + 8]
        total = value if total is None else total + value
    return total


def send_y_kernel(push, diffuse, leaving_ref, grid_ref, deposit_ref, y1_ref, y2_ref, tiles_ref, lines_ref):
    comps, size_x, size_y, size_z = grid_ref.shape[0], grid_ref.shape[1] - 2, grid_ref.shape[2] - 8, grid_ref.shape[3]
    count_x, count_y = size_x // BX, size_y // BY
    rows_z = size_z + 8
    rows = (leaving_ref.shape[0] - 8) // 2
    height = comps * SPREAD
    for p in range(count_x):
        at = (p * count_y + count_y - 1) * rows_z
        tiles_ref[p * height : (p + 1) * height] = jnp.transpose(deposit_ref[at : at + size_z])[:height]
    first = jnp.full((rows, LANES), odd("gy")) == 0
    y1_ref[0:rows] = jnp.where(first, leaving_ref[0:rows], leaving_ref[rows : 2 * rows])
    y2_ref[0:rows] = jnp.where(first, leaving_ref[rows : 2 * rows], leaving_ref[0:rows])
    lines_ref[...] = jnp.zeros_like(lines_ref)
    for c in range(comps):
        for p in range(count_x):
            spot = slice(c * ROWS_Y + p * BX, c * ROWS_Y + p * BX + REACH_X)
            line = tiles_ref[pl.ds(p * height + c * SPREAD + BY, REACH_X, stride=REACH_Y)]
            lines_ref[spot] = lines_ref[spot] + line
    wrapped = top_rows(deposit_ref, count_y - 1, count_x, count_y, rows_z, size_z)
    lane = lane_ids(8)
    packed = jnp.zeros((8, LANES), jnp.float32)
    for c in range(comps):
        spot = slice(c * ROWS_Y, (c + 1) * ROWS_Y)
        beside = jnp.concatenate([grid_ref[c, 1 : size_x + 1, size_y - 1], jnp.zeros((8, LANES), jnp.float32)], axis=0)
        line = push * lines_ref[spot] + diffuse * beside
        at = rows + c * (size_x + 1)
        y1_ref[at : at + size_x + 1] = line[: size_x + 1]
        y2_ref[at : at + size_x + 1] = line[: size_x + 1]
        for a in range(REACH_X):
            place = PACK * c + a
            value = turned(wrapped, place - c * SPREAD - a * REACH_Y - BY)
            packed = packed + jnp.where(lane == place, value, 0.0)
    corner = packed[0:1]
    for p in range(1, count_x):
        corner = corner + turned(packed[p : p + 1], p * BX)
    at = rows + comps * (size_x + 1)
    y1_ref[at : at + 1] = push * corner
    y2_ref[at : at + 1] = push * corner


def merge_kernel(deposit_ref, top_tiles_ref, plane_ref, face_ref, tiles_ref, turned_ref):
    comps, planes = plane_ref.shape[:2]
    count_x, size_z = (planes - 1) // BX, plane_ref.shape[3]
    rows_z = size_z + 8
    count_y = deposit_ref.shape[0] // (rows_z * count_x)
    height = comps * SPREAD
    for p in range(count_x):
        for q in range(count_y - 1):
            at = p * count_y + q
            value = jnp.transpose(deposit_ref[at * rows_z : at * rows_z + size_z])
            tiles_ref[at * height : (at + 1) * height] = value[:height]
    top = row_ids(REACH_Y) >= BY
    for c in range(comps):
        for x in range(planes):
            bricks = [(x // BX, x % BX)] if x < planes - 1 else []
            if x and x % BX == 0:
                bricks.append((x // BX - 1, BX))

            def tile(q):
                total = None
                for p, a in bricks:
                    at = c * SPREAD + a * REACH_Y
                    if q < count_y - 1:
                        value = tiles_ref[(p * count_y + q) * height + at : (p * count_y + q) * height + at + REACH_Y]
                    else:
                        value = top_tiles_ref[p * height + at : p * height + at + REACH_Y]
                    total = value if total is None else total + value
                return total

            carried = None
            for q in range(0, count_y, 2):
                here = tile(q)
                if carried is not None:
                    here = here + carried
                between = pltpu.roll(tile(q + 1), BY, 0)
                here = here + jnp.where(top, between, 0.0)
                carried = jnp.where(top, 0.0, between)
                plane_ref[c, x, q * BY : q * BY + REACH_Y] = here
            plane_ref[c, x, count_y * BY :] = carried

    lane = lane_ids(count_x)
    turned_ref[...] = jnp.zeros_like(turned_ref)
    for q in range(count_y):
        wrapped = top_rows(deposit_ref, q, count_x, count_y, rows_z, size_z)[:count_x]
        within = (lane >= q * BY) & (lane <= (q + 1) * BY)
        for c in range(comps):
            for a in range(REACH_X):
                value = turned(wrapped, q * BY - c * SPREAD - a * REACH_Y)
                spot = pl.ds(PACK * c + a, count_x, stride=BX)
                turned_ref[spot] = turned_ref[spot] + jnp.where(within, value, 0.0)
    face_ref[...] = jnp.transpose(turned_ref[...])[: face_ref.shape[0]]


def send_xz_kernel(push, diffuse, grid_ref, deposit_ref, face_ref, x_ref, z_ref):
    comps, size_x = grid_ref.shape[0], grid_ref.shape[1] - 2
    size_y = z_ref.shape[0]
    lane = lane_ids(size_y)
    packed = push * face_ref[0:size_y]
    for c in range(comps):
        for x in range(size_x):
            place = PACK * c + x
            packed = packed + jnp.where(lane == place, diffuse * turned(grid_ref[c, x + 1, 0:size_y], place + 1), 0.0)
        total = push * deposit_ref[c, size_x, 0:size_y]
        x_ref[c * size_y : (c + 1) * size_y] = diffuse * grid_ref[c, size_x, 0:size_y] + total
    z_ref[...] = packed


def base_kernel(push, diffuse, count, grid_ref, deposit_ref, top_ref, y1_ref, y2_ref, state_ref, base_ref, velocity_ref):
    comps, size_x, size_y, size_z = base_ref.shape
    lane, sub = lane_ids(size_y), row_ids(size_y)
    top = top_ref[0:size_y]
    for c in range(comps):
        at = count + c * (size_x + 1)
        lines = below(y1_ref, y2_ref, slice(at, at + size_x))
        for x in range(size_x):
            here = grid_ref[c, x + 1, 0:size_y]
            before = jnp.where(sub == 0, 0.0, pltpu.roll(here, 1, 0))
            laplace = grid_ref[c, x, 0:size_y] + grid_ref[c, x + 2, 0:size_y]
            laplace = laplace + grid_ref[c, x + 1, 1 : size_y + 1] + before
            ahead = jnp.where(lane == size_z - 1, turned(top, size_z - 1 - (PACK * c + x)), turned(here, -1))
            laplace = laplace + ahead + jnp.where(lane == 0, 0.0, turned(here, 1)) - 6.0 * here
            total = here + diffuse * laplace + push * deposit_ref[c, x, 0:size_y]
            line = jnp.broadcast_to(lines[x : x + 1], (size_y, LANES))
            base_ref[c, x] = total + jnp.where(sub == 0, line, 0.0)
        velocity_ref[c] = state_ref[pl.ds(c, velocity_ref.shape[1], stride=STATE)]


def below(first_ref, second_ref, rows):
    got = jnp.where(jnp.full((1, LANES), odd("gy")) == 1, first_ref[rows], second_ref[rows])
    return jnp.where(jnp.full((1, LANES), lax.axis_index("gy")) != 0, got, 0.0)


def relay_kernel(size_x, size_y, comps, count, first_ref, second_ref, x_in_ref, z_in_ref, leaving_ref, x_ref, z1_ref, z2_ref, edge_ref):
    edge = comps * size_y
    x_ref[0:edge] = x_in_ref[...]
    for c in range(comps):
        at = count + c * (size_x + 1) + size_x
        spot = slice(c * size_y, c * size_y + 1)
        x_ref[spot] = x_in_ref[spot] + below(first_ref, second_ref, slice(at, at + 1))
    x_ref[edge : edge + count] = leaving_ref[0:count]
    if x_ref.shape[0] > edge + count:
        x_ref[edge + count : edge + 2 * count] = leaving_ref[count : 2 * count]
    at = count + comps * (size_x + 1)
    edge_ref[size_y:] = jnp.zeros((edge_ref.shape[0] - size_y, LANES), jnp.float32)
    edge_ref[0:size_y] = z_in_ref[...]
    edge_ref[0:1] = z_in_ref[0:1] + below(first_ref, second_ref, slice(at, at + 1))
    first = jnp.full((1, LANES), odd("gz")) == 0
    plus = jnp.concatenate([leaving_ref[2 * count : 3 * count], edge_ref[0:size_y]], axis=0)
    minus = jnp.concatenate([leaving_ref[3 * count : 4 * count], jnp.zeros((size_y, LANES), jnp.float32)], axis=0)
    z1_ref[...] = jnp.where(first, plus, minus)
    z2_ref[0 : count + size_y] = jnp.where(first, minus, plus)
    z2_ref[count + size_y :] = jnp.zeros((z2_ref.shape[0] - count - size_y, LANES), jnp.float32)


def finish_kernel(
    count, base_ref, y1_ref, y2_ref, x_ref, minus_x_ref, z1_ref, z2_ref, edge_ref, gas_out, arrivals_out,
    gas_ref, arrivals_ref, sems,
):
    comps, size_x, size_y, _ = base_ref.shape
    first_lane = lane_ids(size_y) == 0
    odd_y, odd_z = jnp.full((1, LANES), odd("gy")) == 1, jnp.full((1, LANES), odd("gz")) == 1
    place = jnp.full((1, LANES), lax.axis_index("gy"))
    lower, upper = place != 0, place != lax.axis_size("gy") - 1
    rows = slice(count, count + size_y)
    slots = arrivals_ref.shape[2]
    for i in range(arrivals_ref.shape[1]):

        def rows_of(ref, at=0):
            return ref[at + i * slots : at + (i + 1) * slots]

        arrivals_ref[0, i] = rows_of(x_ref, comps * size_y)
        arrivals_ref[1, i] = rows_of(minus_x_ref, minus_x_ref.shape[0] - count)
        y1, y2 = rows_of(y1_ref), rows_of(y2_ref)
        arrivals_ref[2, i] = jnp.where(lower, jnp.where(odd_y, y1, y2), 0.0)
        arrivals_ref[3, i] = jnp.where(upper, jnp.where(odd_y, y2, y1), 0.0)
        z1, z2 = rows_of(z1_ref), rows_of(z2_ref)
        arrivals_ref[4, i] = jnp.where(odd_z, z1, z2)
        arrivals_ref[5, i] = jnp.where(odd_z, z2, z1)
    copies = [pltpu.make_async_copy(arrivals_ref, arrivals_out, sems.at[comps])]
    copies[0].start()
    face = jnp.where(odd_z, z1_ref[rows], z2_ref[rows])
    corner = edge_ref[0:size_y]
    for c in range(comps):
        for x in range(size_x):
            total = base_ref[c, x]
            far = turned(face, -(PACK * c + x))
            if x == 0:
                total = total + x_ref[c * size_y : (c + 1) * size_y]
                far = far + turned(corner, -(PACK * c + size_x))
            gas_ref[c, x] = total + jnp.where(first_lane, far, 0.0)
        copies.append(pltpu.make_async_copy(gas_ref.at[c], gas_out.at[c], sems.at[c]))
        copies[-1].start()
    for copy in copies:
        copy.wait()


def per_device(gas_field, velocity, fraction, response, cell_index, brick_index, crossing):
    comps, size_x, size_y, size_z = gas_field.shape
    nblocks = velocity.shape[0]
    loading = 0.5 * size_x * size_y * size_z / (nblocks * 128)
    push, diffuse = -TIME_STEP * loading, TIME_STEP * VISCOSITY
    velocity = jnp.transpose(velocity, (1, 0, 2))
    fraction = jnp.transpose(fraction, (1, 0, 2))
    spare = nblocks + 8
    rows_z = size_z + 8
    grid_shape = (comps, size_x + 2, ROWS_Y, LANES)
    lines_shape = ((size_x // BX) * (size_y // BY) * comps * rows_z, LANES)
    deposit_shape = ((size_x // BX) * (size_y // BY) * rows_z, LANES)

    inputs = (gas_field, velocity, fraction, response, cell_index, brick_index, crossing)
    inputs = [pltpu.with_memory_space_constraint(array, pltpu.HBM) for array in inputs]
    grid, face, plane, velocity, fraction, response, cell_index, brick_index, crossing = call(
        begin_kernel,
        [grid_shape, (size_y, LANES), (comps * size_y, LANES)]
        + [jax.ShapeDtypeStruct(array.shape, array.dtype) for array in inputs[1:]],
        *inputs, hbm=range(7), scratch=(pltpu.SemaphoreType.DMA((7,)),),
    )
    from_z = moved_along(face, "gz", -1)
    from_x = moved_along(plane, "gx", -1)
    from_xz = moved_diagonally(face, -1)
    lines, deposit, table, ready, blocks = call(
        prepare_kernel,
        [
            lines_shape,
            deposit_shape,
            (TABLE_ROWS * spare, LANES),
            (8, LANES),
            jax.ShapeDtypeStruct((2 * nblocks + 2,), jnp.int32),
        ],
        grid, velocity, fraction, response, cell_index, brick_index,
        smem=(5,), smem_outs=(4,), cycles=3000,
    )
    line_rows = -(-(comps * size_x + comps + 1) // 8) * 8 + 8
    (y_lines,) = call(y_lines_kernel, [(line_rows, LANES)], grid, from_z, from_x, from_xz, ready)
    y1, y2 = swapped_y((y_lines, y_lines))
    square = pltpu.VMEM((LANES, LANES), jnp.float32)
    scalars = (pltpu.SMEM(blocks.shape, jnp.int32), pltpu.SMEM(brick_index.shape, jnp.int32))
    dims = (comps, size_x // BX, size_y // BY, size_z // BZ, rows_z)
    slots = crossing.shape[1]
    count = 7 * slots

    def parts(many):
        return [(many, 2 * comps * REACH_Z, LANES), (many, 2 * LANES, LANES)]

    state, push_parts, spread_parts, grid, lines, top = call(
        functools.partial(gather_kernel, dims),
        [(STATE * spare, LANES)]
        + [jax.ShapeDtypeStruct(shape, jnp.bfloat16) for shape in parts(-(-nblocks // WIDE) * WIDE)]
        + [grid_shape, lines_shape, (LANES, LANES)],
        blocks, brick_index, table, grid, lines, from_z, from_x, from_xz,
        aliases={3: 3, 4: 4}, cycles=4000, scratch=(*scalars, square, pltpu.SemaphoreType.DMA((2,))),
    )
    grid, lines, state, deposit, leaving = call(
        functools.partial(late_kernel, dims),
        [grid_shape, lines_shape, (STATE * spare, LANES), deposit_shape, (2 * count + 8, LANES)],
        blocks, brick_index, crossing, table, grid, lines, top, y1, y2, state, deposit,
        aliases={4: 0, 5: 1, 9: 2, 10: 3}, cycles=2000,
        scratch=[
            *(pltpu.VMEM(shape, jnp.bfloat16) for shape in parts(UNROLL)),
            *scalars,
            pltpu.SMEM(crossing.shape, jnp.int32),
            square,
            pltpu.SemaphoreType.DMA((3,)),
        ],
    )
    height = comps * SPREAD
    to_y1, to_y2, top_tiles = call(
        functools.partial(send_y_kernel, push, diffuse),
        [(count + line_rows, LANES), (count + line_rows, LANES), ((size_x // BX) * height + 8 * REACH_Y, LANES)],
        leaving, grid, deposit, cycles=300, scratch=(pltpu.VMEM((comps * ROWS_Y, LANES), jnp.float32),),
    )
    y1, y2 = swapped_y((to_y1, to_y2))
    deposit, leaving = call(
        functools.partial(deposit_kernel, dims), [deposit_shape, (4 * count + 8, LANES)],
        blocks, brick_index, crossing, push_parts, spread_parts, state, deposit,
        smem=(0, 1, 2), aliases={6: 0}, cycles=4000,
    )
    deposit, over = call(
        merge_kernel, [(comps, size_x + 1, ROWS_Y, LANES), (ROWS_Y, LANES)], deposit, top_tiles,
        cycles=1000, scratch=(pltpu.VMEM(((size_x // BX) * (size_y // BY) * height, LANES), jnp.float32), square),
    )
    to_x, to_z = call(
        functools.partial(send_xz_kernel, push, diffuse), [(comps * size_y, LANES), (size_y, LANES)],
        grid, deposit, over, cycles=500,
    )
    base, velocity_next = call(
        functools.partial(base_kernel, push, diffuse, count), [gas_field.shape, (comps, nblocks, LANES)],
        grid, deposit, top, y1, y2, state, cycles=1000,
    )
    edge = comps * size_y
    both = lax.axis_size("gx") == 2
    to_x, to_z1, to_z2, to_xz = call(
        functools.partial(relay_kernel, size_x, size_y, comps, count),
        [(edge + (2 if both else 1) * count, LANES), *[(count + size_y + 8 * more, LANES) for more in range(3)]],
        y1, y2, to_x, to_z, leaving,
    )
    got_x = moved_along(to_x, "gx", 1)
    z1, z2 = swapped_z((to_z1, to_z2))
    got_xz = moved_diagonally(to_xz, 1)
    got_mx = got_x if both else moved_along(leaving[count : 2 * count], "gx", -1)
    gas_next, arrivals = call(
        functools.partial(finish_kernel, count), [gas_field.shape, (6, 7, slots, LANES)],
        base, y1, y2, got_x, got_mx, z1, z2, got_xz, hbm_outs=(0, 1),
        scratch=(
            pltpu.VMEM(gas_field.shape, jnp.float32),
            pltpu.VMEM((6, 7, slots, LANES), jnp.float32),
            pltpu.SemaphoreType.DMA((comps + 1,)),
        ),
    )
    return gas_next, jnp.transpose(velocity_next, (1, 0, 2)), jnp.transpose(arrivals, (0, 2, 1, 3))


def solution(mesh):
    owner = ("gx", "gz", "gy")
    in_specs = (
        P(None, "gx", "gy", "gz"),
        P(owner, None, None),
        P(owner, None, None),
        P(owner, None),
        P(owner, None),
        P(owner),
        P(owner, None),
    )
    out_specs = (
        P(None, "gx", "gy", "gz"),
        P(owner, None, None),
        P(owner, None, None, None),
    )
    return jax.shard_map(
        per_device, mesh=mesh, in_specs=in_specs, out_specs=out_specs, check_vma=False
    )
```

```python
import functools

import jax
import jax.numpy as jnp
from jax import lax
from jax.experimental import pallas as pl
from jax.experimental.pallas import tpu as pltpu
from jax.sharding import PartitionSpec as P

BX = 4
BY = 4
BZ = 8

TIME_STEP = 0.25
VISCOSITY = 0.4

LANES = 128
PACK = 32
ROWS_Y = 24
REACH_X = BX + 1
REACH_Y = 8
SPREAD = REACH_X * REACH_Y
REACH_Z = 2 * BZ
UNROLL = 8
WIDE = 16

WEIGHT, ALONG_Y, IN_Y, ALONG_Z, IN_Z, RESPONSE, MOVING, OFFSET = 0, 5, 6, 7, 8, 9, 10, 13
TABLE_ROWS = 16
STATE = 8

VMEM = pl.BlockSpec(memory_space=pltpu.VMEM)
SMEM = pl.BlockSpec(memory_space=pltpu.SMEM)
HBM = pl.BlockSpec(memory_space=pltpu.HBM)


def moved_along(block, axis, distance):
    count = lax.axis_size(axis)
    return lax.ppermute(block, axis, [(i, (i + distance) % count) for i in range(count)])


def swapped_z(blocks):
    count = lax.axis_size("gz")
    first = [(i, i ^ 1) for i in range(count)]
    second = [(i, (((i + 1) ^ 1) - 1) % count) for i in range(count)]
    return lax.ppermute(blocks[0], "gz", first), lax.ppermute(blocks[1], "gz", second)


def swapped_y(blocks):
    nz, ny = lax.axis_size("gz"), lax.axis_size("gy")
    first = [(j, j ^ 1) for j in range(ny)]
    second = []
    for k in range(nz):
        second.append((k * ny, (k ^ 1) * ny))
        second.append((k * ny + ny - 1, (k ^ 1) * ny + ny - 1))
        second.extend((k * ny + j, k * ny + ((j + 1) ^ 1) - 1) for j in range(1, ny - 1))
    middle = lax.ppermute(blocks[1], ("gz", "gy"), second)
    return lax.ppermute(blocks[0], "gy", first), middle


def moved_diagonally(block, distance):
    nx, nz = lax.axis_size("gx"), lax.axis_size("gz")
    route = [(i * nz + k, (i + distance) % nx * nz + (k + distance) % nz) for i in range(nx) for k in range(nz)]
    return lax.ppermute(block, ("gx", "gz"), route)


def call(
    body, outs, *operands, smem=(), hbm=(), smem_outs=(), hbm_outs=(), scratch=(), aliases=None, cycles=0, limit=40
):
    return pl.pallas_call(
        body,
        out_shape=[o if isinstance(o, jax.ShapeDtypeStruct) else jax.ShapeDtypeStruct(o, jnp.float32) for o in outs],
        in_specs=[SMEM if i in smem else HBM if i in hbm else VMEM for i in range(len(operands))],
        out_specs=[SMEM if i in smem_outs else HBM if i in hbm_outs else VMEM for i in range(len(outs))],
        scratch_shapes=list(scratch),
        input_output_aliases=aliases or {},
        compiler_params=pltpu.CompilerParams(vmem_limit_bytes=limit * 1024 * 1024),
        cost_estimate=pl.CostEstimate(flops=cycles * 4096, bytes_accessed=cycles * 1024, transcendentals=0),
    )(*operands)


def lane_ids(rows):
    return lax.broadcasted_iota(jnp.int32, (rows, LANES), 1)


def row_ids(rows):
    return lax.broadcasted_iota(jnp.int32, (rows, LANES), 0)


def turned(value, shift):
    shift = shift % LANES
    return pltpu.roll(value, shift, 1) if shift else value


def odd(axis):
    return lax.axis_index(axis) % 2


def begin_kernel(
    gas_ref, velocity_in, fraction_in, response_in, cell_in, brick_in, crossing_in,
    grid_ref, face_ref, plane_ref, velocity_ref, fraction_ref, response_ref, cell_ref, brick_ref, crossing_ref, sems,
):
    comps, size_x, size_y, _ = gas_ref.shape
    pairs = [
        (gas_ref, grid_ref.at[:, 1 : size_x + 1, 0:size_y]),
        (velocity_in, velocity_ref), (fraction_in, fraction_ref), (response_in, response_ref),
        (cell_in, cell_ref), (brick_in, brick_ref), (crossing_in, crossing_ref),
    ]
    copies = [pltpu.make_async_copy(source, target, sems.at[i]) for i, (source, target) in enumerate(pairs)]
    for copy in copies:
        copy.start()
    zeros = jnp.zeros((ROWS_Y, LANES), jnp.float32)
    for c in range(comps):
        grid_ref[c, 0] = zeros
        grid_ref[c, size_x + 1] = zeros
        for x in range(size_x):
            grid_ref[c, x + 1, size_y:] = zeros[size_y:]
    copies[0].wait()
    lane = lane_ids(size_y)
    face = jnp.zeros((size_y, LANES), jnp.float32)
    for c in range(comps):
        plane_ref[c * size_y : (c + 1) * size_y] = grid_ref[c, 1, 0:size_y]
        for x in range(size_x):
            place = PACK * c + x
            face = jnp.where(lane == place, turned(grid_ref[c, x + 1, 0:size_y], place), face)
    face_ref[...] = face
    for copy in copies[1:]:
        copy.wait()


def parts_of(value):
    main = value.astype(jnp.bfloat16).astype(jnp.float32)
    return main, value - main


def lay_out(grid_ref, lines_ref, p, q, size_y, size_z):
    comps = grid_ref.shape[0]
    rows_z = size_z + 8
    count_y = size_y // BY
    for c in range(comps):
        planes = [grid_ref[c, p * BX + a + 1, q * BY : q * BY + REACH_Y] for a in range(REACH_X)]
        main, rest = parts_of(jnp.concatenate(planes, axis=0))
        stack = jnp.concatenate([main, rest, main, jnp.zeros((LANES - 3 * SPREAD, LANES), jnp.float32)], axis=0)
        at = ((p * count_y + q) * comps + c) * rows_z
        lines_ref[at : at + size_z] = jnp.transpose(stack)


def lay_out_top(turned_ref, lines_ref, q, comps, count_x, count_y, size_z):
    lane = lane_ids(count_x)
    rows_z = size_z + 8
    for c in range(comps):
        total = jnp.zeros((count_x, LANES), jnp.float32)
        for a in range(REACH_X):
            rows = turned_ref[pl.ds(PACK * c + a, count_x, stride=BX)]
            total = jnp.where(lane // REACH_Y == a, turned(rows, a * REACH_Y - q * BY), total)
        main, rest = parts_of(total)
        line = main + turned(rest, SPREAD) + turned(main, 2 * SPREAD)
        for p in range(count_x):
            at = ((p * count_y + q) * comps + c) * rows_z + size_z
            lines_ref[at : at + 1] = line[p : p + 1]


def prepare_kernel(
    grid_ref, velocity_ref, fraction_ref, response_ref, cell_ref, brick_ref,
    lines_ref, deposit_ref, table_ref, ready_ref, list_ref,
):
    comps, size_x, size_y, size_z = grid_ref.shape[0], grid_ref.shape[1] - 2, grid_ref.shape[2] - 8, grid_ref.shape[3]
    nblocks = velocity_ref.shape[1]
    count_x, count_y, count_z = size_x // BX, size_y // BY, size_z // BZ
    rows_z = size_z + 8


    def visit(k, counts):
        late = jnp.where(lax.rem(lax.div(brick_ref[k], count_z), count_y) == count_y - 1, 1, 0)
        list_ref[jnp.where(late == 1, nblocks + counts[1], counts[0])] = k
        return counts[0] + 1 - late, counts[1] + late

    early, late = lax.fori_loop(0, nblocks, visit, (jnp.int32(0), jnp.int32(0)), unroll=8)
    list_ref[2 * nblocks] = early
    list_ref[2 * nblocks + 1] = late
    ready_ref[...] = jnp.zeros_like(ready_ref)

    deposit_ref[...] = jnp.zeros_like(deposit_ref)
    for p in range(count_x):
        for q in range(count_y):
            for c in range(comps):
                at = ((p * count_y + q) * comps + c) * rows_z + size_z
                lines_ref[at : at + 8] = jnp.zeros((8, LANES), jnp.float32)
    for p in range(count_x - 1):
        for q in range(count_y - 1):
            lay_out(grid_ref, lines_ref, p, q, size_y, size_z)

    cells = cell_ref[...]
    cell_x, cell_y, cell_z = cells // (BY * BZ), cells // BZ % BY, cells % BZ
    along_x = fraction_ref[0]

    def put(row, value):
        table_ref[pl.ds(row, nblocks, stride=TABLE_ROWS)] = value

    for a in range(REACH_X):
        put(WEIGHT + a, jnp.where(cell_x == a, 1.0 - along_x, 0.0) + jnp.where(cell_x == a - 1, along_x, 0.0))
    put(ALONG_Y, fraction_ref[1])
    put(IN_Y, cell_y.astype(jnp.float32))
    put(ALONG_Z, fraction_ref[2])
    put(IN_Z, cell_z.astype(jnp.float32))
    put(RESPONSE, response_ref[...])
    for c in range(comps):
        put(MOVING + c, velocity_ref[c])
        put(OFFSET + c, fraction_ref[c])
    spare = table_ref.shape[0] - nblocks * TABLE_ROWS
    row = row_ids(spare)
    table_ref[nblocks * TABLE_ROWS :] = jnp.where(row % TABLE_ROWS == RESPONSE, 1.0, 0.0)


def y_lines_kernel(grid_ref, face_ref, from_x_ref, edge_ref, ready_ref, out_ref):
    comps, size_x = grid_ref.shape[0], grid_ref.shape[1] - 2
    size_y = face_ref.shape[0]
    for c in range(comps):
        out_ref[c * size_x : (c + 1) * size_x] = grid_ref[c, 1 : size_x + 1, 0]
        out_ref[comps * size_x + c : comps * size_x + c + 1] = from_x_ref[c * size_y : c * size_y + 1]
    line = jnp.where(lane_ids(8) % PACK == size_x, turned(edge_ref[0:8], size_x), face_ref[0:8])
    out_ref[comps * size_x + comps : comps * size_x + comps + 1] = line[0:1]


def halo_xz_kernel(grid_in_ref, lines_in_ref, face_ref, from_x_ref, edge_ref, grid_ref, lines_ref, top_ref, turned_ref):
    comps, size_x = grid_ref.shape[0], grid_ref.shape[1] - 2
    size_y, size_z = face_ref.shape[0], grid_ref.shape[3]
    count_x, count_y = size_x // BX, size_y // BY
    for c in range(comps):
        grid_ref[c, size_x + 1, 0:size_y] = from_x_ref[c * size_y : (c + 1) * size_y]
    for q in range(count_y - 1):
        lay_out(grid_ref, lines_ref, count_x - 1, q, size_y, size_z)
    top = jnp.where(lane_ids(size_y) % PACK == size_x, turned(edge_ref[...], size_x), face_ref[...])
    top_ref[0:size_y] = top
    top_ref[size_y:] = jnp.zeros((LANES - size_y, LANES), jnp.float32)
    turned_ref[...] = jnp.transpose(top_ref[...])
    for q in range(count_y - 1):
        lay_out_top(turned_ref, lines_ref, q, comps, count_x, count_y, size_z)


def halo_y_kernel(size_y, grid_in_ref, lines_in_ref, top_in_ref, first_ref, second_ref, grid_ref, lines_ref, turned_ref):
    comps, size_x, size_z = grid_ref.shape[0], grid_ref.shape[1] - 2, grid_ref.shape[3]
    count_x, count_y = size_x // BX, size_y // BY
    inside = lax.axis_index("gy") != lax.axis_size("gy") - 1
    kept = (row_ids(8) == 0) & inside
    even = jnp.full((1, LANES), odd("gy")) == 0

    def line_at(row):
        line = jnp.where(even, first_ref[row : row + 1], second_ref[row : row + 1])
        return jnp.where(kept, jnp.broadcast_to(line, (8, LANES)), 0.0)

    for c in range(comps):
        for x in range(size_x + 1):
            grid_ref[c, x + 1, size_y:] = line_at(c * size_x + x if x < size_x else comps * size_x + c)
    for p in range(count_x):
        lay_out(grid_ref, lines_ref, p, count_y - 1, size_y, size_z)
    corner = line_at(comps * size_x + comps)
    rest = jnp.zeros((LANES - size_y - 8, LANES), jnp.float32)
    turned_ref[...] = jnp.transpose(jnp.concatenate([top_in_ref[0:size_y], corner, rest], axis=0))
    lay_out_top(turned_ref, lines_ref, count_y - 1, comps, count_x, count_y, size_z)


def block_steps(dims, list_ref, brick_ref, end):
    comps, _, count_y, count_z, rows_z = dims
    nblocks = brick_ref.shape[0]
    sub = row_ids(8)
    row_y = row_ids(REACH_Y).astype(jnp.float32)
    row_z = row_ids(REACH_Z).astype(jnp.float32)
    lanes = lane_ids(REACH_Z)

    def hat(rows, inside, along):
        return jnp.where(rows == inside, 1.0 - along, 0.0) + jnp.where(rows == inside + 1.0, along, 0.0)

    def place_of(at):
        k = jnp.where(at < end, list_ref[jnp.minimum(at, 2 * nblocks + 1)], nblocks)
        brick = jnp.where(k < nblocks, brick_ref[jnp.minimum(k, nblocks - 1)], 0)
        brick_x = lax.div(brick, count_y * count_z)
        brick_y = lax.rem(lax.div(brick, count_z), count_y)
        return k, brick_x * count_y + brick_y, lax.rem(brick, count_z)

    def loaded(at, lines_ref, table_ref):
        k, pair, brick_z = place_of(at)
        first = pl.multiple_of(pair * comps * rows_z + brick_z * BZ, 8)
        window = jnp.concatenate([lines_ref[pl.ds(first + c * rows_z, REACH_Z)] for c in range(comps)], axis=0)
        table = table_ref[pl.ds(pl.multiple_of(k * TABLE_ROWS, TABLE_ROWS), TABLE_ROWS)]
        return k, window, [table[i : i + 1] for i in range(TABLE_ROWS)]

    def weighted(rows):
        weight_y = hat(row_y, rows[IN_Y], rows[ALONG_Y])
        weight_z = hat(row_z, rows[IN_Z], rows[ALONG_Z])
        weight = jnp.concatenate([rows[WEIGHT + a] * weight_y for a in range(REACH_X)], axis=0)
        return weight_z, *parts_of(weight)

    def stepped(seen, weight_z, rows):
        rate = 1.0 / rows[RESPONSE]
        state, moved, pushed = [], [], []
        for c in range(comps):
            gas_sample = jnp.sum(seen[c * REACH_Z : (c + 1) * REACH_Z] * weight_z, axis=0, keepdims=True)
            drag = (gas_sample - rows[MOVING + c]) * rate
            state.append(rows[MOVING + c] + TIME_STEP * drag)
            moved.append(rows[OFFSET + c] + TIME_STEP * state[c])
            pushed.append(drag * weight_z)
        tile = jnp.broadcast_to(rows[RESPONSE], (STATE, LANES))
        for i, value in enumerate(state + moved):
            tile = jnp.where(sub == i, value, tile)
        return tile, jnp.concatenate(parts_of(jnp.concatenate(pushed, axis=0)), axis=0)

    def gathered(one, two):
        tables, windows, weights = [], [], []
        for _, window, rows in (one, two):
            weight_z, main, rest = weighted(rows)
            weights.append((weight_z, main, rest))
            unused = jnp.zeros((LANES - 3 * SPREAD, LANES), jnp.float32)
            tables.append(jnp.concatenate([main, main, rest, unused], axis=0).astype(jnp.bfloat16))
            windows.append(window)
        seen = lax.dot_general(
            jnp.concatenate(windows, axis=0).astype(jnp.bfloat16), jnp.concatenate(tables, axis=1),
            (((1,), (0,)), ((), ())), preferred_element_type=jnp.float32,
        )
        height = comps * REACH_Z
        tiles, fresh = [], []
        for i, (_, _, rows) in enumerate((one, two)):
            weight_z, main, rest = weights[i]
            mine = seen[i * height : (i + 1) * height, i * LANES : (i + 1) * LANES]
            tile, push = stepped(mine, weight_z, rows)
            tiles.append(tile)
            unused = jnp.zeros((LANES - comps * SPREAD, LANES), jnp.float32)
            spread = jnp.concatenate([main] * comps + [unused] + [rest] * comps + [unused], axis=0)
            fresh.append((push.astype(jnp.bfloat16), spread.astype(jnp.bfloat16)))
        return tiles, fresh

    def shared(push, spread):
        shares = lax.dot_general(push, spread, (((1,), (1,)), ((), ())), preferred_element_type=jnp.float32)
        height = comps * REACH_Z
        total = shares[:height, :LANES] + shares[:height, LANES:] + shares[height:, :LANES]
        result = jnp.zeros((REACH_Z, LANES), jnp.float32)
        for c in range(comps):
            inside = (lanes >= c * SPREAD) & (lanes < (c + 1) * SPREAD)
            result = jnp.where(inside, total[c * REACH_Z : (c + 1) * REACH_Z], result)
        return result

    def add(deposit_ref, at, shares):
        spots = []
        for u in range(len(shares)):
            _, pair, brick_z = place_of(at + u)
            spots.append(pl.ds(pl.multiple_of(pair * rows_z + brick_z * BZ, 8), REACH_Z))
        for spot, share in zip(spots, shares):
            deposit_ref[spot] = deposit_ref[spot] + share

    def group_of(taken):
        tiles, fresh = [], []
        for u in range(0, len(taken), 2):
            both, kept = gathered(taken[u], taken[u + 1])
            tiles.extend(both)
            fresh.extend(kept)
        return tiles, fresh

    def keep(state_ref, taken, tiles):
        for (k, _, _), tile in zip(taken, tiles):
            state_ref[pl.ds(pl.multiple_of(STATE * k, STATE), STATE)] = tile

    def deposits_of(kept):
        return [shared(push, spread) for push, spread in kept]

    return loaded, group_of, keep, deposits_of, add


def groups_in(list_ref, late, many=UNROLL):
    room = (list_ref.shape[0] - 2) // 2
    count = list_ref[2 * room + late]
    return late * room, (count + many - 1) // many, late * room + count


def leave(crossing_ref, state_ref, leaving_ref, faces):
    slots = crossing_ref.shape[1]
    rows = (leaving_ref.shape[0] - 8) // (len(faces) * slots)
    for i, face in enumerate(faces):
        tiles = []
        for slot in range(slots):
            block = crossing_ref[face, slot]
            spot = pl.ds(pl.multiple_of(jnp.maximum(block, 0) * STATE, STATE), STATE)
            live = jnp.full((STATE, LANES), block, jnp.int32) >= 0
            tiles.append(jnp.where(live, state_ref[spot], 0.0))
        for slot, tile in enumerate(tiles):
            leaving_ref[pl.ds(i * rows * slots + slot, rows, stride=slots)] = tile[:rows]


def fetched(sems, *pairs):
    copies = [pltpu.make_async_copy(source, target, sems.at[i]) for i, (source, target) in enumerate(pairs)]
    for copy in copies:
        copy.start()
    return copies


def gather_kernel(
    dims, list_in, brick_in, table_ref, grid_in_ref, lines_in_ref, face_ref, from_x_ref, edge_ref,
    state_ref, push_ref, spread_ref, grid_ref, lines_ref, top_ref, list_ref, brick_ref, turned_ref, sems,
):
    copies = fetched(sems, (list_in, list_ref), (brick_in, brick_ref))
    halo_xz_kernel(grid_in_ref, lines_in_ref, face_ref, from_x_ref, edge_ref, grid_ref, lines_ref, top_ref, turned_ref)
    for copy in copies:
        copy.wait()
    base, groups, end = groups_in(list_ref, 0, WIDE)
    loaded, group_of, keep, _, _ = block_steps(dims, list_ref, brick_ref, end)

    @pl.loop(0, groups)
    def _(group):
        taken = [loaded(base + group * WIDE + u, lines_ref, table_ref) for u in range(WIDE)]
        tiles, fresh = group_of(taken)
        keep(state_ref, taken, tiles)
        for i, (push, spread) in enumerate(fresh):
            push_ref[group * WIDE + i] = push
            spread_ref[group * WIDE + i] = spread


def deposit_kernel(
    dims, push, diffuse, list_ref, brick_ref, crossing_ref, push_ref, spread_ref, state_ref, deposit_in_ref, top_tiles_ref,
    grid_ref, deposit_ref, leaving_ref, plane_ref, x_ref, z_ref, face_ref, tiles_ref, turned_ref,
):
    base, groups, end = groups_in(list_ref, 0, WIDE)
    _, _, _, deposits_of, add = block_steps(dims, list_ref, brick_ref, end)
    leave(crossing_ref, state_ref, leaving_ref, (0, 1, 4, 5))

    @pl.loop(0, groups)
    def _(group):
        mine = [group * WIDE + i for i in range(WIDE)]
        add(deposit_ref, base + group * WIDE, deposits_of([(push_ref[i], spread_ref[i]) for i in mine]))

    merge(deposit_ref, top_tiles_ref, plane_ref, face_ref, tiles_ref, turned_ref)
    send_xz(push, diffuse, grid_ref, plane_ref, face_ref, x_ref, z_ref)


def late_kernel(
    dims, push, diffuse, list_in, brick_in, crossing_in, table_ref, grid_in_ref, lines_in_ref, top_in_ref,
    first_ref, second_ref,
    state_in_ref, deposit_in_ref,
    grid_ref, lines_ref, state_ref, deposit_ref, y1_ref, y2_ref, tiles_ref,
    push_ref, spread_ref, list_ref, brick_ref, crossing_ref, turned_ref, leaving_ref, y_lines_ref, sems,
):
    copies = fetched(sems, (list_in, list_ref), (brick_in, brick_ref), (crossing_in, crossing_ref))
    halo_y_kernel(
        dims[2] * BY, grid_in_ref, lines_in_ref, top_in_ref, first_ref, second_ref, grid_ref, lines_ref, turned_ref
    )
    for copy in copies:
        copy.wait()
    base, groups, end = groups_in(list_ref, 1)
    loaded, group_of, keep, deposits_of, add = block_steps(dims, list_ref, brick_ref, end)
    push_ref[...] = jnp.zeros_like(push_ref)
    spread_ref[...] = jnp.zeros_like(spread_ref)

    @pl.loop(0, groups + 1)
    def _(group):
        now = base + jnp.maximum(jnp.minimum(group, groups - 1), 0) * UNROLL
        before = base + jnp.maximum(group - 1, 0) * UNROLL
        taken = [loaded(now + u, lines_ref, table_ref) for u in range(UNROLL)]
        shares = deposits_of([(push_ref[i], spread_ref[i]) for i in range(UNROLL)])
        tiles, fresh = group_of(taken)
        add(deposit_ref, before, shares)
        keep(state_ref, taken, tiles)
        for i, (kept, spread) in enumerate(fresh):
            push_ref[i] = kept
            spread_ref[i] = spread

    leave(crossing_ref, state_ref, leaving_ref, (2, 3))
    send_y(push, diffuse, leaving_ref, grid_ref, deposit_ref, y1_ref, y2_ref, tiles_ref, y_lines_ref)


def top_rows(deposit_ref, q, count_x, count_y, rows_z, size_z):
    total = None
    for p in range(count_x):
        at = (p * count_y + q) * rows_z + size_z
        value = pltpu.roll(deposit_ref[at : at + 8], p, 0) if p else deposit_ref[at : at + 8]
        total = value if total is None else total + value
    return total


def send_y(push, diffuse, leaving_ref, grid_ref, deposit_ref, y1_ref, y2_ref, tiles_ref, lines_ref):
    comps, size_x, size_y, size_z = grid_ref.shape[0], grid_ref.shape[1] - 2, grid_ref.shape[2] - 8, grid_ref.shape[3]
    count_x, count_y = size_x // BX, size_y // BY
    rows_z = size_z + 8
    rows = (leaving_ref.shape[0] - 8) // 2
    height = comps * SPREAD
    for p in range(count_x):
        at = (p * count_y + count_y - 1) * rows_z
        tiles_ref[p * height : (p + 1) * height] = jnp.transpose(deposit_ref[at : at + size_z])[:height]
    first = jnp.full((rows, LANES), odd("gy")) == 0
    y1_ref[0:rows] = jnp.where(first, leaving_ref[0:rows], leaving_ref[rows : 2 * rows])
    y2_ref[0:rows] = jnp.where(first, leaving_ref[rows : 2 * rows], leaving_ref[0:rows])
    lines_ref[...] = jnp.zeros_like(lines_ref)
    for c in range(comps):
        for p in range(count_x):
            spot = slice(c * ROWS_Y + p * BX, c * ROWS_Y + p * BX + REACH_X)
            line = tiles_ref[pl.ds(p * height + c * SPREAD + BY, REACH_X, stride=REACH_Y)]
            lines_ref[spot] = lines_ref[spot] + line
    wrapped = top_rows(deposit_ref, count_y - 1, count_x, count_y, rows_z, size_z)
    lane = lane_ids(8)
    packed = jnp.zeros((8, LANES), jnp.float32)
    for c in range(comps):
        spot = slice(c * ROWS_Y, (c + 1) * ROWS_Y)
        beside = jnp.concatenate([grid_ref[c, 1 : size_x + 1, size_y - 1], jnp.zeros((8, LANES), jnp.float32)], axis=0)
        line = push * lines_ref[spot] + diffuse * beside
        at = rows + c * (size_x + 1)
        y1_ref[at : at + size_x + 1] = line[: size_x + 1]
        y2_ref[at : at + size_x + 1] = line[: size_x + 1]
        for a in range(REACH_X):
            place = PACK * c + a
            value = turned(wrapped, place - c * SPREAD - a * REACH_Y - BY)
            packed = packed + jnp.where(lane == place, value, 0.0)
    corner = packed[0:1]
    for p in range(1, count_x):
        corner = corner + turned(packed[p : p + 1], p * BX)
    at = rows + comps * (size_x + 1)
    y1_ref[at : at + 1] = push * corner
    y2_ref[at : at + 1] = push * corner


def merge(deposit_ref, top_tiles_ref, plane_ref, face_ref, tiles_ref, turned_ref):
    comps, planes = plane_ref.shape[:2]
    count_x, size_z = (planes - 1) // BX, plane_ref.shape[3]
    rows_z = size_z + 8
    count_y = deposit_ref.shape[0] // (rows_z * count_x)
    height = comps * SPREAD
    for p in range(count_x):
        for q in range(count_y - 1):
            at = p * count_y + q
            value = jnp.transpose(deposit_ref[at * rows_z : at * rows_z + size_z])
            tiles_ref[at * height : (at + 1) * height] = value[:height]
    top = row_ids(REACH_Y) >= BY
    for c in range(comps):
        for x in range(planes):
            bricks = [(x // BX, x % BX)] if x < planes - 1 else []
            if x and x % BX == 0:
                bricks.append((x // BX - 1, BX))

            def tile(q):
                total = None
                for p, a in bricks:
                    at = c * SPREAD + a * REACH_Y
                    if q < count_y - 1:
                        value = tiles_ref[(p * count_y + q) * height + at : (p * count_y + q) * height + at + REACH_Y]
                    else:
                        value = top_tiles_ref[p * height + at : p * height + at + REACH_Y]
                    total = value if total is None else total + value
                return total

            carried = None
            for q in range(0, count_y, 2):
                here = tile(q)
                if carried is not None:
                    here = here + carried
                between = pltpu.roll(tile(q + 1), BY, 0)
                here = here + jnp.where(top, between, 0.0)
                carried = jnp.where(top, 0.0, between)
                plane_ref[c, x, q * BY : q * BY + REACH_Y] = here
            plane_ref[c, x, count_y * BY :] = carried

    lane = lane_ids(count_x)
    turned_ref[...] = jnp.zeros_like(turned_ref)
    for q in range(count_y):
        wrapped = top_rows(deposit_ref, q, count_x, count_y, rows_z, size_z)[:count_x]
        within = (lane >= q * BY) & (lane <= (q + 1) * BY)
        for c in range(comps):
            for a in range(REACH_X):
                value = turned(wrapped, q * BY - c * SPREAD - a * REACH_Y)
                spot = pl.ds(PACK * c + a, count_x, stride=BX)
                turned_ref[spot] = turned_ref[spot] + jnp.where(within, value, 0.0)
    face_ref[...] = jnp.transpose(turned_ref[...])[: face_ref.shape[0]]


def send_xz(push, diffuse, grid_ref, deposit_ref, face_ref, x_ref, z_ref):
    comps, size_x = grid_ref.shape[0], grid_ref.shape[1] - 2
    size_y = z_ref.shape[0]
    lane = lane_ids(size_y)
    packed = push * face_ref[0:size_y]
    for c in range(comps):
        for x in range(size_x):
            place = PACK * c + x
            packed = packed + jnp.where(lane == place, diffuse * turned(grid_ref[c, x + 1, 0:size_y], place + 1), 0.0)
        total = push * deposit_ref[c, size_x, 0:size_y]
        x_ref[c * size_y : (c + 1) * size_y] = diffuse * grid_ref[c, size_x, 0:size_y] + total
    z_ref[...] = packed


def base_kernel(push, diffuse, count, grid_ref, deposit_ref, top_ref, y1_ref, y2_ref, state_ref, base_ref, velocity_ref):
    comps, size_x, size_y, size_z = base_ref.shape
    lane, sub = lane_ids(size_y), row_ids(size_y)
    top = top_ref[0:size_y]
    for c in range(comps):
        at = count + c * (size_x + 1)
        lines = below(y1_ref, y2_ref, slice(at, at + size_x))
        for x in range(size_x):
            here = grid_ref[c, x + 1, 0:size_y]
            before = jnp.where(sub == 0, 0.0, pltpu.roll(here, 1, 0))
            laplace = grid_ref[c, x, 0:size_y] + grid_ref[c, x + 2, 0:size_y]
            laplace = laplace + grid_ref[c, x + 1, 1 : size_y + 1] + before
            ahead = jnp.where(lane == size_z - 1, turned(top, size_z - 1 - (PACK * c + x)), turned(here, -1))
            laplace = laplace + ahead + jnp.where(lane == 0, 0.0, turned(here, 1)) - 6.0 * here
            total = here + diffuse * laplace + push * deposit_ref[c, x, 0:size_y]
            line = jnp.broadcast_to(lines[x : x + 1], (size_y, LANES))
            base_ref[c, x] = total + jnp.where(sub == 0, line, 0.0)
        velocity_ref[c] = state_ref[pl.ds(c, velocity_ref.shape[1], stride=STATE)]


def below(first_ref, second_ref, rows):
    got = jnp.where(jnp.full((1, LANES), odd("gy")) == 1, first_ref[rows], second_ref[rows])
    return jnp.where(jnp.full((1, LANES), lax.axis_index("gy")) != 0, got, 0.0)


def relay_kernel(size_x, size_y, comps, count, first_ref, second_ref, x_in_ref, z_in_ref, leaving_ref, x_ref, z1_ref, z2_ref, edge_ref):
    edge = comps * size_y
    x_ref[0:edge] = x_in_ref[...]
    for c in range(comps):
        at = count + c * (size_x + 1) + size_x
        spot = slice(c * size_y, c * size_y + 1)
        x_ref[spot] = x_in_ref[spot] + below(first_ref, second_ref, slice(at, at + 1))
    x_ref[edge : edge + count] = leaving_ref[0:count]
    if x_ref.shape[0] > edge + count:
        x_ref[edge + count : edge + 2 * count] = leaving_ref[count : 2 * count]
    at = count + comps * (size_x + 1)
    edge_ref[size_y:] = jnp.zeros((edge_ref.shape[0] - size_y, LANES), jnp.float32)
    edge_ref[0:size_y] = z_in_ref[...]
    edge_ref[0:1] = z_in_ref[0:1] + below(first_ref, second_ref, slice(at, at + 1))
    first = jnp.full((1, LANES), odd("gz")) == 0
    plus = jnp.concatenate([leaving_ref[2 * count : 3 * count], edge_ref[0:size_y]], axis=0)
    minus = jnp.concatenate([leaving_ref[3 * count : 4 * count], jnp.zeros((size_y, LANES), jnp.float32)], axis=0)
    z1_ref[...] = jnp.where(first, plus, minus)
    z2_ref[0 : count + size_y] = jnp.where(first, minus, plus)
    z2_ref[count + size_y :] = jnp.zeros((z2_ref.shape[0] - count - size_y, LANES), jnp.float32)


def finish_kernel(
    count, base_ref, y1_ref, y2_ref, x_ref, minus_x_ref, z1_ref, z2_ref, edge_ref, gas_out, arrivals_out,
    gas_ref, arrivals_ref, sems,
):
    comps, size_x, size_y, _ = base_ref.shape
    first_lane = lane_ids(size_y) == 0
    odd_y, odd_z = jnp.full((1, LANES), odd("gy")) == 1, jnp.full((1, LANES), odd("gz")) == 1
    place = jnp.full((1, LANES), lax.axis_index("gy"))
    lower, upper = place != 0, place != lax.axis_size("gy") - 1
    rows = slice(count, count + size_y)
    slots = arrivals_ref.shape[2]
    for i in range(arrivals_ref.shape[1]):

        def rows_of(ref, at=0):
            return ref[at + i * slots : at + (i + 1) * slots]

        arrivals_ref[0, i] = rows_of(x_ref, comps * size_y)
        arrivals_ref[1, i] = rows_of(minus_x_ref, minus_x_ref.shape[0] - count)
        y1, y2 = rows_of(y1_ref), rows_of(y2_ref)
        arrivals_ref[2, i] = jnp.where(lower, jnp.where(odd_y, y1, y2), 0.0)
        arrivals_ref[3, i] = jnp.where(upper, jnp.where(odd_y, y2, y1), 0.0)
        z1, z2 = rows_of(z1_ref), rows_of(z2_ref)
        arrivals_ref[4, i] = jnp.where(odd_z, z1, z2)
        arrivals_ref[5, i] = jnp.where(odd_z, z2, z1)
    copies = [pltpu.make_async_copy(arrivals_ref, arrivals_out, sems.at[comps])]
    copies[0].start()
    face = jnp.where(odd_z, z1_ref[rows], z2_ref[rows])
    corner = edge_ref[0:size_y]
    for c in range(comps):
        for x in range(size_x):
            total = base_ref[c, x]
            far = turned(face, -(PACK * c + x))
            if x == 0:
                total = total + x_ref[c * size_y : (c + 1) * size_y]
                far = far + turned(corner, -(PACK * c + size_x))
            gas_ref[c, x] = total + jnp.where(first_lane, far, 0.0)
        copies.append(pltpu.make_async_copy(gas_ref.at[c], gas_out.at[c], sems.at[c]))
        copies[-1].start()
    for copy in copies:
        copy.wait()


def per_device(gas_field, velocity, fraction, response, cell_index, brick_index, crossing):
    comps, size_x, size_y, size_z = gas_field.shape
    nblocks = velocity.shape[0]
    loading = 0.5 * size_x * size_y * size_z / (nblocks * 128)
    push, diffuse = -TIME_STEP * loading, TIME_STEP * VISCOSITY
    velocity = jnp.transpose(velocity, (1, 0, 2))
    fraction = jnp.transpose(fraction, (1, 0, 2))
    spare = nblocks + 8
    rows_z = size_z + 8
    grid_shape = (comps, size_x + 2, ROWS_Y, LANES)
    lines_shape = ((size_x // BX) * (size_y // BY) * comps * rows_z, LANES)
    deposit_shape = ((size_x // BX) * (size_y // BY) * rows_z, LANES)

    inputs = (gas_field, velocity, fraction, response, cell_index, brick_index, crossing)
    inputs = [pltpu.with_memory_space_constraint(array, pltpu.HBM) for array in inputs]
    grid, face, plane, velocity, fraction, response, cell_index, brick_index, crossing = call(
        begin_kernel,
        [grid_shape, (size_y, LANES), (comps * size_y, LANES)]
        + [jax.ShapeDtypeStruct(array.shape, array.dtype) for array in inputs[1:]],
        *inputs, hbm=range(7), scratch=(pltpu.SemaphoreType.DMA((7,)),),
    )
    from_z = moved_along(face, "gz", -1)
    from_x = moved_along(plane, "gx", -1)
    from_xz = moved_diagonally(face, -1)
    lines, deposit, table, ready, blocks = call(
        prepare_kernel,
        [
            lines_shape,
            deposit_shape,
            (TABLE_ROWS * spare, LANES),
            (8, LANES),
            jax.ShapeDtypeStruct((2 * nblocks + 2,), jnp.int32),
        ],
        grid, velocity, fraction, response, cell_index, brick_index,
        smem=(5,), smem_outs=(4,), cycles=3000,
    )
    line_rows = -(-(comps * size_x + comps + 1) // 8) * 8 + 8
    (y_lines,) = call(y_lines_kernel, [(line_rows, LANES)], grid, from_z, from_x, from_xz, ready)
    y1, y2 = swapped_y((y_lines, y_lines))
    square = pltpu.VMEM((LANES, LANES), jnp.float32)
    scalars = (pltpu.SMEM(blocks.shape, jnp.int32), pltpu.SMEM(brick_index.shape, jnp.int32))
    dims = (comps, size_x // BX, size_y // BY, size_z // BZ, rows_z)
    slots = crossing.shape[1]
    count = 7 * slots

    def parts(many):
        return [(many, 2 * comps * REACH_Z, LANES), (many, 2 * LANES, LANES)]

    state, push_parts, spread_parts, grid, lines, top = call(
        functools.partial(gather_kernel, dims),
        [(STATE * spare, LANES)]
        + [jax.ShapeDtypeStruct(shape, jnp.bfloat16) for shape in parts(-(-nblocks // WIDE) * WIDE)]
        + [grid_shape, lines_shape, (LANES, LANES)],
        blocks, brick_index, table, grid, lines, from_z, from_x, from_xz,
        aliases={3: 3, 4: 4}, cycles=4000, scratch=(*scalars, square, pltpu.SemaphoreType.DMA((2,))),
    )
    height = comps * SPREAD
    grid, lines, state, deposit, to_y1, to_y2, top_tiles = call(
        functools.partial(late_kernel, dims, push, diffuse),
        [
            grid_shape,
            lines_shape,
            (STATE * spare, LANES),
            deposit_shape,
            (count + line_rows, LANES),
            (count + line_rows, LANES),
            ((size_x // BX) * height + 8 * REACH_Y, LANES),
        ],
        blocks, brick_index, crossing, table, grid, lines, top, y1, y2, state, deposit,
        aliases={4: 0, 5: 1, 9: 2, 10: 3}, cycles=2000,
        scratch=[
            *(pltpu.VMEM(shape, jnp.bfloat16) for shape in parts(UNROLL)),
            *scalars,
            pltpu.SMEM(crossing.shape, jnp.int32),
            square,
            pltpu.VMEM((2 * count + 8, LANES), jnp.float32),
            pltpu.VMEM((comps * ROWS_Y, LANES), jnp.float32),
            pltpu.SemaphoreType.DMA((3,)),
        ],
    )
    y1, y2 = swapped_y((to_y1, to_y2))
    _, leaving, deposit, to_x, to_z = call(
        functools.partial(deposit_kernel, dims, push, diffuse),
        [
            deposit_shape,
            (4 * count + 8, LANES),
            (comps, size_x + 1, ROWS_Y, LANES),
            (comps * size_y, LANES),
            (size_y, LANES),
        ],
        blocks, brick_index, crossing, push_parts, spread_parts, state, deposit, top_tiles, grid,
        smem=(0, 1, 2), aliases={6: 0}, cycles=5000,
        scratch=(
            pltpu.VMEM((ROWS_Y, LANES), jnp.float32),
            pltpu.VMEM(((size_x // BX) * (size_y // BY) * height, LANES), jnp.float32),
            square,
        ),
    )
    base, velocity_next = call(
        functools.partial(base_kernel, push, diffuse, count), [gas_field.shape, (comps, nblocks, LANES)],
        grid, deposit, top, y1, y2, state, cycles=1000,
    )
    edge = comps * size_y
    both = lax.axis_size("gx") == 2
    to_x, to_z1, to_z2, to_xz = call(
        functools.partial(relay_kernel, size_x, size_y, comps, count),
        [(edge + (2 if both else 1) * count, LANES), *[(count + size_y + 8 * more, LANES) for more in range(3)]],
        y1, y2, to_x, to_z, leaving,
    )
    got_x = moved_along(to_x, "gx", 1)
    z1, z2 = swapped_z((to_z1, to_z2))
    got_xz = moved_diagonally(to_xz, 1)
    got_mx = got_x if both else moved_along(leaving[count : 2 * count], "gx", -1)
    gas_next, arrivals = call(
        functools.partial(finish_kernel, count), [gas_field.shape, (6, 7, slots, LANES)],
        base, y1, y2, got_x, got_mx, z1, z2, got_xz, hbm_outs=(0, 1),
        scratch=(
            pltpu.VMEM(gas_field.shape, jnp.float32),
            pltpu.VMEM((6, 7, slots, LANES), jnp.float32),
            pltpu.SemaphoreType.DMA((comps + 1,)),
        ),
    )
    return gas_next, jnp.transpose(velocity_next, (1, 0, 2)), jnp.transpose(arrivals, (0, 2, 1, 3))


def solution(mesh):
    owner = ("gx", "gz", "gy")
    in_specs = (
        P(None, "gx", "gy", "gz"),
        P(owner, None, None),
        P(owner, None, None),
        P(owner, None),
        P(owner, None),
        P(owner),
        P(owner, None),
    )
    out_specs = (
        P(None, "gx", "gy", "gz"),
        P(owner, None, None),
        P(owner, None, None, None),
    )
    return jax.shard_map(
        per_device, mesh=mesh, in_specs=in_specs, out_specs=out_specs, check_vma=False
    )
```

```python
import functools

import jax
import jax.numpy as jnp
from jax import lax
from jax.experimental import pallas as pl
from jax.experimental.pallas import tpu as pltpu
from jax.sharding import PartitionSpec as P

BX = 4
BY = 4
BZ = 8

TIME_STEP = 0.25
VISCOSITY = 0.4

LANES = 128
PACK = 32
ROWS_Y = 24
REACH_X = BX + 1
REACH_Y = 8
SPREAD = REACH_X * REACH_Y
REACH_Z = 2 * BZ
UNROLL = 8
WIDE = 16

WEIGHT, ALONG_Y, IN_Y, ALONG_Z, IN_Z, RESPONSE, MOVING, OFFSET = 0, 5, 6, 7, 8, 9, 10, 13
TABLE_ROWS = 16
STATE = 8

VMEM = pl.BlockSpec(memory_space=pltpu.VMEM)
SMEM = pl.BlockSpec(memory_space=pltpu.SMEM)
HBM = pl.BlockSpec(memory_space=pltpu.HBM)


def moved_along(block, axis, distance):
    count = lax.axis_size(axis)
    return lax.ppermute(block, axis, [(i, (i + distance) % count) for i in range(count)])


def swapped_z(blocks):
    count = lax.axis_size("gz")
    first = [(i, i ^ 1) for i in range(count)]
    second = [(i, (((i + 1) ^ 1) - 1) % count) for i in range(count)]
    return lax.ppermute(blocks[0], "gz", first), lax.ppermute(blocks[1], "gz", second)


def swapped_y(blocks):
    nz, ny = lax.axis_size("gz"), lax.axis_size("gy")
    first = [(j, j ^ 1) for j in range(ny)]
    second = []
    for k in range(nz):
        second.append((k * ny, (k ^ 1) * ny))
        second.append((k * ny + ny - 1, (k ^ 1) * ny + ny - 1))
        second.extend((k * ny + j, k * ny + ((j + 1) ^ 1) - 1) for j in range(1, ny - 1))
    middle = lax.ppermute(blocks[1], ("gz", "gy"), second)
    return lax.ppermute(blocks[0], "gy", first), middle


def moved_diagonally(block, distance):
    nx, nz = lax.axis_size("gx"), lax.axis_size("gz")
    route = [(i * nz + k, (i + distance) % nx * nz + (k + distance) % nz) for i in range(nx) for k in range(nz)]
    return lax.ppermute(block, ("gx", "gz"), route)


def call(
    body, outs, *operands, smem=(), hbm=(), smem_outs=(), hbm_outs=(), scratch=(), aliases=None, cycles=0, limit=40
):
    return pl.pallas_call(
        body,
        out_shape=[o if isinstance(o, jax.ShapeDtypeStruct) else jax.ShapeDtypeStruct(o, jnp.float32) for o in outs],
        in_specs=[SMEM if i in smem else HBM if i in hbm else VMEM for i in range(len(operands))],
        out_specs=[SMEM if i in smem_outs else HBM if i in hbm_outs else VMEM for i in range(len(outs))],
        scratch_shapes=list(scratch),
        input_output_aliases=aliases or {},
        compiler_params=pltpu.CompilerParams(vmem_limit_bytes=limit * 1024 * 1024),
        cost_estimate=pl.CostEstimate(flops=cycles * 4096, bytes_accessed=cycles * 1024, transcendentals=0),
    )(*operands)


def lane_ids(rows):
    return lax.broadcasted_iota(jnp.int32, (rows, LANES), 1)


def row_ids(rows):
    return lax.broadcasted_iota(jnp.int32, (rows, LANES), 0)


def turned(value, shift):
    shift = shift % LANES
    return pltpu.roll(value, shift, 1) if shift else value


def odd(axis):
    return lax.axis_index(axis) % 2


def begin_kernel(
    gas_ref, velocity_in, fraction_in, response_in, cell_in, brick_in, crossing_in,
    grid_ref, face_ref, plane_ref, velocity_ref, fraction_ref, response_ref, cell_ref, brick_ref, crossing_ref, sems,
):
    comps, size_x, size_y, _ = gas_ref.shape
    pairs = [
        (gas_ref, grid_ref.at[:, 1 : size_x + 1, 0:size_y]),
        (velocity_in, velocity_ref), (fraction_in, fraction_ref), (response_in, response_ref),
        (cell_in, cell_ref), (brick_in, brick_ref), (crossing_in, crossing_ref),
    ]
    copies = [pltpu.make_async_copy(source, target, sems.at[i]) for i, (source, target) in enumerate(pairs)]
    for copy in copies:
        copy.start()
    zeros = jnp.zeros((ROWS_Y, LANES), jnp.float32)
    for c in range(comps):
        grid_ref[c, 0] = zeros
        grid_ref[c, size_x + 1] = zeros
        for x in range(size_x):
            grid_ref[c, x + 1, size_y:] = zeros[size_y:]
    copies[0].wait()
    lane = lane_ids(size_y)
    face = jnp.zeros((size_y, LANES), jnp.float32)
    for c in range(comps):
        plane_ref[c * size_y : (c + 1) * size_y] = grid_ref[c, 1, 0:size_y]
        for x in range(size_x):
            place = PACK * c + x
            face = jnp.where(lane == place, turned(grid_ref[c, x + 1, 0:size_y], place), face)
    face_ref[...] = face
    for copy in copies[1:]:
        copy.wait()


def parts_of(value):
    main = value.astype(jnp.bfloat16).astype(jnp.float32)
    return main, value - main


def lay_out(grid_ref, lines_ref, p, q, size_y, size_z):
    comps = grid_ref.shape[0]
    rows_z = size_z + 8
    count_y = size_y // BY
    for c in range(comps):
        planes = [grid_ref[c, p * BX + a + 1, q * BY : q * BY + REACH_Y] for a in range(REACH_X)]
        main, rest = parts_of(jnp.concatenate(planes, axis=0))
        stack = jnp.concatenate([main, rest, main, jnp.zeros((LANES - 3 * SPREAD, LANES), jnp.float32)], axis=0)
        at = ((p * count_y + q) * comps + c) * rows_z
        lines_ref[at : at + size_z] = jnp.transpose(stack)


def lay_out_top(turned_ref, lines_ref, q, comps, count_x, count_y, size_z):
    lane = lane_ids(count_x)
    rows_z = size_z + 8
    for c in range(comps):
        total = jnp.zeros((count_x, LANES), jnp.float32)
        for a in range(REACH_X):
            rows = turned_ref[pl.ds(PACK * c + a, count_x, stride=BX)]
            total = jnp.where(lane // REACH_Y == a, turned(rows, a * REACH_Y - q * BY), total)
        main, rest = parts_of(total)
        line = main + turned(rest, SPREAD) + turned(main, 2 * SPREAD)
        for p in range(count_x):
            at = ((p * count_y + q) * comps + c) * rows_z + size_z
            lines_ref[at : at + 1] = line[p : p + 1]


def prepare_kernel(
    grid_ref, velocity_ref, fraction_ref, response_ref, cell_ref, brick_ref,
    lines_ref, deposit_ref, table_ref, ready_ref, list_ref,
):
    comps, size_x, size_y, size_z = grid_ref.shape[0], grid_ref.shape[1] - 2, grid_ref.shape[2] - 8, grid_ref.shape[3]
    nblocks = velocity_ref.shape[1]
    count_x, count_y, count_z = size_x // BX, size_y // BY, size_z // BZ
    rows_z = size_z + 8


    def visit(k, counts):
        late = jnp.where(lax.rem(lax.div(brick_ref[k], count_z), count_y) == count_y - 1, 1, 0)
        list_ref[jnp.where(late == 1, nblocks + counts[1], counts[0])] = k
        return counts[0] + 1 - late, counts[1] + late

    early, late = lax.fori_loop(0, nblocks, visit, (jnp.int32(0), jnp.int32(0)), unroll=8)
    list_ref[2 * nblocks] = early
    list_ref[2 * nblocks + 1] = late
    ready_ref[...] = jnp.zeros_like(ready_ref)

    deposit_ref[...] = jnp.zeros_like(deposit_ref)
    for p in range(count_x):
        for q in range(count_y):
            for c in range(comps):
                at = ((p * count_y + q) * comps + c) * rows_z + size_z
                lines_ref[at : at + 8] = jnp.zeros((8, LANES), jnp.float32)
    for p in range(count_x - 1):
        for q in range(count_y - 1):
            lay_out(grid_ref, lines_ref, p, q, size_y, size_z)

    cells = cell_ref[...]
    cell_x, cell_y, cell_z = cells // (BY * BZ), cells // BZ % BY, cells % BZ
    along_x = fraction_ref[0]

    def put(row, value):
        table_ref[pl.ds(row, nblocks, stride=TABLE_ROWS)] = value

    for a in range(REACH_X):
        put(WEIGHT + a, jnp.where(cell_x == a, 1.0 - along_x, 0.0) + jnp.where(cell_x == a - 1, along_x, 0.0))
    put(ALONG_Y, fraction_ref[1])
    put(IN_Y, cell_y.astype(jnp.float32))
    put(ALONG_Z, fraction_ref[2])
    put(IN_Z, cell_z.astype(jnp.float32))
    put(RESPONSE, response_ref[...])
    for c in range(comps):
        put(MOVING + c, velocity_ref[c])
        put(OFFSET + c, fraction_ref[c])
    spare = table_ref.shape[0] - nblocks * TABLE_ROWS
    row = row_ids(spare)
    table_ref[nblocks * TABLE_ROWS :] = jnp.where(row % TABLE_ROWS == RESPONSE, 1.0, 0.0)


def y_lines_kernel(grid_ref, face_ref, from_x_ref, edge_ref, ready_ref, out_ref):
    comps, size_x = grid_ref.shape[0], grid_ref.shape[1] - 2
    size_y = face_ref.shape[0]
    for c in range(comps):
        out_ref[c * size_x : (c + 1) * size_x] = grid_ref[c, 1 : size_x + 1, 0]
        out_ref[comps * size_x + c : comps * size_x + c + 1] = from_x_ref[c * size_y : c * size_y + 1]
    line = jnp.where(lane_ids(8) % PACK == size_x, turned(edge_ref[0:8], size_x), face_ref[0:8])
    out_ref[comps * size_x + comps : comps * size_x + comps + 1] = line[0:1]


def halo_xz_kernel(grid_in_ref, lines_in_ref, face_ref, from_x_ref, edge_ref, grid_ref, lines_ref, top_ref, turned_ref):
    comps, size_x = grid_ref.shape[0], grid_ref.shape[1] - 2
    size_y, size_z = face_ref.shape[0], grid_ref.shape[3]
    count_x, count_y = size_x // BX, size_y // BY
    for c in range(comps):
        grid_ref[c, size_x + 1, 0:size_y] = from_x_ref[c * size_y : (c + 1) * size_y]
    for q in range(count_y - 1):
        lay_out(grid_ref, lines_ref, count_x - 1, q, size_y, size_z)
    top = jnp.where(lane_ids(size_y) % PACK == size_x, turned(edge_ref[...], size_x), face_ref[...])
    top_ref[0:size_y] = top
    top_ref[size_y:] = jnp.zeros((LANES - size_y, LANES), jnp.float32)
    turned_ref[...] = jnp.transpose(top_ref[...])
    for q in range(count_y - 1):
        lay_out_top(turned_ref, lines_ref, q, comps, count_x, count_y, size_z)


def halo_y_kernel(size_y, grid_in_ref, lines_in_ref, top_in_ref, first_ref, second_ref, grid_ref, lines_ref, turned_ref):
    comps, size_x, size_z = grid_ref.shape[0], grid_ref.shape[1] - 2, grid_ref.shape[3]
    count_x, count_y = size_x // BX, size_y // BY
    inside = lax.axis_index("gy") != lax.axis_size("gy") - 1
    kept = (row_ids(8) == 0) & inside
    even = jnp.full((1, LANES), odd("gy")) == 0

    def line_at(row):
        line = jnp.where(even, first_ref[row : row + 1], second_ref[row : row + 1])
        return jnp.where(kept, jnp.broadcast_to(line, (8, LANES)), 0.0)

    for c in range(comps):
        for x in range(size_x + 1):
            grid_ref[c, x + 1, size_y:] = line_at(c * size_x + x if x < size_x else comps * size_x + c)
    for p in range(count_x):
        lay_out(grid_ref, lines_ref, p, count_y - 1, size_y, size_z)
    corner = line_at(comps * size_x + comps)
    rest = jnp.zeros((LANES - size_y - 8, LANES), jnp.float32)
    turned_ref[...] = jnp.transpose(jnp.concatenate([top_in_ref[0:size_y], corner, rest], axis=0))
    lay_out_top(turned_ref, lines_ref, count_y - 1, comps, count_x, count_y, size_z)


def block_steps(dims, list_ref, brick_ref, end):
    comps, _, count_y, count_z, rows_z = dims
    nblocks = brick_ref.shape[0]
    sub = row_ids(8)
    row_y = row_ids(REACH_Y).astype(jnp.float32)
    row_z = row_ids(REACH_Z).astype(jnp.float32)
    lanes = lane_ids(REACH_Z)

    def hat(rows, inside, along):
        return jnp.where(rows == inside, 1.0 - along, 0.0) + jnp.where(rows == inside + 1.0, along, 0.0)

    def place_of(at):
        k = jnp.where(at < end, list_ref[jnp.minimum(at, 2 * nblocks + 1)], nblocks)
        brick = jnp.where(k < nblocks, brick_ref[jnp.minimum(k, nblocks - 1)], 0)
        brick_x = lax.div(brick, count_y * count_z)
        brick_y = lax.rem(lax.div(brick, count_z), count_y)
        return k, brick_x * count_y + brick_y, lax.rem(brick, count_z)

    def loaded(at, lines_ref, table_ref):
        k, pair, brick_z = place_of(at)
        first = pl.multiple_of(pair * comps * rows_z + brick_z * BZ, 8)
        window = jnp.concatenate([lines_ref[pl.ds(first + c * rows_z, REACH_Z)] for c in range(comps)], axis=0)
        table = table_ref[pl.ds(pl.multiple_of(k * TABLE_ROWS, TABLE_ROWS), TABLE_ROWS)]
        return k, window, [table[i : i + 1] for i in range(TABLE_ROWS)]

    def weighted(rows):
        weight_y = hat(row_y, rows[IN_Y], rows[ALONG_Y])
        weight_z = hat(row_z, rows[IN_Z], rows[ALONG_Z])
        weight = jnp.concatenate([rows[WEIGHT + a] * weight_y for a in range(REACH_X)], axis=0)
        return weight_z, *parts_of(weight)

    def stepped(seen, weight_z, rows):
        rate = 1.0 / rows[RESPONSE]
        state, moved, pushed = [], [], []
        for c in range(comps):
            gas_sample = jnp.sum(seen[c * REACH_Z : (c + 1) * REACH_Z] * weight_z, axis=0, keepdims=True)
            drag = (gas_sample - rows[MOVING + c]) * rate
            state.append(rows[MOVING + c] + TIME_STEP * drag)
            moved.append(rows[OFFSET + c] + TIME_STEP * state[c])
            pushed.append(drag * weight_z)
        tile = jnp.broadcast_to(rows[RESPONSE], (STATE, LANES))
        for i, value in enumerate(state + moved):
            tile = jnp.where(sub == i, value, tile)
        return tile, jnp.concatenate(parts_of(jnp.concatenate(pushed, axis=0)), axis=0)

    def gathered(one, two):
        tables, windows, weights = [], [], []
        for _, window, rows in (one, two):
            weight_z, main, rest = weighted(rows)
            weights.append((weight_z, main, rest))
            unused = jnp.zeros((LANES - 3 * SPREAD, LANES), jnp.float32)
            tables.append(jnp.concatenate([main, main, rest, unused], axis=0).astype(jnp.bfloat16))
            windows.append(window)
        seen = lax.dot_general(
            jnp.concatenate(windows, axis=0).astype(jnp.bfloat16), jnp.concatenate(tables, axis=1),
            (((1,), (0,)), ((), ())), preferred_element_type=jnp.float32,
        )
        height = comps * REACH_Z
        tiles, fresh = [], []
        for i, (_, _, rows) in enumerate((one, two)):
            weight_z, main, rest = weights[i]
            mine = seen[i * height : (i + 1) * height, i * LANES : (i + 1) * LANES]
            tile, push = stepped(mine, weight_z, rows)
            tiles.append(tile)
            unused = jnp.zeros((LANES - comps * SPREAD, LANES), jnp.float32)
            spread = jnp.concatenate([main] * comps + [unused] + [rest] * comps + [unused], axis=0)
            fresh.append((push.astype(jnp.bfloat16), spread.astype(jnp.bfloat16)))
        return tiles, fresh

    def shared(push, spread):
        shares = lax.dot_general(push, spread, (((1,), (1,)), ((), ())), preferred_element_type=jnp.float32)
        height = comps * REACH_Z
        total = shares[:height, :LANES] + shares[:height, LANES:] + shares[height:, :LANES]
        result = jnp.zeros((REACH_Z, LANES), jnp.float32)
        for c in range(comps):
            inside = (lanes >= c * SPREAD) & (lanes < (c + 1) * SPREAD)
            result = jnp.where(inside, total[c * REACH_Z : (c + 1) * REACH_Z], result)
        return result

    def add(deposit_ref, at, shares):
        spots = []
        for u in range(len(shares)):
            _, pair, brick_z = place_of(at + u)
            spots.append(pl.ds(pl.multiple_of(pair * rows_z + brick_z * BZ, 8), REACH_Z))
        for spot, share in zip(spots, shares):
            deposit_ref[spot] = deposit_ref[spot] + share

    def group_of(taken):
        tiles, fresh = [], []
        for u in range(0, len(taken), 2):
            both, kept = gathered(taken[u], taken[u + 1])
            tiles.extend(both)
            fresh.extend(kept)
        return tiles, fresh

    def keep(state_ref, taken, tiles):
        for (k, _, _), tile in zip(taken, tiles):
            state_ref[pl.ds(pl.multiple_of(STATE * k, STATE), STATE)] = tile

    def deposits_of(kept):
        return [shared(push, spread) for push, spread in kept]

    return loaded, group_of, keep, deposits_of, add


def groups_in(list_ref, late, many=UNROLL):
    room = (list_ref.shape[0] - 2) // 2
    count = list_ref[2 * room + late]
    return late * room, (count + many - 1) // many, late * room + count


def leave(crossing_ref, state_ref, leaving_ref, faces):
    slots = crossing_ref.shape[1]
    rows = (leaving_ref.shape[0] - 8) // (len(faces) * slots)
    for i, face in enumerate(faces):
        tiles = []
        for slot in range(slots):
            block = crossing_ref[face, slot]
            spot = pl.ds(pl.multiple_of(jnp.maximum(block, 0) * STATE, STATE), STATE)
            live = jnp.full((STATE, LANES), block, jnp.int32) >= 0
            tiles.append(jnp.where(live, state_ref[spot], 0.0))
        for slot, tile in enumerate(tiles):
            leaving_ref[pl.ds(i * rows * slots + slot, rows, stride=slots)] = tile[:rows]


def fetched(sems, *pairs):
    copies = [pltpu.make_async_copy(source, target, sems.at[i]) for i, (source, target) in enumerate(pairs)]
    for copy in copies:
        copy.start()
    return copies


def gather_kernel(
    dims, list_in, brick_in, table_ref, grid_in_ref, lines_in_ref, face_ref, from_x_ref, edge_ref,
    state_ref, push_ref, spread_ref, grid_ref, lines_ref, top_ref, list_ref, brick_ref, turned_ref, sems,
):
    copies = fetched(sems, (list_in, list_ref), (brick_in, brick_ref))
    halo_xz_kernel(grid_in_ref, lines_in_ref, face_ref, from_x_ref, edge_ref, grid_ref, lines_ref, top_ref, turned_ref)
    for copy in copies:
        copy.wait()
    base, groups, end = groups_in(list_ref, 0, WIDE)
    loaded, group_of, keep, _, _ = block_steps(dims, list_ref, brick_ref, end)

    @pl.loop(0, groups)
    def _(group):
        taken = [loaded(base + group * WIDE + u, lines_ref, table_ref) for u in range(WIDE)]
        tiles, fresh = group_of(taken)
        keep(state_ref, taken, tiles)
        for i, (push, spread) in enumerate(fresh):
            push_ref[group * WIDE + i] = push
            spread_ref[group * WIDE + i] = spread


def deposit_kernel(
    dims, push, diffuse, list_ref, brick_ref, crossing_ref, push_ref, spread_ref, state_ref, deposit_in_ref, top_tiles_ref,
    grid_ref, deposit_ref, leaving_ref, plane_ref, x_ref, z_ref, face_ref, tiles_ref, turned_ref,
):
    base, groups, end = groups_in(list_ref, 0, WIDE)
    _, _, _, deposits_of, add = block_steps(dims, list_ref, brick_ref, end)
    leave(crossing_ref, state_ref, leaving_ref, (0, 1, 4, 5))

    @pl.loop(0, groups)
    def _(group):
        mine = [group * WIDE + i for i in range(WIDE)]
        add(deposit_ref, base + group * WIDE, deposits_of([(push_ref[i], spread_ref[i]) for i in mine]))

    merge(deposit_ref, top_tiles_ref, plane_ref, face_ref, tiles_ref, turned_ref)
    send_xz(push, diffuse, grid_ref, plane_ref, face_ref, x_ref, z_ref)


def late_kernel(
    dims, push, diffuse, list_in, brick_in, crossing_in, table_ref, grid_in_ref, lines_in_ref, top_in_ref,
    first_ref, second_ref,
    state_in_ref, deposit_in_ref,
    grid_ref, lines_ref, state_ref, deposit_ref, y1_ref, y2_ref, tiles_ref,
    push_ref, spread_ref, list_ref, brick_ref, crossing_ref, turned_ref, leaving_ref, y_lines_ref, sems,
):
    copies = fetched(sems, (list_in, list_ref), (brick_in, brick_ref), (crossing_in, crossing_ref))
    halo_y_kernel(
        dims[2] * BY, grid_in_ref, lines_in_ref, top_in_ref, first_ref, second_ref, grid_ref, lines_ref, turned_ref
    )
    for copy in copies:
        copy.wait()
    base, groups, end = groups_in(list_ref, 1)
    loaded, group_of, keep, deposits_of, add = block_steps(dims, list_ref, brick_ref, end)
    push_ref[...] = jnp.zeros_like(push_ref)
    spread_ref[...] = jnp.zeros_like(spread_ref)

    @pl.loop(0, groups + 1)
    def _(group):
        now = base + jnp.maximum(jnp.minimum(group, groups - 1), 0) * UNROLL
        before = base + jnp.maximum(group - 1, 0) * UNROLL
        taken = [loaded(now + u, lines_ref, table_ref) for u in range(UNROLL)]
        shares = deposits_of([(push_ref[i], spread_ref[i]) for i in range(UNROLL)])
        tiles, fresh = group_of(taken)
        add(deposit_ref, before, shares)
        keep(state_ref, taken, tiles)
        for i, (kept, spread) in enumerate(fresh):
            push_ref[i] = kept
            spread_ref[i] = spread

    leave(crossing_ref, state_ref, leaving_ref, (2, 3))
    send_y(push, diffuse, leaving_ref, grid_ref, deposit_ref, y1_ref, y2_ref, tiles_ref, y_lines_ref)


def top_rows(deposit_ref, q, count_x, count_y, rows_z, size_z):
    total = None
    for p in range(count_x):
        at = (p * count_y + q) * rows_z + size_z
        value = pltpu.roll(deposit_ref[at : at + 8], p, 0) if p else deposit_ref[at : at + 8]
        total = value if total is None else total + value
    return total


def send_y(push, diffuse, leaving_ref, grid_ref, deposit_ref, y1_ref, y2_ref, tiles_ref, lines_ref):
    comps, size_x, size_y, size_z = grid_ref.shape[0], grid_ref.shape[1] - 2, grid_ref.shape[2] - 8, grid_ref.shape[3]
    count_x, count_y = size_x // BX, size_y // BY
    rows_z = size_z + 8
    rows = (leaving_ref.shape[0] - 8) // 2
    height = comps * SPREAD
    for p in range(count_x):
        at = (p * count_y + count_y - 1) * rows_z
        tiles_ref[p * height : (p + 1) * height] = jnp.transpose(deposit_ref[at : at + size_z])[:height]
    first = jnp.full((rows, LANES), odd("gy")) == 0
    y1_ref[0:rows] = jnp.where(first, leaving_ref[0:rows], leaving_ref[rows : 2 * rows])
    y2_ref[0:rows] = jnp.where(first, leaving_ref[rows : 2 * rows], leaving_ref[0:rows])
    lines_ref[...] = jnp.zeros_like(lines_ref)
    for c in range(comps):
        for p in range(count_x):
            spot = slice(c * ROWS_Y + p * BX, c * ROWS_Y + p * BX + REACH_X)
            line = tiles_ref[pl.ds(p * height + c * SPREAD + BY, REACH_X, stride=REACH_Y)]
            lines_ref[spot] = lines_ref[spot] + line
    wrapped = top_rows(deposit_ref, count_y - 1, count_x, count_y, rows_z, size_z)
    lane = lane_ids(8)
    packed = jnp.zeros((8, LANES), jnp.float32)
    for c in range(comps):
        spot = slice(c * ROWS_Y, (c + 1) * ROWS_Y)
        beside = jnp.concatenate([grid_ref[c, 1 : size_x + 1, size_y - 1], jnp.zeros((8, LANES), jnp.float32)], axis=0)
        line = push * lines_ref[spot] + diffuse * beside
        at = rows + c * (size_x + 1)
        y1_ref[at : at + size_x + 1] = line[: size_x + 1]
        y2_ref[at : at + size_x + 1] = line[: size_x + 1]
        for a in range(REACH_X):
            place = PACK * c + a
            value = turned(wrapped, place - c * SPREAD - a * REACH_Y - BY)
            packed = packed + jnp.where(lane == place, value, 0.0)
    corner = packed[0:1]
    for p in range(1, count_x):
        corner = corner + turned(packed[p : p + 1], p * BX)
    at = rows + comps * (size_x + 1)
    y1_ref[at : at + 1] = push * corner
    y2_ref[at : at + 1] = push * corner


def merge(deposit_ref, top_tiles_ref, plane_ref, face_ref, tiles_ref, turned_ref):
    comps, planes = plane_ref.shape[:2]
    count_x, size_z = (planes - 1) // BX, plane_ref.shape[3]
    rows_z = size_z + 8
    count_y = deposit_ref.shape[0] // (rows_z * count_x)
    height = comps * SPREAD
    for p in range(count_x):
        for q in range(count_y - 1):
            at = p * count_y + q
            value = jnp.transpose(deposit_ref[at * rows_z : at * rows_z + size_z])
            tiles_ref[at * height : (at + 1) * height] = value[:height]
    top = row_ids(REACH_Y) >= BY
    for c in range(comps):
        for x in range(planes):
            bricks = [(x // BX, x % BX)] if x < planes - 1 else []
            if x and x % BX == 0:
                bricks.append((x // BX - 1, BX))

            def tile(q):
                total = None
                for p, a in bricks:
                    at = c * SPREAD + a * REACH_Y
                    if q < count_y - 1:
                        value = tiles_ref[(p * count_y + q) * height + at : (p * count_y + q) * height + at + REACH_Y]
                    else:
                        value = top_tiles_ref[p * height + at : p * height + at + REACH_Y]
                    total = value if total is None else total + value
                return total

            carried = None
            for q in range(0, count_y, 2):
                here = tile(q)
                if carried is not None:
                    here = here + carried
                between = pltpu.roll(tile(q + 1), BY, 0)
                here = here + jnp.where(top, between, 0.0)
                carried = jnp.where(top, 0.0, between)
                plane_ref[c, x, q * BY : q * BY + REACH_Y] = here
            plane_ref[c, x, count_y * BY :] = carried

    lane = lane_ids(count_x)
    turned_ref[...] = jnp.zeros_like(turned_ref)
    for q in range(count_y):
        wrapped = top_rows(deposit_ref, q, count_x, count_y, rows_z, size_z)[:count_x]
        within = (lane >= q * BY) & (lane <= (q + 1) * BY)
        for c in range(comps):
            for a in range(REACH_X):
                value = turned(wrapped, q * BY - c * SPREAD - a * REACH_Y)
                spot = pl.ds(PACK * c + a, count_x, stride=BX)
                turned_ref[spot] = turned_ref[spot] + jnp.where(within, value, 0.0)
    face_ref[...] = jnp.transpose(turned_ref[...])[: face_ref.shape[0]]


def send_xz(push, diffuse, grid_ref, deposit_ref, face_ref, x_ref, z_ref):
    comps, size_x = grid_ref.shape[0], grid_ref.shape[1] - 2
    size_y = z_ref.shape[0]
    lane = lane_ids(size_y)
    packed = push * face_ref[0:size_y]
    for c in range(comps):
        for x in range(size_x):
            place = PACK * c + x
            packed = packed + jnp.where(lane == place, diffuse * turned(grid_ref[c, x + 1, 0:size_y], place + 1), 0.0)
        total = push * deposit_ref[c, size_x, 0:size_y]
        x_ref[c * size_y : (c + 1) * size_y] = diffuse * grid_ref[c, size_x, 0:size_y] + total
    z_ref[...] = packed


def base_kernel(push, diffuse, count, grid_ref, deposit_ref, top_ref, y1_ref, y2_ref, state_ref, base_ref, velocity_ref):
    comps, size_x, size_y, size_z = base_ref.shape
    lane, sub = lane_ids(size_y), row_ids(size_y)
    top = top_ref[0:size_y]
    for c in range(comps):
        at = count + c * (size_x + 1)
        lines = below(y1_ref, y2_ref, slice(at, at + size_x))
        for x in range(size_x):
            here = grid_ref[c, x + 1, 0:size_y]
            before = jnp.where(sub == 0, 0.0, pltpu.roll(here, 1, 0))
            laplace = grid_ref[c, x, 0:size_y] + grid_ref[c, x + 2, 0:size_y]
            laplace = laplace + grid_ref[c, x + 1, 1 : size_y + 1] + before
            ahead = jnp.where(lane == size_z - 1, turned(top, size_z - 1 - (PACK * c + x)), turned(here, -1))
            laplace = laplace + ahead + jnp.where(lane == 0, 0.0, turned(here, 1)) - 6.0 * here
            total = here + diffuse * laplace + push * deposit_ref[c, x, 0:size_y]
            line = jnp.broadcast_to(lines[x : x + 1], (size_y, LANES))
            base_ref[c, x] = total + jnp.where(sub == 0, line, 0.0)
        velocity_ref[c] = state_ref[pl.ds(c, velocity_ref.shape[1], stride=STATE)]


def below(first_ref, second_ref, rows):
    got = jnp.where(jnp.full((1, LANES), odd("gy")) == 1, first_ref[rows], second_ref[rows])
    return jnp.where(jnp.full((1, LANES), lax.axis_index("gy")) != 0, got, 0.0)


def relay_kernel(size_x, size_y, comps, count, first_ref, second_ref, x_in_ref, z_in_ref, leaving_ref, x_ref, z1_ref, z2_ref, edge_ref):
    edge = comps * size_y
    x_ref[0:edge] = x_in_ref[...]
    for c in range(comps):
        at = count + c * (size_x + 1) + size_x
        spot = slice(c * size_y, c * size_y + 1)
        x_ref[spot] = x_in_ref[spot] + below(first_ref, second_ref, slice(at, at + 1))
    x_ref[edge : edge + count] = leaving_ref[0:count]
    if x_ref.shape[0] > edge + count:
        x_ref[edge + count : edge + 2 * count] = leaving_ref[count : 2 * count]
    at = count + comps * (size_x + 1)
    edge_ref[size_y:] = jnp.zeros((edge_ref.shape[0] - size_y, LANES), jnp.float32)
    edge_ref[0:size_y] = z_in_ref[...]
    edge_ref[0:1] = z_in_ref[0:1] + below(first_ref, second_ref, slice(at, at + 1))
    first = jnp.full((1, LANES), odd("gz")) == 0
    plus = jnp.concatenate([leaving_ref[2 * count : 3 * count], edge_ref[0:size_y]], axis=0)
    minus = jnp.concatenate([leaving_ref[3 * count : 4 * count], jnp.zeros((size_y, LANES), jnp.float32)], axis=0)
    z1_ref[...] = jnp.where(first, plus, minus)
    z2_ref[0 : count + size_y] = jnp.where(first, minus, plus)
    z2_ref[count + size_y :] = jnp.zeros((z2_ref.shape[0] - count - size_y, LANES), jnp.float32)


def finish_kernel(
    count, base_ref, y1_ref, y2_ref, x_ref, minus_x_ref, z1_ref, z2_ref, edge_ref, gas_out, arrivals_out,
    gas_ref, arrivals_ref, sems,
):
    comps, size_x, size_y, _ = base_ref.shape
    first_lane = lane_ids(size_y) == 0
    odd_y, odd_z = jnp.full((1, LANES), odd("gy")) == 1, jnp.full((1, LANES), odd("gz")) == 1
    place = jnp.full((1, LANES), lax.axis_index("gy"))
    lower, upper = place != 0, place != lax.axis_size("gy") - 1
    rows = slice(count, count + size_y)
    slots = arrivals_ref.shape[2]
    for i in range(arrivals_ref.shape[1]):

        def rows_of(ref, at=0):
            return ref[at + i * slots : at + (i + 1) * slots]

        arrivals_ref[0, i] = rows_of(x_ref, comps * size_y)
        arrivals_ref[1, i] = rows_of(minus_x_ref, minus_x_ref.shape[0] - count)
        y1, y2 = rows_of(y1_ref), rows_of(y2_ref)
        arrivals_ref[2, i] = jnp.where(lower, jnp.where(odd_y, y1, y2), 0.0)
        arrivals_ref[3, i] = jnp.where(upper, jnp.where(odd_y, y2, y1), 0.0)
        z1, z2 = rows_of(z1_ref), rows_of(z2_ref)
        arrivals_ref[4, i] = jnp.where(odd_z, z1, z2)
        arrivals_ref[5, i] = jnp.where(odd_z, z2, z1)
    copies = [pltpu.make_async_copy(arrivals_ref, arrivals_out, sems.at[comps])]
    copies[0].start()
    face = jnp.where(odd_z, z1_ref[rows], z2_ref[rows])
    corner = edge_ref[0:size_y]
    for c in range(comps):
        for x in range(size_x):
            total = base_ref[c, x]
            far = turned(face, -(PACK * c + x))
            if x == 0:
                total = total + x_ref[c * size_y : (c + 1) * size_y]
                far = far + turned(corner, -(PACK * c + size_x))
            gas_ref[c, x] = total + jnp.where(first_lane, far, 0.0)
        copies.append(pltpu.make_async_copy(gas_ref.at[c], gas_out.at[c], sems.at[c]))
        copies[-1].start()
    for copy in copies:
        copy.wait()


def per_device(gas_field, velocity, fraction, response, cell_index, brick_index, crossing):
    comps, size_x, size_y, size_z = gas_field.shape
    nblocks = velocity.shape[0]
    loading = 0.5 * size_x * size_y * size_z / (nblocks * 128)
    push, diffuse = -TIME_STEP * loading, TIME_STEP * VISCOSITY
    velocity = jnp.transpose(velocity, (1, 0, 2))
    fraction = jnp.transpose(fraction, (1, 0, 2))
    spare = nblocks + 8
    rows_z = size_z + 8
    grid_shape = (comps, size_x + 2, ROWS_Y, LANES)
    lines_shape = ((size_x // BX) * (size_y // BY) * comps * rows_z, LANES)
    deposit_shape = ((size_x // BX) * (size_y // BY) * rows_z, LANES)

    inputs = (gas_field, velocity, fraction, response, cell_index, brick_index, crossing)
    inputs = [pltpu.with_memory_space_constraint(array, pltpu.HBM) for array in inputs]
    grid, face, plane, velocity, fraction, response, cell_index, brick_index, crossing = call(
        begin_kernel,
        [grid_shape, (size_y, LANES), (comps * size_y, LANES)]
        + [jax.ShapeDtypeStruct(array.shape, array.dtype) for array in inputs[1:]],
        *inputs, hbm=range(7), scratch=(pltpu.SemaphoreType.DMA((7,)),),
    )
    from_z = moved_along(face, "gz", -1)
    from_x = moved_along(plane, "gx", -1)
    from_xz = moved_diagonally(face, -1)
    lines, deposit, table, ready, blocks = call(
        prepare_kernel,
        [
            lines_shape,
            deposit_shape,
            (TABLE_ROWS * spare, LANES),
            (8, LANES),
            jax.ShapeDtypeStruct((2 * nblocks + 2,), jnp.int32),
        ],
        grid, velocity, fraction, response, cell_index, brick_index,
        smem=(5,), smem_outs=(4,), cycles=3000,
    )
    line_rows = -(-(comps * size_x + comps + 1) // 8) * 8 + 8
    (y_lines,) = call(y_lines_kernel, [(line_rows, LANES)], grid, from_z, from_x, from_xz, ready)
    y1, y2 = swapped_y((y_lines, y_lines))
    square = pltpu.VMEM((LANES, LANES), jnp.float32)
    scalars = (pltpu.SMEM(blocks.shape, jnp.int32), pltpu.SMEM(brick_index.shape, jnp.int32))
    dims = (comps, size_x // BX, size_y // BY, size_z // BZ, rows_z)
    slots = crossing.shape[1]
    count = 7 * slots

    def parts(many):
        return [(many, 2 * comps * REACH_Z, LANES), (many, 2 * LANES, LANES)]

    state, push_parts, spread_parts, grid, lines, top = call(
        functools.partial(gather_kernel, dims),
        [(STATE * spare, LANES)]
        + [jax.ShapeDtypeStruct(shape, jnp.bfloat16) for shape in parts(-(-nblocks // WIDE) * WIDE)]
        + [grid_shape, lines_shape, (LANES, LANES)],
        blocks, brick_index, table, grid, lines, from_z, from_x, from_xz,
        aliases={3: 3, 4: 4}, cycles=4000, scratch=(*scalars, square, pltpu.SemaphoreType.DMA((2,))),
    )
    height = comps * SPREAD
    grid, lines, state, deposit, to_y1, to_y2, top_tiles = call(
        functools.partial(late_kernel, dims, push, diffuse),
        [
            grid_shape,
            lines_shape,
            (STATE * spare, LANES),
            deposit_shape,
            (count + line_rows, LANES),
            (count + line_rows, LANES),
            ((size_x // BX) * height + 8 * REACH_Y, LANES),
        ],
        blocks, brick_index, crossing, table, grid, lines, top, y1, y2, state, deposit,
        aliases={4: 0, 5: 1, 9: 2, 10: 3}, cycles=2000,
        scratch=[
            *(pltpu.VMEM(shape, jnp.bfloat16) for shape in parts(UNROLL)),
            *scalars,
            pltpu.SMEM(crossing.shape, jnp.int32),
            square,
            pltpu.VMEM((2 * count + 8, LANES), jnp.float32),
            pltpu.VMEM((comps * ROWS_Y, LANES), jnp.float32),
            pltpu.SemaphoreType.DMA((3,)),
        ],
    )
    y1, y2 = swapped_y((to_y1, to_y2))
    _, leaving, deposit, to_x, to_z = call(
        functools.partial(deposit_kernel, dims, push, diffuse),
        [
            deposit_shape,
            (4 * count + 8, LANES),
            (comps, size_x + 1, ROWS_Y, LANES),
            (comps * size_y, LANES),
            (size_y, LANES),
        ],
        blocks, brick_index, crossing, push_parts, spread_parts, state, deposit, top_tiles, grid,
        smem=(0, 1, 2), aliases={6: 0}, cycles=5000,
        scratch=(
            pltpu.VMEM((ROWS_Y, LANES), jnp.float32),
            pltpu.VMEM(((size_x // BX) * (size_y // BY) * height, LANES), jnp.float32),
            square,
        ),
    )
    base, velocity_next = call(
        functools.partial(base_kernel, push, diffuse, count), [gas_field.shape, (comps, nblocks, LANES)],
        grid, deposit, top, y1, y2, state, cycles=1000,
    )
    edge = comps * size_y
    both = lax.axis_size("gx") == 2
    to_x, to_z1, to_z2, to_xz = call(
        functools.partial(relay_kernel, size_x, size_y, comps, count),
        [(edge + (2 if both else 1) * count, LANES), *[(count + size_y + 8 * more, LANES) for more in (0, 2, 1)]],
        y1, y2, to_x, to_z, leaving,
    )
    got_x = moved_along(to_x, "gx", 1)
    z1, z2 = swapped_z((to_z1, to_z2))
    got_xz = moved_diagonally(to_xz, 1)
    got_mx = got_x if both else moved_along(leaving[count : 2 * count], "gx", -1)
    gas_next, arrivals = call(
        functools.partial(finish_kernel, count), [gas_field.shape, (6, 7, slots, LANES)],
        base, y1, y2, got_x, got_mx, z1, z2, got_xz, hbm_outs=(0, 1),
        scratch=(
            pltpu.VMEM(gas_field.shape, jnp.float32),
            pltpu.VMEM((6, 7, slots, LANES), jnp.float32),
            pltpu.SemaphoreType.DMA((comps + 1,)),
        ),
    )
    return gas_next, jnp.transpose(velocity_next, (1, 0, 2)), jnp.transpose(arrivals, (0, 2, 1, 3))


def solution(mesh):
    owner = ("gx", "gz", "gy")
    in_specs = (
        P(None, "gx", "gy", "gz"),
        P(owner, None, None),
        P(owner, None, None),
        P(owner, None),
        P(owner, None),
        P(owner),
        P(owner, None),
    )
    out_specs = (
        P(None, "gx", "gy", "gz"),
        P(owner, None, None),
        P(owner, None, None, None),
    )
    return jax.shard_map(
        per_device, mesh=mesh, in_specs=in_specs, out_specs=out_specs, check_vma=False
    )
```

```python
import functools

import jax
import jax.numpy as jnp
from jax import lax
from jax.experimental import pallas as pl
from jax.experimental.pallas import tpu as pltpu
from jax.sharding import PartitionSpec as P

BX = 4
BY = 4
BZ = 8

TIME_STEP = 0.25
VISCOSITY = 0.4

LANES = 128
PACK = 32
ROWS_Y = 24
REACH_X = BX + 1
REACH_Y = 8
SPREAD = REACH_X * REACH_Y
REACH_Z = 2 * BZ
UNROLL = 8
WIDE = 20

WEIGHT, ALONG_Y, IN_Y, ALONG_Z, IN_Z, RESPONSE, MOVING, OFFSET = 0, 5, 6, 7, 8, 9, 10, 13
TABLE_ROWS = 16
STATE = 8

VMEM = pl.BlockSpec(memory_space=pltpu.VMEM)
SMEM = pl.BlockSpec(memory_space=pltpu.SMEM)
HBM = pl.BlockSpec(memory_space=pltpu.HBM)


def moved_along(block, axis, distance):
    count = lax.axis_size(axis)
    return lax.ppermute(block, axis, [(i, (i + distance) % count) for i in range(count)])


def swapped_z(blocks):
    count = lax.axis_size("gz")
    first = [(i, i ^ 1) for i in range(count)]
    second = [(i, (((i + 1) ^ 1) - 1) % count) for i in range(count)]
    return lax.ppermute(blocks[0], "gz", first), lax.ppermute(blocks[1], "gz", second)


def swapped_y(blocks):
    nz, ny = lax.axis_size("gz"), lax.axis_size("gy")
    first = [(j, j ^ 1) for j in range(ny)]
    second = []
    for k in range(nz):
        second.append((k * ny, (k ^ 1) * ny))
        second.append((k * ny + ny - 1, (k ^ 1) * ny + ny - 1))
        second.extend((k * ny + j, k * ny + ((j + 1) ^ 1) - 1) for j in range(1, ny - 1))
    middle = lax.ppermute(blocks[1], ("gz", "gy"), second)
    return lax.ppermute(blocks[0], "gy", first), middle


def moved_diagonally(block, distance):
    nx, nz = lax.axis_size("gx"), lax.axis_size("gz")
    route = [(i * nz + k, (i + distance) % nx * nz + (k + distance) % nz) for i in range(nx) for k in range(nz)]
    return lax.ppermute(block, ("gx", "gz"), route)


def call(
    body, outs, *operands, smem=(), hbm=(), smem_outs=(), hbm_outs=(), scratch=(), aliases=None, cycles=0, limit=40
):
    return pl.pallas_call(
        body,
        out_shape=[o if isinstance(o, jax.ShapeDtypeStruct) else jax.ShapeDtypeStruct(o, jnp.float32) for o in outs],
        in_specs=[SMEM if i in smem else HBM if i in hbm else VMEM for i in range(len(operands))],
        out_specs=[SMEM if i in smem_outs else HBM if i in hbm_outs else VMEM for i in range(len(outs))],
        scratch_shapes=list(scratch),
        input_output_aliases=aliases or {},
        compiler_params=pltpu.CompilerParams(vmem_limit_bytes=limit * 1024 * 1024),
        cost_estimate=pl.CostEstimate(flops=cycles * 4096, bytes_accessed=cycles * 1024, transcendentals=0),
    )(*operands)


def lane_ids(rows):
    return lax.broadcasted_iota(jnp.int32, (rows, LANES), 1)


def row_ids(rows):
    return lax.broadcasted_iota(jnp.int32, (rows, LANES), 0)


def turned(value, shift):
    shift = shift % LANES
    return pltpu.roll(value, shift, 1) if shift else value


def odd(axis):
    return lax.axis_index(axis) % 2


def begin_kernel(
    gas_ref, velocity_in, fraction_in, response_in, cell_in, brick_in, crossing_in,
    grid_ref, face_ref, plane_ref, velocity_ref, fraction_ref, response_ref, cell_ref, brick_ref, crossing_ref, sems,
):
    comps, size_x, size_y, _ = gas_ref.shape
    pairs = [
        (gas_ref, grid_ref.at[:, 1 : size_x + 1, 0:size_y]),
        (velocity_in, velocity_ref), (fraction_in, fraction_ref), (response_in, response_ref),
        (cell_in, cell_ref), (brick_in, brick_ref), (crossing_in, crossing_ref),
    ]
    copies = [pltpu.make_async_copy(source, target, sems.at[i]) for i, (source, target) in enumerate(pairs)]
    for copy in copies:
        copy.start()
    zeros = jnp.zeros((ROWS_Y, LANES), jnp.float32)
    for c in range(comps):
        grid_ref[c, 0] = zeros
        grid_ref[c, size_x + 1] = zeros
        for x in range(size_x):
            grid_ref[c, x + 1, size_y:] = zeros[size_y:]
    copies[0].wait()
    lane = lane_ids(size_y)
    face = jnp.zeros((size_y, LANES), jnp.float32)
    for c in range(comps):
        plane_ref[c * size_y : (c + 1) * size_y] = grid_ref[c, 1, 0:size_y]
        for x in range(size_x):
            place = PACK * c + x
            face = jnp.where(lane == place, turned(grid_ref[c, x + 1, 0:size_y], place), face)
    face_ref[...] = face
    for copy in copies[1:]:
        copy.wait()


def parts_of(value):
    main = value.astype(jnp.bfloat16).astype(jnp.float32)
    return main, value - main


def lay_out(grid_ref, lines_ref, p, q, size_y, size_z):
    comps = grid_ref.shape[0]
    rows_z = size_z + 8
    count_y = size_y // BY
    for c in range(comps):
        planes = [grid_ref[c, p * BX + a + 1, q * BY : q * BY + REACH_Y] for a in range(REACH_X)]
        main, rest = parts_of(jnp.concatenate(planes, axis=0))
        stack = jnp.concatenate([main, rest, main, jnp.zeros((LANES - 3 * SPREAD, LANES), jnp.float32)], axis=0)
        at = ((p * count_y + q) * comps + c) * rows_z
        lines_ref[at : at + size_z] = jnp.transpose(stack)


def lay_out_top(turned_ref, lines_ref, q, comps, count_x, count_y, size_z):
    lane = lane_ids(count_x)
    rows_z = size_z + 8
    for c in range(comps):
        total = jnp.zeros((count_x, LANES), jnp.float32)
        for a in range(REACH_X):
            rows = turned_ref[pl.ds(PACK * c + a, count_x, stride=BX)]
            total = jnp.where(lane // REACH_Y == a, turned(rows, a * REACH_Y - q * BY), total)
        main, rest = parts_of(total)
        line = main + turned(rest, SPREAD) + turned(main, 2 * SPREAD)
        for p in range(count_x):
            at = ((p * count_y + q) * comps + c) * rows_z + size_z
            lines_ref[at : at + 1] = line[p : p + 1]


def prepare_kernel(
    grid_ref, velocity_ref, fraction_ref, response_ref, cell_ref, brick_ref,
    lines_ref, deposit_ref, table_ref, ready_ref, list_ref,
):
    comps, size_x, size_y, size_z = grid_ref.shape[0], grid_ref.shape[1] - 2, grid_ref.shape[2] - 8, grid_ref.shape[3]
    nblocks = velocity_ref.shape[1]
    count_x, count_y, count_z = size_x // BX, size_y // BY, size_z // BZ
    rows_z = size_z + 8


    def visit(k, counts):
        late = jnp.where(lax.rem(lax.div(brick_ref[k], count_z), count_y) == count_y - 1, 1, 0)
        list_ref[jnp.where(late == 1, nblocks + counts[1], counts[0])] = k
        return counts[0] + 1 - late, counts[1] + late

    early, late = lax.fori_loop(0, nblocks, visit, (jnp.int32(0), jnp.int32(0)), unroll=8)
    list_ref[2 * nblocks] = early
    list_ref[2 * nblocks + 1] = late
    ready_ref[...] = jnp.zeros_like(ready_ref)

    deposit_ref[...] = jnp.zeros_like(deposit_ref)
    for p in range(count_x):
        for q in range(count_y):
            for c in range(comps):
                at = ((p * count_y + q) * comps + c) * rows_z + size_z
                lines_ref[at : at + 8] = jnp.zeros((8, LANES), jnp.float32)
    for p in range(count_x - 1):
        for q in range(count_y - 1):
            lay_out(grid_ref, lines_ref, p, q, size_y, size_z)

    cells = cell_ref[...]
    cell_x, cell_y, cell_z = cells // (BY * BZ), cells // BZ % BY, cells % BZ
    along_x = fraction_ref[0]

    def put(row, value):
        table_ref[pl.ds(row, nblocks, stride=TABLE_ROWS)] = value

    for a in range(REACH_X):
        put(WEIGHT + a, jnp.where(cell_x == a, 1.0 - along_x, 0.0) + jnp.where(cell_x == a - 1, along_x, 0.0))
    put(ALONG_Y, fraction_ref[1])
    put(IN_Y, cell_y.astype(jnp.float32))
    put(ALONG_Z, fraction_ref[2])
    put(IN_Z, cell_z.astype(jnp.float32))
    put(RESPONSE, response_ref[...])
    for c in range(comps):
        put(MOVING + c, velocity_ref[c])
        put(OFFSET + c, fraction_ref[c])
    spare = table_ref.shape[0] - nblocks * TABLE_ROWS
    row = row_ids(spare)
    table_ref[nblocks * TABLE_ROWS :] = jnp.where(row % TABLE_ROWS == RESPONSE, 1.0, 0.0)


def y_lines_kernel(grid_ref, face_ref, from_x_ref, edge_ref, ready_ref, out_ref):
    comps, size_x = grid_ref.shape[0], grid_ref.shape[1] - 2
    size_y = face_ref.shape[0]
    for c in range(comps):
        out_ref[c * size_x : (c + 1) * size_x] = grid_ref[c, 1 : size_x + 1, 0]
        out_ref[comps * size_x + c : comps * size_x + c + 1] = from_x_ref[c * size_y : c * size_y + 1]
    line = jnp.where(lane_ids(8) % PACK == size_x, turned(edge_ref[0:8], size_x), face_ref[0:8])
    out_ref[comps * size_x + comps : comps * size_x + comps + 1] = line[0:1]


def halo_xz_kernel(grid_in_ref, lines_in_ref, face_ref, from_x_ref, edge_ref, grid_ref, lines_ref, top_ref, turned_ref):
    comps, size_x = grid_ref.shape[0], grid_ref.shape[1] - 2
    size_y, size_z = face_ref.shape[0], grid_ref.shape[3]
    count_x, count_y = size_x // BX, size_y // BY
    for c in range(comps):
        grid_ref[c, size_x + 1, 0:size_y] = from_x_ref[c * size_y : (c + 1) * size_y]
    for q in range(count_y - 1):
        lay_out(grid_ref, lines_ref, count_x - 1, q, size_y, size_z)
    top = jnp.where(lane_ids(size_y) % PACK == size_x, turned(edge_ref[...], size_x), face_ref[...])
    top_ref[0:size_y] = top
    top_ref[size_y:] = jnp.zeros((LANES - size_y, LANES), jnp.float32)
    turned_ref[...] = jnp.transpose(top_ref[...])
    for q in range(count_y - 1):
        lay_out_top(turned_ref, lines_ref, q, comps, count_x, count_y, size_z)


def halo_y_kernel(size_y, grid_in_ref, lines_in_ref, top_in_ref, first_ref, second_ref, grid_ref, lines_ref, turned_ref):
    comps, size_x, size_z = grid_ref.shape[0], grid_ref.shape[1] - 2, grid_ref.shape[3]
    count_x, count_y = size_x // BX, size_y // BY
    inside = lax.axis_index("gy") != lax.axis_size("gy") - 1
    kept = (row_ids(8) == 0) & inside
    even = jnp.full((1, LANES), odd("gy")) == 0

    def line_at(row):
        line = jnp.where(even, first_ref[row : row + 1], second_ref[row : row + 1])
        return jnp.where(kept, jnp.broadcast_to(line, (8, LANES)), 0.0)

    for c in range(comps):
        for x in range(size_x + 1):
            grid_ref[c, x + 1, size_y:] = line_at(c * size_x + x if x < size_x else comps * size_x + c)
    for p in range(count_x):
        lay_out(grid_ref, lines_ref, p, count_y - 1, size_y, size_z)
    corner = line_at(comps * size_x + comps)
    rest = jnp.zeros((LANES - size_y - 8, LANES), jnp.float32)
    turned_ref[...] = jnp.transpose(jnp.concatenate([top_in_ref[0:size_y], corner, rest], axis=0))
    lay_out_top(turned_ref, lines_ref, count_y - 1, comps, count_x, count_y, size_z)


def block_steps(dims, list_ref, brick_ref, end):
    comps, _, count_y, count_z, rows_z = dims
    nblocks = brick_ref.shape[0]
    sub = row_ids(8)
    row_y = row_ids(REACH_Y).astype(jnp.float32)
    row_z = row_ids(REACH_Z).astype(jnp.float32)
    lanes = lane_ids(REACH_Z)

    def hat(rows, inside, along):
        return jnp.where(rows == inside, 1.0 - along, 0.0) + jnp.where(rows == inside + 1.0, along, 0.0)

    def place_of(at):
        k = jnp.where(at < end, list_ref[jnp.minimum(at, 2 * nblocks + 1)], nblocks)
        brick = jnp.where(k < nblocks, brick_ref[jnp.minimum(k, nblocks - 1)], 0)
        brick_x = lax.div(brick, count_y * count_z)
        brick_y = lax.rem(lax.div(brick, count_z), count_y)
        return k, brick_x * count_y + brick_y, lax.rem(brick, count_z)

    def loaded(at, lines_ref, table_ref):
        k, pair, brick_z = place_of(at)
        first = pl.multiple_of(pair * comps * rows_z + brick_z * BZ, 8)
        window = jnp.concatenate([lines_ref[pl.ds(first + c * rows_z, REACH_Z)] for c in range(comps)], axis=0)
        table = table_ref[pl.ds(pl.multiple_of(k * TABLE_ROWS, TABLE_ROWS), TABLE_ROWS)]
        return k, window, [table[i : i + 1] for i in range(TABLE_ROWS)]

    def weighted(rows):
        weight_y = hat(row_y, rows[IN_Y], rows[ALONG_Y])
        weight_z = hat(row_z, rows[IN_Z], rows[ALONG_Z])
        weight = jnp.concatenate([rows[WEIGHT + a] * weight_y for a in range(REACH_X)], axis=0)
        return weight_z, *parts_of(weight)

    def stepped(seen, weight_z, rows):
        rate = 1.0 / rows[RESPONSE]
        state, moved, pushed = [], [], []
        for c in range(comps):
            gas_sample = jnp.sum(seen[c * REACH_Z : (c + 1) * REACH_Z] * weight_z, axis=0, keepdims=True)
            drag = (gas_sample - rows[MOVING + c]) * rate
            state.append(rows[MOVING + c] + TIME_STEP * drag)
            moved.append(rows[OFFSET + c] + TIME_STEP * state[c])
            pushed.append(drag * weight_z)
        tile = jnp.broadcast_to(rows[RESPONSE], (STATE, LANES))
        for i, value in enumerate(state + moved):
            tile = jnp.where(sub == i, value, tile)
        return tile, jnp.concatenate(parts_of(jnp.concatenate(pushed, axis=0)), axis=0)

    def gathered(one, two):
        tables, windows, weights = [], [], []
        for _, window, rows in (one, two):
            weight_z, main, rest = weighted(rows)
            weights.append((weight_z, main, rest))
            unused = jnp.zeros((LANES - 3 * SPREAD, LANES), jnp.float32)
            tables.append(jnp.concatenate([main, main, rest, unused], axis=0).astype(jnp.bfloat16))
            windows.append(window)
        seen = lax.dot_general(
            jnp.concatenate(windows, axis=0).astype(jnp.bfloat16), jnp.concatenate(tables, axis=1),
            (((1,), (0,)), ((), ())), preferred_element_type=jnp.float32,
        )
        height = comps * REACH_Z
        tiles, fresh = [], []
        for i, (_, _, rows) in enumerate((one, two)):
            weight_z, main, rest = weights[i]
            mine = seen[i * height : (i + 1) * height, i * LANES : (i + 1) * LANES]
            tile, push = stepped(mine, weight_z, rows)
            tiles.append(tile)
            unused = jnp.zeros((LANES - comps * SPREAD, LANES), jnp.float32)
            spread = jnp.concatenate([main] * comps + [unused] + [rest] * comps + [unused], axis=0)
            fresh.append((push.astype(jnp.bfloat16), spread.astype(jnp.bfloat16)))
        return tiles, fresh

    def shared(push, spread):
        shares = lax.dot_general(push, spread, (((1,), (1,)), ((), ())), preferred_element_type=jnp.float32)
        height = comps * REACH_Z
        total = shares[:height, :LANES] + shares[:height, LANES:] + shares[height:, :LANES]
        result = jnp.zeros((REACH_Z, LANES), jnp.float32)
        for c in range(comps):
            inside = (lanes >= c * SPREAD) & (lanes < (c + 1) * SPREAD)
            result = jnp.where(inside, total[c * REACH_Z : (c + 1) * REACH_Z], result)
        return result

    def add(deposit_ref, at, shares):
        spots = []
        for u in range(len(shares)):
            _, pair, brick_z = place_of(at + u)
            spots.append(pl.ds(pl.multiple_of(pair * rows_z + brick_z * BZ, 8), REACH_Z))
        for spot, share in zip(spots, shares):
            deposit_ref[spot] = deposit_ref[spot] + share

    def group_of(taken):
        tiles, fresh = [], []
        for u in range(0, len(taken), 2):
            both, kept = gathered(taken[u], taken[u + 1])
            tiles.extend(both)
            fresh.extend(kept)
        return tiles, fresh

    def keep(state_ref, taken, tiles):
        for (k, _, _), tile in zip(taken, tiles):
            state_ref[pl.ds(pl.multiple_of(STATE * k, STATE), STATE)] = tile

    def deposits_of(kept):
        return [shared(push, spread) for push, spread in kept]

    return loaded, group_of, keep, deposits_of, add


def groups_in(list_ref, late, many=UNROLL):
    room = (list_ref.shape[0] - 2) // 2
    count = list_ref[2 * room + late]
    return late * room, (count + many - 1) // many, late * room + count


def leave(crossing_ref, state_ref, leaving_ref, faces):
    slots = crossing_ref.shape[1]
    rows = (leaving_ref.shape[0] - 8) // (len(faces) * slots)
    for i, face in enumerate(faces):
        tiles = []
        for slot in range(slots):
            block = crossing_ref[face, slot]
            spot = pl.ds(pl.multiple_of(jnp.maximum(block, 0) * STATE, STATE), STATE)
            live = jnp.full((STATE, LANES), block, jnp.int32) >= 0
            tiles.append(jnp.where(live, state_ref[spot], 0.0))
        for slot, tile in enumerate(tiles):
            leaving_ref[pl.ds(i * rows * slots + slot, rows, stride=slots)] = tile[:rows]


def fetched(sems, *pairs):
    copies = [pltpu.make_async_copy(source, target, sems.at[i]) for i, (source, target) in enumerate(pairs)]
    for copy in copies:
        copy.start()
    return copies


def gather_kernel(
    dims, list_in, brick_in, table_ref, grid_in_ref, lines_in_ref, face_ref, from_x_ref, edge_ref,
    state_ref, push_ref, spread_ref, grid_ref, lines_ref, top_ref, list_ref, brick_ref, turned_ref, sems,
):
    copies = fetched(sems, (list_in, list_ref), (brick_in, brick_ref))
    halo_xz_kernel(grid_in_ref, lines_in_ref, face_ref, from_x_ref, edge_ref, grid_ref, lines_ref, top_ref, turned_ref)
    for copy in copies:
        copy.wait()
    base, groups, end = groups_in(list_ref, 0, WIDE)
    loaded, group_of, keep, _, _ = block_steps(dims, list_ref, brick_ref, end)

    @pl.loop(0, groups)
    def _(group):
        taken = [loaded(base + group * WIDE + u, lines_ref, table_ref) for u in range(WIDE)]
        tiles, fresh = group_of(taken)
        keep(state_ref, taken, tiles)
        for i, (push, spread) in enumerate(fresh):
            push_ref[group * WIDE + i] = push
            spread_ref[group * WIDE + i] = spread


def deposit_kernel(
    dims, push, diffuse, list_ref, brick_ref, crossing_ref, push_ref, spread_ref, state_ref, deposit_in_ref, top_tiles_ref,
    grid_ref, deposit_ref, leaving_ref, plane_ref, x_ref, z_ref, face_ref, tiles_ref, turned_ref,
):
    base, groups, end = groups_in(list_ref, 0, WIDE)
    _, _, _, deposits_of, add = block_steps(dims, list_ref, brick_ref, end)
    leave(crossing_ref, state_ref, leaving_ref, (0, 1, 4, 5))

    @pl.loop(0, groups)
    def _(group):
        mine = [group * WIDE + i for i in range(WIDE)]
        add(deposit_ref, base + group * WIDE, deposits_of([(push_ref[i], spread_ref[i]) for i in mine]))

    merge(deposit_ref, top_tiles_ref, plane_ref, face_ref, tiles_ref, turned_ref)
    send_xz(push, diffuse, grid_ref, plane_ref, face_ref, x_ref, z_ref)


def late_kernel(
    dims, push, diffuse, list_in, brick_in, crossing_in, table_ref, grid_in_ref, lines_in_ref, top_in_ref,
    first_ref, second_ref,
    state_in_ref, deposit_in_ref,
    grid_ref, lines_ref, state_ref, deposit_ref, y1_ref, y2_ref, tiles_ref,
    push_ref, spread_ref, list_ref, brick_ref, crossing_ref, turned_ref, leaving_ref, y_lines_ref, sems,
):
    copies = fetched(sems, (list_in, list_ref), (brick_in, brick_ref), (crossing_in, crossing_ref))
    halo_y_kernel(
        dims[2] * BY, grid_in_ref, lines_in_ref, top_in_ref, first_ref, second_ref, grid_ref, lines_ref, turned_ref
    )
    for copy in copies:
        copy.wait()
    base, groups, end = groups_in(list_ref, 1)
    loaded, group_of, keep, deposits_of, add = block_steps(dims, list_ref, brick_ref, end)
    push_ref[...] = jnp.zeros_like(push_ref)
    spread_ref[...] = jnp.zeros_like(spread_ref)

    @pl.loop(0, groups + 1)
    def _(group):
        now = base + jnp.maximum(jnp.minimum(group, groups - 1), 0) * UNROLL
        before = base + jnp.maximum(group - 1, 0) * UNROLL
        taken = [loaded(now + u, lines_ref, table_ref) for u in range(UNROLL)]
        shares = deposits_of([(push_ref[i], spread_ref[i]) for i in range(UNROLL)])
        tiles, fresh = group_of(taken)
        add(deposit_ref, before, shares)
        keep(state_ref, taken, tiles)
        for i, (kept, spread) in enumerate(fresh):
            push_ref[i] = kept
            spread_ref[i] = spread

    leave(crossing_ref, state_ref, leaving_ref, (2, 3))
    send_y(push, diffuse, leaving_ref, grid_ref, deposit_ref, y1_ref, y2_ref, tiles_ref, y_lines_ref)


def top_rows(deposit_ref, q, count_x, count_y, rows_z, size_z):
    total = None
    for p in range(count_x):
        at = (p * count_y + q) * rows_z + size_z
        value = pltpu.roll(deposit_ref[at : at + 8], p, 0) if p else deposit_ref[at : at + 8]
        total = value if total is None else total + value
    return total


def send_y(push, diffuse, leaving_ref, grid_ref, deposit_ref, y1_ref, y2_ref, tiles_ref, lines_ref):
    comps, size_x, size_y, size_z = grid_ref.shape[0], grid_ref.shape[1] - 2, grid_ref.shape[2] - 8, grid_ref.shape[3]
    count_x, count_y = size_x // BX, size_y // BY
    rows_z = size_z + 8
    rows = (leaving_ref.shape[0] - 8) // 2
    height = comps * SPREAD
    for p in range(count_x):
        at = (p * count_y + count_y - 1) * rows_z
        tiles_ref[p * height : (p + 1) * height] = jnp.transpose(deposit_ref[at : at + size_z])[:height]
    first = jnp.full((rows, LANES), odd("gy")) == 0
    y1_ref[0:rows] = jnp.where(first, leaving_ref[0:rows], leaving_ref[rows : 2 * rows])
    y2_ref[0:rows] = jnp.where(first, leaving_ref[rows : 2 * rows], leaving_ref[0:rows])
    lines_ref[...] = jnp.zeros_like(lines_ref)
    for c in range(comps):
        for p in range(count_x):
            spot = slice(c * ROWS_Y + p * BX, c * ROWS_Y + p * BX + REACH_X)
            line = tiles_ref[pl.ds(p * height + c * SPREAD + BY, REACH_X, stride=REACH_Y)]
            lines_ref[spot] = lines_ref[spot] + line
    wrapped = top_rows(deposit_ref, count_y - 1, count_x, count_y, rows_z, size_z)
    lane = lane_ids(8)
    packed = jnp.zeros((8, LANES), jnp.float32)
    for c in range(comps):
        spot = slice(c * ROWS_Y, (c + 1) * ROWS_Y)
        beside = jnp.concatenate([grid_ref[c, 1 : size_x + 1, size_y - 1], jnp.zeros((8, LANES), jnp.float32)], axis=0)
        line = push * lines_ref[spot] + diffuse * beside
        at = rows + c * (size_x + 1)
        y1_ref[at : at + size_x + 1] = line[: size_x + 1]
        y2_ref[at : at + size_x + 1] = line[: size_x + 1]
        for a in range(REACH_X):
            place = PACK * c + a
            value = turned(wrapped, place - c * SPREAD - a * REACH_Y - BY)
            packed = packed + jnp.where(lane == place, value, 0.0)
    corner = packed[0:1]
    for p in range(1, count_x):
        corner = corner + turned(packed[p : p + 1], p * BX)
    at = rows + comps * (size_x + 1)
    y1_ref[at : at + 1] = push * corner
    y2_ref[at : at + 1] = push * corner


def merge(deposit_ref, top_tiles_ref, plane_ref, face_ref, tiles_ref, turned_ref):
    comps, planes = plane_ref.shape[:2]
    count_x, size_z = (planes - 1) // BX, plane_ref.shape[3]
    rows_z = size_z + 8
    count_y = deposit_ref.shape[0] // (rows_z * count_x)
    height = comps * SPREAD
    for p in range(count_x):
        for q in range(count_y - 1):
            at = p * count_y + q
            value = jnp.transpose(deposit_ref[at * rows_z : at * rows_z + size_z])
            tiles_ref[at * height : (at + 1) * height] = value[:height]
    top = row_ids(REACH_Y) >= BY
    for c in range(comps):
        for x in range(planes):
            bricks = [(x // BX, x % BX)] if x < planes - 1 else []
            if x and x % BX == 0:
                bricks.append((x // BX - 1, BX))

            def tile(q):
                total = None
                for p, a in bricks:
                    at = c * SPREAD + a * REACH_Y
                    if q < count_y - 1:
                        value = tiles_ref[(p * count_y + q) * height + at : (p * count_y + q) * height + at + REACH_Y]
                    else:
                        value = top_tiles_ref[p * height + at : p * height + at + REACH_Y]
                    total = value if total is None else total + value
                return total

            carried = None
            for q in range(0, count_y, 2):
                here = tile(q)
                if carried is not None:
                    here = here + carried
                between = pltpu.roll(tile(q + 1), BY, 0)
                here = here + jnp.where(top, between, 0.0)
                carried = jnp.where(top, 0.0, between)
                plane_ref[c, x, q * BY : q * BY + REACH_Y] = here
            plane_ref[c, x, count_y * BY :] = carried

    lane = lane_ids(count_x)
    turned_ref[...] = jnp.zeros_like(turned_ref)
    for q in range(count_y):
        wrapped = top_rows(deposit_ref, q, count_x, count_y, rows_z, size_z)[:count_x]
        within = (lane >= q * BY) & (lane <= (q + 1) * BY)
        for c in range(comps):
            for a in range(REACH_X):
                value = turned(wrapped, q * BY - c * SPREAD - a * REACH_Y)
                spot = pl.ds(PACK * c + a, count_x, stride=BX)
                turned_ref[spot] = turned_ref[spot] + jnp.where(within, value, 0.0)
    face_ref[...] = jnp.transpose(turned_ref[...])[: face_ref.shape[0]]


def send_xz(push, diffuse, grid_ref, deposit_ref, face_ref, x_ref, z_ref):
    comps, size_x = grid_ref.shape[0], grid_ref.shape[1] - 2
    size_y = z_ref.shape[0]
    lane = lane_ids(size_y)
    packed = push * face_ref[0:size_y]
    for c in range(comps):
        for x in range(size_x):
            place = PACK * c + x
            packed = packed + jnp.where(lane == place, diffuse * turned(grid_ref[c, x + 1, 0:size_y], place + 1), 0.0)
        total = push * deposit_ref[c, size_x, 0:size_y]
        x_ref[c * size_y : (c + 1) * size_y] = diffuse * grid_ref[c, size_x, 0:size_y] + total
    z_ref[...] = packed


def base_kernel(push, diffuse, count, grid_ref, deposit_ref, top_ref, y1_ref, y2_ref, state_ref, base_ref, velocity_ref):
    comps, size_x, size_y, size_z = base_ref.shape
    lane, sub = lane_ids(size_y), row_ids(size_y)
    top = top_ref[0:size_y]
    for c in range(comps):
        at = count + c * (size_x + 1)
        lines = below(y1_ref, y2_ref, slice(at, at + size_x))
        for x in range(size_x):
            here = grid_ref[c, x + 1, 0:size_y]
            before = jnp.where(sub == 0, 0.0, pltpu.roll(here, 1, 0))
            laplace = grid_ref[c, x, 0:size_y] + grid_ref[c, x + 2, 0:size_y]
            laplace = laplace + grid_ref[c, x + 1, 1 : size_y + 1] + before
            ahead = jnp.where(lane == size_z - 1, turned(top, size_z - 1 - (PACK * c + x)), turned(here, -1))
            laplace = laplace + ahead + jnp.where(lane == 0, 0.0, turned(here, 1)) - 6.0 * here
            total = here + diffuse * laplace + push * deposit_ref[c, x, 0:size_y]
            line = jnp.broadcast_to(lines[x : x + 1], (size_y, LANES))
            base_ref[c, x] = total + jnp.where(sub == 0, line, 0.0)
        velocity_ref[c] = state_ref[pl.ds(c, velocity_ref.shape[1], stride=STATE)]


def below(first_ref, second_ref, rows):
    got = jnp.where(jnp.full((1, LANES), odd("gy")) == 1, first_ref[rows], second_ref[rows])
    return jnp.where(jnp.full((1, LANES), lax.axis_index("gy")) != 0, got, 0.0)


def relay_kernel(size_x, size_y, comps, count, first_ref, second_ref, x_in_ref, z_in_ref, leaving_ref, x_ref, z1_ref, z2_ref, edge_ref):
    edge = comps * size_y
    x_ref[0:edge] = x_in_ref[...]
    for c in range(comps):
        at = count + c * (size_x + 1) + size_x
        spot = slice(c * size_y, c * size_y + 1)
        x_ref[spot] = x_in_ref[spot] + below(first_ref, second_ref, slice(at, at + 1))
    x_ref[edge : edge + count] = leaving_ref[0:count]
    if x_ref.shape[0] > edge + count:
        x_ref[edge + count : edge + 2 * count] = leaving_ref[count : 2 * count]
    at = count + comps * (size_x + 1)
    edge_ref[size_y:] = jnp.zeros((edge_ref.shape[0] - size_y, LANES), jnp.float32)
    edge_ref[0:size_y] = z_in_ref[...]
    edge_ref[0:1] = z_in_ref[0:1] + below(first_ref, second_ref, slice(at, at + 1))
    first = jnp.full((1, LANES), odd("gz")) == 0
    plus = jnp.concatenate([leaving_ref[2 * count : 3 * count], edge_ref[0:size_y]], axis=0)
    minus = jnp.concatenate([leaving_ref[3 * count : 4 * count], jnp.zeros((size_y, LANES), jnp.float32)], axis=0)
    z1_ref[...] = jnp.where(first, plus, minus)
    z2_ref[0 : count + size_y] = jnp.where(first, minus, plus)
    z2_ref[count + size_y :] = jnp.zeros((z2_ref.shape[0] - count - size_y, LANES), jnp.float32)


def finish_kernel(
    count, base_ref, y1_ref, y2_ref, x_ref, minus_x_ref, z1_ref, z2_ref, edge_ref, gas_out, arrivals_out,
    gas_ref, arrivals_ref, sems,
):
    comps, size_x, size_y, _ = base_ref.shape
    first_lane = lane_ids(size_y) == 0
    odd_y, odd_z = jnp.full((1, LANES), odd("gy")) == 1, jnp.full((1, LANES), odd("gz")) == 1
    place = jnp.full((1, LANES), lax.axis_index("gy"))
    lower, upper = place != 0, place != lax.axis_size("gy") - 1
    rows = slice(count, count + size_y)
    slots = arrivals_ref.shape[2]
    for i in range(arrivals_ref.shape[1]):

        def rows_of(ref, at=0):
            return ref[at + i * slots : at + (i + 1) * slots]

        arrivals_ref[0, i] = rows_of(x_ref, comps * size_y)
        arrivals_ref[1, i] = rows_of(minus_x_ref, minus_x_ref.shape[0] - count)
        y1, y2 = rows_of(y1_ref), rows_of(y2_ref)
        arrivals_ref[2, i] = jnp.where(lower, jnp.where(odd_y, y1, y2), 0.0)
        arrivals_ref[3, i] = jnp.where(upper, jnp.where(odd_y, y2, y1), 0.0)
        z1, z2 = rows_of(z1_ref), rows_of(z2_ref)
        arrivals_ref[4, i] = jnp.where(odd_z, z1, z2)
        arrivals_ref[5, i] = jnp.where(odd_z, z2, z1)
    copies = [pltpu.make_async_copy(arrivals_ref, arrivals_out, sems.at[comps])]
    copies[0].start()
    face = jnp.where(odd_z, z1_ref[rows], z2_ref[rows])
    corner = edge_ref[0:size_y]
    for c in range(comps):
        for x in range(size_x):
            total = base_ref[c, x]
            far = turned(face, -(PACK * c + x))
            if x == 0:
                total = total + x_ref[c * size_y : (c + 1) * size_y]
                far = far + turned(corner, -(PACK * c + size_x))
            gas_ref[c, x] = total + jnp.where(first_lane, far, 0.0)
        copies.append(pltpu.make_async_copy(gas_ref.at[c], gas_out.at[c], sems.at[c]))
        copies[-1].start()
    for copy in copies:
        copy.wait()


def per_device(gas_field, velocity, fraction, response, cell_index, brick_index, crossing):
    comps, size_x, size_y, size_z = gas_field.shape
    nblocks = velocity.shape[0]
    loading = 0.5 * size_x * size_y * size_z / (nblocks * 128)
    push, diffuse = -TIME_STEP * loading, TIME_STEP * VISCOSITY
    velocity = jnp.transpose(velocity, (1, 0, 2))
    fraction = jnp.transpose(fraction, (1, 0, 2))
    spare = nblocks + 8
    rows_z = size_z + 8
    grid_shape = (comps, size_x + 2, ROWS_Y, LANES)
    lines_shape = ((size_x // BX) * (size_y // BY) * comps * rows_z, LANES)
    deposit_shape = ((size_x // BX) * (size_y // BY) * rows_z, LANES)

    inputs = (gas_field, velocity, fraction, response, cell_index, brick_index, crossing)
    inputs = [pltpu.with_memory_space_constraint(array, pltpu.HBM) for array in inputs]
    grid, face, plane, velocity, fraction, response, cell_index, brick_index, crossing = call(
        begin_kernel,
        [grid_shape, (size_y, LANES), (comps * size_y, LANES)]
        + [jax.ShapeDtypeStruct(array.shape, array.dtype) for array in inputs[1:]],
        *inputs, hbm=range(7), scratch=(pltpu.SemaphoreType.DMA((7,)),),
    )
    from_z = moved_along(face, "gz", -1)
    from_x = moved_along(plane, "gx", -1)
    from_xz = moved_diagonally(face, -1)
    lines, deposit, table, ready, blocks = call(
        prepare_kernel,
        [
            lines_shape,
            deposit_shape,
            (TABLE_ROWS * spare, LANES),
            (8, LANES),
            jax.ShapeDtypeStruct((2 * nblocks + 2,), jnp.int32),
        ],
        grid, velocity, fraction, response, cell_index, brick_index,
        smem=(5,), smem_outs=(4,), cycles=3000,
    )
    line_rows = -(-(comps * size_x + comps + 1) // 8) * 8 + 8
    (y_lines,) = call(y_lines_kernel, [(line_rows, LANES)], grid, from_z, from_x, from_xz, ready)
    y1, y2 = swapped_y((y_lines, y_lines))
    square = pltpu.VMEM((LANES, LANES), jnp.float32)
    scalars = (pltpu.SMEM(blocks.shape, jnp.int32), pltpu.SMEM(brick_index.shape, jnp.int32))
    dims = (comps, size_x // BX, size_y // BY, size_z // BZ, rows_z)
    slots = crossing.shape[1]
    count = 7 * slots

    def parts(many):
        return [(many, 2 * comps * REACH_Z, LANES), (many, 2 * LANES, LANES)]

    state, push_parts, spread_parts, grid, lines, top = call(
        functools.partial(gather_kernel, dims),
        [(STATE * spare, LANES)]
        + [jax.ShapeDtypeStruct(shape, jnp.bfloat16) for shape in parts(-(-nblocks // WIDE) * WIDE)]
        + [grid_shape, lines_shape, (LANES, LANES)],
        blocks, brick_index, table, grid, lines, from_z, from_x, from_xz,
        aliases={3: 3, 4: 4}, cycles=4000, scratch=(*scalars, square, pltpu.SemaphoreType.DMA((2,))),
    )
    height = comps * SPREAD
    grid, lines, state, deposit, to_y1, to_y2, top_tiles = call(
        functools.partial(late_kernel, dims, push, diffuse),
        [
            grid_shape,
            lines_shape,
            (STATE * spare, LANES),
            deposit_shape,
            (count + line_rows, LANES),
            (count + line_rows, LANES),
            ((size_x // BX) * height + 8 * REACH_Y, LANES),
        ],
        blocks, brick_index, crossing, table, grid, lines, top, y1, y2, state, deposit,
        aliases={4: 0, 5: 1, 9: 2, 10: 3}, cycles=2000,
        scratch=[
            *(pltpu.VMEM(shape, jnp.bfloat16) for shape in parts(UNROLL)),
            *scalars,
            pltpu.SMEM(crossing.shape, jnp.int32),
            square,
            pltpu.VMEM((2 * count + 8, LANES), jnp.float32),
            pltpu.VMEM((comps * ROWS_Y, LANES), jnp.float32),
            pltpu.SemaphoreType.DMA((3,)),
        ],
    )
    y1, y2 = swapped_y((to_y1, to_y2))
    _, leaving, deposit, to_x, to_z = call(
        functools.partial(deposit_kernel, dims, push, diffuse),
        [
            deposit_shape,
            (4 * count + 8, LANES),
            (comps, size_x + 1, ROWS_Y, LANES),
            (comps * size_y, LANES),
            (size_y, LANES),
        ],
        blocks, brick_index, crossing, push_parts, spread_parts, state, deposit, top_tiles, grid,
        smem=(0, 1, 2), aliases={6: 0}, cycles=5000,
        scratch=(
            pltpu.VMEM((ROWS_Y, LANES), jnp.float32),
            pltpu.VMEM(((size_x // BX) * (size_y // BY) * height, LANES), jnp.float32),
            square,
        ),
    )
    base, velocity_next = call(
        functools.partial(base_kernel, push, diffuse, count), [gas_field.shape, (comps, nblocks, LANES)],
        grid, deposit, top, y1, y2, state, cycles=1000,
    )
    edge = comps * size_y
    both = lax.axis_size("gx") == 2
    to_x, to_z1, to_z2, to_xz = call(
        functools.partial(relay_kernel, size_x, size_y, comps, count),
        [(edge + (2 if both else 1) * count, LANES), *[(count + size_y + 8 * more, LANES) for more in range(3)]],
        y1, y2, to_x, to_z, leaving,
    )
    got_x = moved_along(to_x, "gx", 1)
    z1, z2 = swapped_z((to_z1, to_z2))
    got_xz = moved_diagonally(to_xz, 1)
    got_mx = got_x if both else moved_along(leaving[count : 2 * count], "gx", -1)
    gas_next, arrivals = call(
        functools.partial(finish_kernel, count), [gas_field.shape, (6, 7, slots, LANES)],
        base, y1, y2, got_x, got_mx, z1, z2, got_xz, hbm_outs=(0, 1),
        scratch=(
            pltpu.VMEM(gas_field.shape, jnp.float32),
            pltpu.VMEM((6, 7, slots, LANES), jnp.float32),
            pltpu.SemaphoreType.DMA((comps + 1,)),
        ),
    )
    return gas_next, jnp.transpose(velocity_next, (1, 0, 2)), jnp.transpose(arrivals, (0, 2, 1, 3))


def solution(mesh):
    owner = ("gx", "gz", "gy")
    in_specs = (
        P(None, "gx", "gy", "gz"),
        P(owner, None, None),
        P(owner, None, None),
        P(owner, None),
        P(owner, None),
        P(owner),
        P(owner, None),
    )
    out_specs = (
        P(None, "gx", "gy", "gz"),
        P(owner, None, None),
        P(owner, None, None, None),
    )
    return jax.shard_map(
        per_device, mesh=mesh, in_specs=in_specs, out_specs=out_specs, check_vma=False
    )
```
